32 devices in a mesh: dp: 8 (over z, y), tensor: 4 (over x, core).
Axes of the slice: x: 2, y: 2, z: 4, core: 2. Of those that a mesh axis runs over, the one named last changes fastest.
Arguments:
- tokens: bfloat16 [8, 512, 2048], P('dp', 'tensor'), may hold values from -6 to 6
- cotangent: bfloat16 [8, 512, 2048], P('dp', 'tensor'), may hold values from -6 to 6
- block_ids: int32 [8, 512], P('dp'), may hold values from 0 to 3, never falling along the last dimension, each value on 1 to 256 neighbouring positions
- w_qkv: float32 [3, 2048, 2048], P(None, 'dp', 'tensor'), may hold values from -0.110485435 to 0.110485435
- m_qkv: float32 [3, 2048, 2048], P(None, 'dp', 'tensor'), may hold values from -40 to 40
- v_qkv: float32 [3, 2048, 2048], P(None, 'dp', 'tensor'), may hold values from 204.8 to 819.2
- w_out: float32 [2048, 2048], P('tensor', 'dp'), may hold values from -0.125 to 0.125
- m_out: float32 [2048, 2048], P('tensor', 'dp'), may hold values from -40 to 40
- v_out: float32 [2048, 2048], P('tensor', 'dp'), may hold values from 204.8 to 819.2
- w_gu: float32 [2, 2048, 8192], P(None, 'dp', 'tensor'), may hold values from -0.125 to 0.125
- m_gu: float32 [2, 2048, 8192], P(None, 'dp', 'tensor'), may hold values from -40 to 40
- v_gu: float32 [2, 2048, 8192], P(None, 'dp', 'tensor'), may hold values from 204.8 to 819.2
- w_down: float32 [8192, 2048], P('tensor', 'dp'), may hold values from -0.0625 to 0.0625
- m_down: float32 [8192, 2048], P('tensor', 'dp'), may hold values from -40 to 40
- v_down: float32 [8192, 2048], P('tensor', 'dp'), may hold values from 204.8 to 819.2
- gains: float32 [4, 2048], P(None, 'dp'), may hold values from 0.7 to 1.6
- gain_m: float32 [4, 2048], P(None, 'dp'), may hold values from -40 to 40
- gain_v: float32 [4, 2048], P(None, 'dp'), may hold values from 204.8 to 819.2
Outputs:
- output: bfloat16 [8, 512, 2048], P('dp', 'tensor')
- grad_tokens: float32 [8, 512, 2048], P('dp', 'tensor')
- new_w_qkv: float32 [3, 2048, 2048], P(None, 'dp', 'tensor')
- new_m_qkv: float32 [3, 2048, 2048], P(None, 'dp', 'tensor')
- new_v_qkv: float32 [3, 2048, 2048], P(None, 'dp', 'tensor')
- copy_qkv: bfloat16 [3, 2048, 2048], P(None, 'dp', 'tensor')
- new_w_out: float32 [2048, 2048], P('tensor', 'dp')
- new_m_out: float32 [2048, 2048], P('tensor', 'dp')
- new_v_out: float32 [2048, 2048], P('tensor', 'dp')
- copy_out: bfloat16 [2048, 2048], P('tensor', 'dp')
- new_w_gu: float32 [2, 2048, 8192], P(None, 'dp', 'tensor')
- new_m_gu: float32 [2, 2048, 8192], P(None, 'dp', 'tensor')
- new_v_gu: float32 [2, 2048, 8192], P(None, 'dp', 'tensor')
- copy_gu: bfloat16 [2, 2048, 8192], P(None, 'dp', 'tensor')
- new_w_down: float32 [8192, 2048], P('tensor', 'dp')
- new_m_down: float32 [8192, 2048], P('tensor', 'dp')
- new_v_down: float32 [8192, 2048], P('tensor', 'dp')
- copy_down: bfloat16 [8192, 2048], P('tensor', 'dp')
- new_gains: float32 [4, 2048], P(None, 'dp')
- new_gain_m: float32 [4, 2048], P(None, 'dp')
- new_gain_v: float32 [4, 2048], P(None, 'dp')
- clip_factor: float32 [16], P('tensor')
The draws below stay inside these ranges and needn't reach their ends.
Inputs may be any that keep to these rules, and one draw needn't show every extreme that they name: `block_ids`: along a row block numbers never fall; every block holds 1 to 256 positions and some block holds exactly 256.
All inputs are finite; a program needn't handle non-finite values.
Results may differ from the reference program's by a relative error of at most 0.025.
Values may be sent and summed in bfloat16 or wider, within the bound.
A program may use at most 192 MiB of HBM per device.

```python
import math
import jax
import jax.numpy as jnp
import numpy as np
from jax import lax

D = 2048
HEADS = 16
HEAD = 128
FF = 8192
BLOCK = 256
STEP = 5
BATCH = 8
SEQ = 512
NBLK = 4
TOKENS = 4096


def draw_w_qkv(key, part):
    key = jax.random.fold_in(key, 7)
    base = jax.random.truncated_normal(key, -4.0, 4.0, (3, D, D), jnp.float32)
    head_number = (jnp.arange(D) // HEAD).astype(jnp.float32)
    rising = jnp.sqrt(0.5 + head_number / (HEADS - 1))
    column = jnp.stack([rising, rising, jnp.ones((D,), jnp.float32)])
    return base * column[:, None, :] * D ** (-0.5)


def draw_gains(key, part):
    key = jax.random.fold_in(key, 8)
    spread = jax.random.uniform(key, (4, D), jnp.float32)
    lower = jnp.array([1.2, 1.2, 0.7, 0.7], jnp.float32)[:, None]
    reach = jnp.array([0.4, 0.4, 0.6, 0.6], jnp.float32)[:, None]
    return lower + reach * spread


def shard_levels(stream_key, extent, cuts, low, top_value):
    def one(axis_at, parts):
        steps = jax.random.uniform(jax.random.fold_in(jax.random.fold_in(stream_key, 6), axis_at), (parts,), jnp.float32, low / len(cuts), top_value / len(cuts))
        return jnp.repeat(jnp.exp(steps), extent[axis_at] // parts).reshape((-1,) + (1,) * (len(extent) - axis_at - 1))

    gain = one(*cuts[0])
    for cut in cuts[1:]:
        gain = gain * one(*cut)
    return gain


def length_profile(amount, total, bound, slope):
    portions = [(1 << 20) // math.isqrt(rank ** slope) + 1 for rank in range(2, amount + 1)]
    surplus, counts = total - bound - (amount - 1), [1] * (amount - 1)
    while surplus > 0:
        candidates = [i for i in range(amount - 1) if counts[i] < bound]
        mass, left = sum([portions[i] for i in candidates]), surplus
        for i in candidates:
            addition = min(bound - counts[i], max(1, left * portions[i] // mass), surplus)
            counts[i] = counts[i] + addition
            surplus = surplus - addition
    return np.array([bound] + counts)


def uneven_parts(stream_key, amount, total, most, lean):
    if amount == 2:
        one = jax.random.randint(stream_key, (), max(1, total - most), min(most, total - 1) + 1)
        return jnp.stack([one, total - one])
    lengths = jnp.asarray(length_profile(amount, total, most, lean), jnp.int32)
    pairs = (amount - 1) // 2
    source_of, sink = lengths[1:1 + 2 * pairs:2], lengths[2:2 + 2 * pairs:2]
    margin = jnp.minimum(source_of - 1, most - sink)
    passed = jax.random.randint(jax.random.fold_in(stream_key, 1), (pairs,), 0, 1 << 20) % (margin + 1)
    lengths = lengths.at[1:1 + 2 * pairs:2].set(source_of - passed).at[2:2 + 2 * pairs:2].set(sink + passed)
    return lengths[jax.random.permutation(jax.random.fold_in(stream_key, 2), amount)]


def bell_draw(stream_key, shape, scale, most, cuts=(), held_as=jnp.bfloat16):
    values = scale * jax.random.normal(stream_key, shape, jnp.float32)
    if cuts:
        values = values * shard_levels(stream_key, shape, cuts, -0.22, 0.18)
    return jnp.clip(values, -most, most).astype(held_as)


def setup_inputs(seed: int = 0) -> dict:
    streams_of = jax.random.split(jax.random.key(seed), 19)
    return {
        "tokens": bell_draw(streams_of[0], (BATCH, SEQ, D), 1.0, 6.0, ((0, 8), (1, 4))),
        "cotangent": bell_draw(streams_of[1], (BATCH, SEQ, D), 1.0, 6.0, ((0, 8), (1, 4))),
        "block_ids": jax.vmap(lambda own: jnp.searchsorted(jnp.cumsum(uneven_parts(own, NBLK, SEQ, BLOCK, 0)), jnp.arange(SEQ), side="right"))(jax.random.split(streams_of[2], BATCH)).reshape((BATCH, SEQ)).astype(jnp.int32),
        "w_qkv": draw_w_qkv(jax.random.fold_in(streams_of[18], 71), 0),
        "m_qkv": bell_draw(streams_of[4], (3, D, D), (0.1 * TOKENS ** 0.5), 40.0, ((1, 8), (2, 4)), jnp.float32),
        "v_qkv": jnp.clip(jnp.exp(math.log(819.2) - 1.3862944 * jax.random.uniform(streams_of[5], (3, D, D), jnp.float32) ** shard_levels(streams_of[5], (3, D, D), ((1, 8), (2, 4)), -0.2, 0.2)), 204.8, 819.2),
        "w_out": bell_draw(streams_of[6], (D, D), D ** -0.5, 0.125, ((0, 4), (1, 8)), jnp.float32),
        "m_out": bell_draw(streams_of[7], (D, D), (0.1 * TOKENS ** 0.5), 40.0, ((0, 4), (1, 8)), jnp.float32),
        "v_out": jnp.clip(jnp.exp(math.log(819.2) - 1.3862944 * jax.random.uniform(streams_of[8], (D, D), jnp.float32) ** shard_levels(streams_of[8], (D, D), ((0, 4), (1, 8)), -0.2, 0.2)), 204.8, 819.2),
        "w_gu": bell_draw(streams_of[9], (2, D, FF), D ** -0.5, 0.125, ((1, 8), (2, 4)), jnp.float32),
        "m_gu": bell_draw(streams_of[10], (2, D, FF), (0.1 * TOKENS ** 0.5), 40.0, ((1, 8), (2, 4)), jnp.float32),
        "v_gu": jnp.clip(jnp.exp(math.log(819.2) - 1.3862944 * jax.random.uniform(streams_of[11], (2, D, FF), jnp.float32) ** shard_levels(streams_of[11], (2, D, FF), ((1, 8), (2, 4)), -0.2, 0.2)), 204.8, 819.2),
        "w_down": bell_draw(streams_of[12], (FF, D), FF ** -0.5, 0.0625, ((0, 4), (1, 8)), jnp.float32),
        "m_down": bell_draw(streams_of[13], (FF, D), (0.1 * TOKENS ** 0.5), 40.0, ((0, 4), (1, 8)), jnp.float32),
        "v_down": jnp.clip(jnp.exp(math.log(819.2) - 1.3862944 * jax.random.uniform(streams_of[14], (FF, D), jnp.float32) ** shard_levels(streams_of[14], (FF, D), ((0, 4), (1, 8)), -0.2, 0.2)), 204.8, 819.2),
        "gains": draw_gains(jax.random.fold_in(streams_of[18], 71), 0),
        "gain_m": bell_draw(streams_of[16], (4, D), (0.1 * TOKENS ** 0.5), 40.0, ((1, 8),), jnp.float32),
        "gain_v": jnp.clip(jnp.exp(math.log(819.2) - 1.3862944 * jax.random.uniform(streams_of[17], (4, D), jnp.float32) ** shard_levels(streams_of[17], (4, D), ((1, 8),), -0.2, 0.2)), 204.8, 819.2),
    }


@jax.custom_vjp
def low(v):
    return lax.optimization_barrier(v.astype(jnp.bfloat16)).astype(jnp.float32)

@jax.custom_vjp
def low_back(v):
    return v

def low_keep(v):
    return (low(v), None)

def low_pass(kept, grad):
    return (grad,)

def back_keep(v):
    return (v, None)

def back_low(kept, grad):
    return (low(grad),)
low.defvjp(low_keep, low_pass)
low_back.defvjp(back_keep, back_low)
norm_eps = 1e-06
rope_base = 500000.0
beta_one = 0.9
beta_two = 0.95
rate_matrix = 0.01
rate_gain = 0.6
weight_decay = 0.1
adam_eps = 1e-08
clip_tau = 9.0
masked_value = -1e+30
highest = lax.Precision.HIGHEST

def rms_scale(value):
    return value * lax.rsqrt(lax.optimization_barrier(jnp.mean(value * value, axis=-1, keepdims=True)) + norm_eps)

def rope_tables(length, size):
    half = size // 2
    freq = rope_base ** (-(jnp.arange(half, dtype=jnp.float32) * 2.0 / size))
    angle = jnp.arange(length, dtype=jnp.float32)[:, None] * freq[None, :]
    angle = jnp.concatenate([angle, angle], axis=1)
    return (jnp.cos(angle)[:, None, :], jnp.sin(angle)[:, None, :])

def rotate_fwd(value):
    half = value.shape[-1] // 2
    return jnp.concatenate([-value[..., half:], value[..., :half]], axis=-1)

def adam_step(param, grad, first, second, rate, decay):
    first = beta_one * first + (1.0 - beta_one) * grad
    second = beta_two * second + (1.0 - beta_two) * grad * grad
    fix_one = 1.0 - beta_one ** STEP
    fix_two = 1.0 - beta_two ** STEP
    update = first / fix_one / (jnp.sqrt(second / fix_two) + adam_eps)
    return (param - rate * (update + decay * param), first, second)

def layer(x_float, w_qkv, w_out, w_gu, w_down, gains, blocks):
    c_qkv = low(w_qkv)
    c_out = low(w_out)
    c_gu = low(w_gu)
    c_down = low(w_down)
    gain_rows = low(gains)
    projected = jnp.einsum('sd,cde->cse', x_float, c_qkv, precision=highest)
    queries = low_back(projected[0])
    keys = low_back(projected[1])
    values = low_back(projected[2])
    q_norm = rms_scale(queries) * gain_rows[0]
    k_norm = rms_scale(keys) * gain_rows[1]
    cosine, sine = rope_tables(SEQ, HEAD)

    def rotary(value):
        shaped = value.reshape(SEQ, HEADS, HEAD)
        return shaped * cosine + rotate_fwd(shaped) * sine
    q_low = low(rotary(q_norm))
    k_low = low(rotary(k_norm))
    v_low = low(values).reshape(SEQ, HEADS, HEAD)
    block_rows = min(512, SEQ)
    scale = HEAD ** (-0.5)

    def attend(start):
        q_part = lax.dynamic_slice_in_dim(q_low, start, block_rows, 0)
        b_part = lax.dynamic_slice_in_dim(blocks, start, block_rows, 0)
        raw = low_back(jnp.einsum('qhd,khd->hqk', q_part, k_low, precision=highest) * scale)
        allowed = blocks[None, None, :] <= b_part[None, :, None]
        masked = jnp.where(allowed, raw, masked_value)
        top = lax.optimization_barrier(jnp.max(masked, axis=2, keepdims=True))
        weight = jnp.exp(masked - top)
        probs = weight / lax.optimization_barrier(jnp.sum(weight, axis=2, keepdims=True))
        context = jnp.einsum('hqk,khd->qhd', low(probs), v_low, precision=highest)
        return (context, lax.optimization_barrier(jnp.max(top[:, :, 0], axis=1)))
    starts = jnp.arange(SEQ // block_rows).astype(jnp.int32) * block_rows
    context, block_top = lax.map(jax.checkpoint(attend), starts)
    context = low(low_back(context.reshape(SEQ, D)))
    attn_raw = low_back(jnp.dot(context, c_out, precision=highest, preferred_element_type=jnp.float32))
    resid = x_float + rms_scale(attn_raw) * gain_rows[2]
    resid_low = low(resid)
    gate_up = jnp.einsum('sd,cdf->csf', resid_low, c_gu, precision=highest)
    gate = low_back(gate_up[0])
    up = low_back(gate_up[1])
    act = low(jax.nn.silu(gate) * up)
    mlp_raw = low_back(jnp.dot(act, c_down, precision=highest, preferred_element_type=jnp.float32))
    result = resid + rms_scale(mlp_raw) * gain_rows[3]
    return (result, lax.optimization_barrier(jnp.max(block_top, axis=0)))

def reference(tokens, cotangent, block_ids, w_qkv, m_qkv, v_qkv, w_out, m_out, v_out, w_gu, m_gu, v_gu, w_down, m_down, v_down, gains, gain_m, gain_v):
    masters = (w_qkv, w_out, w_gu, w_down, gains)

    def per_sequence(carry, item):
        totals, best = carry
        x_seq, cot_seq, blocks = item

        def run(x_float, one, two, three, four, five):
            return layer(x_float, one, two, three, four, five, blocks)
        result, pull, top = jax.vjp(run, x_seq.astype(jnp.float32), w_qkv, w_out, w_gu, w_down, gains, has_aux=True)
        pulled = pull(cot_seq.astype(jnp.float32))
        totals = tuple((total + part for total, part in zip(totals, pulled[1:])))
        return ((totals, jnp.maximum(best, top)), (result.astype(jnp.bfloat16), pulled[0]))
    zeros = tuple((jnp.zeros_like(master) for master in masters))
    start_best = jnp.full((HEADS,), masked_value, dtype=jnp.float32)
    (grads, best), (output, grad_tokens) = lax.scan(per_sequence, (zeros, start_best), (tokens, cotangent, block_ids))
    factor = clip_tau / jnp.maximum(best, clip_tau)
    column = jnp.repeat(jnp.sqrt(factor), HEAD)
    new_qkv, new_m_qkv, new_v_qkv = adam_step(w_qkv, grads[0], m_qkv, v_qkv, rate_matrix, weight_decay)
    new_qkv = new_qkv * jnp.stack([column, column, jnp.ones_like(column)])[:, None, :]
    new_out, new_m_out, new_v_out = adam_step(w_out, grads[1], m_out, v_out, rate_matrix, weight_decay)
    new_gu, new_m_gu, new_v_gu = adam_step(w_gu, grads[2], m_gu, v_gu, rate_matrix, weight_decay)
    new_down, new_m_down, new_v_down = adam_step(w_down, grads[3], m_down, v_down, rate_matrix, weight_decay)
    new_gains, new_gain_m, new_gain_v = adam_step(gains, grads[4], gain_m, gain_v, rate_gain, 0.0)
    return (output, grad_tokens, new_qkv, new_m_qkv, new_v_qkv, new_qkv.astype(jnp.bfloat16), new_out, new_m_out, new_v_out, new_out.astype(jnp.bfloat16), new_gu, new_m_gu, new_v_gu, new_gu.astype(jnp.bfloat16), new_down, new_m_down, new_v_down, new_down.astype(jnp.bfloat16), new_gains, new_gain_m, new_gain_v, factor)
```

```python
import jax
import jax.numpy as jnp
from jax import lax
from jax.sharding import PartitionSpec as P

HEAD = 128
STEP = 5


norm_eps = 1e-06
rope_base = 500000.0
beta_one = 0.9
beta_two = 0.95
rate_matrix = 0.01
rate_gain = 0.6
weight_decay = 0.1
adam_eps = 1e-08
clip_tau = 9.0
masked_value = -1e30


def rope_tables(length, size):
    half = size // 2
    freq = rope_base ** (-(jnp.arange(half, dtype=jnp.float32) * 2.0 / size))
    angle = jnp.arange(length, dtype=jnp.float32)[:, None] * freq[None, :]
    angle = jnp.concatenate([angle, angle], axis=1)
    return (jnp.cos(angle)[:, None, :], jnp.sin(angle)[:, None, :])


def rotate_fwd(value):
    half = value.shape[-1] // 2
    return jnp.concatenate([-value[..., half:], value[..., :half]], axis=-1)


def rotate_back(value):
    half = value.shape[-1] // 2
    return jnp.concatenate([value[..., half:], -value[..., :half]], axis=-1)


def adam_step(param, grad, first, second, rate, decay):
    first = beta_one * first + (1.0 - beta_one) * grad
    second = beta_two * second + (1.0 - beta_two) * grad * grad
    fix_one = 1.0 - beta_one**STEP
    fix_two = 1.0 - beta_two**STEP
    update = first / fix_one / (jnp.sqrt(second / fix_two) + adam_eps)
    return (param - rate * (update + decay * param), first, second)


def norm_back(scale_factor, normed, upstream):
    inner = jnp.mean(upstream * normed, axis=1, keepdims=True)
    return scale_factor * (upstream - normed * inner)


def ring_order(count):
    inner = 1
    while inner * inner * 4 <= count:
        inner *= 2
    outer = count // inner
    path = []
    for row in range(inner):
        columns = range(outer) if row % 2 == 0 else range(outer - 1, -1, -1)
        path += [column * inner + row for column in columns]
    return path


def ring_pairs(count, step):
    path = ring_order(count)
    return [(path[i], path[(i + step) % count]) for i in range(count)]


def ring_place(count):
    path = ring_order(count)
    place = [0] * count
    for i, index in enumerate(path):
        place[index] = i
    return jnp.array(place, jnp.int32)[lax.axis_index("dp")], jnp.array(path, jnp.int32)


def ring_gather(shard, axis, split):
    count = lax.axis_size("dp")
    place, path = ring_place(count)
    wide = shard.shape[axis]
    shape = list(shard.shape)
    shape[axis] *= count
    half = shard.shape[split] // 2
    full = jnp.zeros(shape, shard.dtype)

    def put(full, part, place_of, side):
        start = [0] * len(shape)
        start[axis] = path[place_of % count] * wide
        if axis == split:
            start[axis] += side * half
        else:
            start[split] = side * half
        return lax.dynamic_update_slice(full, part, start)

    parts = [lax.slice_in_dim(shard, side * half, (side + 1) * half, axis=split) for side in (0, 1)]
    for side in (0, 1):
        full = put(full, parts[side], place, side)
    for step in range(1, count):
        for side, way in ((0, 1), (1, -1)):
            parts[side] = lax.ppermute(parts[side], "dp", ring_pairs(count, way))
            full = put(full, parts[side], place - way * step + count, side)
    return full


def ring_scatter(whole, axis, split):
    count = lax.axis_size("dp")
    place, path = ring_place(count)
    wide = whole.shape[axis] // count
    out = []
    for side, way in ((0, 1), (1, -1)):
        sizes = list(whole.shape)
        sizes[axis] = wide
        sizes[split] = sizes[split] // 2

        def take(place_of):
            start = [0] * len(sizes)
            start[axis] = path[place_of % count] * wide
            start[split] += side * sizes[split]
            return lax.dynamic_slice(whole, start, sizes)

        total = take(place - way + count)
        for step in range(1, count):
            total = lax.ppermute(total, "dp", ring_pairs(count, way))
            own = take(place - way * (step + 1) + 2 * count)
            total = total.astype(jnp.float32) + own.astype(jnp.float32)
            if step < count - 1:
                total = total.astype(whole.dtype)
        out.append(total)
    return jnp.concatenate(out, axis=split)


def local(
    tokens,
    cotangent,
    block_ids,
    w_qkv,
    m_qkv,
    v_qkv,
    w_out,
    m_out,
    v_out,
    w_gu,
    m_gu,
    v_gu,
    w_down,
    m_down,
    v_down,
    gains,
    gain_m,
    gain_v,
):
    low_qkv = w_qkv.astype(jnp.bfloat16)
    low_out = w_out.astype(jnp.bfloat16)
    low_gu = w_gu.astype(jnp.bfloat16)
    low_down = w_down.astype(jnp.bfloat16)
    low_gains = gains.astype(jnp.bfloat16)
    full_qkv, full_out, full_gu, full_down, full_gains = (
        ring_gather(low_qkv, 1, 2),
        ring_gather(low_out, 1, 0),
        ring_gather(low_gu, 1, 0),
        ring_gather(low_down, 1, 0),
        lax.all_gather(low_gains, "dp", axis=1, tiled=True),
    )
    gain_rows = full_gains.astype(jnp.float32)
    local_x = tokens[0]
    model_width = local_x.shape[1]
    seq_x = lax.all_gather(local_x, "tensor", axis=0, tiled=True)
    length = seq_x.shape[0]
    span = full_qkv.shape[2]
    heads_here = span // HEAD
    offset = lax.axis_index("tensor") * span
    projected = jnp.einsum("sd,cde->cse", seq_x, full_qkv, preferred_element_type=jnp.float32)
    queries, keys, values = (projected[0], projected[1], projected[2])
    q_square, k_square = lax.psum(
        (jnp.sum(queries * queries, axis=1), jnp.sum(keys * keys, axis=1)), "tensor"
    )
    q_scale = lax.rsqrt(q_square / model_width + norm_eps)[:, None]
    k_scale = lax.rsqrt(k_square / model_width + norm_eps)[:, None]
    q_hat = queries * q_scale
    k_hat = keys * k_scale
    q_gain = lax.dynamic_slice_in_dim(gain_rows[0], offset, span)
    k_gain = lax.dynamic_slice_in_dim(gain_rows[1], offset, span)
    cosine, sine = rope_tables(length, HEAD)

    def rotary(value):
        shaped = value.reshape(length, heads_here, HEAD)
        return shaped * cosine + rotate_fwd(shaped) * sine

    def unrotary(grad):
        return (grad * cosine + rotate_back(grad * sine)).reshape(length, span)

    q_low = rotary(q_hat * q_gain).astype(jnp.bfloat16)
    k_low = rotary(k_hat * k_gain).astype(jnp.bfloat16)
    v_low = values.astype(jnp.bfloat16).reshape(length, heads_here, HEAD)
    blocks = block_ids[0]
    block_rows = min(512, length)
    block_count = length // block_rows
    scale = HEAD ** (-0.5)
    starts = jnp.arange(block_count, dtype=jnp.int32) * block_rows

    def scores_of(start):
        q_part = lax.dynamic_slice_in_dim(q_low, start, block_rows, 0)
        b_part = lax.dynamic_slice_in_dim(blocks, start, block_rows, 0)
        raw = jnp.einsum("qhd,khd->hqk", q_part, k_low, preferred_element_type=jnp.float32) * scale
        allowed = blocks[None, None, :] <= b_part[None, :, None]
        return (jnp.where(allowed, raw, masked_value), q_part)

    def forward_block(start):
        masked, q_part = scores_of(start)
        top = jnp.max(masked, axis=2, keepdims=True)
        weight = jnp.exp(masked - top)
        total = jnp.sum(weight, axis=2, keepdims=True)
        probs = (weight / total).astype(jnp.bfloat16)
        context = jnp.einsum("hqk,khd->qhd", probs, v_low, preferred_element_type=jnp.float32)
        return (
            context.astype(jnp.bfloat16),
            (top + jnp.log(total))[:, :, 0],
            jnp.max(top[:, :, 0], axis=1),
        )

    context_low, log_total, block_top = lax.map(forward_block, starts)
    context_low = context_low.reshape(length, span)
    head_top = jnp.max(block_top, axis=0)
    attn_raw = lax.psum_scatter(
        jnp.dot(context_low, full_out, preferred_element_type=jnp.float32).astype(jnp.bfloat16),
        "tensor",
        scatter_dimension=0,
        tiled=True,
    ).astype(jnp.float32)
    x_float = local_x.astype(jnp.float32)
    o_scale = lax.rsqrt(jnp.mean(attn_raw * attn_raw, axis=1, keepdims=True) + norm_eps)
    attn_hat = attn_raw * o_scale
    resid = x_float + attn_hat * gain_rows[2]
    seq_h = lax.all_gather(resid.astype(jnp.bfloat16), "tensor", axis=0, tiled=True)
    gate_up = jnp.einsum("sd,cdf->csf", seq_h, full_gu, preferred_element_type=jnp.float32)
    gate, up = (gate_up[0], gate_up[1])
    sigma = jax.nn.sigmoid(gate)
    act = (gate * sigma * up).astype(jnp.bfloat16)
    mlp_raw = lax.psum_scatter(
        jnp.dot(act, full_down, preferred_element_type=jnp.float32).astype(jnp.bfloat16),
        "tensor",
        scatter_dimension=0,
        tiled=True,
    ).astype(jnp.float32)
    m_scale = lax.rsqrt(jnp.mean(mlp_raw * mlp_raw, axis=1, keepdims=True) + norm_eps)
    mlp_hat = mlp_raw * m_scale
    output = (resid + mlp_hat * gain_rows[3]).astype(jnp.bfloat16)[None]
    grad_top = cotangent[0].astype(jnp.float32)
    gain_last = jnp.sum(grad_top * mlp_hat, axis=0)
    d_mlp = norm_back(m_scale, mlp_hat, grad_top * gain_rows[3]).astype(jnp.bfloat16)
    seq_dm = lax.all_gather(d_mlp, "tensor", axis=0, tiled=True)
    back_qkv, back_out, back_gu, back_down = (full_qkv, full_out, full_gu, full_down)
    grad_down = jnp.einsum("sf,sd->fd", act, seq_dm, preferred_element_type=jnp.float32)
    d_act = jnp.einsum("sd,fd->sf", seq_dm, back_down, preferred_element_type=jnp.float32)
    d_gate = d_act * up * sigma * (1.0 + gate * (1.0 - sigma))
    d_up = d_act * gate * sigma
    d_gu = jnp.stack([d_gate, d_up]).astype(jnp.bfloat16)
    grad_gu = jnp.einsum("sd,csf->cdf", seq_h, d_gu, preferred_element_type=jnp.float32)
    d_resid = grad_top + lax.psum_scatter(
        jnp.einsum("csf,cdf->sd", d_gu, back_gu, preferred_element_type=jnp.float32).astype(jnp.bfloat16),
        "tensor",
        scatter_dimension=0,
        tiled=True,
    ).astype(jnp.float32)
    gain_attn = jnp.sum(d_resid * attn_hat, axis=0)
    d_attn = norm_back(o_scale, attn_hat, d_resid * gain_rows[2]).astype(jnp.bfloat16)
    seq_do = lax.all_gather(d_attn, "tensor", axis=0, tiled=True)
    grad_out = jnp.einsum("se,sd->ed", context_low, seq_do, preferred_element_type=jnp.float32)
    d_context = jnp.einsum("sd,ed->se", seq_do, back_out, preferred_element_type=jnp.float32)
    d_context = d_context.astype(jnp.bfloat16).reshape(length, heads_here, HEAD)

    def backward_block(carry, item):
        key_acc, value_acc = carry
        start, log_part = item
        masked, q_part = scores_of(start)
        probs = jnp.exp(masked - log_part[:, :, None])
        dc_part = lax.dynamic_slice_in_dim(d_context, start, block_rows, 0)
        d_probs = jnp.einsum("qhd,khd->hqk", dc_part, v_low, preferred_element_type=jnp.float32)
        inner = jnp.sum(probs * d_probs, axis=2, keepdims=True)
        d_scores = (probs * (d_probs - inner)).astype(jnp.bfloat16)
        d_query = (
            jnp.einsum("hqk,khd->qhd", d_scores, k_low, preferred_element_type=jnp.float32) * scale
        )
        key_acc = (
            key_acc
            + jnp.einsum("hqk,qhd->khd", d_scores, q_part, preferred_element_type=jnp.float32)
            * scale
        )
        value_acc = value_acc + jnp.einsum(
            "hqk,qhd->khd", probs.astype(jnp.bfloat16), dc_part, preferred_element_type=jnp.float32
        )
        return ((key_acc, value_acc), d_query)

    empty = jnp.zeros((length, heads_here, HEAD), jnp.float32)
    (d_krot, d_values), d_qrot = lax.scan(backward_block, (empty, empty), (starts, log_total))
    d_qrot = d_qrot.reshape(length, heads_here, HEAD)
    d_qnorm = unrotary(d_qrot)
    d_knorm = unrotary(d_krot)
    head_gains = jnp.stack([jnp.sum(d_qnorm * q_hat, axis=0), jnp.sum(d_knorm * k_hat, axis=0)])
    placed = lax.dynamic_update_slice(
        jnp.zeros((2, model_width), jnp.float32), head_gains, (0, offset)
    )
    gain_terms = jnp.concatenate([placed, jnp.stack([gain_attn, gain_last])], axis=0)
    dq_hat = d_qnorm * q_gain
    dk_hat = d_knorm * k_gain
    q_inner, k_inner, gain_total = (
        lax.psum(jnp.sum(dq_hat * q_hat, axis=1).astype(jnp.bfloat16), "tensor").astype(
            jnp.float32
        ),
        lax.psum(jnp.sum(dk_hat * k_hat, axis=1).astype(jnp.bfloat16), "tensor").astype(
            jnp.float32
        ),
        lax.psum(gain_terms.astype(jnp.bfloat16), "tensor").astype(jnp.float32),
    )
    d_query = q_scale * (dq_hat - q_hat * (q_inner / model_width)[:, None])
    d_key = k_scale * (dk_hat - k_hat * (k_inner / model_width)[:, None])
    d_qkv = jnp.stack([d_query, d_key, d_values.reshape(length, span)]).astype(jnp.bfloat16)
    grad_qkv = jnp.einsum("sd,cse->cde", seq_x, d_qkv, preferred_element_type=jnp.float32)
    grad_tokens = d_resid + lax.psum_scatter(
        jnp.einsum("cse,cde->sd", d_qkv, back_qkv, preferred_element_type=jnp.float32).astype(
            jnp.bfloat16
        ),
        "tensor",
        scatter_dimension=0,
        tiled=True,
    ).astype(jnp.float32)
    part_qkv, part_out, part_gu, part_down, part_gains = (
        ring_scatter(grad_qkv.astype(jnp.bfloat16), 1, 2),
        ring_scatter(grad_out.astype(jnp.bfloat16), 1, 0),
        ring_scatter(grad_gu.astype(jnp.bfloat16), 1, 0),
        ring_scatter(grad_down.astype(jnp.bfloat16), 1, 0),
        lax.psum_scatter(
            gain_total.astype(jnp.bfloat16), "dp", scatter_dimension=1, tiled=True
        ).astype(jnp.float32),
    )
    head_top = lax.pmax(head_top, "dp")
    factor = clip_tau / jnp.maximum(head_top, clip_tau)
    column = jnp.repeat(jnp.sqrt(factor), HEAD)
    new_qkv, new_m_qkv, new_v_qkv = adam_step(
        w_qkv, part_qkv, m_qkv, v_qkv, rate_matrix, weight_decay
    )
    new_qkv = new_qkv * jnp.stack([column, column, jnp.ones_like(column)])[:, None, :]
    new_out, new_m_out, new_v_out = adam_step(
        w_out, part_out, m_out, v_out, rate_matrix, weight_decay
    )
    new_gu, new_m_gu, new_v_gu = adam_step(w_gu, part_gu, m_gu, v_gu, rate_matrix, weight_decay)
    new_down, new_m_down, new_v_down = adam_step(
        w_down, part_down, m_down, v_down, rate_matrix, weight_decay
    )
    new_gains, new_gain_m, new_gain_v = adam_step(gains, part_gains, gain_m, gain_v, rate_gain, 0.0)
    return (
        output,
        grad_tokens[None],
        new_qkv,
        new_m_qkv,
        new_v_qkv,
        new_qkv.astype(jnp.bfloat16),
        new_out,
        new_m_out,
        new_v_out,
        new_out.astype(jnp.bfloat16),
        new_gu,
        new_m_gu,
        new_v_gu,
        new_gu.astype(jnp.bfloat16),
        new_down,
        new_m_down,
        new_v_down,
        new_down.astype(jnp.bfloat16),
        new_gains,
        new_gain_m,
        new_gain_v,
        factor,
    )


def solution(mesh):
    return jax.shard_map(
        local,
        mesh=mesh,
        in_specs=(
            P("dp", "tensor", None),
            P("dp", "tensor", None),
            P("dp", None),
            P(None, "dp", "tensor"),
            P(None, "dp", "tensor"),
            P(None, "dp", "tensor"),
            P("tensor", "dp"),
            P("tensor", "dp"),
            P("tensor", "dp"),
            P(None, "dp", "tensor"),
            P(None, "dp", "tensor"),
            P(None, "dp", "tensor"),
            P("tensor", "dp"),
            P("tensor", "dp"),
            P("tensor", "dp"),
            P(None, "dp"),
            P(None, "dp"),
            P(None, "dp"),
        ),
        out_specs=(
            P("dp", "tensor", None),
            P("dp", "tensor", None),
            P(None, "dp", "tensor"),
            P(None, "dp", "tensor"),
            P(None, "dp", "tensor"),
            P(None, "dp", "tensor"),
            P("tensor", "dp"),
            P("tensor", "dp"),
            P("tensor", "dp"),
            P("tensor", "dp"),
            P(None, "dp", "tensor"),
            P(None, "dp", "tensor"),
            P(None, "dp", "tensor"),
            P(None, "dp", "tensor"),
            P("tensor", "dp"),
            P("tensor", "dp"),
            P("tensor", "dp"),
            P("tensor", "dp"),
            P(None, "dp"),
            P(None, "dp"),
            P(None, "dp"),
            P("tensor"),
        ),
        check_vma=False,
    )
```

```python
import jax
import jax.numpy as jnp
from jax import lax
from jax.experimental import pallas as pl
from jax.experimental.pallas import tpu as pltpu
from jax.sharding import PartitionSpec as P

HEAD = 128
STEP = 5


norm_eps = 1e-06
rope_base = 500000.0
beta_one = 0.9
beta_two = 0.95
rate_matrix = 0.01
rate_gain = 0.6
weight_decay = 0.1
adam_eps = 1e-08
clip_tau = 9.0
masked_value = -1e30


def rope_tables(length, size):
    half = size // 2
    freq = rope_base ** (-(jnp.arange(half, dtype=jnp.float32) * 2.0 / size))
    angle = jnp.arange(length, dtype=jnp.float32)[:, None] * freq[None, :]
    angle = jnp.concatenate([angle, angle], axis=1)
    return (jnp.cos(angle)[:, None, :], jnp.sin(angle)[:, None, :])


def rotate_fwd(value):
    half = value.shape[-1] // 2
    return jnp.concatenate([-value[..., half:], value[..., :half]], axis=-1)


def rotate_back(value):
    half = value.shape[-1] // 2
    return jnp.concatenate([value[..., half:], -value[..., :half]], axis=-1)


def adam_step(param, grad, first, second, rate, decay):
    first = beta_one * first + (1.0 - beta_one) * grad
    second = beta_two * second + (1.0 - beta_two) * grad * grad
    fix_one = 1.0 - beta_one**STEP
    fix_two = 1.0 - beta_two**STEP
    update = first / fix_one / (jnp.sqrt(second / fix_two) + adam_eps)
    return (param - rate * (update + decay * param), first, second)


def norm_back(scale_factor, normed, upstream):
    inner = jnp.mean(upstream * normed, axis=1, keepdims=True)
    return scale_factor * (upstream - normed * inner)


class Grid:
    def __init__(self):
        self.dp = lax.axis_size("dp")
        self.tensor = lax.axis_size("tensor")
        self.inner = 1
        while self.inner * self.inner * 4 <= self.dp:
            self.inner *= 2
        self.outer = self.dp // self.inner
        self.chips = self.tensor // 2
        self.dp_at = lax.axis_index("dp")
        self.tensor_at = lax.axis_index("tensor")
        self.outer_at = self.dp_at // self.inner
        self.inner_at = self.dp_at % self.inner
        self.chip_at = self.tensor_at // 2
        self.core_at = self.tensor_at % 2
        path = []
        for row in range(self.inner):
            columns = range(self.outer) if row % 2 == 0 else range(self.outer - 1, -1, -1)
            path += [column * self.inner + row for column in columns]
        place = [0] * self.dp
        for at, index in enumerate(path):
            place[index] = at
        self.path = path
        self.path_table = jnp.array(path, jnp.int32)
        self.path_at = jnp.array(place, jnp.int32)[self.dp_at]

    def to_outer(self, value, step):
        n, m = self.outer, self.inner
        pairs = [(a * m + b, (a + step) % n * m + b) for a in range(n) for b in range(m)]
        return lax.ppermute(value, "dp", pairs)

    def to_inner(self, value, step):
        n, m = self.outer, self.inner
        pairs = [(a * m + b, a * m + (b + step) % m) for a in range(n) for b in range(m)]
        return lax.ppermute(value, "dp", pairs)

    def to_chip(self, value, step):
        n = self.chips
        pairs = [(a * 2 + b, (a + step) % n * 2 + b) for a in range(n) for b in range(2)]
        return lax.ppermute(value, "tensor", pairs)

    def to_core(self, value):
        pairs = [(a * 2 + b, a * 2 + 1 - b) for a in range(self.chips) for b in range(2)]
        return lax.ppermute(value, "tensor", pairs)

    def along_path(self, value, step):
        n = self.dp
        pairs = [(self.path[i], self.path[(i + step) % n]) for i in range(n)]
        return lax.ppermute(value, "dp", pairs)

    def across(self, value, axis, bit):
        count = lax.axis_size(axis)
        return lax.ppermute(value, axis, [(i, i ^ bit) for i in range(count)])


def bits(count):
    return [1 << k for k in range(count.bit_length() - 1)]


def part(value, axis, index, size):
    return lax.dynamic_slice_in_dim(value, index * size, size, axis)


def put(whole, piece, axis, index):
    return lax.dynamic_update_slice_in_dim(whole, piece, index * piece.shape[axis], axis)


def low_sum(*terms):
    total = terms[0].astype(jnp.float32)
    for term in terms[1:]:
        total = total + term.astype(jnp.float32)
    return total.astype(jnp.bfloat16)


def path_gather(grid, shard, axis, split):
    n = grid.dp
    wide = shard.shape[axis]
    shape = list(shard.shape)
    shape[axis] *= n
    half = shard.shape[split] // 2
    full = jnp.zeros(shape, shard.dtype)

    def place(full, piece, at, side):
        start = [0] * len(shape)
        start[axis] = grid.path_table[at % n] * wide
        start[split] = start[split] + side * half
        return lax.dynamic_update_slice(full, piece, start)

    pieces = [lax.slice_in_dim(shard, k * half, (k + 1) * half, axis=split) for k in (0, 1)]
    for side in (0, 1):
        full = place(full, pieces[side], grid.path_at, side)
    for step in range(1, n):
        for side, way in ((0, 1), (1, -1)):
            pieces[side] = grid.along_path(pieces[side], way)
            full = place(full, pieces[side], grid.path_at - way * step + n, side)
    return full


def path_scatter(grid, whole, axis, split):
    n = grid.dp
    wide = whole.shape[axis] // n
    out = []
    for side, way in ((0, 1), (1, -1)):
        sizes = list(whole.shape)
        sizes[axis] = wide
        sizes[split] = sizes[split] // 2

        def take(at):
            start = [0] * len(sizes)
            start[axis] = grid.path_table[at % n] * wide
            start[split] += side * sizes[split]
            return lax.dynamic_slice(whole, start, sizes)

        total = take(grid.path_at - way + n)
        for step in range(1, n):
            total = grid.along_path(total, way)
            own = take(grid.path_at - way * (step + 1) + 2 * n)
            total = total.astype(jnp.float32) + own.astype(jnp.float32)
            if step < n - 1:
                total = total.astype(whole.dtype)
        out.append(total)
    return jnp.concatenate(out, axis=split)


def unit_gather(grid, shard, width_axis):
    unit_axis = 1 - width_axis
    n, m = grid.outer, grid.inner
    wide = shard.shape[width_axis]
    units = shard.shape[unit_axis] // n
    shape = [0, 0]
    shape[unit_axis] = units
    shape[width_axis] = wide * n
    held = jnp.zeros(shape, shard.dtype)
    for step in range(n):
        piece = part(shard, unit_axis, (grid.outer_at + step) % n, units)
        if step:
            piece = grid.to_outer(piece, step)
        held = put(held, piece, width_axis, (grid.outer_at - step) % n)
    shape[width_axis] = wide * n * m
    full = jnp.zeros(shape, shard.dtype)
    for step in range(m):
        if step:
            held = grid.to_inner(held, 1)
        inner = (grid.inner_at - step) % m
        for k in range(n):
            slab = lax.slice_in_dim(held, k * wide, (k + 1) * wide, axis=width_axis)
            full = put(full, slab, width_axis, k * m + inner)
    blocks = [full]
    for step in range(1, grid.chips):
        blocks.append(grid.to_chip(full, step))
    return jnp.concatenate(blocks, axis=unit_axis)


def unit_scatter(grid, whole, width_axis):
    unit_axis = 1 - width_axis
    n, m = grid.outer, grid.inner
    units = whole.shape[unit_axis] // grid.chips
    blocks = [
        lax.slice_in_dim(whole, k * units, (k + 1) * units, axis=unit_axis)
        for k in range(grid.chips)
    ]
    total = low_sum(
        blocks[0], *[grid.to_chip(blocks[k], -k) for k in range(1, grid.chips)]
    )
    wide = total.shape[width_axis] // (n * m)

    def slabs(inner):
        return jnp.concatenate(
            [part(total, width_axis, k * m + inner, wide) for k in range(n)], axis=width_axis
        )

    total = low_sum(
        slabs(grid.inner_at),
        *[grid.to_inner(slabs((grid.inner_at + k) % m), k) for k in range(1, m)],
    )
    shape = [0, 0]
    shape[unit_axis] = units * n
    shape[width_axis] = wide
    shard = jnp.zeros(shape, whole.dtype)
    for step in range(n):
        piece = part(total, width_axis, (grid.outer_at + step) % n, wide)
        if step:
            piece = grid.to_outer(piece, step)
        shard = put(shard, piece, unit_axis, (grid.outer_at - step) % n)
    return shard


def group_gather(grid, rows):
    blocks = []
    for step in range(grid.outer):
        here = grid.to_outer(rows, step) if step else rows
        blocks.append(jnp.concatenate([here, grid.to_core(here)], axis=0))
    return blocks


def group_return(grid, block, step):
    rows = block.shape[0] // 2
    mine = block[:rows] + grid.to_core(block[rows:].astype(jnp.bfloat16)).astype(jnp.float32)
    if step == 0:
        return mine
    return grid.to_outer(mine.astype(jnp.bfloat16), -step).astype(jnp.float32)


def sequence_scatter(grid, whole):
    rows = whole.shape[0] // grid.tensor
    shaped = whole.reshape(grid.chips, 2, rows, whole.shape[1])
    other = part(shaped, 1, 1 - grid.core_at, 1)[:, 0].astype(jnp.bfloat16)
    own = part(shaped, 1, grid.core_at, 1)[:, 0]
    pair = own + grid.to_core(other).astype(jnp.float32)
    total = part(pair, 0, grid.chip_at, 1)[0]
    for step in range(1, grid.chips):
        away = part(pair, 0, (grid.chip_at + step) % grid.chips, 1)[0].astype(jnp.bfloat16)
        total = total + grid.to_chip(away, step).astype(jnp.float32)
    return total


def sequence_gather(grid, rows):
    count, width = rows.shape
    whole = jnp.zeros((grid.chips, 2, count, width), rows.dtype)
    for step in range(grid.chips):
        here = grid.to_chip(rows, step) if step else rows
        chip = (grid.chip_at - step) % grid.chips
        for value, core in ((here, grid.core_at), (grid.to_core(here), 1 - grid.core_at)):
            whole = lax.dynamic_update_slice(whole, value[None, None], (chip, core, 0, 0))
    return whole.reshape(grid.tensor * count, width)


def gains_gather(grid, shard):
    held = shard[None]
    for bit in bits(grid.dp):
        other = grid.across(held, "dp", bit)
        low_side = (grid.dp_at // bit) % 2 == 0
        held = jnp.where(
            low_side, jnp.concatenate([held, other]), jnp.concatenate([other, held])
        )
    return jnp.swapaxes(held, 0, 1).reshape(shard.shape[0], -1)


def gains_scatter(grid, whole):
    rows = whole.shape[0]
    held = jnp.swapaxes(whole.reshape(rows, grid.dp, -1), 0, 1)
    for bit in reversed(bits(grid.dp)):
        low_side = (grid.dp_at // bit) % 2 == 0
        keep = jnp.where(low_side, held[:bit], held[bit:])
        give = jnp.where(low_side, held[bit:], held[:bit])
        held = keep + grid.across(give, "dp", bit)
    held = held[0]
    for bit in bits(grid.tensor):
        held = held + grid.across(held, "tensor", bit)
    return held


def adam_kernel(w_ref, m_ref, v_ref, g_ref, *rest):
    scale_ref = rest[0] if len(rest) == 5 else None
    w_out, m_out, v_out, c_out = rest[-4:]
    grad = g_ref[...].astype(jnp.float32)
    new, first, second = adam_step(
        w_ref[...], grad, m_ref[...], v_ref[...], rate_matrix, weight_decay
    )
    if scale_ref is not None:
        new = new * scale_ref[...]
    w_out[...] = new
    m_out[...] = first
    v_out[...] = second
    c_out[...] = new.astype(jnp.bfloat16)


def adam_call(param, grad, first, second, scale=None):
    shape = param.shape
    flat = [v.reshape(-1, shape[-1]) for v in (param, first, second, grad)]
    rows, width = flat[0].shape
    block = min(rows, max(16, (1 << 17) // width))
    spec = pl.BlockSpec((block, width), lambda k: (k, 0))
    specs = [spec] * 4
    if scale is not None:
        per = shape[1] // block
        flat.append(scale)
        specs.append(pl.BlockSpec((None, 1, width), lambda k: (k // per, 0, 0)))
    outs = [jax.ShapeDtypeStruct((rows, width), jnp.float32)] * 3
    outs.append(jax.ShapeDtypeStruct((rows, width), jnp.bfloat16))
    size = rows * width
    result = pl.pallas_call(
        adam_kernel,
        grid=(rows // block,),
        in_specs=specs,
        out_specs=[spec] * 4,
        out_shape=outs,
        cost_estimate=pl.CostEstimate(
            flops=20 * size, bytes_accessed=28 * size, transcendentals=2 * size
        ),
        compiler_params=pltpu.CompilerParams(vmem_limit_bytes=32 * 2**20),
    )(*flat)
    return [v.reshape(shape) for v in result]


def local(
    tokens,
    cotangent,
    block_ids,
    w_qkv,
    m_qkv,
    v_qkv,
    w_out,
    m_out,
    v_out,
    w_gu,
    m_gu,
    v_gu,
    w_down,
    m_down,
    v_down,
    gains,
    gain_m,
    gain_v,
):
    grid = Grid()
    low_gains = gains.astype(jnp.bfloat16)
    full_qkv = path_gather(grid, w_qkv.astype(jnp.bfloat16), 1, 2)
    gain_rows = gains_gather(grid, low_gains).astype(jnp.float32)
    full_out = path_gather(grid, w_out.astype(jnp.bfloat16), 1, 0)
    unit_gate = unit_gather(grid, w_gu[0].astype(jnp.bfloat16), 0)
    unit_up = unit_gather(grid, w_gu[1].astype(jnp.bfloat16), 0)
    unit_down = unit_gather(grid, w_down.astype(jnp.bfloat16), 1)
    local_x = tokens[0]
    model_width = local_x.shape[1]
    seq_x = sequence_gather(grid, local_x)
    length = seq_x.shape[0]
    span = full_qkv.shape[2]
    heads_here = span // HEAD
    offset = lax.axis_index("tensor") * span
    projected = jnp.einsum("sd,cde->cse", seq_x, full_qkv, preferred_element_type=jnp.float32)
    queries, keys, values = (projected[0], projected[1], projected[2])
    q_square, k_square = lax.psum(
        (jnp.sum(queries * queries, axis=1), jnp.sum(keys * keys, axis=1)), "tensor"
    )
    q_scale = lax.rsqrt(q_square / model_width + norm_eps)[:, None]
    k_scale = lax.rsqrt(k_square / model_width + norm_eps)[:, None]
    q_hat = queries * q_scale
    k_hat = keys * k_scale
    q_gain = lax.dynamic_slice_in_dim(gain_rows[0], offset, span)
    k_gain = lax.dynamic_slice_in_dim(gain_rows[1], offset, span)
    cosine, sine = rope_tables(length, HEAD)

    def rotary(value):
        shaped = value.reshape(length, heads_here, HEAD)
        return shaped * cosine + rotate_fwd(shaped) * sine

    def unrotary(grad):
        return (grad * cosine + rotate_back(grad * sine)).reshape(length, span)

    q_low = rotary(q_hat * q_gain).astype(jnp.bfloat16)
    k_low = rotary(k_hat * k_gain).astype(jnp.bfloat16)
    v_low = values.astype(jnp.bfloat16).reshape(length, heads_here, HEAD)
    blocks = block_ids[0]
    block_rows = min(512, length)
    block_count = length // block_rows
    scale = HEAD ** (-0.5)
    starts = jnp.arange(block_count, dtype=jnp.int32) * block_rows

    def scores_of(start):
        q_part = lax.dynamic_slice_in_dim(q_low, start, block_rows, 0)
        b_part = lax.dynamic_slice_in_dim(blocks, start, block_rows, 0)
        raw = jnp.einsum("qhd,khd->hqk", q_part, k_low, preferred_element_type=jnp.float32) * scale
        allowed = blocks[None, None, :] <= b_part[None, :, None]
        return (jnp.where(allowed, raw, masked_value), q_part)

    def forward_block(start):
        masked, q_part = scores_of(start)
        top = jnp.max(masked, axis=2, keepdims=True)
        weight = jnp.exp(masked - top)
        total = jnp.sum(weight, axis=2, keepdims=True)
        probs = (weight / total).astype(jnp.bfloat16)
        context = jnp.einsum("hqk,khd->qhd", probs, v_low, preferred_element_type=jnp.float32)
        return (
            context.astype(jnp.bfloat16),
            (top + jnp.log(total))[:, :, 0],
            jnp.max(top[:, :, 0], axis=1),
        )

    context_low, log_total, block_top = lax.map(forward_block, starts)
    context_low = context_low.reshape(length, span)
    head_top = jnp.max(block_top, axis=0)
    attn_raw = sequence_scatter(
        grid, jnp.dot(context_low, full_out, preferred_element_type=jnp.float32)
    )
    x_float = local_x.astype(jnp.float32)
    o_scale = lax.rsqrt(jnp.mean(attn_raw * attn_raw, axis=1, keepdims=True) + norm_eps)
    attn_hat = attn_raw * o_scale
    resid = x_float + attn_hat * gain_rows[2]
    blocks_h = group_gather(grid, resid.astype(jnp.bfloat16))
    kept = []
    mlp_raw = jnp.zeros_like(resid)
    for step, rows in enumerate(blocks_h):
        gate = jnp.dot(rows, unit_gate, preferred_element_type=jnp.float32)
        up = jnp.dot(rows, unit_up, preferred_element_type=jnp.float32)
        act = (gate * jax.nn.sigmoid(gate) * up).astype(jnp.bfloat16)
        kept.append((gate, up, act))
        partial = jnp.dot(act, unit_down, preferred_element_type=jnp.float32)
        mlp_raw = mlp_raw + group_return(grid, partial, step)
    m_scale = lax.rsqrt(jnp.mean(mlp_raw * mlp_raw, axis=1, keepdims=True) + norm_eps)
    mlp_hat = mlp_raw * m_scale
    output = (resid + mlp_hat * gain_rows[3]).astype(jnp.bfloat16)[None]
    grad_top = cotangent[0].astype(jnp.float32)
    gain_last = jnp.sum(grad_top * mlp_hat, axis=0)
    d_mlp = norm_back(m_scale, mlp_hat, grad_top * gain_rows[3]).astype(jnp.bfloat16)
    blocks_dm = group_gather(grid, d_mlp)
    d_resid = grad_top
    d_gates, d_ups = [], []
    for step, rows in enumerate(blocks_dm):
        gate, up, act = kept[step]
        sigma = jax.nn.sigmoid(gate)
        d_act = lax.dot_general(
            rows, unit_down, (((1,), (1,)), ((), ())), preferred_element_type=jnp.float32
        )
        d_gate = (d_act * up * sigma * (1.0 + gate * (1.0 - sigma))).astype(jnp.bfloat16)
        d_up = (d_act * gate * sigma).astype(jnp.bfloat16)
        d_gates.append(d_gate)
        d_ups.append(d_up)
        partial = lax.dot_general(
            d_gate, unit_gate, (((1,), (1,)), ((), ())), preferred_element_type=jnp.float32
        ) + lax.dot_general(
            d_up, unit_up, (((1,), (1,)), ((), ())), preferred_element_type=jnp.float32
        )
        d_resid = d_resid + group_return(grid, partial, step)
    all_h = jnp.concatenate(blocks_h, axis=0)

    def weight_grad(left, right):
        return lax.dot_general(
            left, right, (((0,), (0,)), ((), ())), preferred_element_type=jnp.float32
        ).astype(jnp.bfloat16)

    part_down = unit_scatter(
        grid,
        weight_grad(
            jnp.concatenate([item[2] for item in kept], axis=0),
            jnp.concatenate(blocks_dm, axis=0),
        ),
        1,
    )
    part_gate = unit_scatter(grid, weight_grad(all_h, jnp.concatenate(d_gates, axis=0)), 0)
    part_up = unit_scatter(grid, weight_grad(all_h, jnp.concatenate(d_ups, axis=0)), 0)
    gain_attn = jnp.sum(d_resid * attn_hat, axis=0)
    d_attn = norm_back(o_scale, attn_hat, d_resid * gain_rows[2]).astype(jnp.bfloat16)
    seq_do = sequence_gather(grid, d_attn)
    grad_out = jnp.einsum("se,sd->ed", context_low, seq_do, preferred_element_type=jnp.float32)
    part_out = path_scatter(grid, grad_out.astype(jnp.bfloat16), 1, 0)
    d_context = jnp.einsum("sd,ed->se", seq_do, full_out, preferred_element_type=jnp.float32)
    d_context = d_context.astype(jnp.bfloat16).reshape(length, heads_here, HEAD)

    def backward_block(carry, item):
        key_acc, value_acc = carry
        start, log_part = item
        masked, q_part = scores_of(start)
        probs = jnp.exp(masked - log_part[:, :, None])
        dc_part = lax.dynamic_slice_in_dim(d_context, start, block_rows, 0)
        d_probs = jnp.einsum("qhd,khd->hqk", dc_part, v_low, preferred_element_type=jnp.float32)
        inner = jnp.sum(probs * d_probs, axis=2, keepdims=True)
        d_scores = (probs * (d_probs - inner)).astype(jnp.bfloat16)
        d_query = (
            jnp.einsum("hqk,khd->qhd", d_scores, k_low, preferred_element_type=jnp.float32) * scale
        )
        key_acc = (
            key_acc
            + jnp.einsum("hqk,qhd->khd", d_scores, q_part, preferred_element_type=jnp.float32)
            * scale
        )
        value_acc = value_acc + jnp.einsum(
            "hqk,qhd->khd", probs.astype(jnp.bfloat16), dc_part, preferred_element_type=jnp.float32
        )
        return ((key_acc, value_acc), d_query)

    empty = jnp.zeros((length, heads_here, HEAD), jnp.float32)
    (d_krot, d_values), d_qrot = lax.scan(backward_block, (empty, empty), (starts, log_total))
    d_qrot = d_qrot.reshape(length, heads_here, HEAD)
    d_qnorm = unrotary(d_qrot)
    d_knorm = unrotary(d_krot)
    head_gains = jnp.stack([jnp.sum(d_qnorm * q_hat, axis=0), jnp.sum(d_knorm * k_hat, axis=0)])
    placed = lax.dynamic_update_slice(
        jnp.zeros((2, model_width), jnp.float32), head_gains, (0, offset)
    )
    gain_terms = jnp.concatenate([placed, jnp.stack([gain_attn, gain_last])], axis=0)
    dq_hat = d_qnorm * q_gain
    dk_hat = d_knorm * k_gain
    q_inner, k_inner = lax.psum(
        (jnp.sum(dq_hat * q_hat, axis=1), jnp.sum(dk_hat * k_hat, axis=1)), "tensor"
    )
    part_gains = gains_scatter(grid, gain_terms)
    d_query = q_scale * (dq_hat - q_hat * (q_inner / model_width)[:, None])
    d_key = k_scale * (dk_hat - k_hat * (k_inner / model_width)[:, None])
    d_qkv = jnp.stack([d_query, d_key, d_values.reshape(length, span)]).astype(jnp.bfloat16)
    grad_qkv = jnp.einsum("sd,cse->cde", seq_x, d_qkv, preferred_element_type=jnp.float32)
    part_qkv = path_scatter(grid, grad_qkv.astype(jnp.bfloat16), 1, 2)
    grad_tokens = d_resid + sequence_scatter(
        grid, jnp.einsum("cse,cde->sd", d_qkv, full_qkv, preferred_element_type=jnp.float32)
    )
    for bit in bits(grid.dp):
        head_top = jnp.maximum(head_top, grid.across(head_top, "dp", bit))
    factor = clip_tau / jnp.maximum(head_top, clip_tau)
    column = jnp.repeat(jnp.sqrt(factor), HEAD)
    column_scale = jnp.stack([column, column, jnp.ones_like(column)])[:, None, :]
    new_qkv, new_m_qkv, new_v_qkv, copy_qkv = adam_call(
        w_qkv, part_qkv, m_qkv, v_qkv, column_scale
    )
    new_out, new_m_out, new_v_out, copy_out = adam_call(w_out, part_out, m_out, v_out)
    new_gu, new_m_gu, new_v_gu, copy_gu = adam_call(
        w_gu, jnp.stack([part_gate, part_up]), m_gu, v_gu
    )
    new_down, new_m_down, new_v_down, copy_down = adam_call(w_down, part_down, m_down, v_down)
    new_gains, new_gain_m, new_gain_v = adam_step(gains, part_gains, gain_m, gain_v, rate_gain, 0.0)
    return (
        output,
        grad_tokens[None],
        new_qkv,
        new_m_qkv,
        new_v_qkv,
        copy_qkv,
        new_out,
        new_m_out,
        new_v_out,
        copy_out,
        new_gu,
        new_m_gu,
        new_v_gu,
        copy_gu,
        new_down,
        new_m_down,
        new_v_down,
        copy_down,
        new_gains,
        new_gain_m,
        new_gain_v,
        factor,
    )


def solution(mesh):
    return jax.shard_map(
        local,
        mesh=mesh,
        in_specs=(
            P("dp", "tensor", None),
            P("dp", "tensor", None),
            P("dp", None),
            P(None, "dp", "tensor"),
            P(None, "dp", "tensor"),
            P(None, "dp", "tensor"),
            P("tensor", "dp"),
            P("tensor", "dp"),
            P("tensor", "dp"),
            P(None, "dp", "tensor"),
            P(None, "dp", "tensor"),
            P(None, "dp", "tensor"),
            P("tensor", "dp"),
            P("tensor", "dp"),
            P("tensor", "dp"),
            P(None, "dp"),
            P(None, "dp"),
            P(None, "dp"),
        ),
        out_specs=(
            P("dp", "tensor", None),
            P("dp", "tensor", None),
            P(None, "dp", "tensor"),
            P(None, "dp", "tensor"),
            P(None, "dp", "tensor"),
            P(None, "dp", "tensor"),
            P("tensor", "dp"),
            P("tensor", "dp"),
            P("tensor", "dp"),
            P("tensor", "dp"),
            P(None, "dp", "tensor"),
            P(None, "dp", "tensor"),
            P(None, "dp", "tensor"),
            P(None, "dp", "tensor"),
            P("tensor", "dp"),
            P("tensor", "dp"),
            P("tensor", "dp"),
            P("tensor", "dp"),
            P(None, "dp"),
            P(None, "dp"),
            P(None, "dp"),
            P("tensor"),
        ),
        check_vma=False,
    )
```

```python
import jax
import jax.numpy as jnp
from jax import lax
from jax.experimental import pallas as pl
from jax.experimental.pallas import tpu as pltpu
from jax.sharding import PartitionSpec as P

HEAD = 128
STEP = 5


norm_eps = 1e-06
rope_base = 500000.0
beta_one = 0.9
beta_two = 0.95
rate_matrix = 0.01
rate_gain = 0.6
weight_decay = 0.1
adam_eps = 1e-08
clip_tau = 9.0
masked_value = -1e30


def rope_tables(length, size):
    half = size // 2
    freq = rope_base ** (-(jnp.arange(half, dtype=jnp.float32) * 2.0 / size))
    angle = jnp.arange(length, dtype=jnp.float32)[:, None] * freq[None, :]
    angle = jnp.concatenate([angle, angle], axis=1)
    return (jnp.cos(angle)[:, None, :], jnp.sin(angle)[:, None, :])


def rotate_fwd(value):
    half = value.shape[-1] // 2
    return jnp.concatenate([-value[..., half:], value[..., :half]], axis=-1)


def rotate_back(value):
    half = value.shape[-1] // 2
    return jnp.concatenate([value[..., half:], -value[..., :half]], axis=-1)


def adam_step(param, grad, first, second, rate, decay):
    first = beta_one * first + (1.0 - beta_one) * grad
    second = beta_two * second + (1.0 - beta_two) * grad * grad
    fix_one = 1.0 - beta_one**STEP
    fix_two = 1.0 - beta_two**STEP
    update = first / fix_one / (jnp.sqrt(second / fix_two) + adam_eps)
    return (param - rate * (update + decay * param), first, second)


def norm_back(scale_factor, normed, upstream):
    inner = jnp.mean(upstream * normed, axis=1, keepdims=True)
    return scale_factor * (upstream - normed * inner)


class Grid:
    def __init__(self):
        self.dp = lax.axis_size("dp")
        self.tensor = lax.axis_size("tensor")
        self.inner = 1
        while self.inner * self.inner * 4 <= self.dp:
            self.inner *= 2
        self.outer = self.dp // self.inner
        self.chips = self.tensor // 2
        self.dp_at = lax.axis_index("dp")
        self.tensor_at = lax.axis_index("tensor")
        self.inner_at = self.dp_at % self.inner
        self.chip_at = self.tensor_at // 2
        self.core_at = self.tensor_at % 2
        self.outer_at = self.dp_at // self.inner

    def path_of(self, index):
        column, row = index // self.inner, index % self.inner
        return row * self.outer + column + (row % 2) * (self.outer - 1 - 2 * column)

    def index_of(self, place):
        row, column = place // self.outer, place % self.outer
        return (column + (row % 2) * (self.outer - 1 - 2 * column)) * self.inner + row

    def to_outer(self, value, step):
        n, m = self.outer, self.inner
        pairs = [(a * m + b, (a + step) % n * m + b) for a in range(n) for b in range(m)]
        return lax.ppermute(value, "dp", pairs)

    def to_inner(self, value, step):
        n, m = self.outer, self.inner
        pairs = [(a * m + b, a * m + (b + step) % m) for a in range(n) for b in range(m)]
        return lax.ppermute(value, "dp", pairs)

    def to_chip(self, value, step):
        n = self.chips
        pairs = [(a * 2 + b, (a + step) % n * 2 + b) for a in range(n) for b in range(2)]
        return lax.ppermute(value, "tensor", pairs)

    def to_core(self, value):
        pairs = [(a * 2 + b, a * 2 + 1 - b) for a in range(self.chips) for b in range(2)]
        return lax.ppermute(value, "tensor", pairs)

    def across(self, value, axis, bit):
        count = lax.axis_size(axis)
        return lax.ppermute(value, axis, [(i, i ^ bit) for i in range(count)])


def bits(count):
    return [1 << k for k in range(count.bit_length() - 1)]


def part(value, axis, index, size):
    return lax.dynamic_slice_in_dim(value, index * size, size, axis)


def put(whole, piece, axis, index):
    return lax.dynamic_update_slice_in_dim(whole, piece, index * piece.shape[axis], axis)


def low_sum(*terms):
    total = terms[0].astype(jnp.float32)
    for term in terms[1:]:
        total = total + term.astype(jnp.float32)
    return total.astype(jnp.bfloat16)


def greet(peers):
    barrier = pltpu.get_barrier_semaphore()
    for peer in peers:
        pl.semaphore_signal(barrier, inc=1, device_id=peer, device_id_type=pl.DeviceIdType.MESH)
    pl.semaphore_wait(barrier, len(peers))


def path_gather(shard, gains, rows):
    grid = Grid()
    n, chips, tensor = grid.dp, grid.chips, grid.tensor
    lead, deep, wide = shard.shape
    half = deep // 2
    count = rows.shape[0]
    ring = 2 * lead + 1

    def kernel(shard_ref, gains_ref, rows_ref, full, full_gains, sequence, sends, lands, row_sends, row_lands, own):
        g = Grid()
        dp_at, t_at = g.dp_at, g.tensor_at
        chip_at, core_at = t_at // 2, t_at % 2
        place = g.path_of(dp_at)
        after = g.index_of(lax.rem(place + 1, n))
        before = g.index_of(lax.rem(place + n - 1, n))
        core_peer = (dp_at, chip_at * 2 + 1 - core_at)
        chip_peers = [
            (dp_at, lax.rem(chip_at + k, chips) * 2 + core_at) for k in range(1, chips)
        ]
        greet([(after, t_at), (before, t_at), core_peer] + chip_peers)

        def views(item, index):
            if item == 2 * lead:
                return gains_ref, full_gains.at[index]
            side, c = item // lead, item % lead
            span = pl.ds(pl.multiple_of(index * deep + side * half, half), half)
            return shard_ref.at[c, pl.ds(side * half, half)], full.at[c, span]

        def hop(step, item):
            way = -1 if item // lead == 1 and item != 2 * lead else 1
            index = g.index_of(lax.rem(place - way * step + n, n))
            source, target = views(item, index)
            return pltpu.make_async_remote_copy(
                src_ref=source if step == 0 else target,
                dst_ref=target,
                send_sem=sends.at[step, item],
                recv_sem=lands.at[step, item],
                device_id=(after if way == 1 else before, t_at),
                device_id_type=pl.DeviceIdType.MESH,
            )

        def rows_at(index):
            return sequence.at[pl.ds(pl.multiple_of(index * count, count), count)]

        def row_copy(slot, index, peer, first):
            return pltpu.make_async_remote_copy(
                src_ref=rows_ref if first else rows_at(index),
                dst_ref=rows_at(index),
                send_sem=row_sends.at[slot],
                recv_sem=row_lands.at[slot],
                device_id=peer,
                device_id_type=pl.DeviceIdType.MESH,
            )

        order = [c + side * lead for c in range(lead) for side in (0, 1)] + [2 * lead]
        hops = {}
        for item in order:
            hops[0, item] = hop(0, item)
            hops[0, item].start()
        moves = []
        for k in range(1, chips):
            moves.append(row_copy(k - 1, t_at, chip_peers[k - 1], True))
            moves[-1].start()
        mine = row_copy(chips - 1, t_at, core_peer, True)
        mine.start()
        keep = [
            pltpu.make_async_copy(
                shard_ref, full.at[:, pl.ds(pl.multiple_of(dp_at * deep, deep), deep)], own.at[0]
            ),
            pltpu.make_async_copy(gains_ref, full_gains.at[dp_at], own.at[1]),
            pltpu.make_async_copy(rows_ref, rows_at(t_at), own.at[2]),
        ]
        for copy in keep:
            copy.start()
        passed = []
        for step in range(1, n - 1):
            for item in order:
                hops[step - 1, item].wait_recv()
                hops[step, item] = hop(step, item)
                hops[step, item].start()
            if step <= chips - 1:
                moves[step - 1].wait_recv()
                source = lax.rem(chip_at - step + chips, chips) * 2 + core_at
                passed.append(row_copy(chips - 1 + step, source, core_peer, False))
                passed[-1].start()
        for item in order:
            hops[n - 2, item].wait_recv()
        mine.wait_recv()
        for copy in passed:
            copy.wait_recv()
        for key in hops:
            hops[key].wait_send()
        for copy in moves + [mine] + passed:
            copy.wait_send()
        for copy in keep:
            copy.wait()

    bf16 = jnp.bfloat16
    return pl.pallas_call(
        kernel,
        out_shape=(
            jax.ShapeDtypeStruct((lead, deep * n, wide), bf16),
            jax.ShapeDtypeStruct((n,) + gains.shape, bf16),
            jax.ShapeDtypeStruct((count * tensor, rows.shape[1]), bf16),
        ),
        in_specs=[pl.BlockSpec(memory_space=pl.ANY)] * 3,
        out_specs=(pl.BlockSpec(memory_space=pl.ANY),) * 3,
        scratch_shapes=[
            pltpu.SemaphoreType.DMA((n - 1, ring)),
            pltpu.SemaphoreType.DMA((n - 1, ring)),
            pltpu.SemaphoreType.DMA((2 * chips - 1,)),
            pltpu.SemaphoreType.DMA((2 * chips - 1,)),
            pltpu.SemaphoreType.DMA((3,)),
        ],
        compiler_params=pltpu.CompilerParams(collective_id=0, has_side_effects=True),
    )(shard, gains, rows)


def path_scatter(whole):
    grid = Grid()
    n = grid.dp
    lead, total, wide = whole.shape
    deep = total // n
    half = deep // 2
    ring = 2 * lead

    def kernel(whole_ref, out_ref, land, sends, lands):
        g = Grid()
        place = g.path_of(g.dp_at)
        after = g.index_of(lax.rem(place + 1, n))
        before = g.index_of(lax.rem(place + n - 1, n))
        greet([(after, g.tensor_at), (before, g.tensor_at)])

        def own(item, away):
            side, c = item // lead, item % lead
            way = -1 if side else 1
            index = g.index_of(lax.rem(place - way * away + 2 * n, n))
            return whole_ref.at[c, pl.ds(pl.multiple_of(index * deep + side * half, half), half)]

        def hop(step, item):
            return pltpu.make_async_remote_copy(
                src_ref=own(item, 1) if step == 0 else land.at[step - 1, item],
                dst_ref=land.at[step, item],
                send_sem=sends.at[step, item],
                recv_sem=lands.at[step, item],
                device_id=(before if item // lead else after, g.tensor_at),
                device_id_type=pl.DeviceIdType.MESH,
            )

        order = [c + side * lead for c in range(lead) for side in (0, 1)]
        hops = {}
        for item in order:
            hops[0, item] = hop(0, item)
            hops[0, item].start()
        for step in range(1, n):
            for item in order:
                hops[step - 1, item].wait_recv()
                summed = land[step - 1, item].astype(jnp.float32) + own(item, step + 1)[
                    ...
                ].astype(jnp.float32)
                if step < n - 1:
                    land[step - 1, item] = summed.astype(jnp.bfloat16)
                    hops[step, item] = hop(step, item)
                    hops[step, item].start()
                else:
                    side, c = item // lead, item % lead
                    out_ref[c, pl.ds(side * half, half)] = summed
        for key in hops:
            hops[key].wait_send()

    return pl.pallas_call(
        kernel,
        out_shape=jax.ShapeDtypeStruct((lead, deep, wide), jnp.float32),
        in_specs=[pl.BlockSpec(memory_space=pltpu.VMEM)],
        out_specs=pl.BlockSpec(memory_space=pltpu.VMEM),
        scratch_shapes=[
            pltpu.VMEM((n - 1, ring, half, wide), jnp.bfloat16),
            pltpu.SemaphoreType.DMA((n - 1, ring)),
            pltpu.SemaphoreType.DMA((n - 1, ring)),
        ],
        compiler_params=pltpu.CompilerParams(
            collective_id=1, has_side_effects=True, vmem_limit_bytes=40 * 2**20
        ),
    )(whole)


def width_gather(grid, shard):
    n, m = grid.outer, grid.inner
    rows, wide = shard.shape
    held = jnp.zeros((rows, wide * n), shard.dtype)
    for step in range(n):
        piece = grid.to_outer(shard, step) if step else shard
        held = put(held, piece, 1, (grid.outer_at - step) % n)
    return inner_gather(grid, held, 1)


def width_scatter(grid, whole):
    n = grid.outer
    total = inner_scatter(grid, whole, 1)
    wide = total.shape[1] // n
    result = part(total, 1, grid.outer_at, wide).astype(jnp.float32)
    for step in range(1, n):
        piece = grid.to_outer(part(total, 1, (grid.outer_at + step) % n, wide), step)
        result = result + piece.astype(jnp.float32)
    return result


def inner_gather(grid, held, axis):
    n, m = grid.outer, grid.inner
    wide = held.shape[axis] // n
    shape = list(held.shape)
    shape[axis] *= m
    full = jnp.zeros(shape, held.dtype)
    for step in range(m):
        if step:
            held = grid.to_inner(held, 1)
        inner = (grid.inner_at - step) % m
        for k in range(n):
            slab = lax.slice_in_dim(held, k * wide, (k + 1) * wide, axis=axis)
            full = put(full, slab, axis, k * m + inner)
    return full


def inner_scatter(grid, whole, axis):
    n, m = grid.outer, grid.inner
    wide = whole.shape[axis] // (n * m)

    def slabs(inner):
        return jnp.concatenate(
            [part(whole, axis, k * m + inner, wide) for k in range(n)], axis=axis
        )

    return low_sum(
        slabs(grid.inner_at),
        *[grid.to_inner(slabs((grid.inner_at + k) % m), k) for k in range(1, m)],
    )


def unit_gather(grid, shard, width_axis):
    unit_axis = 1 - width_axis
    n, m = grid.outer, grid.inner
    wide = shard.shape[width_axis]
    units = shard.shape[unit_axis] // n
    shape = [0, 0]
    shape[unit_axis] = units
    shape[width_axis] = wide * n
    held = jnp.zeros(shape, shard.dtype)
    for step in range(n):
        piece = part(shard, unit_axis, (grid.outer_at + step) % n, units)
        if step:
            piece = grid.to_outer(piece, step)
        held = put(held, piece, width_axis, (grid.outer_at - step) % n)
    return inner_gather(grid, held, width_axis)


def unit_scatter(grid, whole, width_axis):
    unit_axis = 1 - width_axis
    n, m = grid.outer, grid.inner
    units = whole.shape[unit_axis]
    total = inner_scatter(grid, whole, width_axis)
    wide = total.shape[width_axis] // n
    shape = [0, 0]
    shape[unit_axis] = units * n
    shape[width_axis] = wide
    shard = jnp.zeros(shape, whole.dtype)
    for step in range(n):
        piece = part(total, width_axis, (grid.outer_at + step) % n, wide)
        if step:
            piece = grid.to_outer(piece, step)
        shard = put(shard, piece, unit_axis, (grid.outer_at - step) % n)
    return shard


def group_gather(grid, rows):
    blocks = []
    for step in range(grid.outer):
        here = grid.to_outer(rows, step) if step else rows
        there = [here] + [grid.to_chip(here, k) for k in range(1, grid.chips)]
        blocks.append(jnp.concatenate(there + [grid.to_core(v) for v in there], axis=0))
    return blocks


def group_return(grid, block, step):
    rows = block.shape[0] // 2
    mine = block[:rows] + grid.to_core(block[rows:].astype(jnp.bfloat16)).astype(jnp.float32)
    count = rows // grid.chips
    total = mine[:count]
    for k in range(1, grid.chips):
        away = mine[k * count : (k + 1) * count].astype(jnp.bfloat16)
        total = total + grid.to_chip(away, -k).astype(jnp.float32)
    if step == 0:
        return total
    return grid.to_outer(total.astype(jnp.bfloat16), -step).astype(jnp.float32)


def sequence_scatter(grid, whole):
    rows = whole.shape[0] // grid.tensor
    shaped = whole.reshape(grid.chips, 2, rows, whole.shape[1])
    other = part(shaped, 1, 1 - grid.core_at, 1)[:, 0].astype(jnp.bfloat16)
    own = part(shaped, 1, grid.core_at, 1)[:, 0]
    pair = own + grid.to_core(other).astype(jnp.float32)
    total = part(pair, 0, grid.chip_at, 1)[0]
    for step in range(1, grid.chips):
        away = part(pair, 0, (grid.chip_at + step) % grid.chips, 1)[0].astype(jnp.bfloat16)
        total = total + grid.to_chip(away, step).astype(jnp.float32)
    return total


def sequence_gather(grid, rows):
    count, width = rows.shape
    whole = jnp.zeros((grid.chips, 2, count, width), rows.dtype)
    for step in range(grid.chips):
        here = grid.to_chip(rows, step) if step else rows
        chip = (grid.chip_at - step) % grid.chips
        for value, core in ((here, grid.core_at), (grid.to_core(here), 1 - grid.core_at)):
            whole = lax.dynamic_update_slice(whole, value[None, None], (chip, core, 0, 0))
    return whole.reshape(grid.tensor * count, width)


def gains_scatter(grid, whole):
    rows = whole.shape[0]
    held = jnp.swapaxes(whole.reshape(rows, grid.dp, -1), 0, 1)
    for bit in reversed(bits(grid.dp)):
        low_side = (grid.dp_at // bit) % 2 == 0
        keep = jnp.where(low_side, held[:bit], held[bit:])
        give = jnp.where(low_side, held[bit:], held[:bit])
        held = keep + grid.across(give, "dp", bit)
    held = held[0]
    for bit in bits(grid.tensor):
        held = held + grid.across(held, "tensor", bit)
    return held


def adam_kernel(w_ref, m_ref, v_ref, g_ref, *rest):
    scale_ref = rest[0] if len(rest) == 5 else None
    w_out, m_out, v_out, c_out = rest[-4:]
    grad = g_ref[...].astype(jnp.float32)
    new, first, second = adam_step(
        w_ref[...], grad, m_ref[...], v_ref[...], rate_matrix, weight_decay
    )
    if scale_ref is not None:
        new = new * scale_ref[...]
    w_out[...] = new
    m_out[...] = first
    v_out[...] = second
    c_out[...] = new.astype(jnp.bfloat16)


def adam_call(param, grad, first, second, scale=None):
    shape = param.shape
    flat = [v.reshape(-1, shape[-1]) for v in (param, first, second, grad)]
    rows, width = flat[0].shape
    block = min(rows, max(16, (1 << 17) // width))
    spec = pl.BlockSpec((block, width), lambda k: (k, 0))
    specs = [spec] * 4
    if scale is not None:
        per = shape[1] // block
        flat.append(scale)
        specs.append(pl.BlockSpec((None, 1, width), lambda k: (k // per, 0, 0)))
    outs = [jax.ShapeDtypeStruct((rows, width), jnp.float32)] * 3
    outs.append(jax.ShapeDtypeStruct((rows, width), jnp.bfloat16))
    size = rows * width
    result = pl.pallas_call(
        adam_kernel,
        grid=(rows // block,),
        in_specs=specs,
        out_specs=[spec] * 4,
        out_shape=outs,
        cost_estimate=pl.CostEstimate(
            flops=20 * size, bytes_accessed=28 * size, transcendentals=2 * size
        ),
        compiler_params=pltpu.CompilerParams(vmem_limit_bytes=32 * 2**20),
    )(*flat)
    return [v.reshape(shape) for v in result]


def local(
    tokens,
    cotangent,
    block_ids,
    w_qkv,
    m_qkv,
    v_qkv,
    w_out,
    m_out,
    v_out,
    w_gu,
    m_gu,
    v_gu,
    w_down,
    m_down,
    v_down,
    gains,
    gain_m,
    gain_v,
):
    grid = Grid()
    local_x = tokens[0]
    gain_count = gains.shape[0]
    low_gains = jnp.pad(gains.astype(jnp.bfloat16), ((0, 16 - gain_count), (0, 0)))
    full_qkv, full_gains, seq_x = path_gather(w_qkv.astype(jnp.bfloat16), low_gains, local_x)
    gain_rows = jnp.swapaxes(full_gains[:, :gain_count], 0, 1).reshape(gain_count, -1)
    gain_rows = gain_rows.astype(jnp.float32)
    shards = (
        w_out.astype(jnp.bfloat16),
        w_gu[0].astype(jnp.bfloat16),
        w_gu[1].astype(jnp.bfloat16),
        w_down.astype(jnp.bfloat16),
    )
    full_qkv, shards = lax.optimization_barrier((full_qkv, shards))
    full_out = width_gather(grid, shards[0])
    unit_gate = unit_gather(grid, shards[1], 0)
    unit_up = unit_gather(grid, shards[2], 0)
    unit_down = unit_gather(grid, shards[3], 1)
    model_width = local_x.shape[1]
    length = seq_x.shape[0]
    span = full_qkv.shape[2]
    heads_here = span // HEAD
    offset = lax.axis_index("tensor") * span
    projected = jnp.einsum("sd,cde->cse", seq_x, full_qkv, preferred_element_type=jnp.float32)
    queries, keys, values = (projected[0], projected[1], projected[2])
    q_square, k_square = lax.psum(
        (jnp.sum(queries * queries, axis=1), jnp.sum(keys * keys, axis=1)), "tensor"
    )
    q_scale = lax.rsqrt(q_square / model_width + norm_eps)[:, None]
    k_scale = lax.rsqrt(k_square / model_width + norm_eps)[:, None]
    q_hat = queries * q_scale
    k_hat = keys * k_scale
    q_gain = lax.dynamic_slice_in_dim(gain_rows[0], offset, span)
    k_gain = lax.dynamic_slice_in_dim(gain_rows[1], offset, span)
    cosine, sine = rope_tables(length, HEAD)

    def rotary(value):
        shaped = value.reshape(length, heads_here, HEAD)
        return shaped * cosine + rotate_fwd(shaped) * sine

    def unrotary(grad):
        return (grad * cosine + rotate_back(grad * sine)).reshape(length, span)

    q_low = rotary(q_hat * q_gain).astype(jnp.bfloat16)
    k_low = rotary(k_hat * k_gain).astype(jnp.bfloat16)
    v_low = values.astype(jnp.bfloat16).reshape(length, heads_here, HEAD)
    blocks = block_ids[0]
    block_rows = min(512, length)
    block_count = length // block_rows
    scale = HEAD ** (-0.5)
    starts = jnp.arange(block_count, dtype=jnp.int32) * block_rows

    def scores_of(start):
        q_part = lax.dynamic_slice_in_dim(q_low, start, block_rows, 0)
        b_part = lax.dynamic_slice_in_dim(blocks, start, block_rows, 0)
        raw = jnp.einsum("qhd,khd->hqk", q_part, k_low, preferred_element_type=jnp.float32) * scale
        allowed = blocks[None, None, :] <= b_part[None, :, None]
        return (jnp.where(allowed, raw, masked_value), q_part)

    def forward_block(start):
        masked, q_part = scores_of(start)
        top = jnp.max(masked, axis=2, keepdims=True)
        weight = jnp.exp(masked - top)
        total = jnp.sum(weight, axis=2, keepdims=True)
        probs = (weight / total).astype(jnp.bfloat16)
        context = jnp.einsum("hqk,khd->qhd", probs, v_low, preferred_element_type=jnp.float32)
        return (
            context.astype(jnp.bfloat16),
            (top + jnp.log(total))[:, :, 0],
            jnp.max(top[:, :, 0], axis=1),
        )

    context_low, log_total, block_top = lax.map(forward_block, starts)
    context_low = context_low.reshape(length, span)
    head_top = jnp.max(block_top, axis=0)
    attn_raw = sequence_scatter(
        grid, jnp.dot(context_low, full_out, preferred_element_type=jnp.float32)
    )
    x_float = local_x.astype(jnp.float32)
    o_scale = lax.rsqrt(jnp.mean(attn_raw * attn_raw, axis=1, keepdims=True) + norm_eps)
    attn_hat = attn_raw * o_scale
    resid = x_float + attn_hat * gain_rows[2]
    blocks_h = group_gather(grid, resid.astype(jnp.bfloat16))
    kept = []
    mlp_raw = jnp.zeros_like(resid)
    for step, rows in enumerate(blocks_h):
        gate = jnp.dot(rows, unit_gate, preferred_element_type=jnp.float32)
        up = jnp.dot(rows, unit_up, preferred_element_type=jnp.float32)
        act = (gate * jax.nn.sigmoid(gate) * up).astype(jnp.bfloat16)
        kept.append((gate, up, act))
        partial = jnp.dot(act, unit_down, preferred_element_type=jnp.float32)
        mlp_raw = mlp_raw + group_return(grid, partial, step)
    m_scale = lax.rsqrt(jnp.mean(mlp_raw * mlp_raw, axis=1, keepdims=True) + norm_eps)
    mlp_hat = mlp_raw * m_scale
    output = (resid + mlp_hat * gain_rows[3]).astype(jnp.bfloat16)[None]
    grad_top = cotangent[0].astype(jnp.float32)
    gain_last = jnp.sum(grad_top * mlp_hat, axis=0)
    d_mlp = norm_back(m_scale, mlp_hat, grad_top * gain_rows[3]).astype(jnp.bfloat16)
    blocks_dm = group_gather(grid, d_mlp)
    d_resid = grad_top
    d_gates, d_ups = [], []
    for step, rows in enumerate(blocks_dm):
        gate, up, act = kept[step]
        sigma = jax.nn.sigmoid(gate)
        d_act = lax.dot_general(
            rows, unit_down, (((1,), (1,)), ((), ())), preferred_element_type=jnp.float32
        )
        d_gate = (d_act * up * sigma * (1.0 + gate * (1.0 - sigma))).astype(jnp.bfloat16)
        d_up = (d_act * gate * sigma).astype(jnp.bfloat16)
        d_gates.append(d_gate)
        d_ups.append(d_up)
        partial = lax.dot_general(
            d_gate, unit_gate, (((1,), (1,)), ((), ())), preferred_element_type=jnp.float32
        ) + lax.dot_general(
            d_up, unit_up, (((1,), (1,)), ((), ())), preferred_element_type=jnp.float32
        )
        d_resid = d_resid + group_return(grid, partial, step)
    all_h = jnp.concatenate(blocks_h, axis=0)

    def weight_grad(left, right):
        return lax.dot_general(
            left, right, (((0,), (0,)), ((), ())), preferred_element_type=jnp.float32
        ).astype(jnp.bfloat16)

    part_down = unit_scatter(
        grid,
        weight_grad(
            jnp.concatenate([item[2] for item in kept], axis=0),
            jnp.concatenate(blocks_dm, axis=0),
        ),
        1,
    )
    part_gate = unit_scatter(grid, weight_grad(all_h, jnp.concatenate(d_gates, axis=0)), 0)
    part_up = unit_scatter(grid, weight_grad(all_h, jnp.concatenate(d_ups, axis=0)), 0)
    gain_attn = jnp.sum(d_resid * attn_hat, axis=0)
    d_attn = norm_back(o_scale, attn_hat, d_resid * gain_rows[2]).astype(jnp.bfloat16)
    seq_do = sequence_gather(grid, d_attn)
    grad_out = jnp.einsum("se,sd->ed", context_low, seq_do, preferred_element_type=jnp.float32)
    part_out = width_scatter(grid, grad_out.astype(jnp.bfloat16))
    d_context = jnp.einsum("sd,ed->se", seq_do, full_out, preferred_element_type=jnp.float32)
    d_context = d_context.astype(jnp.bfloat16).reshape(length, heads_here, HEAD)

    def backward_block(carry, item):
        key_acc, value_acc = carry
        start, log_part = item
        masked, q_part = scores_of(start)
        probs = jnp.exp(masked - log_part[:, :, None])
        dc_part = lax.dynamic_slice_in_dim(d_context, start, block_rows, 0)
        d_probs = jnp.einsum("qhd,khd->hqk", dc_part, v_low, preferred_element_type=jnp.float32)
        inner = jnp.sum(probs * d_probs, axis=2, keepdims=True)
        d_scores = (probs * (d_probs - inner)).astype(jnp.bfloat16)
        d_query = (
            jnp.einsum("hqk,khd->qhd", d_scores, k_low, preferred_element_type=jnp.float32) * scale
        )
        key_acc = (
            key_acc
            + jnp.einsum("hqk,qhd->khd", d_scores, q_part, preferred_element_type=jnp.float32)
            * scale
        )
        value_acc = value_acc + jnp.einsum(
            "hqk,qhd->khd", probs.astype(jnp.bfloat16), dc_part, preferred_element_type=jnp.float32
        )
        return ((key_acc, value_acc), d_query)

    empty = jnp.zeros((length, heads_here, HEAD), jnp.float32)
    (d_krot, d_values), d_qrot = lax.scan(backward_block, (empty, empty), (starts, log_total))
    d_qrot = d_qrot.reshape(length, heads_here, HEAD)
    d_qnorm = unrotary(d_qrot)
    d_knorm = unrotary(d_krot)
    head_gains = jnp.stack([jnp.sum(d_qnorm * q_hat, axis=0), jnp.sum(d_knorm * k_hat, axis=0)])
    placed = lax.dynamic_update_slice(
        jnp.zeros((2, model_width), jnp.float32), head_gains, (0, offset)
    )
    gain_terms = jnp.concatenate([placed, jnp.stack([gain_attn, gain_last])], axis=0)
    dq_hat = d_qnorm * q_gain
    dk_hat = d_knorm * k_gain
    q_inner, k_inner = lax.psum(
        (jnp.sum(dq_hat * q_hat, axis=1), jnp.sum(dk_hat * k_hat, axis=1)), "tensor"
    )
    part_gains = gains_scatter(grid, gain_terms)
    d_query = q_scale * (dq_hat - q_hat * (q_inner / model_width)[:, None])
    d_key = k_scale * (dk_hat - k_hat * (k_inner / model_width)[:, None])
    d_qkv = jnp.stack([d_query, d_key, d_values.reshape(length, span)]).astype(jnp.bfloat16)
    grad_qkv = jnp.einsum("sd,cse->cde", seq_x, d_qkv, preferred_element_type=jnp.float32)
    part_qkv = path_scatter(grad_qkv.astype(jnp.bfloat16))
    grad_tokens = d_resid + sequence_scatter(
        grid, jnp.einsum("cse,cde->sd", d_qkv, full_qkv, preferred_element_type=jnp.float32)
    )
    for bit in bits(grid.dp):
        head_top = jnp.maximum(head_top, grid.across(head_top, "dp", bit))
    factor = clip_tau / jnp.maximum(head_top, clip_tau)
    column = jnp.repeat(jnp.sqrt(factor), HEAD)
    column_scale = jnp.stack([column, column, jnp.ones_like(column)])[:, None, :]
    new_qkv, new_m_qkv, new_v_qkv, copy_qkv = adam_call(
        w_qkv, part_qkv, m_qkv, v_qkv, column_scale
    )
    new_out, new_m_out, new_v_out, copy_out = adam_call(w_out, part_out, m_out, v_out)
    new_gu, new_m_gu, new_v_gu, copy_gu = adam_call(
        w_gu, jnp.stack([part_gate, part_up]), m_gu, v_gu
    )
    new_down, new_m_down, new_v_down, copy_down = adam_call(w_down, part_down, m_down, v_down)
    new_gains, new_gain_m, new_gain_v = adam_step(gains, part_gains, gain_m, gain_v, rate_gain, 0.0)
    return (
        output,
        grad_tokens[None],
        new_qkv,
        new_m_qkv,
        new_v_qkv,
        copy_qkv,
        new_out,
        new_m_out,
        new_v_out,
        copy_out,
        new_gu,
        new_m_gu,
        new_v_gu,
        copy_gu,
        new_down,
        new_m_down,
        new_v_down,
        copy_down,
        new_gains,
        new_gain_m,
        new_gain_v,
        factor,
    )


def solution(mesh):
    return jax.shard_map(
        local,
        mesh=mesh,
        in_specs=(
            P("dp", "tensor", None),
            P("dp", "tensor", None),
            P("dp", None),
            P(None, "dp", "tensor"),
            P(None, "dp", "tensor"),
            P(None, "dp", "tensor"),
            P("tensor", "dp"),
            P("tensor", "dp"),
            P("tensor", "dp"),
            P(None, "dp", "tensor"),
            P(None, "dp", "tensor"),
            P(None, "dp", "tensor"),
            P("tensor", "dp"),
            P("tensor", "dp"),
            P("tensor", "dp"),
            P(None, "dp"),
            P(None, "dp"),
            P(None, "dp"),
        ),
        out_specs=(
            P("dp", "tensor", None),
            P("dp", "tensor", None),
            P(None, "dp", "tensor"),
            P(None, "dp", "tensor"),
            P(None, "dp", "tensor"),
            P(None, "dp", "tensor"),
            P("tensor", "dp"),
            P("tensor", "dp"),
            P("tensor", "dp"),
            P("tensor", "dp"),
            P(None, "dp", "tensor"),
            P(None, "dp", "tensor"),
            P(None, "dp", "tensor"),
            P(None, "dp", "tensor"),
            P("tensor", "dp"),
            P("tensor", "dp"),
            P("tensor", "dp"),
            P("tensor", "dp"),
            P(None, "dp"),
            P(None, "dp"),
            P(None, "dp"),
            P("tensor"),
        ),
        check_vma=False,
    )
```

```python
import jax
import jax.numpy as jnp
from jax import lax
from jax.experimental import pallas as pl
from jax.experimental.pallas import tpu as pltpu
from jax.sharding import PartitionSpec as P

HEAD = 128
STEP = 5


norm_eps = 1e-06
rope_base = 500000.0
beta_one = 0.9
beta_two = 0.95
rate_matrix = 0.01
rate_gain = 0.6
weight_decay = 0.1
adam_eps = 1e-08
clip_tau = 9.0
masked_value = -1e30


def rope_tables(length, size):
    half = size // 2
    freq = rope_base ** (-(jnp.arange(half, dtype=jnp.float32) * 2.0 / size))
    angle = jnp.arange(length, dtype=jnp.float32)[:, None] * freq[None, :]
    angle = jnp.concatenate([angle, angle], axis=1)
    return (jnp.cos(angle)[:, None, :], jnp.sin(angle)[:, None, :])


def rotate_fwd(value):
    half = value.shape[-1] // 2
    return jnp.concatenate([-value[..., half:], value[..., :half]], axis=-1)


def rotate_back(value):
    half = value.shape[-1] // 2
    return jnp.concatenate([value[..., half:], -value[..., :half]], axis=-1)


def adam_step(param, grad, first, second, rate, decay):
    first = beta_one * first + (1.0 - beta_one) * grad
    second = beta_two * second + (1.0 - beta_two) * grad * grad
    fix_one = 1.0 - beta_one**STEP
    fix_two = 1.0 - beta_two**STEP
    update = first / fix_one / (jnp.sqrt(second / fix_two) + adam_eps)
    return (param - rate * (update + decay * param), first, second)


def norm_back(scale_factor, normed, upstream):
    inner = jnp.mean(upstream * normed, axis=1, keepdims=True)
    return scale_factor * (upstream - normed * inner)


class Grid:
    def __init__(self):
        self.dp = lax.axis_size("dp")
        self.tensor = lax.axis_size("tensor")
        self.inner = 1
        while self.inner * self.inner * 4 <= self.dp:
            self.inner *= 2
        self.outer = self.dp // self.inner
        self.chips = self.tensor // 2
        self.dp_at = lax.axis_index("dp")
        self.tensor_at = lax.axis_index("tensor")
        self.inner_at = self.dp_at % self.inner
        self.chip_at = self.tensor_at // 2
        self.core_at = self.tensor_at % 2
        self.outer_at = self.dp_at // self.inner

    def path_of(self, index):
        column, row = index // self.inner, index % self.inner
        return row * self.outer + column + (row % 2) * (self.outer - 1 - 2 * column)

    def index_of(self, place):
        row, column = place // self.outer, place % self.outer
        return (column + (row % 2) * (self.outer - 1 - 2 * column)) * self.inner + row

    def to_outer(self, value, step):
        n, m = self.outer, self.inner
        pairs = [(a * m + b, (a + step) % n * m + b) for a in range(n) for b in range(m)]
        return lax.ppermute(value, "dp", pairs)

    def to_inner(self, value, step):
        n, m = self.outer, self.inner
        pairs = [(a * m + b, a * m + (b + step) % m) for a in range(n) for b in range(m)]
        return lax.ppermute(value, "dp", pairs)

    def to_chip(self, value, step):
        n = self.chips
        pairs = [(a * 2 + b, (a + step) % n * 2 + b) for a in range(n) for b in range(2)]
        return lax.ppermute(value, "tensor", pairs)

    def to_core(self, value):
        pairs = [(a * 2 + b, a * 2 + 1 - b) for a in range(self.chips) for b in range(2)]
        return lax.ppermute(value, "tensor", pairs)

    def across(self, value, axis, bit):
        count = lax.axis_size(axis)
        return lax.ppermute(value, axis, [(i, i ^ bit) for i in range(count)])


def bits(count):
    return [1 << k for k in range(count.bit_length() - 1)]


def part(value, axis, index, size):
    return lax.dynamic_slice_in_dim(value, index * size, size, axis)


def put(whole, piece, axis, index):
    return lax.dynamic_update_slice_in_dim(whole, piece, index * piece.shape[axis], axis)


def low_sum(*terms):
    total = terms[0].astype(jnp.float32)
    for term in terms[1:]:
        total = total + term.astype(jnp.float32)
    return total.astype(jnp.bfloat16)


def greet(peers):
    barrier = pltpu.get_barrier_semaphore()
    for peer in peers:
        pl.semaphore_signal(barrier, inc=1, device_id=peer, device_id_type=pl.DeviceIdType.MESH)
    pl.semaphore_wait(barrier, len(peers))


def path_gather(shard, gains, rows):
    grid = Grid()
    n, chips, tensor = grid.dp, grid.chips, grid.tensor
    lead, deep, wide = shard.shape
    half = deep // 2
    count = rows.shape[0]
    ring = 2 * lead + 1

    def kernel(shard_ref, gains_ref, rows_ref, full, full_gains, sequence, sends, lands, row_sends, row_lands, own):
        g = Grid()
        dp_at, t_at = g.dp_at, g.tensor_at
        chip_at, core_at = t_at // 2, t_at % 2
        place = g.path_of(dp_at)
        after = g.index_of(lax.rem(place + 1, n))
        before = g.index_of(lax.rem(place + n - 1, n))
        core_peer = (dp_at, chip_at * 2 + 1 - core_at)
        chip_peers = [
            (dp_at, lax.rem(chip_at + k, chips) * 2 + core_at) for k in range(1, chips)
        ]
        greet([(after, t_at), (before, t_at), core_peer] + chip_peers)

        def views(item, index):
            if item == 2 * lead:
                return gains_ref, full_gains.at[index]
            side, c = item // lead, item % lead
            span = pl.ds(pl.multiple_of(index * deep + side * half, half), half)
            return shard_ref.at[c, pl.ds(side * half, half)], full.at[c, span]

        def hop(step, item):
            way = -1 if item // lead == 1 and item != 2 * lead else 1
            index = g.index_of(lax.rem(place - way * step + n, n))
            source, target = views(item, index)
            return pltpu.make_async_remote_copy(
                src_ref=source if step == 0 else target,
                dst_ref=target,
                send_sem=sends.at[step, item],
                recv_sem=lands.at[step, item],
                device_id=(after if way == 1 else before, t_at),
                device_id_type=pl.DeviceIdType.MESH,
            )

        def rows_at(index):
            return sequence.at[pl.ds(pl.multiple_of(index * count, count), count)]

        def row_copy(slot, index, peer, first):
            return pltpu.make_async_remote_copy(
                src_ref=rows_ref if first else rows_at(index),
                dst_ref=rows_at(index),
                send_sem=row_sends.at[slot],
                recv_sem=row_lands.at[slot],
                device_id=peer,
                device_id_type=pl.DeviceIdType.MESH,
            )

        order = [c + side * lead for c in range(lead) for side in (0, 1)] + [2 * lead]
        hops = {}
        for item in order:
            hops[0, item] = hop(0, item)
            hops[0, item].start()
        moves = []
        for k in range(1, chips):
            moves.append(row_copy(k - 1, t_at, chip_peers[k - 1], True))
            moves[-1].start()
        mine = row_copy(chips - 1, t_at, core_peer, True)
        mine.start()
        keep = [
            pltpu.make_async_copy(
                shard_ref, full.at[:, pl.ds(pl.multiple_of(dp_at * deep, deep), deep)], own.at[0]
            ),
            pltpu.make_async_copy(gains_ref, full_gains.at[dp_at], own.at[1]),
            pltpu.make_async_copy(rows_ref, rows_at(t_at), own.at[2]),
        ]
        for copy in keep:
            copy.start()
        passed = []
        for step in range(1, n - 1):
            for item in order:
                hops[step - 1, item].wait_recv()
                hops[step, item] = hop(step, item)
                hops[step, item].start()
            if step <= chips - 1:
                moves[step - 1].wait_recv()
                source = lax.rem(chip_at - step + chips, chips) * 2 + core_at
                passed.append(row_copy(chips - 1 + step, source, core_peer, False))
                passed[-1].start()
        for item in order:
            hops[n - 2, item].wait_recv()
        mine.wait_recv()
        for copy in passed:
            copy.wait_recv()
        for key in hops:
            hops[key].wait_send()
        for copy in moves + [mine] + passed:
            copy.wait_send()
        for copy in keep:
            copy.wait()

    bf16 = jnp.bfloat16
    return pl.pallas_call(
        kernel,
        out_shape=(
            jax.ShapeDtypeStruct((lead, deep * n, wide), bf16),
            jax.ShapeDtypeStruct((n,) + gains.shape, bf16),
            jax.ShapeDtypeStruct((count * tensor, rows.shape[1]), bf16),
        ),
        in_specs=[pl.BlockSpec(memory_space=pl.ANY)] * 3,
        out_specs=(pl.BlockSpec(memory_space=pl.ANY),) * 3,
        scratch_shapes=[
            pltpu.SemaphoreType.DMA((n - 1, ring)),
            pltpu.SemaphoreType.DMA((n - 1, ring)),
            pltpu.SemaphoreType.DMA((2 * chips - 1,)),
            pltpu.SemaphoreType.DMA((2 * chips - 1,)),
            pltpu.SemaphoreType.DMA((3,)),
        ],
        compiler_params=pltpu.CompilerParams(collective_id=0, has_side_effects=True),
    )(shard, gains, rows)


def path_scatter(whole):
    grid = Grid()
    n = grid.dp
    lead, total, wide = whole.shape
    deep = total // n
    half = deep // 2
    ring = 2 * lead

    def kernel(whole_ref, out_ref, land, sends, lands):
        g = Grid()
        place = g.path_of(g.dp_at)
        after = g.index_of(lax.rem(place + 1, n))
        before = g.index_of(lax.rem(place + n - 1, n))
        greet([(after, g.tensor_at), (before, g.tensor_at)])

        def own(item, away):
            side, c = item // lead, item % lead
            way = -1 if side else 1
            index = g.index_of(lax.rem(place - way * away + 2 * n, n))
            return whole_ref.at[c, pl.ds(pl.multiple_of(index * deep + side * half, half), half)]

        def hop(step, item):
            return pltpu.make_async_remote_copy(
                src_ref=own(item, 1) if step == 0 else land.at[step - 1, item],
                dst_ref=land.at[step, item],
                send_sem=sends.at[step, item],
                recv_sem=lands.at[step, item],
                device_id=(before if item // lead else after, g.tensor_at),
                device_id_type=pl.DeviceIdType.MESH,
            )

        order = [c + side * lead for c in range(lead) for side in (0, 1)]
        hops = {}
        for item in order:
            hops[0, item] = hop(0, item)
            hops[0, item].start()
        for step in range(1, n):
            for item in order:
                hops[step - 1, item].wait_recv()
                summed = land[step - 1, item].astype(jnp.float32) + own(item, step + 1)[
                    ...
                ].astype(jnp.float32)
                if step < n - 1:
                    land[step - 1, item] = summed.astype(jnp.bfloat16)
                    hops[step, item] = hop(step, item)
                    hops[step, item].start()
                else:
                    side, c = item // lead, item % lead
                    out_ref[c, pl.ds(side * half, half)] = summed
        for key in hops:
            hops[key].wait_send()

    return pl.pallas_call(
        kernel,
        out_shape=jax.ShapeDtypeStruct((lead, deep, wide), jnp.float32),
        in_specs=[pl.BlockSpec(memory_space=pltpu.VMEM)],
        out_specs=pl.BlockSpec(memory_space=pltpu.VMEM),
        scratch_shapes=[
            pltpu.VMEM((n - 1, ring, half, wide), jnp.bfloat16),
            pltpu.SemaphoreType.DMA((n - 1, ring)),
            pltpu.SemaphoreType.DMA((n - 1, ring)),
        ],
        compiler_params=pltpu.CompilerParams(
            collective_id=1, has_side_effects=True, vmem_limit_bytes=40 * 2**20
        ),
    )(whole)


def width_gather(grid, shard):
    n, m = grid.outer, grid.inner
    rows, wide = shard.shape
    held = jnp.zeros((rows, wide * n), shard.dtype)
    for step in range(n):
        piece = grid.to_outer(shard, step) if step else shard
        held = put(held, piece, 1, (grid.outer_at - step) % n)
    return inner_join(grid, inner_pieces(grid, held), 1)


def width_scatter(grid, whole):
    n = grid.outer
    total = inner_scatter(grid, whole, 1)
    wide = total.shape[1] // n
    result = part(total, 1, grid.outer_at, wide).astype(jnp.float32)
    for step in range(1, n):
        piece = grid.to_outer(part(total, 1, (grid.outer_at + step) % n, wide), step)
        result = result + piece.astype(jnp.float32)
    return result


def inner_pieces(grid, held):
    pieces = [held]
    for _ in range(1, grid.inner):
        pieces.append(grid.to_inner(pieces[-1], 1))
    return pieces


def inner_join(grid, pieces, axis):
    n, m = grid.outer, grid.inner
    wide = pieces[0].shape[axis] // n
    shape = list(pieces[0].shape)
    shape[axis] *= m
    full = jnp.zeros(shape, pieces[0].dtype)
    for step, held in enumerate(pieces):
        inner = (grid.inner_at - step) % m
        for k in range(n):
            slab = lax.slice_in_dim(held, k * wide, (k + 1) * wide, axis=axis)
            full = put(full, slab, axis, k * m + inner)
    return full


def inner_scatter(grid, whole, axis):
    n, m = grid.outer, grid.inner
    wide = whole.shape[axis] // (n * m)

    def slabs(inner):
        return jnp.concatenate(
            [part(whole, axis, k * m + inner, wide) for k in range(n)], axis=axis
        )

    return low_sum(
        slabs(grid.inner_at),
        *[grid.to_inner(slabs((grid.inner_at + k) % m), k) for k in range(1, m)],
    )


def unit_gather(grid, shard, width_axis):
    unit_axis = 1 - width_axis
    n = grid.outer
    wide = shard.shape[width_axis]
    units = shard.shape[unit_axis] // n
    shape = [0, 0]
    shape[unit_axis] = units
    shape[width_axis] = wide * n
    held = jnp.zeros(shape, shard.dtype)
    for step in range(n):
        piece = part(shard, unit_axis, (grid.outer_at + step) % n, units)
        if step:
            piece = grid.to_outer(piece, step)
        held = put(held, piece, width_axis, (grid.outer_at - step) % n)
    return inner_pieces(grid, held)


def unit_scatter(grid, whole, width_axis):
    unit_axis = 1 - width_axis
    n, m = grid.outer, grid.inner
    units = whole.shape[unit_axis]
    total = inner_scatter(grid, whole, width_axis)
    wide = total.shape[width_axis] // n
    shape = [0, 0]
    shape[unit_axis] = units * n
    shape[width_axis] = wide
    shard = jnp.zeros(shape, whole.dtype)
    for step in range(n):
        piece = part(total, width_axis, (grid.outer_at + step) % n, wide)
        if step:
            piece = grid.to_outer(piece, step)
        shard = put(shard, piece, unit_axis, (grid.outer_at - step) % n)
    return shard


def sequence_scatter(grid, whole):
    rows = whole.shape[0] // grid.tensor
    shaped = whole.reshape(grid.chips, 2, rows, whole.shape[1])
    other = part(shaped, 1, 1 - grid.core_at, 1)[:, 0].astype(jnp.bfloat16)
    own = part(shaped, 1, grid.core_at, 1)[:, 0]
    pair = own + grid.to_core(other).astype(jnp.float32)
    total = part(pair, 0, grid.chip_at, 1)[0]
    for step in range(1, grid.chips):
        away = part(pair, 0, (grid.chip_at + step) % grid.chips, 1)[0].astype(jnp.bfloat16)
        total = total + grid.to_chip(away, step).astype(jnp.float32)
    return total


def sequence_gather(grid, rows):
    count, width = rows.shape
    whole = jnp.zeros((grid.chips, 2, count, width), rows.dtype)
    for step in range(grid.chips):
        here = grid.to_chip(rows, step) if step else rows
        chip = (grid.chip_at - step) % grid.chips
        for value, core in ((here, grid.core_at), (grid.to_core(here), 1 - grid.core_at)):
            whole = lax.dynamic_update_slice(whole, value[None, None], (chip, core, 0, 0))
    return whole.reshape(grid.tensor * count, width)


def gains_scatter(grid, whole):
    rows = whole.shape[0]
    held = jnp.swapaxes(whole.reshape(rows, grid.dp, -1), 0, 1)
    for bit in reversed(bits(grid.dp)):
        low_side = (grid.dp_at // bit) % 2 == 0
        keep = jnp.where(low_side, held[:bit], held[bit:])
        give = jnp.where(low_side, held[bit:], held[:bit])
        held = keep + grid.across(give, "dp", bit)
    held = held[0]
    for bit in bits(grid.tensor):
        held = held + grid.across(held, "tensor", bit)
    return held


def unit_kernel_call(rows_low, resid, cotangent, gain, unit_gate, unit_up, unit_down):
    grid = Grid()
    outer, chips = grid.outer, grid.chips
    count, width = rows_low.shape
    units = unit_gate.shape[1]
    both = 2 * count
    blocks = outer * chips
    steps = [0] + sorted(range(1, outer), key=lambda s: (min(s, outer - s), s))
    order = [(s, k) for s in steps for k in range(chips)]
    tile = 512
    wide_tiles = width // tile
    unit_tile = min(256, units)
    lines = 32
    bf16, f32 = jnp.bfloat16, jnp.float32
    mesh_id = pl.DeviceIdType.MESH

    def plan(phase):
        block_us, core_us, hop_us = 10.5, 1.0, 2.0
        free = {"tc": 0.0, "x": 0.0, "core": 0.0, "z": 0.0}
        done = {}
        tasks = {}

        def send(link, when, us):
            free[link] = max(free[link], when) + us
            return free[link] + hop_us

        def add(name, needs, us, after=None):
            tasks[name] = (needs, us, after)

        arrive = {}
        for i, s in enumerate(steps[1:]):
            arrive["z", s] = 15.0 + 13.0 * i
        for k in range(1, chips):
            arrive["x", 0, k] = send("x", 0.0, block_us)
        arrive["c", 0, 0] = send("core", 0.0, core_us)

        def zf(s):
            def then(now):
                for k in range(1, chips):
                    arrive["x", s, k] = send("x", now, block_us)
                arrive["c", s, 0] = send("core", now, core_us)

            return then

        def xf(s, k):
            def then(now):
                arrive["c", s, k] = send("core", now, core_us)

            return then

        def compute(u):
            def then(now):
                arrive["cr", u] = send("core", now, core_us)

            return then

        def cr(s, k):
            def then(now):
                if k:
                    arrive["xr", s, k] = send("x", now, block_us)

            return then

        def xr(s):
            def then(now):
                if s:
                    arrive["zr", s] = send("z", now, block_us) + 3.0

            return then

        for s in steps[1:]:
            add(("zf", s), [("at", ("z", s))], 0.3, zf(s))
        for s in steps:
            for k in range(1, chips):
                add(("xf", s, k), [("at", ("x", s, k))], 0.3, xf(s, k))
        for i, (s, k) in enumerate(order):
            needs = [("at", ("c", s, k))]
            if i >= 2:
                needs.append(("do", ("grads" if phase else "compute",) + order[i - 2]))
            add(("load", s, k), needs, 0.2, None)
            needs = [("do", ("load", s, k))]
            if i >= 2:
                needs.append(("do", ("cr",) + order[i - 2]))
            add(("compute", s, k), needs, 3.0, compute((s, k)))
            if phase:
                add(("grads", s, k), [("do", ("compute", s, k))], 3.5, None)
            add(("cr", s, k), [("at", ("cr", (s, k))), ("do", ("compute", s, k))], 0.6, cr(s, k))
        for s in steps:
            needs = [("do", ("cr", s, 0))] + [("at", ("xr", s, k)) for k in range(1, chips)]
            add(("xr", s), needs, 0.6, xr(s))
        for s in steps[1:]:
            add(("zr", s), [("at", ("zr", s)), ("do", ("xr", 0))], 0.6, None)
        if phase:
            needs = [("do", ("xr", s)) for s in steps]
            add(("write", 0), needs + [("do", ("grads",) + unit) for unit in order], 4.0, None)
        result = []
        now = 0.0
        while tasks:
            best = None
            for name, (needs, us, after) in tasks.items():
                ready = 0.0
                for kind, key in needs:
                    table = arrive if kind == "at" else done
                    if key not in table:
                        ready = None
                        break
                    ready = max(ready, table[key] + (1.0 if key[0] == "load" else 0.0))
                if ready is None:
                    continue
                ready = max(ready, now)
                rank = {"compute": 1, "grads": 2, "write": 3}.get(name[0], 0)
                if best is None or (ready, rank) < best[:2]:
                    best = (ready, rank, name)
            ready, _, name = best
            needs, us, after = tasks.pop(name)
            now = ready + us
            done[name] = now
            if after is not None:
                after(now)
            result.append(name)
        return result

    def kernel(
        rows_ref, resid_ref, cot_ref, gain_ref, wg, wu, wd,
        out_ref, dres_ref, gain_out, all_x, all_dm, grad_gate, grad_up, grad_down,
        xb, db, act, coef_gate, coef_up, d_gate, d_up, acc_gate, acc_up, acc_down, stage, stage_down,
        core_send, core_land, hold, keep, chip_send, chip_land, outer_send, outer_land, raw, d_mlp,
        s_outer, r_outer, s_chip, r_chip, s_core, r_core,
        s_core_sum, r_core_sum, s_chip_sum, r_chip_sum, s_outer_sum, r_outer_sum, local,
    ):
        g = Grid()
        core_peer = (g.dp_at, g.chip_at * 2 + 1 - g.core_at)

        def chip_peer(k):
            return (g.dp_at, lax.rem(g.chip_at + k + chips, chips) * 2 + g.core_at)

        def outer_peer(s):
            return (lax.rem(g.outer_at + s + outer, outer) * g.inner + g.inner_at, g.tensor_at)

        greet(
            [core_peer]
            + [chip_peer(k) for k in range(1, chips)]
            + [outer_peer(s) for s in range(1, outer)]
        )

        def remote(src, dst, send, recv, peer):
            return pltpu.make_async_remote_copy(
                src_ref=src, dst_ref=dst, send_sem=send, recv_sem=recv,
                device_id=peer, device_id_type=mesh_id,
            )

        def dot(a, b, contract):
            return lax.dot_general(a, b, (contract, ((), ())), preferred_element_type=f32)

        def looped(total, body):
            lax.fori_loop(0, total, lambda i, c: (body(i), c)[1], 0)

        def by_lines(body):
            looped(count // lines, lambda i: body(pl.ds(pl.multiple_of(i * lines, lines), lines)))

        def by_tiles(body):
            looped(wide_tiles, lambda i: body(pl.ds(pl.multiple_of(i * tile, tile), tile)))

        started = []

        def run(phase, source, everything, fetched, compute, grads, write):
            mine = pl.ds(0, count)
            theirs = pl.ds(count, count)
            copies = {}

            def start(key, copy):
                copy.start()
                copies[key] = copy
                started.append(copy)

            def at(s, k, half):
                return everything.at[s, k, half]

            def core_copy(s, k, src):
                start(
                    ("c", s, k),
                    remote(src, at(s, k, theirs), s_core.at[phase, s, k], r_core.at[phase, s, k], core_peer),
                )

            def chip_copy(s, k, src):
                start(
                    ("x", s, k),
                    remote(src, at(s, k, mine), s_chip.at[phase, s, k], r_chip.at[phase, s, k], chip_peer(k)),
                )

            for s in steps[1:]:
                start(
                    ("z", s),
                    remote(source, at(s, 0, mine), s_outer.at[phase, s], r_outer.at[phase, s], outer_peer(s)),
                )
            for k in range(1, chips):
                chip_copy(0, k, source)
            core_copy(0, 0, source)
            own = pltpu.make_async_copy(source, at(0, 0, mine), local.at[phase, 0, blocks])
            own.start()
            slots = {unit: i % 2 for i, unit in enumerate(order)}
            loads = {}
            sums = {}
            for task in plan(phase):
                name, s = task[:2]
                k = task[2] if len(task) > 2 else 0
                unit = s * chips + k
                if name == "zf":
                    copies["z", s].wait_recv()
                    for j in range(1, chips):
                        chip_copy(s, j, at(s, 0, mine))
                    core_copy(s, 0, at(s, 0, mine))
                elif name == "xf":
                    copies["x", s, k].wait_recv()
                    core_copy(s, k, at(s, k, mine))
                elif name == "load":
                    copies["c", s, k].wait_recv()
                    if (s, k) == (0, 0):
                        own.wait()
                    slot = slots[s, k]
                    loads[s, k] = []
                    for j, (src, dst) in enumerate(fetched):
                        copy = pltpu.make_async_copy(
                            src.at[s, k], dst.at[slot], local.at[phase, j, unit]
                        )
                        copy.start()
                        loads[s, k].append(copy)
                elif name == "compute":
                    for copy in loads[s, k]:
                        copy.wait()
                    i = order.index((s, k))
                    if i >= 2:
                        sums["core", order[i - 2]].wait_send()
                    slot = slots[s, k]

                    def send(slot=slot, unit=unit, s=s, k=k):
                        copy = remote(
                            core_send.at[slot], core_land.at[unit],
                            s_core_sum.at[phase, unit], r_core_sum.at[phase, unit], core_peer,
                        )
                        copy.start()
                        sums["core", (s, k)] = copy

                    compute(slot, unit, send)
                elif name == "grads":
                    grads(slots[s, k], unit)
                elif name == "write":
                    write()
                elif name == "cr":
                    sums["core", (s, k)].wait_recv()
                    slot = slots[s, k]
                    if k == 0:

                        def add_core(at_rows, s=s, slot=slot, unit=unit):
                            keep[s, at_rows] = hold[slot, at_rows] + core_land[unit, at_rows].astype(f32)

                        by_lines(add_core)
                    else:
                        there = s * (chips - 1) + k - 1

                        def add_core(at_rows, there=there, slot=slot, unit=unit):
                            total = hold[slot, at_rows] + core_land[unit, at_rows].astype(f32)
                            chip_send[there, at_rows] = total.astype(bf16)

                        by_lines(add_core)
                        copy = remote(
                            chip_send.at[there], chip_land.at[there],
                            s_chip_sum.at[phase, there], r_chip_sum.at[phase, there], chip_peer(-k),
                        )
                        copy.start()
                        sums["chip", (s, k)] = copy
                elif name == "xr":
                    for j in range(1, chips):
                        sums["chip", (s, j)].wait_recv()

                    def add_chip(at_rows, s=s):
                        total = keep[s, at_rows]
                        for j in range(1, chips):
                            total = total + chip_land[s * (chips - 1) + j - 1, at_rows].astype(f32)
                        if s == 0:
                            raw[at_rows] = total
                        else:
                            outer_send[s - 1, at_rows] = total.astype(bf16)

                    by_lines(add_chip)
                    if s:
                        copy = remote(
                            outer_send.at[s - 1], outer_land.at[s - 1],
                            s_outer_sum.at[phase, s], r_outer_sum.at[phase, s], outer_peer(-s),
                        )
                        copy.start()
                        sums["outer", s] = copy
                elif name == "zr":
                    sums["outer", s].wait_recv()

                    def add_outer(at_rows, s=s):
                        raw[at_rows] = raw[at_rows] + outer_land[s - 1, at_rows].astype(f32)

                    by_lines(add_outer)
            waited = [sums["core", unit] for unit in order[-2:]]
            waited += [copy for key, copy in sums.items() if key[0] != "core"]
            for copy in waited:
                copy.wait_send()
            for copy in started:
                copy.wait_send()
            started.clear()

        def forward(slot, unit, send):
            for j in range(units // unit_tile):
                cols = pl.ds(j * unit_tile, unit_tile)
                rows = xb[slot]
                gate = dot(rows, wg[:, cols], ((1,), (0,)))
                up = dot(rows, wu[:, cols], ((1,), (0,)))
                sigma = jax.nn.sigmoid(gate)
                silu = gate * sigma
                act[unit, :, cols] = (silu * up).astype(bf16)
                coef_up[unit, :, cols] = silu.astype(bf16)
                coef_gate[unit, :, cols] = (up * sigma * (1.0 + gate * (1.0 - sigma))).astype(bf16)

            def down(cols):
                part_sum = dot(act[unit], wd[:, cols], ((1,), (0,)))
                hold[slot, :, cols] = part_sum[:count]
                core_send[slot, :, cols] = part_sum[count:].astype(bf16)

            by_tiles(down)
            send()

        def between():
            def lines_of(i, total):
                at_rows = pl.ds(pl.multiple_of(i * lines, lines), lines)
                value = raw[at_rows]
                scale = lax.rsqrt(jnp.mean(value * value, axis=1, keepdims=True) + norm_eps)
                hat = value * scale
                gain_row = gain_ref[...]
                out_ref[at_rows] = (resid_ref[at_rows] + hat * gain_row).astype(bf16)
                top = cot_ref[at_rows].astype(f32)
                upstream = top * gain_row
                inner = jnp.mean(upstream * hat, axis=1, keepdims=True)
                d_mlp[at_rows] = (scale * (upstream - hat * inner)).astype(bf16)
                return total + jnp.sum(top * hat, axis=0, keepdims=True)

            gain_out[...] = lax.fori_loop(
                0, count // lines, lines_of, jnp.zeros((1, width), f32)
            )

        def backward(slot, unit, send):
            for j in range(units // unit_tile):
                cols = pl.ds(j * unit_tile, unit_tile)
                d_act = dot(db[slot], wd[cols, :], ((1,), (1,)))
                d_gate[slot, :, cols] = (d_act * coef_gate[unit, :, cols].astype(f32)).astype(bf16)
                d_up[slot, :, cols] = (d_act * coef_up[unit, :, cols].astype(f32)).astype(bf16)

            def into(cols):
                part_sum = dot(d_gate[slot], wg[cols, :], ((1,), (1,)))
                part_sum = part_sum + dot(d_up[slot], wu[cols, :], ((1,), (1,)))
                hold[slot, :, cols] = part_sum[:count]
                core_send[slot, :, cols] = part_sum[count:].astype(bf16)

            by_tiles(into)
            send()

        def weight_grads(slot, unit):
            first = unit == order[0][0] * chips + order[0][1]

            def grads(cols):
                def put_sum(ref, where, value):
                    if first:
                        ref[where] = value
                    else:
                        ref[where] = ref[where] + value

                rows = xb[slot, :, cols]
                put_sum(acc_gate, (cols, slice(None)), dot(rows, d_gate[slot], ((0,), (0,))))
                put_sum(acc_up, (cols, slice(None)), dot(rows, d_up[slot], ((0,), (0,))))
                put_sum(
                    acc_down, (slice(None), cols), dot(act[unit], db[slot, :, cols], ((0,), (0,)))
                )

            by_tiles(grads)

        def write_grads():
            def write(i, c):
                cols = pl.ds(pl.multiple_of(i * tile, tile), tile)
                stage[0] = acc_gate[cols, :].astype(bf16)
                stage[1] = acc_up[cols, :].astype(bf16)
                stage_down[...] = acc_down[:, cols].astype(bf16)
                copies = [
                    pltpu.make_async_copy(stage.at[0], grad_gate.at[cols], local.at[1, 2, 0]),
                    pltpu.make_async_copy(stage.at[1], grad_up.at[cols], local.at[1, 2, 1]),
                    pltpu.make_async_copy(stage_down, grad_down.at[:, cols], local.at[1, 2, 2]),
                ]
                for copy in copies:
                    copy.start()
                for copy in copies:
                    copy.wait()
                return c

            lax.fori_loop(0, wide_tiles, write, 0)

        run(0, rows_ref, all_x, [(all_x, xb)], forward, None, None)
        between()
        run(1, d_mlp, all_dm, [(all_dm, db), (all_x, xb)], backward, weight_grads, write_grads)

        def close(at_rows):
            dres_ref[at_rows] = raw[at_rows] + cot_ref[at_rows].astype(f32)

        by_lines(close)

    def held_in(space):
        return pl.BlockSpec(memory_space=space)

    shape = jax.ShapeDtypeStruct
    anywhere, near = held_in(pl.ANY), held_in(pltpu.VMEM)
    sems = pltpu.SemaphoreType.DMA
    links = outer * (chips - 1)
    flops = 2 * 9 * both * blocks * width * units
    results = pl.pallas_call(
        kernel,
        out_shape=(
            shape((count, width), bf16),
            shape((count, width), f32),
            shape((1, width), f32),
            shape((outer, chips, both, width), bf16),
            shape((outer, chips, both, width), bf16),
            shape((width, units), bf16),
            shape((width, units), bf16),
            shape((units, width), bf16),
        ),
        in_specs=[anywhere] + [near] * 6,
        out_specs=(near, near, near) + (anywhere,) * 5,
        scratch_shapes=[
            pltpu.VMEM((2, both, width), bf16),
            pltpu.VMEM((2, both, width), bf16),
            pltpu.VMEM((blocks, both, units), bf16),
            pltpu.VMEM((blocks, both, units), bf16),
            pltpu.VMEM((blocks, both, units), bf16),
            pltpu.VMEM((2, both, units), bf16),
            pltpu.VMEM((2, both, units), bf16),
            pltpu.VMEM((width, units), f32),
            pltpu.VMEM((width, units), f32),
            pltpu.VMEM((units, width), f32),
            pltpu.VMEM((2, tile, units), bf16),
            pltpu.VMEM((units, tile), bf16),
            pltpu.VMEM((2, count, width), bf16),
            pltpu.VMEM((blocks, count, width), bf16),
            pltpu.VMEM((2, count, width), f32),
            pltpu.VMEM((outer, count, width), f32),
            pltpu.VMEM((links, count, width), bf16),
            pltpu.VMEM((links, count, width), bf16),
            pltpu.VMEM((outer - 1, count, width), bf16),
            pltpu.VMEM((outer - 1, count, width), bf16),
            pltpu.VMEM((count, width), f32),
            pltpu.VMEM((count, width), bf16),
            sems((2, outer)),
            sems((2, outer)),
            sems((2, outer, chips)),
            sems((2, outer, chips)),
            sems((2, outer, chips)),
            sems((2, outer, chips)),
            sems((2, blocks)),
            sems((2, blocks)),
            sems((2, links)),
            sems((2, links)),
            sems((2, outer)),
            sems((2, outer)),
            sems((2, 3, blocks + 1)),
        ],
        compiler_params=pltpu.CompilerParams(
            collective_id=2, has_side_effects=True, vmem_limit_bytes=60 * 2**20
        ),
        cost_estimate=pl.CostEstimate(flops=flops, bytes_accessed=64 * 2**20, transcendentals=0),
    )(rows_low, resid, cotangent, gain, unit_gate, unit_up, unit_down)
    return results[:3] + results[5:]


def adam_kernel(w_ref, m_ref, v_ref, g_ref, *rest):
    scale_ref = rest[0] if len(rest) == 5 else None
    w_out, m_out, v_out, c_out = rest[-4:]
    grad = g_ref[...].astype(jnp.float32)
    new, first, second = adam_step(
        w_ref[...], grad, m_ref[...], v_ref[...], rate_matrix, weight_decay
    )
    if scale_ref is not None:
        new = new * scale_ref[...]
    w_out[...] = new
    m_out[...] = first
    v_out[...] = second
    c_out[...] = new.astype(jnp.bfloat16)


def adam_call(param, grad, first, second, scale=None):
    shape = param.shape
    flat = [v.reshape(-1, shape[-1]) for v in (param, first, second, grad)]
    rows, width = flat[0].shape
    block = min(rows, max(16, (1 << 17) // width))
    spec = pl.BlockSpec((block, width), lambda k: (k, 0))
    specs = [spec] * 4
    if scale is not None:
        per = shape[1] // block
        flat.append(scale)
        specs.append(pl.BlockSpec((None, 1, width), lambda k: (k // per, 0, 0)))
    outs = [jax.ShapeDtypeStruct((rows, width), jnp.float32)] * 3
    outs.append(jax.ShapeDtypeStruct((rows, width), jnp.bfloat16))
    size = rows * width
    result = pl.pallas_call(
        adam_kernel,
        grid=(rows // block,),
        in_specs=specs,
        out_specs=[spec] * 4,
        out_shape=outs,
        cost_estimate=pl.CostEstimate(
            flops=20 * size, bytes_accessed=28 * size, transcendentals=2 * size
        ),
        compiler_params=pltpu.CompilerParams(vmem_limit_bytes=32 * 2**20),
    )(*flat)
    return [v.reshape(shape) for v in result]


def local(
    tokens,
    cotangent,
    block_ids,
    w_qkv,
    m_qkv,
    v_qkv,
    w_out,
    m_out,
    v_out,
    w_gu,
    m_gu,
    v_gu,
    w_down,
    m_down,
    v_down,
    gains,
    gain_m,
    gain_v,
):
    grid = Grid()
    local_x = tokens[0]
    gain_count = gains.shape[0]
    low_gains = jnp.pad(gains.astype(jnp.bfloat16), ((0, 16 - gain_count), (0, 0)))
    full_qkv, full_gains, seq_x = path_gather(w_qkv.astype(jnp.bfloat16), low_gains, local_x)
    gain_rows = jnp.swapaxes(full_gains[:, :gain_count], 0, 1).reshape(gain_count, -1)
    gain_rows = gain_rows.astype(jnp.float32)
    shards = (
        w_out.astype(jnp.bfloat16),
        w_gu[0].astype(jnp.bfloat16),
        w_gu[1].astype(jnp.bfloat16),
        w_down.astype(jnp.bfloat16),
    )
    full_qkv, shards = lax.optimization_barrier((full_qkv, shards))
    full_out = width_gather(grid, shards[0])
    unit_pieces = [
        unit_gather(grid, shards[1], 0),
        unit_gather(grid, shards[2], 0),
        unit_gather(grid, shards[3], 1),
    ]
    model_width = local_x.shape[1]
    length = seq_x.shape[0]
    span = full_qkv.shape[2]
    heads_here = span // HEAD
    offset = lax.axis_index("tensor") * span
    projected = jnp.einsum("sd,cde->cse", seq_x, full_qkv, preferred_element_type=jnp.float32)
    queries, keys, values = (projected[0], projected[1], projected[2])
    q_square, k_square = lax.psum(
        (jnp.sum(queries * queries, axis=1), jnp.sum(keys * keys, axis=1)), "tensor"
    )
    q_scale = lax.rsqrt(q_square / model_width + norm_eps)[:, None]
    k_scale = lax.rsqrt(k_square / model_width + norm_eps)[:, None]
    q_hat = queries * q_scale
    k_hat = keys * k_scale
    q_gain = lax.dynamic_slice_in_dim(gain_rows[0], offset, span)
    k_gain = lax.dynamic_slice_in_dim(gain_rows[1], offset, span)
    cosine, sine = rope_tables(length, HEAD)

    def rotary(value):
        shaped = value.reshape(length, heads_here, HEAD)
        return shaped * cosine + rotate_fwd(shaped) * sine

    def unrotary(grad):
        return (grad * cosine + rotate_back(grad * sine)).reshape(length, span)

    q_low = rotary(q_hat * q_gain).astype(jnp.bfloat16)
    k_low = rotary(k_hat * k_gain).astype(jnp.bfloat16)
    v_low = values.astype(jnp.bfloat16).reshape(length, heads_here, HEAD)
    blocks = block_ids[0]
    block_rows = min(512, length)
    block_count = length // block_rows
    scale = HEAD ** (-0.5)
    starts = jnp.arange(block_count, dtype=jnp.int32) * block_rows

    def scores_of(start):
        q_part = lax.dynamic_slice_in_dim(q_low, start, block_rows, 0)
        b_part = lax.dynamic_slice_in_dim(blocks, start, block_rows, 0)
        raw = jnp.einsum("qhd,khd->hqk", q_part, k_low, preferred_element_type=jnp.float32) * scale
        allowed = blocks[None, None, :] <= b_part[None, :, None]
        return (jnp.where(allowed, raw, masked_value), q_part)

    def forward_block(start):
        masked, q_part = scores_of(start)
        top = jnp.max(masked, axis=2, keepdims=True)
        weight = jnp.exp(masked - top)
        total = jnp.sum(weight, axis=2, keepdims=True)
        probs = (weight / total).astype(jnp.bfloat16)
        context = jnp.einsum("hqk,khd->qhd", probs, v_low, preferred_element_type=jnp.float32)
        return (
            context.astype(jnp.bfloat16),
            (top + jnp.log(total))[:, :, 0],
            jnp.max(top[:, :, 0], axis=1),
        )

    context_low, log_total, block_top = lax.map(forward_block, starts)
    context_low = context_low.reshape(length, span)
    head_top = jnp.max(block_top, axis=0)
    attn_raw = sequence_scatter(
        grid, jnp.dot(context_low, full_out, preferred_element_type=jnp.float32)
    )
    x_float = local_x.astype(jnp.float32)
    o_scale = lax.rsqrt(jnp.mean(attn_raw * attn_raw, axis=1, keepdims=True) + norm_eps)
    attn_hat = attn_raw * o_scale
    resid = x_float + attn_hat * gain_rows[2]
    rows_low, unit_pieces = lax.optimization_barrier((resid.astype(jnp.bfloat16), unit_pieces))
    output, d_resid, gain_last, grad_gate, grad_up, grad_down = unit_kernel_call(
        rows_low,
        resid,
        cotangent[0],
        gain_rows[3:4],
        inner_join(grid, unit_pieces[0], 0),
        inner_join(grid, unit_pieces[1], 0),
        inner_join(grid, unit_pieces[2], 1),
    )
    part_down = unit_scatter(grid, grad_down, 1)
    part_gate = unit_scatter(grid, grad_gate, 0)
    part_up = unit_scatter(grid, grad_up, 0)
    gain_attn = jnp.sum(d_resid * attn_hat, axis=0)
    d_attn = norm_back(o_scale, attn_hat, d_resid * gain_rows[2]).astype(jnp.bfloat16)
    seq_do = sequence_gather(grid, d_attn)
    grad_out = jnp.einsum("se,sd->ed", context_low, seq_do, preferred_element_type=jnp.float32)
    part_out = width_scatter(grid, grad_out.astype(jnp.bfloat16))
    d_context = jnp.einsum("sd,ed->se", seq_do, full_out, preferred_element_type=jnp.float32)
    d_context = d_context.astype(jnp.bfloat16).reshape(length, heads_here, HEAD)

    def backward_block(carry, item):
        key_acc, value_acc = carry
        start, log_part = item
        masked, q_part = scores_of(start)
        probs = jnp.exp(masked - log_part[:, :, None])
        dc_part = lax.dynamic_slice_in_dim(d_context, start, block_rows, 0)
        d_probs = jnp.einsum("qhd,khd->hqk", dc_part, v_low, preferred_element_type=jnp.float32)
        inner = jnp.sum(probs * d_probs, axis=2, keepdims=True)
        d_scores = (probs * (d_probs - inner)).astype(jnp.bfloat16)
        d_query = (
            jnp.einsum("hqk,khd->qhd", d_scores, k_low, preferred_element_type=jnp.float32) * scale
        )
        key_acc = (
            key_acc
            + jnp.einsum("hqk,qhd->khd", d_scores, q_part, preferred_element_type=jnp.float32)
            * scale
        )
        value_acc = value_acc + jnp.einsum(
            "hqk,qhd->khd", probs.astype(jnp.bfloat16), dc_part, preferred_element_type=jnp.float32
        )
        return ((key_acc, value_acc), d_query)

    empty = jnp.zeros((length, heads_here, HEAD), jnp.float32)
    (d_krot, d_values), d_qrot = lax.scan(backward_block, (empty, empty), (starts, log_total))
    d_qrot = d_qrot.reshape(length, heads_here, HEAD)
    d_qnorm = unrotary(d_qrot)
    d_knorm = unrotary(d_krot)
    head_gains = jnp.stack([jnp.sum(d_qnorm * q_hat, axis=0), jnp.sum(d_knorm * k_hat, axis=0)])
    placed = lax.dynamic_update_slice(
        jnp.zeros((2, model_width), jnp.float32), head_gains, (0, offset)
    )
    gain_terms = jnp.concatenate([placed, jnp.stack([gain_attn, gain_last[0]])], axis=0)
    dq_hat = d_qnorm * q_gain
    dk_hat = d_knorm * k_gain
    q_inner, k_inner = lax.psum(
        (jnp.sum(dq_hat * q_hat, axis=1), jnp.sum(dk_hat * k_hat, axis=1)), "tensor"
    )
    part_gains = gains_scatter(grid, gain_terms)
    d_query = q_scale * (dq_hat - q_hat * (q_inner / model_width)[:, None])
    d_key = k_scale * (dk_hat - k_hat * (k_inner / model_width)[:, None])
    d_qkv = jnp.stack([d_query, d_key, d_values.reshape(length, span)]).astype(jnp.bfloat16)
    grad_qkv = jnp.einsum("sd,cse->cde", seq_x, d_qkv, preferred_element_type=jnp.float32)
    part_qkv = path_scatter(grad_qkv.astype(jnp.bfloat16))
    grad_tokens = d_resid + sequence_scatter(
        grid, jnp.einsum("cse,cde->sd", d_qkv, full_qkv, preferred_element_type=jnp.float32)
    )
    for bit in bits(grid.dp):
        head_top = jnp.maximum(head_top, grid.across(head_top, "dp", bit))
    factor = clip_tau / jnp.maximum(head_top, clip_tau)
    column = jnp.repeat(jnp.sqrt(factor), HEAD)
    column_scale = jnp.stack([column, column, jnp.ones_like(column)])[:, None, :]
    new_qkv, new_m_qkv, new_v_qkv, copy_qkv = adam_call(
        w_qkv, part_qkv, m_qkv, v_qkv, column_scale
    )
    new_out, new_m_out, new_v_out, copy_out = adam_call(w_out, part_out, m_out, v_out)
    new_gu, new_m_gu, new_v_gu, copy_gu = adam_call(
        w_gu, jnp.stack([part_gate, part_up]), m_gu, v_gu
    )
    new_down, new_m_down, new_v_down, copy_down = adam_call(w_down, part_down, m_down, v_down)
    new_gains, new_gain_m, new_gain_v = adam_step(gains, part_gains, gain_m, gain_v, rate_gain, 0.0)
    return (
        output[None],
        grad_tokens[None],
        new_qkv,
        new_m_qkv,
        new_v_qkv,
        copy_qkv,
        new_out,
        new_m_out,
        new_v_out,
        copy_out,
        new_gu,
        new_m_gu,
        new_v_gu,
        copy_gu,
        new_down,
        new_m_down,
        new_v_down,
        copy_down,
        new_gains,
        new_gain_m,
        new_gain_v,
        factor,
    )


def solution(mesh):
    return jax.shard_map(
        local,
        mesh=mesh,
        in_specs=(
            P("dp", "tensor", None),
            P("dp", "tensor", None),
            P("dp", None),
            P(None, "dp", "tensor"),
            P(None, "dp", "tensor"),
            P(None, "dp", "tensor"),
            P("tensor", "dp"),
            P("tensor", "dp"),
            P("tensor", "dp"),
            P(None, "dp", "tensor"),
            P(None, "dp", "tensor"),
            P(None, "dp", "tensor"),
            P("tensor", "dp"),
            P("tensor", "dp"),
            P("tensor", "dp"),
            P(None, "dp"),
            P(None, "dp"),
            P(None, "dp"),
        ),
        out_specs=(
            P("dp", "tensor", None),
            P("dp", "tensor", None),
            P(None, "dp", "tensor"),
            P(None, "dp", "tensor"),
            P(None, "dp", "tensor"),
            P(None, "dp", "tensor"),
            P("tensor", "dp"),
            P("tensor", "dp"),
            P("tensor", "dp"),
            P("tensor", "dp"),
            P(None, "dp", "tensor"),
            P(None, "dp", "tensor"),
            P(None, "dp", "tensor"),
            P(None, "dp", "tensor"),
            P("tensor", "dp"),
            P("tensor", "dp"),
            P("tensor", "dp"),
            P("tensor", "dp"),
            P(None, "dp"),
            P(None, "dp"),
            P(None, "dp"),
            P("tensor"),
        ),
        check_vma=False,
    )
```

```python
import functools

import jax
import jax.numpy as jnp
from jax import lax
from jax.experimental import pallas as pl
from jax.experimental.pallas import tpu as pltpu
from jax.sharding import PartitionSpec as P

HEAD = 128
STEP = 5


norm_eps = 1e-06
rope_base = 500000.0
beta_one = 0.9
beta_two = 0.95
rate_matrix = 0.01
rate_gain = 0.6
weight_decay = 0.1
adam_eps = 1e-08
clip_tau = 9.0
masked_value = -1e30


def rope_tables(length, size):
    half = size // 2
    freq = rope_base ** (-(jnp.arange(half, dtype=jnp.float32) * 2.0 / size))
    angle = jnp.arange(length, dtype=jnp.float32)[:, None] * freq[None, :]
    angle = jnp.concatenate([angle, angle], axis=1)
    return (jnp.cos(angle)[:, None, :], jnp.sin(angle)[:, None, :])


def rotate_fwd(value):
    half = value.shape[-1] // 2
    return jnp.concatenate([-value[..., half:], value[..., :half]], axis=-1)


def rotate_back(value):
    half = value.shape[-1] // 2
    return jnp.concatenate([value[..., half:], -value[..., :half]], axis=-1)


def adam_step(param, grad, first, second, rate, decay):
    first = beta_one * first + (1.0 - beta_one) * grad
    second = beta_two * second + (1.0 - beta_two) * grad * grad
    fix_one = 1.0 - beta_one**STEP
    fix_two = 1.0 - beta_two**STEP
    update = first / fix_one / (jnp.sqrt(second / fix_two) + adam_eps)
    return (param - rate * (update + decay * param), first, second)


def norm_back(scale_factor, normed, upstream):
    inner = jnp.mean(upstream * normed, axis=1, keepdims=True)
    return scale_factor * (upstream - normed * inner)


class Grid:
    def __init__(self):
        self.dp = lax.axis_size("dp")
        self.tensor = lax.axis_size("tensor")
        self.inner = 1
        while self.inner * self.inner * 4 <= self.dp:
            self.inner *= 2
        self.outer = self.dp // self.inner
        self.chips = self.tensor // 2
        self.dp_at = lax.axis_index("dp")
        self.tensor_at = lax.axis_index("tensor")
        self.inner_at = self.dp_at % self.inner
        self.chip_at = self.tensor_at // 2
        self.core_at = self.tensor_at % 2
        self.outer_at = self.dp_at // self.inner

    def path_of(self, index):
        column, row = index // self.inner, index % self.inner
        return row * self.outer + column + (row % 2) * (self.outer - 1 - 2 * column)

    def index_of(self, place):
        row, column = place // self.outer, place % self.outer
        return (column + (row % 2) * (self.outer - 1 - 2 * column)) * self.inner + row

    def to_outer(self, value, step):
        n, m = self.outer, self.inner
        pairs = [(a * m + b, (a + step) % n * m + b) for a in range(n) for b in range(m)]
        return lax.ppermute(value, "dp", pairs)

    def to_inner(self, value, step):
        n, m = self.outer, self.inner
        pairs = [(a * m + b, a * m + (b + step) % m) for a in range(n) for b in range(m)]
        return lax.ppermute(value, "dp", pairs)

    def to_chip(self, value, step):
        n = self.chips
        pairs = [(a * 2 + b, (a + step) % n * 2 + b) for a in range(n) for b in range(2)]
        return lax.ppermute(value, "tensor", pairs)

    def to_core(self, value):
        pairs = [(a * 2 + b, a * 2 + 1 - b) for a in range(self.chips) for b in range(2)]
        return lax.ppermute(value, "tensor", pairs)

    def across(self, value, axis, bit):
        count = lax.axis_size(axis)
        return lax.ppermute(value, axis, [(i, i ^ bit) for i in range(count)])


def bits(count):
    return [1 << k for k in range(count.bit_length() - 1)]


def part(value, axis, index, size):
    return lax.dynamic_slice_in_dim(value, index * size, size, axis)


def put(whole, piece, axis, index):
    return lax.dynamic_update_slice_in_dim(whole, piece, index * piece.shape[axis], axis)


def low_sum(*terms):
    total = terms[0].astype(jnp.float32)
    for term in terms[1:]:
        total = total + term.astype(jnp.float32)
    return total.astype(jnp.bfloat16)


def greet(peers):
    barrier = pltpu.get_barrier_semaphore()
    for peer in peers:
        pl.semaphore_signal(barrier, inc=1, device_id=peer, device_id_type=pl.DeviceIdType.MESH)
    pl.semaphore_wait(barrier, len(peers))


def path_gather(shard, flat, gains, rows):
    grid = Grid()
    n, chips, tensor = grid.dp, grid.chips, grid.tensor
    lead, deep, wide = shard.shape
    half = deep // 2
    tall, thin = flat.shape
    part_tall = tall // 2
    count = rows.shape[0]
    ring = 2 * lead + 3

    def kernel(
        shard_ref, flat_ref, gains_ref, rows_ref, full, full_flat, full_gains, sequence,
        sends, lands, row_sends, row_lands, own,
    ):
        g = Grid()
        dp_at, t_at = g.dp_at, g.tensor_at
        chip_at, core_at = t_at // 2, t_at % 2
        place = g.path_of(dp_at)
        after = g.index_of(lax.rem(place + 1, n))
        before = g.index_of(lax.rem(place + n - 1, n))
        core_peer = (dp_at, chip_at * 2 + 1 - core_at)
        chip_peers = [
            (dp_at, lax.rem(chip_at + k, chips) * 2 + core_at) for k in range(1, chips)
        ]
        greet([(after, t_at), (before, t_at), core_peer] + chip_peers)

        def views(item, index):
            if item == ring - 1:
                return 1, gains_ref, full_gains.at[index]
            if item >= 2 * lead:
                side = item - 2 * lead
                span = pl.ds(side * part_tall, part_tall)
                cols = pl.ds(pl.multiple_of(index * thin, thin), thin)
                return 1 - 2 * side, flat_ref.at[span], full_flat.at[span, cols]
            side, c = item // lead, item % lead
            span = pl.ds(pl.multiple_of(index * deep + side * half, half), half)
            return 1 - 2 * side, shard_ref.at[c, pl.ds(side * half, half)], full.at[c, span]

        def hop(step, item):
            way = views(item, 0)[0]
            index = g.index_of(lax.rem(place - way * step + n, n))
            _, source, target = views(item, index)
            return pltpu.make_async_remote_copy(
                src_ref=source if step == 0 else target,
                dst_ref=target,
                send_sem=sends.at[step, item],
                recv_sem=lands.at[step, item],
                device_id=(after if way == 1 else before, t_at),
                device_id_type=pl.DeviceIdType.MESH,
            )

        def rows_at(index):
            return sequence.at[pl.ds(pl.multiple_of(index * count, count), count)]

        def row_copy(slot, index, peer, first):
            return pltpu.make_async_remote_copy(
                src_ref=rows_ref if first else rows_at(index),
                dst_ref=rows_at(index),
                send_sem=row_sends.at[slot],
                recv_sem=row_lands.at[slot],
                device_id=peer,
                device_id_type=pl.DeviceIdType.MESH,
            )

        order = [c + side * lead for c in range(lead) for side in (0, 1)]
        order += list(range(2 * lead, ring))
        hops = {}
        for item in order:
            hops[0, item] = hop(0, item)
            hops[0, item].start()
        moves = []
        for k in range(1, chips):
            moves.append(row_copy(k - 1, t_at, chip_peers[k - 1], True))
            moves[-1].start()
        mine = row_copy(chips - 1, t_at, core_peer, True)
        mine.start()
        keep = [
            pltpu.make_async_copy(
                shard_ref, full.at[:, pl.ds(pl.multiple_of(dp_at * deep, deep), deep)], own.at[0]
            ),
            pltpu.make_async_copy(gains_ref, full_gains.at[dp_at], own.at[1]),
            pltpu.make_async_copy(rows_ref, rows_at(t_at), own.at[2]),
            pltpu.make_async_copy(
                flat_ref, full_flat.at[:, pl.ds(pl.multiple_of(dp_at * thin, thin), thin)], own.at[3]
            ),
        ]
        for copy in keep:
            copy.start()
        passed = []
        for step in range(1, n - 1):
            for item in order:
                hops[step - 1, item].wait_recv()
                hops[step, item] = hop(step, item)
                hops[step, item].start()
            if step <= chips - 1:
                moves[step - 1].wait_recv()
                source = lax.rem(chip_at - step + chips, chips) * 2 + core_at
                passed.append(row_copy(chips - 1 + step, source, core_peer, False))
                passed[-1].start()
        for item in order:
            hops[n - 2, item].wait_recv()
        mine.wait_recv()
        for copy in passed:
            copy.wait_recv()
        for key in hops:
            hops[key].wait_send()
        for copy in moves + [mine] + passed:
            copy.wait_send()
        for copy in keep:
            copy.wait()

    bf16 = jnp.bfloat16
    return pl.pallas_call(
        kernel,
        out_shape=(
            jax.ShapeDtypeStruct((lead, deep * n, wide), bf16),
            jax.ShapeDtypeStruct((tall, thin * n), bf16),
            jax.ShapeDtypeStruct((n,) + gains.shape, bf16),
            jax.ShapeDtypeStruct((count * tensor, rows.shape[1]), bf16),
        ),
        in_specs=[pl.BlockSpec(memory_space=pl.ANY)] * 4,
        out_specs=(pl.BlockSpec(memory_space=pl.ANY),) * 4,
        scratch_shapes=[
            pltpu.SemaphoreType.DMA((n - 1, ring)),
            pltpu.SemaphoreType.DMA((n - 1, ring)),
            pltpu.SemaphoreType.DMA((2 * chips - 1,)),
            pltpu.SemaphoreType.DMA((2 * chips - 1,)),
            pltpu.SemaphoreType.DMA((4,)),
        ],
        compiler_params=pltpu.CompilerParams(collective_id=0, has_side_effects=True),
    )(shard, flat, gains, rows)


def path_scatter(whole, flat, gains):
    grid = Grid()
    n, chips = grid.dp, grid.chips
    lead, total, wide = whole.shape
    deep = total // n
    half = deep // 2
    tall, thin = flat.shape[0], flat.shape[1] // n
    part_tall = tall // 2
    ring = 2 * lead + 3
    gain_item = ring - 1
    bf16, f32 = jnp.bfloat16, jnp.float32

    def kernel(
        whole_ref, flat_ref, gains_ref, out_ref, flat_out, gains_out,
        land, land_flat, land_gain, own_gain, peer_gain, sends, lands, gain_sends, gain_lands,
    ):
        g = Grid()
        place = g.path_of(g.dp_at)
        after = g.index_of(lax.rem(place + 1, n))
        before = g.index_of(lax.rem(place + n - 1, n))
        core_peer = (g.dp_at, g.chip_at * 2 + 1 - g.core_at)
        chip_peers = [
            (g.dp_at, lax.rem(g.chip_at + k, chips) * 2 + g.core_at) for k in range(1, chips)
        ]
        greet([(after, g.tensor_at), (before, g.tensor_at), core_peer] + chip_peers)

        def way_of(item):
            if item == gain_item:
                return 1
            return 1 - 2 * (item - 2 * lead if item >= 2 * lead else item // lead)

        def own(item, away):
            index = g.index_of(lax.rem(place - way_of(item) * away + 2 * n, n))
            if item == gain_item:
                return gains_ref.at[index]
            if item >= 2 * lead:
                cols = pl.ds(pl.multiple_of(index * thin, thin), thin)
                return flat_ref.at[pl.ds((item - 2 * lead) * part_tall, part_tall), cols]
            side, c = item // lead, item % lead
            return whole_ref.at[c, pl.ds(pl.multiple_of(index * deep + side * half, half), half)]

        def landed(step, item):
            if item == gain_item:
                return land_gain.at[step]
            if item >= 2 * lead:
                return land_flat.at[step, item - 2 * lead]
            return land.at[step, item]

        def hop(step, item):
            return pltpu.make_async_remote_copy(
                src_ref=own(item, 1) if step == 0 else landed(step - 1, item),
                dst_ref=landed(step, item),
                send_sem=sends.at[step, item],
                recv_sem=lands.at[step, item],
                device_id=(after if way_of(item) == 1 else before, g.tensor_at),
                device_id_type=pl.DeviceIdType.MESH,
            )

        order = [gain_item] + [c + side * lead for c in range(lead) for side in (0, 1)]
        order += [2 * lead, 2 * lead + 1]
        hops = {}
        for item in order:
            hops[0, item] = hop(0, item)
            hops[0, item].start()
        for step in range(1, n):
            for item in order:
                hops[step - 1, item].wait_recv()
                here = landed(step - 1, item)
                summed = here[...].astype(f32) + own(item, step + 1)[...].astype(f32)
                if step < n - 1:
                    here[...] = summed.astype(here.dtype)
                    hops[step, item] = hop(step, item)
                    hops[step, item].start()
                elif item == gain_item:
                    own_gain[0] = summed
                elif item >= 2 * lead:
                    side = item - 2 * lead
                    flat_out[pl.ds(side * part_tall, part_tall)] = summed
                else:
                    side, c = item // lead, item % lead
                    out_ref[c, pl.ds(side * half, half)] = summed
            if step == n - 1:
                continue
        peers = [core_peer] + chip_peers
        copies = []
        for k, peer in enumerate(peers):
            level = min(k, 1)
            copies.append(
                pltpu.make_async_remote_copy(
                    src_ref=own_gain.at[level],
                    dst_ref=peer_gain.at[k],
                    send_sem=gain_sends.at[k],
                    recv_sem=gain_lands.at[k],
                    device_id=peer,
                    device_id_type=pl.DeviceIdType.MESH,
                )
            )
        copies[0].start()
        copies[0].wait_recv()
        own_gain[1] = own_gain[0] + peer_gain[0]
        for copy in copies[1:]:
            copy.start()
        for copy in copies[1:]:
            copy.wait_recv()
        result = own_gain[1]
        for k in range(1, len(peers)):
            result = result + peer_gain[k]
        gains_out[...] = result
        for key in hops:
            hops[key].wait_send()
        for copy in copies:
            copy.wait_send()

    near = pl.BlockSpec(memory_space=pltpu.VMEM)
    gain_shape = gains.shape[1:]
    return pl.pallas_call(
        kernel,
        out_shape=(
            jax.ShapeDtypeStruct((lead, deep, wide), f32),
            jax.ShapeDtypeStruct((tall, thin), f32),
            jax.ShapeDtypeStruct(gain_shape, f32),
        ),
        in_specs=[near] * 3,
        out_specs=(near,) * 3,
        scratch_shapes=[
            pltpu.VMEM((n - 1, 2 * lead, half, wide), bf16),
            pltpu.VMEM((n - 1, 2, part_tall, thin), bf16),
            pltpu.VMEM((n - 1,) + gain_shape, f32),
            pltpu.VMEM((2,) + gain_shape, f32),
            pltpu.VMEM((chips,) + gain_shape, f32),
            pltpu.SemaphoreType.DMA((n - 1, ring)),
            pltpu.SemaphoreType.DMA((n - 1, ring)),
            pltpu.SemaphoreType.DMA((chips,)),
            pltpu.SemaphoreType.DMA((chips,)),
        ],
        compiler_params=pltpu.CompilerParams(
            collective_id=1, has_side_effects=True, vmem_limit_bytes=40 * 2**20
        ),
    )(whole, flat, gains)


def unit_pieces_of(grid, shard):
    n, m = grid.outer, grid.inner
    units = shard.shape[2] // n
    first = []
    for step in range(n):
        piece = part(shard, 2, (grid.outer_at + step) % n, units)
        first.append(grid.to_outer(piece, step) if step else piece)
    pieces = [first]
    for _ in range(1, m):
        pieces.append([grid.to_inner(piece, 1) for piece in pieces[-1]])
    return pieces


def after(value, event):
    return lax.optimization_barrier((value, event))[0]


def inner_sum(grid, grads, event):
    others = [grid.to_inner(grads[j], j) for j in range(1, grid.inner)]
    return low_sum(grads[0], *after(others, event))


def outer_spread(grid, total):
    return [total[0]] + [grid.to_outer(total[step], step) for step in range(1, grid.outer)]


def sequence_scatter(grid, whole):
    rows = whole.shape[0] // grid.tensor
    shaped = whole.reshape(grid.chips, 2, rows, whole.shape[1])
    other = part(shaped, 1, 1 - grid.core_at, 1)[:, 0].astype(jnp.bfloat16)
    own = part(shaped, 1, grid.core_at, 1)[:, 0]
    pair = own + grid.to_core(other).astype(jnp.float32)
    total = part(pair, 0, grid.chip_at, 1)[0]
    for step in range(1, grid.chips):
        away = part(pair, 0, (grid.chip_at + step) % grid.chips, 1)[0].astype(jnp.bfloat16)
        total = total + grid.to_chip(away, step).astype(jnp.float32)
    return total


def sequence_gather(grid, rows):
    count, width = rows.shape
    whole = jnp.zeros((grid.chips, 2, count, width), rows.dtype)
    for step in range(grid.chips):
        here = grid.to_chip(rows, step) if step else rows
        chip = (grid.chip_at - step) % grid.chips
        for value, core in ((here, grid.core_at), (grid.to_core(here), 1 - grid.core_at)):
            whole = lax.dynamic_update_slice(whole, value[None, None], (chip, core, 0, 0))
    return whole.reshape(grid.tensor * count, width)


def unit_kernel_call(rows_low, resid, cotangent, gain, pieces):
    grid = Grid()
    outer, chips = grid.outer, grid.chips
    count, width = rows_low.shape
    units = pieces[0][0].shape[2]
    slab = pieces[0][0].shape[1]
    inner = grid.inner
    flat_pieces = [piece for row in pieces for piece in row]
    parts = len(flat_pieces)
    both = 2 * count
    blocks = outer * chips
    steps = [0] + sorted(range(1, outer), key=lambda s: (min(s, outer - s), s))
    order = [(s, k) for s in steps for k in range(chips)]
    tile = 512
    wide_tiles = width // tile
    unit_tile = min(256, units)
    lines = 32
    bf16, f32 = jnp.bfloat16, jnp.float32
    mesh_id = pl.DeviceIdType.MESH

    def plan(phase):
        block_us, core_us, hop_us = 10.5, 1.0, 2.0
        free = {"tc": 0.0, "x": 0.0, "core": 0.0, "z": 0.0}
        done = {}
        tasks = {}

        def send(link, when, us):
            free[link] = max(free[link], when) + us
            return free[link] + hop_us

        def add(name, needs, us, after=None):
            tasks[name] = (needs, us, after)

        arrive = {}
        for i, s in enumerate(steps[1:]):
            arrive["z", s] = 15.0 + 13.0 * i
        for k in range(1, chips):
            arrive["x", 0, k] = send("x", 0.0, block_us)
        arrive["c", 0, 0] = send("core", 0.0, core_us)

        def zf(s):
            def then(now):
                for k in range(1, chips):
                    arrive["x", s, k] = send("x", now, block_us)
                arrive["c", s, 0] = send("core", now, core_us)

            return then

        def xf(s, k):
            def then(now):
                arrive["c", s, k] = send("core", now, core_us)

            return then

        def compute(u):
            def then(now):
                arrive["cr", u] = send("core", now, core_us)

            return then

        def cr(s, k):
            def then(now):
                if k:
                    arrive["xr", s, k] = send("x", now, block_us)

            return then

        def xr(s):
            def then(now):
                if s:
                    arrive["zr", s] = send("z", now, block_us) + 3.0

            return then

        for s in steps[1:]:
            add(("zf", s), [("at", ("z", s))], 0.3, zf(s))
        for s in steps:
            for k in range(1, chips):
                add(("xf", s, k), [("at", ("x", s, k))], 0.3, xf(s, k))
        for i, (s, k) in enumerate(order):
            needs = [("at", ("c", s, k))]
            if i >= 2:
                needs.append(("do", ("grads" if phase else "compute",) + order[i - 2]))
            add(("load", s, k), needs, 0.2, None)
            needs = [("do", ("load", s, k))]
            if i >= 2:
                needs.append(("do", ("cr",) + order[i - 2]))
            add(("compute", s, k), needs, 3.0, compute((s, k)))
            if phase:
                add(("grads", s, k), [("do", ("compute", s, k))], 3.5, None)
            add(("cr", s, k), [("at", ("cr", (s, k))), ("do", ("compute", s, k))], 0.6, cr(s, k))
        for s in steps:
            needs = [("do", ("cr", s, 0))] + [("at", ("xr", s, k)) for k in range(1, chips)]
            add(("xr", s), needs, 0.6, xr(s))
        for s in steps[1:]:
            add(("zr", s), [("at", ("zr", s)), ("do", ("xr", 0))], 0.6, None)
        if phase:
            needs = [("do", ("xr", s)) for s in steps]
            add(("write", 0), needs + [("do", ("grads",) + unit) for unit in order], 4.0, None)
        result = []
        now = 0.0
        while tasks:
            best = None
            for name, (needs, us, after) in tasks.items():
                ready = 0.0
                for kind, key in needs:
                    table = arrive if kind == "at" else done
                    if key not in table:
                        ready = None
                        break
                    ready = max(ready, table[key] + (1.0 if key[0] == "load" else 0.0))
                if ready is None:
                    continue
                ready = max(ready, now)
                rank = {"compute": 1, "grads": 2, "write": 3}.get(name[0], 0)
                if best is None or (ready, rank) < best[:2]:
                    best = (ready, rank, name)
            ready, _, name = best
            needs, us, after = tasks.pop(name)
            now = ready + us
            done[name] = now
            if after is not None:
                after(now)
            result.append(name)
        return result

    def kernel(
        *refs
    ):
        piece_refs = refs[:parts]
        rows_ref, resid_ref, cot_ref, gain_ref = refs[parts : parts + 4]
        out_ref, dres_ref, gain_out, all_x, all_dm = refs[parts + 4 : parts + 9]
        grad_refs = refs[parts + 9 : parts + 9 + 3 * inner]
        rest = refs[parts + 9 + 3 * inner :]
        body(piece_refs, rows_ref, resid_ref, cot_ref, gain_ref, out_ref, dres_ref, gain_out, all_x, all_dm, grad_refs, *rest)

    def body(
        piece_refs, rows_ref, resid_ref, cot_ref, gain_ref,
        out_ref, dres_ref, gain_out, all_x, all_dm, grad_refs,
        wg, wu, wd, xb, db, act, coef_gate, coef_up, d_gate, d_up, acc_gate, acc_up, acc_down, stage,
        core_send, core_land, hold, keep, chip_send, chip_land, outer_send, outer_land, raw, d_mlp,
        s_outer, r_outer, s_chip, r_chip, s_core, r_core,
        s_core_sum, r_core_sum, s_chip_sum, r_chip_sum, s_outer_sum, r_outer_sum, local, local_w, local_g,
    ):
        g = Grid()
        core_peer = (g.dp_at, g.chip_at * 2 + 1 - g.core_at)

        def chip_peer(k):
            return (g.dp_at, lax.rem(g.chip_at + k + chips, chips) * 2 + g.core_at)

        def outer_peer(s):
            return (lax.rem(g.outer_at + s + outer, outer) * g.inner + g.inner_at, g.tensor_at)

        greet(
            [core_peer]
            + [chip_peer(k) for k in range(1, chips)]
            + [outer_peer(s) for s in range(1, outer)]
        )

        def remote(src, dst, send, recv, peer):
            return pltpu.make_async_remote_copy(
                src_ref=src, dst_ref=dst, send_sem=send, recv_sem=recv,
                device_id=peer, device_id_type=mesh_id,
            )

        def dot(a, b, contract):
            return lax.dot_general(a, b, (contract, ((), ())), preferred_element_type=f32)

        def looped(total, body):
            lax.fori_loop(0, total, lambda i, c: (body(i), c)[1], 0)

        def by_lines(body):
            looped(count // lines, lambda i: body(pl.ds(pl.multiple_of(i * lines, lines), lines)))

        def by_tiles(body):
            looped(wide_tiles, lambda i: body(pl.ds(pl.multiple_of(i * tile, tile), tile)))

        weights = (wg, wu, wd)
        fetches = []
        for j in range(inner):
            for s in range(outer):
                index = lax.rem(g.outer_at - s + outer, outer) * inner
                index = index + lax.rem(g.inner_at - j + inner, inner)
                span = pl.ds(pl.multiple_of(index * slab, slab), slab)
                for c in range(3):
                    at = j * outer + s
                    fetches.append(
                        pltpu.make_async_copy(
                            piece_refs[at].at[c], weights[c].at[span], local_w.at[at, c]
                        )
                    )
        started = []

        def run(phase, source, everything, fetched, compute, grads, write):
            mine = pl.ds(0, count)
            theirs = pl.ds(count, count)
            copies = {}

            def start(key, copy):
                copy.start()
                copies[key] = copy
                started.append(copy)

            def at(s, k, half):
                return everything.at[s, k, half]

            def core_copy(s, k, src):
                start(
                    ("c", s, k),
                    remote(src, at(s, k, theirs), s_core.at[phase, s, k], r_core.at[phase, s, k], core_peer),
                )

            def chip_copy(s, k, src):
                start(
                    ("x", s, k),
                    remote(src, at(s, k, mine), s_chip.at[phase, s, k], r_chip.at[phase, s, k], chip_peer(k)),
                )

            for s in steps[1:]:
                start(
                    ("z", s),
                    remote(source, at(s, 0, mine), s_outer.at[phase, s], r_outer.at[phase, s], outer_peer(s)),
                )
            for k in range(1, chips):
                chip_copy(0, k, source)
            core_copy(0, 0, source)
            own = pltpu.make_async_copy(source, at(0, 0, mine), local.at[phase, 0, blocks])
            own.start()
            if phase == 0:
                for copy in fetches:
                    copy.start()
            slots = {unit: i % 2 for i, unit in enumerate(order)}
            loads = {}
            sums = {}
            for task in plan(phase):
                name, s = task[:2]
                k = task[2] if len(task) > 2 else 0
                unit = s * chips + k
                if name == "zf":
                    copies["z", s].wait_recv()
                    for j in range(1, chips):
                        chip_copy(s, j, at(s, 0, mine))
                    core_copy(s, 0, at(s, 0, mine))
                elif name == "xf":
                    copies["x", s, k].wait_recv()
                    core_copy(s, k, at(s, k, mine))
                elif name == "load":
                    copies["c", s, k].wait_recv()
                    if (s, k) == (0, 0):
                        own.wait()
                    slot = slots[s, k]
                    loads[s, k] = []
                    for j, (src, dst) in enumerate(fetched):
                        copy = pltpu.make_async_copy(
                            src.at[s, k], dst.at[slot], local.at[phase, j, unit]
                        )
                        copy.start()
                        loads[s, k].append(copy)
                elif name == "compute":
                    if phase == 0 and (s, k) == order[0]:
                        for copy in fetches:
                            copy.wait()
                    for copy in loads[s, k]:
                        copy.wait()
                    i = order.index((s, k))
                    if i >= 2:
                        sums["core", order[i - 2]].wait_send()
                    slot = slots[s, k]

                    def send(slot=slot, unit=unit, s=s, k=k):
                        copy = remote(
                            core_send.at[slot], core_land.at[unit],
                            s_core_sum.at[phase, unit], r_core_sum.at[phase, unit], core_peer,
                        )
                        copy.start()
                        sums["core", (s, k)] = copy

                    compute(slot, unit, send)
                elif name == "grads":
                    grads(slots[s, k], unit)
                elif name == "write":
                    write()
                elif name == "cr":
                    sums["core", (s, k)].wait_recv()
                    slot = slots[s, k]
                    if k == 0:

                        def add_core(at_rows, s=s, slot=slot, unit=unit):
                            keep[s, at_rows] = hold[slot, at_rows] + core_land[unit, at_rows].astype(f32)

                        by_lines(add_core)
                    else:
                        there = s * (chips - 1) + k - 1

                        def add_core(at_rows, there=there, slot=slot, unit=unit):
                            total = hold[slot, at_rows] + core_land[unit, at_rows].astype(f32)
                            chip_send[there, at_rows] = total.astype(bf16)

                        by_lines(add_core)
                        copy = remote(
                            chip_send.at[there], chip_land.at[there],
                            s_chip_sum.at[phase, there], r_chip_sum.at[phase, there], chip_peer(-k),
                        )
                        copy.start()
                        sums["chip", (s, k)] = copy
                elif name == "xr":
                    for j in range(1, chips):
                        sums["chip", (s, j)].wait_recv()

                    def add_chip(at_rows, s=s):
                        total = keep[s, at_rows]
                        for j in range(1, chips):
                            total = total + chip_land[s * (chips - 1) + j - 1, at_rows].astype(f32)
                        if s == 0:
                            raw[at_rows] = total
                        else:
                            outer_send[s - 1, at_rows] = total.astype(bf16)

                    by_lines(add_chip)
                    if s:
                        copy = remote(
                            outer_send.at[s - 1], outer_land.at[s - 1],
                            s_outer_sum.at[phase, s], r_outer_sum.at[phase, s], outer_peer(-s),
                        )
                        copy.start()
                        sums["outer", s] = copy
                elif name == "zr":
                    sums["outer", s].wait_recv()

                    def add_outer(at_rows, s=s):
                        raw[at_rows] = raw[at_rows] + outer_land[s - 1, at_rows].astype(f32)

                    by_lines(add_outer)
            waited = [sums["core", unit] for unit in order[-2:]]
            waited += [copy for key, copy in sums.items() if key[0] != "core"]
            for copy in waited:
                copy.wait_send()
            for copy in started:
                copy.wait_send()
            started.clear()

        def forward(slot, unit, send):
            for j in range(units // unit_tile):
                cols = pl.ds(j * unit_tile, unit_tile)
                rows = xb[slot]
                gate = dot(rows, wg[:, cols], ((1,), (0,)))
                up = dot(rows, wu[:, cols], ((1,), (0,)))
                sigma = jax.nn.sigmoid(gate)
                silu = gate * sigma
                act[unit, :, cols] = (silu * up).astype(bf16)
                coef_up[unit, :, cols] = silu.astype(bf16)
                coef_gate[unit, :, cols] = (up * sigma * (1.0 + gate * (1.0 - sigma))).astype(bf16)

            def down(cols):
                part_sum = dot(act[unit], wd[cols, :], ((1,), (1,)))
                hold[slot, :, cols] = part_sum[:count]
                core_send[slot, :, cols] = part_sum[count:].astype(bf16)

            by_tiles(down)
            send()

        def between():
            def lines_of(i, total):
                at_rows = pl.ds(pl.multiple_of(i * lines, lines), lines)
                value = raw[at_rows]
                scale = lax.rsqrt(jnp.mean(value * value, axis=1, keepdims=True) + norm_eps)
                hat = value * scale
                gain_row = gain_ref[...]
                out_ref[at_rows] = (resid_ref[at_rows] + hat * gain_row).astype(bf16)
                top = cot_ref[at_rows].astype(f32)
                upstream = top * gain_row
                inner = jnp.mean(upstream * hat, axis=1, keepdims=True)
                d_mlp[at_rows] = (scale * (upstream - hat * inner)).astype(bf16)
                return total + jnp.sum(top * hat, axis=0, keepdims=True)

            gain_out[...] = lax.fori_loop(
                0, count // lines, lines_of, jnp.zeros((1, width), f32)
            )

        def backward(slot, unit, send):
            for j in range(units // unit_tile):
                cols = pl.ds(j * unit_tile, unit_tile)
                d_act = dot(db[slot], wd[:, cols], ((1,), (0,)))
                d_gate[slot, :, cols] = (d_act * coef_gate[unit, :, cols].astype(f32)).astype(bf16)
                d_up[slot, :, cols] = (d_act * coef_up[unit, :, cols].astype(f32)).astype(bf16)

            def into(cols):
                part_sum = dot(d_gate[slot], wg[cols, :], ((1,), (1,)))
                part_sum = part_sum + dot(d_up[slot], wu[cols, :], ((1,), (1,)))
                hold[slot, :, cols] = part_sum[:count]
                core_send[slot, :, cols] = part_sum[count:].astype(bf16)

            by_tiles(into)
            send()

        def weight_grads(slot, unit):
            first = unit == order[0][0] * chips + order[0][1]

            def grads(cols):
                def put_sum(ref, where, value):
                    if first:
                        ref[where] = value
                    else:
                        ref[where] = ref[where] + value

                rows = xb[slot, :, cols]
                put_sum(acc_gate, (cols, slice(None)), dot(rows, d_gate[slot], ((0,), (0,))))
                put_sum(acc_up, (cols, slice(None)), dot(rows, d_up[slot], ((0,), (0,))))
                put_sum(
                    acc_down, (cols, slice(None)), dot(db[slot, :, cols], act[unit], ((0,), (0,)))
                )

            by_tiles(grads)

        def write_grads():
            copies = []
            for j in range(inner):
                for s in range(outer):
                    index = lax.rem(g.outer_at + s, outer) * inner
                    index = index + lax.rem(g.inner_at + j, inner)
                    span = pl.ds(pl.multiple_of(index * slab, slab), slab)
                    slot = len(copies) % 2
                    if len(copies) >= 2:
                        for copy in copies[-2]:
                            copy.wait()
                    batch = []
                    for c, acc in enumerate((acc_gate, acc_up, acc_down)):
                        stage[slot, c] = acc[span].astype(bf16)
                        copy = pltpu.make_async_copy(
                            stage.at[slot, c], grad_refs[j * 3 + c].at[s], local_g.at[slot, c]
                        )
                        copy.start()
                        batch.append(copy)
                    copies.append(batch)
            for batch in copies[-2:]:
                for copy in batch:
                    copy.wait()

        run(0, rows_ref, all_x, [(all_x, xb)], forward, None, None)
        between()
        run(1, d_mlp, all_dm, [(all_dm, db), (all_x, xb)], backward, weight_grads, write_grads)

        def close(at_rows):
            dres_ref[at_rows] = raw[at_rows] + cot_ref[at_rows].astype(f32)

        by_lines(close)

    def held_in(space):
        return pl.BlockSpec(memory_space=space)

    shape = jax.ShapeDtypeStruct
    anywhere, near = held_in(pl.ANY), held_in(pltpu.VMEM)
    sems = pltpu.SemaphoreType.DMA
    links = outer * (chips - 1)
    flops = 2 * 9 * both * blocks * width * units
    results = pl.pallas_call(
        kernel,
        out_shape=(
            shape((count, width), bf16),
            shape((count, width), f32),
            shape((1, width), f32),
            shape((outer, chips, both, width), bf16),
            shape((outer, chips, both, width), bf16),
        )
        + (shape((outer, slab, units), bf16),) * (3 * inner),
        in_specs=[anywhere] * (parts + 1) + [near] * 3,
        out_specs=(near, near, near) + (anywhere,) * (2 + 3 * inner),
        scratch_shapes=[
            pltpu.VMEM((width, units), bf16),
            pltpu.VMEM((width, units), bf16),
            pltpu.VMEM((width, units), bf16),
            pltpu.VMEM((2, both, width), bf16),
            pltpu.VMEM((2, both, width), bf16),
            pltpu.VMEM((blocks, both, units), bf16),
            pltpu.VMEM((blocks, both, units), bf16),
            pltpu.VMEM((blocks, both, units), bf16),
            pltpu.VMEM((2, both, units), bf16),
            pltpu.VMEM((2, both, units), bf16),
            pltpu.VMEM((width, units), f32),
            pltpu.VMEM((width, units), f32),
            pltpu.VMEM((width, units), f32),
            pltpu.VMEM((2, 3, slab, units), bf16),
            pltpu.VMEM((2, count, width), bf16),
            pltpu.VMEM((blocks, count, width), bf16),
            pltpu.VMEM((2, count, width), f32),
            pltpu.VMEM((outer, count, width), f32),
            pltpu.VMEM((links, count, width), bf16),
            pltpu.VMEM((links, count, width), bf16),
            pltpu.VMEM((outer - 1, count, width), bf16),
            pltpu.VMEM((outer - 1, count, width), bf16),
            pltpu.VMEM((count, width), f32),
            pltpu.VMEM((count, width), bf16),
            sems((2, outer)),
            sems((2, outer)),
            sems((2, outer, chips)),
            sems((2, outer, chips)),
            sems((2, outer, chips)),
            sems((2, outer, chips)),
            sems((2, blocks)),
            sems((2, blocks)),
            sems((2, links)),
            sems((2, links)),
            sems((2, outer)),
            sems((2, outer)),
            sems((2, 2, blocks + 1)),
            sems((parts, 3)),
            sems((2, 3)),
        ],
        compiler_params=pltpu.CompilerParams(
            collective_id=2, has_side_effects=True, vmem_limit_bytes=60 * 2**20
        ),
        cost_estimate=pl.CostEstimate(flops=flops, bytes_accessed=64 * 2**20, transcendentals=0),
    )(*flat_pieces, rows_low, resid, cotangent, gain)
    grads = results[5:]
    return results[:3] + ([[grads[j * 3 + c] for j in range(inner)] for c in range(3)],)


def adam_kernel(w_ref, m_ref, v_ref, g_ref, *rest):
    scale_ref = rest[0] if len(rest) == 5 else None
    w_out, m_out, v_out, c_out = rest[-4:]
    grad = g_ref[...].astype(jnp.float32)
    new, first, second = adam_step(
        w_ref[...], grad, m_ref[...], v_ref[...], rate_matrix, weight_decay
    )
    if scale_ref is not None:
        new = new * scale_ref[...]
    w_out[...] = new
    m_out[...] = first
    v_out[...] = second
    c_out[...] = new.astype(jnp.bfloat16)


def adam_call(param, grad, first, second, scale=None):
    shape = param.shape
    flat = [v.reshape(-1, shape[-1]) for v in (param, first, second, grad)]
    rows, width = flat[0].shape
    block = min(rows, max(16, (1 << 17) // width))
    spec = pl.BlockSpec((block, width), lambda k: (k, 0))
    specs = [spec] * 4
    if scale is not None:
        per = shape[1] // block
        flat.append(scale)
        specs.append(pl.BlockSpec((None, 1, width), lambda k: (k // per, 0, 0)))
    outs = [jax.ShapeDtypeStruct((rows, width), jnp.float32)] * 3
    outs.append(jax.ShapeDtypeStruct((rows, width), jnp.bfloat16))
    size = rows * width
    result = pl.pallas_call(
        adam_kernel,
        grid=(rows // block,),
        in_specs=specs,
        out_specs=[spec] * 4,
        out_shape=outs,
        cost_estimate=pl.CostEstimate(
            flops=20 * size, bytes_accessed=28 * size, transcendentals=2 * size
        ),
        compiler_params=pltpu.CompilerParams(vmem_limit_bytes=32 * 2**20),
    )(*flat)
    return [v.reshape(shape) for v in result]


def adam_units_kernel(turned, at_ref, w_ref, m_ref, v_ref, g_ref, w_out, m_out, v_out, c_out):
    grad = g_ref[...].astype(jnp.float32)
    if turned:
        grad = grad.T
    new, first, second = adam_step(
        w_ref[...], grad, m_ref[...], v_ref[...], rate_matrix, weight_decay
    )
    w_out[...] = new
    m_out[...] = first
    v_out[...] = second
    c_out[...] = new.astype(jnp.bfloat16)


def adam_units(grid, param, first, second, grads, turned):
    n = grid.outer
    stacked = jnp.stack([jnp.stack(pieces) for pieces in grads])
    mats, _, wide, units = stacked.shape
    if turned:
        spec = pl.BlockSpec((units, wide), lambda c, k, at: (k, 0))
    else:
        spec = pl.BlockSpec((None, wide, units), lambda c, k, at: (c, 0, k))
    grad_spec = pl.BlockSpec(
        (None, None, wide, units), lambda c, k, at: (c, lax.rem(at[0] - k + n, n), 0, 0)
    )
    size = param.size
    outs = [jax.ShapeDtypeStruct(param.shape, jnp.float32)] * 3
    outs.append(jax.ShapeDtypeStruct(param.shape, jnp.bfloat16))
    return pl.pallas_call(
        functools.partial(adam_units_kernel, turned),
        grid_spec=pltpu.PrefetchScalarGridSpec(
            num_scalar_prefetch=1,
            grid=(mats, n),
            in_specs=[spec] * 3 + [grad_spec],
            out_specs=[spec] * 4,
        ),
        out_shape=outs,
        cost_estimate=pl.CostEstimate(
            flops=20 * size, bytes_accessed=28 * size, transcendentals=2 * size
        ),
        compiler_params=pltpu.CompilerParams(vmem_limit_bytes=32 * 2**20),
    )(grid.outer_at.astype(jnp.int32)[None], param, first, second, stacked)


def local(
    tokens,
    cotangent,
    block_ids,
    w_qkv,
    m_qkv,
    v_qkv,
    w_out,
    m_out,
    v_out,
    w_gu,
    m_gu,
    v_gu,
    w_down,
    m_down,
    v_down,
    gains,
    gain_m,
    gain_v,
):
    grid = Grid()
    local_x = tokens[0]
    gain_count = gains.shape[0]
    low_gains = jnp.pad(gains.astype(jnp.bfloat16), ((0, 16 - gain_count), (0, 0)))
    full_qkv, full_out, full_gains, seq_x = path_gather(
        w_qkv.astype(jnp.bfloat16), w_out.astype(jnp.bfloat16), low_gains, local_x
    )
    gain_rows = jnp.swapaxes(full_gains[:, :gain_count], 0, 1).reshape(gain_count, -1)
    gain_rows = gain_rows.astype(jnp.float32)
    shard = jnp.stack([w_gu[0], w_gu[1], w_down.T]).astype(jnp.bfloat16)
    full_qkv, shard = lax.optimization_barrier((full_qkv, shard))
    pieces = unit_pieces_of(grid, shard)
    model_width = local_x.shape[1]
    length = seq_x.shape[0]
    span = full_qkv.shape[2]
    heads_here = span // HEAD
    offset = lax.axis_index("tensor") * span
    projected = jnp.einsum("sd,cde->cse", seq_x, full_qkv, preferred_element_type=jnp.float32)
    queries, keys, values = (projected[0], projected[1], projected[2])
    q_square, k_square = lax.psum(
        (jnp.sum(queries * queries, axis=1), jnp.sum(keys * keys, axis=1)), "tensor"
    )
    q_scale = lax.rsqrt(q_square / model_width + norm_eps)[:, None]
    k_scale = lax.rsqrt(k_square / model_width + norm_eps)[:, None]
    q_hat = queries * q_scale
    k_hat = keys * k_scale
    q_gain = lax.dynamic_slice_in_dim(gain_rows[0], offset, span)
    k_gain = lax.dynamic_slice_in_dim(gain_rows[1], offset, span)
    cosine, sine = rope_tables(length, HEAD)

    def rotary(value):
        shaped = value.reshape(length, heads_here, HEAD)
        return shaped * cosine + rotate_fwd(shaped) * sine

    def unrotary(grad):
        return (grad * cosine + rotate_back(grad * sine)).reshape(length, span)

    q_low = rotary(q_hat * q_gain).astype(jnp.bfloat16)
    k_low = rotary(k_hat * k_gain).astype(jnp.bfloat16)
    v_low = values.astype(jnp.bfloat16).reshape(length, heads_here, HEAD)
    blocks = block_ids[0]
    block_rows = min(512, length)
    block_count = length // block_rows
    scale = HEAD ** (-0.5)
    starts = jnp.arange(block_count, dtype=jnp.int32) * block_rows

    def scores_of(start):
        q_part = lax.dynamic_slice_in_dim(q_low, start, block_rows, 0)
        b_part = lax.dynamic_slice_in_dim(blocks, start, block_rows, 0)
        raw = jnp.einsum("qhd,khd->hqk", q_part, k_low, preferred_element_type=jnp.float32) * scale
        allowed = blocks[None, None, :] <= b_part[None, :, None]
        return (jnp.where(allowed, raw, masked_value), q_part)

    def forward_block(start):
        masked, q_part = scores_of(start)
        top = jnp.max(masked, axis=2, keepdims=True)
        weight = jnp.exp(masked - top)
        total = jnp.sum(weight, axis=2, keepdims=True)
        probs = (weight / total).astype(jnp.bfloat16)
        context = jnp.einsum("hqk,khd->qhd", probs, v_low, preferred_element_type=jnp.float32)
        return (
            context.astype(jnp.bfloat16),
            (top + jnp.log(total))[:, :, 0],
            jnp.max(top[:, :, 0], axis=1),
        )

    context_low, log_total, block_top = lax.map(forward_block, starts)
    context_low = context_low.reshape(length, span)
    head_top = jnp.max(block_top, axis=0)
    attn_raw = sequence_scatter(
        grid, jnp.dot(context_low, full_out, preferred_element_type=jnp.float32)
    )
    x_float = local_x.astype(jnp.float32)
    o_scale = lax.rsqrt(jnp.mean(attn_raw * attn_raw, axis=1, keepdims=True) + norm_eps)
    attn_hat = attn_raw * o_scale
    resid = x_float + attn_hat * gain_rows[2]
    for bit in bits(grid.dp):
        head_top = jnp.maximum(head_top, grid.across(head_top, "dp", bit))
    rows_low, pieces, head_top = lax.optimization_barrier(
        (resid.astype(jnp.bfloat16), pieces, head_top)
    )
    output, d_resid, gain_last, unit_grads = unit_kernel_call(
        rows_low, resid, cotangent[0], gain_rows[3:4], pieces
    )
    gain_attn = jnp.sum(d_resid * attn_hat, axis=0)
    d_attn = norm_back(o_scale, attn_hat, d_resid * gain_rows[2]).astype(jnp.bfloat16)
    seq_do = sequence_gather(grid, d_attn)
    grad_out = jnp.einsum("se,sd->ed", context_low, seq_do, preferred_element_type=jnp.float32)
    d_context = jnp.einsum("sd,ed->se", seq_do, full_out, preferred_element_type=jnp.float32)
    d_context = d_context.astype(jnp.bfloat16).reshape(length, heads_here, HEAD)
    part_gate = outer_spread(grid, inner_sum(grid, unit_grads[0], d_context))

    def backward_block(carry, item):
        key_acc, value_acc = carry
        start, log_part = item
        masked, q_part = scores_of(start)
        probs = jnp.exp(masked - log_part[:, :, None])
        dc_part = lax.dynamic_slice_in_dim(d_context, start, block_rows, 0)
        d_probs = jnp.einsum("qhd,khd->hqk", dc_part, v_low, preferred_element_type=jnp.float32)
        inner = jnp.sum(probs * d_probs, axis=2, keepdims=True)
        d_scores = (probs * (d_probs - inner)).astype(jnp.bfloat16)
        d_query = (
            jnp.einsum("hqk,khd->qhd", d_scores, k_low, preferred_element_type=jnp.float32) * scale
        )
        key_acc = (
            key_acc
            + jnp.einsum("hqk,qhd->khd", d_scores, q_part, preferred_element_type=jnp.float32)
            * scale
        )
        value_acc = value_acc + jnp.einsum(
            "hqk,qhd->khd", probs.astype(jnp.bfloat16), dc_part, preferred_element_type=jnp.float32
        )
        return ((key_acc, value_acc), d_query)

    empty = jnp.zeros((length, heads_here, HEAD), jnp.float32)
    (d_krot, d_values), d_qrot = lax.scan(backward_block, (empty, empty), (starts, log_total))
    d_qrot = d_qrot.reshape(length, heads_here, HEAD)
    d_qnorm = unrotary(d_qrot)
    d_knorm = unrotary(d_krot)
    head_gains = jnp.stack([jnp.sum(d_qnorm * q_hat, axis=0), jnp.sum(d_knorm * k_hat, axis=0)])
    placed = lax.dynamic_update_slice(
        jnp.zeros((2, model_width), jnp.float32), head_gains, (0, offset)
    )
    gain_terms = jnp.concatenate([placed, jnp.stack([gain_attn, gain_last[0]])], axis=0)
    dq_hat = d_qnorm * q_gain
    dk_hat = d_knorm * k_gain
    q_inner, k_inner = lax.psum(
        (jnp.sum(dq_hat * q_hat, axis=1), jnp.sum(dk_hat * k_hat, axis=1)), "tensor"
    )
    part_up = outer_spread(grid, inner_sum(grid, unit_grads[1], d_qrot))
    d_query = q_scale * (dq_hat - q_hat * (q_inner / model_width)[:, None])
    d_key = k_scale * (dk_hat - k_hat * (k_inner / model_width)[:, None])
    d_qkv = jnp.stack([d_query, d_key, d_values.reshape(length, span)]).astype(jnp.bfloat16)
    grad_qkv = jnp.einsum("sd,cse->cde", seq_x, d_qkv, preferred_element_type=jnp.float32)
    part_down = outer_spread(grid, inner_sum(grid, unit_grads[2], grad_qkv))
    terms = jnp.swapaxes(gain_terms.reshape(gain_count, grid.dp, -1), 0, 1)
    part_qkv, part_out, part_gains = path_scatter(
        grad_qkv.astype(jnp.bfloat16),
        grad_out.astype(jnp.bfloat16),
        jnp.pad(terms, ((0, 0), (0, 8 - gain_count), (0, 0))),
    )
    part_gains = part_gains[:gain_count]
    part_gate, part_up, part_down = after((part_gate, part_up, part_down), part_qkv)
    grad_tokens = d_resid + sequence_scatter(
        grid, jnp.einsum("cse,cde->sd", d_qkv, full_qkv, preferred_element_type=jnp.float32)
    )
    factor = clip_tau / jnp.maximum(head_top, clip_tau)
    column = jnp.repeat(jnp.sqrt(factor), HEAD)
    column_scale = jnp.stack([column, column, jnp.ones_like(column)])[:, None, :]
    new_qkv, new_m_qkv, new_v_qkv, copy_qkv = adam_call(
        w_qkv, part_qkv, m_qkv, v_qkv, column_scale
    )
    new_out, new_m_out, new_v_out, copy_out = adam_call(w_out, part_out, m_out, v_out)
    new_gu, new_m_gu, new_v_gu, copy_gu = adam_units(
        grid, w_gu, m_gu, v_gu, [part_gate, part_up], False
    )
    new_down, new_m_down, new_v_down, copy_down = adam_units(
        grid, w_down, m_down, v_down, [part_down], True
    )
    new_gains, new_gain_m, new_gain_v = adam_step(gains, part_gains, gain_m, gain_v, rate_gain, 0.0)
    return (
        output[None],
        grad_tokens[None],
        new_qkv,
        new_m_qkv,
        new_v_qkv,
        copy_qkv,
        new_out,
        new_m_out,
        new_v_out,
        copy_out,
        new_gu,
        new_m_gu,
        new_v_gu,
        copy_gu,
        new_down,
        new_m_down,
        new_v_down,
        copy_down,
        new_gains,
        new_gain_m,
        new_gain_v,
        factor,
    )


def solution(mesh):
    return jax.shard_map(
        local,
        mesh=mesh,
        in_specs=(
            P("dp", "tensor", None),
            P("dp", "tensor", None),
            P("dp", None),
            P(None, "dp", "tensor"),
            P(None, "dp", "tensor"),
            P(None, "dp", "tensor"),
            P("tensor", "dp"),
            P("tensor", "dp"),
            P("tensor", "dp"),
            P(None, "dp", "tensor"),
            P(None, "dp", "tensor"),
            P(None, "dp", "tensor"),
            P("tensor", "dp"),
            P("tensor", "dp"),
            P("tensor", "dp"),
            P(None, "dp"),
            P(None, "dp"),
            P(None, "dp"),
        ),
        out_specs=(
            P("dp", "tensor", None),
            P("dp", "tensor", None),
            P(None, "dp", "tensor"),
            P(None, "dp", "tensor"),
            P(None, "dp", "tensor"),
            P(None, "dp", "tensor"),
            P("tensor", "dp"),
            P("tensor", "dp"),
            P("tensor", "dp"),
            P("tensor", "dp"),
            P(None, "dp", "tensor"),
            P(None, "dp", "tensor"),
            P(None, "dp", "tensor"),
            P(None, "dp", "tensor"),
            P("tensor", "dp"),
            P("tensor", "dp"),
            P("tensor", "dp"),
            P("tensor", "dp"),
            P(None, "dp"),
            P(None, "dp"),
            P(None, "dp"),
            P("tensor"),
        ),
        check_vma=False,
    )
```

```python
import functools

import jax
import jax.numpy as jnp
from jax import lax
from jax.experimental import pallas as pl
from jax.experimental.pallas import tpu as pltpu
from jax.sharding import PartitionSpec as P

HEAD = 128
STEP = 5


norm_eps = 1e-06
rope_base = 500000.0
beta_one = 0.9
beta_two = 0.95
rate_matrix = 0.01
rate_gain = 0.6
weight_decay = 0.1
adam_eps = 1e-08
clip_tau = 9.0
masked_value = -1e30


def rope_tables(length, size):
    half = size // 2
    freq = rope_base ** (-(jnp.arange(half, dtype=jnp.float32) * 2.0 / size))
    angle = jnp.arange(length, dtype=jnp.float32)[:, None] * freq[None, :]
    angle = jnp.concatenate([angle, angle], axis=1)
    return (jnp.cos(angle)[:, None, :], jnp.sin(angle)[:, None, :])


def rotate_fwd(value):
    half = value.shape[-1] // 2
    return jnp.concatenate([-value[..., half:], value[..., :half]], axis=-1)


def rotate_back(value):
    half = value.shape[-1] // 2
    return jnp.concatenate([value[..., half:], -value[..., :half]], axis=-1)


def adam_step(param, grad, first, second, rate, decay):
    first = beta_one * first + (1.0 - beta_one) * grad
    second = beta_two * second + (1.0 - beta_two) * grad * grad
    fix_one = 1.0 - beta_one**STEP
    fix_two = 1.0 - beta_two**STEP
    update = first / fix_one / (jnp.sqrt(second / fix_two) + adam_eps)
    return (param - rate * (update + decay * param), first, second)


def norm_back(scale_factor, normed, upstream):
    inner = jnp.mean(upstream * normed, axis=1, keepdims=True)
    return scale_factor * (upstream - normed * inner)


class Grid:
    def __init__(self):
        self.dp = lax.axis_size("dp")
        self.tensor = lax.axis_size("tensor")
        self.inner = 1
        while self.inner * self.inner * 4 <= self.dp:
            self.inner *= 2
        self.outer = self.dp // self.inner
        self.chips = self.tensor // 2
        self.dp_at = lax.axis_index("dp")
        self.tensor_at = lax.axis_index("tensor")
        self.inner_at = self.dp_at % self.inner
        self.chip_at = self.tensor_at // 2
        self.core_at = self.tensor_at % 2
        self.outer_at = self.dp_at // self.inner

    def path_of(self, index):
        column, row = index // self.inner, index % self.inner
        return row * self.outer + column + (row % 2) * (self.outer - 1 - 2 * column)

    def index_of(self, place):
        row, column = place // self.outer, place % self.outer
        return (column + (row % 2) * (self.outer - 1 - 2 * column)) * self.inner + row

    def to_outer(self, value, step):
        n, m = self.outer, self.inner
        pairs = [(a * m + b, (a + step) % n * m + b) for a in range(n) for b in range(m)]
        return lax.ppermute(value, "dp", pairs)

    def to_inner(self, value, step):
        n, m = self.outer, self.inner
        pairs = [(a * m + b, a * m + (b + step) % m) for a in range(n) for b in range(m)]
        return lax.ppermute(value, "dp", pairs)

    def to_chip(self, value, step):
        n = self.chips
        pairs = [(a * 2 + b, (a + step) % n * 2 + b) for a in range(n) for b in range(2)]
        return lax.ppermute(value, "tensor", pairs)

    def to_core(self, value):
        pairs = [(a * 2 + b, a * 2 + 1 - b) for a in range(self.chips) for b in range(2)]
        return lax.ppermute(value, "tensor", pairs)

    def across(self, value, axis, bit):
        count = lax.axis_size(axis)
        return lax.ppermute(value, axis, [(i, i ^ bit) for i in range(count)])


def bits(count):
    return [1 << k for k in range(count.bit_length() - 1)]


def part(value, axis, index, size):
    return lax.dynamic_slice_in_dim(value, index * size, size, axis)


def put(whole, piece, axis, index):
    return lax.dynamic_update_slice_in_dim(whole, piece, index * piece.shape[axis], axis)


def low_sum(*terms):
    total = terms[0].astype(jnp.float32)
    for term in terms[1:]:
        total = total + term.astype(jnp.float32)
    return total.astype(jnp.bfloat16)


def greet(peers):
    barrier = pltpu.get_barrier_semaphore()
    for peer in peers:
        pl.semaphore_signal(barrier, inc=1, device_id=peer, device_id_type=pl.DeviceIdType.MESH)
    pl.semaphore_wait(barrier, len(peers))


def path_gather(shard, flat, gains, rows):
    grid = Grid()
    n, chips, tensor = grid.dp, grid.chips, grid.tensor
    lead, deep, wide = shard.shape
    half = deep // 2
    tall, thin = flat.shape
    part_tall = tall // 2
    count = rows.shape[0]
    ring = 2 * lead + 3

    def kernel(
        shard_ref, flat_ref, gains_ref, rows_ref, full, full_flat, full_gains, sequence,
        sends, lands, row_sends, row_lands, own,
    ):
        g = Grid()
        dp_at, t_at = g.dp_at, g.tensor_at
        chip_at, core_at = t_at // 2, t_at % 2
        place = g.path_of(dp_at)
        after = g.index_of(lax.rem(place + 1, n))
        before = g.index_of(lax.rem(place + n - 1, n))
        core_peer = (dp_at, chip_at * 2 + 1 - core_at)
        chip_peers = [
            (dp_at, lax.rem(chip_at + k, chips) * 2 + core_at) for k in range(1, chips)
        ]
        greet([(after, t_at), (before, t_at), core_peer] + chip_peers)

        def views(item, index):
            if item == ring - 1:
                return 1, gains_ref, full_gains.at[index]
            if item >= 2 * lead:
                side = item - 2 * lead
                span = pl.ds(side * part_tall, part_tall)
                cols = pl.ds(pl.multiple_of(index * thin, thin), thin)
                return 1 - 2 * side, flat_ref.at[span], full_flat.at[span, cols]
            side, c = item // lead, item % lead
            span = pl.ds(pl.multiple_of(index * deep + side * half, half), half)
            return 1 - 2 * side, shard_ref.at[c, pl.ds(side * half, half)], full.at[c, span]

        def hop(step, item):
            way = views(item, 0)[0]
            index = g.index_of(lax.rem(place - way * step + n, n))
            _, source, target = views(item, index)
            return pltpu.make_async_remote_copy(
                src_ref=source if step == 0 else target,
                dst_ref=target,
                send_sem=sends.at[step, item],
                recv_sem=lands.at[step, item],
                device_id=(after if way == 1 else before, t_at),
                device_id_type=pl.DeviceIdType.MESH,
            )

        def rows_at(index):
            return sequence.at[pl.ds(pl.multiple_of(index * count, count), count)]

        def row_copy(slot, index, peer, first):
            return pltpu.make_async_remote_copy(
                src_ref=rows_ref if first else rows_at(index),
                dst_ref=rows_at(index),
                send_sem=row_sends.at[slot],
                recv_sem=row_lands.at[slot],
                device_id=peer,
                device_id_type=pl.DeviceIdType.MESH,
            )

        order = [c + side * lead for c in range(lead) for side in (0, 1)]
        order += list(range(2 * lead, ring))
        hops = {}
        for item in order:
            hops[0, item] = hop(0, item)
            hops[0, item].start()
        moves = []
        for k in range(1, chips):
            moves.append(row_copy(k - 1, t_at, chip_peers[k - 1], True))
            moves[-1].start()
        mine = row_copy(chips - 1, t_at, core_peer, True)
        mine.start()
        keep = [
            pltpu.make_async_copy(
                shard_ref, full.at[:, pl.ds(pl.multiple_of(dp_at * deep, deep), deep)], own.at[0]
            ),
            pltpu.make_async_copy(gains_ref, full_gains.at[dp_at], own.at[1]),
            pltpu.make_async_copy(rows_ref, rows_at(t_at), own.at[2]),
            pltpu.make_async_copy(
                flat_ref, full_flat.at[:, pl.ds(pl.multiple_of(dp_at * thin, thin), thin)], own.at[3]
            ),
        ]
        for copy in keep:
            copy.start()
        passed = []
        for step in range(1, n - 1):
            for item in order:
                hops[step - 1, item].wait_recv()
                hops[step, item] = hop(step, item)
                hops[step, item].start()
            if step <= chips - 1:
                moves[step - 1].wait_recv()
                source = lax.rem(chip_at - step + chips, chips) * 2 + core_at
                passed.append(row_copy(chips - 1 + step, source, core_peer, False))
                passed[-1].start()
        for item in order:
            hops[n - 2, item].wait_recv()
        mine.wait_recv()
        for copy in passed:
            copy.wait_recv()
        for key in hops:
            hops[key].wait_send()
        for copy in moves + [mine] + passed:
            copy.wait_send()
        for copy in keep:
            copy.wait()

    bf16 = jnp.bfloat16
    return pl.pallas_call(
        kernel,
        out_shape=(
            jax.ShapeDtypeStruct((lead, deep * n, wide), bf16),
            jax.ShapeDtypeStruct((tall, thin * n), bf16),
            jax.ShapeDtypeStruct((n,) + gains.shape, bf16),
            jax.ShapeDtypeStruct((count * tensor, rows.shape[1]), bf16),
        ),
        in_specs=[pl.BlockSpec(memory_space=pl.ANY)] * 4,
        out_specs=(pl.BlockSpec(memory_space=pl.ANY),) * 4,
        scratch_shapes=[
            pltpu.SemaphoreType.DMA((n - 1, ring)),
            pltpu.SemaphoreType.DMA((n - 1, ring)),
            pltpu.SemaphoreType.DMA((2 * chips - 1,)),
            pltpu.SemaphoreType.DMA((2 * chips - 1,)),
            pltpu.SemaphoreType.DMA((4,)),
        ],
        compiler_params=pltpu.CompilerParams(collective_id=0, has_side_effects=True),
    )(shard, flat, gains, rows)


def path_scatter(whole, flat, gains, tops):
    grid = Grid()
    n, chips = grid.dp, grid.chips
    lead, total, wide = whole.shape
    deep = total // n
    half = deep // 2
    tall, thin = flat.shape[0], flat.shape[1] // n
    part_tall = tall // 2
    ring = 2 * lead + 4
    gain_item, top_item = ring - 2, ring - 1
    bf16, f32 = jnp.bfloat16, jnp.float32

    def kernel(
        whole_ref, flat_ref, gains_ref, tops_ref, out_ref, flat_out, gains_out, tops_out,
        land, land_flat, land_gain, land_top, own_gain, peer_gain, sends, lands, gain_sends, gain_lands,
    ):
        g = Grid()
        place = g.path_of(g.dp_at)
        after = g.index_of(lax.rem(place + 1, n))
        before = g.index_of(lax.rem(place + n - 1, n))
        core_peer = (g.dp_at, g.chip_at * 2 + 1 - g.core_at)
        chip_peers = [
            (g.dp_at, lax.rem(g.chip_at + k, chips) * 2 + g.core_at) for k in range(1, chips)
        ]
        greet([(after, g.tensor_at), (before, g.tensor_at), core_peer] + chip_peers)

        def way_of(item):
            if item >= gain_item:
                return 1
            return 1 - 2 * (item - 2 * lead if item >= 2 * lead else item // lead)

        def own(item, away):
            index = g.index_of(lax.rem(place - way_of(item) * away + 2 * n, n))
            if item == gain_item:
                return gains_ref.at[index]
            if item == top_item:
                return tops_ref
            if item >= 2 * lead:
                cols = pl.ds(pl.multiple_of(index * thin, thin), thin)
                return flat_ref.at[pl.ds((item - 2 * lead) * part_tall, part_tall), cols]
            side, c = item // lead, item % lead
            return whole_ref.at[c, pl.ds(pl.multiple_of(index * deep + side * half, half), half)]

        def landed(step, item):
            if item == gain_item:
                return land_gain.at[step]
            if item == top_item:
                return land_top.at[step]
            if item >= 2 * lead:
                return land_flat.at[step, item - 2 * lead]
            return land.at[step, item]

        def hop(step, item):
            return pltpu.make_async_remote_copy(
                src_ref=own(item, 1) if step == 0 else landed(step - 1, item),
                dst_ref=landed(step, item),
                send_sem=sends.at[step, item],
                recv_sem=lands.at[step, item],
                device_id=(after if way_of(item) == 1 else before, g.tensor_at),
                device_id_type=pl.DeviceIdType.MESH,
            )

        order = [gain_item, top_item] + [c + side * lead for c in range(lead) for side in (0, 1)]
        order += [2 * lead, 2 * lead + 1]
        hops = {}
        for item in order:
            hops[0, item] = hop(0, item)
            hops[0, item].start()
        for step in range(1, n):
            for item in order:
                hops[step - 1, item].wait_recv()
                here = landed(step - 1, item)
                if item == top_item:
                    summed = jnp.maximum(here[...], tops_ref[...])
                else:
                    summed = here[...].astype(f32) + own(item, step + 1)[...].astype(f32)
                if step < n - 1:
                    here[...] = summed.astype(here.dtype)
                    hops[step, item] = hop(step, item)
                    hops[step, item].start()
                elif item == gain_item:
                    own_gain[0] = summed
                elif item == top_item:
                    tops_out[...] = summed
                elif item >= 2 * lead:
                    side = item - 2 * lead
                    flat_out[pl.ds(side * part_tall, part_tall)] = summed
                else:
                    side, c = item // lead, item % lead
                    out_ref[c, pl.ds(side * half, half)] = summed
        peers = [core_peer] + chip_peers
        copies = []
        for k, peer in enumerate(peers):
            level = min(k, 1)
            copies.append(
                pltpu.make_async_remote_copy(
                    src_ref=own_gain.at[level],
                    dst_ref=peer_gain.at[k],
                    send_sem=gain_sends.at[k],
                    recv_sem=gain_lands.at[k],
                    device_id=peer,
                    device_id_type=pl.DeviceIdType.MESH,
                )
            )
        copies[0].start()
        copies[0].wait_recv()
        own_gain[1] = own_gain[0] + peer_gain[0]
        for copy in copies[1:]:
            copy.start()
        for copy in copies[1:]:
            copy.wait_recv()
        result = own_gain[1]
        for k in range(1, len(peers)):
            result = result + peer_gain[k]
        gains_out[...] = result
        for key in hops:
            hops[key].wait_send()
        for copy in copies:
            copy.wait_send()

    near = pl.BlockSpec(memory_space=pltpu.VMEM)
    gain_shape = gains.shape[1:]
    return pl.pallas_call(
        kernel,
        out_shape=(
            jax.ShapeDtypeStruct((lead, deep, wide), f32),
            jax.ShapeDtypeStruct((tall, thin), f32),
            jax.ShapeDtypeStruct(gain_shape, f32),
            jax.ShapeDtypeStruct(tops.shape, f32),
        ),
        in_specs=[near] * 4,
        out_specs=(near,) * 4,
        scratch_shapes=[
            pltpu.VMEM((n - 1, 2 * lead, half, wide), bf16),
            pltpu.VMEM((n - 1, 2, part_tall, thin), bf16),
            pltpu.VMEM((n - 1,) + gain_shape, f32),
            pltpu.VMEM((n - 1,) + tops.shape, f32),
            pltpu.VMEM((2,) + gain_shape, f32),
            pltpu.VMEM((chips,) + gain_shape, f32),
            pltpu.SemaphoreType.DMA((n - 1, ring)),
            pltpu.SemaphoreType.DMA((n - 1, ring)),
            pltpu.SemaphoreType.DMA((chips,)),
            pltpu.SemaphoreType.DMA((chips,)),
        ],
        compiler_params=pltpu.CompilerParams(
            collective_id=1, has_side_effects=True, vmem_limit_bytes=40 * 2**20
        ),
    )(whole, flat, gains, tops)


def attend_call(seq, full_qkv, full_out, head_gains, out_gain, tables, blocks, rows, shard):
    grid = Grid()
    outer, inner, chips, tensor = grid.outer, grid.inner, grid.chips, grid.tensor
    length, width = seq.shape
    span = full_qkv.shape[2]
    heads = span // HEAD
    count = rows.shape[0]
    slab = shard.shape[1]
    units = shard.shape[2] // outer
    parts = outer * inner
    steps = sorted(range(1, outer), key=lambda s: (min(s, outer - s), s))
    tall = min(256, length)
    tile = 512
    lines = 32
    bf16, f32 = jnp.bfloat16, jnp.float32
    mesh_id = pl.DeviceIdType.MESH

    def kernel(
        seq_ref, qkv_ref, out_w_ref, gains_ref, out_gain_ref, cos_ref, sin_ref, id_col, id_row, rows_ref, shard_ref,
        *refs
    ):
        pieces = [refs[j * outer : (j + 1) * outer] for j in range(inner)]
        body(
            seq_ref, qkv_ref, out_w_ref, gains_ref, out_gain_ref, cos_ref, sin_ref, id_col, id_row, rows_ref, shard_ref,
            pieces, *refs[parts:],
        )

    def body(
        seq_ref, qkv_ref, out_w_ref, gains_ref, out_gain_ref, cos_ref, sin_ref, id_col, id_row, rows_ref, shard_ref,
        pieces, hat_ref, scale_ref, q_low, k_low, v_low, lse_ref, context, attn_hat, o_scale, resid, resid_low, top_ref,
        square, squares, core_send, core_land, hold, chip_send, chip_land,
        s_z, r_z, s_y, r_y, s_sq, r_sq, s_core, r_core, s_chip, r_chip, local,
    ):
        g = Grid()

        def tensor_peer(k, flip):
            core = 1 - g.core_at if flip else g.core_at
            return (g.dp_at, lax.rem(g.chip_at + k + chips, chips) * 2 + core)

        def dp_peer(s, j):
            across = lax.rem(g.outer_at + s + outer, outer) * inner
            return (across + lax.rem(g.inner_at + j + inner, inner), g.tensor_at)

        near = [tensor_peer(k, f) for k in range(chips) for f in (0, 1) if (k, f) != (0, 0)]
        far = [dp_peer(s, 0) for s in range(1, outer)]
        far += [dp_peer(0, j) for j in sorted({1 % inner, inner - 1} - {0})]
        greet(near + far)

        def remote(src, dst, send, recv, peer):
            copy = pltpu.make_async_remote_copy(
                src_ref=src, dst_ref=dst, send_sem=send, recv_sem=recv,
                device_id=peer, device_id_type=mesh_id,
            )
            copy.start()
            return copy

        def dot(a, b, contract):
            return lax.dot_general(a, b, (contract, ((), ())), preferred_element_type=f32)

        def looped(total, make):
            lax.fori_loop(0, total, lambda i, c: (make(i), c)[1], 0)

        def rows_of(i, size):
            return pl.ds(pl.multiple_of(i * size, size), size)

        def cut(s):
            at = lax.rem(g.outer_at + s, outer)
            return shard_ref.at[:, :, rows_of(at, units)]

        z_copies = {
            s: remote(cut(s), pieces[0][s], s_z.at[s], r_z.at[s], dp_peer(s, 0)) for s in steps
        }
        own = pltpu.make_async_copy(cut(0), pieces[0][0], local)
        own.start()
        y_copies = {}

        def pass_on(j, s):
            src = cut(0) if (j, s) == (1, 0) else pieces[j - 1][s]
            y_copies[j, s] = remote(src, pieces[j][s], s_y.at[j, s], r_y.at[j, s], dp_peer(0, 1))

        if inner > 1:
            pass_on(1, 0)
        duties = []
        for s in steps:

            def duty(s=s):
                z_copies[s].wait_recv()
                if inner > 1:
                    pass_on(1, s)

            duties.append(duty)
        for j in range(2, inner):
            for s in [0] + steps:

                def duty(j=j, s=s):
                    y_copies[j - 1, s].wait_recv()
                    pass_on(j, s)

                duties.append(duty)

        def next_duty():
            if duties:
                duties.pop(0)()

        def project(i):
            at = rows_of(i, tall)
            x = seq_ref[at]
            lane = lax.broadcasted_iota(jnp.int32, (tall, 128), 1)
            sums = jnp.zeros((tall, 128), f32)
            for c in range(2):
                value = dot(x, qkv_ref[c], ((1,), (0,)))
                hat_ref[c, at] = value
                sums = jnp.where(lane == c, jnp.sum(value * value, axis=1, keepdims=True), sums)
            v_low[at] = dot(x, qkv_ref[2], ((1,), (0,))).astype(bf16)
            square[:, at] = sums.T[:8]

        looped(length // tall, project)
        sq_copies = []
        for k in range(chips):
            for f in (0, 1):
                if (k, f) != (0, 0):
                    at = k * 2 + f - 1
                    sq_copies.append(
                        remote(square, squares.at[at], s_sq.at[at], r_sq.at[at], tensor_peer(k, f))
                    )
        for copy in sq_copies:
            copy.wait_recv()
        sign = jnp.where(lax.broadcasted_iota(jnp.int32, (tall, HEAD), 1) < HEAD // 2, -1.0, 1.0)

        def rotate(i):
            at = rows_of(i, tall)
            sums = square[:, at]
            for copy_at in range(tensor - 1):
                sums = sums + squares[copy_at, :, at]
            column = jnp.concatenate([sums, jnp.zeros((120, tall), f32)], axis=0).T
            scales = lax.rsqrt(column / width + norm_eps)
            scale_ref[at] = scales
            cosine, sine = cos_ref[at], sin_ref[at] * sign
            for c, low in ((0, q_low), (1, k_low)):
                hat = hat_ref[c, at] * scales[:, c : c + 1]
                hat_ref[c, at] = hat
                normed = hat * gains_ref[c : c + 1]
                for h in range(heads):
                    cols = slice(h * HEAD, (h + 1) * HEAD)
                    value = normed[:, cols]
                    turned = pltpu.roll(value, HEAD // 2, 1)
                    low[at, cols] = (value * cosine + turned * sine).astype(bf16)

        looped(length // tall, rotate)
        scale = HEAD ** (-0.5)
        top_ref[...] = jnp.full((8, 128), masked_value, f32)
        for h in range(heads):
            cols = slice(h * HEAD, (h + 1) * HEAD)

            def attend(i, best, cols=cols, h=h):
                at = rows_of(i, tall)
                raw = dot(q_low[at, cols], k_low[:, cols], ((1,), (1,))) * scale
                masked = jnp.where(id_row[...] <= id_col[at], raw, masked_value)
                top = jnp.max(masked, axis=1, keepdims=True)
                weight = jnp.exp(masked - top)
                total = jnp.sum(weight, axis=1, keepdims=True)
                probs = (weight / total).astype(bf16)
                context[at, cols] = dot(probs, v_low[:, cols], ((1,), (0,))).astype(bf16)
                lse_ref[at, h : h + 1] = top + jnp.log(total)
                return jnp.maximum(best, jnp.max(top, axis=0, keepdims=True))

            best = lax.fori_loop(
                0, length // tall, attend, jnp.full((1, 1), masked_value, f32)
            )
            top_ref[h : h + 1] = jnp.broadcast_to(best, (1, 128))
        next_duty()

        def out_rows(k, flip, store):
            chip = lax.rem(g.chip_at + k, chips)
            core = 1 - g.core_at if flip else g.core_at
            at = rows_of(chip * 2 + core, count)

            def columns(i):
                cols = rows_of(i, tile)
                store(cols, dot(context[at], out_w_ref[:, cols], ((1,), (0,))))

            looped(width // tile, columns)

        chip_order = list(range(1, chips)) + [0]
        core_copies, chip_copies = {}, {}
        for k in chip_order:

            def store(cols, value, k=k):
                core_send[k, :, cols] = value.astype(bf16)

            out_rows(k, True, store)
            core_copies[k] = remote(
                core_send.at[k], core_land.at[k], s_core.at[k], r_core.at[k], tensor_peer(0, 1)
            )
        for k in chip_order:

            def store(cols, value, k=k):
                hold[k, :, cols] = value

            out_rows(k, False, store)
            if k:
                core_copies[k].wait_recv()

                def add(i, k=k):
                    at = rows_of(i, lines)
                    chip_send[k - 1, at] = (hold[k, at] + core_land[k, at].astype(f32)).astype(bf16)

                looped(count // lines, add)
                chip_copies[k] = remote(
                    chip_send.at[k - 1], chip_land.at[k - 1], s_chip.at[k], r_chip.at[k], tensor_peer(k, 0)
                )
        next_duty()
        core_copies[0].wait_recv()
        for k in range(1, chips):
            chip_copies[k].wait_recv()

        def close(i):
            at = rows_of(i, lines)
            raw = hold[0, at] + core_land[0, at].astype(f32)
            for k in range(1, chips):
                raw = raw + chip_land[k - 1, at].astype(f32)
            scale_o = lax.rsqrt(jnp.mean(raw * raw, axis=1, keepdims=True) + norm_eps)
            hat = raw * scale_o
            attn_hat[at] = hat
            o_scale[at] = scale_o
            value = rows_ref[at].astype(f32) + hat * out_gain_ref[...]
            resid[at] = value
            resid_low[at] = value.astype(bf16)

        looped(count // lines, close)
        while duties:
            next_duty()
        own.wait()
        for key, copy in y_copies.items():
            if key[0] == inner - 1:
                copy.wait_recv()
        sent = list(z_copies.values()) + list(y_copies.values()) + sq_copies
        for copy in sent + list(core_copies.values()) + list(chip_copies.values()):
            copy.wait_send()

    shape = jax.ShapeDtypeStruct
    anywhere = pl.BlockSpec(memory_space=pl.ANY)
    vmem = pl.BlockSpec(memory_space=pltpu.VMEM)
    sems = pltpu.SemaphoreType.DMA
    results = pl.pallas_call(
        kernel,
        out_shape=(shape((3, slab, units), bf16),) * parts
        + (
            shape((2, length, span), f32),
            shape((length, 128), f32),
            shape((length, span), bf16),
            shape((length, span), bf16),
            shape((length, span), bf16),
            shape((length, heads), f32),
            shape((length, span), bf16),
            shape((count, width), f32),
            shape((count, 1), f32),
            shape((count, width), f32),
            shape((count, width), bf16),
            shape((8, 128), f32),
        ),
        in_specs=[vmem] * 10 + [anywhere],
        out_specs=(anywhere,) * parts + (vmem,) * 12,
        scratch_shapes=[
            pltpu.VMEM((8, length), f32),
            pltpu.VMEM((tensor - 1, 8, length), f32),
            pltpu.VMEM((chips, count, width), bf16),
            pltpu.VMEM((chips, count, width), bf16),
            pltpu.VMEM((chips, count, width), f32),
            pltpu.VMEM((max(chips - 1, 1), count, width), bf16),
            pltpu.VMEM((max(chips - 1, 1), count, width), bf16),
            sems((outer,)),
            sems((outer,)),
            sems((inner, outer)),
            sems((inner, outer)),
            sems((tensor - 1,)),
            sems((tensor - 1,)),
            sems((chips,)),
            sems((chips,)),
            sems((chips,)),
            sems((chips,)),
            sems(()),
        ],
        compiler_params=pltpu.CompilerParams(
            collective_id=3, has_side_effects=True, vmem_limit_bytes=56 * 2**20
        ),
    )(
        seq, full_qkv, full_out, head_gains, out_gain, tables[0], tables[1],
        blocks[:, None], blocks[None, :], rows, shard,
    )
    pieces = [results[j * outer : (j + 1) * outer] for j in range(inner)]
    return pieces, results[parts:]


def after(value, event):
    return lax.optimization_barrier((value, event))[0]


def inner_sum(grid, grads, event):
    others = [grid.to_inner(grads[j], j) for j in range(1, grid.inner)]
    return low_sum(grads[0], *after(others, event))


def outer_spread(grid, total):
    return [total[0]] + [grid.to_outer(total[step], step) for step in range(1, grid.outer)]


def sequence_scatter(grid, whole):
    rows = whole.shape[0] // grid.tensor
    shaped = whole.reshape(grid.chips, 2, rows, whole.shape[1])
    other = part(shaped, 1, 1 - grid.core_at, 1)[:, 0].astype(jnp.bfloat16)
    own = part(shaped, 1, grid.core_at, 1)[:, 0]
    pair = own + grid.to_core(other).astype(jnp.float32)
    total = part(pair, 0, grid.chip_at, 1)[0]
    for step in range(1, grid.chips):
        away = part(pair, 0, (grid.chip_at + step) % grid.chips, 1)[0].astype(jnp.bfloat16)
        total = total + grid.to_chip(away, step).astype(jnp.float32)
    return total


def sequence_gather(grid, rows):
    count, width = rows.shape
    whole = jnp.zeros((grid.chips, 2, count, width), rows.dtype)
    for step in range(grid.chips):
        here = grid.to_chip(rows, step) if step else rows
        chip = (grid.chip_at - step) % grid.chips
        for value, core in ((here, grid.core_at), (grid.to_core(here), 1 - grid.core_at)):
            whole = lax.dynamic_update_slice(whole, value[None, None], (chip, core, 0, 0))
    return whole.reshape(grid.tensor * count, width)


def unit_kernel_call(rows_low, resid, cotangent, gain, pieces):
    grid = Grid()
    outer, chips = grid.outer, grid.chips
    count, width = rows_low.shape
    units = pieces[0][0].shape[2]
    slab = pieces[0][0].shape[1]
    inner = grid.inner
    flat_pieces = [piece for row in pieces for piece in row]
    parts = len(flat_pieces)
    both = 2 * count
    blocks = outer * chips
    steps = [0] + sorted(range(1, outer), key=lambda s: (min(s, outer - s), s))
    order = [(s, k) for s in steps for k in range(chips)]
    tile = 512
    wide_tiles = width // tile
    unit_tile = min(256, units)
    lines = 32
    bf16, f32 = jnp.bfloat16, jnp.float32
    mesh_id = pl.DeviceIdType.MESH

    def plan(phase):
        block_us, core_us, hop_us = 10.5, 1.0, 2.0
        free = {"tc": 0.0, "x": 0.0, "core": 0.0, "z": 0.0}
        done = {}
        tasks = {}

        def send(link, when, us):
            free[link] = max(free[link], when) + us
            return free[link] + hop_us

        def add(name, needs, us, after=None):
            tasks[name] = (needs, us, after)

        arrive = {}
        for i, s in enumerate(steps[1:]):
            arrive["z", s] = 15.0 + 13.0 * i
        for k in range(1, chips):
            arrive["x", 0, k] = send("x", 0.0, block_us)
        arrive["c", 0, 0] = send("core", 0.0, core_us)

        def zf(s):
            def then(now):
                for k in range(1, chips):
                    arrive["x", s, k] = send("x", now, block_us)
                arrive["c", s, 0] = send("core", now, core_us)

            return then

        def xf(s, k):
            def then(now):
                arrive["c", s, k] = send("core", now, core_us)

            return then

        def compute(u):
            def then(now):
                arrive["cr", u] = send("core", now, core_us)

            return then

        def cr(s, k):
            def then(now):
                if k:
                    arrive["xr", s, k] = send("x", now, block_us)

            return then

        def xr(s):
            def then(now):
                if s:
                    arrive["zr", s] = send("z", now, block_us) + 3.0

            return then

        for s in steps[1:]:
            add(("zf", s), [("at", ("z", s))], 0.3, zf(s))
        for s in steps:
            for k in range(1, chips):
                add(("xf", s, k), [("at", ("x", s, k))], 0.3, xf(s, k))
        for i, (s, k) in enumerate(order):
            needs = [("at", ("c", s, k))]
            if i >= 2:
                needs.append(("do", ("grads" if phase else "compute",) + order[i - 2]))
            add(("load", s, k), needs, 0.2, None)
            needs = [("do", ("load", s, k))]
            if i >= 2:
                needs.append(("do", ("cr",) + order[i - 2]))
            add(("compute", s, k), needs, 3.0, compute((s, k)))
            if phase:
                add(("grads", s, k), [("do", ("compute", s, k))], 3.5, None)
            add(("cr", s, k), [("at", ("cr", (s, k))), ("do", ("compute", s, k))], 0.6, cr(s, k))
        for s in steps:
            needs = [("do", ("cr", s, 0))] + [("at", ("xr", s, k)) for k in range(1, chips)]
            add(("xr", s), needs, 0.6, xr(s))
        for s in steps[1:]:
            add(("zr", s), [("at", ("zr", s)), ("do", ("xr", 0))], 0.6, None)
        if phase:
            needs = [("do", ("xr", s)) for s in steps]
            add(("write", 0), needs + [("do", ("grads",) + unit) for unit in order], 4.0, None)
        result = []
        now = 0.0
        while tasks:
            best = None
            for name, (needs, us, after) in tasks.items():
                ready = 0.0
                for kind, key in needs:
                    table = arrive if kind == "at" else done
                    if key not in table:
                        ready = None
                        break
                    ready = max(ready, table[key] + (1.0 if key[0] == "load" else 0.0))
                if ready is None:
                    continue
                ready = max(ready, now)
                rank = {"compute": 1, "grads": 2, "write": 3}.get(name[0], 0)
                if best is None or (ready, rank) < best[:2]:
                    best = (ready, rank, name)
            ready, _, name = best
            needs, us, after = tasks.pop(name)
            now = ready + us
            done[name] = now
            if after is not None:
                after(now)
            result.append(name)
        return result

    def kernel(
        *refs
    ):
        piece_refs = refs[:parts]
        rows_ref, resid_ref, cot_ref, gain_ref = refs[parts : parts + 4]
        out_ref, dres_ref, gain_out, all_x, all_dm = refs[parts + 4 : parts + 9]
        grad_refs = refs[parts + 9 : parts + 9 + 3 * inner]
        rest = refs[parts + 9 + 3 * inner :]
        body(piece_refs, rows_ref, resid_ref, cot_ref, gain_ref, out_ref, dres_ref, gain_out, all_x, all_dm, grad_refs, *rest)

    def body(
        piece_refs, rows_ref, resid_ref, cot_ref, gain_ref,
        out_ref, dres_ref, gain_out, all_x, all_dm, grad_refs,
        wg, wu, wd, xb, db, act, act_t, coef_gate, coef_up, d_gate, d_up, d_gate_t, d_up_t, acc_gate, acc_up, acc_down, stage,
        core_send, core_land, hold, keep, chip_send, chip_land, outer_send, outer_land, raw, d_mlp,
        s_outer, r_outer, s_chip, r_chip, s_core, r_core,
        s_core_sum, r_core_sum, s_chip_sum, r_chip_sum, s_outer_sum, r_outer_sum, local, local_w, local_g,
    ):
        g = Grid()
        core_peer = (g.dp_at, g.chip_at * 2 + 1 - g.core_at)

        def chip_peer(k):
            return (g.dp_at, lax.rem(g.chip_at + k + chips, chips) * 2 + g.core_at)

        def outer_peer(s):
            return (lax.rem(g.outer_at + s + outer, outer) * g.inner + g.inner_at, g.tensor_at)

        greet(
            [core_peer]
            + [chip_peer(k) for k in range(1, chips)]
            + [outer_peer(s) for s in range(1, outer)]
        )

        def remote(src, dst, send, recv, peer):
            return pltpu.make_async_remote_copy(
                src_ref=src, dst_ref=dst, send_sem=send, recv_sem=recv,
                device_id=peer, device_id_type=mesh_id,
            )

        def dot(a, b, contract):
            return lax.dot_general(a, b, (contract, ((), ())), preferred_element_type=f32)

        def looped(total, body):
            lax.fori_loop(0, total, lambda i, c: (body(i), c)[1], 0)

        def by_lines(body):
            looped(count // lines, lambda i: body(pl.ds(pl.multiple_of(i * lines, lines), lines)))

        def by_tiles(body):
            looped(wide_tiles, lambda i: body(pl.ds(pl.multiple_of(i * tile, tile), tile)))

        weights = (wg, wu, wd)
        fetches = []
        for j in range(inner):
            for s in range(outer):
                index = lax.rem(g.outer_at - s + outer, outer) * inner
                index = index + lax.rem(g.inner_at - j + inner, inner)
                span = pl.ds(pl.multiple_of(index * slab, slab), slab)
                for c in range(3):
                    at = j * outer + s
                    fetches.append(
                        pltpu.make_async_copy(
                            piece_refs[at].at[c], weights[c].at[span], local_w.at[at, c]
                        )
                    )
        started = []

        def run(phase, source, everything, fetched, compute, grads, write):
            mine = pl.ds(0, count)
            theirs = pl.ds(count, count)
            copies = {}

            def start(key, copy):
                copy.start()
                copies[key] = copy
                started.append(copy)

            def at(s, k, half):
                return everything.at[s, k, half]

            def core_copy(s, k, src):
                start(
                    ("c", s, k),
                    remote(src, at(s, k, theirs), s_core.at[phase, s, k], r_core.at[phase, s, k], core_peer),
                )

            def chip_copy(s, k, src):
                start(
                    ("x", s, k),
                    remote(src, at(s, k, mine), s_chip.at[phase, s, k], r_chip.at[phase, s, k], chip_peer(k)),
                )

            for s in steps[1:]:
                start(
                    ("z", s),
                    remote(source, at(s, 0, mine), s_outer.at[phase, s], r_outer.at[phase, s], outer_peer(s)),
                )
            for k in range(1, chips):
                chip_copy(0, k, source)
            core_copy(0, 0, source)
            own = pltpu.make_async_copy(source, at(0, 0, mine), local.at[phase, 0, blocks])
            own.start()
            if phase == 0:
                for copy in fetches:
                    copy.start()
            slots = {unit: i % 2 for i, unit in enumerate(order)}
            loads = {}
            sums = {}
            for task in plan(phase):
                name, s = task[:2]
                k = task[2] if len(task) > 2 else 0
                unit = s * chips + k
                if name == "zf":
                    copies["z", s].wait_recv()
                    for j in range(1, chips):
                        chip_copy(s, j, at(s, 0, mine))
                    core_copy(s, 0, at(s, 0, mine))
                elif name == "xf":
                    copies["x", s, k].wait_recv()
                    core_copy(s, k, at(s, k, mine))
                elif name == "load":
                    copies["c", s, k].wait_recv()
                    if (s, k) == (0, 0):
                        own.wait()
                    slot = slots[s, k]
                    loads[s, k] = []
                    for j, (src, dst) in enumerate(fetched):
                        copy = pltpu.make_async_copy(
                            src.at[s, k], dst.at[slot], local.at[phase, j, unit]
                        )
                        copy.start()
                        loads[s, k].append(copy)
                elif name == "compute":
                    if phase == 0 and (s, k) == order[0]:
                        for copy in fetches:
                            copy.wait()
                    for copy in loads[s, k]:
                        copy.wait()
                    i = order.index((s, k))
                    if i >= 2:
                        sums["core", order[i - 2]].wait_send()
                    slot = slots[s, k]

                    def send(slot=slot, unit=unit, s=s, k=k):
                        copy = remote(
                            core_send.at[slot], core_land.at[unit],
                            s_core_sum.at[phase, unit], r_core_sum.at[phase, unit], core_peer,
                        )
                        copy.start()
                        sums["core", (s, k)] = copy

                    compute(slot, unit, send)
                elif name == "grads":
                    grads(slots[s, k], unit)
                elif name == "write":
                    write()
                elif name == "cr":
                    sums["core", (s, k)].wait_recv()
                    slot = slots[s, k]
                    if k == 0:

                        def add_core(at_rows, s=s, slot=slot, unit=unit):
                            keep[s, at_rows] = hold[slot, at_rows] + core_land[unit, at_rows].astype(f32)

                        by_lines(add_core)
                    else:
                        there = s * (chips - 1) + k - 1

                        def add_core(at_rows, there=there, slot=slot, unit=unit):
                            total = hold[slot, at_rows] + core_land[unit, at_rows].astype(f32)
                            chip_send[there, at_rows] = total.astype(bf16)

                        by_lines(add_core)
                        copy = remote(
                            chip_send.at[there], chip_land.at[there],
                            s_chip_sum.at[phase, there], r_chip_sum.at[phase, there], chip_peer(-k),
                        )
                        copy.start()
                        sums["chip", (s, k)] = copy
                elif name == "xr":
                    for j in range(1, chips):
                        sums["chip", (s, j)].wait_recv()

                    def add_chip(at_rows, s=s):
                        total = keep[s, at_rows]
                        for j in range(1, chips):
                            total = total + chip_land[s * (chips - 1) + j - 1, at_rows].astype(f32)
                        if s == 0:
                            raw[at_rows] = total
                        else:
                            outer_send[s - 1, at_rows] = total.astype(bf16)

                    by_lines(add_chip)
                    if s:
                        copy = remote(
                            outer_send.at[s - 1], outer_land.at[s - 1],
                            s_outer_sum.at[phase, s], r_outer_sum.at[phase, s], outer_peer(-s),
                        )
                        copy.start()
                        sums["outer", s] = copy
                elif name == "zr":
                    sums["outer", s].wait_recv()

                    def add_outer(at_rows, s=s):
                        raw[at_rows] = raw[at_rows] + outer_land[s - 1, at_rows].astype(f32)

                    by_lines(add_outer)
            waited = [sums["core", unit] for unit in order[-2:]]
            waited += [copy for key, copy in sums.items() if key[0] != "core"]
            for copy in waited:
                copy.wait_send()
            for copy in started:
                copy.wait_send()
            started.clear()

        def forward(slot, unit, send):
            for j in range(units // unit_tile):
                cols = pl.ds(j * unit_tile, unit_tile)
                rows = xb[slot]
                gate = dot(rows, wg[:, cols], ((1,), (0,)))
                up = dot(rows, wu[:, cols], ((1,), (0,)))
                sigma = jax.nn.sigmoid(gate)
                silu = gate * sigma
                value = silu * up
                act[:, cols] = value.astype(bf16)
                act_t[unit, cols] = value.T.astype(bf16)
                coef_up[unit, :, cols] = silu.astype(bf16)
                coef_gate[unit, :, cols] = (up * sigma * (1.0 + gate * (1.0 - sigma))).astype(bf16)

            def down(cols):
                part_sum = dot(act[...], wd[cols, :], ((1,), (1,)))
                hold[slot, :, cols] = part_sum[:count]
                core_send[slot, :, cols] = part_sum[count:].astype(bf16)

            by_tiles(down)
            send()

        def between():
            def lines_of(i, total):
                at_rows = pl.ds(pl.multiple_of(i * lines, lines), lines)
                value = raw[at_rows]
                scale = lax.rsqrt(jnp.mean(value * value, axis=1, keepdims=True) + norm_eps)
                hat = value * scale
                gain_row = gain_ref[...]
                out_ref[at_rows] = (resid_ref[at_rows] + hat * gain_row).astype(bf16)
                top = cot_ref[at_rows].astype(f32)
                upstream = top * gain_row
                inner = jnp.mean(upstream * hat, axis=1, keepdims=True)
                d_mlp[at_rows] = (scale * (upstream - hat * inner)).astype(bf16)
                return total + jnp.sum(top * hat, axis=0, keepdims=True)

            gain_out[...] = lax.fori_loop(
                0, count // lines, lines_of, jnp.zeros((1, width), f32)
            )

        def backward(slot, unit, send):
            for j in range(units // unit_tile):
                cols = pl.ds(j * unit_tile, unit_tile)
                d_act = dot(db[slot], wd[:, cols], ((1,), (0,)))
                value = d_act * coef_gate[unit, :, cols].astype(f32)
                d_gate[:, cols] = value.astype(bf16)
                d_gate_t[slot, cols] = value.T.astype(bf16)
                value = d_act * coef_up[unit, :, cols].astype(f32)
                d_up[:, cols] = value.astype(bf16)
                d_up_t[slot, cols] = value.T.astype(bf16)

            def into(cols):
                part_sum = dot(d_gate[...], wg[cols, :], ((1,), (1,)))
                part_sum = part_sum + dot(d_up[...], wu[cols, :], ((1,), (1,)))
                hold[slot, :, cols] = part_sum[:count]
                core_send[slot, :, cols] = part_sum[count:].astype(bf16)

            by_tiles(into)
            send()

        def weight_grads(slot, unit):
            first = unit == order[0][0] * chips + order[0][1]

            def grads(cols):
                def put_sum(ref, where, value):
                    if first:
                        ref[where] = value
                    else:
                        ref[where] = ref[where] + value

                rows = xb[slot, :, cols]
                put_sum(acc_gate, (slice(None), cols), dot(d_gate_t[slot], rows, ((1,), (0,))))
                put_sum(acc_up, (slice(None), cols), dot(d_up_t[slot], rows, ((1,), (0,))))
                rows = db[slot, :, cols]
                put_sum(acc_down, (slice(None), cols), dot(act_t[unit], rows, ((1,), (0,))))

            by_tiles(grads)

        def write_grads():
            copies = []
            for j in range(inner):
                for s in range(outer):
                    index = lax.rem(g.outer_at + s, outer) * inner
                    index = index + lax.rem(g.inner_at + j, inner)
                    span = pl.ds(pl.multiple_of(index * slab, slab), slab)
                    slot = len(copies) % 2
                    if len(copies) >= 2:
                        for copy in copies[-2]:
                            copy.wait()
                    batch = []
                    for c, acc in enumerate((acc_gate, acc_up, acc_down)):
                        stage[slot, c] = acc[:, span].astype(bf16)
                        copy = pltpu.make_async_copy(
                            stage.at[slot, c], grad_refs[j * 3 + c].at[s], local_g.at[slot, c]
                        )
                        copy.start()
                        batch.append(copy)
                    copies.append(batch)
            for batch in copies[-2:]:
                for copy in batch:
                    copy.wait()

        run(0, rows_ref, all_x, [(all_x, xb)], forward, None, None)
        between()
        run(1, d_mlp, all_dm, [(all_dm, db), (all_x, xb)], backward, weight_grads, write_grads)

        def close(at_rows):
            dres_ref[at_rows] = raw[at_rows] + cot_ref[at_rows].astype(f32)

        by_lines(close)

    def held_in(space):
        return pl.BlockSpec(memory_space=space)

    shape = jax.ShapeDtypeStruct
    anywhere, near = held_in(pl.ANY), held_in(pltpu.VMEM)
    sems = pltpu.SemaphoreType.DMA
    links = outer * (chips - 1)
    flops = 2 * 9 * both * blocks * width * units
    results = pl.pallas_call(
        kernel,
        out_shape=(
            shape((count, width), bf16),
            shape((count, width), f32),
            shape((1, width), f32),
            shape((outer, chips, both, width), bf16),
            shape((outer, chips, both, width), bf16),
        )
        + (shape((outer, units, slab), bf16),) * (3 * inner),
        in_specs=[anywhere] * (parts + 1) + [near] * 3,
        out_specs=(near, near, near) + (anywhere,) * (2 + 3 * inner),
        scratch_shapes=[
            pltpu.VMEM((width, units), bf16),
            pltpu.VMEM((width, units), bf16),
            pltpu.VMEM((width, units), bf16),
            pltpu.VMEM((2, both, width), bf16),
            pltpu.VMEM((2, both, width), bf16),
            pltpu.VMEM((both, units), bf16),
            pltpu.VMEM((blocks, units, both), bf16),
            pltpu.VMEM((blocks, both, units), bf16),
            pltpu.VMEM((blocks, both, units), bf16),
            pltpu.VMEM((both, units), bf16),
            pltpu.VMEM((both, units), bf16),
            pltpu.VMEM((2, units, both), bf16),
            pltpu.VMEM((2, units, both), bf16),
            pltpu.VMEM((units, width), f32),
            pltpu.VMEM((units, width), f32),
            pltpu.VMEM((units, width), f32),
            pltpu.VMEM((2, 3, units, slab), bf16),
            pltpu.VMEM((2, count, width), bf16),
            pltpu.VMEM((blocks, count, width), bf16),
            pltpu.VMEM((2, count, width), f32),
            pltpu.VMEM((outer, count, width), f32),
            pltpu.VMEM((links, count, width), bf16),
            pltpu.VMEM((links, count, width), bf16),
            pltpu.VMEM((outer - 1, count, width), bf16),
            pltpu.VMEM((outer - 1, count, width), bf16),
            pltpu.VMEM((count, width), f32),
            pltpu.VMEM((count, width), bf16),
            sems((2, outer)),
            sems((2, outer)),
            sems((2, outer, chips)),
            sems((2, outer, chips)),
            sems((2, outer, chips)),
            sems((2, outer, chips)),
            sems((2, blocks)),
            sems((2, blocks)),
            sems((2, links)),
            sems((2, links)),
            sems((2, outer)),
            sems((2, outer)),
            sems((2, 2, blocks + 1)),
            sems((parts, 3)),
            sems((2, 3)),
        ],
        compiler_params=pltpu.CompilerParams(
            collective_id=2, has_side_effects=True, vmem_limit_bytes=60 * 2**20
        ),
        cost_estimate=pl.CostEstimate(flops=flops, bytes_accessed=64 * 2**20, transcendentals=0),
    )(*flat_pieces, rows_low, resid, cotangent, gain)
    grads = results[5:]
    return results[:3] + ([[grads[j * 3 + c] for j in range(inner)] for c in range(3)],)


def adam_kernel(w_ref, m_ref, v_ref, g_ref, *rest):
    scale_ref = rest[0] if len(rest) == 5 else None
    w_out, m_out, v_out, c_out = rest[-4:]
    grad = g_ref[...].astype(jnp.float32)
    new, first, second = adam_step(
        w_ref[...], grad, m_ref[...], v_ref[...], rate_matrix, weight_decay
    )
    if scale_ref is not None:
        new = new * scale_ref[...]
    w_out[...] = new
    m_out[...] = first
    v_out[...] = second
    c_out[...] = new.astype(jnp.bfloat16)


def adam_call(param, grad, first, second, scale=None):
    shape = param.shape
    flat = [v.reshape(-1, shape[-1]) for v in (param, first, second, grad)]
    rows, width = flat[0].shape
    block = min(rows, max(16, (1 << 17) // width))
    spec = pl.BlockSpec((block, width), lambda k: (k, 0))
    specs = [spec] * 4
    if scale is not None:
        per = shape[1] // block
        flat.append(scale)
        specs.append(pl.BlockSpec((None, 1, width), lambda k: (k // per, 0, 0)))
    outs = [jax.ShapeDtypeStruct((rows, width), jnp.float32)] * 3
    outs.append(jax.ShapeDtypeStruct((rows, width), jnp.bfloat16))
    size = rows * width
    result = pl.pallas_call(
        adam_kernel,
        grid=(rows // block,),
        in_specs=specs,
        out_specs=[spec] * 4,
        out_shape=outs,
        cost_estimate=pl.CostEstimate(
            flops=20 * size, bytes_accessed=28 * size, transcendentals=2 * size
        ),
        compiler_params=pltpu.CompilerParams(vmem_limit_bytes=32 * 2**20),
    )(*flat)
    return [v.reshape(shape) for v in result]


def adam_units_kernel(turned, at_ref, w_ref, m_ref, v_ref, g_ref, w_out, m_out, v_out, c_out):
    grad = g_ref[...].astype(jnp.float32)
    if turned:
        grad = grad.T
    new, first, second = adam_step(
        w_ref[...], grad, m_ref[...], v_ref[...], rate_matrix, weight_decay
    )
    w_out[...] = new
    m_out[...] = first
    v_out[...] = second
    c_out[...] = new.astype(jnp.bfloat16)


def adam_units(grid, param, first, second, grads, turned):
    n = grid.outer
    stacked = jnp.stack([jnp.stack(pieces) for pieces in grads])
    mats, _, units, wide = stacked.shape
    if not turned:
        spec = pl.BlockSpec((units, wide), lambda c, k, at: (k, 0))
    else:
        spec = pl.BlockSpec((None, wide, units), lambda c, k, at: (c, 0, k))
    grad_spec = pl.BlockSpec(
        (None, None, units, wide), lambda c, k, at: (c, lax.rem(at[0] - k + n, n), 0, 0)
    )
    size = param.size
    outs = [jax.ShapeDtypeStruct(param.shape, jnp.float32)] * 3
    outs.append(jax.ShapeDtypeStruct(param.shape, jnp.bfloat16))
    return pl.pallas_call(
        functools.partial(adam_units_kernel, turned),
        grid_spec=pltpu.PrefetchScalarGridSpec(
            num_scalar_prefetch=1,
            grid=(mats, n),
            in_specs=[spec] * 3 + [grad_spec],
            out_specs=[spec] * 4,
        ),
        out_shape=outs,
        cost_estimate=pl.CostEstimate(
            flops=20 * size, bytes_accessed=28 * size, transcendentals=2 * size
        ),
        compiler_params=pltpu.CompilerParams(vmem_limit_bytes=32 * 2**20),
    )(grid.outer_at.astype(jnp.int32)[None], param, first, second, stacked)


def local(
    tokens,
    cotangent,
    block_ids,
    w_qkv,
    m_qkv,
    v_qkv,
    w_out,
    m_out,
    v_out,
    w_gu,
    m_gu,
    v_gu,
    w_down,
    m_down,
    v_down,
    gains,
    gain_m,
    gain_v,
):
    grid = Grid()
    local_x = tokens[0]
    gain_count = gains.shape[0]
    low_gains = jnp.pad(gains.astype(jnp.bfloat16), ((0, 16 - gain_count), (0, 0)))
    full_qkv, full_out, full_gains, seq_x = path_gather(
        w_qkv.astype(jnp.bfloat16), w_out.astype(jnp.bfloat16), low_gains, local_x
    )
    gain_rows = jnp.swapaxes(full_gains[:, :gain_count], 0, 1).reshape(gain_count, -1)
    gain_rows = gain_rows.astype(jnp.float32)
    shard = jnp.stack([w_gu[0], w_gu[1], w_down.T]).astype(jnp.bfloat16)
    full_qkv, shard = lax.optimization_barrier((full_qkv, shard))
    model_width = local_x.shape[1]
    length = seq_x.shape[0]
    span = full_qkv.shape[2]
    heads_here = span // HEAD
    offset = lax.axis_index("tensor") * span
    q_gain = lax.dynamic_slice_in_dim(gain_rows[0], offset, span)
    k_gain = lax.dynamic_slice_in_dim(gain_rows[1], offset, span)
    cosine, sine = rope_tables(length, HEAD)

    def unrotary(grad):
        return (grad * cosine + rotate_back(grad * sine)).reshape(length, span)

    pieces, kept = attend_call(
        seq_x,
        full_qkv,
        full_out,
        jnp.stack([q_gain, k_gain]),
        gain_rows[2:3],
        (cosine[:, 0], sine[:, 0]),
        block_ids[0],
        local_x,
        shard,
    )
    hats, scales, q_low, k_low, v_low, log_total, context_low = kept[:7]
    attn_hat, o_scale, resid, resid_low, tops = kept[7:]
    q_hat, k_hat = hats[0], hats[1]
    q_scale, k_scale = scales[:, 0:1], scales[:, 1:2]
    q_low, k_low, v_low = [v.reshape(length, heads_here, HEAD) for v in (q_low, k_low, v_low)]
    blocks = block_ids[0]
    block_rows = min(512, length)
    block_count = length // block_rows
    scale = HEAD ** (-0.5)
    starts = jnp.arange(block_count, dtype=jnp.int32) * block_rows

    def scores_of(start):
        q_part = lax.dynamic_slice_in_dim(q_low, start, block_rows, 0)
        b_part = lax.dynamic_slice_in_dim(blocks, start, block_rows, 0)
        raw = jnp.einsum("qhd,khd->hqk", q_part, k_low, preferred_element_type=jnp.float32) * scale
        allowed = blocks[None, None, :] <= b_part[None, :, None]
        return (jnp.where(allowed, raw, masked_value), q_part)

    log_total = jnp.swapaxes(log_total.reshape(block_count, block_rows, heads_here), 1, 2)
    output, d_resid, gain_last, unit_grads = unit_kernel_call(
        resid_low, resid, cotangent[0], gain_rows[3:4], pieces
    )
    gain_attn = jnp.sum(d_resid * attn_hat, axis=0)
    d_attn = norm_back(o_scale, attn_hat, d_resid * gain_rows[2]).astype(jnp.bfloat16)
    seq_do = sequence_gather(grid, d_attn)
    grad_out = jnp.einsum("se,sd->ed", context_low, seq_do, preferred_element_type=jnp.float32)
    d_context = jnp.einsum("sd,ed->se", seq_do, full_out, preferred_element_type=jnp.float32)
    d_context = d_context.astype(jnp.bfloat16).reshape(length, heads_here, HEAD)
    part_gate = outer_spread(grid, inner_sum(grid, unit_grads[0], d_context))

    def backward_block(carry, item):
        key_acc, value_acc = carry
        start, log_part = item
        masked, q_part = scores_of(start)
        probs = jnp.exp(masked - log_part[:, :, None])
        dc_part = lax.dynamic_slice_in_dim(d_context, start, block_rows, 0)
        d_probs = jnp.einsum("qhd,khd->hqk", dc_part, v_low, preferred_element_type=jnp.float32)
        inner = jnp.sum(probs * d_probs, axis=2, keepdims=True)
        d_scores = (probs * (d_probs - inner)).astype(jnp.bfloat16)
        d_query = (
            jnp.einsum("hqk,khd->qhd", d_scores, k_low, preferred_element_type=jnp.float32) * scale
        )
        key_acc = (
            key_acc
            + jnp.einsum("hqk,qhd->khd", d_scores, q_part, preferred_element_type=jnp.float32)
            * scale
        )
        value_acc = value_acc + jnp.einsum(
            "hqk,qhd->khd", probs.astype(jnp.bfloat16), dc_part, preferred_element_type=jnp.float32
        )
        return ((key_acc, value_acc), d_query)

    empty = jnp.zeros((length, heads_here, HEAD), jnp.float32)
    (d_krot, d_values), d_qrot = lax.scan(backward_block, (empty, empty), (starts, log_total))
    d_qrot = d_qrot.reshape(length, heads_here, HEAD)
    d_qnorm = unrotary(d_qrot)
    d_knorm = unrotary(d_krot)
    head_gains = jnp.stack([jnp.sum(d_qnorm * q_hat, axis=0), jnp.sum(d_knorm * k_hat, axis=0)])
    placed = lax.dynamic_update_slice(
        jnp.zeros((2, model_width), jnp.float32), head_gains, (0, offset)
    )
    gain_terms = jnp.concatenate([placed, jnp.stack([gain_attn, gain_last[0]])], axis=0)
    dq_hat = d_qnorm * q_gain
    dk_hat = d_knorm * k_gain
    q_inner, k_inner = lax.psum(
        (jnp.sum(dq_hat * q_hat, axis=1), jnp.sum(dk_hat * k_hat, axis=1)), "tensor"
    )
    part_up = outer_spread(grid, inner_sum(grid, unit_grads[1], d_qrot))
    d_query = q_scale * (dq_hat - q_hat * (q_inner / model_width)[:, None])
    d_key = k_scale * (dk_hat - k_hat * (k_inner / model_width)[:, None])
    d_qkv = jnp.stack([d_query, d_key, d_values.reshape(length, span)]).astype(jnp.bfloat16)
    grad_qkv = jnp.einsum("sd,cse->cde", seq_x, d_qkv, preferred_element_type=jnp.float32)
    part_down = outer_spread(grid, inner_sum(grid, unit_grads[2], grad_qkv))
    terms = jnp.swapaxes(gain_terms.reshape(gain_count, grid.dp, -1), 0, 1)
    part_qkv, part_out, part_gains, tops = path_scatter(
        grad_qkv.astype(jnp.bfloat16),
        grad_out.astype(jnp.bfloat16),
        jnp.pad(terms, ((0, 0), (0, 8 - gain_count), (0, 0))),
        tops,
    )
    part_gains = part_gains[:gain_count]
    part_gate, part_up, part_down = after((part_gate, part_up, part_down), part_qkv)
    grad_tokens = d_resid + sequence_scatter(
        grid, jnp.einsum("cse,cde->sd", d_qkv, full_qkv, preferred_element_type=jnp.float32)
    )
    head_top = tops[:heads_here, 0]
    factor = clip_tau / jnp.maximum(head_top, clip_tau)
    column = jnp.repeat(jnp.sqrt(factor), HEAD)
    column_scale = jnp.stack([column, column, jnp.ones_like(column)])[:, None, :]
    new_qkv, new_m_qkv, new_v_qkv, copy_qkv = adam_call(
        w_qkv, part_qkv, m_qkv, v_qkv, column_scale
    )
    new_out, new_m_out, new_v_out, copy_out = adam_call(w_out, part_out, m_out, v_out)
    new_gu, new_m_gu, new_v_gu, copy_gu = adam_units(
        grid, w_gu, m_gu, v_gu, [part_gate, part_up], True
    )
    new_down, new_m_down, new_v_down, copy_down = adam_units(
        grid, w_down, m_down, v_down, [part_down], False
    )
    new_gains, new_gain_m, new_gain_v = adam_step(gains, part_gains, gain_m, gain_v, rate_gain, 0.0)
    return (
        output[None],
        grad_tokens[None],
        new_qkv,
        new_m_qkv,
        new_v_qkv,
        copy_qkv,
        new_out,
        new_m_out,
        new_v_out,
        copy_out,
        new_gu,
        new_m_gu,
        new_v_gu,
        copy_gu,
        new_down,
        new_m_down,
        new_v_down,
        copy_down,
        new_gains,
        new_gain_m,
        new_gain_v,
        factor,
    )


def solution(mesh):
    return jax.shard_map(
        local,
        mesh=mesh,
        in_specs=(
            P("dp", "tensor", None),
            P("dp", "tensor", None),
            P("dp", None),
            P(None, "dp", "tensor"),
            P(None, "dp", "tensor"),
            P(None, "dp", "tensor"),
            P("tensor", "dp"),
            P("tensor", "dp"),
            P("tensor", "dp"),
            P(None, "dp", "tensor"),
            P(None, "dp", "tensor"),
            P(None, "dp", "tensor"),
            P("tensor", "dp"),
            P("tensor", "dp"),
            P("tensor", "dp"),
            P(None, "dp"),
            P(None, "dp"),
            P(None, "dp"),
        ),
        out_specs=(
            P("dp", "tensor", None),
            P("dp", "tensor", None),
            P(None, "dp", "tensor"),
            P(None, "dp", "tensor"),
            P(None, "dp", "tensor"),
            P(None, "dp", "tensor"),
            P("tensor", "dp"),
            P("tensor", "dp"),
            P("tensor", "dp"),
            P("tensor", "dp"),
            P(None, "dp", "tensor"),
            P(None, "dp", "tensor"),
            P(None, "dp", "tensor"),
            P(None, "dp", "tensor"),
            P("tensor", "dp"),
            P("tensor", "dp"),
            P("tensor", "dp"),
            P("tensor", "dp"),
            P(None, "dp"),
            P(None, "dp"),
            P(None, "dp"),
            P("tensor"),
        ),
        check_vma=False,
    )
```

```python
import functools

import jax
import jax.numpy as jnp
from jax import lax
from jax.experimental import pallas as pl
from jax.experimental.pallas import tpu as pltpu
from jax.sharding import PartitionSpec as P

HEAD = 128
STEP = 5


norm_eps = 1e-06
rope_base = 500000.0
beta_one = 0.9
beta_two = 0.95
rate_matrix = 0.01
rate_gain = 0.6
weight_decay = 0.1
adam_eps = 1e-08
clip_tau = 9.0
masked_value = -1e30


def rope_tables(length, size):
    half = size // 2
    freq = rope_base ** (-(jnp.arange(half, dtype=jnp.float32) * 2.0 / size))
    angle = jnp.arange(length, dtype=jnp.float32)[:, None] * freq[None, :]
    angle = jnp.concatenate([angle, angle], axis=1)
    return (jnp.cos(angle)[:, None, :], jnp.sin(angle)[:, None, :])


def rotate_fwd(value):
    half = value.shape[-1] // 2
    return jnp.concatenate([-value[..., half:], value[..., :half]], axis=-1)


def rotate_back(value):
    half = value.shape[-1] // 2
    return jnp.concatenate([value[..., half:], -value[..., :half]], axis=-1)


def adam_step(param, grad, first, second, rate, decay):
    first = beta_one * first + (1.0 - beta_one) * grad
    second = beta_two * second + (1.0 - beta_two) * grad * grad
    fix_one = 1.0 - beta_one**STEP
    fix_two = 1.0 - beta_two**STEP
    update = first / fix_one / (jnp.sqrt(second / fix_two) + adam_eps)
    return (param - rate * (update + decay * param), first, second)


def norm_back(scale_factor, normed, upstream):
    inner = jnp.mean(upstream * normed, axis=1, keepdims=True)
    return scale_factor * (upstream - normed * inner)


class Grid:
    def __init__(self):
        self.dp = lax.axis_size("dp")
        self.tensor = lax.axis_size("tensor")
        self.inner = 1
        while self.inner * self.inner * 4 <= self.dp:
            self.inner *= 2
        self.outer = self.dp // self.inner
        self.chips = self.tensor // 2
        self.dp_at = lax.axis_index("dp")
        self.tensor_at = lax.axis_index("tensor")
        self.inner_at = self.dp_at % self.inner
        self.chip_at = self.tensor_at // 2
        self.core_at = self.tensor_at % 2
        self.outer_at = self.dp_at // self.inner

    def path_of(self, index):
        column, row = index // self.inner, index % self.inner
        return row * self.outer + column + (row % 2) * (self.outer - 1 - 2 * column)

    def index_of(self, place):
        row, column = place // self.outer, place % self.outer
        return (column + (row % 2) * (self.outer - 1 - 2 * column)) * self.inner + row

    def to_outer(self, value, step):
        n, m = self.outer, self.inner
        pairs = [(a * m + b, (a + step) % n * m + b) for a in range(n) for b in range(m)]
        return lax.ppermute(value, "dp", pairs)

    def to_inner(self, value, step):
        n, m = self.outer, self.inner
        pairs = [(a * m + b, a * m + (b + step) % m) for a in range(n) for b in range(m)]
        return lax.ppermute(value, "dp", pairs)

    def to_chip(self, value, step):
        n = self.chips
        pairs = [(a * 2 + b, (a + step) % n * 2 + b) for a in range(n) for b in range(2)]
        return lax.ppermute(value, "tensor", pairs)

    def to_core(self, value):
        pairs = [(a * 2 + b, a * 2 + 1 - b) for a in range(self.chips) for b in range(2)]
        return lax.ppermute(value, "tensor", pairs)

    def across(self, value, axis, bit):
        count = lax.axis_size(axis)
        return lax.ppermute(value, axis, [(i, i ^ bit) for i in range(count)])


def bits(count):
    return [1 << k for k in range(count.bit_length() - 1)]


def part(value, axis, index, size):
    return lax.dynamic_slice_in_dim(value, index * size, size, axis)


def put(whole, piece, axis, index):
    return lax.dynamic_update_slice_in_dim(whole, piece, index * piece.shape[axis], axis)


def low_sum(*terms):
    total = terms[0].astype(jnp.float32)
    for term in terms[1:]:
        total = total + term.astype(jnp.float32)
    return total.astype(jnp.bfloat16)


def greet(peers):
    barrier = pltpu.get_barrier_semaphore()
    for peer in peers:
        pl.semaphore_signal(barrier, inc=1, device_id=peer, device_id_type=pl.DeviceIdType.MESH)
    pl.semaphore_wait(barrier, len(peers))


def path_gather(shard, flat, gains, rows):
    grid = Grid()
    n, chips, tensor = grid.dp, grid.chips, grid.tensor
    lead, deep, wide = shard.shape
    half = deep // 2
    tall, thin = flat.shape
    part_tall = tall // 2
    count = rows.shape[0]
    ring = 2 * lead + 3

    def kernel(
        shard_ref, flat_ref, gains_ref, rows_ref, full, full_flat, full_gains, sequence,
        sends, lands, row_sends, row_lands, own,
    ):
        g = Grid()
        dp_at, t_at = g.dp_at, g.tensor_at
        chip_at, core_at = t_at // 2, t_at % 2
        place = g.path_of(dp_at)
        after = g.index_of(lax.rem(place + 1, n))
        before = g.index_of(lax.rem(place + n - 1, n))
        core_peer = (dp_at, chip_at * 2 + 1 - core_at)
        chip_peers = [
            (dp_at, lax.rem(chip_at + k, chips) * 2 + core_at) for k in range(1, chips)
        ]
        greet([(after, t_at), (before, t_at), core_peer] + chip_peers)

        def views(item, index):
            if item == ring - 1:
                return 1, gains_ref, full_gains.at[index]
            if item >= 2 * lead:
                side = item - 2 * lead
                span = pl.ds(side * part_tall, part_tall)
                cols = pl.ds(pl.multiple_of(index * thin, thin), thin)
                return 1 - 2 * side, flat_ref.at[span], full_flat.at[span, cols]
            side, c = item // lead, item % lead
            span = pl.ds(pl.multiple_of(index * deep + side * half, half), half)
            return 1 - 2 * side, shard_ref.at[c, pl.ds(side * half, half)], full.at[c, span]

        def hop(step, item):
            way = views(item, 0)[0]
            index = g.index_of(lax.rem(place - way * step + n, n))
            _, source, target = views(item, index)
            return pltpu.make_async_remote_copy(
                src_ref=source if step == 0 else target,
                dst_ref=target,
                send_sem=sends.at[step, item],
                recv_sem=lands.at[step, item],
                device_id=(after if way == 1 else before, t_at),
                device_id_type=pl.DeviceIdType.MESH,
            )

        def rows_at(index):
            return sequence.at[pl.ds(pl.multiple_of(index * count, count), count)]

        def row_copy(slot, index, peer, first):
            return pltpu.make_async_remote_copy(
                src_ref=rows_ref if first else rows_at(index),
                dst_ref=rows_at(index),
                send_sem=row_sends.at[slot],
                recv_sem=row_lands.at[slot],
                device_id=peer,
                device_id_type=pl.DeviceIdType.MESH,
            )

        order = [c + side * lead for c in range(lead) for side in (0, 1)]
        order += list(range(2 * lead, ring))
        hops = {}
        for item in order:
            hops[0, item] = hop(0, item)
            hops[0, item].start()
        moves = []
        for k in range(1, chips):
            moves.append(row_copy(k - 1, t_at, chip_peers[k - 1], True))
            moves[-1].start()
        mine = row_copy(chips - 1, t_at, core_peer, True)
        mine.start()
        keep = [
            pltpu.make_async_copy(
                shard_ref, full.at[:, pl.ds(pl.multiple_of(dp_at * deep, deep), deep)], own.at[0]
            ),
            pltpu.make_async_copy(gains_ref, full_gains.at[dp_at], own.at[1]),
            pltpu.make_async_copy(rows_ref, rows_at(t_at), own.at[2]),
            pltpu.make_async_copy(
                flat_ref, full_flat.at[:, pl.ds(pl.multiple_of(dp_at * thin, thin), thin)], own.at[3]
            ),
        ]
        for copy in keep:
            copy.start()
        passed = []
        for step in range(1, n - 1):
            for item in order:
                hops[step - 1, item].wait_recv()
                hops[step, item] = hop(step, item)
                hops[step, item].start()
            if step <= chips - 1:
                moves[step - 1].wait_recv()
                source = lax.rem(chip_at - step + chips, chips) * 2 + core_at
                passed.append(row_copy(chips - 1 + step, source, core_peer, False))
                passed[-1].start()
        for item in order:
            hops[n - 2, item].wait_recv()
        mine.wait_recv()
        for copy in passed:
            copy.wait_recv()
        for key in hops:
            hops[key].wait_send()
        for copy in moves + [mine] + passed:
            copy.wait_send()
        for copy in keep:
            copy.wait()

    bf16 = jnp.bfloat16
    return pl.pallas_call(
        kernel,
        out_shape=(
            jax.ShapeDtypeStruct((lead, deep * n, wide), bf16),
            jax.ShapeDtypeStruct((tall, thin * n), bf16),
            jax.ShapeDtypeStruct((n,) + gains.shape, bf16),
            jax.ShapeDtypeStruct((count * tensor, rows.shape[1]), bf16),
        ),
        in_specs=[pl.BlockSpec(memory_space=pl.ANY)] * 4,
        out_specs=(pl.BlockSpec(memory_space=pl.ANY),) * 4,
        scratch_shapes=[
            pltpu.SemaphoreType.DMA((n - 1, ring)),
            pltpu.SemaphoreType.DMA((n - 1, ring)),
            pltpu.SemaphoreType.DMA((2 * chips - 1,)),
            pltpu.SemaphoreType.DMA((2 * chips - 1,)),
            pltpu.SemaphoreType.DMA((4,)),
        ],
        compiler_params=pltpu.CompilerParams(collective_id=0, has_side_effects=True),
    )(shard, flat, gains, rows)


def path_scatter(whole, flat, gains, tops):
    grid = Grid()
    n, chips = grid.dp, grid.chips
    lead, total, wide = whole.shape
    deep = total // n
    half = deep // 2
    tall, thin = flat.shape[0], flat.shape[1] // n
    part_tall = tall // 2
    ring = 2 * lead + 4
    gain_item, top_item = ring - 2, ring - 1
    bf16, f32 = jnp.bfloat16, jnp.float32

    def kernel(
        whole_ref, flat_ref, gains_ref, tops_ref, out_ref, flat_out, gains_out, tops_out,
        land, land_flat, land_gain, land_top, own_gain, peer_gain, sends, lands, gain_sends, gain_lands,
    ):
        g = Grid()
        place = g.path_of(g.dp_at)
        after = g.index_of(lax.rem(place + 1, n))
        before = g.index_of(lax.rem(place + n - 1, n))
        core_peer = (g.dp_at, g.chip_at * 2 + 1 - g.core_at)
        chip_peers = [
            (g.dp_at, lax.rem(g.chip_at + k, chips) * 2 + g.core_at) for k in range(1, chips)
        ]
        greet([(after, g.tensor_at), (before, g.tensor_at), core_peer] + chip_peers)

        def way_of(item):
            if item >= gain_item:
                return 1
            return 1 - 2 * (item - 2 * lead if item >= 2 * lead else item // lead)

        def own(item, away):
            index = g.index_of(lax.rem(place - way_of(item) * away + 2 * n, n))
            if item == gain_item:
                return gains_ref.at[index]
            if item == top_item:
                return tops_ref
            if item >= 2 * lead:
                cols = pl.ds(pl.multiple_of(index * thin, thin), thin)
                return flat_ref.at[pl.ds((item - 2 * lead) * part_tall, part_tall), cols]
            side, c = item // lead, item % lead
            return whole_ref.at[c, pl.ds(pl.multiple_of(index * deep + side * half, half), half)]

        def landed(step, item):
            if item == gain_item:
                return land_gain.at[step]
            if item == top_item:
                return land_top.at[step]
            if item >= 2 * lead:
                return land_flat.at[step, item - 2 * lead]
            return land.at[step, item]

        def hop(step, item):
            return pltpu.make_async_remote_copy(
                src_ref=own(item, 1) if step == 0 else landed(step - 1, item),
                dst_ref=landed(step, item),
                send_sem=sends.at[step, item],
                recv_sem=lands.at[step, item],
                device_id=(after if way_of(item) == 1 else before, g.tensor_at),
                device_id_type=pl.DeviceIdType.MESH,
            )

        order = [gain_item, top_item] + [c + side * lead for c in range(lead) for side in (0, 1)]
        order += [2 * lead, 2 * lead + 1]
        hops = {}
        for item in order:
            hops[0, item] = hop(0, item)
            hops[0, item].start()
        for step in range(1, n):
            for item in order:
                hops[step - 1, item].wait_recv()
                here = landed(step - 1, item)
                if item == top_item:
                    summed = jnp.maximum(here[...], tops_ref[...])
                else:
                    summed = here[...].astype(f32) + own(item, step + 1)[...].astype(f32)
                if step < n - 1:
                    here[...] = summed.astype(here.dtype)
                    hops[step, item] = hop(step, item)
                    hops[step, item].start()
                elif item == gain_item:
                    own_gain[0] = summed
                elif item == top_item:
                    tops_out[...] = summed
                elif item >= 2 * lead:
                    side = item - 2 * lead
                    flat_out[pl.ds(side * part_tall, part_tall)] = summed
                else:
                    side, c = item // lead, item % lead
                    out_ref[c, pl.ds(side * half, half)] = summed
        peers = [core_peer] + chip_peers
        copies = []
        for k, peer in enumerate(peers):
            level = min(k, 1)
            copies.append(
                pltpu.make_async_remote_copy(
                    src_ref=own_gain.at[level],
                    dst_ref=peer_gain.at[k],
                    send_sem=gain_sends.at[k],
                    recv_sem=gain_lands.at[k],
                    device_id=peer,
                    device_id_type=pl.DeviceIdType.MESH,
                )
            )
        copies[0].start()
        copies[0].wait_recv()
        own_gain[1] = own_gain[0] + peer_gain[0]
        for copy in copies[1:]:
            copy.start()
        for copy in copies[1:]:
            copy.wait_recv()
        result = own_gain[1]
        for k in range(1, len(peers)):
            result = result + peer_gain[k]
        gains_out[...] = result
        for key in hops:
            hops[key].wait_send()
        for copy in copies:
            copy.wait_send()

    near = pl.BlockSpec(memory_space=pltpu.VMEM)
    gain_shape = gains.shape[1:]
    return pl.pallas_call(
        kernel,
        out_shape=(
            jax.ShapeDtypeStruct((lead, deep, wide), f32),
            jax.ShapeDtypeStruct((tall, thin), f32),
            jax.ShapeDtypeStruct(gain_shape, f32),
            jax.ShapeDtypeStruct(tops.shape, f32),
        ),
        in_specs=[near] * 4,
        out_specs=(near,) * 4,
        scratch_shapes=[
            pltpu.VMEM((n - 1, 2 * lead, half, wide), bf16),
            pltpu.VMEM((n - 1, 2, part_tall, thin), bf16),
            pltpu.VMEM((n - 1,) + gain_shape, f32),
            pltpu.VMEM((n - 1,) + tops.shape, f32),
            pltpu.VMEM((2,) + gain_shape, f32),
            pltpu.VMEM((chips,) + gain_shape, f32),
            pltpu.SemaphoreType.DMA((n - 1, ring)),
            pltpu.SemaphoreType.DMA((n - 1, ring)),
            pltpu.SemaphoreType.DMA((chips,)),
            pltpu.SemaphoreType.DMA((chips,)),
        ],
        compiler_params=pltpu.CompilerParams(
            collective_id=1, has_side_effects=True, vmem_limit_bytes=40 * 2**20
        ),
    )(whole, flat, gains, tops)


def attend_call(seq, full_qkv, full_out, head_gains, out_gain, tables, blocks, rows, shard):
    grid = Grid()
    outer, inner, chips, tensor = grid.outer, grid.inner, grid.chips, grid.tensor
    length, width = seq.shape
    span = full_qkv.shape[2]
    heads = span // HEAD
    count = rows.shape[0]
    slab = shard.shape[1]
    units = shard.shape[2] // outer
    parts = outer * inner
    steps = sorted(range(1, outer), key=lambda s: (min(s, outer - s), s))
    tall = min(256, length)
    tile = 512
    lines = 32
    bf16, f32 = jnp.bfloat16, jnp.float32
    mesh_id = pl.DeviceIdType.MESH

    def kernel(
        seq_ref, qkv_ref, out_w_ref, gains_ref, out_gain_ref, cos_ref, sin_ref, id_col, id_row, rows_ref, shard_ref,
        *refs
    ):
        pieces = [refs[j * outer : (j + 1) * outer] for j in range(inner)]
        body(
            seq_ref, qkv_ref, out_w_ref, gains_ref, out_gain_ref, cos_ref, sin_ref, id_col, id_row, rows_ref, shard_ref,
            pieces, *refs[parts:],
        )

    def body(
        seq_ref, qkv_ref, out_w_ref, gains_ref, out_gain_ref, cos_ref, sin_ref, id_col, id_row, rows_ref, shard_ref,
        pieces, hat_ref, scale_ref, q_low, k_low, v_low, lse_ref, context, attn_hat, o_scale, resid, resid_low, top_ref,
        square, squares, core_send, core_land, hold, chip_send, chip_land,
        s_z, r_z, s_y, r_y, s_sq, r_sq, s_core, r_core, s_chip, r_chip, local,
    ):
        g = Grid()

        def tensor_peer(k, flip):
            core = 1 - g.core_at if flip else g.core_at
            return (g.dp_at, lax.rem(g.chip_at + k + chips, chips) * 2 + core)

        def dp_peer(s, j):
            across = lax.rem(g.outer_at + s + outer, outer) * inner
            return (across + lax.rem(g.inner_at + j + inner, inner), g.tensor_at)

        near = [tensor_peer(k, f) for k in range(chips) for f in (0, 1) if (k, f) != (0, 0)]
        far = [dp_peer(s, 0) for s in range(1, outer)]
        far += [dp_peer(0, j) for j in sorted({1 % inner, inner - 1} - {0})]
        greet(near + far)

        def remote(src, dst, send, recv, peer):
            copy = pltpu.make_async_remote_copy(
                src_ref=src, dst_ref=dst, send_sem=send, recv_sem=recv,
                device_id=peer, device_id_type=mesh_id,
            )
            copy.start()
            return copy

        def dot(a, b, contract):
            return lax.dot_general(a, b, (contract, ((), ())), preferred_element_type=f32)

        def looped(total, make):
            lax.fori_loop(0, total, lambda i, c: (make(i), c)[1], 0)

        def rows_of(i, size):
            return pl.ds(pl.multiple_of(i * size, size), size)

        def cut(s):
            at = lax.rem(g.outer_at + s, outer)
            return shard_ref.at[:, :, rows_of(at, units)]

        z_copies = {
            s: remote(cut(s), pieces[0][s], s_z.at[s], r_z.at[s], dp_peer(s, 0)) for s in steps
        }
        own = pltpu.make_async_copy(cut(0), pieces[0][0], local)
        own.start()
        y_copies = {}

        def pass_on(j, s):
            src = cut(0) if (j, s) == (1, 0) else pieces[j - 1][s]
            y_copies[j, s] = remote(src, pieces[j][s], s_y.at[j, s], r_y.at[j, s], dp_peer(0, 1))

        if inner > 1:
            pass_on(1, 0)
        duties = []
        for s in steps:

            def duty(s=s):
                z_copies[s].wait_recv()
                if inner > 1:
                    pass_on(1, s)

            duties.append(duty)
        for j in range(2, inner):
            for s in [0] + steps:

                def duty(j=j, s=s):
                    y_copies[j - 1, s].wait_recv()
                    pass_on(j, s)

                duties.append(duty)

        def next_duty():
            if duties:
                duties.pop(0)()

        def project(i):
            at = rows_of(i, tall)
            x = seq_ref[at]
            lane = lax.broadcasted_iota(jnp.int32, (tall, 128), 1)
            sums = jnp.zeros((tall, 128), f32)
            for c in range(2):
                value = dot(x, qkv_ref[c], ((1,), (0,)))
                hat_ref[c, at] = value
                sums = jnp.where(lane == c, jnp.sum(value * value, axis=1, keepdims=True), sums)
            v_low[at] = dot(x, qkv_ref[2], ((1,), (0,))).astype(bf16)
            square[:, at] = sums.T[:8]

        looped(length // tall, project)
        sq_copies = []
        for k in range(chips):
            for f in (0, 1):
                if (k, f) != (0, 0):
                    at = k * 2 + f - 1
                    sq_copies.append(
                        remote(square, squares.at[at], s_sq.at[at], r_sq.at[at], tensor_peer(k, f))
                    )
        for copy in sq_copies:
            copy.wait_recv()
        sign = jnp.where(lax.broadcasted_iota(jnp.int32, (tall, HEAD), 1) < HEAD // 2, -1.0, 1.0)

        def rotate(i):
            at = rows_of(i, tall)
            sums = square[:, at]
            for copy_at in range(tensor - 1):
                sums = sums + squares[copy_at, :, at]
            column = jnp.concatenate([sums, jnp.zeros((120, tall), f32)], axis=0).T
            scales = lax.rsqrt(column / width + norm_eps)
            scale_ref[at] = scales
            cosine, sine = cos_ref[at], sin_ref[at] * sign
            for c, low in ((0, q_low), (1, k_low)):
                hat = hat_ref[c, at] * scales[:, c : c + 1]
                hat_ref[c, at] = hat
                normed = hat * gains_ref[c : c + 1]
                for h in range(heads):
                    cols = slice(h * HEAD, (h + 1) * HEAD)
                    value = normed[:, cols]
                    turned = pltpu.roll(value, HEAD // 2, 1)
                    low[at, cols] = (value * cosine + turned * sine).astype(bf16)

        looped(length // tall, rotate)
        scale = HEAD ** (-0.5)
        top_ref[...] = jnp.full((8, 128), masked_value, f32)
        for h in range(heads):
            cols = slice(h * HEAD, (h + 1) * HEAD)

            def attend(i, best, cols=cols, h=h):
                at = rows_of(i, tall)
                raw = dot(q_low[at, cols], k_low[:, cols], ((1,), (1,))) * scale
                masked = jnp.where(id_row[...] <= id_col[at], raw, masked_value)
                top = jnp.max(masked, axis=1, keepdims=True)
                weight = jnp.exp(masked - top)
                total = jnp.sum(weight, axis=1, keepdims=True)
                probs = (weight / total).astype(bf16)
                context[at, cols] = dot(probs, v_low[:, cols], ((1,), (0,))).astype(bf16)
                lse_ref[at, h : h + 1] = top + jnp.log(total)
                return jnp.maximum(best, jnp.max(top, axis=0, keepdims=True))

            best = lax.fori_loop(
                0, length // tall, attend, jnp.full((1, 1), masked_value, f32)
            )
            top_ref[h : h + 1] = jnp.broadcast_to(best, (1, 128))
        next_duty()

        def out_rows(k, flip, store):
            chip = lax.rem(g.chip_at + k, chips)
            core = 1 - g.core_at if flip else g.core_at
            at = rows_of(chip * 2 + core, count)

            def columns(i):
                cols = rows_of(i, tile)
                store(cols, dot(context[at], out_w_ref[:, cols], ((1,), (0,))))

            looped(width // tile, columns)

        chip_order = list(range(1, chips)) + [0]
        core_copies, chip_copies = {}, {}
        for k in chip_order:

            def store(cols, value, k=k):
                core_send[k, :, cols] = value.astype(bf16)

            out_rows(k, True, store)
            core_copies[k] = remote(
                core_send.at[k], core_land.at[k], s_core.at[k], r_core.at[k], tensor_peer(0, 1)
            )
        for k in chip_order:

            def store(cols, value, k=k):
                hold[k, :, cols] = value

            out_rows(k, False, store)
            if k:
                core_copies[k].wait_recv()

                def add(i, k=k):
                    at = rows_of(i, lines)
                    chip_send[k - 1, at] = (hold[k, at] + core_land[k, at].astype(f32)).astype(bf16)

                looped(count // lines, add)
                chip_copies[k] = remote(
                    chip_send.at[k - 1], chip_land.at[k - 1], s_chip.at[k], r_chip.at[k], tensor_peer(k, 0)
                )
        next_duty()
        core_copies[0].wait_recv()
        for k in range(1, chips):
            chip_copies[k].wait_recv()

        def close(i):
            at = rows_of(i, lines)
            raw = hold[0, at] + core_land[0, at].astype(f32)
            for k in range(1, chips):
                raw = raw + chip_land[k - 1, at].astype(f32)
            scale_o = lax.rsqrt(jnp.mean(raw * raw, axis=1, keepdims=True) + norm_eps)
            hat = raw * scale_o
            attn_hat[at] = hat
            o_scale[at] = scale_o
            value = rows_ref[at].astype(f32) + hat * out_gain_ref[...]
            resid[at] = value
            resid_low[at] = value.astype(bf16)

        looped(count // lines, close)
        while duties:
            next_duty()
        own.wait()
        for key, copy in y_copies.items():
            if key[0] == inner - 1:
                copy.wait_recv()
        sent = list(z_copies.values()) + list(y_copies.values()) + sq_copies
        for copy in sent + list(core_copies.values()) + list(chip_copies.values()):
            copy.wait_send()

    shape = jax.ShapeDtypeStruct
    anywhere = pl.BlockSpec(memory_space=pl.ANY)
    vmem = pl.BlockSpec(memory_space=pltpu.VMEM)
    sems = pltpu.SemaphoreType.DMA
    results = pl.pallas_call(
        kernel,
        out_shape=(shape((3, slab, units), bf16),) * parts
        + (
            shape((2, length, span), f32),
            shape((length, 128), f32),
            shape((length, span), bf16),
            shape((length, span), bf16),
            shape((length, span), bf16),
            shape((length, heads), f32),
            shape((length, span), bf16),
            shape((count, width), f32),
            shape((count, 1), f32),
            shape((count, width), f32),
            shape((count, width), bf16),
            shape((8, 128), f32),
        ),
        in_specs=[vmem] * 10 + [anywhere],
        out_specs=(anywhere,) * parts + (vmem,) * 12,
        scratch_shapes=[
            pltpu.VMEM((8, length), f32),
            pltpu.VMEM((tensor - 1, 8, length), f32),
            pltpu.VMEM((chips, count, width), bf16),
            pltpu.VMEM((chips, count, width), bf16),
            pltpu.VMEM((chips, count, width), f32),
            pltpu.VMEM((max(chips - 1, 1), count, width), bf16),
            pltpu.VMEM((max(chips - 1, 1), count, width), bf16),
            sems((outer,)),
            sems((outer,)),
            sems((inner, outer)),
            sems((inner, outer)),
            sems((tensor - 1,)),
            sems((tensor - 1,)),
            sems((chips,)),
            sems((chips,)),
            sems((chips,)),
            sems((chips,)),
            sems(()),
        ],
        compiler_params=pltpu.CompilerParams(
            collective_id=3, has_side_effects=True, vmem_limit_bytes=56 * 2**20
        ),
    )(
        seq, full_qkv, full_out, head_gains, out_gain, tables[0], tables[1],
        blocks[:, None], blocks[None, :], rows, shard,
    )
    pieces = [results[j * outer : (j + 1) * outer] for j in range(inner)]
    return pieces, results[parts:]


def after(value, event):
    return lax.optimization_barrier((value, event))[0]


def inner_sum(grid, grads, event):
    others = [grid.to_inner(grads[j], j) for j in range(1, grid.inner)]
    return low_sum(grads[0], *after(others, event))


def outer_spread(grid, total):
    return [total[0]] + [grid.to_outer(total[step], step) for step in range(1, grid.outer)]


def sequence_scatter(grid, whole):
    rows = whole.shape[0] // grid.tensor
    shaped = whole.reshape(grid.chips, 2, rows, whole.shape[1])
    other = part(shaped, 1, 1 - grid.core_at, 1)[:, 0].astype(jnp.bfloat16)
    own = part(shaped, 1, grid.core_at, 1)[:, 0]
    pair = own + grid.to_core(other).astype(jnp.float32)
    total = part(pair, 0, grid.chip_at, 1)[0]
    for step in range(1, grid.chips):
        away = part(pair, 0, (grid.chip_at + step) % grid.chips, 1)[0].astype(jnp.bfloat16)
        total = total + grid.to_chip(away, step).astype(jnp.float32)
    return total


def sequence_gather(grid, rows):
    count, width = rows.shape
    whole = jnp.zeros((grid.chips, 2, count, width), rows.dtype)
    for step in range(grid.chips):
        here = grid.to_chip(rows, step) if step else rows
        chip = (grid.chip_at - step) % grid.chips
        for value, core in ((here, grid.core_at), (grid.to_core(here), 1 - grid.core_at)):
            whole = lax.dynamic_update_slice(whole, value[None, None], (chip, core, 0, 0))
    return whole.reshape(grid.tensor * count, width)


def unit_kernel_call(rows_low, resid, cotangent, gain, pieces):
    grid = Grid()
    outer, chips = grid.outer, grid.chips
    count, width = rows_low.shape
    units = pieces[0][0].shape[2]
    slab = pieces[0][0].shape[1]
    inner = grid.inner
    flat_pieces = [piece for row in pieces for piece in row]
    parts = len(flat_pieces)
    both = 2 * count
    per = min(2, chips)
    groups = chips // per
    blocks = outer * groups
    tall = per * both
    held = per if groups > 1 else max(per - 1, 1)
    steps = [0] + sorted(range(1, outer), key=lambda s: (min(s, outer - s), s))
    order = [(s, i) for s in steps for i in range(groups)]
    tile = 512
    wide_tiles = width // tile
    unit_tile = min(256, units)
    lines = 32
    bf16, f32 = jnp.bfloat16, jnp.float32
    mesh_id = pl.DeviceIdType.MESH

    def plan(phase):
        block_us, core_us, hop_us = 10.5, 1.0, 2.0
        free = {"tc": 0.0, "x": 0.0, "core": 0.0, "z": 0.0}
        done = {}
        tasks = {}

        def send(link, when, us):
            free[link] = max(free[link], when) + us
            return free[link] + hop_us

        def add(name, needs, us, after=None):
            tasks[name] = (needs, us, after)

        arrive = {}
        for i, s in enumerate(steps[1:]):
            arrive["z", s] = 15.0 + 13.0 * i
        for k in range(1, chips):
            arrive["x", 0, k] = send("x", 0.0, block_us)
        arrive["c", 0, 0] = send("core", 0.0, core_us)

        def zf(s):
            def then(now):
                for k in range(1, chips):
                    arrive["x", s, k] = send("x", now, block_us)
                arrive["c", s, 0] = send("core", now, core_us)

            return then

        def xf(s, k):
            def then(now):
                arrive["c", s, k] = send("core", now, core_us)

            return then

        def compute(u):
            def then(now):
                arrive["cr", u] = send("core", now, core_us)

            return then

        def cr(s, i):
            def then(now):
                for k in range(i * per, i * per + per):
                    if k:
                        arrive["xr", s, k] = send("x", now, block_us)

            return then

        def xr(s):
            def then(now):
                if s:
                    arrive["zr", s] = send("z", now, block_us) + 3.0

            return then

        for s in steps[1:]:
            add(("zf", s), [("at", ("z", s))], 0.3, zf(s))
        for s in steps:
            for k in range(1, chips):
                add(("xf", s, k), [("at", ("x", s, k))], 0.3, xf(s, k))
        for i, (s, k) in enumerate(order):
            needs = [("at", ("c", s, k * per + j)) for j in range(per)]
            if phase and i:
                needs.append(("do", ("grads",) + order[i - 1]))
            elif i >= 2:
                needs.append(("do", ("compute",) + order[i - 2]))
            add(("load", s, k), needs, 0.2, None)
            needs = [("do", ("load", s, k))]
            if i >= 2:
                needs.append(("do", ("cr",) + order[i - 2]))
            add(("compute", s, k), needs, 5.0, compute((s, k)))
            if phase:
                add(("grads", s, k), [("do", ("compute", s, k))], 6.0, None)
            add(("cr", s, k), [("at", ("cr", (s, k))), ("do", ("compute", s, k))], 0.6, cr(s, k))
        for s in steps:
            needs = [("do", ("cr", s, 0))] + [("at", ("xr", s, k)) for k in range(1, chips)]
            add(("xr", s), needs, 0.6, xr(s))
        for s in steps[1:]:
            add(("zr", s), [("at", ("zr", s)), ("do", ("xr", 0))], 0.6, None)
        if phase:
            needs = [("do", ("xr", s)) for s in steps]
            add(("write", 0), needs + [("do", ("grads",) + unit) for unit in order], 4.0, None)
        result = []
        now = 0.0
        while tasks:
            best = None
            for name, (needs, us, after) in tasks.items():
                ready = 0.0
                for kind, key in needs:
                    table = arrive if kind == "at" else done
                    if key not in table:
                        ready = None
                        break
                    ready = max(ready, table[key] + (1.0 if key[0] == "load" else 0.0))
                if ready is None:
                    continue
                ready = max(ready, now)
                rank = {"compute": 1, "grads": 2, "write": 3}.get(name[0], 0)
                if best is None or (ready, rank) < best[:2]:
                    best = (ready, rank, name)
            ready, _, name = best
            needs, us, after = tasks.pop(name)
            now = ready + us
            done[name] = now
            if after is not None:
                after(now)
            result.append(name)
        return result

    def kernel(
        *refs
    ):
        piece_refs = refs[:parts]
        rows_ref, resid_ref, cot_ref, gain_ref = refs[parts : parts + 4]
        out_ref, dres_ref, gain_out, all_x, all_dm = refs[parts + 4 : parts + 9]
        grad_refs = refs[parts + 9 : parts + 9 + 3 * inner]
        rest = refs[parts + 9 + 3 * inner :]
        body(piece_refs, rows_ref, resid_ref, cot_ref, gain_ref, out_ref, dres_ref, gain_out, all_x, all_dm, grad_refs, *rest)

    def body(
        piece_refs, rows_ref, resid_ref, cot_ref, gain_ref,
        out_ref, dres_ref, gain_out, all_x, all_dm, grad_refs,
        wg, wu, wd, buf, act, coef_gate, coef_up, d_gate, d_up, turned, acc_gate, acc_up, acc_down, stage,
        core_send, core_land, hold, keep, chip_send, chip_land, outer_send, outer_land, raw, d_mlp,
        s_outer, r_outer, s_chip, r_chip, s_core, r_core,
        s_core_sum, r_core_sum, s_chip_sum, r_chip_sum, s_outer_sum, r_outer_sum, local, local_w, local_g,
    ):
        g = Grid()
        core_peer = (g.dp_at, g.chip_at * 2 + 1 - g.core_at)

        def chip_peer(k):
            return (g.dp_at, lax.rem(g.chip_at + k + chips, chips) * 2 + g.core_at)

        def outer_peer(s):
            return (lax.rem(g.outer_at + s + outer, outer) * g.inner + g.inner_at, g.tensor_at)

        greet(
            [core_peer]
            + [chip_peer(k) for k in range(1, chips)]
            + [outer_peer(s) for s in range(1, outer)]
        )

        def remote(src, dst, send, recv, peer):
            return pltpu.make_async_remote_copy(
                src_ref=src, dst_ref=dst, send_sem=send, recv_sem=recv,
                device_id=peer, device_id_type=mesh_id,
            )

        def dot(a, b, contract):
            return lax.dot_general(a, b, (contract, ((), ())), preferred_element_type=f32)

        def looped(total, body):
            lax.fori_loop(0, total, lambda i, c: (body(i), c)[1], 0)

        def by_lines(body):
            looped(count // lines, lambda i: body(pl.ds(pl.multiple_of(i * lines, lines), lines)))

        def by_tiles(body):
            looped(wide_tiles, lambda i: body(pl.ds(pl.multiple_of(i * tile, tile), tile)))

        weights = (wg, wu, wd)
        fetches = []
        for j in range(inner):
            for s in range(outer):
                index = lax.rem(g.outer_at - s + outer, outer) * inner
                index = index + lax.rem(g.inner_at - j + inner, inner)
                span = pl.ds(pl.multiple_of(index * slab, slab), slab)
                for c in range(3):
                    at = j * outer + s
                    fetches.append(
                        pltpu.make_async_copy(
                            piece_refs[at].at[c], weights[c].at[span], local_w.at[at, c]
                        )
                    )
        started = []

        def run(phase, source, everything, fetched, compute, grads, write):
            mine = pl.ds(0, count)
            theirs = pl.ds(count, count)
            copies = {}

            def start(key, copy):
                copy.start()
                copies[key] = copy
                started.append(copy)

            def at(s, k, half):
                return everything.at[s, k, half]

            def core_copy(s, k, src):
                start(
                    ("c", s, k),
                    remote(src, at(s, k, theirs), s_core.at[phase, s, k], r_core.at[phase, s, k], core_peer),
                )

            def chip_copy(s, k, src):
                start(
                    ("x", s, k),
                    remote(src, at(s, k, mine), s_chip.at[phase, s, k], r_chip.at[phase, s, k], chip_peer(k)),
                )

            for s in steps[1:]:
                start(
                    ("z", s),
                    remote(source, at(s, 0, mine), s_outer.at[phase, s], r_outer.at[phase, s], outer_peer(s)),
                )
            for k in range(1, chips):
                chip_copy(0, k, source)
            core_copy(0, 0, source)
            own = pltpu.make_async_copy(source, at(0, 0, mine), local.at[phase, 0, blocks])
            own.start()
            if phase == 0:
                for copy in fetches:
                    copy.start()
            slots = {unit: i % 2 for i, unit in enumerate(order)}
            span_of = {u: pl.ds(u[1] * per, per) for u in order}
            loads = {}
            sums = {}
            for task in plan(phase):
                name, s = task[:2]
                k = task[2] if len(task) > 2 else 0
                unit = s * groups + k
                if name == "zf":
                    copies["z", s].wait_recv()
                    for j in range(1, chips):
                        chip_copy(s, j, at(s, 0, mine))
                    core_copy(s, 0, at(s, 0, mine))
                elif name == "xf":
                    copies["x", s, k].wait_recv()
                    core_copy(s, k, at(s, k, mine))
                elif name == "load":
                    for j in range(per):
                        copies["c", s, k * per + j].wait_recv()
                    if (s, k) == (0, 0):
                        own.wait()
                    loads[s, k] = []
                    places = [slots[s, k], 2]
                    for j, src in enumerate(fetched):
                        copy = pltpu.make_async_copy(
                            src.at[s, span_of[s, k]], buf.at[places[j]], local.at[phase, j, unit]
                        )
                        copy.start()
                        loads[s, k].append(copy)
                elif name == "compute":
                    if phase == 0 and (s, k) == order[0]:
                        for copy in fetches:
                            copy.wait()
                    for copy in loads[s, k]:
                        copy.wait()
                    i = order.index((s, k))
                    if i >= 2:
                        sums["core", order[i - 2]].wait_send()
                    slot = slots[s, k]

                    def send(slot=slot, unit=unit, s=s, k=k):
                        copy = remote(
                            core_send.at[slot], core_land.at[unit],
                            s_core_sum.at[phase, unit], r_core_sum.at[phase, unit], core_peer,
                        )
                        copy.start()
                        sums["core", (s, k)] = copy

                    compute(slot, unit, s, k, send)
                elif name == "grads":
                    grads(slots[s, k], unit)
                elif name == "write":
                    write()
                elif name == "cr":
                    sums["core", (s, k)].wait_recv()
                    slot = slots[s, k]
                    for j in range(per):
                        chip = k * per + j
                        if chip == 0:

                            def add_core(at_rows, s=s, unit=unit, j=j):
                                keep[s, at_rows] = keep[s, at_rows] + core_land[unit, j, at_rows].astype(f32)

                            by_lines(add_core)
                            continue
                        there = s * (chips - 1) + chip - 1

                        def add_core(at_rows, there=there, slot=slot, unit=unit, j=j, i=min(j, held - 1)):
                            total = hold[slot, i, at_rows] + core_land[unit, j, at_rows].astype(f32)
                            chip_send[there, at_rows] = total.astype(bf16)

                        by_lines(add_core)
                        copy = remote(
                            chip_send.at[there], chip_land.at[there],
                            s_chip_sum.at[phase, there], r_chip_sum.at[phase, there], chip_peer(-chip),
                        )
                        copy.start()
                        sums["chip", (s, chip)] = copy
                elif name == "xr":
                    for j in range(1, chips):
                        sums["chip", (s, j)].wait_recv()

                    def add_chip(at_rows, s=s):
                        total = keep[s, at_rows]
                        for j in range(1, chips):
                            total = total + chip_land[s * (chips - 1) + j - 1, at_rows].astype(f32)
                        if s == 0:
                            raw[at_rows] = total
                        else:
                            outer_send[s - 1, at_rows] = total.astype(bf16)

                    by_lines(add_chip)
                    if s:
                        copy = remote(
                            outer_send.at[s - 1], outer_land.at[s - 1],
                            s_outer_sum.at[phase, s], r_outer_sum.at[phase, s], outer_peer(-s),
                        )
                        copy.start()
                        sums["outer", s] = copy
                elif name == "zr":
                    sums["outer", s].wait_recv()

                    def add_outer(at_rows, s=s):
                        raw[at_rows] = raw[at_rows] + outer_land[s - 1, at_rows].astype(f32)

                    by_lines(add_outer)
            waited = [sums["core", unit] for unit in order[-2:]]
            waited += [copy for key, copy in sums.items() if key[0] != "core"]
            for copy in waited:
                copy.wait_send()
            for copy in started:
                copy.wait_send()
            started.clear()

        def part_out(slot, s, i, cols, part_sum):
            for j in range(per):
                own_rows = part_sum[j * both : j * both + count]
                if i * per + j == 0:
                    keep[s, :, cols] = own_rows
                else:
                    hold[slot, min(j, held - 1), :, cols] = own_rows
                core_send[slot, j, :, cols] = part_sum[j * both + count : (j + 1) * both].astype(bf16)

        def forward(slot, unit, s, i, send):
            for j in range(units // unit_tile):
                cols = pl.ds(j * unit_tile, unit_tile)
                rows = buf[slot].reshape(tall, width)
                gate = dot(rows, wg[:, cols], ((1,), (0,)))
                up = dot(rows, wu[:, cols], ((1,), (0,)))
                sigma = jax.nn.sigmoid(gate)
                silu = gate * sigma
                act[unit, :, cols] = (silu * up).astype(bf16)
                coef_up[unit, :, cols] = silu.astype(bf16)
                coef_gate[unit, :, cols] = (up * sigma * (1.0 + gate * (1.0 - sigma))).astype(bf16)

            def down(cols):
                part_out(slot, s, i, cols, dot(act[unit], wd[cols, :], ((1,), (1,))))

            by_tiles(down)
            send()

        def between():
            def lines_of(i, total):
                at_rows = pl.ds(pl.multiple_of(i * lines, lines), lines)
                value = raw[at_rows]
                scale = lax.rsqrt(jnp.mean(value * value, axis=1, keepdims=True) + norm_eps)
                hat = value * scale
                gain_row = gain_ref[...]
                out_ref[at_rows] = (resid_ref[at_rows] + hat * gain_row).astype(bf16)
                top = cot_ref[at_rows].astype(f32)
                upstream = top * gain_row
                inner = jnp.mean(upstream * hat, axis=1, keepdims=True)
                d_mlp[at_rows] = (scale * (upstream - hat * inner)).astype(bf16)
                return total + jnp.sum(top * hat, axis=0, keepdims=True)

            gain_out[...] = lax.fori_loop(
                0, count // lines, lines_of, jnp.zeros((1, width), f32)
            )

        def backward(slot, unit, s, i, send):
            for j in range(units // unit_tile):
                cols = pl.ds(j * unit_tile, unit_tile)
                d_act = dot(buf[slot].reshape(tall, width), wd[:, cols], ((1,), (0,)))
                d_gate[:, cols] = (d_act * coef_gate[unit, :, cols].astype(f32)).astype(bf16)
                d_up[:, cols] = (d_act * coef_up[unit, :, cols].astype(f32)).astype(bf16)

            def into(cols):
                part_sum = dot(d_gate[...], wg[cols, :], ((1,), (1,)))
                part_sum = part_sum + dot(d_up[...], wu[cols, :], ((1,), (1,)))
                part_out(slot, s, i, cols, part_sum)

            by_tiles(into)
            send()

        def weight_grads(slot, unit):
            first = unit == order[0][0] * groups + order[0][1]
            for left, right, acc in (
                (d_gate[...], 2, acc_gate),
                (d_up[...], 2, acc_up),
                (act[unit], slot, acc_down),
            ):
                turned[...] = left.T

                def grads(cols, right=right, acc=acc):
                    rows = buf[right, :, :, cols].reshape(tall, tile)
                    value = dot(turned[...], rows, ((1,), (0,)))
                    acc[:, cols] = value if first else acc[:, cols] + value

                by_tiles(grads)

        def write_grads():
            copies = []
            for j in range(inner):
                for s in range(outer):
                    index = lax.rem(g.outer_at + s, outer) * inner
                    index = index + lax.rem(g.inner_at + j, inner)
                    span = pl.ds(pl.multiple_of(index * slab, slab), slab)
                    slot = len(copies) % 2
                    if len(copies) >= 2:
                        for copy in copies[-2]:
                            copy.wait()
                    batch = []
                    for c, acc in enumerate((acc_gate, acc_up, acc_down)):
                        stage[slot, c] = acc[:, span].astype(bf16)
                        copy = pltpu.make_async_copy(
                            stage.at[slot, c], grad_refs[j * 3 + c].at[s], local_g.at[slot, c]
                        )
                        copy.start()
                        batch.append(copy)
                    copies.append(batch)
            for batch in copies[-2:]:
                for copy in batch:
                    copy.wait()

        run(0, rows_ref, all_x, [all_x], forward, None, None)
        between()
        run(1, d_mlp, all_dm, [all_dm, all_x], backward, weight_grads, write_grads)

        def close(at_rows):
            dres_ref[at_rows] = raw[at_rows] + cot_ref[at_rows].astype(f32)

        by_lines(close)

    def held_in(space):
        return pl.BlockSpec(memory_space=space)

    shape = jax.ShapeDtypeStruct
    anywhere, near = held_in(pl.ANY), held_in(pltpu.VMEM)
    sems = pltpu.SemaphoreType.DMA
    links = outer * (chips - 1)
    flops = 2 * 9 * tall * blocks * width * units
    results = pl.pallas_call(
        kernel,
        out_shape=(
            shape((count, width), bf16),
            shape((count, width), f32),
            shape((1, width), f32),
            shape((outer, chips, both, width), bf16),
            shape((outer, chips, both, width), bf16),
        )
        + (shape((outer, units, slab), bf16),) * (3 * inner),
        in_specs=[anywhere] * (parts + 1) + [near] * 3,
        out_specs=(near, near, near) + (anywhere,) * (2 + 3 * inner),
        scratch_shapes=[
            pltpu.VMEM((width, units), bf16),
            pltpu.VMEM((width, units), bf16),
            pltpu.VMEM((width, units), bf16),
            pltpu.VMEM((3, per, both, width), bf16),
            pltpu.VMEM((blocks, tall, units), bf16),
            pltpu.VMEM((blocks, tall, units), bf16),
            pltpu.VMEM((blocks, tall, units), bf16),
            pltpu.VMEM((tall, units), bf16),
            pltpu.VMEM((tall, units), bf16),
            pltpu.VMEM((units, tall), bf16),
            pltpu.VMEM((units, width), f32),
            pltpu.VMEM((units, width), f32),
            pltpu.VMEM((units, width), f32),
            pltpu.VMEM((2, 3, units, slab), bf16),
            pltpu.VMEM((2, per, count, width), bf16),
            pltpu.VMEM((blocks, per, count, width), bf16),
            pltpu.VMEM((2, held, count, width), f32),
            pltpu.VMEM((outer, count, width), f32),
            pltpu.VMEM((links, count, width), bf16),
            pltpu.VMEM((links, count, width), bf16),
            pltpu.VMEM((outer - 1, count, width), bf16),
            pltpu.VMEM((outer - 1, count, width), bf16),
            pltpu.VMEM((count, width), f32),
            pltpu.VMEM((count, width), bf16),
            sems((2, outer)),
            sems((2, outer)),
            sems((2, outer, chips)),
            sems((2, outer, chips)),
            sems((2, outer, chips)),
            sems((2, outer, chips)),
            sems((2, blocks)),
            sems((2, blocks)),
            sems((2, links)),
            sems((2, links)),
            sems((2, outer)),
            sems((2, outer)),
            sems((2, 2, blocks + 1)),
            sems((parts, 3)),
            sems((2, 3)),
        ],
        compiler_params=pltpu.CompilerParams(
            collective_id=2, has_side_effects=True, vmem_limit_bytes=61 * 2**20
        ),
        cost_estimate=pl.CostEstimate(flops=flops, bytes_accessed=64 * 2**20, transcendentals=0),
    )(*flat_pieces, rows_low, resid, cotangent, gain)
    grads = results[5:]
    return results[:3] + ([[grads[j * 3 + c] for j in range(inner)] for c in range(3)],)


def adam_kernel(w_ref, m_ref, v_ref, g_ref, *rest):
    scale_ref = rest[0] if len(rest) == 5 else None
    w_out, m_out, v_out, c_out = rest[-4:]
    grad = g_ref[...].astype(jnp.float32)
    new, first, second = adam_step(
        w_ref[...], grad, m_ref[...], v_ref[...], rate_matrix, weight_decay
    )
    if scale_ref is not None:
        new = new * scale_ref[...]
    w_out[...] = new
    m_out[...] = first
    v_out[...] = second
    c_out[...] = new.astype(jnp.bfloat16)


def adam_call(param, grad, first, second, scale=None):
    shape = param.shape
    flat = [v.reshape(-1, shape[-1]) for v in (param, first, second, grad)]
    rows, width = flat[0].shape
    block = min(rows, max(16, (1 << 17) // width))
    spec = pl.BlockSpec((block, width), lambda k: (k, 0))
    specs = [spec] * 4
    if scale is not None:
        per = shape[1] // block
        flat.append(scale)
        specs.append(pl.BlockSpec((None, 1, width), lambda k: (k // per, 0, 0)))
    outs = [jax.ShapeDtypeStruct((rows, width), jnp.float32)] * 3
    outs.append(jax.ShapeDtypeStruct((rows, width), jnp.bfloat16))
    size = rows * width
    result = pl.pallas_call(
        adam_kernel,
        grid=(rows // block,),
        in_specs=specs,
        out_specs=[spec] * 4,
        out_shape=outs,
        cost_estimate=pl.CostEstimate(
            flops=20 * size, bytes_accessed=28 * size, transcendentals=2 * size
        ),
        compiler_params=pltpu.CompilerParams(vmem_limit_bytes=32 * 2**20),
    )(*flat)
    return [v.reshape(shape) for v in result]


def adam_units_kernel(turned, at_ref, w_ref, m_ref, v_ref, g_ref, w_out, m_out, v_out, c_out):
    grad = g_ref[...].astype(jnp.float32)
    if turned:
        grad = grad.T
    new, first, second = adam_step(
        w_ref[...], grad, m_ref[...], v_ref[...], rate_matrix, weight_decay
    )
    w_out[...] = new
    m_out[...] = first
    v_out[...] = second
    c_out[...] = new.astype(jnp.bfloat16)


def adam_units(grid, param, first, second, grads, turned):
    n = grid.outer
    stacked = jnp.stack([jnp.stack(pieces) for pieces in grads])
    mats, _, units, wide = stacked.shape
    if not turned:
        spec = pl.BlockSpec((units, wide), lambda c, k, at: (k, 0))
    else:
        spec = pl.BlockSpec((None, wide, units), lambda c, k, at: (c, 0, k))
    grad_spec = pl.BlockSpec(
        (None, None, units, wide), lambda c, k, at: (c, lax.rem(at[0] - k + n, n), 0, 0)
    )
    size = param.size
    outs = [jax.ShapeDtypeStruct(param.shape, jnp.float32)] * 3
    outs.append(jax.ShapeDtypeStruct(param.shape, jnp.bfloat16))
    return pl.pallas_call(
        functools.partial(adam_units_kernel, turned),
        grid_spec=pltpu.PrefetchScalarGridSpec(
            num_scalar_prefetch=1,
            grid=(mats, n),
            in_specs=[spec] * 3 + [grad_spec],
            out_specs=[spec] * 4,
        ),
        out_shape=outs,
        cost_estimate=pl.CostEstimate(
            flops=20 * size, bytes_accessed=28 * size, transcendentals=2 * size
        ),
        compiler_params=pltpu.CompilerParams(vmem_limit_bytes=32 * 2**20),
    )(grid.outer_at.astype(jnp.int32)[None], param, first, second, stacked)


def local(
    tokens,
    cotangent,
    block_ids,
    w_qkv,
    m_qkv,
    v_qkv,
    w_out,
    m_out,
    v_out,
    w_gu,
    m_gu,
    v_gu,
    w_down,
    m_down,
    v_down,
    gains,
    gain_m,
    gain_v,
):
    grid = Grid()
    local_x = tokens[0]
    gain_count = gains.shape[0]
    low_gains = jnp.pad(gains.astype(jnp.bfloat16), ((0, 16 - gain_count), (0, 0)))
    full_qkv, full_out, full_gains, seq_x = path_gather(
        w_qkv.astype(jnp.bfloat16), w_out.astype(jnp.bfloat16), low_gains, local_x
    )
    gain_rows = jnp.swapaxes(full_gains[:, :gain_count], 0, 1).reshape(gain_count, -1)
    gain_rows = gain_rows.astype(jnp.float32)
    shard = jnp.stack([w_gu[0], w_gu[1], w_down.T]).astype(jnp.bfloat16)
    full_qkv, shard = lax.optimization_barrier((full_qkv, shard))
    model_width = local_x.shape[1]
    length = seq_x.shape[0]
    span = full_qkv.shape[2]
    heads_here = span // HEAD
    offset = lax.axis_index("tensor") * span
    q_gain = lax.dynamic_slice_in_dim(gain_rows[0], offset, span)
    k_gain = lax.dynamic_slice_in_dim(gain_rows[1], offset, span)
    cosine, sine = rope_tables(length, HEAD)

    def unrotary(grad):
        return (grad * cosine + rotate_back(grad * sine)).reshape(length, span)

    pieces, kept = attend_call(
        seq_x,
        full_qkv,
        full_out,
        jnp.stack([q_gain, k_gain]),
        gain_rows[2:3],
        (cosine[:, 0], sine[:, 0]),
        block_ids[0],
        local_x,
        shard,
    )
    hats, scales, q_low, k_low, v_low, log_total, context_low = kept[:7]
    attn_hat, o_scale, resid, resid_low, tops = kept[7:]
    q_hat, k_hat = hats[0], hats[1]
    q_scale, k_scale = scales[:, 0:1], scales[:, 1:2]
    q_low, k_low, v_low = [v.reshape(length, heads_here, HEAD) for v in (q_low, k_low, v_low)]
    blocks = block_ids[0]
    block_rows = min(512, length)
    block_count = length // block_rows
    scale = HEAD ** (-0.5)
    starts = jnp.arange(block_count, dtype=jnp.int32) * block_rows

    def scores_of(start):
        q_part = lax.dynamic_slice_in_dim(q_low, start, block_rows, 0)
        b_part = lax.dynamic_slice_in_dim(blocks, start, block_rows, 0)
        raw = jnp.einsum("qhd,khd->hqk", q_part, k_low, preferred_element_type=jnp.float32) * scale
        allowed = blocks[None, None, :] <= b_part[None, :, None]
        return (jnp.where(allowed, raw, masked_value), q_part)

    log_total = jnp.swapaxes(log_total.reshape(block_count, block_rows, heads_here), 1, 2)
    output, d_resid, gain_last, unit_grads = unit_kernel_call(
        resid_low, resid, cotangent[0], gain_rows[3:4], pieces
    )
    gain_attn = jnp.sum(d_resid * attn_hat, axis=0)
    d_attn = norm_back(o_scale, attn_hat, d_resid * gain_rows[2]).astype(jnp.bfloat16)
    seq_do = sequence_gather(grid, d_attn)
    grad_out = jnp.einsum("se,sd->ed", context_low, seq_do, preferred_element_type=jnp.float32)
    d_context = jnp.einsum("sd,ed->se", seq_do, full_out, preferred_element_type=jnp.float32)
    d_context = d_context.astype(jnp.bfloat16).reshape(length, heads_here, HEAD)
    part_gate = outer_spread(grid, inner_sum(grid, unit_grads[0], d_context))

    def backward_block(carry, item):
        key_acc, value_acc = carry
        start, log_part = item
        masked, q_part = scores_of(start)
        probs = jnp.exp(masked - log_part[:, :, None])
        dc_part = lax.dynamic_slice_in_dim(d_context, start, block_rows, 0)
        d_probs = jnp.einsum("qhd,khd->hqk", dc_part, v_low, preferred_element_type=jnp.float32)
        inner = jnp.sum(probs * d_probs, axis=2, keepdims=True)
        d_scores = (probs * (d_probs - inner)).astype(jnp.bfloat16)
        d_query = (
            jnp.einsum("hqk,khd->qhd", d_scores, k_low, preferred_element_type=jnp.float32) * scale
        )
        key_acc = (
            key_acc
            + jnp.einsum("hqk,qhd->khd", d_scores, q_part, preferred_element_type=jnp.float32)
            * scale
        )
        value_acc = value_acc + jnp.einsum(
            "hqk,qhd->khd", probs.astype(jnp.bfloat16), dc_part, preferred_element_type=jnp.float32
        )
        return ((key_acc, value_acc), d_query)

    empty = jnp.zeros((length, heads_here, HEAD), jnp.float32)
    (d_krot, d_values), d_qrot = lax.scan(backward_block, (empty, empty), (starts, log_total))
    d_qrot = d_qrot.reshape(length, heads_here, HEAD)
    d_qnorm = unrotary(d_qrot)
    d_knorm = unrotary(d_krot)
    head_gains = jnp.stack([jnp.sum(d_qnorm * q_hat, axis=0), jnp.sum(d_knorm * k_hat, axis=0)])
    placed = lax.dynamic_update_slice(
        jnp.zeros((2, model_width), jnp.float32), head_gains, (0, offset)
    )
    gain_terms = jnp.concatenate([placed, jnp.stack([gain_attn, gain_last[0]])], axis=0)
    dq_hat = d_qnorm * q_gain
    dk_hat = d_knorm * k_gain
    q_inner, k_inner = lax.psum(
        (jnp.sum(dq_hat * q_hat, axis=1), jnp.sum(dk_hat * k_hat, axis=1)), "tensor"
    )
    part_up = outer_spread(grid, inner_sum(grid, unit_grads[1], d_qrot))
    d_query = q_scale * (dq_hat - q_hat * (q_inner / model_width)[:, None])
    d_key = k_scale * (dk_hat - k_hat * (k_inner / model_width)[:, None])
    d_qkv = jnp.stack([d_query, d_key, d_values.reshape(length, span)]).astype(jnp.bfloat16)
    grad_qkv = jnp.einsum("sd,cse->cde", seq_x, d_qkv, preferred_element_type=jnp.float32)
    part_down = outer_spread(grid, inner_sum(grid, unit_grads[2], grad_qkv))
    terms = jnp.swapaxes(gain_terms.reshape(gain_count, grid.dp, -1), 0, 1)
    part_qkv, part_out, part_gains, tops = path_scatter(
        grad_qkv.astype(jnp.bfloat16),
        grad_out.astype(jnp.bfloat16),
        jnp.pad(terms, ((0, 0), (0, 8 - gain_count), (0, 0))),
        tops,
    )
    part_gains = part_gains[:gain_count]
    part_gate, part_up, part_down = after((part_gate, part_up, part_down), part_qkv)
    grad_tokens = d_resid + sequence_scatter(
        grid, jnp.einsum("cse,cde->sd", d_qkv, full_qkv, preferred_element_type=jnp.float32)
    )
    head_top = tops[:heads_here, 0]
    factor = clip_tau / jnp.maximum(head_top, clip_tau)
    column = jnp.repeat(jnp.sqrt(factor), HEAD)
    column_scale = jnp.stack([column, column, jnp.ones_like(column)])[:, None, :]
    new_qkv, new_m_qkv, new_v_qkv, copy_qkv = adam_call(
        w_qkv, part_qkv, m_qkv, v_qkv, column_scale
    )
    new_out, new_m_out, new_v_out, copy_out = adam_call(w_out, part_out, m_out, v_out)
    new_gu, new_m_gu, new_v_gu, copy_gu = adam_units(
        grid, w_gu, m_gu, v_gu, [part_gate, part_up], True
    )
    new_down, new_m_down, new_v_down, copy_down = adam_units(
        grid, w_down, m_down, v_down, [part_down], False
    )
    new_gains, new_gain_m, new_gain_v = adam_step(gains, part_gains, gain_m, gain_v, rate_gain, 0.0)
    return (
        output[None],
        grad_tokens[None],
        new_qkv,
        new_m_qkv,
        new_v_qkv,
        copy_qkv,
        new_out,
        new_m_out,
        new_v_out,
        copy_out,
        new_gu,
        new_m_gu,
        new_v_gu,
        copy_gu,
        new_down,
        new_m_down,
        new_v_down,
        copy_down,
        new_gains,
        new_gain_m,
        new_gain_v,
        factor,
    )


def solution(mesh):
    return jax.shard_map(
        local,
        mesh=mesh,
        in_specs=(
            P("dp", "tensor", None),
            P("dp", "tensor", None),
            P("dp", None),
            P(None, "dp", "tensor"),
            P(None, "dp", "tensor"),
            P(None, "dp", "tensor"),
            P("tensor", "dp"),
            P("tensor", "dp"),
            P("tensor", "dp"),
            P(None, "dp", "tensor"),
            P(None, "dp", "tensor"),
            P(None, "dp", "tensor"),
            P("tensor", "dp"),
            P("tensor", "dp"),
            P("tensor", "dp"),
            P(None, "dp"),
            P(None, "dp"),
            P(None, "dp"),
        ),
        out_specs=(
            P("dp", "tensor", None),
            P("dp", "tensor", None),
            P(None, "dp", "tensor"),
            P(None, "dp", "tensor"),
            P(None, "dp", "tensor"),
            P(None, "dp", "tensor"),
            P("tensor", "dp"),
            P("tensor", "dp"),
            P("tensor", "dp"),
            P("tensor", "dp"),
            P(None, "dp", "tensor"),
            P(None, "dp", "tensor"),
            P(None, "dp", "tensor"),
            P(None, "dp", "tensor"),
            P("tensor", "dp"),
            P("tensor", "dp"),
            P("tensor", "dp"),
            P("tensor", "dp"),
            P(None, "dp"),
            P(None, "dp"),
            P(None, "dp"),
            P("tensor"),
        ),
        check_vma=False,
    )
```

```python
import functools

import jax
import jax.numpy as jnp
from jax import lax
from jax.experimental import pallas as pl
from jax.experimental.pallas import tpu as pltpu
from jax.sharding import PartitionSpec as P

HEAD = 128
STEP = 5


norm_eps = 1e-06
rope_base = 500000.0
beta_one = 0.9
beta_two = 0.95
rate_matrix = 0.01
rate_gain = 0.6
weight_decay = 0.1
adam_eps = 1e-08
clip_tau = 9.0
masked_value = -1e30


def rope_tables(length, size):
    half = size // 2
    freq = rope_base ** (-(jnp.arange(half, dtype=jnp.float32) * 2.0 / size))
    angle = jnp.arange(length, dtype=jnp.float32)[:, None] * freq[None, :]
    angle = jnp.concatenate([angle, angle], axis=1)
    return (jnp.cos(angle)[:, None, :], jnp.sin(angle)[:, None, :])


def adam_step(param, grad, first, second, rate, decay):
    first = beta_one * first + (1.0 - beta_one) * grad
    second = beta_two * second + (1.0 - beta_two) * grad * grad
    fix_one = 1.0 - beta_one**STEP
    fix_two = 1.0 - beta_two**STEP
    update = first / fix_one / (jnp.sqrt(second / fix_two) + adam_eps)
    return (param - rate * (update + decay * param), first, second)


class Grid:
    def __init__(self):
        self.dp = lax.axis_size("dp")
        self.tensor = lax.axis_size("tensor")
        self.inner = 1
        while self.inner * self.inner * 4 <= self.dp:
            self.inner *= 2
        self.outer = self.dp // self.inner
        self.chips = self.tensor // 2
        self.dp_at = lax.axis_index("dp")
        self.tensor_at = lax.axis_index("tensor")
        self.inner_at = self.dp_at % self.inner
        self.chip_at = self.tensor_at // 2
        self.core_at = self.tensor_at % 2
        self.outer_at = self.dp_at // self.inner

    def path_of(self, index):
        column, row = index // self.inner, index % self.inner
        return row * self.outer + column + (row % 2) * (self.outer - 1 - 2 * column)

    def index_of(self, place):
        row, column = place // self.outer, place % self.outer
        return (column + (row % 2) * (self.outer - 1 - 2 * column)) * self.inner + row

    def to_outer(self, value, step):
        n, m = self.outer, self.inner
        pairs = [(a * m + b, (a + step) % n * m + b) for a in range(n) for b in range(m)]
        return lax.ppermute(value, "dp", pairs)

    def to_inner(self, value, step):
        n, m = self.outer, self.inner
        pairs = [(a * m + b, a * m + (b + step) % m) for a in range(n) for b in range(m)]
        return lax.ppermute(value, "dp", pairs)

    def to_chip(self, value, step):
        n = self.chips
        pairs = [(a * 2 + b, (a + step) % n * 2 + b) for a in range(n) for b in range(2)]
        return lax.ppermute(value, "tensor", pairs)

    def to_core(self, value):
        pairs = [(a * 2 + b, a * 2 + 1 - b) for a in range(self.chips) for b in range(2)]
        return lax.ppermute(value, "tensor", pairs)

    def across(self, value, axis, bit):
        count = lax.axis_size(axis)
        return lax.ppermute(value, axis, [(i, i ^ bit) for i in range(count)])


def bits(count):
    return [1 << k for k in range(count.bit_length() - 1)]


def part(value, axis, index, size):
    return lax.dynamic_slice_in_dim(value, index * size, size, axis)


def put(whole, piece, axis, index):
    return lax.dynamic_update_slice_in_dim(whole, piece, index * piece.shape[axis], axis)


def greet(peers):
    barrier = pltpu.get_barrier_semaphore()
    for peer in peers:
        pl.semaphore_signal(barrier, inc=1, device_id=peer, device_id_type=pl.DeviceIdType.MESH)
    pl.semaphore_wait(barrier, len(peers))


def path_gather(shard, flat, gains, rows):
    grid = Grid()
    n, chips, tensor = grid.dp, grid.chips, grid.tensor
    lead, deep, wide = shard.shape
    half = deep // 2
    tall, thin = flat.shape
    part_tall = tall // 2
    count = rows.shape[0]
    ring = 2 * lead + 3

    def kernel(
        shard_ref, flat_ref, gains_ref, rows_ref, full, full_flat, full_gains, sequence,
        sends, lands, row_sends, row_lands, own,
    ):
        g = Grid()
        dp_at, t_at = g.dp_at, g.tensor_at
        chip_at, core_at = t_at // 2, t_at % 2
        place = g.path_of(dp_at)
        after = g.index_of(lax.rem(place + 1, n))
        before = g.index_of(lax.rem(place + n - 1, n))
        core_peer = (dp_at, chip_at * 2 + 1 - core_at)
        chip_peers = [
            (dp_at, lax.rem(chip_at + k, chips) * 2 + core_at) for k in range(1, chips)
        ]
        greet([(after, t_at), (before, t_at), core_peer] + chip_peers)

        def views(item, index):
            if item == ring - 1:
                return 1, gains_ref, full_gains.at[index]
            if item >= 2 * lead:
                side = item - 2 * lead
                span = pl.ds(side * part_tall, part_tall)
                cols = pl.ds(pl.multiple_of(index * thin, thin), thin)
                return 1 - 2 * side, flat_ref.at[span], full_flat.at[span, cols]
            side, c = item // lead, item % lead
            span = pl.ds(pl.multiple_of(index * deep + side * half, half), half)
            return 1 - 2 * side, shard_ref.at[c, pl.ds(side * half, half)], full.at[c, span]

        def hop(step, item):
            way = views(item, 0)[0]
            index = g.index_of(lax.rem(place - way * step + n, n))
            _, source, target = views(item, index)
            return pltpu.make_async_remote_copy(
                src_ref=source if step == 0 else target,
                dst_ref=target,
                send_sem=sends.at[step, item],
                recv_sem=lands.at[step, item],
                device_id=(after if way == 1 else before, t_at),
                device_id_type=pl.DeviceIdType.MESH,
            )

        def rows_at(index):
            return sequence.at[pl.ds(pl.multiple_of(index * count, count), count)]

        def row_copy(slot, index, peer, first):
            return pltpu.make_async_remote_copy(
                src_ref=rows_ref if first else rows_at(index),
                dst_ref=rows_at(index),
                send_sem=row_sends.at[slot],
                recv_sem=row_lands.at[slot],
                device_id=peer,
                device_id_type=pl.DeviceIdType.MESH,
            )

        order = [c + side * lead for c in range(lead) for side in (0, 1)]
        order += list(range(2 * lead, ring))
        hops = {}
        for item in order:
            hops[0, item] = hop(0, item)
            hops[0, item].start()
        moves = []
        for k in range(1, chips):
            moves.append(row_copy(k - 1, t_at, chip_peers[k - 1], True))
            moves[-1].start()
        mine = row_copy(chips - 1, t_at, core_peer, True)
        mine.start()
        keep = [
            pltpu.make_async_copy(
                shard_ref, full.at[:, pl.ds(pl.multiple_of(dp_at * deep, deep), deep)], own.at[0]
            ),
            pltpu.make_async_copy(gains_ref, full_gains.at[dp_at], own.at[1]),
            pltpu.make_async_copy(rows_ref, rows_at(t_at), own.at[2]),
            pltpu.make_async_copy(
                flat_ref, full_flat.at[:, pl.ds(pl.multiple_of(dp_at * thin, thin), thin)], own.at[3]
            ),
        ]
        for copy in keep:
            copy.start()
        passed = []
        for step in range(1, n - 1):
            for item in order:
                hops[step - 1, item].wait_recv()
                hops[step, item] = hop(step, item)
                hops[step, item].start()
            if step <= chips - 1:
                moves[step - 1].wait_recv()
                source = lax.rem(chip_at - step + chips, chips) * 2 + core_at
                passed.append(row_copy(chips - 1 + step, source, core_peer, False))
                passed[-1].start()
        for item in order:
            hops[n - 2, item].wait_recv()
        mine.wait_recv()
        for copy in passed:
            copy.wait_recv()
        for key in hops:
            hops[key].wait_send()
        for copy in moves + [mine] + passed:
            copy.wait_send()
        for copy in keep:
            copy.wait()

    bf16 = jnp.bfloat16
    return pl.pallas_call(
        kernel,
        out_shape=(
            jax.ShapeDtypeStruct((lead, deep * n, wide), bf16),
            jax.ShapeDtypeStruct((tall, thin * n), bf16),
            jax.ShapeDtypeStruct((n,) + gains.shape, bf16),
            jax.ShapeDtypeStruct((count * tensor, rows.shape[1]), bf16),
        ),
        in_specs=[pl.BlockSpec(memory_space=pl.ANY)] * 4,
        out_specs=(pl.BlockSpec(memory_space=pl.ANY),) * 4,
        scratch_shapes=[
            pltpu.SemaphoreType.DMA((n - 1, ring)),
            pltpu.SemaphoreType.DMA((n - 1, ring)),
            pltpu.SemaphoreType.DMA((2 * chips - 1,)),
            pltpu.SemaphoreType.DMA((2 * chips - 1,)),
            pltpu.SemaphoreType.DMA((4,)),
        ],
        compiler_params=pltpu.CompilerParams(collective_id=0, has_side_effects=True),
    )(shard, flat, gains, rows)


def attend_back_call(
    d_resid, attn_hat, o_scale, out_gain, full_out, context, q_low, k_low, v_low, lse, hats, scales,
    head_gains, tables, blocks, seq, full_qkv, gain_last, tops, unit_grads,
):
    grid = Grid()
    n, outer, inner, chips, tensor = grid.dp, grid.outer, grid.inner, grid.chips, grid.tensor
    count, width = d_resid.shape
    length, span = context.shape
    heads = span // HEAD
    units, slab = unit_grads[0][0].shape[1:]
    thin = width // n
    half = span // 2
    tall = min(256, length)
    tile = 512
    lines = 32
    ring = 8 + 2
    gain_item, top_item = 8, 9
    bf16, f32 = jnp.bfloat16, jnp.float32
    mesh_id = pl.DeviceIdType.MESH
    flat_grads = [unit_grads[c][j] for j in range(inner) for c in range(3)]
    some = len(flat_grads)
    z_steps = sorted(range(1, outer), key=lambda s: (min(s, outer - s), s))

    def kernel(*refs):
        fixed, far_in, grads_in = refs[:18], refs[18:21], refs[21 : 21 + some]
        rest = refs[21 + some :]
        backs = [rest[c * outer : (c + 1) * outer] for c in range(3)]
        body(*fixed, far_in, grads_in, backs, *rest[3 * outer :])

    def body(
        dres_ref, hat_ref, o_scale_ref, out_gain_ref, out_w, ctx, q_ref, k_ref, v_ref, lse_ref, scale_ref,
        gain_ref, cos_ref, sin_ref, id_col, id_row, last_ref, tops_ref, far_in, grads_in,
        backs, part_ref, gains_out, tops_out, tokens_out,
        hats, seq, qkv_w, seq_do, d_ctx, d_q, d_k, d_v, d_low, whole, terms, row_terms, turned,
        land, land_gain, land_top, own_gain, peer_gain, inners, peer_inners,
        grad_own, grad_land, grad_sum, core_send, core_land, hold, chip_send, chip_land,
        s_ring, r_ring, s_row, r_row, s_in, r_in, s_y, r_y, s_z, r_z, s_core, r_core, s_chip, r_chip, s_gain, r_gain, local,
    ):
        hats_in, seq_in, qkv_in = far_in
        g = Grid()

        def tensor_peer(k, flip):
            core = 1 - g.core_at if flip else g.core_at
            return (g.dp_at, lax.rem(g.chip_at + k + chips, chips) * 2 + core)

        def dp_peer(s, j):
            across = lax.rem(g.outer_at + s + outer, outer) * inner
            return (across + lax.rem(g.inner_at + j + inner, inner), g.tensor_at)

        place = g.path_of(g.dp_at)
        after_dp = (g.index_of(lax.rem(place + 1, n)), g.tensor_at)
        before_dp = (g.index_of(lax.rem(place + n - 1, n)), g.tensor_at)
        near = [tensor_peer(k, f) for k in range(chips) for f in (0, 1) if (k, f) != (0, 0)]
        far = [dp_peer(s, 0) for s in range(1, outer)] + [dp_peer(0, j) for j in range(1, inner)]
        greet(near + far + [after_dp, before_dp])

        def remote(src, dst, send, recv, peer):
            copy = pltpu.make_async_remote_copy(
                src_ref=src, dst_ref=dst, send_sem=send, recv_sem=recv,
                device_id=peer, device_id_type=mesh_id,
            )
            copy.start()
            return copy

        def fetch(src, dst, at):
            copy = pltpu.make_async_copy(src, dst, local.at[at])
            copy.start()
            return copy

        def dot(a, b, contract):
            return lax.dot_general(a, b, (contract, ((), ())), preferred_element_type=f32)

        def looped(total, make):
            lax.fori_loop(0, total, lambda i, c: (make(i), c)[1], 0)

        def rows_of(i, size):
            return pl.ds(pl.multiple_of(i * size, size), size)

        sent = []
        y_copies = {}
        for j in range(1, inner):
            for c in range(3):
                copy = remote(
                    grads_in[j * 3 + c], grad_land.at[j - 1, c], s_y.at[j, c], r_y.at[j, c], dp_peer(0, j)
                )
                y_copies[j, c] = copy
                sent.append(copy)
        own_grads = [fetch(grads_in[c], grad_own.at[c], c) for c in range(3)]
        fetched = [fetch(hats_in, hats, 3), fetch(seq_in, seq, 4), fetch(qkv_in, qkv_w, 5)]
        z_copies = []
        keeps = []

        def unit_sums(c):
            own_grads[c].wait()
            for j in range(1, inner):
                y_copies[j, c].wait_recv()

            def add(i):
                s, at = i // (units // 64), lax.rem(i, units // 64)
                rows = rows_of(at, 64)
                total = grad_own[c, s, rows].astype(f32)
                for j in range(1, inner):
                    total = total + grad_land[j - 1, c, s, rows].astype(f32)
                grad_sum[c, s, rows] = total.astype(bf16)

            looped(outer * (units // 64), add)
            for s in z_steps:
                z_copies.append(
                    remote(grad_sum.at[c, s], backs[c][s], s_z.at[c, s], r_z.at[c, s], dp_peer(s, 0))
                )
            keeps.append(fetch(grad_sum.at[c, 0], backs[c][0], 6 + c))

        t_at = g.tensor_at
        mine = rows_of(t_at, count)

        def open_rows(i, total):
            at = rows_of(i, lines)
            value, hat = dres_ref[at], hat_ref[at]
            upstream = value * out_gain_ref[...]
            mean = jnp.mean(upstream * hat, axis=1, keepdims=True)
            d_attn = (o_scale_ref[at] * (upstream - hat * mean)).astype(bf16)
            seq_do[pl.ds(pl.multiple_of(t_at * count + i * lines, lines), lines)] = d_attn
            return total + jnp.sum(value * hat, axis=0, keepdims=True)

        gain_attn = lax.fori_loop(0, count // lines, open_rows, jnp.zeros((1, width), f32))
        row_terms[...] = jnp.zeros((8, width), f32)
        row_terms[2:3] = gain_attn
        row_terms[3:4] = last_ref[...]
        moves, passed = [], []

        def row_copy(slot, index, peer):
            at = rows_of(index, count)
            copy = remote(seq_do.at[at], seq_do.at[at], s_row.at[slot], r_row.at[slot], peer)
            sent.append(copy)
            return copy

        for k in range(1, chips):
            moves.append(row_copy(k - 1, t_at, tensor_peer(k, 0)))
        to_core = row_copy(chips - 1, t_at, tensor_peer(0, 1))
        for k in range(1, chips):
            moves[k - 1].wait_recv()
            source = lax.rem(g.chip_at - k + chips, chips) * 2 + g.core_at
            passed.append(row_copy(chips - 1 + k, source, tensor_peer(0, 1)))
        to_core.wait_recv()
        for copy in passed:
            copy.wait_recv()

        def context_grad(i):
            at = rows_of(i, tall)
            d_ctx[at] = dot(seq_do[at], out_w[...], ((1,), (1,))).astype(bf16)

        looped(length // tall, context_grad)
        unit_sums(0)

        scale = HEAD ** (-0.5)
        for h in range(heads):
            cols = slice(h * HEAD, (h + 1) * HEAD)

            def head(i, c, cols=cols, h=h):
                at = rows_of(i, tall)
                q_part, ctx_part = q_ref[at, cols], d_ctx[at, cols]
                raw = dot(q_part, k_ref[:, cols], ((1,), (1,))) * scale
                masked = jnp.where(id_row[...] <= id_col[at], raw, masked_value)
                probs = jnp.exp(masked - lse_ref[at, h : h + 1])
                d_probs = dot(ctx_part, v_ref[:, cols], ((1,), (1,)))
                mean = jnp.sum(probs * d_probs, axis=1, keepdims=True)
                d_scores = (probs * (d_probs - mean)).astype(bf16)
                d_q[at, cols] = dot(d_scores, k_ref[:, cols], ((1,), (0,))) * scale
                key = dot(d_scores, q_part, ((0,), (0,))) * scale
                value = dot(probs.astype(bf16), ctx_part, ((0,), (0,)))
                d_k[:, cols] = jnp.where(i == 0, key, d_k[:, cols] + key)
                d_v[:, cols] = jnp.where(i == 0, value, d_v[:, cols] + value)
                return c

            d_k[:, cols] = jnp.zeros((length, HEAD), f32)
            d_v[:, cols] = jnp.zeros((length, HEAD), f32)
            lax.fori_loop(0, length // tall, head, 0)
        if inner > 1 or outer > 1:
            unit_sums(1)
        fetched[0].wait()
        sign = jnp.where(lax.broadcasted_iota(jnp.int32, (tall, HEAD), 1) < HEAD // 2, -1.0, 1.0)

        def unrotate(i, sums):
            at = rows_of(i, tall)
            cosine, sine = cos_ref[at], sin_ref[at]
            lane = lax.broadcasted_iota(jnp.int32, (tall, 128), 1)
            columns = jnp.zeros((tall, 128), f32)
            result = []
            for c, grad in ((0, d_q), (1, d_k)):
                total = jnp.zeros((tall, 1), f32)
                terms_row = []
                for h in range(heads):
                    cols = slice(h * HEAD, (h + 1) * HEAD)
                    value = grad[at, cols]
                    back = value * cosine - pltpu.roll(value * sine, HEAD // 2, 1) * sign
                    hat = hats[c, at, cols]
                    terms_row.append(jnp.sum(back * hat, axis=0, keepdims=True))
                    back = back * gain_ref[c : c + 1, cols]
                    grad[at, cols] = back
                    total = total + jnp.sum(back * hat, axis=1, keepdims=True)
                columns = jnp.where(lane == c, total, columns)
                result.append(sums[c] + jnp.concatenate(terms_row, axis=1))
            inners[:, at] = columns.T[:8]
            return tuple(result)

        zero = jnp.zeros((1, span), f32)
        gain_q, gain_k = lax.fori_loop(0, length // tall, unrotate, (zero, zero))
        offset = rows_of(t_at, span)
        row_terms[0:1, offset] = gain_q
        row_terms[1:2, offset] = gain_k
        in_copies = []
        for k in range(chips):
            for f in (0, 1):
                if (k, f) != (0, 0):
                    at = k * 2 + f - 1
                    in_copies.append(
                        remote(inners, peer_inners.at[at], s_in.at[at], r_in.at[at], tensor_peer(k, f))
                    )
        sent.extend(in_copies)
        turned[...] = ctx[...].T

        def out_grad(i):
            cols = rows_of(i, tile)
            whole[3, :, cols] = dot(turned[...], seq_do[:, cols], ((1,), (0,))).astype(bf16)

        looped(width // tile, out_grad)
        for copy in in_copies:
            copy.wait_recv()

        def normed(i):
            at = rows_of(i, tall)
            sums = inners[:, at]
            for other in range(tensor - 1):
                sums = sums + peer_inners[other, :, at]
            column = jnp.concatenate([sums, jnp.zeros((120, tall), f32)], axis=0).T / width
            for c, grad in ((0, d_q), (1, d_k)):
                value = grad[at] - hats[c, at] * column[:, c : c + 1]
                d_low[c, at] = (scale_ref[at, c : c + 1] * value).astype(bf16)
            d_low[2, at] = d_v[at].astype(bf16)

        looped(length // tall, normed)
        fetched[1].wait()
        for c in range(3):
            turned[...] = d_low[c].T

            def weight_grad(i, c=c):
                cols = rows_of(i, tile)
                whole[c, :, cols] = dot(turned[...], seq[:, cols], ((1,), (0,))).astype(bf16)

            looped(width // tile, weight_grad)

        def place_terms(i, c):
            cols = pl.ds(pl.multiple_of(i * thin, thin), thin)
            terms[i] = row_terms[:, cols]
            return c

        lax.fori_loop(0, n, place_terms, 0)

        def way_of(item):
            return 1 if item >= 8 else 1 - 2 * (item // 4)

        def own(item, away):
            index = g.index_of(lax.rem(place - way_of(item) * away + 2 * n, n))
            if item == gain_item:
                return terms.at[index]
            if item == top_item:
                return tops_ref
            side, c = item // 4, item % 4
            return whole.at[c, pl.ds(side * half, half), rows_of(index, thin)]

        def landed(step, item):
            if item == gain_item:
                return land_gain.at[step]
            if item == top_item:
                return land_top.at[step]
            return land.at[step, item]

        hops = {}

        def hop(step, item):
            hops[step, item] = remote(
                own(item, 1) if step == 0 else landed(step - 1, item),
                landed(step, item),
                s_ring.at[step, item],
                r_ring.at[step, item],
                after_dp if way_of(item) == 1 else before_dp,
            )

        order = [gain_item, top_item] + [c + side * 4 for c in range(4) for side in (0, 1)]
        for item in order:
            hop(0, item)
        unit_sums(2)

        fetched[2].wait()
        chip_order = list(range(1, chips)) + [0]
        core_copies, chip_copies = {}, {}

        def token_rows(k, flip, store):
            chip = lax.rem(g.chip_at + k, chips)
            core = 1 - g.core_at if flip else g.core_at
            at = rows_of(chip * 2 + core, count)

            def columns(i):
                cols = rows_of(i, tile)
                total = dot(d_low[0, at], qkv_w[0, cols], ((1,), (1,)))
                for c in (1, 2):
                    total = total + dot(d_low[c, at], qkv_w[c, cols], ((1,), (1,)))
                store(cols, total)

            looped(width // tile, columns)

        duties = []
        for k in chip_order:

            def away(k=k):
                def store(cols, value):
                    core_send[k, :, cols] = value.astype(bf16)

                token_rows(k, True, store)
                core_copies[k] = remote(
                    core_send.at[k], core_land.at[k], s_core.at[k], r_core.at[k], tensor_peer(0, 1)
                )

            def here(k=k):
                def store(cols, value):
                    hold[k, :, cols] = value

                token_rows(k, False, store)

            def join(k=k):
                core_copies[k].wait_recv()

                def add(i):
                    at = rows_of(i, lines)
                    chip_send[k - 1, at] = (hold[k, at] + core_land[k, at].astype(f32)).astype(bf16)

                looped(count // lines, add)
                chip_copies[k] = remote(
                    chip_send.at[k - 1], chip_land.at[k - 1], s_chip.at[k], r_chip.at[k], tensor_peer(k, 0)
                )

            duties += [away, here] + ([join] if k else [])

        def close_tokens():
            core_copies[0].wait_recv()
            for k in range(1, chips):
                chip_copies[k].wait_recv()

            def close(i):
                at = rows_of(i, lines)
                total = dres_ref[at] + hold[0, at] + core_land[0, at].astype(f32)
                for k in range(1, chips):
                    total = total + chip_land[k - 1, at].astype(f32)
                tokens_out[at] = total

            looped(count // lines, close)

        duties.append(close_tokens)
        per_step = -(-len(duties) // (n - 2))
        for step in range(1, n):
            for item in order:
                hops[step - 1, item].wait_recv()
                here = landed(step - 1, item)
                if item == top_item:
                    summed = jnp.maximum(here[...], tops_ref[...])
                else:
                    summed = here[...].astype(f32) + own(item, step + 1)[...].astype(f32)
                if step < n - 1:
                    here[...] = summed.astype(here.dtype)
                    hop(step, item)
                elif item == gain_item:
                    own_gain[0] = summed
                elif item == top_item:
                    tops_out[...] = summed
                else:
                    side, c = item // 4, item % 4
                    part_ref[c, pl.ds(side * half, half)] = summed
            for _ in range(per_step):
                if duties:
                    duties.pop(0)()
        peers = [tensor_peer(0, 1)] + [tensor_peer(k, 0) for k in range(1, chips)]
        first = remote(own_gain.at[0], peer_gain.at[0], s_gain.at[0], r_gain.at[0], peers[0])
        first.wait_recv()
        own_gain[1] = own_gain[0] + peer_gain[0]
        others = [
            remote(own_gain.at[1], peer_gain.at[k], s_gain.at[k], r_gain.at[k], peers[k])
            for k in range(1, chips)
        ]
        result = own_gain[1]
        for k in range(1, chips):
            others[k - 1].wait_recv()
            result = result + peer_gain[k]
        gains_out[...] = result
        for copy in z_copies:
            copy.wait()
        for copy in keeps:
            copy.wait()
        for copy in sent + list(hops.values()) + list(core_copies.values()):
            copy.wait_send()
        for copy in list(chip_copies.values()) + [first] + others:
            copy.wait_send()

    shape = jax.ShapeDtypeStruct
    anywhere = pl.BlockSpec(memory_space=pl.ANY)
    vmem = pl.BlockSpec(memory_space=pltpu.VMEM)
    sems = pltpu.SemaphoreType.DMA
    results = pl.pallas_call(
        kernel,
        out_shape=(shape((units, slab), bf16),) * (3 * outer)
        + (
            shape((4, span, thin), f32),
            shape((8, thin), f32),
            shape(tops.shape, f32),
            shape((count, width), f32),
        ),
        in_specs=[vmem] * 18 + [anywhere] * 3 + [anywhere] * some,
        out_specs=(anywhere,) * (3 * outer) + (vmem,) * 4,
        scratch_shapes=[
            pltpu.VMEM(hats.shape, f32),
            pltpu.VMEM(seq.shape, bf16),
            pltpu.VMEM(full_qkv.shape, bf16),
            pltpu.VMEM((length, width), bf16),
            pltpu.VMEM((length, span), bf16),
            pltpu.VMEM((length, span), f32),
            pltpu.VMEM((length, span), f32),
            pltpu.VMEM((length, span), f32),
            pltpu.VMEM((3, length, span), bf16),
            pltpu.VMEM((4, span, width), bf16),
            pltpu.VMEM((n, 8, thin), f32),
            pltpu.VMEM((8, width), f32),
            pltpu.VMEM((span, length), bf16),
            pltpu.VMEM((n - 1, 8, half, thin), bf16),
            pltpu.VMEM((n - 1, 8, thin), f32),
            pltpu.VMEM((n - 1,) + tops.shape, f32),
            pltpu.VMEM((2, 8, thin), f32),
            pltpu.VMEM((chips, 8, thin), f32),
            pltpu.VMEM((8, length), f32),
            pltpu.VMEM((tensor - 1, 8, length), f32),
            pltpu.VMEM((3, outer, units, slab), bf16),
            pltpu.VMEM((max(inner - 1, 1), 3, outer, units, slab), bf16),
            pltpu.VMEM((3, outer, units, slab), bf16),
            pltpu.VMEM((chips, count, width), bf16),
            pltpu.VMEM((chips, count, width), bf16),
            pltpu.VMEM((chips, count, width), f32),
            pltpu.VMEM((max(chips - 1, 1), count, width), bf16),
            pltpu.VMEM((max(chips - 1, 1), count, width), bf16),
            sems((n - 1, ring)),
            sems((n - 1, ring)),
            sems((2 * chips - 1,)),
            sems((2 * chips - 1,)),
            sems((tensor - 1,)),
            sems((tensor - 1,)),
            sems((inner, 3)),
            sems((inner, 3)),
            sems((3, outer)),
            sems((3, outer)),
            sems((chips,)),
            sems((chips,)),
            sems((chips,)),
            sems((chips,)),
            sems((chips,)),
            sems((chips,)),
            sems((9,)),
        ],
        compiler_params=pltpu.CompilerParams(
            collective_id=1, has_side_effects=True, vmem_limit_bytes=62 * 2**20
        ),
    )(
        d_resid, attn_hat, o_scale, out_gain, full_out, context, q_low, k_low, v_low, lse, scales,
        head_gains, tables[0], tables[1], blocks[:, None], blocks[None, :], gain_last, tops,
        hats, seq, full_qkv, *flat_grads,
    )
    backs = [results[c * outer : (c + 1) * outer] for c in range(3)]
    return backs, results[3 * outer :]


def attend_call(seq, full_qkv, full_out, head_gains, out_gain, tables, blocks, rows, shard):
    grid = Grid()
    outer, inner, chips, tensor = grid.outer, grid.inner, grid.chips, grid.tensor
    length, width = seq.shape
    span = full_qkv.shape[2]
    heads = span // HEAD
    count = rows.shape[0]
    slab = shard.shape[1]
    units = shard.shape[2] // outer
    parts = outer * inner
    steps = sorted(range(1, outer), key=lambda s: (min(s, outer - s), s))
    tall = min(256, length)
    tile = 512
    lines = 32
    bf16, f32 = jnp.bfloat16, jnp.float32
    mesh_id = pl.DeviceIdType.MESH

    def kernel(
        seq_ref, qkv_ref, out_w_ref, gains_ref, out_gain_ref, cos_ref, sin_ref, id_col, id_row, rows_ref, shard_ref,
        *refs
    ):
        pieces = [refs[j * outer : (j + 1) * outer] for j in range(inner)]
        body(
            seq_ref, qkv_ref, out_w_ref, gains_ref, out_gain_ref, cos_ref, sin_ref, id_col, id_row, rows_ref, shard_ref,
            pieces, *refs[parts:],
        )

    def body(
        seq_ref, qkv_ref, out_w_ref, gains_ref, out_gain_ref, cos_ref, sin_ref, id_col, id_row, rows_ref, shard_ref,
        pieces, hat_ref, scale_ref, q_low, k_low, v_low, lse_ref, context, attn_hat, o_scale, resid, resid_low, top_ref,
        square, squares, core_send, core_land, hold, chip_send, chip_land,
        s_z, r_z, s_y, r_y, s_sq, r_sq, s_core, r_core, s_chip, r_chip, local,
    ):
        g = Grid()

        def tensor_peer(k, flip):
            core = 1 - g.core_at if flip else g.core_at
            return (g.dp_at, lax.rem(g.chip_at + k + chips, chips) * 2 + core)

        def dp_peer(s, j):
            across = lax.rem(g.outer_at + s + outer, outer) * inner
            return (across + lax.rem(g.inner_at + j + inner, inner), g.tensor_at)

        near = [tensor_peer(k, f) for k in range(chips) for f in (0, 1) if (k, f) != (0, 0)]
        far = [dp_peer(s, 0) for s in range(1, outer)]
        far += [dp_peer(0, j) for j in sorted({1 % inner, inner - 1} - {0})]
        greet(near + far)

        def remote(src, dst, send, recv, peer):
            copy = pltpu.make_async_remote_copy(
                src_ref=src, dst_ref=dst, send_sem=send, recv_sem=recv,
                device_id=peer, device_id_type=mesh_id,
            )
            copy.start()
            return copy

        def dot(a, b, contract):
            return lax.dot_general(a, b, (contract, ((), ())), preferred_element_type=f32)

        def looped(total, make):
            lax.fori_loop(0, total, lambda i, c: (make(i), c)[1], 0)

        def rows_of(i, size):
            return pl.ds(pl.multiple_of(i * size, size), size)

        def cut(s):
            at = lax.rem(g.outer_at + s, outer)
            return shard_ref.at[:, :, rows_of(at, units)]

        z_copies = {
            s: remote(cut(s), pieces[0][s], s_z.at[s], r_z.at[s], dp_peer(s, 0)) for s in steps
        }
        own = pltpu.make_async_copy(cut(0), pieces[0][0], local)
        own.start()
        y_copies = {}

        def pass_on(j, s):
            src = cut(0) if (j, s) == (1, 0) else pieces[j - 1][s]
            y_copies[j, s] = remote(src, pieces[j][s], s_y.at[j, s], r_y.at[j, s], dp_peer(0, 1))

        if inner > 1:
            pass_on(1, 0)
        duties = []
        for s in steps:

            def duty(s=s):
                z_copies[s].wait_recv()
                if inner > 1:
                    pass_on(1, s)

            duties.append(duty)
        for j in range(2, inner):
            for s in [0] + steps:

                def duty(j=j, s=s):
                    y_copies[j - 1, s].wait_recv()
                    pass_on(j, s)

                duties.append(duty)

        def next_duty():
            if duties:
                duties.pop(0)()

        def project(i):
            at = rows_of(i, tall)
            x = seq_ref[at]
            lane = lax.broadcasted_iota(jnp.int32, (tall, 128), 1)
            sums = jnp.zeros((tall, 128), f32)
            for c in range(2):
                value = dot(x, qkv_ref[c], ((1,), (0,)))
                hat_ref[c, at] = value
                sums = jnp.where(lane == c, jnp.sum(value * value, axis=1, keepdims=True), sums)
            v_low[at] = dot(x, qkv_ref[2], ((1,), (0,))).astype(bf16)
            square[:, at] = sums.T[:8]

        looped(length // tall, project)
        sq_copies = []
        for k in range(chips):
            for f in (0, 1):
                if (k, f) != (0, 0):
                    at = k * 2 + f - 1
                    sq_copies.append(
                        remote(square, squares.at[at], s_sq.at[at], r_sq.at[at], tensor_peer(k, f))
                    )
        for copy in sq_copies:
            copy.wait_recv()
        sign = jnp.where(lax.broadcasted_iota(jnp.int32, (tall, HEAD), 1) < HEAD // 2, -1.0, 1.0)

        def rotate(i):
            at = rows_of(i, tall)
            sums = square[:, at]
            for copy_at in range(tensor - 1):
                sums = sums + squares[copy_at, :, at]
            column = jnp.concatenate([sums, jnp.zeros((120, tall), f32)], axis=0).T
            scales = lax.rsqrt(column / width + norm_eps)
            scale_ref[at] = scales
            cosine, sine = cos_ref[at], sin_ref[at] * sign
            for c, low in ((0, q_low), (1, k_low)):
                hat = hat_ref[c, at] * scales[:, c : c + 1]
                hat_ref[c, at] = hat
                normed = hat * gains_ref[c : c + 1]
                for h in range(heads):
                    cols = slice(h * HEAD, (h + 1) * HEAD)
                    value = normed[:, cols]
                    turned = pltpu.roll(value, HEAD // 2, 1)
                    low[at, cols] = (value * cosine + turned * sine).astype(bf16)

        looped(length // tall, rotate)
        scale = HEAD ** (-0.5)
        top_ref[...] = jnp.full((8, 128), masked_value, f32)
        for h in range(heads):
            cols = slice(h * HEAD, (h + 1) * HEAD)

            def attend(i, best, cols=cols, h=h):
                at = rows_of(i, tall)
                raw = dot(q_low[at, cols], k_low[:, cols], ((1,), (1,))) * scale
                masked = jnp.where(id_row[...] <= id_col[at], raw, masked_value)
                top = jnp.max(masked, axis=1, keepdims=True)
                weight = jnp.exp(masked - top)
                total = jnp.sum(weight, axis=1, keepdims=True)
                probs = (weight / total).astype(bf16)
                context[at, cols] = dot(probs, v_low[:, cols], ((1,), (0,))).astype(bf16)
                lse_ref[at, h : h + 1] = top + jnp.log(total)
                return jnp.maximum(best, jnp.max(top, axis=0, keepdims=True))

            best = lax.fori_loop(
                0, length // tall, attend, jnp.full((1, 1), masked_value, f32)
            )
            top_ref[h : h + 1] = jnp.broadcast_to(best, (1, 128))
        next_duty()

        def out_rows(k, flip, store):
            chip = lax.rem(g.chip_at + k, chips)
            core = 1 - g.core_at if flip else g.core_at
            at = rows_of(chip * 2 + core, count)

            def columns(i):
                cols = rows_of(i, tile)
                store(cols, dot(context[at], out_w_ref[:, cols], ((1,), (0,))))

            looped(width // tile, columns)

        chip_order = list(range(1, chips)) + [0]
        core_copies, chip_copies = {}, {}
        for k in chip_order:

            def store(cols, value, k=k):
                core_send[k, :, cols] = value.astype(bf16)

            out_rows(k, True, store)
            core_copies[k] = remote(
                core_send.at[k], core_land.at[k], s_core.at[k], r_core.at[k], tensor_peer(0, 1)
            )
        for k in chip_order:

            def store(cols, value, k=k):
                hold[k, :, cols] = value

            out_rows(k, False, store)
            if k:
                core_copies[k].wait_recv()

                def add(i, k=k):
                    at = rows_of(i, lines)
                    chip_send[k - 1, at] = (hold[k, at] + core_land[k, at].astype(f32)).astype(bf16)

                looped(count // lines, add)
                chip_copies[k] = remote(
                    chip_send.at[k - 1], chip_land.at[k - 1], s_chip.at[k], r_chip.at[k], tensor_peer(k, 0)
                )
        next_duty()
        core_copies[0].wait_recv()
        for k in range(1, chips):
            chip_copies[k].wait_recv()

        def close(i):
            at = rows_of(i, lines)
            raw = hold[0, at] + core_land[0, at].astype(f32)
            for k in range(1, chips):
                raw = raw + chip_land[k - 1, at].astype(f32)
            scale_o = lax.rsqrt(jnp.mean(raw * raw, axis=1, keepdims=True) + norm_eps)
            hat = raw * scale_o
            attn_hat[at] = hat
            o_scale[at] = scale_o
            value = rows_ref[at].astype(f32) + hat * out_gain_ref[...]
            resid[at] = value
            resid_low[at] = value.astype(bf16)

        looped(count // lines, close)
        while duties:
            next_duty()
        own.wait()
        for key, copy in y_copies.items():
            if key[0] == inner - 1:
                copy.wait_recv()
        sent = list(z_copies.values()) + list(y_copies.values()) + sq_copies
        for copy in sent + list(core_copies.values()) + list(chip_copies.values()):
            copy.wait_send()

    shape = jax.ShapeDtypeStruct
    anywhere = pl.BlockSpec(memory_space=pl.ANY)
    vmem = pl.BlockSpec(memory_space=pltpu.VMEM)
    sems = pltpu.SemaphoreType.DMA
    results = pl.pallas_call(
        kernel,
        out_shape=(shape((3, slab, units), bf16),) * parts
        + (
            shape((2, length, span), f32),
            shape((length, 128), f32),
            shape((length, span), bf16),
            shape((length, span), bf16),
            shape((length, span), bf16),
            shape((length, heads), f32),
            shape((length, span), bf16),
            shape((count, width), f32),
            shape((count, 1), f32),
            shape((count, width), f32),
            shape((count, width), bf16),
            shape((8, 128), f32),
        ),
        in_specs=[vmem] * 10 + [anywhere],
        out_specs=(anywhere,) * parts + (vmem,) * 12,
        scratch_shapes=[
            pltpu.VMEM((8, length), f32),
            pltpu.VMEM((tensor - 1, 8, length), f32),
            pltpu.VMEM((chips, count, width), bf16),
            pltpu.VMEM((chips, count, width), bf16),
            pltpu.VMEM((chips, count, width), f32),
            pltpu.VMEM((max(chips - 1, 1), count, width), bf16),
            pltpu.VMEM((max(chips - 1, 1), count, width), bf16),
            sems((outer,)),
            sems((outer,)),
            sems((inner, outer)),
            sems((inner, outer)),
            sems((tensor - 1,)),
            sems((tensor - 1,)),
            sems((chips,)),
            sems((chips,)),
            sems((chips,)),
            sems((chips,)),
            sems(()),
        ],
        compiler_params=pltpu.CompilerParams(
            collective_id=3, has_side_effects=True, vmem_limit_bytes=56 * 2**20
        ),
    )(
        seq, full_qkv, full_out, head_gains, out_gain, tables[0], tables[1],
        blocks[:, None], blocks[None, :], rows, shard,
    )
    pieces = [results[j * outer : (j + 1) * outer] for j in range(inner)]
    return pieces, results[parts:]


def unit_kernel_call(rows_low, resid, cotangent, gain, pieces):
    grid = Grid()
    outer, chips = grid.outer, grid.chips
    count, width = rows_low.shape
    units = pieces[0][0].shape[2]
    slab = pieces[0][0].shape[1]
    inner = grid.inner
    flat_pieces = [piece for row in pieces for piece in row]
    parts = len(flat_pieces)
    both = 2 * count
    per = min(2, chips)
    groups = chips // per
    blocks = outer * groups
    tall = per * both
    held = per if groups > 1 else max(per - 1, 1)
    steps = [0] + sorted(range(1, outer), key=lambda s: (min(s, outer - s), s))
    order = [(s, i) for s in steps for i in range(groups)]
    tile = 512
    wide_tiles = width // tile
    unit_tile = min(256, units)
    lines = 32
    bf16, f32 = jnp.bfloat16, jnp.float32
    mesh_id = pl.DeviceIdType.MESH

    def plan(phase):
        block_us, core_us, hop_us = 10.5, 1.0, 2.0
        free = {"tc": 0.0, "x": 0.0, "core": 0.0, "z": 0.0}
        done = {}
        tasks = {}

        def send(link, when, us):
            free[link] = max(free[link], when) + us
            return free[link] + hop_us

        def add(name, needs, us, after=None):
            tasks[name] = (needs, us, after)

        arrive = {}
        for i, s in enumerate(steps[1:]):
            arrive["z", s] = 15.0 + 13.0 * i
        for k in range(1, chips):
            arrive["x", 0, k] = send("x", 0.0, block_us)
        arrive["c", 0, 0] = send("core", 0.0, core_us)

        def zf(s):
            def then(now):
                for k in range(1, chips):
                    arrive["x", s, k] = send("x", now, block_us)
                arrive["c", s, 0] = send("core", now, core_us)

            return then

        def xf(s, k):
            def then(now):
                arrive["c", s, k] = send("core", now, core_us)

            return then

        def compute(u):
            def then(now):
                arrive["cr", u] = send("core", now, core_us)

            return then

        def cr(s, i):
            def then(now):
                for k in range(i * per, i * per + per):
                    if k:
                        arrive["xr", s, k] = send("x", now, block_us)

            return then

        def xr(s):
            def then(now):
                if s:
                    arrive["zr", s] = send("z", now, block_us) + 3.0

            return then

        for s in steps[1:]:
            add(("zf", s), [("at", ("z", s))], 0.3, zf(s))
        for s in steps:
            for k in range(1, chips):
                add(("xf", s, k), [("at", ("x", s, k))], 0.3, xf(s, k))
        for i, (s, k) in enumerate(order):
            needs = [("at", ("c", s, k * per + j)) for j in range(per)]
            if phase and i:
                needs.append(("do", ("grads",) + order[i - 1]))
            elif i >= 2:
                needs.append(("do", ("compute",) + order[i - 2]))
            add(("load", s, k), needs, 0.2, None)
            needs = [("do", ("load", s, k))]
            if i >= 2:
                needs.append(("do", ("cr",) + order[i - 2]))
            add(("compute", s, k), needs, 5.0, compute((s, k)))
            if phase:
                add(("grads", s, k), [("do", ("compute", s, k))], 6.0, None)
            add(("cr", s, k), [("at", ("cr", (s, k))), ("do", ("compute", s, k))], 0.6, cr(s, k))
        for s in steps:
            needs = [("do", ("cr", s, 0))] + [("at", ("xr", s, k)) for k in range(1, chips)]
            add(("xr", s), needs, 0.6, xr(s))
        for s in steps[1:]:
            add(("zr", s), [("at", ("zr", s)), ("do", ("xr", 0))], 0.6, None)
        if phase:
            needs = [("do", ("xr", s)) for s in steps]
            add(("write", 0), needs + [("do", ("grads",) + unit) for unit in order], 4.0, None)
        result = []
        now = 0.0
        while tasks:
            best = None
            for name, (needs, us, after) in tasks.items():
                ready = 0.0
                for kind, key in needs:
                    table = arrive if kind == "at" else done
                    if key not in table:
                        ready = None
                        break
                    ready = max(ready, table[key] + (1.0 if key[0] == "load" else 0.0))
                if ready is None:
                    continue
                ready = max(ready, now)
                rank = {"compute": 1, "grads": 2, "write": 3}.get(name[0], 0)
                if best is None or (ready, rank) < best[:2]:
                    best = (ready, rank, name)
            ready, _, name = best
            needs, us, after = tasks.pop(name)
            now = ready + us
            done[name] = now
            if after is not None:
                after(now)
            result.append(name)
        return result

    def kernel(
        *refs
    ):
        piece_refs = refs[:parts]
        rows_ref, resid_ref, cot_ref, gain_ref = refs[parts : parts + 4]
        out_ref, dres_ref, gain_out, all_x, all_dm = refs[parts + 4 : parts + 9]
        grad_refs = refs[parts + 9 : parts + 9 + 3 * inner]
        rest = refs[parts + 9 + 3 * inner :]
        body(piece_refs, rows_ref, resid_ref, cot_ref, gain_ref, out_ref, dres_ref, gain_out, all_x, all_dm, grad_refs, *rest)

    def body(
        piece_refs, rows_ref, resid_ref, cot_ref, gain_ref,
        out_ref, dres_ref, gain_out, all_x, all_dm, grad_refs,
        wg, wu, wd, buf, act, coef_gate, coef_up, d_gate, d_up, turned, acc_gate, acc_up, acc_down, stage,
        core_send, core_land, hold, keep, chip_send, chip_land, outer_send, outer_land, raw, d_mlp,
        s_outer, r_outer, s_chip, r_chip, s_core, r_core,
        s_core_sum, r_core_sum, s_chip_sum, r_chip_sum, s_outer_sum, r_outer_sum, local, local_w, local_g,
    ):
        g = Grid()
        core_peer = (g.dp_at, g.chip_at * 2 + 1 - g.core_at)

        def chip_peer(k):
            return (g.dp_at, lax.rem(g.chip_at + k + chips, chips) * 2 + g.core_at)

        def outer_peer(s):
            return (lax.rem(g.outer_at + s + outer, outer) * g.inner + g.inner_at, g.tensor_at)

        greet(
            [core_peer]
            + [chip_peer(k) for k in range(1, chips)]
            + [outer_peer(s) for s in range(1, outer)]
        )

        def remote(src, dst, send, recv, peer):
            return pltpu.make_async_remote_copy(
                src_ref=src, dst_ref=dst, send_sem=send, recv_sem=recv,
                device_id=peer, device_id_type=mesh_id,
            )

        def dot(a, b, contract):
            return lax.dot_general(a, b, (contract, ((), ())), preferred_element_type=f32)

        def looped(total, body):
            lax.fori_loop(0, total, lambda i, c: (body(i), c)[1], 0)

        def by_lines(body):
            looped(count // lines, lambda i: body(pl.ds(pl.multiple_of(i * lines, lines), lines)))

        def by_tiles(body):
            looped(wide_tiles, lambda i: body(pl.ds(pl.multiple_of(i * tile, tile), tile)))

        weights = (wg, wu, wd)
        fetches = []
        for j in range(inner):
            for s in range(outer):
                index = lax.rem(g.outer_at - s + outer, outer) * inner
                index = index + lax.rem(g.inner_at - j + inner, inner)
                span = pl.ds(pl.multiple_of(index * slab, slab), slab)
                for c in range(3):
                    at = j * outer + s
                    fetches.append(
                        pltpu.make_async_copy(
                            piece_refs[at].at[c], weights[c].at[span], local_w.at[at, c]
                        )
                    )
        started = []

        def run(phase, source, everything, fetched, compute, grads, write):
            mine = pl.ds(0, count)
            theirs = pl.ds(count, count)
            copies = {}

            def start(key, copy):
                copy.start()
                copies[key] = copy
                started.append(copy)

            def at(s, k, half):
                return everything.at[s, k, half]

            def core_copy(s, k, src):
                start(
                    ("c", s, k),
                    remote(src, at(s, k, theirs), s_core.at[phase, s, k], r_core.at[phase, s, k], core_peer),
                )

            def chip_copy(s, k, src):
                start(
                    ("x", s, k),
                    remote(src, at(s, k, mine), s_chip.at[phase, s, k], r_chip.at[phase, s, k], chip_peer(k)),
                )

            for s in steps[1:]:
                start(
                    ("z", s),
                    remote(source, at(s, 0, mine), s_outer.at[phase, s], r_outer.at[phase, s], outer_peer(s)),
                )
            for k in range(1, chips):
                chip_copy(0, k, source)
            core_copy(0, 0, source)
            own = pltpu.make_async_copy(source, at(0, 0, mine), local.at[phase, 0, blocks])
            own.start()
            if phase == 0:
                for copy in fetches:
                    copy.start()
            slots = {unit: i % 2 for i, unit in enumerate(order)}
            span_of = {u: pl.ds(u[1] * per, per) for u in order}
            loads = {}
            sums = {}
            for task in plan(phase):
                name, s = task[:2]
                k = task[2] if len(task) > 2 else 0
                unit = s * groups + k
                if name == "zf":
                    copies["z", s].wait_recv()
                    for j in range(1, chips):
                        chip_copy(s, j, at(s, 0, mine))
                    core_copy(s, 0, at(s, 0, mine))
                elif name == "xf":
                    copies["x", s, k].wait_recv()
                    core_copy(s, k, at(s, k, mine))
                elif name == "load":
                    for j in range(per):
                        copies["c", s, k * per + j].wait_recv()
                    if (s, k) == (0, 0):
                        own.wait()
                    loads[s, k] = []
                    places = [slots[s, k], 2]
                    for j, src in enumerate(fetched):
                        copy = pltpu.make_async_copy(
                            src.at[s, span_of[s, k]], buf.at[places[j]], local.at[phase, j, unit]
                        )
                        copy.start()
                        loads[s, k].append(copy)
                elif name == "compute":
                    if phase == 0 and (s, k) == order[0]:
                        for copy in fetches:
                            copy.wait()
                    for copy in loads[s, k]:
                        copy.wait()
                    i = order.index((s, k))
                    if i >= 2:
                        sums["core", order[i - 2]].wait_send()
                    slot = slots[s, k]

                    def send(slot=slot, unit=unit, s=s, k=k):
                        copy = remote(
                            core_send.at[slot], core_land.at[unit],
                            s_core_sum.at[phase, unit], r_core_sum.at[phase, unit], core_peer,
                        )
                        copy.start()
                        sums["core", (s, k)] = copy

                    compute(slot, unit, s, k, send)
                elif name == "grads":
                    grads(slots[s, k], unit)
                elif name == "write":
                    write()
                elif name == "cr":
                    sums["core", (s, k)].wait_recv()
                    slot = slots[s, k]
                    for j in range(per):
                        chip = k * per + j
                        if chip == 0:

                            def add_core(at_rows, s=s, unit=unit, j=j):
                                keep[s, at_rows] = keep[s, at_rows] + core_land[unit, j, at_rows].astype(f32)

                            by_lines(add_core)
                            continue
                        there = s * (chips - 1) + chip - 1

                        def add_core(at_rows, there=there, slot=slot, unit=unit, j=j, i=min(j, held - 1)):
                            total = hold[slot, i, at_rows] + core_land[unit, j, at_rows].astype(f32)
                            chip_send[there, at_rows] = total.astype(bf16)

                        by_lines(add_core)
                        copy = remote(
                            chip_send.at[there], chip_land.at[there],
                            s_chip_sum.at[phase, there], r_chip_sum.at[phase, there], chip_peer(-chip),
                        )
                        copy.start()
                        sums["chip", (s, chip)] = copy
                elif name == "xr":
                    for j in range(1, chips):
                        sums["chip", (s, j)].wait_recv()

                    def add_chip(at_rows, s=s):
                        total = keep[s, at_rows]
                        for j in range(1, chips):
                            total = total + chip_land[s * (chips - 1) + j - 1, at_rows].astype(f32)
                        if s == 0:
                            raw[at_rows] = total
                        else:
                            outer_send[s - 1, at_rows] = total.astype(bf16)

                    by_lines(add_chip)
                    if s:
                        copy = remote(
                            outer_send.at[s - 1], outer_land.at[s - 1],
                            s_outer_sum.at[phase, s], r_outer_sum.at[phase, s], outer_peer(-s),
                        )
                        copy.start()
                        sums["outer", s] = copy
                elif name == "zr":
                    sums["outer", s].wait_recv()

                    def add_outer(at_rows, s=s):
                        raw[at_rows] = raw[at_rows] + outer_land[s - 1, at_rows].astype(f32)

                    by_lines(add_outer)
            waited = [sums["core", unit] for unit in order[-2:]]
            waited += [copy for key, copy in sums.items() if key[0] != "core"]
            for copy in waited:
                copy.wait_send()
            for copy in started:
                copy.wait_send()
            started.clear()

        def part_out(slot, s, i, cols, part_sum):
            for j in range(per):
                own_rows = part_sum[j * both : j * both + count]
                if i * per + j == 0:
                    keep[s, :, cols] = own_rows
                else:
                    hold[slot, min(j, held - 1), :, cols] = own_rows
                core_send[slot, j, :, cols] = part_sum[j * both + count : (j + 1) * both].astype(bf16)

        def forward(slot, unit, s, i, send):
            for j in range(units // unit_tile):
                cols = pl.ds(j * unit_tile, unit_tile)
                rows = buf[slot].reshape(tall, width)
                gate = dot(rows, wg[:, cols], ((1,), (0,)))
                up = dot(rows, wu[:, cols], ((1,), (0,)))
                sigma = jax.nn.sigmoid(gate)
                silu = gate * sigma
                act[unit, :, cols] = (silu * up).astype(bf16)
                coef_up[unit, :, cols] = silu.astype(bf16)
                coef_gate[unit, :, cols] = (up * sigma * (1.0 + gate * (1.0 - sigma))).astype(bf16)

            def down(cols):
                part_out(slot, s, i, cols, dot(act[unit], wd[cols, :], ((1,), (1,))))

            by_tiles(down)
            send()

        def between():
            def lines_of(i, total):
                at_rows = pl.ds(pl.multiple_of(i * lines, lines), lines)
                value = raw[at_rows]
                scale = lax.rsqrt(jnp.mean(value * value, axis=1, keepdims=True) + norm_eps)
                hat = value * scale
                gain_row = gain_ref[...]
                out_ref[at_rows] = (resid_ref[at_rows] + hat * gain_row).astype(bf16)
                top = cot_ref[at_rows].astype(f32)
                upstream = top * gain_row
                inner = jnp.mean(upstream * hat, axis=1, keepdims=True)
                d_mlp[at_rows] = (scale * (upstream - hat * inner)).astype(bf16)
                return total + jnp.sum(top * hat, axis=0, keepdims=True)

            gain_out[...] = lax.fori_loop(
                0, count // lines, lines_of, jnp.zeros((1, width), f32)
            )

        def backward(slot, unit, s, i, send):
            for j in range(units // unit_tile):
                cols = pl.ds(j * unit_tile, unit_tile)
                d_act = dot(buf[slot].reshape(tall, width), wd[:, cols], ((1,), (0,)))
                d_gate[:, cols] = (d_act * coef_gate[unit, :, cols].astype(f32)).astype(bf16)
                d_up[:, cols] = (d_act * coef_up[unit, :, cols].astype(f32)).astype(bf16)

            def into(cols):
                part_sum = dot(d_gate[...], wg[cols, :], ((1,), (1,)))
                part_sum = part_sum + dot(d_up[...], wu[cols, :], ((1,), (1,)))
                part_out(slot, s, i, cols, part_sum)

            by_tiles(into)
            send()

        def weight_grads(slot, unit):
            first = unit == order[0][0] * groups + order[0][1]
            for left, right, acc in (
                (d_gate[...], 2, acc_gate),
                (d_up[...], 2, acc_up),
                (act[unit], slot, acc_down),
            ):
                turned[...] = left.T

                def grads(cols, right=right, acc=acc):
                    rows = buf[right, :, :, cols].reshape(tall, tile)
                    value = dot(turned[...], rows, ((1,), (0,)))
                    acc[:, cols] = value if first else acc[:, cols] + value

                by_tiles(grads)

        def write_grads():
            copies = []
            for j in range(inner):
                for s in range(outer):
                    index = lax.rem(g.outer_at + s, outer) * inner
                    index = index + lax.rem(g.inner_at + j, inner)
                    span = pl.ds(pl.multiple_of(index * slab, slab), slab)
                    slot = len(copies) % 2
                    if len(copies) >= 2:
                        for copy in copies[-2]:
                            copy.wait()
                    batch = []
                    for c, acc in enumerate((acc_gate, acc_up, acc_down)):
                        stage[slot, c] = acc[:, span].astype(bf16)
                        copy = pltpu.make_async_copy(
                            stage.at[slot, c], grad_refs[j * 3 + c].at[s], local_g.at[slot, c]
                        )
                        copy.start()
                        batch.append(copy)
                    copies.append(batch)
            for batch in copies[-2:]:
                for copy in batch:
                    copy.wait()

        run(0, rows_ref, all_x, [all_x], forward, None, None)
        between()
        run(1, d_mlp, all_dm, [all_dm, all_x], backward, weight_grads, write_grads)

        def close(at_rows):
            dres_ref[at_rows] = raw[at_rows] + cot_ref[at_rows].astype(f32)

        by_lines(close)

    def held_in(space):
        return pl.BlockSpec(memory_space=space)

    shape = jax.ShapeDtypeStruct
    anywhere, near = held_in(pl.ANY), held_in(pltpu.VMEM)
    sems = pltpu.SemaphoreType.DMA
    links = outer * (chips - 1)
    flops = 2 * 9 * tall * blocks * width * units
    results = pl.pallas_call(
        kernel,
        out_shape=(
            shape((count, width), bf16),
            shape((count, width), f32),
            shape((1, width), f32),
            shape((outer, chips, both, width), bf16),
            shape((outer, chips, both, width), bf16),
        )
        + (shape((outer, units, slab), bf16),) * (3 * inner),
        in_specs=[anywhere] * (parts + 1) + [near] * 3,
        out_specs=(near, near, near) + (anywhere,) * (2 + 3 * inner),
        scratch_shapes=[
            pltpu.VMEM((width, units), bf16),
            pltpu.VMEM((width, units), bf16),
            pltpu.VMEM((width, units), bf16),
            pltpu.VMEM((3, per, both, width), bf16),
            pltpu.VMEM((blocks, tall, units), bf16),
            pltpu.VMEM((blocks, tall, units), bf16),
            pltpu.VMEM((blocks, tall, units), bf16),
            pltpu.VMEM((tall, units), bf16),
            pltpu.VMEM((tall, units), bf16),
            pltpu.VMEM((units, tall), bf16),
            pltpu.VMEM((units, width), f32),
            pltpu.VMEM((units, width), f32),
            pltpu.VMEM((units, width), f32),
            pltpu.VMEM((2, 3, units, slab), bf16),
            pltpu.VMEM((2, per, count, width), bf16),
            pltpu.VMEM((blocks, per, count, width), bf16),
            pltpu.VMEM((2, held, count, width), f32),
            pltpu.VMEM((outer, count, width), f32),
            pltpu.VMEM((links, count, width), bf16),
            pltpu.VMEM((links, count, width), bf16),
            pltpu.VMEM((outer - 1, count, width), bf16),
            pltpu.VMEM((outer - 1, count, width), bf16),
            pltpu.VMEM((count, width), f32),
            pltpu.VMEM((count, width), bf16),
            sems((2, outer)),
            sems((2, outer)),
            sems((2, outer, chips)),
            sems((2, outer, chips)),
            sems((2, outer, chips)),
            sems((2, outer, chips)),
            sems((2, blocks)),
            sems((2, blocks)),
            sems((2, links)),
            sems((2, links)),
            sems((2, outer)),
            sems((2, outer)),
            sems((2, 2, blocks + 1)),
            sems((parts, 3)),
            sems((2, 3)),
        ],
        compiler_params=pltpu.CompilerParams(
            collective_id=2, has_side_effects=True, vmem_limit_bytes=61 * 2**20
        ),
        cost_estimate=pl.CostEstimate(flops=flops, bytes_accessed=64 * 2**20, transcendentals=0),
    )(*flat_pieces, rows_low, resid, cotangent, gain)
    grads = results[5:]
    return results[:3] + ([[grads[j * 3 + c] for j in range(inner)] for c in range(3)],)


def adam_kernel(turned, w_ref, m_ref, v_ref, g_ref, *rest):
    scale_ref = rest[0] if len(rest) == 5 else None
    w_out, m_out, v_out, c_out = rest[-4:]
    grad = g_ref[...].T if turned else g_ref[...]
    new, first, second = adam_step(
        w_ref[...], grad, m_ref[...], v_ref[...], rate_matrix, weight_decay
    )
    if scale_ref is not None:
        new = new * scale_ref[...]
    w_out[...] = new
    m_out[...] = first
    v_out[...] = second
    c_out[...] = new.astype(jnp.bfloat16)


def adam_call(param, grads, at, first, second, scale=None):
    mats, rows, columns = param.shape
    turned = scale is not None
    spec = pl.BlockSpec((None, rows, columns), lambda k: (k, 0, 0))
    grad_spec = pl.BlockSpec((None,) + grads.shape[1:], lambda k: (at + k, 0, 0))
    specs = [spec] * 3 + [grad_spec]
    values = [param, first, second, grads]
    if turned:
        values.append(scale)
        specs.append(pl.BlockSpec((None, 1, columns), lambda k: (k, 0, 0)))
    outs = [jax.ShapeDtypeStruct(param.shape, jnp.float32)] * 3
    outs.append(jax.ShapeDtypeStruct(param.shape, jnp.bfloat16))
    size = param.size
    return pl.pallas_call(
        functools.partial(adam_kernel, turned),
        grid=(mats,),
        in_specs=specs,
        out_specs=[spec] * 4,
        out_shape=outs,
        cost_estimate=pl.CostEstimate(
            flops=20 * size, bytes_accessed=28 * size, transcendentals=2 * size
        ),
        compiler_params=pltpu.CompilerParams(vmem_limit_bytes=32 * 2**20),
    )(*values)


def adam_units_kernel(turned, at_ref, w_ref, m_ref, v_ref, g_ref, w_out, m_out, v_out, c_out):
    grad = g_ref[...].astype(jnp.float32)
    if turned:
        grad = grad.T
    new, first, second = adam_step(
        w_ref[...], grad, m_ref[...], v_ref[...], rate_matrix, weight_decay
    )
    w_out[...] = new
    m_out[...] = first
    v_out[...] = second
    c_out[...] = new.astype(jnp.bfloat16)


def adam_units(grid, param, first, second, grads, turned):
    n = grid.outer
    stacked = jnp.stack([jnp.stack(list(pieces)) for pieces in grads])
    mats, _, units, wide = stacked.shape
    if not turned:
        spec = pl.BlockSpec((units, wide), lambda c, k, at: (k, 0))
    else:
        spec = pl.BlockSpec((None, wide, units), lambda c, k, at: (c, 0, k))
    grad_spec = pl.BlockSpec(
        (None, None, units, wide), lambda c, k, at: (c, lax.rem(at[0] - k + n, n), 0, 0)
    )
    size = param.size
    outs = [jax.ShapeDtypeStruct(param.shape, jnp.float32)] * 3
    outs.append(jax.ShapeDtypeStruct(param.shape, jnp.bfloat16))
    return pl.pallas_call(
        functools.partial(adam_units_kernel, turned),
        grid_spec=pltpu.PrefetchScalarGridSpec(
            num_scalar_prefetch=1,
            grid=(mats, n),
            in_specs=[spec] * 3 + [grad_spec],
            out_specs=[spec] * 4,
        ),
        out_shape=outs,
        cost_estimate=pl.CostEstimate(
            flops=20 * size, bytes_accessed=28 * size, transcendentals=2 * size
        ),
        compiler_params=pltpu.CompilerParams(vmem_limit_bytes=32 * 2**20),
    )(grid.outer_at.astype(jnp.int32)[None], param, first, second, stacked)


def local(
    tokens,
    cotangent,
    block_ids,
    w_qkv,
    m_qkv,
    v_qkv,
    w_out,
    m_out,
    v_out,
    w_gu,
    m_gu,
    v_gu,
    w_down,
    m_down,
    v_down,
    gains,
    gain_m,
    gain_v,
):
    grid = Grid()
    local_x = tokens[0]
    gain_count = gains.shape[0]
    low_gains = jnp.pad(gains.astype(jnp.bfloat16), ((0, 16 - gain_count), (0, 0)))
    full_qkv, full_out, full_gains, seq_x = path_gather(
        w_qkv.astype(jnp.bfloat16), w_out.astype(jnp.bfloat16), low_gains, local_x
    )
    gain_rows = jnp.swapaxes(full_gains[:, :gain_count], 0, 1).reshape(gain_count, -1)
    gain_rows = gain_rows.astype(jnp.float32)
    shard = jnp.stack([w_gu[0], w_gu[1], w_down.T]).astype(jnp.bfloat16)
    full_qkv, shard = lax.optimization_barrier((full_qkv, shard))
    model_width = local_x.shape[1]
    length = seq_x.shape[0]
    span = full_qkv.shape[2]
    heads_here = span // HEAD
    offset = lax.axis_index("tensor") * span
    q_gain = lax.dynamic_slice_in_dim(gain_rows[0], offset, span)
    k_gain = lax.dynamic_slice_in_dim(gain_rows[1], offset, span)
    cosine, sine = rope_tables(length, HEAD)

    head_gains = jnp.stack([q_gain, k_gain])
    tables = (cosine[:, 0], sine[:, 0])
    pieces, kept = attend_call(
        seq_x,
        full_qkv,
        full_out,
        head_gains,
        gain_rows[2:3],
        tables,
        block_ids[0],
        local_x,
        shard,
    )
    hats, scales, q_low, k_low, v_low, log_total, context_low = kept[:7]
    attn_hat, o_scale, resid, resid_low, tops = kept[7:]
    output, d_resid, gain_last, unit_grads = unit_kernel_call(
        resid_low, resid, cotangent[0], gain_rows[3:4], pieces
    )
    backs, (part, part_gains, tops, grad_tokens) = attend_back_call(
        d_resid,
        attn_hat,
        o_scale,
        gain_rows[2:3],
        full_out,
        context_low,
        q_low,
        k_low,
        v_low,
        log_total,
        hats,
        scales,
        head_gains,
        tables,
        block_ids[0],
        seq_x,
        full_qkv,
        gain_last,
        tops,
        unit_grads,
    )
    part_gains = part_gains[:gain_count]
    head_top = tops[:heads_here, 0]
    factor = clip_tau / jnp.maximum(head_top, clip_tau)
    column = jnp.repeat(jnp.sqrt(factor), HEAD)
    column_scale = jnp.stack([column, column, jnp.ones_like(column)])[:, None, :]
    new_qkv, new_m_qkv, new_v_qkv, copy_qkv = adam_call(w_qkv, part, 0, m_qkv, v_qkv, column_scale)
    new_out, new_m_out, new_v_out, copy_out = [
        v[0] for v in adam_call(w_out[None], part, 3, m_out[None], v_out[None])
    ]
    new_gu, new_m_gu, new_v_gu, copy_gu = adam_units(grid, w_gu, m_gu, v_gu, backs[:2], True)
    new_down, new_m_down, new_v_down, copy_down = adam_units(
        grid, w_down, m_down, v_down, backs[2:], False
    )
    new_gains, new_gain_m, new_gain_v = adam_step(gains, part_gains, gain_m, gain_v, rate_gain, 0.0)
    return (
        output[None],
        grad_tokens[None],
        new_qkv,
        new_m_qkv,
        new_v_qkv,
        copy_qkv,
        new_out,
        new_m_out,
        new_v_out,
        copy_out,
        new_gu,
        new_m_gu,
        new_v_gu,
        copy_gu,
        new_down,
        new_m_down,
        new_v_down,
        copy_down,
        new_gains,
        new_gain_m,
        new_gain_v,
        factor,
    )


def solution(mesh):
    return jax.shard_map(
        local,
        mesh=mesh,
        in_specs=(
            P("dp", "tensor", None),
            P("dp", "tensor", None),
            P("dp", None),
            P(None, "dp", "tensor"),
            P(None, "dp", "tensor"),
            P(None, "dp", "tensor"),
            P("tensor", "dp"),
            P("tensor", "dp"),
            P("tensor", "dp"),
            P(None, "dp", "tensor"),
            P(None, "dp", "tensor"),
            P(None, "dp", "tensor"),
            P("tensor", "dp"),
            P("tensor", "dp"),
            P("tensor", "dp"),
            P(None, "dp"),
            P(None, "dp"),
            P(None, "dp"),
        ),
        out_specs=(
            P("dp", "tensor", None),
            P("dp", "tensor", None),
            P(None, "dp", "tensor"),
            P(None, "dp", "tensor"),
            P(None, "dp", "tensor"),
            P(None, "dp", "tensor"),
            P("tensor", "dp"),
            P("tensor", "dp"),
            P("tensor", "dp"),
            P("tensor", "dp"),
            P(None, "dp", "tensor"),
            P(None, "dp", "tensor"),
            P(None, "dp", "tensor"),
            P(None, "dp", "tensor"),
            P("tensor", "dp"),
            P("tensor", "dp"),
            P("tensor", "dp"),
            P("tensor", "dp"),
            P(None, "dp"),
            P(None, "dp"),
            P(None, "dp"),
            P("tensor"),
        ),
        check_vma=False,
    )
```

```python
import functools

import jax
import jax.numpy as jnp
from jax import lax
from jax.experimental import pallas as pl
from jax.experimental.pallas import tpu as pltpu
from jax.sharding import PartitionSpec as P

HEAD = 128
STEP = 5


norm_eps = 1e-06
rope_base = 500000.0
beta_one = 0.9
beta_two = 0.95
rate_matrix = 0.01
rate_gain = 0.6
weight_decay = 0.1
adam_eps = 1e-08
clip_tau = 9.0
masked_value = -1e30


def rope_tables(length, size):
    half = size // 2
    freq = rope_base ** (-(jnp.arange(half, dtype=jnp.float32) * 2.0 / size))
    angle = jnp.arange(length, dtype=jnp.float32)[:, None] * freq[None, :]
    angle = jnp.concatenate([angle, angle], axis=1)
    return (jnp.cos(angle)[:, None, :], jnp.sin(angle)[:, None, :])


def adam_step(param, grad, first, second, rate, decay):
    first = beta_one * first + (1.0 - beta_one) * grad
    second = beta_two * second + (1.0 - beta_two) * grad * grad
    fix_one = 1.0 - beta_one**STEP
    fix_two = 1.0 - beta_two**STEP
    update = first / fix_one / (jnp.sqrt(second / fix_two) + adam_eps)
    return (param - rate * (update + decay * param), first, second)


class Grid:
    def __init__(self):
        self.dp = lax.axis_size("dp")
        self.tensor = lax.axis_size("tensor")
        self.inner = 1
        while self.inner * self.inner * 4 <= self.dp:
            self.inner *= 2
        self.outer = self.dp // self.inner
        self.chips = self.tensor // 2
        self.dp_at = lax.axis_index("dp")
        self.tensor_at = lax.axis_index("tensor")
        self.inner_at = self.dp_at % self.inner
        self.chip_at = self.tensor_at // 2
        self.core_at = self.tensor_at % 2
        self.outer_at = self.dp_at // self.inner

    def path_of(self, index):
        column, row = index // self.inner, index % self.inner
        return row * self.outer + column + (row % 2) * (self.outer - 1 - 2 * column)

    def index_of(self, place):
        row, column = place // self.outer, place % self.outer
        return (column + (row % 2) * (self.outer - 1 - 2 * column)) * self.inner + row

    def to_outer(self, value, step):
        n, m = self.outer, self.inner
        pairs = [(a * m + b, (a + step) % n * m + b) for a in range(n) for b in range(m)]
        return lax.ppermute(value, "dp", pairs)

    def to_inner(self, value, step):
        n, m = self.outer, self.inner
        pairs = [(a * m + b, a * m + (b + step) % m) for a in range(n) for b in range(m)]
        return lax.ppermute(value, "dp", pairs)

    def to_chip(self, value, step):
        n = self.chips
        pairs = [(a * 2 + b, (a + step) % n * 2 + b) for a in range(n) for b in range(2)]
        return lax.ppermute(value, "tensor", pairs)

    def to_core(self, value):
        pairs = [(a * 2 + b, a * 2 + 1 - b) for a in range(self.chips) for b in range(2)]
        return lax.ppermute(value, "tensor", pairs)

    def across(self, value, axis, bit):
        count = lax.axis_size(axis)
        return lax.ppermute(value, axis, [(i, i ^ bit) for i in range(count)])


def bits(count):
    return [1 << k for k in range(count.bit_length() - 1)]


def part(value, axis, index, size):
    return lax.dynamic_slice_in_dim(value, index * size, size, axis)


def put(whole, piece, axis, index):
    return lax.dynamic_update_slice_in_dim(whole, piece, index * piece.shape[axis], axis)


def greet(peers):
    barrier = pltpu.get_barrier_semaphore()
    for peer in peers:
        pl.semaphore_signal(barrier, inc=1, device_id=peer, device_id_type=pl.DeviceIdType.MESH)
    pl.semaphore_wait(barrier, len(peers))


def path_gather(shard, flat, gains, rows):
    grid = Grid()
    n, chips, tensor = grid.dp, grid.chips, grid.tensor
    lead, deep, wide = shard.shape
    half = deep // 2
    tall, thin = flat.shape
    part_tall = tall // 2
    count = rows.shape[0]
    ring = 2 * lead + 3

    def kernel(
        shard_ref, flat_ref, gains_ref, rows_ref, full, full_flat, full_gains, sequence,
        sends, lands, row_sends, row_lands, own,
    ):
        g = Grid()
        dp_at, t_at = g.dp_at, g.tensor_at
        chip_at, core_at = t_at // 2, t_at % 2
        place = g.path_of(dp_at)
        after = g.index_of(lax.rem(place + 1, n))
        before = g.index_of(lax.rem(place + n - 1, n))
        core_peer = (dp_at, chip_at * 2 + 1 - core_at)
        chip_peers = [
            (dp_at, lax.rem(chip_at + k, chips) * 2 + core_at) for k in range(1, chips)
        ]
        greet([(after, t_at), (before, t_at), core_peer] + chip_peers)

        def views(item, index):
            if item == ring - 1:
                return 1, gains_ref, full_gains.at[index]
            if item >= 2 * lead:
                side = item - 2 * lead
                span = pl.ds(side * part_tall, part_tall)
                cols = pl.ds(pl.multiple_of(index * thin, thin), thin)
                return 1 - 2 * side, flat_ref.at[span], full_flat.at[span, cols]
            side, c = item // lead, item % lead
            span = pl.ds(pl.multiple_of(index * deep + side * half, half), half)
            return 1 - 2 * side, shard_ref.at[c, pl.ds(side * half, half)], full.at[c, span]

        def hop(step, item):
            way = views(item, 0)[0]
            index = g.index_of(lax.rem(place - way * step + n, n))
            _, source, target = views(item, index)
            return pltpu.make_async_remote_copy(
                src_ref=source if step == 0 else target,
                dst_ref=target,
                send_sem=sends.at[step, item],
                recv_sem=lands.at[step, item],
                device_id=(after if way == 1 else before, t_at),
                device_id_type=pl.DeviceIdType.MESH,
            )

        def rows_at(index):
            return sequence.at[pl.ds(pl.multiple_of(index * count, count), count)]

        def row_copy(slot, index, peer, first):
            return pltpu.make_async_remote_copy(
                src_ref=rows_ref if first else rows_at(index),
                dst_ref=rows_at(index),
                send_sem=row_sends.at[slot],
                recv_sem=row_lands.at[slot],
                device_id=peer,
                device_id_type=pl.DeviceIdType.MESH,
            )

        order = [c + side * lead for c in range(lead) for side in (0, 1)]
        order += list(range(2 * lead, ring))
        hops = {}
        for item in order:
            hops[0, item] = hop(0, item)
            hops[0, item].start()
        moves = []
        for k in range(1, chips):
            moves.append(row_copy(k - 1, t_at, chip_peers[k - 1], True))
            moves[-1].start()
        mine = row_copy(chips - 1, t_at, core_peer, True)
        mine.start()
        keep = [
            pltpu.make_async_copy(
                shard_ref, full.at[:, pl.ds(pl.multiple_of(dp_at * deep, deep), deep)], own.at[0]
            ),
            pltpu.make_async_copy(gains_ref, full_gains.at[dp_at], own.at[1]),
            pltpu.make_async_copy(rows_ref, rows_at(t_at), own.at[2]),
            pltpu.make_async_copy(
                flat_ref, full_flat.at[:, pl.ds(pl.multiple_of(dp_at * thin, thin), thin)], own.at[3]
            ),
        ]
        for copy in keep:
            copy.start()
        passed = []
        for step in range(1, n - 1):
            for item in order:
                hops[step - 1, item].wait_recv()
                hops[step, item] = hop(step, item)
                hops[step, item].start()
            if step <= chips - 1:
                moves[step - 1].wait_recv()
                source = lax.rem(chip_at - step + chips, chips) * 2 + core_at
                passed.append(row_copy(chips - 1 + step, source, core_peer, False))
                passed[-1].start()
        for item in order:
            hops[n - 2, item].wait_recv()
        mine.wait_recv()
        for copy in passed:
            copy.wait_recv()
        for key in hops:
            hops[key].wait_send()
        for copy in moves + [mine] + passed:
            copy.wait_send()
        for copy in keep:
            copy.wait()

    bf16 = jnp.bfloat16
    return pl.pallas_call(
        kernel,
        out_shape=(
            jax.ShapeDtypeStruct((lead, deep * n, wide), bf16),
            jax.ShapeDtypeStruct((tall, thin * n), bf16),
            jax.ShapeDtypeStruct((n,) + gains.shape, bf16),
            jax.ShapeDtypeStruct((count * tensor, rows.shape[1]), bf16),
        ),
        in_specs=[pl.BlockSpec(memory_space=pl.ANY)] * 4,
        out_specs=(pl.BlockSpec(memory_space=pl.ANY),) * 4,
        scratch_shapes=[
            pltpu.SemaphoreType.DMA((n - 1, ring)),
            pltpu.SemaphoreType.DMA((n - 1, ring)),
            pltpu.SemaphoreType.DMA((2 * chips - 1,)),
            pltpu.SemaphoreType.DMA((2 * chips - 1,)),
            pltpu.SemaphoreType.DMA((4,)),
        ],
        compiler_params=pltpu.CompilerParams(collective_id=0, has_side_effects=True),
    )(shard, flat, gains, rows)


def attend_back_call(
    d_resid, attn_hat, o_scale, out_gain, full_out, context, q_low, k_low, v_low, lse, hats, scales,
    head_gains, tables, blocks, seq, full_qkv, gain_last, tops, unit_grads,
):
    grid = Grid()
    n, outer, inner, chips, tensor = grid.dp, grid.outer, grid.inner, grid.chips, grid.tensor
    count, width = d_resid.shape
    length, span = context.shape
    heads = span // HEAD
    units, slab = unit_grads[0][0].shape[1:]
    thin = width // n
    half = span // 2
    tall = min(256, length)
    tile = 512
    lines = 32
    ring = 8 + 2
    gain_item, top_item = 8, 9
    bf16, f32 = jnp.bfloat16, jnp.float32
    mesh_id = pl.DeviceIdType.MESH
    flat_grads = [unit_grads[c][j] for j in range(inner) for c in range(3)]
    some = len(flat_grads)
    z_steps = sorted(range(1, outer), key=lambda s: (min(s, outer - s), s))

    def kernel(*refs):
        fixed, far_in, grads_in = refs[:18], refs[18:21], refs[21 : 21 + some]
        rest = refs[21 + some :]
        backs = [rest[c * outer : (c + 1) * outer] for c in range(3)]
        body(*fixed, far_in, grads_in, backs, *rest[3 * outer :])

    def body(
        dres_ref, hat_ref, o_scale_ref, out_gain_ref, out_w, ctx, q_ref, k_ref, v_ref, lse_ref, scale_ref,
        gain_ref, cos_ref, sin_ref, id_col, id_row, last_ref, tops_ref, far_in, grads_in,
        backs, part_ref, gains_out, tops_out, tokens_out,
        hats, seq, qkv_w, seq_do, d_ctx, d_q, d_k, d_v, d_low, whole, terms, row_terms, turned,
        land, land_gain, land_top, own_gain, peer_gain, inners, peer_inners,
        grad_own, grad_land, grad_sum, core_send, core_land, hold, chip_send, chip_land,
        s_ring, r_ring, s_row, r_row, s_in, r_in, s_y, r_y, s_z, r_z, s_core, r_core, s_chip, r_chip, s_gain, r_gain, local,
    ):
        hats_in, seq_in, qkv_in = far_in
        g = Grid()

        def tensor_peer(k, flip):
            core = 1 - g.core_at if flip else g.core_at
            return (g.dp_at, lax.rem(g.chip_at + k + chips, chips) * 2 + core)

        def dp_peer(s, j):
            across = lax.rem(g.outer_at + s + outer, outer) * inner
            return (across + lax.rem(g.inner_at + j + inner, inner), g.tensor_at)

        place = g.path_of(g.dp_at)
        after_dp = (g.index_of(lax.rem(place + 1, n)), g.tensor_at)
        before_dp = (g.index_of(lax.rem(place + n - 1, n)), g.tensor_at)
        near = [tensor_peer(k, f) for k in range(chips) for f in (0, 1) if (k, f) != (0, 0)]
        far = [dp_peer(s, 0) for s in range(1, outer)] + [dp_peer(0, j) for j in range(1, inner)]
        greet(near + far + [after_dp, before_dp])

        def remote(src, dst, send, recv, peer):
            copy = pltpu.make_async_remote_copy(
                src_ref=src, dst_ref=dst, send_sem=send, recv_sem=recv,
                device_id=peer, device_id_type=mesh_id,
            )
            copy.start()
            return copy

        def fetch(src, dst, at):
            copy = pltpu.make_async_copy(src, dst, local.at[at])
            copy.start()
            return copy

        def dot(a, b, contract):
            return lax.dot_general(a, b, (contract, ((), ())), preferred_element_type=f32)

        def looped(total, make):
            lax.fori_loop(0, total, lambda i, c: (make(i), c)[1], 0)

        def rows_of(i, size):
            return pl.ds(pl.multiple_of(i * size, size), size)

        sent = []
        y_copies = {}
        for j in range(1, inner):
            for c in range(3):
                copy = remote(
                    grads_in[j * 3 + c], grad_land.at[j - 1, c], s_y.at[j, c], r_y.at[j, c], dp_peer(0, j)
                )
                y_copies[j, c] = copy
                sent.append(copy)
        own_grads = [fetch(grads_in[c], grad_own.at[c], c) for c in range(3)]
        fetched = [fetch(hats_in, hats, 3), fetch(seq_in, seq, 4), fetch(qkv_in, qkv_w, 5)]
        z_copies = []
        keeps = []

        def unit_sums(c):
            own_grads[c].wait()
            for j in range(1, inner):
                y_copies[j, c].wait_recv()

            def add(i):
                s, at = i // (units // 64), lax.rem(i, units // 64)
                rows = rows_of(at, 64)
                total = grad_own[c, s, rows].astype(f32)
                for j in range(1, inner):
                    total = total + grad_land[j - 1, c, s, rows].astype(f32)
                grad_sum[c, s, rows] = total.astype(bf16)

            looped(outer * (units // 64), add)
            for s in z_steps:
                z_copies.append(
                    remote(grad_sum.at[c, s], backs[c][s], s_z.at[c, s], r_z.at[c, s], dp_peer(s, 0))
                )
            keeps.append(fetch(grad_sum.at[c, 0], backs[c][0], 6 + c))

        t_at = g.tensor_at
        mine = rows_of(t_at, count)

        def open_rows(i, total):
            at = rows_of(i, lines)
            value, hat = dres_ref[at], hat_ref[at]
            upstream = value * out_gain_ref[...]
            mean = jnp.mean(upstream * hat, axis=1, keepdims=True)
            d_attn = (o_scale_ref[at] * (upstream - hat * mean)).astype(bf16)
            seq_do[pl.ds(pl.multiple_of(t_at * count + i * lines, lines), lines)] = d_attn
            return total + jnp.sum(value * hat, axis=0, keepdims=True)

        gain_attn = lax.fori_loop(0, count // lines, open_rows, jnp.zeros((1, width), f32))
        row_terms[...] = jnp.zeros((8, width), f32)
        row_terms[2:3] = gain_attn
        row_terms[3:4] = last_ref[...]
        moves, passed = [], []

        def row_copy(slot, index, peer):
            at = rows_of(index, count)
            copy = remote(seq_do.at[at], seq_do.at[at], s_row.at[slot], r_row.at[slot], peer)
            sent.append(copy)
            return copy

        for k in range(1, chips):
            moves.append(row_copy(k - 1, t_at, tensor_peer(k, 0)))
        to_core = row_copy(chips - 1, t_at, tensor_peer(0, 1))
        for k in range(1, chips):
            moves[k - 1].wait_recv()
            source = lax.rem(g.chip_at - k + chips, chips) * 2 + g.core_at
            passed.append(row_copy(chips - 1 + k, source, tensor_peer(0, 1)))
        to_core.wait_recv()
        for copy in passed:
            copy.wait_recv()

        def context_grad(i):
            at = rows_of(i, tall)
            d_ctx[at] = dot(seq_do[at], out_w[...], ((1,), (1,))).astype(bf16)

        looped(length // tall, context_grad)
        unit_sums(0)

        scale = HEAD ** (-0.5)
        for h in range(heads):
            cols = slice(h * HEAD, (h + 1) * HEAD)

            def head(i, c, cols=cols, h=h):
                at = rows_of(i, tall)
                q_part, ctx_part = q_ref[at, cols], d_ctx[at, cols]
                raw = dot(q_part, k_ref[:, cols], ((1,), (1,))) * scale
                masked = jnp.where(id_row[...] <= id_col[at], raw, masked_value)
                probs = jnp.exp(masked - lse_ref[at, h : h + 1])
                d_probs = dot(ctx_part, v_ref[:, cols], ((1,), (1,)))
                mean = jnp.sum(probs * d_probs, axis=1, keepdims=True)
                d_scores = (probs * (d_probs - mean)).astype(bf16)
                d_q[at, cols] = dot(d_scores, k_ref[:, cols], ((1,), (0,))) * scale
                key = dot(d_scores, q_part, ((0,), (0,))) * scale
                value = dot(probs.astype(bf16), ctx_part, ((0,), (0,)))
                d_k[:, cols] = jnp.where(i == 0, key, d_k[:, cols] + key)
                d_v[:, cols] = jnp.where(i == 0, value, d_v[:, cols] + value)
                return c

            d_k[:, cols] = jnp.zeros((length, HEAD), f32)
            d_v[:, cols] = jnp.zeros((length, HEAD), f32)
            lax.fori_loop(0, length // tall, head, 0)
        if inner > 1 or outer > 1:
            unit_sums(1)
        fetched[0].wait()
        sign = jnp.where(lax.broadcasted_iota(jnp.int32, (tall, HEAD), 1) < HEAD // 2, -1.0, 1.0)

        def unrotate(i, sums):
            at = rows_of(i, tall)
            cosine, sine = cos_ref[at], sin_ref[at]
            lane = lax.broadcasted_iota(jnp.int32, (tall, 128), 1)
            columns = jnp.zeros((tall, 128), f32)
            result = []
            for c, grad in ((0, d_q), (1, d_k)):
                total = jnp.zeros((tall, 1), f32)
                terms_row = []
                for h in range(heads):
                    cols = slice(h * HEAD, (h + 1) * HEAD)
                    value = grad[at, cols]
                    back = value * cosine - pltpu.roll(value * sine, HEAD // 2, 1) * sign
                    hat = hats[c, at, cols]
                    terms_row.append(jnp.sum(back * hat, axis=0, keepdims=True))
                    back = back * gain_ref[c : c + 1, cols]
                    grad[at, cols] = back
                    total = total + jnp.sum(back * hat, axis=1, keepdims=True)
                columns = jnp.where(lane == c, total, columns)
                result.append(sums[c] + jnp.concatenate(terms_row, axis=1))
            inners[:, at] = columns.T[:8]
            return tuple(result)

        zero = jnp.zeros((1, span), f32)
        gain_q, gain_k = lax.fori_loop(0, length // tall, unrotate, (zero, zero))
        offset = rows_of(t_at, span)
        row_terms[0:1, offset] = gain_q
        row_terms[1:2, offset] = gain_k
        in_copies = []
        for k in range(chips):
            for f in (0, 1):
                if (k, f) != (0, 0):
                    at = k * 2 + f - 1
                    in_copies.append(
                        remote(inners, peer_inners.at[at], s_in.at[at], r_in.at[at], tensor_peer(k, f))
                    )
        sent.extend(in_copies)
        turned[...] = ctx[...].T

        def out_grad(i):
            cols = rows_of(i, tile)
            whole[3, :, cols] = dot(turned[...], seq_do[:, cols], ((1,), (0,))).astype(bf16)

        looped(width // tile, out_grad)
        for copy in in_copies:
            copy.wait_recv()

        def normed(i):
            at = rows_of(i, tall)
            sums = inners[:, at]
            for other in range(tensor - 1):
                sums = sums + peer_inners[other, :, at]
            column = jnp.concatenate([sums, jnp.zeros((120, tall), f32)], axis=0).T / width
            for c, grad in ((0, d_q), (1, d_k)):
                value = grad[at] - hats[c, at] * column[:, c : c + 1]
                d_low[c, at] = (scale_ref[at, c : c + 1] * value).astype(bf16)
            d_low[2, at] = d_v[at].astype(bf16)

        looped(length // tall, normed)
        fetched[1].wait()
        for c in range(3):
            turned[...] = d_low[c].T

            def weight_grad(i, c=c):
                cols = rows_of(i, tile)
                whole[c, :, cols] = dot(turned[...], seq[:, cols], ((1,), (0,))).astype(bf16)

            looped(width // tile, weight_grad)

        def place_terms(i, c):
            cols = pl.ds(pl.multiple_of(i * thin, thin), thin)
            terms[i] = row_terms[:, cols]
            return c

        lax.fori_loop(0, n, place_terms, 0)

        def way_of(item):
            return 1 if item >= 8 else 1 - 2 * (item // 4)

        def own(item, away):
            index = g.index_of(lax.rem(place - way_of(item) * away + 2 * n, n))
            if item == gain_item:
                return terms.at[index]
            if item == top_item:
                return tops_ref
            side, c = item // 4, item % 4
            return whole.at[c, pl.ds(side * half, half), rows_of(index, thin)]

        def landed(step, item):
            if item == gain_item:
                return land_gain.at[step]
            if item == top_item:
                return land_top.at[step]
            return land.at[step, item]

        hops = {}

        def hop(step, item):
            hops[step, item] = remote(
                own(item, 1) if step == 0 else landed(step - 1, item),
                landed(step, item),
                s_ring.at[step, item],
                r_ring.at[step, item],
                after_dp if way_of(item) == 1 else before_dp,
            )

        order = [gain_item, top_item] + [c + side * 4 for c in range(4) for side in (0, 1)]
        for item in order:
            hop(0, item)
        unit_sums(2)

        fetched[2].wait()
        chip_order = list(range(1, chips)) + [0]
        core_copies, chip_copies = {}, {}

        def token_rows(k, flip, store):
            chip = lax.rem(g.chip_at + k, chips)
            core = 1 - g.core_at if flip else g.core_at
            at = rows_of(chip * 2 + core, count)

            def columns(i):
                cols = rows_of(i, tile)
                total = dot(d_low[0, at], qkv_w[0, cols], ((1,), (1,)))
                for c in (1, 2):
                    total = total + dot(d_low[c, at], qkv_w[c, cols], ((1,), (1,)))
                store(cols, total)

            looped(width // tile, columns)

        duties = []
        for k in chip_order:

            def away(k=k):
                def store(cols, value):
                    core_send[k, :, cols] = value.astype(bf16)

                token_rows(k, True, store)
                core_copies[k] = remote(
                    core_send.at[k], core_land.at[k], s_core.at[k], r_core.at[k], tensor_peer(0, 1)
                )

            def here(k=k):
                def store(cols, value):
                    hold[k, :, cols] = value

                token_rows(k, False, store)

            def join(k=k):
                core_copies[k].wait_recv()

                def add(i):
                    at = rows_of(i, lines)
                    chip_send[k - 1, at] = (hold[k, at] + core_land[k, at].astype(f32)).astype(bf16)

                looped(count // lines, add)
                chip_copies[k] = remote(
                    chip_send.at[k - 1], chip_land.at[k - 1], s_chip.at[k], r_chip.at[k], tensor_peer(k, 0)
                )

            duties += [away, here] + ([join] if k else [])

        def close_tokens():
            core_copies[0].wait_recv()
            for k in range(1, chips):
                chip_copies[k].wait_recv()

            def close(i):
                at = rows_of(i, lines)
                total = dres_ref[at] + hold[0, at] + core_land[0, at].astype(f32)
                for k in range(1, chips):
                    total = total + chip_land[k - 1, at].astype(f32)
                tokens_out[at] = total

            looped(count // lines, close)

        duties.append(close_tokens)
        per_step = -(-len(duties) // (n - 2))
        for step in range(1, n):
            for item in order:
                hops[step - 1, item].wait_recv()
                here = landed(step - 1, item)
                if item == top_item:
                    summed = jnp.maximum(here[...], tops_ref[...])
                else:
                    summed = here[...].astype(f32) + own(item, step + 1)[...].astype(f32)
                if step < n - 1:
                    here[...] = summed.astype(here.dtype)
                    hop(step, item)
                elif item == gain_item:
                    own_gain[0] = summed
                elif item == top_item:
                    tops_out[...] = summed
                else:
                    side, c = item // 4, item % 4
                    part_ref[c, pl.ds(side * half, half)] = summed
            for _ in range(per_step):
                if duties:
                    duties.pop(0)()
        peers = [tensor_peer(0, 1)] + [tensor_peer(k, 0) for k in range(1, chips)]
        first = remote(own_gain.at[0], peer_gain.at[0], s_gain.at[0], r_gain.at[0], peers[0])
        first.wait_recv()
        own_gain[1] = own_gain[0] + peer_gain[0]
        others = [
            remote(own_gain.at[1], peer_gain.at[k], s_gain.at[k], r_gain.at[k], peers[k])
            for k in range(1, chips)
        ]
        result = own_gain[1]
        for k in range(1, chips):
            others[k - 1].wait_recv()
            result = result + peer_gain[k]
        gains_out[...] = result
        for copy in z_copies:
            copy.wait()
        for copy in keeps:
            copy.wait()
        for copy in sent + list(hops.values()) + list(core_copies.values()):
            copy.wait_send()
        for copy in list(chip_copies.values()) + [first] + others:
            copy.wait_send()

    shape = jax.ShapeDtypeStruct
    anywhere = pl.BlockSpec(memory_space=pl.ANY)
    vmem = pl.BlockSpec(memory_space=pltpu.VMEM)
    sems = pltpu.SemaphoreType.DMA
    results = pl.pallas_call(
        kernel,
        out_shape=(shape((units, slab), bf16),) * (3 * outer)
        + (
            shape((4, span, thin), f32),
            shape((8, thin), f32),
            shape(tops.shape, f32),
            shape((count, width), f32),
        ),
        in_specs=[vmem] * 18 + [anywhere] * 3 + [anywhere] * some,
        out_specs=(anywhere,) * (3 * outer) + (vmem,) * 4,
        scratch_shapes=[
            pltpu.VMEM(hats.shape, f32),
            pltpu.VMEM(seq.shape, bf16),
            pltpu.VMEM(full_qkv.shape, bf16),
            pltpu.VMEM((length, width), bf16),
            pltpu.VMEM((length, span), bf16),
            pltpu.VMEM((length, span), f32),
            pltpu.VMEM((length, span), f32),
            pltpu.VMEM((length, span), f32),
            pltpu.VMEM((3, length, span), bf16),
            pltpu.VMEM((4, span, width), bf16),
            pltpu.VMEM((n, 8, thin), f32),
            pltpu.VMEM((8, width), f32),
            pltpu.VMEM((span, length), bf16),
            pltpu.VMEM((n - 1, 8, half, thin), bf16),
            pltpu.VMEM((n - 1, 8, thin), f32),
            pltpu.VMEM((n - 1,) + tops.shape, f32),
            pltpu.VMEM((2, 8, thin), f32),
            pltpu.VMEM((chips, 8, thin), f32),
            pltpu.VMEM((8, length), f32),
            pltpu.VMEM((tensor - 1, 8, length), f32),
            pltpu.VMEM((3, outer, units, slab), bf16),
            pltpu.VMEM((max(inner - 1, 1), 3, outer, units, slab), bf16),
            pltpu.VMEM((3, outer, units, slab), bf16),
            pltpu.VMEM((chips, count, width), bf16),
            pltpu.VMEM((chips, count, width), bf16),
            pltpu.VMEM((chips, count, width), f32),
            pltpu.VMEM((max(chips - 1, 1), count, width), bf16),
            pltpu.VMEM((max(chips - 1, 1), count, width), bf16),
            sems((n - 1, ring)),
            sems((n - 1, ring)),
            sems((2 * chips - 1,)),
            sems((2 * chips - 1,)),
            sems((tensor - 1,)),
            sems((tensor - 1,)),
            sems((inner, 3)),
            sems((inner, 3)),
            sems((3, outer)),
            sems((3, outer)),
            sems((chips,)),
            sems((chips,)),
            sems((chips,)),
            sems((chips,)),
            sems((chips,)),
            sems((chips,)),
            sems((9,)),
        ],
        compiler_params=pltpu.CompilerParams(
            collective_id=1, has_side_effects=True, vmem_limit_bytes=62 * 2**20
        ),
    )(
        d_resid, attn_hat, o_scale, out_gain, full_out, context, q_low, k_low, v_low, lse, scales,
        head_gains, tables[0], tables[1], blocks[:, None], blocks[None, :], gain_last, tops,
        hats, seq, full_qkv, *flat_grads,
    )
    backs = [results[c * outer : (c + 1) * outer] for c in range(3)]
    return backs, results[3 * outer :]


def attend_call(seq, full_qkv, full_out, head_gains, out_gain, tables, blocks, rows, shard):
    grid = Grid()
    outer, inner, chips, tensor = grid.outer, grid.inner, grid.chips, grid.tensor
    length, width = seq.shape
    span = full_qkv.shape[2]
    heads = span // HEAD
    count = rows.shape[0]
    slab = shard.shape[1]
    units = shard.shape[2] // outer
    parts = outer * inner
    steps = sorted(range(1, outer), key=lambda s: (min(s, outer - s), s))
    tall = min(256, length)
    tile = 512
    lines = 32
    bf16, f32 = jnp.bfloat16, jnp.float32
    mesh_id = pl.DeviceIdType.MESH

    def kernel(
        seq_ref, qkv_ref, out_w_ref, gains_ref, out_gain_ref, cos_ref, sin_ref, id_col, id_row, rows_ref, shard_ref,
        *refs
    ):
        pieces = [refs[j * outer : (j + 1) * outer] for j in range(inner)]
        body(
            seq_ref, qkv_ref, out_w_ref, gains_ref, out_gain_ref, cos_ref, sin_ref, id_col, id_row, rows_ref, shard_ref,
            pieces, *refs[parts:],
        )

    def body(
        seq_ref, qkv_ref, out_w_ref, gains_ref, out_gain_ref, cos_ref, sin_ref, id_col, id_row, rows_ref, shard_ref,
        pieces, hat_ref, scale_ref, q_low, k_low, v_low, lse_ref, context, attn_hat, o_scale, resid, resid_low, top_ref,
        square, squares, core_send, core_land, hold, chip_send, chip_land,
        s_z, r_z, s_y, r_y, s_sq, r_sq, s_core, r_core, s_chip, r_chip, local,
    ):
        g = Grid()

        def tensor_peer(k, flip):
            core = 1 - g.core_at if flip else g.core_at
            return (g.dp_at, lax.rem(g.chip_at + k + chips, chips) * 2 + core)

        def dp_peer(s, j):
            across = lax.rem(g.outer_at + s + outer, outer) * inner
            return (across + lax.rem(g.inner_at + j + inner, inner), g.tensor_at)

        near = [tensor_peer(k, f) for k in range(chips) for f in (0, 1) if (k, f) != (0, 0)]
        far = [dp_peer(s, 0) for s in range(1, outer)]
        far += [dp_peer(0, j) for j in sorted({1 % inner, inner - 1} - {0})]
        greet(near + far)

        def remote(src, dst, send, recv, peer):
            copy = pltpu.make_async_remote_copy(
                src_ref=src, dst_ref=dst, send_sem=send, recv_sem=recv,
                device_id=peer, device_id_type=mesh_id,
            )
            copy.start()
            return copy

        def dot(a, b, contract):
            return lax.dot_general(a, b, (contract, ((), ())), preferred_element_type=f32)

        def looped(total, make):
            lax.fori_loop(0, total, lambda i, c: (make(i), c)[1], 0)

        def rows_of(i, size):
            return pl.ds(pl.multiple_of(i * size, size), size)

        def cut(s):
            at = lax.rem(g.outer_at + s, outer)
            return shard_ref.at[:, :, rows_of(at, units)]

        z_copies = {
            s: remote(cut(s), pieces[0][s], s_z.at[s], r_z.at[s], dp_peer(s, 0)) for s in steps
        }
        own = pltpu.make_async_copy(cut(0), pieces[0][0], local)
        own.start()
        y_copies = {}

        def pass_on(j, s):
            src = cut(0) if (j, s) == (1, 0) else pieces[j - 1][s]
            y_copies[j, s] = remote(src, pieces[j][s], s_y.at[j, s], r_y.at[j, s], dp_peer(0, 1))

        if inner > 1:
            pass_on(1, 0)
        duties = []
        for s in steps:

            def duty(s=s):
                z_copies[s].wait_recv()
                if inner > 1:
                    pass_on(1, s)

            duties.append(duty)
        for j in range(2, inner):
            for s in [0] + steps:

                def duty(j=j, s=s):
                    y_copies[j - 1, s].wait_recv()
                    pass_on(j, s)

                duties.append(duty)

        def next_duty():
            if duties:
                duties.pop(0)()

        def project(i):
            at = rows_of(i, tall)
            x = seq_ref[at]
            lane = lax.broadcasted_iota(jnp.int32, (tall, 128), 1)
            sums = jnp.zeros((tall, 128), f32)
            for c in range(2):
                value = dot(x, qkv_ref[c], ((1,), (0,)))
                hat_ref[c, at] = value
                sums = jnp.where(lane == c, jnp.sum(value * value, axis=1, keepdims=True), sums)
            v_low[at] = dot(x, qkv_ref[2], ((1,), (0,))).astype(bf16)
            square[:, at] = sums.T[:8]

        looped(length // tall, project)
        sq_copies = []
        for k in range(chips):
            for f in (0, 1):
                if (k, f) != (0, 0):
                    at = k * 2 + f - 1
                    sq_copies.append(
                        remote(square, squares.at[at], s_sq.at[at], r_sq.at[at], tensor_peer(k, f))
                    )
        for copy in sq_copies:
            copy.wait_recv()
        sign = jnp.where(lax.broadcasted_iota(jnp.int32, (tall, HEAD), 1) < HEAD // 2, -1.0, 1.0)

        def rotate(i):
            at = rows_of(i, tall)
            sums = square[:, at]
            for copy_at in range(tensor - 1):
                sums = sums + squares[copy_at, :, at]
            column = jnp.concatenate([sums, jnp.zeros((120, tall), f32)], axis=0).T
            scales = lax.rsqrt(column / width + norm_eps)
            scale_ref[at] = scales
            cosine, sine = cos_ref[at], sin_ref[at] * sign
            for c, low in ((0, q_low), (1, k_low)):
                hat = hat_ref[c, at] * scales[:, c : c + 1]
                hat_ref[c, at] = hat
                normed = hat * gains_ref[c : c + 1]
                for h in range(heads):
                    cols = slice(h * HEAD, (h + 1) * HEAD)
                    value = normed[:, cols]
                    turned = pltpu.roll(value, HEAD // 2, 1)
                    low[at, cols] = (value * cosine + turned * sine).astype(bf16)

        looped(length // tall, rotate)
        scale = HEAD ** (-0.5)
        top_ref[...] = jnp.full((8, 128), masked_value, f32)
        for h in range(heads):
            cols = slice(h * HEAD, (h + 1) * HEAD)

            def attend(i, best, cols=cols, h=h):
                at = rows_of(i, tall)
                raw = dot(q_low[at, cols], k_low[:, cols], ((1,), (1,))) * scale
                masked = jnp.where(id_row[...] <= id_col[at], raw, masked_value)
                top = jnp.max(masked, axis=1, keepdims=True)
                weight = jnp.exp(masked - top)
                total = jnp.sum(weight, axis=1, keepdims=True)
                probs = (weight / total).astype(bf16)
                context[at, cols] = dot(probs, v_low[:, cols], ((1,), (0,))).astype(bf16)
                lse_ref[at, h : h + 1] = top + jnp.log(total)
                return jnp.maximum(best, jnp.max(top, axis=0, keepdims=True))

            best = lax.fori_loop(
                0, length // tall, attend, jnp.full((1, 1), masked_value, f32)
            )
            top_ref[h : h + 1] = jnp.broadcast_to(best, (1, 128))
        next_duty()

        def out_rows(k, flip, store):
            chip = lax.rem(g.chip_at + k, chips)
            core = 1 - g.core_at if flip else g.core_at
            at = rows_of(chip * 2 + core, count)

            def columns(i):
                cols = rows_of(i, tile)
                store(cols, dot(context[at], out_w_ref[:, cols], ((1,), (0,))))

            looped(width // tile, columns)

        chip_order = list(range(1, chips)) + [0]
        core_copies, chip_copies = {}, {}
        for k in chip_order:

            def store(cols, value, k=k):
                core_send[k, :, cols] = value.astype(bf16)

            out_rows(k, True, store)
            core_copies[k] = remote(
                core_send.at[k], core_land.at[k], s_core.at[k], r_core.at[k], tensor_peer(0, 1)
            )
        for k in chip_order:

            def store(cols, value, k=k):
                hold[k, :, cols] = value

            out_rows(k, False, store)
            if k:
                core_copies[k].wait_recv()

                def add(i, k=k):
                    at = rows_of(i, lines)
                    chip_send[k - 1, at] = (hold[k, at] + core_land[k, at].astype(f32)).astype(bf16)

                looped(count // lines, add)
                chip_copies[k] = remote(
                    chip_send.at[k - 1], chip_land.at[k - 1], s_chip.at[k], r_chip.at[k], tensor_peer(k, 0)
                )
        next_duty()
        core_copies[0].wait_recv()
        for k in range(1, chips):
            chip_copies[k].wait_recv()

        def close(i):
            at = rows_of(i, lines)
            raw = hold[0, at] + core_land[0, at].astype(f32)
            for k in range(1, chips):
                raw = raw + chip_land[k - 1, at].astype(f32)
            scale_o = lax.rsqrt(jnp.mean(raw * raw, axis=1, keepdims=True) + norm_eps)
            hat = raw * scale_o
            attn_hat[at] = hat
            o_scale[at] = scale_o
            value = rows_ref[at].astype(f32) + hat * out_gain_ref[...]
            resid[at] = value
            resid_low[at] = value.astype(bf16)

        looped(count // lines, close)
        while duties:
            next_duty()
        own.wait()
        for key, copy in y_copies.items():
            if key[0] == inner - 1:
                copy.wait_recv()
        sent = list(z_copies.values()) + list(y_copies.values()) + sq_copies
        for copy in sent + list(core_copies.values()) + list(chip_copies.values()):
            copy.wait_send()

    shape = jax.ShapeDtypeStruct
    anywhere = pl.BlockSpec(memory_space=pl.ANY)
    vmem = pl.BlockSpec(memory_space=pltpu.VMEM)
    sems = pltpu.SemaphoreType.DMA
    results = pl.pallas_call(
        kernel,
        out_shape=(shape((3, slab, units), bf16),) * parts
        + (
            shape((2, length, span), f32),
            shape((length, 128), f32),
            shape((length, span), bf16),
            shape((length, span), bf16),
            shape((length, span), bf16),
            shape((length, heads), f32),
            shape((length, span), bf16),
            shape((count, width), f32),
            shape((count, 1), f32),
            shape((count, width), f32),
            shape((count, width), bf16),
            shape((8, 128), f32),
        ),
        in_specs=[vmem] * 10 + [anywhere],
        out_specs=(anywhere,) * parts + (vmem,) * 12,
        scratch_shapes=[
            pltpu.VMEM((8, length), f32),
            pltpu.VMEM((tensor - 1, 8, length), f32),
            pltpu.VMEM((chips, count, width), bf16),
            pltpu.VMEM((chips, count, width), bf16),
            pltpu.VMEM((chips, count, width), f32),
            pltpu.VMEM((max(chips - 1, 1), count, width), bf16),
            pltpu.VMEM((max(chips - 1, 1), count, width), bf16),
            sems((outer,)),
            sems((outer,)),
            sems((inner, outer)),
            sems((inner, outer)),
            sems((tensor - 1,)),
            sems((tensor - 1,)),
            sems((chips,)),
            sems((chips,)),
            sems((chips,)),
            sems((chips,)),
            sems(()),
        ],
        compiler_params=pltpu.CompilerParams(
            collective_id=3, has_side_effects=True, vmem_limit_bytes=56 * 2**20
        ),
    )(
        seq, full_qkv, full_out, head_gains, out_gain, tables[0], tables[1],
        blocks[:, None], blocks[None, :], rows, shard,
    )
    pieces = [results[j * outer : (j + 1) * outer] for j in range(inner)]
    return pieces, results[parts:]


def unit_kernel_call(rows_low, resid, cotangent, gain, pieces):
    grid = Grid()
    outer, chips, inner = grid.outer, grid.chips, grid.inner
    total_rows, width = rows_low.shape
    units = pieces[0][0].shape[2]
    slab = pieces[0][0].shape[1]
    flat_pieces = [piece for row in pieces for piece in row]
    parts = len(flat_pieces)
    halves = 2
    count = total_rows // halves
    both = 2 * count
    per = min(2, chips)
    groups = chips // per
    blocks = outer * groups
    tall = per * both
    held = per if groups > 1 else max(per - 1, 1)
    links = outer * (chips - 1)
    steps = [0] + sorted(range(1, outer), key=lambda s: (min(s, outer - s), s))
    order = [(s, i) for s in steps for i in range(groups)]
    tile = 512
    wide_tiles = width // tile
    unit_tile = min(256, units)
    lines = 32
    bf16, f32 = jnp.bfloat16, jnp.float32
    mesh_id = pl.DeviceIdType.MESH

    def plan():
        chip_us, core_us, outer_us, hop_us = 5.3, 0.6, 7.0, 2.0
        free = {"x": 0.0, "core": 0.0, "z": 0.0}
        arrive, done, tasks = {}, {}, {}

        def send(link, when, us):
            free[link] = max(free[link], when) + us
            return free[link] + hop_us

        def add(name, needs, us, after=None):
            tasks[name] = (needs, us, after)

        def go(p, h):
            def then(now):
                for s in steps[1:]:
                    arrive["z", p, h, s] = send("z", now, outer_us)
                for k in range(1, chips):
                    arrive["x", p, h, 0, k] = send("x", now, chip_us)
                arrive["c", p, h, 0, 0] = send("core", now, core_us)

            return then

        def zf(p, h, s):
            def then(now):
                for k in range(1, chips):
                    arrive["x", p, h, s, k] = send("x", now, chip_us)
                arrive["c", p, h, s, 0] = send("core", now, core_us)

            return then

        def xf(p, h, s, k):
            def then(now):
                arrive["c", p, h, s, k] = send("core", now, core_us)

            return then

        def compute(p, h, s, i):
            def then(now):
                arrive["cr", p, h, s, i] = send("core", now, per * core_us)

            return then

        def cr(p, h, s, i):
            def then(now):
                for k in range(i * per, i * per + per):
                    if k:
                        arrive["xr", p, h, s, k] = send("x", now, chip_us)

            return then

        def xr(p, h, s):
            def then(now):
                if s:
                    arrive["zr", p, h, s] = send("z", now, outer_us)

            return then

        for p in (0, 1):
            for h in range(halves):
                if p == 0:
                    needs = [("do", ("go", 0, h - 1))] if h else []
                else:
                    needs = [("do", ("between", h))]
                add(("go", p, h), needs, 0.2, go(p, h))
                for s in steps[1:]:
                    add(("zf", p, h, s), [("at", ("z", p, h, s))], 0.2, zf(p, h, s))
                for s in steps:
                    for k in range(1, chips):
                        add(("xf", p, h, s, k), [("at", ("x", p, h, s, k))], 0.2, xf(p, h, s, k))
                for n, (s, i) in enumerate(order):
                    needs = [("at", ("c", p, h, s, i * per + j)) for j in range(per)]
                    if n:
                        needs.append(("do", ("compute", p, h) + order[n - 1]))
                    add(("load", p, h, s, i), needs, 0.2)
                    needs = [("do", ("load", p, h, s, i))]
                    if n:
                        needs.append(("do", ("cr", p, h) + order[n - 1]))
                    add(("compute", p, h, s, i), needs, 3.2, compute(p, h, s, i))
                    needs = [("at", ("cr", p, h, s, i)), ("do", ("compute", p, h, s, i))]
                    add(("cr", p, h, s, i), needs, 0.5, cr(p, h, s, i))
                for s in steps:
                    needs = [("do", ("cr", p, h, s, 0))]
                    needs += [("at", ("xr", p, h, s, k)) for k in range(1, chips)]
                    add(("xr", p, h, s), needs, 0.4, xr(p, h, s))
                for s in steps[1:]:
                    needs = [("at", ("zr", p, h, s)), ("do", ("xr", p, h, 0))]
                    add(("zr", p, h, s), needs, 0.4)
        for h in range(halves):
            needs = [("do", ("zr", 0, h, s)) for s in steps[1:]] + [("do", ("xr", 0, h, 0))]
            add(("between", h), needs, 1.0)
        for n, (s, i) in enumerate(order):
            needs = [("do", ("compute", 1, h, s, i)) for h in range(halves)]
            if n:
                needs.append(("do", ("grads",) + order[n - 1]))
            add(("fetch", s, i), needs, 0.2)
            add(("grads", s, i), [("do", ("fetch", s, i))], 7.0)
        add(("write",), [("do", ("grads",) + order[-1])], 4.0)
        rank = {"compute": 1, "fetch": 2, "grads": 2, "write": 3}
        result = []
        now = 0.0
        while tasks:
            best = None
            for name, (needs, us, then) in tasks.items():
                ready = 0.0
                for kind, key in needs:
                    table = arrive if kind == "at" else done
                    if key not in table:
                        ready = None
                        break
                    ready = max(ready, table[key] + (1.0 if key[0] in ("load", "fetch") else 0.0))
                if ready is None:
                    continue
                key = (max(ready, now), rank.get(name[0], 0))
                if best is None or key < best[0]:
                    best = (key, name)
            (ready, _), name = best
            needs, us, then = tasks.pop(name)
            now = ready + us
            done[name] = now
            if then is not None:
                then(now)
            result.append(name)
        return result

    def kernel(*refs):
        piece_refs = refs[:parts]
        fixed = refs[parts : parts + 9]
        grad_refs = refs[parts + 9 : parts + 9 + 3 * inner]
        body(piece_refs, *fixed, grad_refs, *refs[parts + 9 + 3 * inner :])

    def body(
        piece_refs, rows_ref, resid_ref, cot_ref, gain_ref,
        out_ref, dres_ref, gain_out, all_x, all_dm, grad_refs,
        wg, wu, wd, buf, wide_buf, act, coef_gate, coef_up, d_gate, d_up, turned, acc_gate, acc_up, acc_down, stage,
        core_send, core_land, hold, keep, chip_send, chip_land, outer_send, outer_land, raw, d_mlp,
        s_outer, r_outer, s_chip, r_chip, s_core, r_core,
        s_core_sum, r_core_sum, s_chip_sum, r_chip_sum, s_outer_sum, r_outer_sum,
        local, local_own, local_wide, local_w, local_g,
    ):
        g = Grid()
        core_peer = (g.dp_at, g.chip_at * 2 + 1 - g.core_at)

        def chip_peer(k):
            return (g.dp_at, lax.rem(g.chip_at + k + chips, chips) * 2 + g.core_at)

        def outer_peer(s):
            return (lax.rem(g.outer_at + s + outer, outer) * g.inner + g.inner_at, g.tensor_at)

        greet(
            [core_peer]
            + [chip_peer(k) for k in range(1, chips)]
            + [outer_peer(s) for s in range(1, outer)]
        )

        def remote(src, dst, send, recv, peer):
            copy = pltpu.make_async_remote_copy(
                src_ref=src, dst_ref=dst, send_sem=send, recv_sem=recv,
                device_id=peer, device_id_type=mesh_id,
            )
            copy.start()
            return copy

        def fetch(src, dst, sem):
            copy = pltpu.make_async_copy(src, dst, sem)
            copy.start()
            return copy

        def dot(a, b, contract):
            return lax.dot_general(a, b, (contract, ((), ())), preferred_element_type=f32)

        def looped(total, make):
            lax.fori_loop(0, total, lambda i, c: (make(i), c)[1], 0)

        def by_lines(make):
            looped(count // lines, lambda i: make(pl.ds(pl.multiple_of(i * lines, lines), lines)))

        def by_tiles(make):
            looped(wide_tiles, lambda i: make(pl.ds(pl.multiple_of(i * tile, tile), tile)))

        weights = (wg, wu, wd)
        fetches = []

        def fetch_weights():
            for j in range(inner):
                for s in range(outer):
                    index = lax.rem(g.outer_at - s + outer, outer) * inner
                    index = index + lax.rem(g.inner_at - j + inner, inner)
                    span = pl.ds(pl.multiple_of(index * slab, slab), slab)
                    for c in range(3):
                        at = j * outer + s
                        fetches.append(
                            fetch(piece_refs[at].at[c], weights[c].at[span], local_w.at[at, c])
                        )

        mine, theirs = pl.ds(0, count), pl.ds(count, count)
        every = (all_x, all_dm)
        copies, sums, loads, own = {}, {}, {}, {}
        unsent = {(p, h): [] for p in (0, 1) for h in range(halves)}

        def track(p, h, copy):
            unsent[p, h].append(copy)
            return copy

        def core_copy(p, h, s, k, src):
            dst = every[p].at[h, s, k, theirs]
            copies["c", p, h, s, k] = track(
                p, h, remote(src, dst, s_core.at[p, h, s, k], r_core.at[p, h, s, k], core_peer)
            )

        def chip_copy(p, h, s, k, src):
            dst = every[p].at[h, s, k, mine]
            copies["x", p, h, s, k] = track(
                p, h, remote(src, dst, s_chip.at[p, h, s, k], r_chip.at[p, h, s, k], chip_peer(k))
            )

        def go(p, h):
            source = (rows_ref, d_mlp)[p].at[pl.ds(h * count, count)]
            for s in steps[1:]:
                dst = every[p].at[h, s, 0, mine]
                copies["z", p, h, s] = track(
                    p, h, remote(source, dst, s_outer.at[p, h, s], r_outer.at[p, h, s], outer_peer(s))
                )
            for k in range(1, chips):
                chip_copy(p, h, 0, k, source)
            core_copy(p, h, 0, 0, source)
            own[p, h] = fetch(source, every[p].at[h, 0, 0, mine], local_own.at[p, h])
            if p == 0 and h == 0:
                fetch_weights()

        def part_out(h, s, i, cols, part_sum):
            for j in range(per):
                own_rows = part_sum[j * both : j * both + count]
                if i * per + j == 0:
                    keep[h, s, :, cols] = own_rows
                else:
                    hold[h, min(j, held - 1), :, cols] = own_rows
                core_send[h, j, :, cols] = part_sum[j * both + count : (j + 1) * both].astype(bf16)

        def forward(h, unit, s, i):
            for j in range(units // unit_tile):
                cols = pl.ds(j * unit_tile, unit_tile)
                rows = buf[h].reshape(tall, width)
                gate = dot(rows, wg[:, cols], ((1,), (0,)))
                up = dot(rows, wu[:, cols], ((1,), (0,)))
                sigma = jax.nn.sigmoid(gate)
                silu = gate * sigma
                act[unit, h, :, cols] = (silu * up).astype(bf16)
                coef_up[unit, h, :, cols] = silu.astype(bf16)
                coef_gate[unit, h, :, cols] = (
                    up * sigma * (1.0 + gate * (1.0 - sigma))
                ).astype(bf16)
            by_tiles(
                lambda cols: part_out(h, s, i, cols, dot(act[unit, h], wd[cols, :], ((1,), (1,))))
            )

        def backward(h, unit, s, i):
            for j in range(units // unit_tile):
                cols = pl.ds(j * unit_tile, unit_tile)
                d_act = dot(buf[h].reshape(tall, width), wd[:, cols], ((1,), (0,)))
                d_gate[unit, h, :, cols] = (d_act * coef_gate[unit, h, :, cols].astype(f32)).astype(bf16)
                d_up[unit, h, :, cols] = (d_act * coef_up[unit, h, :, cols].astype(f32)).astype(bf16)

            def into(cols):
                part_sum = dot(d_gate[unit, h], wg[cols, :], ((1,), (1,)))
                part_sum = part_sum + dot(d_up[unit, h], wu[cols, :], ((1,), (1,)))
                part_out(h, s, i, cols, part_sum)

            by_tiles(into)

        def weight_grads(unit):
            first = unit == order[0][0] * groups + order[0][1]
            for left, right, acc in ((d_gate, 0, acc_gate), (d_up, 0, acc_up), (act, 1, acc_down)):
                turned[...] = left[unit].reshape(halves * tall, units).T

                def grads(cols, right=right, acc=acc):
                    rows = wide_buf[right, :, :, :, cols].reshape(halves * tall, tile)
                    value = dot(turned[...], rows, ((1,), (0,)))
                    acc[:, cols] = value if first else acc[:, cols] + value

                by_tiles(grads)

        def between(h):
            def lines_of(i, total):
                at_rows = pl.ds(pl.multiple_of(h * count + i * lines, lines), lines)
                value = raw[at_rows]
                scale = lax.rsqrt(jnp.mean(value * value, axis=1, keepdims=True) + norm_eps)
                hat = value * scale
                gain_row = gain_ref[...]
                out_ref[at_rows] = (resid_ref[at_rows] + hat * gain_row).astype(bf16)
                top = cot_ref[at_rows].astype(f32)
                upstream = top * gain_row
                mean = jnp.mean(upstream * hat, axis=1, keepdims=True)
                d_mlp[at_rows] = (scale * (upstream - hat * mean)).astype(bf16)
                return total + jnp.sum(top * hat, axis=0, keepdims=True)

            zero = jnp.zeros((1, width), f32)
            total = lax.fori_loop(0, count // lines, lines_of, zero)
            gain_out[...] = total if h == 0 else gain_out[...] + total

        def write_grads():
            batches = []
            for j in range(inner):
                for s in range(outer):
                    index = lax.rem(g.outer_at + s, outer) * inner
                    index = index + lax.rem(g.inner_at + j, inner)
                    span = pl.ds(pl.multiple_of(index * slab, slab), slab)
                    slot = len(batches) % 2
                    if len(batches) >= 2:
                        for copy in batches[-2]:
                            copy.wait()
                    batch = []
                    for c, acc in enumerate((acc_gate, acc_up, acc_down)):
                        stage[slot, c] = acc[:, span].astype(bf16)
                        batch.append(
                            fetch(stage.at[slot, c], grad_refs[j * 3 + c].at[s], local_g.at[slot, c])
                        )
                    batches.append(batch)
            for batch in batches[-2:]:
                for copy in batch:
                    copy.wait()

        def core_sum(p, h, s, i):
            unit = s * groups + i
            sums["c", p, h, unit].wait_recv()
            for j in range(per):
                chip = i * per + j
                if chip == 0:

                    def add(at_rows):
                        keep[h, s, at_rows] = keep[h, s, at_rows] + core_land[h, unit, j, at_rows].astype(f32)

                    by_lines(add)
                    continue
                there = s * (chips - 1) + chip - 1

                def add(at_rows):
                    total = hold[h, min(j, held - 1), at_rows] + core_land[h, unit, j, at_rows].astype(f32)
                    chip_send[h, there, at_rows] = total.astype(bf16)

                by_lines(add)
                sums["x", p, h, s, chip] = track(
                    p, h,
                    remote(
                        chip_send.at[h, there], chip_land.at[h, there],
                        s_chip_sum.at[p, h, there], r_chip_sum.at[p, h, there], chip_peer(-chip),
                    ),
                )

        def chip_sum(p, h, s):
            for k in range(1, chips):
                sums["x", p, h, s, k].wait_recv()

            def add(at_rows):
                total = keep[h, s, at_rows]
                for k in range(1, chips):
                    total = total + chip_land[h, s * (chips - 1) + k - 1, at_rows].astype(f32)
                if s == 0:
                    raw[pl.ds(pl.multiple_of(h * count + at_rows.start, lines), lines)] = total
                else:
                    outer_send[h, s - 1, at_rows] = total.astype(bf16)

            by_lines(add)
            if s:
                sums["z", p, h, s] = track(
                    p, h,
                    remote(
                        outer_send.at[h, s - 1], outer_land.at[h, s - 1],
                        s_outer_sum.at[p, h, s], r_outer_sum.at[p, h, s], outer_peer(-s),
                    ),
                )

        def outer_sum(p, h, s):
            sums["z", p, h, s].wait_recv()

            def add(at_rows):
                there = pl.ds(pl.multiple_of(h * count + at_rows.start, lines), lines)
                raw[there] = raw[there] + outer_land[h, s - 1, at_rows].astype(f32)

            by_lines(add)

        def all_sent(p, h):
            for copy in unsent[p, h]:
                copy.wait_send()

        last_core = {}
        for task in plan():
            name, args = task[0], task[1:]
            if name == "go":
                go(*args)
            elif name == "zf":
                p, h, s = args
                copies["z", p, h, s].wait_recv()
                source = every[p].at[h, s, 0, mine]
                for k in range(1, chips):
                    chip_copy(p, h, s, k, source)
                core_copy(p, h, s, 0, source)
            elif name == "xf":
                p, h, s, k = args
                copies["x", p, h, s, k].wait_recv()
                core_copy(p, h, s, k, every[p].at[h, s, k, mine])
            elif name == "load":
                p, h, s, i = args
                for j in range(per):
                    copies["c", p, h, s, i * per + j].wait_recv()
                if (s, i) == order[0]:
                    own[p, h].wait()
                src = every[p].at[h, s, pl.ds(i * per, per)]
                loads[args] = fetch(src, buf.at[h], local.at[p, h, s * groups + i])
            elif name == "compute":
                p, h, s, i = args
                unit = s * groups + i
                if p == 0 and not loads.get("weights"):
                    loads["weights"] = True
                    for copy in fetches:
                        copy.wait()
                loads[args].wait()
                if h in last_core:
                    last_core[h].wait_send()
                (forward, backward)[p](h, unit, s, i)
                last_core[h] = remote(
                    core_send.at[h], core_land.at[h, unit],
                    s_core_sum.at[p, h, unit], r_core_sum.at[p, h, unit], core_peer,
                )
                sums["c", p, h, unit] = last_core[h]
            elif name == "cr":
                core_sum(*args)
            elif name == "xr":
                chip_sum(*args)
            elif name == "zr":
                outer_sum(*args)
            elif name == "between":
                all_sent(0, args[0])
                between(args[0])
            elif name == "fetch":
                s, i = args
                loads[task] = []
                for at, src in enumerate((all_x, all_dm)):
                    for h in range(halves):
                        loads[task].append(
                            fetch(
                                src.at[h, s, pl.ds(i * per, per)],
                                wide_buf.at[at, h],
                                local_wide.at[s * groups + i, at * halves + h],
                            )
                        )
            elif name == "grads":
                for copy in loads[("fetch",) + args]:
                    copy.wait()
                weight_grads(args[0] * groups + args[1])
            elif name == "write":
                write_grads()

        looped(
            total_rows // lines,
            lambda i: close_rows(pl.ds(pl.multiple_of(i * lines, lines), lines), dres_ref, raw, cot_ref),
        )
        for h in range(halves):
            all_sent(1, h)
            last_core[h].wait_send()

    shape = jax.ShapeDtypeStruct
    anywhere = pl.BlockSpec(memory_space=pl.ANY)
    near = pl.BlockSpec(memory_space=pltpu.VMEM)
    sems = pltpu.SemaphoreType.DMA
    flops = 2 * 9 * halves * tall * blocks * width * units
    results = pl.pallas_call(
        kernel,
        out_shape=(
            shape((total_rows, width), bf16),
            shape((total_rows, width), f32),
            shape((1, width), f32),
            shape((halves, outer, chips, both, width), bf16),
            shape((halves, outer, chips, both, width), bf16),
        )
        + (shape((outer, units, slab), bf16),) * (3 * inner),
        in_specs=[anywhere] * (parts + 1) + [near] * 3,
        out_specs=(near, near, near) + (anywhere,) * (2 + 3 * inner),
        scratch_shapes=[
            pltpu.VMEM((width, units), bf16),
            pltpu.VMEM((width, units), bf16),
            pltpu.VMEM((width, units), bf16),
            pltpu.VMEM((halves, per, both, width), bf16),
            pltpu.VMEM((2, halves, per, both, width), bf16),
            pltpu.VMEM((blocks, halves, tall, units), bf16),
            pltpu.VMEM((blocks, halves, tall, units), bf16),
            pltpu.VMEM((blocks, halves, tall, units), bf16),
            pltpu.VMEM((blocks, halves, tall, units), bf16),
            pltpu.VMEM((blocks, halves, tall, units), bf16),
            pltpu.VMEM((units, halves * tall), bf16),
            pltpu.VMEM((units, width), f32),
            pltpu.VMEM((units, width), f32),
            pltpu.VMEM((units, width), f32),
            pltpu.VMEM((2, 3, units, slab), bf16),
            pltpu.VMEM((halves, per, count, width), bf16),
            pltpu.VMEM((halves, blocks, per, count, width), bf16),
            pltpu.VMEM((halves, held, count, width), f32),
            pltpu.VMEM((halves, outer, count, width), f32),
            pltpu.VMEM((halves, links, count, width), bf16),
            pltpu.VMEM((halves, links, count, width), bf16),
            pltpu.VMEM((halves, outer - 1, count, width), bf16),
            pltpu.VMEM((halves, outer - 1, count, width), bf16),
            pltpu.VMEM((total_rows, width), f32),
            pltpu.VMEM((total_rows, width), bf16),
            sems((2, halves, outer)),
            sems((2, halves, outer)),
            sems((2, halves, outer, chips)),
            sems((2, halves, outer, chips)),
            sems((2, halves, outer, chips)),
            sems((2, halves, outer, chips)),
            sems((2, halves, blocks)),
            sems((2, halves, blocks)),
            sems((2, halves, links)),
            sems((2, halves, links)),
            sems((2, halves, outer)),
            sems((2, halves, outer)),
            sems((2, halves, blocks)),
            sems((2, halves)),
            sems((blocks, 2 * halves)),
            sems((parts, 3)),
            sems((2, 3)),
        ],
        compiler_params=pltpu.CompilerParams(
            collective_id=2, has_side_effects=True, vmem_limit_bytes=62 * 2**20
        ),
        cost_estimate=pl.CostEstimate(flops=flops, bytes_accessed=64 * 2**20, transcendentals=0),
    )(*flat_pieces, rows_low, resid, cotangent, gain)
    grads = results[5:]
    return results[:3] + ([[grads[j * 3 + c] for j in range(inner)] for c in range(3)],)


def close_rows(at_rows, dres_ref, raw, cot_ref):
    dres_ref[at_rows] = raw[at_rows] + cot_ref[at_rows].astype(jnp.float32)


def adam_kernel(turned, w_ref, m_ref, v_ref, g_ref, *rest):
    scale_ref = rest[0] if len(rest) == 5 else None
    w_out, m_out, v_out, c_out = rest[-4:]
    grad = g_ref[...].T if turned else g_ref[...]
    new, first, second = adam_step(
        w_ref[...], grad, m_ref[...], v_ref[...], rate_matrix, weight_decay
    )
    if scale_ref is not None:
        new = new * scale_ref[...]
    w_out[...] = new
    m_out[...] = first
    v_out[...] = second
    c_out[...] = new.astype(jnp.bfloat16)


def adam_call(param, grads, at, first, second, scale=None):
    mats, rows, columns = param.shape
    turned = scale is not None
    spec = pl.BlockSpec((None, rows, columns), lambda k: (k, 0, 0))
    grad_spec = pl.BlockSpec((None,) + grads.shape[1:], lambda k: (at + k, 0, 0))
    specs = [spec] * 3 + [grad_spec]
    values = [param, first, second, grads]
    if turned:
        values.append(scale)
        specs.append(pl.BlockSpec((None, 1, columns), lambda k: (k, 0, 0)))
    outs = [jax.ShapeDtypeStruct(param.shape, jnp.float32)] * 3
    outs.append(jax.ShapeDtypeStruct(param.shape, jnp.bfloat16))
    size = param.size
    return pl.pallas_call(
        functools.partial(adam_kernel, turned),
        grid=(mats,),
        in_specs=specs,
        out_specs=[spec] * 4,
        out_shape=outs,
        cost_estimate=pl.CostEstimate(
            flops=20 * size, bytes_accessed=28 * size, transcendentals=2 * size
        ),
        compiler_params=pltpu.CompilerParams(vmem_limit_bytes=32 * 2**20),
    )(*values)


def adam_units_kernel(turned, at_ref, w_ref, m_ref, v_ref, g_ref, w_out, m_out, v_out, c_out):
    grad = g_ref[...].astype(jnp.float32)
    if turned:
        grad = grad.T
    new, first, second = adam_step(
        w_ref[...], grad, m_ref[...], v_ref[...], rate_matrix, weight_decay
    )
    w_out[...] = new
    m_out[...] = first
    v_out[...] = second
    c_out[...] = new.astype(jnp.bfloat16)


def adam_units(grid, param, first, second, grads, turned):
    n = grid.outer
    stacked = jnp.stack([jnp.stack(list(pieces)) for pieces in grads])
    mats, _, units, wide = stacked.shape
    if not turned:
        spec = pl.BlockSpec((units, wide), lambda c, k, at: (k, 0))
    else:
        spec = pl.BlockSpec((None, wide, units), lambda c, k, at: (c, 0, k))
    grad_spec = pl.BlockSpec(
        (None, None, units, wide), lambda c, k, at: (c, lax.rem(at[0] - k + n, n), 0, 0)
    )
    size = param.size
    outs = [jax.ShapeDtypeStruct(param.shape, jnp.float32)] * 3
    outs.append(jax.ShapeDtypeStruct(param.shape, jnp.bfloat16))
    return pl.pallas_call(
        functools.partial(adam_units_kernel, turned),
        grid_spec=pltpu.PrefetchScalarGridSpec(
            num_scalar_prefetch=1,
            grid=(mats, n),
            in_specs=[spec] * 3 + [grad_spec],
            out_specs=[spec] * 4,
        ),
        out_shape=outs,
        cost_estimate=pl.CostEstimate(
            flops=20 * size, bytes_accessed=28 * size, transcendentals=2 * size
        ),
        compiler_params=pltpu.CompilerParams(vmem_limit_bytes=32 * 2**20),
    )(grid.outer_at.astype(jnp.int32)[None], param, first, second, stacked)


def local(
    tokens,
    cotangent,
    block_ids,
    w_qkv,
    m_qkv,
    v_qkv,
    w_out,
    m_out,
    v_out,
    w_gu,
    m_gu,
    v_gu,
    w_down,
    m_down,
    v_down,
    gains,
    gain_m,
    gain_v,
):
    grid = Grid()
    local_x = tokens[0]
    gain_count = gains.shape[0]
    low_gains = jnp.pad(gains.astype(jnp.bfloat16), ((0, 16 - gain_count), (0, 0)))
    full_qkv, full_out, full_gains, seq_x = path_gather(
        w_qkv.astype(jnp.bfloat16), w_out.astype(jnp.bfloat16), low_gains, local_x
    )
    gain_rows = jnp.swapaxes(full_gains[:, :gain_count], 0, 1).reshape(gain_count, -1)
    gain_rows = gain_rows.astype(jnp.float32)
    shard = jnp.stack([w_gu[0], w_gu[1], w_down.T]).astype(jnp.bfloat16)
    full_qkv, shard = lax.optimization_barrier((full_qkv, shard))
    model_width = local_x.shape[1]
    length = seq_x.shape[0]
    span = full_qkv.shape[2]
    heads_here = span // HEAD
    offset = lax.axis_index("tensor") * span
    q_gain = lax.dynamic_slice_in_dim(gain_rows[0], offset, span)
    k_gain = lax.dynamic_slice_in_dim(gain_rows[1], offset, span)
    cosine, sine = rope_tables(length, HEAD)

    head_gains = jnp.stack([q_gain, k_gain])
    tables = (cosine[:, 0], sine[:, 0])
    pieces, kept = attend_call(
        seq_x,
        full_qkv,
        full_out,
        head_gains,
        gain_rows[2:3],
        tables,
        block_ids[0],
        local_x,
        shard,
    )
    hats, scales, q_low, k_low, v_low, log_total, context_low = kept[:7]
    attn_hat, o_scale, resid, resid_low, tops = kept[7:]
    output, d_resid, gain_last, unit_grads = unit_kernel_call(
        resid_low, resid, cotangent[0], gain_rows[3:4], pieces
    )
    backs, (part, part_gains, tops, grad_tokens) = attend_back_call(
        d_resid,
        attn_hat,
        o_scale,
        gain_rows[2:3],
        full_out,
        context_low,
        q_low,
        k_low,
        v_low,
        log_total,
        hats,
        scales,
        head_gains,
        tables,
        block_ids[0],
        seq_x,
        full_qkv,
        gain_last,
        tops,
        unit_grads,
    )
    part_gains = part_gains[:gain_count]
    head_top = tops[:heads_here, 0]
    factor = clip_tau / jnp.maximum(head_top, clip_tau)
    column = jnp.repeat(jnp.sqrt(factor), HEAD)
    column_scale = jnp.stack([column, column, jnp.ones_like(column)])[:, None, :]
    new_qkv, new_m_qkv, new_v_qkv, copy_qkv = adam_call(w_qkv, part, 0, m_qkv, v_qkv, column_scale)
    new_out, new_m_out, new_v_out, copy_out = [
        v[0] for v in adam_call(w_out[None], part, 3, m_out[None], v_out[None])
    ]
    new_gu, new_m_gu, new_v_gu, copy_gu = adam_units(grid, w_gu, m_gu, v_gu, backs[:2], True)
    new_down, new_m_down, new_v_down, copy_down = adam_units(
        grid, w_down, m_down, v_down, backs[2:], False
    )
    new_gains, new_gain_m, new_gain_v = adam_step(gains, part_gains, gain_m, gain_v, rate_gain, 0.0)
    return (
        output[None],
        grad_tokens[None],
        new_qkv,
        new_m_qkv,
        new_v_qkv,
        copy_qkv,
        new_out,
        new_m_out,
        new_v_out,
        copy_out,
        new_gu,
        new_m_gu,
        new_v_gu,
        copy_gu,
        new_down,
        new_m_down,
        new_v_down,
        copy_down,
        new_gains,
        new_gain_m,
        new_gain_v,
        factor,
    )


def solution(mesh):
    return jax.shard_map(
        local,
        mesh=mesh,
        in_specs=(
            P("dp", "tensor", None),
            P("dp", "tensor", None),
            P("dp", None),
            P(None, "dp", "tensor"),
            P(None, "dp", "tensor"),
            P(None, "dp", "tensor"),
            P("tensor", "dp"),
            P("tensor", "dp"),
            P("tensor", "dp"),
            P(None, "dp", "tensor"),
            P(None, "dp", "tensor"),
            P(None, "dp", "tensor"),
            P("tensor", "dp"),
            P("tensor", "dp"),
            P("tensor", "dp"),
            P(None, "dp"),
            P(None, "dp"),
            P(None, "dp"),
        ),
        out_specs=(
            P("dp", "tensor", None),
            P("dp", "tensor", None),
            P(None, "dp", "tensor"),
            P(None, "dp", "tensor"),
            P(None, "dp", "tensor"),
            P(None, "dp", "tensor"),
            P("tensor", "dp"),
            P("tensor", "dp"),
            P("tensor", "dp"),
            P("tensor", "dp"),
            P(None, "dp", "tensor"),
            P(None, "dp", "tensor"),
            P(None, "dp", "tensor"),
            P(None, "dp", "tensor"),
            P("tensor", "dp"),
            P("tensor", "dp"),
            P("tensor", "dp"),
            P("tensor", "dp"),
            P(None, "dp"),
            P(None, "dp"),
            P(None, "dp"),
            P("tensor"),
        ),
        check_vma=False,
    )
```

```python
import functools

import jax
import jax.numpy as jnp
import numpy as np
from jax import lax
from jax.experimental import pallas as pl
from jax.experimental.pallas import tpu as pltpu
from jax.sharding import PartitionSpec as P

HEAD = 128
STEP = 5


norm_eps = 1e-06
rope_base = 500000.0
beta_one = 0.9
beta_two = 0.95
rate_matrix = 0.01
rate_gain = 0.6
weight_decay = 0.1
adam_eps = 1e-08
clip_tau = 9.0
masked_value = -1e30


def rope_tables(length, size):
    half = size // 2
    freq = np.float32(rope_base) ** (-(np.arange(half, dtype=np.float32) * np.float32(2.0 / size)))
    angle = np.arange(length, dtype=np.float32)[:, None] * freq[None, :]
    angle = np.concatenate([angle, angle], axis=1)
    return (jnp.asarray(np.cos(angle)), jnp.asarray(np.sin(angle)))


def adam_step(param, grad, first, second, rate, decay):
    first = beta_one * first + (1.0 - beta_one) * grad
    second = beta_two * second + (1.0 - beta_two) * grad * grad
    fix_one = 1.0 - beta_one**STEP
    fix_two = 1.0 - beta_two**STEP
    update = first / fix_one / (jnp.sqrt(second / fix_two) + adam_eps)
    return (param - rate * (update + decay * param), first, second)


class Grid:
    def __init__(self):
        self.dp = lax.axis_size("dp")
        self.tensor = lax.axis_size("tensor")
        self.inner = 1
        while self.inner * self.inner * 4 <= self.dp:
            self.inner *= 2
        self.outer = self.dp // self.inner
        self.chips = self.tensor // 2
        self.dp_at = lax.axis_index("dp")
        self.tensor_at = lax.axis_index("tensor")
        self.inner_at = self.dp_at % self.inner
        self.chip_at = self.tensor_at // 2
        self.core_at = self.tensor_at % 2
        self.outer_at = self.dp_at // self.inner

    def path_of(self, index):
        column, row = index // self.inner, index % self.inner
        return row * self.outer + column + (row % 2) * (self.outer - 1 - 2 * column)

    def outer_flip(self, index, step):
        result = 0
        for bit in bits(self.outer):
            side = index // bit % 2
            result = result + bit * (1 - side if step & bit else side)
        return result

    def index_of(self, place):
        row, column = place // self.outer, place % self.outer
        return (column + (row % 2) * (self.outer - 1 - 2 * column)) * self.inner + row


def bits(count):
    return [1 << k for k in range(count.bit_length() - 1)]


def greet(peers):
    barrier = pltpu.get_barrier_semaphore()
    for peer in peers:
        pl.semaphore_signal(barrier, inc=1, device_id=peer, device_id_type=pl.DeviceIdType.MESH)
    pl.semaphore_wait(barrier, len(peers))


def attend_back_call(
    d_resid, attn_hat, o_scale, gain_rows, full_out, context, q_low, k_low, v_low, lse, hats, scales,
    tables, blocks, seq, full_qkv, gain_last, tops, unit_grads,
):
    grid = Grid()
    n, outer, inner, chips, tensor = grid.dp, grid.outer, grid.inner, grid.chips, grid.tensor
    count, width = d_resid.shape
    length, span = context.shape
    heads = span // HEAD
    units, slab = unit_grads[0][0].shape[1:]
    thin = width // n
    half = span // 2
    tall = min(256, length)
    tile = 512
    lines = 32
    ring = 8 + 2
    gain_item, top_item = 8, 9
    bf16, f32 = jnp.bfloat16, jnp.float32
    mesh_id = pl.DeviceIdType.MESH
    flat_grads = [unit_grads[c][j] for j in range(inner) for c in range(3)]
    some = len(flat_grads)
    z_steps = list(range(1, outer))

    def kernel(*refs):
        fixed, far_in, grads_in = refs[:17], refs[17:20], refs[20 : 20 + some]
        rest = refs[20 + some :]
        backs = [rest[c * outer : (c + 1) * outer] for c in range(3)]
        body(*fixed, far_in, grads_in, backs, *rest[3 * outer :])

    def body(
        dres_ref, hat_ref, o_scale_ref, gain_ref, out_w, ctx, q_ref, k_ref, v_ref, lse_ref, scale_ref,
        cos_ref, sin_ref, id_col, id_row, last_ref, tops_ref, far_in, grads_in,
        backs, part_ref, gains_out, tops_out, tokens_out,
        hats, seq, qkv_w, seq_do, d_ctx, d_q, d_k, d_v, d_low, whole, terms, row_terms, turned,
        land, land_gain, land_top, own_gain, peer_gain, inners, peer_inners,
        grad_own, grad_land, grad_sum, core_send, core_land, hold, chip_send, chip_land,
        s_ring, r_ring, s_row, r_row, s_in, r_in, s_y, r_y, s_z, r_z, s_core, r_core, s_chip, r_chip, s_gain, r_gain, local,
    ):
        hats_in, seq_in, qkv_in = far_in
        g = Grid()

        def tensor_peer(k, flip):
            core = 1 - g.core_at if flip else g.core_at
            return (g.dp_at, lax.rem(g.chip_at + k + chips, chips) * 2 + core)

        def dp_peer(s, j):
            across = g.outer_flip(g.outer_at, s) * inner
            return (across + lax.rem(g.inner_at + j + inner, inner), g.tensor_at)

        place = g.path_of(g.dp_at)
        after_dp = (g.index_of(lax.rem(place + 1, n)), g.tensor_at)
        before_dp = (g.index_of(lax.rem(place + n - 1, n)), g.tensor_at)
        near = [tensor_peer(k, f) for k in range(chips) for f in (0, 1) if (k, f) != (0, 0)]
        far = [dp_peer(s, 0) for s in range(1, outer)] + [dp_peer(0, j) for j in range(1, inner)]
        greet(near + far + [after_dp, before_dp])

        def remote(src, dst, send, recv, peer):
            copy = pltpu.make_async_remote_copy(
                src_ref=src, dst_ref=dst, send_sem=send, recv_sem=recv,
                device_id=peer, device_id_type=mesh_id,
            )
            copy.start()
            return copy

        def fetch(src, dst, at):
            copy = pltpu.make_async_copy(src, dst, local.at[at])
            copy.start()
            return copy

        def dot(a, b, contract):
            return lax.dot_general(a, b, (contract, ((), ())), preferred_element_type=f32)

        def looped(total, make):
            lax.fori_loop(0, total, lambda i, c: (make(i), c)[1], 0)

        def rows_of(i, size):
            return pl.ds(pl.multiple_of(i * size, size), size)

        sent = []
        y_copies = {}
        for j in range(1, inner):
            for c in range(3):
                copy = remote(
                    grads_in[j * 3 + c], grad_land.at[j - 1, c], s_y.at[j, c], r_y.at[j, c], dp_peer(0, j)
                )
                y_copies[j, c] = copy
                sent.append(copy)
        own_grads = [fetch(grads_in[c], grad_own.at[c], c) for c in range(3)]
        fetched = [fetch(hats_in, hats, 3), fetch(seq_in, seq, 4), fetch(qkv_in, qkv_w, 5)]
        z_copies = []
        keeps = []

        def unit_sums(c):
            own_grads[c].wait()
            for j in range(1, inner):
                y_copies[j, c].wait_recv()

            def add(i):
                s, at = i // (units // 64), lax.rem(i, units // 64)
                rows = rows_of(at, 64)
                total = grad_own[c, s, rows].astype(f32)
                for j in range(1, inner):
                    total = total + grad_land[j - 1, c, s, rows].astype(f32)
                grad_sum[c, s, rows] = total.astype(bf16)

            looped(outer * (units // 64), add)
            for s in z_steps:
                z_copies.append(
                    remote(grad_sum.at[c, s], backs[c][s], s_z.at[c, s], r_z.at[c, s], dp_peer(s, 0))
                )
            keeps.append(fetch(grad_sum.at[c, 0], backs[c][0], 6 + c))

        t_at = g.tensor_at
        mine = rows_of(t_at, count)

        def open_rows(i, total):
            at = rows_of(i, lines)
            value, hat = dres_ref[at], hat_ref[at]
            upstream = value * gain_ref[2:3]
            mean = jnp.mean(upstream * hat, axis=1, keepdims=True)
            d_attn = (o_scale_ref[at] * (upstream - hat * mean)).astype(bf16)
            seq_do[pl.ds(pl.multiple_of(t_at * count + i * lines, lines), lines)] = d_attn
            return total + jnp.sum(value * hat, axis=0, keepdims=True)

        gain_attn = lax.fori_loop(0, count // lines, open_rows, jnp.zeros((1, width), f32))
        row_terms[...] = jnp.zeros((8, width), f32)
        row_terms[2:3] = gain_attn
        row_terms[3:4] = last_ref[...]
        moves, passed = [], []

        def row_copy(slot, index, peer):
            at = rows_of(index, count)
            copy = remote(seq_do.at[at], seq_do.at[at], s_row.at[slot], r_row.at[slot], peer)
            sent.append(copy)
            return copy

        for k in range(1, chips):
            moves.append(row_copy(k - 1, t_at, tensor_peer(k, 0)))
        to_core = row_copy(chips - 1, t_at, tensor_peer(0, 1))
        for k in range(1, chips):
            moves[k - 1].wait_recv()
            source = lax.rem(g.chip_at - k + chips, chips) * 2 + g.core_at
            passed.append(row_copy(chips - 1 + k, source, tensor_peer(0, 1)))
        to_core.wait_recv()
        for copy in passed:
            copy.wait_recv()

        def context_grad(i):
            at = rows_of(i, tall)
            d_ctx[at] = dot(seq_do[at], out_w[...], ((1,), (1,))).astype(bf16)

        looped(length // tall, context_grad)
        unit_sums(0)

        scale = HEAD ** (-0.5)
        for h in range(heads):
            cols = slice(h * HEAD, (h + 1) * HEAD)

            def head(i, c, cols=cols, h=h):
                at = rows_of(i, tall)
                q_part, ctx_part = q_ref[at, cols], d_ctx[at, cols]
                raw = dot(q_part, k_ref[:, cols], ((1,), (1,))) * scale
                masked = jnp.where(id_row[...] <= id_col[at], raw, masked_value)
                probs = jnp.exp(masked - lse_ref[at, h : h + 1])
                d_probs = dot(ctx_part, v_ref[:, cols], ((1,), (1,)))
                mean = jnp.sum(probs * d_probs, axis=1, keepdims=True)
                d_scores = (probs * (d_probs - mean)).astype(bf16)
                d_q[at, cols] = dot(d_scores, k_ref[:, cols], ((1,), (0,))) * scale
                key = dot(d_scores, q_part, ((0,), (0,))) * scale
                value = dot(probs.astype(bf16), ctx_part, ((0,), (0,)))
                d_k[:, cols] = jnp.where(i == 0, key, d_k[:, cols] + key)
                d_v[:, cols] = jnp.where(i == 0, value, d_v[:, cols] + value)
                return c

            d_k[:, cols] = jnp.zeros((length, HEAD), f32)
            d_v[:, cols] = jnp.zeros((length, HEAD), f32)
            lax.fori_loop(0, length // tall, head, 0)
        if inner > 1 or outer > 1:
            unit_sums(1)
        fetched[0].wait()
        sign = jnp.where(lax.broadcasted_iota(jnp.int32, (tall, HEAD), 1) < HEAD // 2, -1.0, 1.0)

        def unrotate(i, sums):
            at = rows_of(i, tall)
            cosine, sine = cos_ref[at], sin_ref[at]
            lane = lax.broadcasted_iota(jnp.int32, (tall, 128), 1)
            columns = jnp.zeros((tall, 128), f32)
            result = []
            for c, grad in ((0, d_q), (1, d_k)):
                total = jnp.zeros((tall, 1), f32)
                terms_row = []
                for h in range(heads):
                    cols = slice(h * HEAD, (h + 1) * HEAD)
                    value = grad[at, cols]
                    back = value * cosine - pltpu.roll(value * sine, HEAD // 2, 1) * sign
                    hat = hats[c, at, cols]
                    terms_row.append(jnp.sum(back * hat, axis=0, keepdims=True))
                    at_head = pl.ds(pl.multiple_of(t_at * span + h * HEAD, HEAD), HEAD)
                    back = back * gain_ref[c : c + 1, at_head]
                    grad[at, cols] = back
                    total = total + jnp.sum(back * hat, axis=1, keepdims=True)
                columns = jnp.where(lane == c, total, columns)
                result.append(sums[c] + jnp.concatenate(terms_row, axis=1))
            inners[:, at] = columns.T[:8]
            return tuple(result)

        zero = jnp.zeros((1, span), f32)
        gain_q, gain_k = lax.fori_loop(0, length // tall, unrotate, (zero, zero))
        offset = rows_of(t_at, span)
        row_terms[0:1, offset] = gain_q
        row_terms[1:2, offset] = gain_k
        in_copies = []
        for k in range(chips):
            for f in (0, 1):
                if (k, f) != (0, 0):
                    at = k * 2 + f - 1
                    in_copies.append(
                        remote(inners, peer_inners.at[at], s_in.at[at], r_in.at[at], tensor_peer(k, f))
                    )
        sent.extend(in_copies)
        turned[...] = ctx[...].T

        def out_grad(i):
            cols = rows_of(i, tile)
            whole[3, :, cols] = dot(turned[...], seq_do[:, cols], ((1,), (0,))).astype(bf16)

        looped(width // tile, out_grad)
        for copy in in_copies:
            copy.wait_recv()

        def normed(i):
            at = rows_of(i, tall)
            sums = inners[:, at]
            for other in range(tensor - 1):
                sums = sums + peer_inners[other, :, at]
            column = jnp.concatenate([sums, jnp.zeros((120, tall), f32)], axis=0).T / width
            for c, grad in ((0, d_q), (1, d_k)):
                value = grad[at] - hats[c, at] * column[:, c : c + 1]
                d_low[c, at] = (scale_ref[at, c : c + 1] * value).astype(bf16)
            d_low[2, at] = d_v[at].astype(bf16)

        looped(length // tall, normed)
        fetched[1].wait()
        for c in range(3):
            turned[...] = d_low[c].T

            def weight_grad(i, c=c):
                cols = rows_of(i, tile)
                whole[c, :, cols] = dot(turned[...], seq[:, cols], ((1,), (0,))).astype(bf16)

            looped(width // tile, weight_grad)

        def place_terms(i, c):
            cols = pl.ds(pl.multiple_of(i * thin, thin), thin)
            terms[i] = row_terms[:, cols]
            return c

        lax.fori_loop(0, n, place_terms, 0)

        def way_of(item):
            return 1 if item >= 8 else 1 - 2 * (item // 4)

        def own(item, away):
            index = g.index_of(lax.rem(place - way_of(item) * away + 2 * n, n))
            if item == gain_item:
                return terms.at[index]
            if item == top_item:
                return tops_ref
            side, c = item // 4, item % 4
            return whole.at[c, pl.ds(side * half, half), rows_of(index, thin)]

        def landed(step, item):
            if item == gain_item:
                return land_gain.at[step]
            if item == top_item:
                return land_top.at[step]
            return land.at[step, item]

        hops = {}

        def hop(step, item):
            hops[step, item] = remote(
                own(item, 1) if step == 0 else landed(step - 1, item),
                landed(step, item),
                s_ring.at[step, item],
                r_ring.at[step, item],
                after_dp if way_of(item) == 1 else before_dp,
            )

        order = [gain_item, top_item] + [c + side * 4 for c in range(4) for side in (0, 1)]
        for item in order:
            hop(0, item)
        unit_sums(2)

        fetched[2].wait()
        chip_order = list(range(1, chips)) + [0]
        core_copies, chip_copies = {}, {}

        def token_rows(k, flip, store):
            chip = lax.rem(g.chip_at + k, chips)
            core = 1 - g.core_at if flip else g.core_at
            at = rows_of(chip * 2 + core, count)

            def columns(i):
                cols = rows_of(i, tile)
                total = dot(d_low[0, at], qkv_w[0, cols], ((1,), (1,)))
                for c in (1, 2):
                    total = total + dot(d_low[c, at], qkv_w[c, cols], ((1,), (1,)))
                store(cols, total)

            looped(width // tile, columns)

        duties = []
        for k in chip_order:

            def away(k=k):
                def store(cols, value):
                    core_send[k, :, cols] = value.astype(bf16)

                token_rows(k, True, store)
                core_copies[k] = remote(
                    core_send.at[k], core_land.at[k], s_core.at[k], r_core.at[k], tensor_peer(0, 1)
                )

            def here(k=k):
                def store(cols, value):
                    hold[k, :, cols] = value

                token_rows(k, False, store)

            def join(k=k):
                core_copies[k].wait_recv()

                def add(i):
                    at = rows_of(i, lines)
                    chip_send[k - 1, at] = (hold[k, at] + core_land[k, at].astype(f32)).astype(bf16)

                looped(count // lines, add)
                chip_copies[k] = remote(
                    chip_send.at[k - 1], chip_land.at[k - 1], s_chip.at[k], r_chip.at[k], tensor_peer(k, 0)
                )

            duties += [away, here] + ([join] if k else [])

        def close_tokens():
            core_copies[0].wait_recv()
            for k in range(1, chips):
                chip_copies[k].wait_recv()

            def close(i):
                at = rows_of(i, lines)
                total = dres_ref[at] + hold[0, at] + core_land[0, at].astype(f32)
                for k in range(1, chips):
                    total = total + chip_land[k - 1, at].astype(f32)
                tokens_out[at] = total

            looped(count // lines, close)

        duties.append(close_tokens)
        per_step = -(-len(duties) // (n - 2))
        for step in range(1, n):
            for item in order:
                hops[step - 1, item].wait_recv()
                here = landed(step - 1, item)
                if item == top_item:
                    summed = jnp.maximum(here[...], tops_ref[...])
                else:
                    summed = here[...].astype(f32) + own(item, step + 1)[...].astype(f32)
                if step < n - 1:
                    here[...] = summed.astype(here.dtype)
                    hop(step, item)
                elif item == gain_item:
                    own_gain[0] = summed
                elif item == top_item:
                    tops_out[...] = summed
                else:
                    side, c = item // 4, item % 4
                    part_ref[c, pl.ds(side * half, half)] = summed
            for _ in range(per_step):
                if duties:
                    duties.pop(0)()
        peers = [tensor_peer(0, 1)] + [tensor_peer(k, 0) for k in range(1, chips)]
        first = remote(own_gain.at[0], peer_gain.at[0], s_gain.at[0], r_gain.at[0], peers[0])
        first.wait_recv()
        own_gain[1] = own_gain[0] + peer_gain[0]
        others = [
            remote(own_gain.at[1], peer_gain.at[k], s_gain.at[k], r_gain.at[k], peers[k])
            for k in range(1, chips)
        ]
        result = own_gain[1]
        for k in range(1, chips):
            others[k - 1].wait_recv()
            result = result + peer_gain[k]
        gains_out[...] = result
        for copy in z_copies:
            copy.wait()
        for copy in keeps:
            copy.wait()
        for copy in sent + list(hops.values()) + list(core_copies.values()):
            copy.wait_send()
        for copy in list(chip_copies.values()) + [first] + others:
            copy.wait_send()

    shape = jax.ShapeDtypeStruct
    anywhere = pl.BlockSpec(memory_space=pl.ANY)
    vmem = pl.BlockSpec(memory_space=pltpu.VMEM)
    sems = pltpu.SemaphoreType.DMA
    results = pl.pallas_call(
        kernel,
        out_shape=(shape((units, slab), bf16),) * (3 * outer)
        + (
            shape((4, span, thin), f32),
            shape((8, thin), f32),
            shape(tops.shape, f32),
            shape((count, width), f32),
        ),
        in_specs=[vmem] * 17 + [anywhere] * 3 + [anywhere] * some,
        out_specs=(anywhere,) * (3 * outer) + (vmem,) * 4,
        scratch_shapes=[
            pltpu.VMEM(hats.shape, f32),
            pltpu.VMEM(seq.shape, bf16),
            pltpu.VMEM(full_qkv.shape, bf16),
            pltpu.VMEM((length, width), bf16),
            pltpu.VMEM((length, span), bf16),
            pltpu.VMEM((length, span), f32),
            pltpu.VMEM((length, span), f32),
            pltpu.VMEM((length, span), f32),
            pltpu.VMEM((3, length, span), bf16),
            pltpu.VMEM((4, span, width), bf16),
            pltpu.VMEM((n, 8, thin), f32),
            pltpu.VMEM((8, width), f32),
            pltpu.VMEM((span, length), bf16),
            pltpu.VMEM((n - 1, 8, half, thin), bf16),
            pltpu.VMEM((n - 1, 8, thin), f32),
            pltpu.VMEM((n - 1,) + tops.shape, f32),
            pltpu.VMEM((2, 8, thin), f32),
            pltpu.VMEM((chips, 8, thin), f32),
            pltpu.VMEM((8, length), f32),
            pltpu.VMEM((tensor - 1, 8, length), f32),
            pltpu.VMEM((3, outer, units, slab), bf16),
            pltpu.VMEM((max(inner - 1, 1), 3, outer, units, slab), bf16),
            pltpu.VMEM((3, outer, units, slab), bf16),
            pltpu.VMEM((chips, count, width), bf16),
            pltpu.VMEM((chips, count, width), bf16),
            pltpu.VMEM((chips, count, width), f32),
            pltpu.VMEM((max(chips - 1, 1), count, width), bf16),
            pltpu.VMEM((max(chips - 1, 1), count, width), bf16),
            sems((n - 1, ring)),
            sems((n - 1, ring)),
            sems((2 * chips - 1,)),
            sems((2 * chips - 1,)),
            sems((tensor - 1,)),
            sems((tensor - 1,)),
            sems((inner, 3)),
            sems((inner, 3)),
            sems((3, outer)),
            sems((3, outer)),
            sems((chips,)),
            sems((chips,)),
            sems((chips,)),
            sems((chips,)),
            sems((chips,)),
            sems((chips,)),
            sems((9,)),
        ],
        compiler_params=pltpu.CompilerParams(
            collective_id=1, has_side_effects=True, vmem_limit_bytes=62 * 2**20
        ),
    )(
        d_resid, attn_hat, o_scale, gain_rows, full_out, context, q_low, k_low, v_low, lse, scales,
        tables[0], tables[1], blocks[:, None], blocks[None, :], gain_last, tops,
        hats, seq, full_qkv, *flat_grads,
    )
    backs = [results[c * outer : (c + 1) * outer] for c in range(3)]
    return backs, results[3 * outer :]


def open_call(shard, flat, gains, rows, w_gu, w_down, tables, blocks):
    grid = Grid()
    n, outer, inner = grid.dp, grid.outer, grid.inner
    chips, tensor = grid.chips, grid.tensor
    count, width = rows.shape
    length = count * tensor
    lead, slab, span = shard.shape
    half = slab // 2
    part_tall = span // 2
    heads = span // HEAD
    shard_units = w_gu.shape[2]
    units = shard_units // outer
    parts = outer * inner
    ring = 2 * lead + 3
    steps = list(range(1, outer))
    tall = min(256, length)
    tile = 512
    lines = 32
    bf16, f32 = jnp.bfloat16, jnp.float32
    mesh_id = pl.DeviceIdType.MESH

    def kernel(*refs):
        pieces = [refs[11 + j * outer : 11 + (j + 1) * outer] for j in range(inner)]
        body(*refs[:11], pieces, *refs[11 + parts :])

    def body(
        shard_ref, flat_ref, gains_ref, rows_any, gu_any, down_any, cos_ref, sin_ref, id_col, id_row, rows_ref,
        pieces, qkv_out, flat_out, seq_out,
        gain_rows, hat_ref, scale_ref, q_low, k_low, v_low, lse_ref, context, attn_hat, o_scale, resid, resid_low, top_ref,
        qkv_ref, out_w_ref, seq_ref, all_gains, gu_wide, down_wide, cast,
        square, squares, core_send, core_land, hold, chip_send, chip_land,
        s_ring, r_ring, s_row, r_row, s_z, r_z, s_y, r_y, s_sq, r_sq, s_core, r_core, s_chip, r_chip, local,
    ):
        g = Grid()

        def tensor_peer(k, flip):
            core = 1 - g.core_at if flip else g.core_at
            return (g.dp_at, lax.rem(g.chip_at + k + chips, chips) * 2 + core)

        def dp_peer(s, j):
            across = g.outer_flip(g.outer_at, s) * inner
            return (across + lax.rem(g.inner_at + j + inner, inner), g.tensor_at)

        near = [tensor_peer(k, f) for k in range(chips) for f in (0, 1) if (k, f) != (0, 0)]
        far = [dp_peer(s, 0) for s in range(1, outer)]
        far += [dp_peer(0, j) for j in sorted({1 % inner, inner - 1} - {0})]
        t_at = g.tensor_at
        place = g.path_of(g.dp_at)
        after = (g.index_of(lax.rem(place + 1, n)), t_at)
        before = (g.index_of(lax.rem(place + n - 1, n)), t_at)
        greet(near + far + [after, before])

        def remote(src, dst, send, recv, peer):
            copy = pltpu.make_async_remote_copy(
                src_ref=src, dst_ref=dst, send_sem=send, recv_sem=recv,
                device_id=peer, device_id_type=mesh_id,
            )
            copy.start()
            return copy

        def dot(a, b, contract):
            return lax.dot_general(a, b, (contract, ((), ())), preferred_element_type=f32)

        def looped(total, make):
            lax.fori_loop(0, total, lambda i, c: (make(i), c)[1], 0)

        def rows_of(i, size):
            return pl.ds(pl.multiple_of(i * size, size), size)

        def fetch(src, dst, at):
            copy = pltpu.make_async_copy(src, dst, local.at[at])
            copy.start()
            return copy

        def views(item, index):
            if item == ring - 1:
                return 1, gains_ref, all_gains.at[index]
            if item >= 2 * lead:
                side = item - 2 * lead
                part = pl.ds(side * part_tall, part_tall)
                return 1 - 2 * side, flat_ref.at[part], out_w_ref.at[part, rows_of(index, slab)]
            side, c = item // lead, item % lead
            at = pl.ds(pl.multiple_of(index * slab + side * half, half), half)
            return 1 - 2 * side, shard_ref.at[c, pl.ds(side * half, half)], qkv_ref.at[c, at]

        hops = {}

        def hop(step, item):
            way = views(item, 0)[0]
            index = g.index_of(lax.rem(place - way * step + n, n))
            _, source, target = views(item, index)
            hops[step, item] = remote(
                source if step == 0 else target,
                target,
                s_ring.at[step, item],
                r_ring.at[step, item],
                after if way == 1 else before,
            )

        def row_copy(slot, index, peer, src=None):
            at = seq_ref.at[rows_of(index, count)]
            return remote(at if src is None else src, at, s_row.at[slot], r_row.at[slot], peer)

        order = [c + side * lead for c in range(lead) for side in (0, 1)]
        order += list(range(2 * lead, ring))
        for item in order:
            hop(0, item)
        row_copies = [
            row_copy(k - 1, t_at, tensor_peer(k, 0), rows_any) for k in range(1, chips)
        ]
        row_copies.append(row_copy(chips - 1, t_at, tensor_peer(0, 1), rows_any))
        wide = [fetch(gu_any, gu_wide, 1), fetch(down_any, down_wide, 2)]
        kept = [
            fetch(shard_ref, qkv_ref.at[:, rows_of(g.dp_at, slab)], 3),
            fetch(gains_ref, all_gains.at[g.dp_at], 4),
            fetch(rows_any, seq_ref.at[rows_of(t_at, count)], 5),
            fetch(flat_ref, out_w_ref.at[:, rows_of(g.dp_at, slab)], 6),
        ]

        def cast_wide(c):
            if c == 0:
                wide[0].wait()

            def cast_rows(i):
                at = rows_of(i, lines)
                cast[c, at] = gu_wide[c, at].astype(bf16)

            looped(slab // lines, cast_rows)

        def cast_turned():
            wide[1].wait()

            def cast_rows(i):
                at = rows_of(i, 256)
                cast[2, :, at] = down_wide[at].T.astype(bf16)

            looped(shard_units // 256, cast_rows)

        shadows = [lambda: cast_wide(0), lambda: cast_wide(1), cast_turned]
        for step in range(1, n - 1):
            for item in order:
                hops[step - 1, item].wait_recv()
                hop(step, item)
            if step <= chips - 1:
                row_copies[step - 1].wait_recv()
                source = lax.rem(g.chip_at - step + chips, chips) * 2 + g.core_at
                row_copies.append(row_copy(chips - 1 + step, source, tensor_peer(0, 1)))
            if shadows:
                shadows.pop(0)()

        def cut(s):
            return cast.at[:, :, rows_of(g.outer_flip(g.outer_at, s), units)]

        z_copies = {
            s: remote(cut(s), pieces[0][s], s_z.at[s], r_z.at[s], dp_peer(s, 0)) for s in steps
        }
        own = fetch(cut(0), pieces[0][0], 0)
        y_copies = {}

        def pass_on(j, s):
            src = cut(0) if (j, s) == (1, 0) else pieces[j - 1][s]
            y_copies[j, s] = remote(src, pieces[j][s], s_y.at[j, s], r_y.at[j, s], dp_peer(0, 1))

        if inner > 1:
            pass_on(1, 0)
        duties = []
        for s in steps:

            def duty(s=s):
                z_copies[s].wait_recv()
                if inner > 1:
                    pass_on(1, s)

            duties.append(duty)
        for j in range(2, inner):
            for s in [0] + steps:

                def duty(j=j, s=s):
                    y_copies[j - 1, s].wait_recv()
                    pass_on(j, s)

                duties.append(duty)

        def next_duty():
            if duties:
                duties.pop(0)()

        for item in order:
            hops[n - 2, item].wait_recv()
        for copy in row_copies[chips - 1 :]:
            copy.wait_recv()
        for copy in kept:
            copy.wait()
        outs = [fetch(qkv_ref, qkv_out, 3), fetch(out_w_ref, flat_out, 4), fetch(seq_ref, seq_out, 5)]

        def spread(i):
            gain_rows[:, rows_of(i, slab)] = all_gains[i].astype(f32)[:8]

        looped(n, spread)

        def project(i):
            at = rows_of(i, tall)
            x = seq_ref[at]
            lane = lax.broadcasted_iota(jnp.int32, (tall, 128), 1)
            sums = jnp.zeros((tall, 128), f32)
            for c in range(2):
                value = dot(x, qkv_ref[c], ((1,), (0,)))
                hat_ref[c, at] = value
                sums = jnp.where(lane == c, jnp.sum(value * value, axis=1, keepdims=True), sums)
            v_low[at] = dot(x, qkv_ref[2], ((1,), (0,))).astype(bf16)
            square[:, at] = sums.T[:8]

        looped(length // tall, project)
        sq_copies = []
        for k in range(chips):
            for f in (0, 1):
                if (k, f) != (0, 0):
                    at = k * 2 + f - 1
                    sq_copies.append(
                        remote(square, squares.at[at], s_sq.at[at], r_sq.at[at], tensor_peer(k, f))
                    )
        for copy in sq_copies:
            copy.wait_recv()
        sign = jnp.where(lax.broadcasted_iota(jnp.int32, (tall, HEAD), 1) < HEAD // 2, -1.0, 1.0)

        def rotate(i):
            at = rows_of(i, tall)
            sums = square[:, at]
            for copy_at in range(tensor - 1):
                sums = sums + squares[copy_at, :, at]
            column = jnp.concatenate([sums, jnp.zeros((120, tall), f32)], axis=0).T
            scales = lax.rsqrt(column / width + norm_eps)
            scale_ref[at] = scales
            cosine, sine = cos_ref[at], sin_ref[at] * sign
            for c, low in ((0, q_low), (1, k_low)):
                hat = hat_ref[c, at] * scales[:, c : c + 1]
                hat_ref[c, at] = hat
                normed = hat * gain_rows[c : c + 1, rows_of(t_at, span)]
                for h in range(heads):
                    cols = slice(h * HEAD, (h + 1) * HEAD)
                    value = normed[:, cols]
                    turned = pltpu.roll(value, HEAD // 2, 1)
                    low[at, cols] = (value * cosine + turned * sine).astype(bf16)

        looped(length // tall, rotate)
        scale = HEAD ** (-0.5)
        top_ref[...] = jnp.full((8, 128), masked_value, f32)
        for h in range(heads):
            cols = slice(h * HEAD, (h + 1) * HEAD)

            def attend(i, best, cols=cols, h=h):
                at = rows_of(i, tall)
                raw = dot(q_low[at, cols], k_low[:, cols], ((1,), (1,))) * scale
                masked = jnp.where(id_row[...] <= id_col[at], raw, masked_value)
                top = jnp.max(masked, axis=1, keepdims=True)
                weight = jnp.exp(masked - top)
                total = jnp.sum(weight, axis=1, keepdims=True)
                probs = (weight / total).astype(bf16)
                context[at, cols] = dot(probs, v_low[:, cols], ((1,), (0,))).astype(bf16)
                lse_ref[at, h : h + 1] = top + jnp.log(total)
                return jnp.maximum(best, jnp.max(top, axis=0, keepdims=True))

            best = lax.fori_loop(
                0, length // tall, attend, jnp.full((1, 1), masked_value, f32)
            )
            top_ref[h : h + 1] = jnp.broadcast_to(best, (1, 128))
        next_duty()

        def out_rows(k, flip, store):
            chip = lax.rem(g.chip_at + k, chips)
            core = 1 - g.core_at if flip else g.core_at
            at = rows_of(chip * 2 + core, count)

            def columns(i):
                cols = rows_of(i, tile)
                store(cols, dot(context[at], out_w_ref[:, cols], ((1,), (0,))))

            looped(width // tile, columns)

        chip_order = list(range(1, chips)) + [0]
        core_copies, chip_copies = {}, {}
        for k in chip_order:

            def store(cols, value, k=k):
                core_send[k, :, cols] = value.astype(bf16)

            out_rows(k, True, store)
            core_copies[k] = remote(
                core_send.at[k], core_land.at[k], s_core.at[k], r_core.at[k], tensor_peer(0, 1)
            )
        for k in chip_order:

            def store(cols, value, k=k):
                hold[k, :, cols] = value

            out_rows(k, False, store)
            if k:
                core_copies[k].wait_recv()

                def add(i, k=k):
                    at = rows_of(i, lines)
                    chip_send[k - 1, at] = (hold[k, at] + core_land[k, at].astype(f32)).astype(bf16)

                looped(count // lines, add)
                chip_copies[k] = remote(
                    chip_send.at[k - 1], chip_land.at[k - 1], s_chip.at[k], r_chip.at[k], tensor_peer(k, 0)
                )
        next_duty()
        core_copies[0].wait_recv()
        for k in range(1, chips):
            chip_copies[k].wait_recv()

        def close(i):
            at = rows_of(i, lines)
            raw = hold[0, at] + core_land[0, at].astype(f32)
            for k in range(1, chips):
                raw = raw + chip_land[k - 1, at].astype(f32)
            scale_o = lax.rsqrt(jnp.mean(raw * raw, axis=1, keepdims=True) + norm_eps)
            hat = raw * scale_o
            attn_hat[at] = hat
            o_scale[at] = scale_o
            value = rows_ref[at].astype(f32) + hat * gain_rows[2:3]
            resid[at] = value
            resid_low[at] = value.astype(bf16)

        looped(count // lines, close)
        while duties:
            next_duty()
        own.wait()
        for key, copy in y_copies.items():
            if key[0] == inner - 1:
                copy.wait_recv()
        for copy in outs:
            copy.wait()
        sent = list(hops.values()) + row_copies + list(z_copies.values()) + list(y_copies.values()) + sq_copies
        for copy in sent + list(core_copies.values()) + list(chip_copies.values()):
            copy.wait_send()

    shape = jax.ShapeDtypeStruct
    anywhere = pl.BlockSpec(memory_space=pl.ANY)
    vmem = pl.BlockSpec(memory_space=pltpu.VMEM)
    sems = pltpu.SemaphoreType.DMA
    results = pl.pallas_call(
        kernel,
        out_shape=(shape((3, slab, units), bf16),) * parts
        + (
            shape((lead, width, span), bf16),
            shape((span, width), bf16),
            shape((length, width), bf16),
            shape((8, width), f32),
            shape((2, length, span), f32),
            shape((length, 128), f32),
            shape((length, span), bf16),
            shape((length, span), bf16),
            shape((length, span), bf16),
            shape((length, heads), f32),
            shape((length, span), bf16),
            shape((count, width), f32),
            shape((count, 1), f32),
            shape((count, width), f32),
            shape((count, width), bf16),
            shape((8, 128), f32),
        ),
        in_specs=[anywhere] * 6 + [vmem] * 5,
        out_specs=(anywhere,) * (parts + 3) + (vmem,) * 13,
        scratch_shapes=[
            pltpu.VMEM((lead, width, span), bf16),
            pltpu.VMEM((span, width), bf16),
            pltpu.VMEM((length, width), bf16),
            pltpu.VMEM((n,) + gains.shape, bf16),
            pltpu.VMEM(w_gu.shape, f32),
            pltpu.VMEM(w_down.shape, f32),
            pltpu.VMEM((3, slab, shard_units), bf16),
            pltpu.VMEM((8, length), f32),
            pltpu.VMEM((tensor - 1, 8, length), f32),
            pltpu.VMEM((chips, count, width), bf16),
            pltpu.VMEM((chips, count, width), bf16),
            pltpu.VMEM((chips, count, width), f32),
            pltpu.VMEM((max(chips - 1, 1), count, width), bf16),
            pltpu.VMEM((max(chips - 1, 1), count, width), bf16),
            sems((n - 1, ring)),
            sems((n - 1, ring)),
            sems((2 * chips - 1,)),
            sems((2 * chips - 1,)),
            sems((outer,)),
            sems((outer,)),
            sems((inner, outer)),
            sems((inner, outer)),
            sems((tensor - 1,)),
            sems((tensor - 1,)),
            sems((chips,)),
            sems((chips,)),
            sems((chips,)),
            sems((chips,)),
            sems((7,)),
        ],
        compiler_params=pltpu.CompilerParams(
            collective_id=0, has_side_effects=True, vmem_limit_bytes=58 * 2**20
        ),
    )(
        shard, flat, gains, rows, w_gu, w_down, tables[0], tables[1],
        blocks[:, None], blocks[None, :], rows,
    )
    pieces = [results[j * outer : (j + 1) * outer] for j in range(inner)]
    return pieces, results[parts:]


def unit_kernel_call(rows_low, resid, cotangent, gain, pieces):
    grid = Grid()
    outer, chips, inner = grid.outer, grid.chips, grid.inner
    total_rows, width = rows_low.shape
    units = pieces[0][0].shape[2]
    slab = pieces[0][0].shape[1]
    flat_pieces = [piece for row in pieces for piece in row]
    parts = len(flat_pieces)
    halves = 2
    count = total_rows // halves
    both = 2 * count
    per = min(2, chips)
    groups = chips // per
    blocks = outer * groups
    tall = per * both
    held = per if groups > 1 else max(per - 1, 1)
    links = outer * (chips - 1)
    steps = list(range(outer))
    order = [(s, i) for s in steps for i in range(groups)]
    tile = 512
    wide_tiles = width // tile
    unit_tile = min(256, units)
    lines = 32
    bf16, f32 = jnp.bfloat16, jnp.float32
    mesh_id = pl.DeviceIdType.MESH

    def plan():
        chip_us, core_us, hop_us = 5.3, 0.6, 2.0
        free = {"x": 0.0, "core": 0.0, "z": 0.0}
        arrive, done, tasks = {}, {}, {}

        def send(link, when, us):
            free[link] = max(free[link], when) + us
            return free[link] + hop_us

        def add(name, needs, us, after=None):
            tasks[name] = (needs, us, after)

        def go(p, h):
            def then(now):
                for s in steps[1:]:
                    arrive["z", p, h, s] = send("z", now, 4.0 if s == 1 else 8.5)
                for k in range(1, chips):
                    arrive["x", p, h, 0, k] = send("x", now, chip_us)
                arrive["c", p, h, 0, 0] = send("core", now, core_us)

            return then

        def zf(p, h, s):
            def then(now):
                for k in range(1, chips):
                    arrive["x", p, h, s, k] = send("x", now, chip_us)
                arrive["c", p, h, s, 0] = send("core", now, core_us)

            return then

        def xf(p, h, s, k):
            def then(now):
                arrive["c", p, h, s, k] = send("core", now, core_us)

            return then

        def compute(p, h, s, i):
            def then(now):
                arrive["cr", p, h, s, i] = send("core", now, per * core_us)

            return then

        def cr(p, h, s, i):
            def then(now):
                for k in range(i * per, i * per + per):
                    if k:
                        arrive["xr", p, h, s, k] = send("x", now, chip_us)

            return then

        def xr(p, h, s):
            def then(now):
                if s:
                    arrive["zr", p, h, s] = send("z", now, 4.0 if s == 1 else 8.5)

            return then

        for p in (0, 1):
            for h in range(halves):
                if p == 0:
                    needs = [("do", ("go", 0, h - 1))] if h else []
                else:
                    needs = [("do", ("between", h))]
                add(("go", p, h), needs, 0.2, go(p, h))
                for s in steps[1:]:
                    add(("zf", p, h, s), [("at", ("z", p, h, s))], 0.2, zf(p, h, s))
                for s in steps:
                    for k in range(1, chips):
                        add(("xf", p, h, s, k), [("at", ("x", p, h, s, k))], 0.2, xf(p, h, s, k))
                for n, (s, i) in enumerate(order):
                    needs = [("at", ("c", p, h, s, i * per + j)) for j in range(per)]
                    if n:
                        needs.append(("do", ("compute", p, h) + order[n - 1]))
                    add(("load", p, h, s, i), needs, 0.2)
                    needs = [("do", ("load", p, h, s, i))]
                    if n:
                        needs.append(("do", ("cr", p, h) + order[n - 1]))
                    add(("compute", p, h, s, i), needs, 3.2, compute(p, h, s, i))
                    needs = [("at", ("cr", p, h, s, i)), ("do", ("compute", p, h, s, i))]
                    add(("cr", p, h, s, i), needs, 0.5, cr(p, h, s, i))
                for s in steps:
                    needs = [("do", ("cr", p, h, s, 0))]
                    needs += [("at", ("xr", p, h, s, k)) for k in range(1, chips)]
                    add(("xr", p, h, s), needs, 0.4, xr(p, h, s))
                for s in steps[1:]:
                    needs = [("at", ("zr", p, h, s)), ("do", ("xr", p, h, 0))]
                    add(("zr", p, h, s), needs, 0.4)
        for h in range(halves):
            needs = [("do", ("zr", 0, h, s)) for s in steps[1:]] + [("do", ("xr", 0, h, 0))]
            add(("between", h), needs, 1.0)
        for n, (s, i) in enumerate(order):
            needs = [("do", ("compute", 1, h, s, i)) for h in range(halves)]
            if n:
                needs.append(("do", ("grads",) + order[n - 1]))
            add(("fetch", s, i), needs, 0.2)
            add(("grads", s, i), [("do", ("fetch", s, i))], 7.0)
        add(("write",), [("do", ("grads",) + order[-1])], 4.0)
        rank = {"compute": 1, "fetch": 2, "grads": 2, "write": 3}
        result = []
        now = 0.0
        while tasks:
            best = None
            for name, (needs, us, then) in tasks.items():
                ready = 0.0
                for kind, key in needs:
                    table = arrive if kind == "at" else done
                    if key not in table:
                        ready = None
                        break
                    ready = max(ready, table[key] + (1.0 if key[0] in ("load", "fetch") else 0.0))
                if ready is None:
                    continue
                key = (max(ready, now), rank.get(name[0], 0))
                if best is None or key < best[0]:
                    best = (key, name)
            (ready, _), name = best
            needs, us, then = tasks.pop(name)
            now = ready + us
            done[name] = now
            if then is not None:
                then(now)
            result.append(name)
        return result

    def kernel(*refs):
        piece_refs = refs[:parts]
        fixed = refs[parts : parts + 9]
        grad_refs = refs[parts + 9 : parts + 9 + 3 * inner]
        body(piece_refs, *fixed, grad_refs, *refs[parts + 9 + 3 * inner :])

    def body(
        piece_refs, rows_ref, resid_ref, cot_ref, gain_ref,
        out_ref, dres_ref, gain_out, all_x, all_dm, grad_refs,
        wg, wu, wd, buf, wide_buf, act, coef_gate, coef_up, d_gate, d_up, turned, acc_gate, acc_up, acc_down, stage,
        core_send, core_land, hold, keep, chip_send, chip_land, outer_send, outer_land, raw, d_mlp,
        s_outer, r_outer, s_chip, r_chip, s_core, r_core,
        s_core_sum, r_core_sum, s_chip_sum, r_chip_sum, s_outer_sum, r_outer_sum,
        local, local_own, local_wide, local_w, local_g,
    ):
        g = Grid()
        core_peer = (g.dp_at, g.chip_at * 2 + 1 - g.core_at)

        def chip_peer(k):
            return (g.dp_at, lax.rem(g.chip_at + k + chips, chips) * 2 + g.core_at)

        def outer_peer(s):
            return (g.outer_flip(g.outer_at, s) * inner + g.inner_at, g.tensor_at)

        greet(
            [core_peer]
            + [chip_peer(k) for k in range(1, chips)]
            + [outer_peer(s) for s in range(1, outer)]
        )

        def remote(src, dst, send, recv, peer):
            copy = pltpu.make_async_remote_copy(
                src_ref=src, dst_ref=dst, send_sem=send, recv_sem=recv,
                device_id=peer, device_id_type=mesh_id,
            )
            copy.start()
            return copy

        def fetch(src, dst, sem):
            copy = pltpu.make_async_copy(src, dst, sem)
            copy.start()
            return copy

        def dot(a, b, contract):
            return lax.dot_general(a, b, (contract, ((), ())), preferred_element_type=f32)

        def looped(total, make):
            lax.fori_loop(0, total, lambda i, c: (make(i), c)[1], 0)

        def by_lines(make):
            looped(count // lines, lambda i: make(pl.ds(pl.multiple_of(i * lines, lines), lines)))

        def by_tiles(make):
            looped(wide_tiles, lambda i: make(pl.ds(pl.multiple_of(i * tile, tile), tile)))

        weights = (wg, wu, wd)
        fetches = []

        def fetch_weights():
            for j in range(inner):
                for s in range(outer):
                    index = g.outer_flip(g.outer_at, s) * inner
                    index = index + lax.rem(g.inner_at - j + inner, inner)
                    span = pl.ds(pl.multiple_of(index * slab, slab), slab)
                    for c in range(3):
                        at = j * outer + s
                        fetches.append(
                            fetch(piece_refs[at].at[c], weights[c].at[span], local_w.at[at, c])
                        )

        mine, theirs = pl.ds(0, count), pl.ds(count, count)
        every = (all_x, all_dm)
        copies, sums, loads, own = {}, {}, {}, {}
        unsent = {(p, h): [] for p in (0, 1) for h in range(halves)}

        def track(p, h, copy):
            unsent[p, h].append(copy)
            return copy

        def core_copy(p, h, s, k, src):
            dst = every[p].at[h, s, k, theirs]
            copies["c", p, h, s, k] = track(
                p, h, remote(src, dst, s_core.at[p, h, s, k], r_core.at[p, h, s, k], core_peer)
            )

        def chip_copy(p, h, s, k, src):
            dst = every[p].at[h, s, k, mine]
            copies["x", p, h, s, k] = track(
                p, h, remote(src, dst, s_chip.at[p, h, s, k], r_chip.at[p, h, s, k], chip_peer(k))
            )

        def go(p, h):
            source = (rows_ref, d_mlp)[p].at[pl.ds(h * count, count)]
            for s in steps[1:]:
                dst = every[p].at[h, s, 0, mine]
                copies["z", p, h, s] = track(
                    p, h, remote(source, dst, s_outer.at[p, h, s], r_outer.at[p, h, s], outer_peer(s))
                )
            for k in range(1, chips):
                chip_copy(p, h, 0, k, source)
            core_copy(p, h, 0, 0, source)
            own[p, h] = fetch(source, every[p].at[h, 0, 0, mine], local_own.at[p, h])
            if p == 0 and h == 0:
                fetch_weights()

        def part_out(h, s, i, cols, part_sum):
            for j in range(per):
                own_rows = part_sum[j * both : j * both + count]
                if i * per + j == 0:
                    keep[h, s, :, cols] = own_rows
                else:
                    hold[h, min(j, held - 1), :, cols] = own_rows
                core_send[h, j, :, cols] = part_sum[j * both + count : (j + 1) * both].astype(bf16)

        def forward(h, unit, s, i):
            for j in range(units // unit_tile):
                cols = pl.ds(j * unit_tile, unit_tile)
                rows = buf[h].reshape(tall, width)
                gate = dot(rows, wg[:, cols], ((1,), (0,)))
                up = dot(rows, wu[:, cols], ((1,), (0,)))
                sigma = jax.nn.sigmoid(gate)
                silu = gate * sigma
                act[unit, h, :, cols] = (silu * up).astype(bf16)
                coef_up[unit, h, :, cols] = silu.astype(bf16)
                coef_gate[unit, h, :, cols] = (
                    up * sigma * (1.0 + gate * (1.0 - sigma))
                ).astype(bf16)
            by_tiles(
                lambda cols: part_out(h, s, i, cols, dot(act[unit, h], wd[cols, :], ((1,), (1,))))
            )

        def backward(h, unit, s, i):
            for j in range(units // unit_tile):
                cols = pl.ds(j * unit_tile, unit_tile)
                d_act = dot(buf[h].reshape(tall, width), wd[:, cols], ((1,), (0,)))
                d_gate[unit, h, :, cols] = (d_act * coef_gate[unit, h, :, cols].astype(f32)).astype(bf16)
                d_up[unit, h, :, cols] = (d_act * coef_up[unit, h, :, cols].astype(f32)).astype(bf16)

            def into(cols):
                part_sum = dot(d_gate[unit, h], wg[cols, :], ((1,), (1,)))
                part_sum = part_sum + dot(d_up[unit, h], wu[cols, :], ((1,), (1,)))
                part_out(h, s, i, cols, part_sum)

            by_tiles(into)

        def weight_grads(unit):
            first = unit == order[0][0] * groups + order[0][1]
            for left, right, acc in ((d_gate, 0, acc_gate), (d_up, 0, acc_up), (act, 1, acc_down)):
                turned[...] = left[unit].reshape(halves * tall, units).T

                def grads(cols, right=right, acc=acc):
                    rows = wide_buf[right, :, :, :, cols].reshape(halves * tall, tile)
                    value = dot(turned[...], rows, ((1,), (0,)))
                    acc[:, cols] = value if first else acc[:, cols] + value

                by_tiles(grads)

        def between(h):
            def lines_of(i, total):
                at_rows = pl.ds(pl.multiple_of(h * count + i * lines, lines), lines)
                value = raw[at_rows]
                scale = lax.rsqrt(jnp.mean(value * value, axis=1, keepdims=True) + norm_eps)
                hat = value * scale
                gain_row = gain_ref[3:4]
                out_ref[at_rows] = (resid_ref[at_rows] + hat * gain_row).astype(bf16)
                top = cot_ref[at_rows].astype(f32)
                upstream = top * gain_row
                mean = jnp.mean(upstream * hat, axis=1, keepdims=True)
                d_mlp[at_rows] = (scale * (upstream - hat * mean)).astype(bf16)
                return total + jnp.sum(top * hat, axis=0, keepdims=True)

            zero = jnp.zeros((1, width), f32)
            total = lax.fori_loop(0, count // lines, lines_of, zero)
            gain_out[...] = total if h == 0 else gain_out[...] + total

        def write_grads():
            batches = []
            for j in range(inner):
                for s in range(outer):
                    index = g.outer_flip(g.outer_at, s) * inner
                    index = index + lax.rem(g.inner_at + j, inner)
                    span = pl.ds(pl.multiple_of(index * slab, slab), slab)
                    slot = len(batches) % 2
                    if len(batches) >= 2:
                        for copy in batches[-2]:
                            copy.wait()
                    batch = []
                    for c, acc in enumerate((acc_gate, acc_up, acc_down)):
                        stage[slot, c] = acc[:, span].astype(bf16)
                        batch.append(
                            fetch(stage.at[slot, c], grad_refs[j * 3 + c].at[s], local_g.at[slot, c])
                        )
                    batches.append(batch)
            for batch in batches[-2:]:
                for copy in batch:
                    copy.wait()

        def core_sum(p, h, s, i):
            unit = s * groups + i
            sums["c", p, h, unit].wait_recv()
            for j in range(per):
                chip = i * per + j
                if chip == 0:

                    def add(at_rows):
                        keep[h, s, at_rows] = keep[h, s, at_rows] + core_land[h, unit, j, at_rows].astype(f32)

                    by_lines(add)
                    continue
                there = s * (chips - 1) + chip - 1

                def add(at_rows):
                    total = hold[h, min(j, held - 1), at_rows] + core_land[h, unit, j, at_rows].astype(f32)
                    chip_send[h, there, at_rows] = total.astype(bf16)

                by_lines(add)
                sums["x", p, h, s, chip] = track(
                    p, h,
                    remote(
                        chip_send.at[h, there], chip_land.at[h, there],
                        s_chip_sum.at[p, h, there], r_chip_sum.at[p, h, there], chip_peer(-chip),
                    ),
                )

        def chip_sum(p, h, s):
            for k in range(1, chips):
                sums["x", p, h, s, k].wait_recv()

            def add(at_rows):
                total = keep[h, s, at_rows]
                for k in range(1, chips):
                    total = total + chip_land[h, s * (chips - 1) + k - 1, at_rows].astype(f32)
                if s == 0:
                    raw[pl.ds(pl.multiple_of(h * count + at_rows.start, lines), lines)] = total
                else:
                    outer_send[h, s - 1, at_rows] = total.astype(bf16)

            by_lines(add)
            if s:
                sums["z", p, h, s] = track(
                    p, h,
                    remote(
                        outer_send.at[h, s - 1], outer_land.at[h, s - 1],
                        s_outer_sum.at[p, h, s], r_outer_sum.at[p, h, s], outer_peer(s),
                    ),
                )

        def outer_sum(p, h, s):
            sums["z", p, h, s].wait_recv()

            def add(at_rows):
                there = pl.ds(pl.multiple_of(h * count + at_rows.start, lines), lines)
                raw[there] = raw[there] + outer_land[h, s - 1, at_rows].astype(f32)

            by_lines(add)

        def all_sent(p, h):
            for copy in unsent[p, h]:
                copy.wait_send()

        last_core = {}
        for task in plan():
            name, args = task[0], task[1:]
            if name == "go":
                go(*args)
            elif name == "zf":
                p, h, s = args
                copies["z", p, h, s].wait_recv()
                source = every[p].at[h, s, 0, mine]
                for k in range(1, chips):
                    chip_copy(p, h, s, k, source)
                core_copy(p, h, s, 0, source)
            elif name == "xf":
                p, h, s, k = args
                copies["x", p, h, s, k].wait_recv()
                core_copy(p, h, s, k, every[p].at[h, s, k, mine])
            elif name == "load":
                p, h, s, i = args
                for j in range(per):
                    copies["c", p, h, s, i * per + j].wait_recv()
                if (s, i) == order[0]:
                    own[p, h].wait()
                src = every[p].at[h, s, pl.ds(i * per, per)]
                loads[args] = fetch(src, buf.at[h], local.at[p, h, s * groups + i])
            elif name == "compute":
                p, h, s, i = args
                unit = s * groups + i
                if p == 0 and not loads.get("weights"):
                    loads["weights"] = True
                    for copy in fetches:
                        copy.wait()
                loads[args].wait()
                if h in last_core:
                    last_core[h].wait_send()
                (forward, backward)[p](h, unit, s, i)
                last_core[h] = remote(
                    core_send.at[h], core_land.at[h, unit],
                    s_core_sum.at[p, h, unit], r_core_sum.at[p, h, unit], core_peer,
                )
                sums["c", p, h, unit] = last_core[h]
            elif name == "cr":
                core_sum(*args)
            elif name == "xr":
                chip_sum(*args)
            elif name == "zr":
                outer_sum(*args)
            elif name == "between":
                all_sent(0, args[0])
                between(args[0])
            elif name == "fetch":
                s, i = args
                loads[task] = []
                for at, src in enumerate((all_x, all_dm)):
                    for h in range(halves):
                        loads[task].append(
                            fetch(
                                src.at[h, s, pl.ds(i * per, per)],
                                wide_buf.at[at, h],
                                local_wide.at[s * groups + i, at * halves + h],
                            )
                        )
            elif name == "grads":
                for copy in loads[("fetch",) + args]:
                    copy.wait()
                weight_grads(args[0] * groups + args[1])
            elif name == "write":
                write_grads()

        looped(
            total_rows // lines,
            lambda i: close_rows(pl.ds(pl.multiple_of(i * lines, lines), lines), dres_ref, raw, cot_ref),
        )
        for h in range(halves):
            all_sent(1, h)
            last_core[h].wait_send()

    shape = jax.ShapeDtypeStruct
    anywhere = pl.BlockSpec(memory_space=pl.ANY)
    near = pl.BlockSpec(memory_space=pltpu.VMEM)
    sems = pltpu.SemaphoreType.DMA
    flops = 2 * 9 * halves * tall * blocks * width * units
    results = pl.pallas_call(
        kernel,
        out_shape=(
            shape((total_rows, width), bf16),
            shape((total_rows, width), f32),
            shape((1, width), f32),
            shape((halves, outer, chips, both, width), bf16),
            shape((halves, outer, chips, both, width), bf16),
        )
        + (shape((outer, units, slab), bf16),) * (3 * inner),
        in_specs=[anywhere] * (parts + 1) + [near] * 3,
        out_specs=(near, near, near) + (anywhere,) * (2 + 3 * inner),
        scratch_shapes=[
            pltpu.VMEM((width, units), bf16),
            pltpu.VMEM((width, units), bf16),
            pltpu.VMEM((width, units), bf16),
            pltpu.VMEM((halves, per, both, width), bf16),
            pltpu.VMEM((2, halves, per, both, width), bf16),
            pltpu.VMEM((blocks, halves, tall, units), bf16),
            pltpu.VMEM((blocks, halves, tall, units), bf16),
            pltpu.VMEM((blocks, halves, tall, units), bf16),
            pltpu.VMEM((blocks, halves, tall, units), bf16),
            pltpu.VMEM((blocks, halves, tall, units), bf16),
            pltpu.VMEM((units, halves * tall), bf16),
            pltpu.VMEM((units, width), f32),
            pltpu.VMEM((units, width), f32),
            pltpu.VMEM((units, width), f32),
            pltpu.VMEM((2, 3, units, slab), bf16),
            pltpu.VMEM((halves, per, count, width), bf16),
            pltpu.VMEM((halves, blocks, per, count, width), bf16),
            pltpu.VMEM((halves, held, count, width), f32),
            pltpu.VMEM((halves, outer, count, width), f32),
            pltpu.VMEM((halves, links, count, width), bf16),
            pltpu.VMEM((halves, links, count, width), bf16),
            pltpu.VMEM((halves, outer - 1, count, width), bf16),
            pltpu.VMEM((halves, outer - 1, count, width), bf16),
            pltpu.VMEM((total_rows, width), f32),
            pltpu.VMEM((total_rows, width), bf16),
            sems((2, halves, outer)),
            sems((2, halves, outer)),
            sems((2, halves, outer, chips)),
            sems((2, halves, outer, chips)),
            sems((2, halves, outer, chips)),
            sems((2, halves, outer, chips)),
            sems((2, halves, blocks)),
            sems((2, halves, blocks)),
            sems((2, halves, links)),
            sems((2, halves, links)),
            sems((2, halves, outer)),
            sems((2, halves, outer)),
            sems((2, halves, blocks)),
            sems((2, halves)),
            sems((blocks, 2 * halves)),
            sems((parts, 3)),
            sems((2, 3)),
        ],
        compiler_params=pltpu.CompilerParams(
            collective_id=2, has_side_effects=True, vmem_limit_bytes=62 * 2**20
        ),
        cost_estimate=pl.CostEstimate(flops=flops, bytes_accessed=64 * 2**20, transcendentals=0),
    )(*flat_pieces, rows_low, resid, cotangent, gain)
    grads = results[5:]
    return results[:3] + ([[grads[j * 3 + c] for j in range(inner)] for c in range(3)],)


def close_rows(at_rows, dres_ref, raw, cot_ref):
    dres_ref[at_rows] = raw[at_rows] + cot_ref[at_rows].astype(jnp.float32)


def adam_kernel(turned, w_ref, m_ref, v_ref, g_ref, *rest):
    scale_ref = rest[0] if len(rest) == 5 else None
    w_out, m_out, v_out, c_out = rest[-4:]
    grad = g_ref[...].T if turned else g_ref[...]
    new, first, second = adam_step(
        w_ref[...], grad, m_ref[...], v_ref[...], rate_matrix, weight_decay
    )
    if scale_ref is not None:
        new = new * scale_ref[...]
    w_out[...] = new
    m_out[...] = first
    v_out[...] = second
    c_out[...] = new.astype(jnp.bfloat16)


def adam_call(param, grads, at, first, second, scale=None):
    mats, rows, columns = param.shape
    turned = scale is not None
    spec = pl.BlockSpec((None, rows, columns), lambda k: (k, 0, 0))
    grad_spec = pl.BlockSpec((None,) + grads.shape[1:], lambda k: (at + k, 0, 0))
    specs = [spec] * 3 + [grad_spec]
    values = [param, first, second, grads]
    if turned:
        values.append(scale)
        specs.append(pl.BlockSpec((None, 1, columns), lambda k: (k, 0, 0)))
    outs = [jax.ShapeDtypeStruct(param.shape, jnp.float32)] * 3
    outs.append(jax.ShapeDtypeStruct(param.shape, jnp.bfloat16))
    size = param.size
    return pl.pallas_call(
        functools.partial(adam_kernel, turned),
        grid=(mats,),
        in_specs=specs,
        out_specs=[spec] * 4,
        out_shape=outs,
        cost_estimate=pl.CostEstimate(
            flops=20 * size, bytes_accessed=28 * size, transcendentals=2 * size
        ),
        compiler_params=pltpu.CompilerParams(vmem_limit_bytes=32 * 2**20),
    )(*values)


def adam_units_kernel(turned, at_ref, w_ref, m_ref, v_ref, g_ref, w_out, m_out, v_out, c_out):
    grad = g_ref[...].astype(jnp.float32)
    if turned:
        grad = grad.T
    new, first, second = adam_step(
        w_ref[...], grad, m_ref[...], v_ref[...], rate_matrix, weight_decay
    )
    w_out[...] = new
    m_out[...] = first
    v_out[...] = second
    c_out[...] = new.astype(jnp.bfloat16)


def adam_units(grid, param, first, second, grads, turned):
    n = grid.outer
    stacked = jnp.stack([jnp.stack(list(pieces)) for pieces in grads])
    mats, _, units, wide = stacked.shape
    if not turned:
        spec = pl.BlockSpec((units, wide), lambda c, k, at: (k, 0))
    else:
        spec = pl.BlockSpec((None, wide, units), lambda c, k, at: (c, 0, k))
    grad_spec = pl.BlockSpec(
        (None, None, units, wide), lambda c, k, at: (c, lax.bitwise_xor(at[0], k), 0, 0)
    )
    size = param.size
    outs = [jax.ShapeDtypeStruct(param.shape, jnp.float32)] * 3
    outs.append(jax.ShapeDtypeStruct(param.shape, jnp.bfloat16))
    return pl.pallas_call(
        functools.partial(adam_units_kernel, turned),
        grid_spec=pltpu.PrefetchScalarGridSpec(
            num_scalar_prefetch=1,
            grid=(mats, n),
            in_specs=[spec] * 3 + [grad_spec],
            out_specs=[spec] * 4,
        ),
        out_shape=outs,
        cost_estimate=pl.CostEstimate(
            flops=20 * size, bytes_accessed=28 * size, transcendentals=2 * size
        ),
        compiler_params=pltpu.CompilerParams(vmem_limit_bytes=32 * 2**20),
    )(grid.outer_at.astype(jnp.int32)[None], param, first, second, stacked)


def local(
    tokens,
    cotangent,
    block_ids,
    w_qkv,
    m_qkv,
    v_qkv,
    w_out,
    m_out,
    v_out,
    w_gu,
    m_gu,
    v_gu,
    w_down,
    m_down,
    v_down,
    gains,
    gain_m,
    gain_v,
):
    grid = Grid()
    local_x = tokens[0]
    gain_count = gains.shape[0]
    low_gains = jnp.pad(gains.astype(jnp.bfloat16), ((0, 16 - gain_count), (0, 0)))
    tables = rope_tables(local_x.shape[0] * grid.tensor, HEAD)
    pieces, kept = open_call(
        w_qkv.astype(jnp.bfloat16),
        w_out.astype(jnp.bfloat16),
        low_gains,
        local_x,
        w_gu,
        w_down,
        tables,
        block_ids[0],
    )
    full_qkv, full_out, seq_x, gain_rows = kept[:4]
    hats, scales, q_low, k_low, v_low, log_total, context_low = kept[4:11]
    attn_hat, o_scale, resid, resid_low, tops = kept[11:]
    output, d_resid, gain_last, unit_grads = unit_kernel_call(
        resid_low, resid, cotangent[0], gain_rows, pieces
    )
    backs, (part, part_gains, tops, grad_tokens) = attend_back_call(
        d_resid,
        attn_hat,
        o_scale,
        gain_rows,
        full_out,
        context_low,
        q_low,
        k_low,
        v_low,
        log_total,
        hats,
        scales,
        tables,
        block_ids[0],
        seq_x,
        full_qkv,
        gain_last,
        tops,
        unit_grads,
    )
    part_gains = part_gains[:gain_count]
    head_top = tops[: w_qkv.shape[2] // HEAD, 0]
    factor = clip_tau / jnp.maximum(head_top, clip_tau)
    column = jnp.repeat(jnp.sqrt(factor), HEAD)
    column_scale = jnp.stack([column, column, jnp.ones_like(column)])[:, None, :]
    new_qkv, new_m_qkv, new_v_qkv, copy_qkv = adam_call(w_qkv, part, 0, m_qkv, v_qkv, column_scale)
    new_out, new_m_out, new_v_out, copy_out = [
        v[0] for v in adam_call(w_out[None], part, 3, m_out[None], v_out[None])
    ]
    new_gu, new_m_gu, new_v_gu, copy_gu = adam_units(grid, w_gu, m_gu, v_gu, backs[:2], True)
    new_down, new_m_down, new_v_down, copy_down = adam_units(
        grid, w_down, m_down, v_down, backs[2:], False
    )
    new_gains, new_gain_m, new_gain_v = adam_step(gains, part_gains, gain_m, gain_v, rate_gain, 0.0)
    return (
        output[None],
        grad_tokens[None],
        new_qkv,
        new_m_qkv,
        new_v_qkv,
        copy_qkv,
        new_out,
        new_m_out,
        new_v_out,
        copy_out,
        new_gu,
        new_m_gu,
        new_v_gu,
        copy_gu,
        new_down,
        new_m_down,
        new_v_down,
        copy_down,
        new_gains,
        new_gain_m,
        new_gain_v,
        factor,
    )


def solution(mesh):
    return jax.shard_map(
        local,
        mesh=mesh,
        in_specs=(
            P("dp", "tensor", None),
            P("dp", "tensor", None),
            P("dp", None),
            P(None, "dp", "tensor"),
            P(None, "dp", "tensor"),
            P(None, "dp", "tensor"),
            P("tensor", "dp"),
            P("tensor", "dp"),
            P("tensor", "dp"),
            P(None, "dp", "tensor"),
            P(None, "dp", "tensor"),
            P(None, "dp", "tensor"),
            P("tensor", "dp"),
            P("tensor", "dp"),
            P("tensor", "dp"),
            P(None, "dp"),
            P(None, "dp"),
            P(None, "dp"),
        ),
        out_specs=(
            P("dp", "tensor", None),
            P("dp", "tensor", None),
            P(None, "dp", "tensor"),
            P(None, "dp", "tensor"),
            P(None, "dp", "tensor"),
            P(None, "dp", "tensor"),
            P("tensor", "dp"),
            P("tensor", "dp"),
            P("tensor", "dp"),
            P("tensor", "dp"),
            P(None, "dp", "tensor"),
            P(None, "dp", "tensor"),
            P(None, "dp", "tensor"),
            P(None, "dp", "tensor"),
            P("tensor", "dp"),
            P("tensor", "dp"),
            P("tensor", "dp"),
            P("tensor", "dp"),
            P(None, "dp"),
            P(None, "dp"),
            P(None, "dp"),
            P("tensor"),
        ),
        check_vma=False,
    )
```

```python
import functools

import jax
import jax.numpy as jnp
import numpy as np
from jax import lax
from jax.experimental import pallas as pl
from jax.experimental.pallas import tpu as pltpu
from jax.sharding import PartitionSpec as P

HEAD = 128
STEP = 5


norm_eps = 1e-06
rope_base = 500000.0
beta_one = 0.9
beta_two = 0.95
rate_matrix = 0.01
rate_gain = 0.6
weight_decay = 0.1
adam_eps = 1e-08
clip_tau = 9.0
masked_value = -1e30


def rope_tables(length, size):
    half = size // 2
    freq = np.float32(rope_base) ** (-(np.arange(half, dtype=np.float32) * np.float32(2.0 / size)))
    angle = np.arange(length, dtype=np.float32)[:, None] * freq[None, :]
    angle = np.concatenate([angle, angle], axis=1)
    return (jnp.asarray(np.cos(angle)), jnp.asarray(np.sin(angle)))


def adam_step(param, grad, first, second, rate, decay):
    first = beta_one * first + (1.0 - beta_one) * grad
    second = beta_two * second + (1.0 - beta_two) * grad * grad
    fix_one = 1.0 - beta_one**STEP
    fix_two = 1.0 - beta_two**STEP
    update = first / fix_one / (jnp.sqrt(second / fix_two) + adam_eps)
    return (param - rate * (update + decay * param), first, second)


class Grid:
    def __init__(self):
        self.dp = lax.axis_size("dp")
        self.tensor = lax.axis_size("tensor")
        self.inner = 1
        while self.inner * self.inner * 4 <= self.dp:
            self.inner *= 2
        self.outer = self.dp // self.inner
        self.chips = self.tensor // 2
        self.dp_at = lax.axis_index("dp")
        self.tensor_at = lax.axis_index("tensor")
        self.inner_at = self.dp_at % self.inner
        self.chip_at = self.tensor_at // 2
        self.core_at = self.tensor_at % 2
        self.outer_at = self.dp_at // self.inner

    def path_of(self, index):
        column, row = index // self.inner, index % self.inner
        return row * self.outer + column + (row % 2) * (self.outer - 1 - 2 * column)

    def outer_flip(self, index, step):
        result = 0
        for bit in bits(self.outer):
            side = index // bit % 2
            result = result + bit * (1 - side if step & bit else side)
        return result

    def index_of(self, place):
        row, column = place // self.outer, place % self.outer
        return (column + (row % 2) * (self.outer - 1 - 2 * column)) * self.inner + row


def bits(count):
    return [1 << k for k in range(count.bit_length() - 1)]


def greet(peers):
    barrier = pltpu.get_barrier_semaphore()
    for peer in peers:
        pl.semaphore_signal(barrier, inc=1, device_id=peer, device_id_type=pl.DeviceIdType.MESH)
    pl.semaphore_wait(barrier, len(peers))


def attend_back_call(
    d_resid, attn_hat, o_scale, gain_rows, full_out, context, q_low, k_low, v_low, lse, hats, scales,
    tables, blocks, seq, full_qkv, gain_last, tops, unit_grads,
):
    grid = Grid()
    n, outer, inner, chips, tensor = grid.dp, grid.outer, grid.inner, grid.chips, grid.tensor
    count, width = d_resid.shape
    length, span = context.shape
    heads = span // HEAD
    units, slab = unit_grads[0][0].shape[1:]
    thin = width // n
    half = span // 2
    tall = min(256, length)
    tile = 512
    lines = 32
    ring = 8 + 2
    gain_item, top_item = 8, 9
    bf16, f32 = jnp.bfloat16, jnp.float32
    mesh_id = pl.DeviceIdType.MESH
    flat_grads = [unit_grads[c][j] for j in range(inner) for c in range(3)]
    some = len(flat_grads)
    z_steps = list(range(1, outer))

    def kernel(*refs):
        fixed, far_in, grads_in = refs[:17], refs[17:20], refs[20 : 20 + some]
        rest = refs[20 + some :]
        backs = [rest[c * outer : (c + 1) * outer] for c in range(3)]
        body(*fixed, far_in, grads_in, backs, *rest[3 * outer :])

    def body(
        dres_ref, hat_ref, o_scale_ref, gain_ref, out_w, ctx, q_ref, k_ref, v_ref, lse_ref, scale_ref,
        cos_ref, sin_ref, id_col, id_row, last_ref, tops_ref, far_in, grads_in,
        backs, part_ref, gains_out, tops_out, tokens_out,
        hats, seq, qkv_w, seq_do, d_ctx, d_q, d_k, d_v, d_low, whole, terms, row_terms, turned,
        land, land_gain, land_top, own_gain, peer_gain, inners, peer_inners,
        grad_own, grad_land, grad_sum, core_send, core_land, hold, chip_send, chip_land,
        s_ring, r_ring, s_row, r_row, s_in, r_in, s_y, r_y, s_z, r_z, s_core, r_core, s_chip, r_chip, s_gain, r_gain, local,
    ):
        hats_in, seq_in, qkv_in = far_in
        g = Grid()

        def tensor_peer(k, flip):
            core = 1 - g.core_at if flip else g.core_at
            return (g.dp_at, lax.rem(g.chip_at + k + chips, chips) * 2 + core)

        def dp_peer(s, j):
            across = g.outer_flip(g.outer_at, s) * inner
            return (across + lax.rem(g.inner_at + j + inner, inner), g.tensor_at)

        place = g.path_of(g.dp_at)
        after_dp = (g.index_of(lax.rem(place + 1, n)), g.tensor_at)
        before_dp = (g.index_of(lax.rem(place + n - 1, n)), g.tensor_at)
        near = [tensor_peer(k, f) for k in range(chips) for f in (0, 1) if (k, f) != (0, 0)]
        far = [dp_peer(s, 0) for s in range(1, outer)] + [dp_peer(0, j) for j in range(1, inner)]
        greet(near + far + [after_dp, before_dp])

        def remote(src, dst, send, recv, peer):
            copy = pltpu.make_async_remote_copy(
                src_ref=src, dst_ref=dst, send_sem=send, recv_sem=recv,
                device_id=peer, device_id_type=mesh_id,
            )
            copy.start()
            return copy

        def fetch(src, dst, at):
            copy = pltpu.make_async_copy(src, dst, local.at[at])
            copy.start()
            return copy

        def dot(a, b, contract):
            return lax.dot_general(a, b, (contract, ((), ())), preferred_element_type=f32)

        def looped(total, make):
            lax.fori_loop(0, total, lambda i, c: (make(i), c)[1], 0)

        def rows_of(i, size):
            return pl.ds(pl.multiple_of(i * size, size), size)

        sent = []
        y_copies = {}
        sum_steps = [(c, s) for c in range(3) for s in z_steps + [0]]
        for c, s in sum_steps:
            for j in range(1, inner):
                copy = remote(
                    grads_in[j * 3 + c].at[s],
                    grad_land.at[j - 1, c, s],
                    s_y.at[j, c, s],
                    r_y.at[j, c, s],
                    dp_peer(0, j),
                )
                y_copies[j, c, s] = copy
                sent.append(copy)
        own_grads = [fetch(grads_in[c], grad_own.at[c], c) for c in range(3)]
        fetched = [fetch(hats_in, hats, 3), fetch(seq_in, seq, 4), fetch(qkv_in, qkv_w, 5)]
        z_copies = []
        keeps = []

        def unit_sums(times):
            for _ in range(times):
                if sum_steps:
                    unit_sum(*sum_steps.pop(0))

        def unit_sum(c, s):
            if s == (z_steps + [0])[0]:
                own_grads[c].wait()
            for j in range(1, inner):
                y_copies[j, c, s].wait_recv()

            def add(i):
                rows = rows_of(i, 64)
                total = grad_own[c, s, rows].astype(f32)
                for j in range(1, inner):
                    total = total + grad_land[j - 1, c, s, rows].astype(f32)
                grad_sum[c, s, rows] = total.astype(bf16)

            looped(units // 64, add)
            if s:
                z_copies.append(
                    remote(grad_sum.at[c, s], backs[c][s], s_z.at[c, s], r_z.at[c, s], dp_peer(s, 0))
                )
            else:
                keeps.append(fetch(grad_sum.at[c, 0], backs[c][0], 6 + c))

        t_at = g.tensor_at
        mine = rows_of(t_at, count)

        def open_rows(i, total):
            at = rows_of(i, lines)
            value, hat = dres_ref[at], hat_ref[at]
            upstream = value * gain_ref[2:3]
            mean = jnp.mean(upstream * hat, axis=1, keepdims=True)
            d_attn = (o_scale_ref[at] * (upstream - hat * mean)).astype(bf16)
            seq_do[pl.ds(pl.multiple_of(t_at * count + i * lines, lines), lines)] = d_attn
            return total + jnp.sum(value * hat, axis=0, keepdims=True)

        gain_attn = lax.fori_loop(0, count // lines, open_rows, jnp.zeros((1, width), f32))
        row_terms[...] = jnp.zeros((8, width), f32)
        row_terms[2:3] = gain_attn
        row_terms[3:4] = last_ref[...]
        moves, passed = [], []

        def row_copy(slot, index, peer):
            at = rows_of(index, count)
            copy = remote(seq_do.at[at], seq_do.at[at], s_row.at[slot], r_row.at[slot], peer)
            sent.append(copy)
            return copy

        for k in range(1, chips):
            moves.append(row_copy(k - 1, t_at, tensor_peer(k, 0)))
        to_core = row_copy(chips - 1, t_at, tensor_peer(0, 1))
        unit_sums(2)
        for k in range(1, chips):
            moves[k - 1].wait_recv()
            source = lax.rem(g.chip_at - k + chips, chips) * 2 + g.core_at
            passed.append(row_copy(chips - 1 + k, source, tensor_peer(0, 1)))
        to_core.wait_recv()
        unit_sums(1)
        for copy in passed:
            copy.wait_recv()

        def context_grad(i):
            at = rows_of(i, tall)
            d_ctx[at] = dot(seq_do[at], out_w[...], ((1,), (1,))).astype(bf16)

        looped(length // tall, context_grad)
        unit_sums(1)

        scale = HEAD ** (-0.5)
        for h in range(heads):
            cols = slice(h * HEAD, (h + 1) * HEAD)

            def head(i, c, cols=cols, h=h):
                at = rows_of(i, tall)
                q_part, ctx_part = q_ref[at, cols], d_ctx[at, cols]
                raw = dot(q_part, k_ref[:, cols], ((1,), (1,))) * scale
                masked = jnp.where(id_row[...] <= id_col[at], raw, masked_value)
                probs = jnp.exp(masked - lse_ref[at, h : h + 1])
                d_probs = dot(ctx_part, v_ref[:, cols], ((1,), (1,)))
                mean = jnp.sum(probs * d_probs, axis=1, keepdims=True)
                d_scores = (probs * (d_probs - mean)).astype(bf16)
                d_q[at, cols] = dot(d_scores, k_ref[:, cols], ((1,), (0,))) * scale
                key = dot(d_scores, q_part, ((0,), (0,))) * scale
                value = dot(probs.astype(bf16), ctx_part, ((0,), (0,)))
                d_k[:, cols] = jnp.where(i == 0, key, d_k[:, cols] + key)
                d_v[:, cols] = jnp.where(i == 0, value, d_v[:, cols] + value)
                return c

            d_k[:, cols] = jnp.zeros((length, HEAD), f32)
            d_v[:, cols] = jnp.zeros((length, HEAD), f32)
            lax.fori_loop(0, length // tall, head, 0)
            unit_sums(1)
        fetched[0].wait()
        sign = jnp.where(lax.broadcasted_iota(jnp.int32, (tall, HEAD), 1) < HEAD // 2, -1.0, 1.0)

        def unrotate(i, sums):
            at = rows_of(i, tall)
            cosine, sine = cos_ref[at], sin_ref[at]
            lane = lax.broadcasted_iota(jnp.int32, (tall, 128), 1)
            columns = jnp.zeros((tall, 128), f32)
            result = []
            for c, grad in ((0, d_q), (1, d_k)):
                total = jnp.zeros((tall, 1), f32)
                terms_row = []
                for h in range(heads):
                    cols = slice(h * HEAD, (h + 1) * HEAD)
                    value = grad[at, cols]
                    back = value * cosine - pltpu.roll(value * sine, HEAD // 2, 1) * sign
                    hat = hats[c, at, cols]
                    terms_row.append(jnp.sum(back * hat, axis=0, keepdims=True))
                    at_head = pl.ds(pl.multiple_of(t_at * span + h * HEAD, HEAD), HEAD)
                    back = back * gain_ref[c : c + 1, at_head]
                    grad[at, cols] = back
                    total = total + jnp.sum(back * hat, axis=1, keepdims=True)
                columns = jnp.where(lane == c, total, columns)
                result.append(sums[c] + jnp.concatenate(terms_row, axis=1))
            inners[:, at] = columns.T[:8]
            return tuple(result)

        zero = jnp.zeros((1, span), f32)
        gain_q, gain_k = lax.fori_loop(0, length // tall, unrotate, (zero, zero))
        offset = rows_of(t_at, span)
        row_terms[0:1, offset] = gain_q
        row_terms[1:2, offset] = gain_k
        in_copies = []
        for k in range(chips):
            for f in (0, 1):
                if (k, f) != (0, 0):
                    at = k * 2 + f - 1
                    in_copies.append(
                        remote(inners, peer_inners.at[at], s_in.at[at], r_in.at[at], tensor_peer(k, f))
                    )
        sent.extend(in_copies)
        turned[...] = ctx[...].T

        def out_grad(i):
            cols = rows_of(i, tile)
            whole[3, :, cols] = dot(turned[...], seq_do[:, cols], ((1,), (0,))).astype(bf16)

        looped(width // tile, out_grad)
        for copy in in_copies:
            copy.wait_recv()
        unit_sums(1)

        def normed(i):
            at = rows_of(i, tall)
            sums = inners[:, at]
            for other in range(tensor - 1):
                sums = sums + peer_inners[other, :, at]
            column = jnp.concatenate([sums, jnp.zeros((120, tall), f32)], axis=0).T / width
            for c, grad in ((0, d_q), (1, d_k)):
                value = grad[at] - hats[c, at] * column[:, c : c + 1]
                d_low[c, at] = (scale_ref[at, c : c + 1] * value).astype(bf16)
            d_low[2, at] = d_v[at].astype(bf16)

        looped(length // tall, normed)
        fetched[1].wait()
        for c in range(3):
            turned[...] = d_low[c].T

            def weight_grad(i, c=c):
                cols = rows_of(i, tile)
                whole[c, :, cols] = dot(turned[...], seq[:, cols], ((1,), (0,))).astype(bf16)

            looped(width // tile, weight_grad)
            unit_sums(1)

        def place_terms(i, c):
            cols = pl.ds(pl.multiple_of(i * thin, thin), thin)
            terms[i] = row_terms[:, cols]
            return c

        lax.fori_loop(0, n, place_terms, 0)

        def way_of(item):
            return 1 if item >= 8 else 1 - 2 * (item // 4)

        def own(item, away):
            index = g.index_of(lax.rem(place - way_of(item) * away + 2 * n, n))
            if item == gain_item:
                return terms.at[index]
            if item == top_item:
                return tops_ref
            side, c = item // 4, item % 4
            return whole.at[c, pl.ds(side * half, half), rows_of(index, thin)]

        def landed(step, item):
            if item == gain_item:
                return land_gain.at[step]
            if item == top_item:
                return land_top.at[step]
            return land.at[step, item]

        hops = {}

        def hop(step, item):
            hops[step, item] = remote(
                own(item, 1) if step == 0 else landed(step - 1, item),
                landed(step, item),
                s_ring.at[step, item],
                r_ring.at[step, item],
                after_dp if way_of(item) == 1 else before_dp,
            )

        order = [gain_item, top_item] + [c + side * 4 for c in range(4) for side in (0, 1)]
        for item in order:
            hop(0, item)
        unit_sums(len(sum_steps))

        fetched[2].wait()
        chip_order = list(range(1, chips)) + [0]
        core_copies, chip_copies = {}, {}

        def token_rows(k, flip, store):
            chip = lax.rem(g.chip_at + k, chips)
            core = 1 - g.core_at if flip else g.core_at
            at = rows_of(chip * 2 + core, count)

            def columns(i):
                cols = rows_of(i, tile)
                total = dot(d_low[0, at], qkv_w[0, cols], ((1,), (1,)))
                for c in (1, 2):
                    total = total + dot(d_low[c, at], qkv_w[c, cols], ((1,), (1,)))
                store(cols, total)

            looped(width // tile, columns)

        duties = []
        for k in chip_order:

            def away(k=k):
                def store(cols, value):
                    core_send[k, :, cols] = value.astype(bf16)

                token_rows(k, True, store)
                core_copies[k] = remote(
                    core_send.at[k], core_land.at[k], s_core.at[k], r_core.at[k], tensor_peer(0, 1)
                )

            def here(k=k):
                def store(cols, value):
                    hold[k, :, cols] = value

                token_rows(k, False, store)

            def join(k=k):
                core_copies[k].wait_recv()

                def add(i):
                    at = rows_of(i, lines)
                    chip_send[k - 1, at] = (hold[k, at] + core_land[k, at].astype(f32)).astype(bf16)

                looped(count // lines, add)
                chip_copies[k] = remote(
                    chip_send.at[k - 1], chip_land.at[k - 1], s_chip.at[k], r_chip.at[k], tensor_peer(k, 0)
                )

            duties += [away, here] + ([join] if k else [])

        def close_tokens():
            core_copies[0].wait_recv()
            for k in range(1, chips):
                chip_copies[k].wait_recv()

            def close(i):
                at = rows_of(i, lines)
                total = dres_ref[at] + hold[0, at] + core_land[0, at].astype(f32)
                for k in range(1, chips):
                    total = total + chip_land[k - 1, at].astype(f32)
                tokens_out[at] = total

            looped(count // lines, close)

        duties.append(close_tokens)
        per_step = -(-len(duties) // (n - 2))
        for step in range(1, n):
            for item in order:
                hops[step - 1, item].wait_recv()
                here = landed(step - 1, item)
                if item == top_item:
                    summed = jnp.maximum(here[...], tops_ref[...])
                else:
                    summed = here[...].astype(f32) + own(item, step + 1)[...].astype(f32)
                if step < n - 1:
                    here[...] = summed.astype(here.dtype)
                    hop(step, item)
                elif item == gain_item:
                    own_gain[0] = summed
                elif item == top_item:
                    tops_out[...] = summed
                else:
                    side, c = item // 4, item % 4
                    part_ref[c, pl.ds(side * half, half)] = summed
            for _ in range(per_step):
                if duties:
                    duties.pop(0)()
        peers = [tensor_peer(0, 1)] + [tensor_peer(k, 0) for k in range(1, chips)]
        first = remote(own_gain.at[0], peer_gain.at[0], s_gain.at[0], r_gain.at[0], peers[0])
        first.wait_recv()
        own_gain[1] = own_gain[0] + peer_gain[0]
        others = [
            remote(own_gain.at[1], peer_gain.at[k], s_gain.at[k], r_gain.at[k], peers[k])
            for k in range(1, chips)
        ]
        result = own_gain[1]
        for k in range(1, chips):
            others[k - 1].wait_recv()
            result = result + peer_gain[k]
        gains_out[...] = result
        for copy in z_copies:
            copy.wait()
        for copy in keeps:
            copy.wait()
        for copy in sent + list(hops.values()) + list(core_copies.values()):
            copy.wait_send()
        for copy in list(chip_copies.values()) + [first] + others:
            copy.wait_send()

    shape = jax.ShapeDtypeStruct
    anywhere = pl.BlockSpec(memory_space=pl.ANY)
    vmem = pl.BlockSpec(memory_space=pltpu.VMEM)
    sems = pltpu.SemaphoreType.DMA
    results = pl.pallas_call(
        kernel,
        out_shape=(shape((units, slab), bf16),) * (3 * outer)
        + (
            shape((4, span, thin), f32),
            shape((8, thin), f32),
            shape(tops.shape, f32),
            shape((count, width), f32),
        ),
        in_specs=[vmem] * 17 + [anywhere] * 3 + [anywhere] * some,
        out_specs=(anywhere,) * (3 * outer) + (vmem,) * 4,
        scratch_shapes=[
            pltpu.VMEM(hats.shape, f32),
            pltpu.VMEM(seq.shape, bf16),
            pltpu.VMEM(full_qkv.shape, bf16),
            pltpu.VMEM((length, width), bf16),
            pltpu.VMEM((length, span), bf16),
            pltpu.VMEM((length, span), f32),
            pltpu.VMEM((length, span), f32),
            pltpu.VMEM((length, span), f32),
            pltpu.VMEM((3, length, span), bf16),
            pltpu.VMEM((4, span, width), bf16),
            pltpu.VMEM((n, 8, thin), f32),
            pltpu.VMEM((8, width), f32),
            pltpu.VMEM((span, length), bf16),
            pltpu.VMEM((n - 1, 8, half, thin), bf16),
            pltpu.VMEM((n - 1, 8, thin), f32),
            pltpu.VMEM((n - 1,) + tops.shape, f32),
            pltpu.VMEM((2, 8, thin), f32),
            pltpu.VMEM((chips, 8, thin), f32),
            pltpu.VMEM((8, length), f32),
            pltpu.VMEM((tensor - 1, 8, length), f32),
            pltpu.VMEM((3, outer, units, slab), bf16),
            pltpu.VMEM((max(inner - 1, 1), 3, outer, units, slab), bf16),
            pltpu.VMEM((3, outer, units, slab), bf16),
            pltpu.VMEM((chips, count, width), bf16),
            pltpu.VMEM((chips, count, width), bf16),
            pltpu.VMEM((chips, count, width), f32),
            pltpu.VMEM((max(chips - 1, 1), count, width), bf16),
            pltpu.VMEM((max(chips - 1, 1), count, width), bf16),
            sems((n - 1, ring)),
            sems((n - 1, ring)),
            sems((2 * chips - 1,)),
            sems((2 * chips - 1,)),
            sems((tensor - 1,)),
            sems((tensor - 1,)),
            sems((inner, 3, outer)),
            sems((inner, 3, outer)),
            sems((3, outer)),
            sems((3, outer)),
            sems((chips,)),
            sems((chips,)),
            sems((chips,)),
            sems((chips,)),
            sems((chips,)),
            sems((chips,)),
            sems((9,)),
        ],
        compiler_params=pltpu.CompilerParams(
            collective_id=1, has_side_effects=True, vmem_limit_bytes=62 * 2**20
        ),
    )(
        d_resid, attn_hat, o_scale, gain_rows, full_out, context, q_low, k_low, v_low, lse, scales,
        tables[0], tables[1], blocks[:, None], blocks[None, :], gain_last, tops,
        hats, seq, full_qkv, *flat_grads,
    )
    backs = [results[c * outer : (c + 1) * outer] for c in range(3)]
    return backs, results[3 * outer :]


def open_call(shard, flat, gains, rows, w_gu, w_down, tables, blocks):
    grid = Grid()
    n, outer, inner = grid.dp, grid.outer, grid.inner
    chips, tensor = grid.chips, grid.tensor
    count, width = rows.shape
    length = count * tensor
    lead, slab, span = shard.shape
    half = slab // 2
    part_tall = span // 2
    heads = span // HEAD
    shard_units = w_gu.shape[2]
    units = shard_units // outer
    parts = outer * inner
    ring = 2 * lead + 3
    steps = list(range(1, outer))
    tall = min(256, length)
    tile = 512
    lines = 32
    bf16, f32 = jnp.bfloat16, jnp.float32
    mesh_id = pl.DeviceIdType.MESH

    def kernel(*refs):
        pieces = [refs[11 + j * outer : 11 + (j + 1) * outer] for j in range(inner)]
        body(*refs[:11], pieces, *refs[11 + parts :])

    def body(
        shard_ref, flat_ref, gains_ref, rows_any, gu_any, down_any, cos_ref, sin_ref, id_col, id_row, rows_ref,
        pieces, qkv_out, flat_out, seq_out,
        gain_rows, hat_ref, scale_ref, q_low, k_low, v_low, lse_ref, context, attn_hat, o_scale, resid, resid_low, top_ref,
        qkv_ref, out_w_ref, seq_ref, all_gains, gu_wide, down_wide, cast,
        square, squares, core_send, core_land, hold, chip_send, chip_land,
        s_ring, r_ring, s_row, r_row, s_z, r_z, s_y, r_y, s_sq, r_sq, s_core, r_core, s_chip, r_chip, local,
    ):
        g = Grid()

        def tensor_peer(k, flip):
            core = 1 - g.core_at if flip else g.core_at
            return (g.dp_at, lax.rem(g.chip_at + k + chips, chips) * 2 + core)

        def dp_peer(s, j):
            across = g.outer_flip(g.outer_at, s) * inner
            return (across + lax.rem(g.inner_at + j + inner, inner), g.tensor_at)

        near = [tensor_peer(k, f) for k in range(chips) for f in (0, 1) if (k, f) != (0, 0)]
        far = [dp_peer(s, 0) for s in range(1, outer)]
        far += [dp_peer(0, j) for j in sorted({1 % inner, inner - 1} - {0})]
        t_at = g.tensor_at
        place = g.path_of(g.dp_at)
        after = (g.index_of(lax.rem(place + 1, n)), t_at)
        before = (g.index_of(lax.rem(place + n - 1, n)), t_at)
        greet(near + far + [after, before])

        def remote(src, dst, send, recv, peer):
            copy = pltpu.make_async_remote_copy(
                src_ref=src, dst_ref=dst, send_sem=send, recv_sem=recv,
                device_id=peer, device_id_type=mesh_id,
            )
            copy.start()
            return copy

        def dot(a, b, contract):
            return lax.dot_general(a, b, (contract, ((), ())), preferred_element_type=f32)

        def looped(total, make):
            lax.fori_loop(0, total, lambda i, c: (make(i), c)[1], 0)

        def rows_of(i, size):
            return pl.ds(pl.multiple_of(i * size, size), size)

        def fetch(src, dst, at):
            copy = pltpu.make_async_copy(src, dst, local.at[at])
            copy.start()
            return copy

        def views(item, index):
            if item == ring - 1:
                return 1, gains_ref, all_gains.at[index]
            if item >= 2 * lead:
                side = item - 2 * lead
                part = pl.ds(side * part_tall, part_tall)
                return 1 - 2 * side, flat_ref.at[part], out_w_ref.at[part, rows_of(index, slab)]
            side, c = item // lead, item % lead
            at = pl.ds(pl.multiple_of(index * slab + side * half, half), half)
            return 1 - 2 * side, shard_ref.at[c, pl.ds(side * half, half)], qkv_ref.at[c, at]

        hops = {}

        def hop(step, item):
            way = views(item, 0)[0]
            index = g.index_of(lax.rem(place - way * step + n, n))
            _, source, target = views(item, index)
            hops[step, item] = remote(
                source if step == 0 else target,
                target,
                s_ring.at[step, item],
                r_ring.at[step, item],
                after if way == 1 else before,
            )

        def row_copy(slot, index, peer, src=None):
            at = seq_ref.at[rows_of(index, count)]
            return remote(at if src is None else src, at, s_row.at[slot], r_row.at[slot], peer)

        order = [c + side * lead for c in range(lead) for side in (0, 1)]
        order += list(range(2 * lead, ring))
        for item in order:
            hop(0, item)
        row_copies = [
            row_copy(k - 1, t_at, tensor_peer(k, 0), rows_any) for k in range(1, chips)
        ]
        row_copies.append(row_copy(chips - 1, t_at, tensor_peer(0, 1), rows_any))
        wide = [fetch(gu_any, gu_wide, 1), fetch(down_any, down_wide, 2)]
        kept = [
            fetch(shard_ref, qkv_ref.at[:, rows_of(g.dp_at, slab)], 3),
            fetch(gains_ref, all_gains.at[g.dp_at], 4),
            fetch(rows_any, seq_ref.at[rows_of(t_at, count)], 5),
            fetch(flat_ref, out_w_ref.at[:, rows_of(g.dp_at, slab)], 6),
        ]

        def cast_wide(c):
            if c == 0:
                wide[0].wait()

            def cast_rows(i):
                at = rows_of(i, lines)
                cast[c, at] = gu_wide[c, at].astype(bf16)

            looped(slab // lines, cast_rows)

        def cast_turned():
            wide[1].wait()

            def cast_rows(i):
                at = rows_of(i, 256)
                cast[2, :, at] = down_wide[at].T.astype(bf16)

            looped(shard_units // 256, cast_rows)

        shadows = [lambda: cast_wide(0), lambda: cast_wide(1), cast_turned]
        for step in range(1, n - 1):
            for item in order:
                hops[step - 1, item].wait_recv()
                hop(step, item)
            if step <= chips - 1:
                row_copies[step - 1].wait_recv()
                source = lax.rem(g.chip_at - step + chips, chips) * 2 + g.core_at
                row_copies.append(row_copy(chips - 1 + step, source, tensor_peer(0, 1)))
            if shadows:
                shadows.pop(0)()

        def cut(s):
            return cast.at[:, :, rows_of(g.outer_flip(g.outer_at, s), units)]

        z_copies = {}

        def z_send(s):
            z_copies[s] = remote(cut(s), pieces[0][s], s_z.at[s], r_z.at[s], dp_peer(s, 0))

        for s in steps[:2]:
            z_send(s)
        own = fetch(cut(0), pieces[0][0], 0)
        y_copies = {}

        def pass_on(j, s):
            src = cut(0) if (j, s) == (1, 0) else pieces[j - 1][s]
            y_copies[j, s] = remote(src, pieces[j][s], s_y.at[j, s], r_y.at[j, s], dp_peer(0, 1))

        if inner > 1:
            pass_on(1, 0)
        duties = []
        for s in steps:

            def duty(s=s):
                z_copies[s].wait_recv()
                if inner > 1:
                    pass_on(1, s)
                if s >= 2 and s + 1 < outer:
                    z_send(s + 1)

            duties.append(duty)
        for j in range(2, inner):
            for s in [0] + steps:

                def duty(j=j, s=s):
                    y_copies[j - 1, s].wait_recv()
                    pass_on(j, s)

                duties.append(duty)

        def next_duty():
            if duties:
                duties.pop(0)()

        for item in order:
            hops[n - 2, item].wait_recv()
        for copy in row_copies[chips - 1 :]:
            copy.wait_recv()
        for copy in kept:
            copy.wait()
        outs = [fetch(qkv_ref, qkv_out, 3), fetch(out_w_ref, flat_out, 4), fetch(seq_ref, seq_out, 5)]

        def spread(i):
            gain_rows[:, rows_of(i, slab)] = all_gains[i].astype(f32)[:8]

        looped(n, spread)

        def project(i):
            at = rows_of(i, tall)
            x = seq_ref[at]
            lane = lax.broadcasted_iota(jnp.int32, (tall, 128), 1)
            sums = jnp.zeros((tall, 128), f32)
            for c in range(2):
                value = dot(x, qkv_ref[c], ((1,), (0,)))
                hat_ref[c, at] = value
                sums = jnp.where(lane == c, jnp.sum(value * value, axis=1, keepdims=True), sums)
            v_low[at] = dot(x, qkv_ref[2], ((1,), (0,))).astype(bf16)
            square[:, at] = sums.T[:8]

        looped(length // tall, project)
        sq_copies = []
        for k in range(chips):
            for f in (0, 1):
                if (k, f) != (0, 0):
                    at = k * 2 + f - 1
                    sq_copies.append(
                        remote(square, squares.at[at], s_sq.at[at], r_sq.at[at], tensor_peer(k, f))
                    )
        for copy in sq_copies:
            copy.wait_recv()
        sign = jnp.where(lax.broadcasted_iota(jnp.int32, (tall, HEAD), 1) < HEAD // 2, -1.0, 1.0)

        def rotate(i):
            at = rows_of(i, tall)
            sums = square[:, at]
            for copy_at in range(tensor - 1):
                sums = sums + squares[copy_at, :, at]
            column = jnp.concatenate([sums, jnp.zeros((120, tall), f32)], axis=0).T
            scales = lax.rsqrt(column / width + norm_eps)
            scale_ref[at] = scales
            cosine, sine = cos_ref[at], sin_ref[at] * sign
            for c, low in ((0, q_low), (1, k_low)):
                hat = hat_ref[c, at] * scales[:, c : c + 1]
                hat_ref[c, at] = hat
                normed = hat * gain_rows[c : c + 1, rows_of(t_at, span)]
                for h in range(heads):
                    cols = slice(h * HEAD, (h + 1) * HEAD)
                    value = normed[:, cols]
                    turned = pltpu.roll(value, HEAD // 2, 1)
                    low[at, cols] = (value * cosine + turned * sine).astype(bf16)

        looped(length // tall, rotate)
        scale = HEAD ** (-0.5)
        top_ref[...] = jnp.full((8, 128), masked_value, f32)
        for h in range(heads):
            cols = slice(h * HEAD, (h + 1) * HEAD)

            def attend(i, best, cols=cols, h=h):
                at = rows_of(i, tall)
                raw = dot(q_low[at, cols], k_low[:, cols], ((1,), (1,))) * scale
                masked = jnp.where(id_row[...] <= id_col[at], raw, masked_value)
                top = jnp.max(masked, axis=1, keepdims=True)
                weight = jnp.exp(masked - top)
                total = jnp.sum(weight, axis=1, keepdims=True)
                probs = (weight / total).astype(bf16)
                context[at, cols] = dot(probs, v_low[:, cols], ((1,), (0,))).astype(bf16)
                lse_ref[at, h : h + 1] = top + jnp.log(total)
                return jnp.maximum(best, jnp.max(top, axis=0, keepdims=True))

            best = lax.fori_loop(
                0, length // tall, attend, jnp.full((1, 1), masked_value, f32)
            )
            top_ref[h : h + 1] = jnp.broadcast_to(best, (1, 128))
        for _ in steps[:2]:
            next_duty()

        def out_rows(k, flip, store):
            chip = lax.rem(g.chip_at + k, chips)
            core = 1 - g.core_at if flip else g.core_at
            at = rows_of(chip * 2 + core, count)

            def columns(i):
                cols = rows_of(i, tile)
                store(cols, dot(context[at], out_w_ref[:, cols], ((1,), (0,))))

            looped(width // tile, columns)

        chip_order = list(range(1, chips)) + [0]
        core_copies, chip_copies = {}, {}
        for k in chip_order:

            def store(cols, value, k=k):
                core_send[k, :, cols] = value.astype(bf16)

            out_rows(k, True, store)
            core_copies[k] = remote(
                core_send.at[k], core_land.at[k], s_core.at[k], r_core.at[k], tensor_peer(0, 1)
            )
        for k in chip_order:

            def store(cols, value, k=k):
                hold[k, :, cols] = value

            out_rows(k, False, store)
            if k:
                core_copies[k].wait_recv()

                def add(i, k=k):
                    at = rows_of(i, lines)
                    chip_send[k - 1, at] = (hold[k, at] + core_land[k, at].astype(f32)).astype(bf16)

                looped(count // lines, add)
                chip_copies[k] = remote(
                    chip_send.at[k - 1], chip_land.at[k - 1], s_chip.at[k], r_chip.at[k], tensor_peer(k, 0)
                )
        core_copies[0].wait_recv()
        for k in range(1, chips):
            chip_copies[k].wait_recv()

        def close(i):
            at = rows_of(i, lines)
            raw = hold[0, at] + core_land[0, at].astype(f32)
            for k in range(1, chips):
                raw = raw + chip_land[k - 1, at].astype(f32)
            scale_o = lax.rsqrt(jnp.mean(raw * raw, axis=1, keepdims=True) + norm_eps)
            hat = raw * scale_o
            attn_hat[at] = hat
            o_scale[at] = scale_o
            value = rows_ref[at].astype(f32) + hat * gain_rows[2:3]
            resid[at] = value
            resid_low[at] = value.astype(bf16)

        looped(count // lines, close)
        while duties:
            next_duty()
        own.wait()
        for key, copy in y_copies.items():
            if key[0] == inner - 1:
                copy.wait_recv()
        for copy in outs:
            copy.wait()
        sent = list(hops.values()) + row_copies + list(z_copies.values()) + list(y_copies.values()) + sq_copies
        for copy in sent + list(core_copies.values()) + list(chip_copies.values()):
            copy.wait_send()

    shape = jax.ShapeDtypeStruct
    anywhere = pl.BlockSpec(memory_space=pl.ANY)
    vmem = pl.BlockSpec(memory_space=pltpu.VMEM)
    sems = pltpu.SemaphoreType.DMA
    results = pl.pallas_call(
        kernel,
        out_shape=(shape((3, slab, units), bf16),) * parts
        + (
            shape((lead, width, span), bf16),
            shape((span, width), bf16),
            shape((length, width), bf16),
            shape((8, width), f32),
            shape((2, length, span), f32),
            shape((length, 128), f32),
            shape((length, span), bf16),
            shape((length, span), bf16),
            shape((length, span), bf16),
            shape((length, heads), f32),
            shape((length, span), bf16),
            shape((count, width), f32),
            shape((count, 1), f32),
            shape((count, width), f32),
            shape((count, width), bf16),
            shape((8, 128), f32),
        ),
        in_specs=[anywhere] * 6 + [vmem] * 5,
        out_specs=(anywhere,) * (parts + 3) + (vmem,) * 13,
        scratch_shapes=[
            pltpu.VMEM((lead, width, span), bf16),
            pltpu.VMEM((span, width), bf16),
            pltpu.VMEM((length, width), bf16),
            pltpu.VMEM((n,) + gains.shape, bf16),
            pltpu.VMEM(w_gu.shape, f32),
            pltpu.VMEM(w_down.shape, f32),
            pltpu.VMEM((3, slab, shard_units), bf16),
            pltpu.VMEM((8, length), f32),
            pltpu.VMEM((tensor - 1, 8, length), f32),
            pltpu.VMEM((chips, count, width), bf16),
            pltpu.VMEM((chips, count, width), bf16),
            pltpu.VMEM((chips, count, width), f32),
            pltpu.VMEM((max(chips - 1, 1), count, width), bf16),
            pltpu.VMEM((max(chips - 1, 1), count, width), bf16),
            sems((n - 1, ring)),
            sems((n - 1, ring)),
            sems((2 * chips - 1,)),
            sems((2 * chips - 1,)),
            sems((outer,)),
            sems((outer,)),
            sems((inner, outer)),
            sems((inner, outer)),
            sems((tensor - 1,)),
            sems((tensor - 1,)),
            sems((chips,)),
            sems((chips,)),
            sems((chips,)),
            sems((chips,)),
            sems((7,)),
        ],
        compiler_params=pltpu.CompilerParams(
            collective_id=0, has_side_effects=True, vmem_limit_bytes=58 * 2**20
        ),
    )(
        shard, flat, gains, rows, w_gu, w_down, tables[0], tables[1],
        blocks[:, None], blocks[None, :], rows,
    )
    pieces = [results[j * outer : (j + 1) * outer] for j in range(inner)]
    return pieces, results[parts:]


def unit_kernel_call(rows_low, resid, cotangent, gain, pieces):
    grid = Grid()
    outer, chips, inner = grid.outer, grid.chips, grid.inner
    total_rows, width = rows_low.shape
    units = pieces[0][0].shape[2]
    slab = pieces[0][0].shape[1]
    flat_pieces = [piece for row in pieces for piece in row]
    parts = len(flat_pieces)
    halves = 2
    count = total_rows // halves
    both = 2 * count
    per = min(2, chips)
    groups = chips // per
    blocks = outer * groups
    tall = per * both
    held = per if groups > 1 else max(per - 1, 1)
    links = outer * (chips - 1)
    steps = list(range(outer))
    order = [(s, i) for s in steps for i in range(groups)]
    tile = 512
    wide_tiles = width // tile
    unit_tile = min(256, units)
    lines = 32
    bf16, f32 = jnp.bfloat16, jnp.float32
    mesh_id = pl.DeviceIdType.MESH

    def plan():
        chip_us, core_us, hop_us = 5.3, 0.6, 2.0
        free = {"x": 0.0, "core": 0.0, "z near": 0.0, "z far": 0.0}
        arrive, done, tasks = {}, {}, {}

        def send(link, when, us):
            free[link] = max(free[link], when) + us
            return free[link] + hop_us

        def add(name, needs, us, after=None):
            tasks[name] = (needs, us, after)

        def send_outer(s, now):
            return send("z near", now, 8.0) if s == 1 else send("z far", now, 10.5)

        def go(p, h):
            def then(now):
                if (p, h) != (0, 1):
                    for s in steps[1:]:
                        arrive["z", p, h, s] = send_outer(s, now)
                for k in range(1, chips):
                    arrive["x", p, h, 0, k] = send("x", now, chip_us)
                arrive["c", p, h, 0, 0] = send("core", now, core_us)

            return then

        def zf(p, h, s):
            def then(now):
                for k in range(1, chips):
                    arrive["x", p, h, s, k] = send("x", now, chip_us)
                arrive["c", p, h, s, 0] = send("core", now, core_us)
                if (p, h) == (0, 0):
                    arrive["z", 0, 1, s] = send_outer(s, now)

            return then

        def xf(p, h, s, k):
            def then(now):
                arrive["c", p, h, s, k] = send("core", now, core_us)

            return then

        def compute(p, h, s, i):
            def then(now):
                arrive["cr", p, h, s, i] = send("core", now, per * core_us)

            return then

        def cr(p, h, s, i):
            def then(now):
                for k in range(i * per, i * per + per):
                    if k:
                        arrive["xr", p, h, s, k] = send("x", now, chip_us)

            return then

        def xr(p, h, s):
            def then(now):
                if s:
                    arrive["zr", p, h, s] = send_outer(s, now)

            return then

        for p in (0, 1):
            for h in range(halves):
                if p == 0:
                    needs = [("do", ("go", 0, h - 1))] if h else []
                else:
                    needs = [("do", ("between", h))]
                add(("go", p, h), needs, 0.2, go(p, h))
                for s in steps[1:]:
                    add(("zf", p, h, s), [("at", ("z", p, h, s))], 0.2, zf(p, h, s))
                for s in steps:
                    for k in range(1, chips):
                        add(("xf", p, h, s, k), [("at", ("x", p, h, s, k))], 0.2, xf(p, h, s, k))
                for n, (s, i) in enumerate(order):
                    needs = [("at", ("c", p, h, s, i * per + j)) for j in range(per)]
                    if n:
                        needs.append(("do", ("compute", p, h) + order[n - 1]))
                    add(("load", p, h, s, i), needs, 0.2)
                    needs = [("do", ("load", p, h, s, i))]
                    if n:
                        needs.append(("do", ("cr", p, h) + order[n - 1]))
                    add(("compute", p, h, s, i), needs, 3.2, compute(p, h, s, i))
                    needs = [("at", ("cr", p, h, s, i)), ("do", ("compute", p, h, s, i))]
                    add(("cr", p, h, s, i), needs, 0.5, cr(p, h, s, i))
                for s in steps:
                    needs = [("do", ("cr", p, h, s, 0))]
                    needs += [("at", ("xr", p, h, s, k)) for k in range(1, chips)]
                    add(("xr", p, h, s), needs, 0.4, xr(p, h, s))
                for s in steps[1:]:
                    needs = [("at", ("zr", p, h, s)), ("do", ("xr", p, h, 0))]
                    add(("zr", p, h, s), needs, 0.4)
        for h in range(halves):
            needs = [("do", ("zr", 0, h, s)) for s in steps[1:]] + [("do", ("xr", 0, h, 0))]
            add(("between", h), needs, 1.0)
        for n, (s, i) in enumerate(order):
            needs = [("do", ("compute", 1, h, s, i)) for h in range(halves)]
            if n:
                needs.append(("do", ("grads",) + order[n - 1] + (2,)))
            add(("fetch", s, i), needs, 0.2)
            for c in range(3):
                needs = [("do", ("grads", s, i, c - 1) if c else ("fetch", s, i))]
                add(("grads", s, i, c), needs, 2.4)
        written = [(j, s) for j in range(inner) for s in range(outer)]
        for n, at in enumerate(written):
            needs = [("do", ("grads",) + order[-1] + (2,))]
            if n:
                needs = [("do", ("write",) + written[n - 1])]
            add(("write",) + at, needs, 0.6)
        rank = {"compute": 1, "fetch": 2, "grads": 2, "write": 3}
        result = []
        now = 0.0
        while tasks:
            best = None
            for name, (needs, us, then) in tasks.items():
                ready = 0.0
                for kind, key in needs:
                    table = arrive if kind == "at" else done
                    if key not in table:
                        ready = None
                        break
                    ready = max(ready, table[key] + (1.0 if key[0] in ("load", "fetch") else 0.0))
                if ready is None:
                    continue
                key = (max(ready, now), rank.get(name[0], 0))
                if best is None or key < best[0]:
                    best = (key, name)
            (ready, _), name = best
            needs, us, then = tasks.pop(name)
            now = ready + us
            done[name] = now
            if then is not None:
                then(now)
            result.append(name)
        return result

    def kernel(*refs):
        piece_refs = refs[:parts]
        fixed = refs[parts : parts + 9]
        grad_refs = refs[parts + 9 : parts + 9 + 3 * inner]
        body(piece_refs, *fixed, grad_refs, *refs[parts + 9 + 3 * inner :])

    def body(
        piece_refs, rows_ref, resid_ref, cot_ref, gain_ref,
        out_ref, dres_ref, gain_out, all_x, all_dm, grad_refs,
        wg, wu, wd, buf, wide_buf, act, coef_gate, coef_up, d_gate, d_up, turned, acc_gate, acc_up, acc_down, stage,
        core_send, core_land, hold, keep, chip_send, chip_land, outer_send, outer_land, raw, d_mlp,
        s_outer, r_outer, s_chip, r_chip, s_core, r_core,
        s_core_sum, r_core_sum, s_chip_sum, r_chip_sum, s_outer_sum, r_outer_sum,
        local, local_own, local_wide, local_w, local_g,
    ):
        g = Grid()
        core_peer = (g.dp_at, g.chip_at * 2 + 1 - g.core_at)

        def chip_peer(k):
            return (g.dp_at, lax.rem(g.chip_at + k + chips, chips) * 2 + g.core_at)

        def outer_peer(s):
            return (g.outer_flip(g.outer_at, s) * inner + g.inner_at, g.tensor_at)

        greet(
            [core_peer]
            + [chip_peer(k) for k in range(1, chips)]
            + [outer_peer(s) for s in range(1, outer)]
        )

        def remote(src, dst, send, recv, peer):
            copy = pltpu.make_async_remote_copy(
                src_ref=src, dst_ref=dst, send_sem=send, recv_sem=recv,
                device_id=peer, device_id_type=mesh_id,
            )
            copy.start()
            return copy

        def fetch(src, dst, sem):
            copy = pltpu.make_async_copy(src, dst, sem)
            copy.start()
            return copy

        def dot(a, b, contract):
            return lax.dot_general(a, b, (contract, ((), ())), preferred_element_type=f32)

        def looped(total, make):
            lax.fori_loop(0, total, lambda i, c: (make(i), c)[1], 0)

        def by_lines(make):
            looped(count // lines, lambda i: make(pl.ds(pl.multiple_of(i * lines, lines), lines)))

        def by_tiles(make):
            looped(wide_tiles, lambda i: make(pl.ds(pl.multiple_of(i * tile, tile), tile)))

        weights = (wg, wu, wd)
        fetches = []

        def fetch_weights():
            for j in range(inner):
                for s in range(outer):
                    index = g.outer_flip(g.outer_at, s) * inner
                    index = index + lax.rem(g.inner_at - j + inner, inner)
                    span = pl.ds(pl.multiple_of(index * slab, slab), slab)
                    for c in range(3):
                        at = j * outer + s
                        fetches.append(
                            fetch(piece_refs[at].at[c], weights[c].at[span], local_w.at[at, c])
                        )

        mine, theirs = pl.ds(0, count), pl.ds(count, count)
        every = (all_x, all_dm)
        copies, sums, loads, own = {}, {}, {}, {}
        unsent = {(p, h): [] for p in (0, 1) for h in range(halves)}

        def track(p, h, copy):
            unsent[p, h].append(copy)
            return copy

        def core_copy(p, h, s, k, src):
            dst = every[p].at[h, s, k, theirs]
            copies["c", p, h, s, k] = track(
                p, h, remote(src, dst, s_core.at[p, h, s, k], r_core.at[p, h, s, k], core_peer)
            )

        def chip_copy(p, h, s, k, src):
            dst = every[p].at[h, s, k, mine]
            copies["x", p, h, s, k] = track(
                p, h, remote(src, dst, s_chip.at[p, h, s, k], r_chip.at[p, h, s, k], chip_peer(k))
            )

        def outer_copy(p, h, s):
            source = (rows_ref, d_mlp)[p].at[pl.ds(h * count, count)]
            dst = every[p].at[h, s, 0, mine]
            copies["z", p, h, s] = track(
                p, h, remote(source, dst, s_outer.at[p, h, s], r_outer.at[p, h, s], outer_peer(s))
            )

        def go(p, h):
            source = (rows_ref, d_mlp)[p].at[pl.ds(h * count, count)]
            if (p, h) != (0, 1):
                for s in steps[1:]:
                    outer_copy(p, h, s)
            for k in range(1, chips):
                chip_copy(p, h, 0, k, source)
            core_copy(p, h, 0, 0, source)
            own[p, h] = fetch(source, every[p].at[h, 0, 0, mine], local_own.at[p, h])
            if p == 0 and h == 0:
                fetch_weights()

        def part_out(h, s, i, cols, part_sum):
            for j in range(per):
                own_rows = part_sum[j * both : j * both + count]
                if i * per + j == 0:
                    keep[h, s, :, cols] = own_rows
                else:
                    hold[h, min(j, held - 1), :, cols] = own_rows
                core_send[h, j, :, cols] = part_sum[j * both + count : (j + 1) * both].astype(bf16)

        def forward(h, unit, s, i):
            for j in range(units // unit_tile):
                cols = pl.ds(j * unit_tile, unit_tile)
                rows = buf[h].reshape(tall, width)
                gate = dot(rows, wg[:, cols], ((1,), (0,)))
                up = dot(rows, wu[:, cols], ((1,), (0,)))
                sigma = jax.nn.sigmoid(gate)
                silu = gate * sigma
                act[unit, h, :, cols] = (silu * up).astype(bf16)
                coef_up[unit, h, :, cols] = silu.astype(bf16)
                coef_gate[unit, h, :, cols] = (
                    up * sigma * (1.0 + gate * (1.0 - sigma))
                ).astype(bf16)
            by_tiles(
                lambda cols: part_out(h, s, i, cols, dot(act[unit, h], wd[cols, :], ((1,), (1,))))
            )

        def backward(h, unit, s, i):
            for j in range(units // unit_tile):
                cols = pl.ds(j * unit_tile, unit_tile)
                d_act = dot(buf[h].reshape(tall, width), wd[:, cols], ((1,), (0,)))
                d_gate[unit, h, :, cols] = (d_act * coef_gate[unit, h, :, cols].astype(f32)).astype(bf16)
                d_up[unit, h, :, cols] = (d_act * coef_up[unit, h, :, cols].astype(f32)).astype(bf16)

            def into(cols):
                part_sum = dot(d_gate[unit, h], wg[cols, :], ((1,), (1,)))
                part_sum = part_sum + dot(d_up[unit, h], wu[cols, :], ((1,), (1,)))
                part_out(h, s, i, cols, part_sum)

            by_tiles(into)

        def weight_grads(unit, c):
            first = unit == order[0][0] * groups + order[0][1]
            left, right, acc = ((d_gate, 0, acc_gate), (d_up, 0, acc_up), (act, 1, acc_down))[c]
            turned[...] = left[unit].reshape(halves * tall, units).T

            def grads(cols):
                rows = wide_buf[right, :, :, :, cols].reshape(halves * tall, tile)
                value = dot(turned[...], rows, ((1,), (0,)))
                acc[:, cols] = value if first else acc[:, cols] + value

            by_tiles(grads)

        def between(h):
            def lines_of(i, total):
                at_rows = pl.ds(pl.multiple_of(h * count + i * lines, lines), lines)
                value = raw[at_rows]
                scale = lax.rsqrt(jnp.mean(value * value, axis=1, keepdims=True) + norm_eps)
                hat = value * scale
                gain_row = gain_ref[3:4]
                out_ref[at_rows] = (resid_ref[at_rows] + hat * gain_row).astype(bf16)
                top = cot_ref[at_rows].astype(f32)
                upstream = top * gain_row
                mean = jnp.mean(upstream * hat, axis=1, keepdims=True)
                d_mlp[at_rows] = (scale * (upstream - hat * mean)).astype(bf16)
                return total + jnp.sum(top * hat, axis=0, keepdims=True)

            zero = jnp.zeros((1, width), f32)
            total = lax.fori_loop(0, count // lines, lines_of, zero)
            gain_out[...] = total if h == 0 else gain_out[...] + total

        batches = []

        def write_grads(j, s):
            index = g.outer_flip(g.outer_at, s) * inner
            index = index + lax.rem(g.inner_at + j, inner)
            span = pl.ds(pl.multiple_of(index * slab, slab), slab)
            slot = len(batches) % 2
            if len(batches) >= 2:
                for copy in batches[-2]:
                    copy.wait()
            batch = []
            for c, acc in enumerate((acc_gate, acc_up, acc_down)):
                stage[slot, c] = acc[:, span].astype(bf16)
                batch.append(
                    fetch(stage.at[slot, c], grad_refs[j * 3 + c].at[s], local_g.at[slot, c])
                )
            batches.append(batch)

        def core_sum(p, h, s, i):
            unit = s * groups + i
            sums["c", p, h, unit].wait_recv()
            for j in range(per):
                chip = i * per + j
                if chip == 0:

                    def add(at_rows):
                        keep[h, s, at_rows] = keep[h, s, at_rows] + core_land[h, unit, j, at_rows].astype(f32)

                    by_lines(add)
                    continue
                there = s * (chips - 1) + chip - 1

                def add(at_rows):
                    total = hold[h, min(j, held - 1), at_rows] + core_land[h, unit, j, at_rows].astype(f32)
                    chip_send[h, there, at_rows] = total.astype(bf16)

                by_lines(add)
                sums["x", p, h, s, chip] = track(
                    p, h,
                    remote(
                        chip_send.at[h, there], chip_land.at[h, there],
                        s_chip_sum.at[p, h, there], r_chip_sum.at[p, h, there], chip_peer(-chip),
                    ),
                )

        def chip_sum(p, h, s):
            for k in range(1, chips):
                sums["x", p, h, s, k].wait_recv()

            def add(at_rows):
                total = keep[h, s, at_rows]
                for k in range(1, chips):
                    total = total + chip_land[h, s * (chips - 1) + k - 1, at_rows].astype(f32)
                if s == 0:
                    raw[pl.ds(pl.multiple_of(h * count + at_rows.start, lines), lines)] = total
                else:
                    outer_send[h, s - 1, at_rows] = total.astype(bf16)

            by_lines(add)
            if s:
                sums["z", p, h, s] = track(
                    p, h,
                    remote(
                        outer_send.at[h, s - 1], outer_land.at[h, s - 1],
                        s_outer_sum.at[p, h, s], r_outer_sum.at[p, h, s], outer_peer(s),
                    ),
                )

        def outer_sum(p, h, s):
            sums["z", p, h, s].wait_recv()

            def add(at_rows):
                there = pl.ds(pl.multiple_of(h * count + at_rows.start, lines), lines)
                raw[there] = raw[there] + outer_land[h, s - 1, at_rows].astype(f32)

            by_lines(add)

        def all_sent(p, h):
            for copy in unsent[p, h]:
                copy.wait_send()

        last_core = {}
        for task in plan():
            name, args = task[0], task[1:]
            if name == "go":
                go(*args)
            elif name == "zf":
                p, h, s = args
                copies["z", p, h, s].wait_recv()
                source = every[p].at[h, s, 0, mine]
                for k in range(1, chips):
                    chip_copy(p, h, s, k, source)
                core_copy(p, h, s, 0, source)
                if (p, h) == (0, 0):
                    outer_copy(0, 1, s)
            elif name == "xf":
                p, h, s, k = args
                copies["x", p, h, s, k].wait_recv()
                core_copy(p, h, s, k, every[p].at[h, s, k, mine])
            elif name == "load":
                p, h, s, i = args
                for j in range(per):
                    copies["c", p, h, s, i * per + j].wait_recv()
                if (s, i) == order[0]:
                    own[p, h].wait()
                src = every[p].at[h, s, pl.ds(i * per, per)]
                loads[args] = fetch(src, buf.at[h], local.at[p, h, s * groups + i])
            elif name == "compute":
                p, h, s, i = args
                unit = s * groups + i
                if p == 0 and not loads.get("weights"):
                    loads["weights"] = True
                    for copy in fetches:
                        copy.wait()
                loads[args].wait()
                if h in last_core:
                    last_core[h].wait_send()
                (forward, backward)[p](h, unit, s, i)
                last_core[h] = remote(
                    core_send.at[h], core_land.at[h, unit],
                    s_core_sum.at[p, h, unit], r_core_sum.at[p, h, unit], core_peer,
                )
                sums["c", p, h, unit] = last_core[h]
            elif name == "cr":
                core_sum(*args)
            elif name == "xr":
                chip_sum(*args)
            elif name == "zr":
                outer_sum(*args)
            elif name == "between":
                all_sent(0, args[0])
                between(args[0])
            elif name == "fetch":
                s, i = args
                loads[task] = []
                for at, src in enumerate((all_x, all_dm)):
                    for h in range(halves):
                        loads[task].append(
                            fetch(
                                src.at[h, s, pl.ds(i * per, per)],
                                wide_buf.at[at, h],
                                local_wide.at[s * groups + i, at * halves + h],
                            )
                        )
            elif name == "grads":
                s, i, c = args
                if c == 0:
                    for copy in loads["fetch", s, i]:
                        copy.wait()
                weight_grads(s * groups + i, c)
            elif name == "write":
                write_grads(*args)

        looped(
            total_rows // lines,
            lambda i: close_rows(pl.ds(pl.multiple_of(i * lines, lines), lines), dres_ref, raw, cot_ref),
        )
        for h in range(halves):
            all_sent(1, h)
            last_core[h].wait_send()
        for batch in batches[-2:]:
            for copy in batch:
                copy.wait()

    shape = jax.ShapeDtypeStruct
    anywhere = pl.BlockSpec(memory_space=pl.ANY)
    near = pl.BlockSpec(memory_space=pltpu.VMEM)
    sems = pltpu.SemaphoreType.DMA
    flops = 2 * 9 * halves * tall * blocks * width * units
    results = pl.pallas_call(
        kernel,
        out_shape=(
            shape((total_rows, width), bf16),
            shape((total_rows, width), f32),
            shape((1, width), f32),
            shape((halves, outer, chips, both, width), bf16),
            shape((halves, outer, chips, both, width), bf16),
        )
        + (shape((outer, units, slab), bf16),) * (3 * inner),
        in_specs=[anywhere] * (parts + 1) + [near] * 3,
        out_specs=(near, near, near) + (anywhere,) * (2 + 3 * inner),
        scratch_shapes=[
            pltpu.VMEM((width, units), bf16),
            pltpu.VMEM((width, units), bf16),
            pltpu.VMEM((width, units), bf16),
            pltpu.VMEM((halves, per, both, width), bf16),
            pltpu.VMEM((2, halves, per, both, width), bf16),
            pltpu.VMEM((blocks, halves, tall, units), bf16),
            pltpu.VMEM((blocks, halves, tall, units), bf16),
            pltpu.VMEM((blocks, halves, tall, units), bf16),
            pltpu.VMEM((blocks, halves, tall, units), bf16),
            pltpu.VMEM((blocks, halves, tall, units), bf16),
            pltpu.VMEM((units, halves * tall), bf16),
            pltpu.VMEM((units, width), f32),
            pltpu.VMEM((units, width), f32),
            pltpu.VMEM((units, width), f32),
            pltpu.VMEM((2, 3, units, slab), bf16),
            pltpu.VMEM((halves, per, count, width), bf16),
            pltpu.VMEM((halves, blocks, per, count, width), bf16),
            pltpu.VMEM((halves, held, count, width), f32),
            pltpu.VMEM((halves, outer, count, width), f32),
            pltpu.VMEM((halves, links, count, width), bf16),
            pltpu.VMEM((halves, links, count, width), bf16),
            pltpu.VMEM((halves, outer - 1, count, width), bf16),
            pltpu.VMEM((halves, outer - 1, count, width), bf16),
            pltpu.VMEM((total_rows, width), f32),
            pltpu.VMEM((total_rows, width), bf16),
            sems((2, halves, outer)),
            sems((2, halves, outer)),
            sems((2, halves, outer, chips)),
            sems((2, halves, outer, chips)),
            sems((2, halves, outer, chips)),
            sems((2, halves, outer, chips)),
            sems((2, halves, blocks)),
            sems((2, halves, blocks)),
            sems((2, halves, links)),
            sems((2, halves, links)),
            sems((2, halves, outer)),
            sems((2, halves, outer)),
            sems((2, halves, blocks)),
            sems((2, halves)),
            sems((blocks, 2 * halves)),
            sems((parts, 3)),
            sems((2, 3)),
        ],
        compiler_params=pltpu.CompilerParams(
            collective_id=2, has_side_effects=True, vmem_limit_bytes=62 * 2**20
        ),
        cost_estimate=pl.CostEstimate(flops=flops, bytes_accessed=64 * 2**20, transcendentals=0),
    )(*flat_pieces, rows_low, resid, cotangent, gain)
    grads = results[5:]
    return results[:3] + ([[grads[j * 3 + c] for j in range(inner)] for c in range(3)],)


def close_rows(at_rows, dres_ref, raw, cot_ref):
    dres_ref[at_rows] = raw[at_rows] + cot_ref[at_rows].astype(jnp.float32)


def adam_kernel(turned, w_ref, m_ref, v_ref, g_ref, *rest):
    scale_ref = rest[0] if len(rest) == 5 else None
    w_out, m_out, v_out, c_out = rest[-4:]
    grad = g_ref[...].T if turned else g_ref[...]
    new, first, second = adam_step(
        w_ref[...], grad, m_ref[...], v_ref[...], rate_matrix, weight_decay
    )
    if scale_ref is not None:
        new = new * scale_ref[...]
    w_out[...] = new
    m_out[...] = first
    v_out[...] = second
    c_out[...] = new.astype(jnp.bfloat16)


def adam_call(param, grads, at, first, second, scale=None):
    mats, rows, columns = param.shape
    turned = scale is not None
    spec = pl.BlockSpec((None, rows, columns), lambda k: (k, 0, 0))
    grad_spec = pl.BlockSpec((None,) + grads.shape[1:], lambda k: (at + k, 0, 0))
    specs = [spec] * 3 + [grad_spec]
    values = [param, first, second, grads]
    if turned:
        values.append(scale)
        specs.append(pl.BlockSpec((None, 1, columns), lambda k: (k, 0, 0)))
    outs = [jax.ShapeDtypeStruct(param.shape, jnp.float32)] * 3
    outs.append(jax.ShapeDtypeStruct(param.shape, jnp.bfloat16))
    size = param.size
    return pl.pallas_call(
        functools.partial(adam_kernel, turned),
        grid=(mats,),
        in_specs=specs,
        out_specs=[spec] * 4,
        out_shape=outs,
        cost_estimate=pl.CostEstimate(
            flops=20 * size, bytes_accessed=28 * size, transcendentals=2 * size
        ),
        compiler_params=pltpu.CompilerParams(vmem_limit_bytes=32 * 2**20),
    )(*values)


def adam_units_kernel(turned, at_ref, w_ref, m_ref, v_ref, g_ref, w_out, m_out, v_out, c_out):
    grad = g_ref[...].astype(jnp.float32)
    if turned:
        grad = grad.T
    new, first, second = adam_step(
        w_ref[...], grad, m_ref[...], v_ref[...], rate_matrix, weight_decay
    )
    w_out[...] = new
    m_out[...] = first
    v_out[...] = second
    c_out[...] = new.astype(jnp.bfloat16)


def adam_units(grid, param, first, second, grads, turned):
    n = grid.outer
    stacked = jnp.stack([jnp.stack(list(pieces)) for pieces in grads])
    mats, _, units, wide = stacked.shape
    if not turned:
        spec = pl.BlockSpec((units, wide), lambda c, k, at: (k, 0))
    else:
        spec = pl.BlockSpec((None, wide, units), lambda c, k, at: (c, 0, k))
    grad_spec = pl.BlockSpec(
        (None, None, units, wide), lambda c, k, at: (c, lax.bitwise_xor(at[0], k), 0, 0)
    )
    size = param.size
    outs = [jax.ShapeDtypeStruct(param.shape, jnp.float32)] * 3
    outs.append(jax.ShapeDtypeStruct(param.shape, jnp.bfloat16))
    return pl.pallas_call(
        functools.partial(adam_units_kernel, turned),
        grid_spec=pltpu.PrefetchScalarGridSpec(
            num_scalar_prefetch=1,
            grid=(mats, n),
            in_specs=[spec] * 3 + [grad_spec],
            out_specs=[spec] * 4,
        ),
        out_shape=outs,
        cost_estimate=pl.CostEstimate(
            flops=20 * size, bytes_accessed=28 * size, transcendentals=2 * size
        ),
        compiler_params=pltpu.CompilerParams(vmem_limit_bytes=32 * 2**20),
    )(grid.outer_at.astype(jnp.int32)[None], param, first, second, stacked)


def local(
    tokens,
    cotangent,
    block_ids,
    w_qkv,
    m_qkv,
    v_qkv,
    w_out,
    m_out,
    v_out,
    w_gu,
    m_gu,
    v_gu,
    w_down,
    m_down,
    v_down,
    gains,
    gain_m,
    gain_v,
):
    grid = Grid()
    local_x = tokens[0]
    gain_count = gains.shape[0]
    low_gains = jnp.pad(gains.astype(jnp.bfloat16), ((0, 16 - gain_count), (0, 0)))
    tables = rope_tables(local_x.shape[0] * grid.tensor, HEAD)
    pieces, kept = open_call(
        w_qkv.astype(jnp.bfloat16),
        w_out.astype(jnp.bfloat16),
        low_gains,
        local_x,
        w_gu,
        w_down,
        tables,
        block_ids[0],
    )
    full_qkv, full_out, seq_x, gain_rows = kept[:4]
    hats, scales, q_low, k_low, v_low, log_total, context_low = kept[4:11]
    attn_hat, o_scale, resid, resid_low, tops = kept[11:]
    output, d_resid, gain_last, unit_grads = unit_kernel_call(
        resid_low, resid, cotangent[0], gain_rows, pieces
    )
    backs, (part, part_gains, tops, grad_tokens) = attend_back_call(
        d_resid,
        attn_hat,
        o_scale,
        gain_rows,
        full_out,
        context_low,
        q_low,
        k_low,
        v_low,
        log_total,
        hats,
        scales,
        tables,
        block_ids[0],
        seq_x,
        full_qkv,
        gain_last,
        tops,
        unit_grads,
    )
    part_gains = part_gains[:gain_count]
    head_top = tops[: w_qkv.shape[2] // HEAD, 0]
    factor = clip_tau / jnp.maximum(head_top, clip_tau)
    column = jnp.repeat(jnp.sqrt(factor), HEAD)
    column_scale = jnp.stack([column, column, jnp.ones_like(column)])[:, None, :]
    new_qkv, new_m_qkv, new_v_qkv, copy_qkv = adam_call(w_qkv, part, 0, m_qkv, v_qkv, column_scale)
    new_out, new_m_out, new_v_out, copy_out = [
        v[0] for v in adam_call(w_out[None], part, 3, m_out[None], v_out[None])
    ]
    new_gu, new_m_gu, new_v_gu, copy_gu = adam_units(grid, w_gu, m_gu, v_gu, backs[:2], True)
    new_down, new_m_down, new_v_down, copy_down = adam_units(
        grid, w_down, m_down, v_down, backs[2:], False
    )
    new_gains, new_gain_m, new_gain_v = adam_step(gains, part_gains, gain_m, gain_v, rate_gain, 0.0)
    return (
        output[None],
        grad_tokens[None],
        new_qkv,
        new_m_qkv,
        new_v_qkv,
        copy_qkv,
        new_out,
        new_m_out,
        new_v_out,
        copy_out,
        new_gu,
        new_m_gu,
        new_v_gu,
        copy_gu,
        new_down,
        new_m_down,
        new_v_down,
        copy_down,
        new_gains,
        new_gain_m,
        new_gain_v,
        factor,
    )


def solution(mesh):
    return jax.shard_map(
        local,
        mesh=mesh,
        in_specs=(
            P("dp", "tensor", None),
            P("dp", "tensor", None),
            P("dp", None),
            P(None, "dp", "tensor"),
            P(None, "dp", "tensor"),
            P(None, "dp", "tensor"),
            P("tensor", "dp"),
            P("tensor", "dp"),
            P("tensor", "dp"),
            P(None, "dp", "tensor"),
            P(None, "dp", "tensor"),
            P(None, "dp", "tensor"),
            P("tensor", "dp"),
            P("tensor", "dp"),
            P("tensor", "dp"),
            P(None, "dp"),
            P(None, "dp"),
            P(None, "dp"),
        ),
        out_specs=(
            P("dp", "tensor", None),
            P("dp", "tensor", None),
            P(None, "dp", "tensor"),
            P(None, "dp", "tensor"),
            P(None, "dp", "tensor"),
            P(None, "dp", "tensor"),
            P("tensor", "dp"),
            P("tensor", "dp"),
            P("tensor", "dp"),
            P("tensor", "dp"),
            P(None, "dp", "tensor"),
            P(None, "dp", "tensor"),
            P(None, "dp", "tensor"),
            P(None, "dp", "tensor"),
            P("tensor", "dp"),
            P("tensor", "dp"),
            P("tensor", "dp"),
            P("tensor", "dp"),
            P(None, "dp"),
            P(None, "dp"),
            P(None, "dp"),
            P("tensor"),
        ),
        check_vma=False,
    )
```

```python
import functools

import jax
import jax.numpy as jnp
import numpy as np
from jax import lax
from jax.experimental import pallas as pl
from jax.experimental.pallas import tpu as pltpu
from jax.sharding import PartitionSpec as P

HEAD = 128
STEP = 5


norm_eps = 1e-06
rope_base = 500000.0
beta_one = 0.9
beta_two = 0.95
rate_matrix = 0.01
rate_gain = 0.6
weight_decay = 0.1
adam_eps = 1e-08
clip_tau = 9.0
masked_value = -1e30


def rope_tables(length, size):
    half = size // 2
    freq = np.float32(rope_base) ** (-(np.arange(half, dtype=np.float32) * np.float32(2.0 / size)))
    angle = np.arange(length, dtype=np.float32)[:, None] * freq[None, :]
    angle = np.concatenate([angle, angle], axis=1)
    return (jnp.asarray(np.cos(angle)), jnp.asarray(np.sin(angle)))


def adam_step(param, grad, first, second, rate, decay):
    first = beta_one * first + (1.0 - beta_one) * grad
    second = beta_two * second + (1.0 - beta_two) * grad * grad
    fix_one = 1.0 - beta_one**STEP
    fix_two = 1.0 - beta_two**STEP
    update = first / fix_one / (jnp.sqrt(second / fix_two) + adam_eps)
    return (param - rate * (update + decay * param), first, second)


class Grid:
    def __init__(self):
        self.dp = lax.axis_size("dp")
        self.tensor = lax.axis_size("tensor")
        self.inner = 1
        while self.inner * self.inner * 4 <= self.dp:
            self.inner *= 2
        self.outer = self.dp // self.inner
        self.chips = self.tensor // 2
        self.dp_at = lax.axis_index("dp")
        self.tensor_at = lax.axis_index("tensor")
        self.inner_at = self.dp_at % self.inner
        self.chip_at = self.tensor_at // 2
        self.core_at = self.tensor_at % 2
        self.outer_at = self.dp_at // self.inner

    def path_of(self, index):
        column, row = index // self.inner, index % self.inner
        return row * self.outer + column + (row % 2) * (self.outer - 1 - 2 * column)

    def outer_flip(self, index, step):
        result = 0
        for bit in bits(self.outer):
            side = index // bit % 2
            result = result + bit * (1 - side if step & bit else side)
        return result

    def index_of(self, place):
        row, column = place // self.outer, place % self.outer
        return (column + (row % 2) * (self.outer - 1 - 2 * column)) * self.inner + row


def bits(count):
    return [1 << k for k in range(count.bit_length() - 1)]


def greet(peers):
    barrier = pltpu.get_barrier_semaphore()
    for peer in peers:
        pl.semaphore_signal(barrier, inc=1, device_id=peer, device_id_type=pl.DeviceIdType.MESH)
    pl.semaphore_wait(barrier, len(peers))


def attend_back_call(
    d_resid, attn_hat, o_scale, gain_rows, full_out, context, q_low, k_low, v_low, lse, hats, scales,
    tables, blocks, seq, full_qkv, gain_last, tops, unit_grads,
):
    grid = Grid()
    n, outer, inner, chips, tensor = grid.dp, grid.outer, grid.inner, grid.chips, grid.tensor
    count, width = d_resid.shape
    length, span = context.shape
    heads = span // HEAD
    units, slab = unit_grads[0][0].shape[1:]
    thin = width // n
    half = span // 2
    tall = min(256, length)
    tile = 512
    lines = 32
    ring = 8 + 2
    gain_item, top_item = 8, 9
    bf16, f32 = jnp.bfloat16, jnp.float32
    mesh_id = pl.DeviceIdType.MESH
    flat_grads = [unit_grads[c][j] for j in range(inner) for c in range(3)]
    some = len(flat_grads)
    z_steps = list(range(1, outer))

    def kernel(*refs):
        fixed, far_in, grads_in = refs[:17], refs[17:20], refs[20 : 20 + some]
        rest = refs[20 + some :]
        body(*fixed, far_in, grads_in, *rest)

    def body(
        dres_ref, hat_ref, o_scale_ref, gain_ref, out_w, ctx, q_ref, k_ref, v_ref, lse_ref, scale_ref,
        cos_ref, sin_ref, id_col, id_row, last_ref, tops_ref, far_in, grads_in,
        backs, part_ref, gains_out, tops_out, tokens_out,
        hats, seq, qkv_w, seq_do, d_ctx, d_q, d_k, d_v, d_low, whole, terms, row_terms, turned,
        land, land_gain, land_top, own_gain, peer_gain, inners, peer_inners,
        grad_own, grad_land, grad_sum, core_send, core_land, hold, chip_send, chip_land,
        s_ring, r_ring, s_row, r_row, s_in, r_in, s_y, r_y, s_z, r_z, s_core, r_core, s_chip, r_chip, s_gain, r_gain, local,
    ):
        hats_in, seq_in, qkv_in = far_in
        g = Grid()

        def tensor_peer(k, flip):
            core = 1 - g.core_at if flip else g.core_at
            return (g.dp_at, lax.rem(g.chip_at + k + chips, chips) * 2 + core)

        def dp_peer(s, j):
            across = g.outer_flip(g.outer_at, s) * inner
            return (across + lax.rem(g.inner_at + j + inner, inner), g.tensor_at)

        place = g.path_of(g.dp_at)
        after_dp = (g.index_of(lax.rem(place + 1, n)), g.tensor_at)
        before_dp = (g.index_of(lax.rem(place + n - 1, n)), g.tensor_at)
        near = [tensor_peer(k, f) for k in range(chips) for f in (0, 1) if (k, f) != (0, 0)]
        far = [dp_peer(s, 0) for s in range(1, outer)] + [dp_peer(0, j) for j in range(1, inner)]
        greet(near + far + [after_dp, before_dp])

        def remote(src, dst, send, recv, peer):
            copy = pltpu.make_async_remote_copy(
                src_ref=src, dst_ref=dst, send_sem=send, recv_sem=recv,
                device_id=peer, device_id_type=mesh_id,
            )
            copy.start()
            return copy

        def fetch(src, dst, at):
            copy = pltpu.make_async_copy(src, dst, local.at[at])
            copy.start()
            return copy

        def dot(a, b, contract):
            return lax.dot_general(a, b, (contract, ((), ())), preferred_element_type=f32)

        def looped(total, make):
            lax.fori_loop(0, total, lambda i, c: (make(i), c)[1], 0)

        def rows_of(i, size):
            return pl.ds(pl.multiple_of(i * size, size), size)

        sent = []
        y_copies = {}
        sum_steps = [(c, s) for c in range(3) for s in z_steps + [0]]
        for c, s in sum_steps:
            for j in range(1, inner):
                copy = remote(
                    grads_in[j * 3 + c].at[s],
                    grad_land.at[j - 1, c, s],
                    s_y.at[j, c, s],
                    r_y.at[j, c, s],
                    dp_peer(0, j),
                )
                y_copies[j, c, s] = copy
                sent.append(copy)
        own_grads = [fetch(grads_in[c], grad_own.at[c], c) for c in range(3)]
        fetched = [fetch(hats_in, hats, 3), fetch(seq_in, seq, 4), fetch(qkv_in, qkv_w, 5)]
        z_copies = []
        keeps = []

        def unit_sums(times):
            for _ in range(times):
                if sum_steps:
                    unit_sum(*sum_steps.pop(0))

        def unit_sum(c, s):
            if s == (z_steps + [0])[0]:
                own_grads[c].wait()
            for j in range(1, inner):
                y_copies[j, c, s].wait_recv()

            def add(i):
                rows = rows_of(i, 64)
                total = grad_own[c, s, rows].astype(f32)
                for j in range(1, inner):
                    total = total + grad_land[j - 1, c, s, rows].astype(f32)
                grad_sum[c, s, rows] = total.astype(bf16)

            looped(units // 64, add)
            if s:
                z_copies.append(
                    remote(grad_sum.at[c, s], backs.at[c, s], s_z.at[c, s], r_z.at[c, s], dp_peer(s, 0))
                )
            else:
                keeps.append(fetch(grad_sum.at[c, 0], backs.at[c, 0], 6 + c))

        def way_of(item):
            return 1 if item >= 8 else 1 - 2 * (item // 4)

        def own(item, away):
            index = g.index_of(lax.rem(place - way_of(item) * away + 2 * n, n))
            if item == gain_item:
                return terms.at[index]
            if item == top_item:
                return tops_ref
            side, c = item // 4, item % 4
            return whole.at[c, pl.ds(side * half, half), rows_of(index, thin)]

        def landed(step, item):
            if item == gain_item:
                return land_gain.at[step]
            if item == top_item:
                return land_top.at[step]
            return land.at[step, item]

        hops = {}
        on_path = {}

        def hop(step, item):
            hops[step, item] = remote(
                own(item, 1) if step == 0 else landed(step - 1, item),
                landed(step, item),
                s_ring.at[step, item],
                r_ring.at[step, item],
                after_dp if way_of(item) == 1 else before_dp,
            )

        def depart(*items):
            for item in items:
                on_path[item] = 0
                hop(0, item)

        def advance(*items):
            for item in items:
                step = on_path.get(item, n) + 1
                if step >= n:
                    continue
                on_path[item] = step
                hops[step - 1, item].wait_recv()
                here = landed(step - 1, item)
                if item == top_item:
                    summed = jnp.maximum(here[...], tops_ref[...])
                else:
                    summed = here[...].astype(f32) + own(item, step + 1)[...].astype(f32)
                if step < n - 1:
                    here[...] = summed.astype(here.dtype)
                    hop(step, item)
                elif item == gain_item:
                    own_gain[0] = summed
                elif item == top_item:
                    tops_out[...] = summed
                else:
                    side, c = item // 4, item % 4
                    part_ref[c, pl.ds(side * half, half)] = summed

        def matrix_grad(c, left, right):
            turned[...] = left.T

            def columns(i):
                cols = rows_of(i, tile)
                whole[c, :, cols] = dot(turned[...], right[:, cols], ((1,), (0,))).astype(bf16)

            looped(width // tile, columns)

        t_at = g.tensor_at
        mine = rows_of(t_at, count)

        def open_rows(i, total):
            at = rows_of(i, lines)
            value, hat = dres_ref[at], hat_ref[at]
            upstream = value * gain_ref[2:3]
            mean = jnp.mean(upstream * hat, axis=1, keepdims=True)
            d_attn = (o_scale_ref[at] * (upstream - hat * mean)).astype(bf16)
            seq_do[pl.ds(pl.multiple_of(t_at * count + i * lines, lines), lines)] = d_attn
            return total + jnp.sum(value * hat, axis=0, keepdims=True)

        gain_attn = lax.fori_loop(0, count // lines, open_rows, jnp.zeros((1, width), f32))
        row_terms[...] = jnp.zeros((8, width), f32)
        row_terms[2:3] = gain_attn
        row_terms[3:4] = last_ref[...]
        moves, passed = [], []

        def row_copy(slot, index, peer):
            at = rows_of(index, count)
            copy = remote(seq_do.at[at], seq_do.at[at], s_row.at[slot], r_row.at[slot], peer)
            sent.append(copy)
            return copy

        for k in range(1, chips):
            moves.append(row_copy(k - 1, t_at, tensor_peer(k, 0)))
        to_core = row_copy(chips - 1, t_at, tensor_peer(0, 1))
        unit_sums(2)
        for k in range(1, chips):
            moves[k - 1].wait_recv()
            source = lax.rem(g.chip_at - k + chips, chips) * 2 + g.core_at
            passed.append(row_copy(chips - 1 + k, source, tensor_peer(0, 1)))
        to_core.wait_recv()
        unit_sums(1)
        for copy in passed:
            copy.wait_recv()

        def context_grad(i):
            at = rows_of(i, tall)
            d_ctx[at] = dot(seq_do[at], out_w[...], ((1,), (1,))).astype(bf16)

        looped(length // tall, context_grad)
        unit_sums(1)
        matrix_grad(3, ctx[...], seq_do)
        depart(3, 7)

        scale = HEAD ** (-0.5)
        for h in range(heads):
            cols = slice(h * HEAD, (h + 1) * HEAD)

            def head(i, c, cols=cols, h=h):
                at = rows_of(i, tall)
                q_part, ctx_part = q_ref[at, cols], d_ctx[at, cols]
                raw = dot(q_part, k_ref[:, cols], ((1,), (1,))) * scale
                masked = jnp.where(id_row[...] <= id_col[at], raw, masked_value)
                probs = jnp.exp(masked - lse_ref[at, h : h + 1])
                d_probs = dot(ctx_part, v_ref[:, cols], ((1,), (1,)))
                mean = jnp.sum(probs * d_probs, axis=1, keepdims=True)
                d_scores = (probs * (d_probs - mean)).astype(bf16)
                d_q[at, cols] = dot(d_scores, k_ref[:, cols], ((1,), (0,))) * scale
                key = dot(d_scores, q_part, ((0,), (0,))) * scale
                value = dot(probs.astype(bf16), ctx_part, ((0,), (0,)))
                d_k[:, cols] = jnp.where(i == 0, key, d_k[:, cols] + key)
                d_v[:, cols] = jnp.where(i == 0, value, d_v[:, cols] + value)
                return c

            d_k[:, cols] = jnp.zeros((length, HEAD), f32)
            d_v[:, cols] = jnp.zeros((length, HEAD), f32)
            lax.fori_loop(0, length // tall, head, 0)
            unit_sums(1)
            advance(3, 7)
        def value_rows(i):
            at = rows_of(i, tall)
            d_low[2, at] = d_v[at].astype(bf16)

        looped(length // tall, value_rows)
        fetched[1].wait()
        matrix_grad(2, d_low[2], seq)
        depart(2, 6)
        fetched[0].wait()
        sign = jnp.where(lax.broadcasted_iota(jnp.int32, (tall, HEAD), 1) < HEAD // 2, -1.0, 1.0)

        def unrotate(i, sums):
            at = rows_of(i, tall)
            cosine, sine = cos_ref[at], sin_ref[at]
            lane = lax.broadcasted_iota(jnp.int32, (tall, 128), 1)
            columns = jnp.zeros((tall, 128), f32)
            result = []
            for c, grad in ((0, d_q), (1, d_k)):
                total = jnp.zeros((tall, 1), f32)
                terms_row = []
                for h in range(heads):
                    cols = slice(h * HEAD, (h + 1) * HEAD)
                    value = grad[at, cols]
                    back = value * cosine - pltpu.roll(value * sine, HEAD // 2, 1) * sign
                    hat = hats[c, at, cols]
                    terms_row.append(jnp.sum(back * hat, axis=0, keepdims=True))
                    at_head = pl.ds(pl.multiple_of(t_at * span + h * HEAD, HEAD), HEAD)
                    back = back * gain_ref[c : c + 1, at_head]
                    grad[at, cols] = back
                    total = total + jnp.sum(back * hat, axis=1, keepdims=True)
                columns = jnp.where(lane == c, total, columns)
                result.append(sums[c] + jnp.concatenate(terms_row, axis=1))
            inners[:, at] = columns.T[:8]
            return tuple(result)

        zero = jnp.zeros((1, span), f32)
        gain_q, gain_k = lax.fori_loop(0, length // tall, unrotate, (zero, zero))
        offset = rows_of(t_at, span)
        row_terms[0:1, offset] = gain_q
        row_terms[1:2, offset] = gain_k
        in_copies = []
        for k in range(chips):
            for f in (0, 1):
                if (k, f) != (0, 0):
                    at = k * 2 + f - 1
                    in_copies.append(
                        remote(inners, peer_inners.at[at], s_in.at[at], r_in.at[at], tensor_peer(k, f))
                    )
        sent.extend(in_copies)
        advance(3, 7)
        for copy in in_copies:
            copy.wait_recv()
        unit_sums(1)

        def normed(i):
            at = rows_of(i, tall)
            sums = inners[:, at]
            for other in range(tensor - 1):
                sums = sums + peer_inners[other, :, at]
            column = jnp.concatenate([sums, jnp.zeros((120, tall), f32)], axis=0).T / width
            for c, grad in ((0, d_q), (1, d_k)):
                value = grad[at] - hats[c, at] * column[:, c : c + 1]
                d_low[c, at] = (scale_ref[at, c : c + 1] * value).astype(bf16)

        looped(length // tall, normed)
        advance(2, 6)
        unit_sums(1)
        for c in range(2):
            matrix_grad(c, d_low[c], seq)
            depart(c, c + 4)
            unit_sums(1)
            advance(2, 6, 3, 7)

        def place_terms(i, c):
            cols = pl.ds(pl.multiple_of(i * thin, thin), thin)
            terms[i] = row_terms[:, cols]
            return c

        lax.fori_loop(0, n, place_terms, 0)

        depart(gain_item, top_item)
        unit_sums(len(sum_steps))

        fetched[2].wait()
        chip_order = list(range(1, chips)) + [0]
        core_copies, chip_copies = {}, {}

        def token_rows(k, flip, store):
            chip = lax.rem(g.chip_at + k, chips)
            core = 1 - g.core_at if flip else g.core_at
            at = rows_of(chip * 2 + core, count)

            def columns(i):
                cols = rows_of(i, tile)
                total = dot(d_low[0, at], qkv_w[0, cols], ((1,), (1,)))
                for c in (1, 2):
                    total = total + dot(d_low[c, at], qkv_w[c, cols], ((1,), (1,)))
                store(cols, total)

            looped(width // tile, columns)

        duties = []
        for k in chip_order:

            def away(k=k):
                def store(cols, value):
                    core_send[k, :, cols] = value.astype(bf16)

                token_rows(k, True, store)
                core_copies[k] = remote(
                    core_send.at[k], core_land.at[k], s_core.at[k], r_core.at[k], tensor_peer(0, 1)
                )

            def here(k=k):
                def store(cols, value):
                    hold[k, :, cols] = value

                token_rows(k, False, store)

            def join(k=k):
                core_copies[k].wait_recv()

                def add(i):
                    at = rows_of(i, lines)
                    chip_send[k - 1, at] = (hold[k, at] + core_land[k, at].astype(f32)).astype(bf16)

                looped(count // lines, add)
                chip_copies[k] = remote(
                    chip_send.at[k - 1], chip_land.at[k - 1], s_chip.at[k], r_chip.at[k], tensor_peer(k, 0)
                )

            duties += [away, here] + ([join] if k else [])

        def close_tokens():
            core_copies[0].wait_recv()
            for k in range(1, chips):
                chip_copies[k].wait_recv()

            def close(i):
                at = rows_of(i, lines)
                total = dres_ref[at] + hold[0, at] + core_land[0, at].astype(f32)
                for k in range(1, chips):
                    total = total + chip_land[k - 1, at].astype(f32)
                tokens_out[at] = total

            looped(count // lines, close)

        duties.append(close_tokens)
        per_step = -(-len(duties) // (n - 2))
        for step in range(1, n):
            advance(3, 7, 2, 6, gain_item, top_item, 0, 4, 1, 5)
            for _ in range(per_step):
                if duties:
                    duties.pop(0)()
        peers = [tensor_peer(0, 1)] + [tensor_peer(k, 0) for k in range(1, chips)]
        first = remote(own_gain.at[0], peer_gain.at[0], s_gain.at[0], r_gain.at[0], peers[0])
        first.wait_recv()
        own_gain[1] = own_gain[0] + peer_gain[0]
        others = [
            remote(own_gain.at[1], peer_gain.at[k], s_gain.at[k], r_gain.at[k], peers[k])
            for k in range(1, chips)
        ]
        result = own_gain[1]
        for k in range(1, chips):
            others[k - 1].wait_recv()
            result = result + peer_gain[k]
        gains_out[...] = result
        for copy in z_copies:
            copy.wait()
        for copy in keeps:
            copy.wait()
        for copy in sent + list(hops.values()) + list(core_copies.values()):
            copy.wait_send()
        for copy in list(chip_copies.values()) + [first] + others:
            copy.wait_send()

    shape = jax.ShapeDtypeStruct
    anywhere = pl.BlockSpec(memory_space=pl.ANY)
    vmem = pl.BlockSpec(memory_space=pltpu.VMEM)
    sems = pltpu.SemaphoreType.DMA
    results = pl.pallas_call(
        kernel,
        out_shape=(
            shape((3, outer, units, slab), bf16),
            shape((4, span, thin), f32),
            shape((8, thin), f32),
            shape(tops.shape, f32),
            shape((count, width), f32),
        ),
        in_specs=[vmem] * 17 + [anywhere] * 3 + [anywhere] * some,
        out_specs=(anywhere,) + (vmem,) * 4,
        scratch_shapes=[
            pltpu.VMEM(hats.shape, f32),
            pltpu.VMEM(seq.shape, bf16),
            pltpu.VMEM(full_qkv.shape, bf16),
            pltpu.VMEM((length, width), bf16),
            pltpu.VMEM((length, span), bf16),
            pltpu.VMEM((length, span), f32),
            pltpu.VMEM((length, span), f32),
            pltpu.VMEM((length, span), f32),
            pltpu.VMEM((3, length, span), bf16),
            pltpu.VMEM((4, span, width), bf16),
            pltpu.VMEM((n, 8, thin), f32),
            pltpu.VMEM((8, width), f32),
            pltpu.VMEM((span, length), bf16),
            pltpu.VMEM((n - 1, 8, half, thin), bf16),
            pltpu.VMEM((n - 1, 8, thin), f32),
            pltpu.VMEM((n - 1,) + tops.shape, f32),
            pltpu.VMEM((2, 8, thin), f32),
            pltpu.VMEM((chips, 8, thin), f32),
            pltpu.VMEM((8, length), f32),
            pltpu.VMEM((tensor - 1, 8, length), f32),
            pltpu.VMEM((3, outer, units, slab), bf16),
            pltpu.VMEM((max(inner - 1, 1), 3, outer, units, slab), bf16),
            pltpu.VMEM((3, outer, units, slab), bf16),
            pltpu.VMEM((chips, count, width), bf16),
            pltpu.VMEM((chips, count, width), bf16),
            pltpu.VMEM((chips, count, width), f32),
            pltpu.VMEM((max(chips - 1, 1), count, width), bf16),
            pltpu.VMEM((max(chips - 1, 1), count, width), bf16),
            sems((n - 1, ring)),
            sems((n - 1, ring)),
            sems((2 * chips - 1,)),
            sems((2 * chips - 1,)),
            sems((tensor - 1,)),
            sems((tensor - 1,)),
            sems((inner, 3, outer)),
            sems((inner, 3, outer)),
            sems((3, outer)),
            sems((3, outer)),
            sems((chips,)),
            sems((chips,)),
            sems((chips,)),
            sems((chips,)),
            sems((chips,)),
            sems((chips,)),
            sems((9,)),
        ],
        compiler_params=pltpu.CompilerParams(
            collective_id=1, has_side_effects=True, vmem_limit_bytes=62 * 2**20
        ),
    )(
        d_resid, attn_hat, o_scale, gain_rows, full_out, context, q_low, k_low, v_low, lse, scales,
        tables[0], tables[1], blocks[:, None], blocks[None, :], gain_last, tops,
        hats, seq, full_qkv, *flat_grads,
    )
    return results


def open_call(w_qkv, w_out, gains, rows, w_gu, w_down, tables, blocks):
    grid = Grid()
    n, outer, inner = grid.dp, grid.outer, grid.inner
    chips, tensor = grid.chips, grid.tensor
    count, width = rows.shape
    length = count * tensor
    lead, slab, span = w_qkv.shape
    gain_count = gains.shape[0]
    half = slab // 2
    part_tall = span // 2
    heads = span // HEAD
    shard_units = w_gu.shape[2]
    units = shard_units // outer
    parts = outer * inner
    ring = 2 * lead + 3
    steps = list(range(1, outer))
    tall = min(256, length)
    tile = 512
    lines = 32
    bf16, f32 = jnp.bfloat16, jnp.float32
    mesh_id = pl.DeviceIdType.MESH

    def kernel(*refs):
        pieces = [refs[11 + j * outer : 11 + (j + 1) * outer] for j in range(inner)]
        body(*refs[:11], pieces, *refs[11 + parts :])

    def body(
        qkv_any, out_any, rows_any, gu_any, down_any, gains_ref, cos_ref, sin_ref, id_col, id_row, rows_ref,
        pieces, qkv_out, flat_out, seq_out,
        gain_rows, hat_ref, scale_ref, q_low, k_low, v_low, lse_ref, context, attn_hat, o_scale, resid, resid_low, top_ref,
        qkv_ref, out_w_ref, seq_ref, all_gains, qkv_wide, out_wide, gu_wide, down_wide, cast,
        square, squares, core_send, core_land, hold, chip_send, chip_land,
        s_ring, r_ring, s_row, r_row, s_z, r_z, s_y, r_y, s_sq, r_sq, s_core, r_core, s_chip, r_chip, local,
    ):
        g = Grid()

        def tensor_peer(k, flip):
            core = 1 - g.core_at if flip else g.core_at
            return (g.dp_at, lax.rem(g.chip_at + k + chips, chips) * 2 + core)

        def dp_peer(s, j):
            across = g.outer_flip(g.outer_at, s) * inner
            return (across + lax.rem(g.inner_at + j + inner, inner), g.tensor_at)

        near = [tensor_peer(k, f) for k in range(chips) for f in (0, 1) if (k, f) != (0, 0)]
        far = [dp_peer(s, 0) for s in range(1, outer)]
        far += [dp_peer(0, j) for j in sorted({1 % inner, inner - 1} - {0})]
        t_at = g.tensor_at
        place = g.path_of(g.dp_at)
        after = (g.index_of(lax.rem(place + 1, n)), t_at)
        before = (g.index_of(lax.rem(place + n - 1, n)), t_at)
        firsts = []
        for at, (src, dst) in enumerate(((qkv_any, qkv_wide), (out_any, out_wide))):
            firsts.append(pltpu.make_async_copy(src, dst, local.at[3 + at]))
            firsts[-1].start()
        greet(near + far + [after, before])

        def remote(src, dst, send, recv, peer):
            copy = pltpu.make_async_remote_copy(
                src_ref=src, dst_ref=dst, send_sem=send, recv_sem=recv,
                device_id=peer, device_id_type=mesh_id,
            )
            copy.start()
            return copy

        def dot(a, b, contract):
            return lax.dot_general(a, b, (contract, ((), ())), preferred_element_type=f32)

        def looped(total, make):
            lax.fori_loop(0, total, lambda i, c: (make(i), c)[1], 0)

        def rows_of(i, size):
            return pl.ds(pl.multiple_of(i * size, size), size)

        def fetch(src, dst, at):
            copy = pltpu.make_async_copy(src, dst, local.at[at])
            copy.start()
            return copy

        def views(item, index):
            if item == ring - 1:
                return 1, all_gains.at[index]
            if item >= 2 * lead:
                side = item - 2 * lead
                part = pl.ds(side * part_tall, part_tall)
                return 1 - 2 * side, out_w_ref.at[part, rows_of(index, slab)]
            side, c = item // lead, item % lead
            at = pl.ds(pl.multiple_of(index * slab + side * half, half), half)
            return 1 - 2 * side, qkv_ref.at[c, at]

        hops = {}

        def hop(step, item):
            way = views(item, 0)[0]
            index = g.index_of(lax.rem(place - way * step + n, n))
            _, view = views(item, index)
            hops[step, item] = remote(
                view,
                view,
                s_ring.at[step, item],
                r_ring.at[step, item],
                after if way == 1 else before,
            )

        def row_copy(slot, index, peer, src=None):
            at = seq_ref.at[rows_of(index, count)]
            return remote(at if src is None else src, at, s_row.at[slot], r_row.at[slot], peer)

        order = [c + side * lead for c in range(lead) for side in (0, 1)]
        order += list(range(2 * lead, ring))
        firsts[0].wait()
        for c in range(lead):

            def cast_own(i, c=c):
                at = rows_of(i, lines)
                there = pl.ds(pl.multiple_of(g.dp_at * slab + i * lines, lines), lines)
                qkv_ref[c, there] = qkv_wide[c, at].astype(bf16)

            looped(slab // lines, cast_own)
            for side in (0, 1):
                hop(0, c + side * lead)
        firsts[1].wait()

        def cast_flat(i):
            at = rows_of(i, lines)
            out_w_ref[at, rows_of(g.dp_at, slab)] = out_wide[at].astype(bf16)

        looped(span // lines, cast_flat)
        empty = jnp.zeros((16 - gain_count, slab), f32)
        all_gains[g.dp_at] = jnp.concatenate([gains_ref[...], empty], axis=0).astype(bf16)
        for item in range(2 * lead, ring):
            hop(0, item)
        row_copies = [
            row_copy(k - 1, t_at, tensor_peer(k, 0), rows_any) for k in range(1, chips)
        ]
        row_copies.append(row_copy(chips - 1, t_at, tensor_peer(0, 1), rows_any))
        wide = [fetch(gu_any, gu_wide, 1), fetch(down_any, down_wide, 2)]
        kept = fetch(rows_any, seq_ref.at[rows_of(t_at, count)], 5)

        def cast_wide(c):
            if c == 0:
                wide[0].wait()

            def cast_rows(i):
                at = rows_of(i, lines)
                cast[c, at] = gu_wide[c, at].astype(bf16)

            looped(slab // lines, cast_rows)

        def cast_turned():
            wide[1].wait()

            def cast_rows(i):
                at = rows_of(i, 256)
                cast[2, :, at] = down_wide[at].T.astype(bf16)

            looped(shard_units // 256, cast_rows)

        shadows = [lambda: cast_wide(0), lambda: cast_wide(1), cast_turned]
        for step in range(1, n - 1):
            for item in order:
                hops[step - 1, item].wait_recv()
                hop(step, item)
            if step <= chips - 1:
                row_copies[step - 1].wait_recv()
                source = lax.rem(g.chip_at - step + chips, chips) * 2 + g.core_at
                row_copies.append(row_copy(chips - 1 + step, source, tensor_peer(0, 1)))
            if shadows:
                shadows.pop(0)()

        def cut(s):
            return cast.at[:, :, rows_of(g.outer_flip(g.outer_at, s), units)]

        z_copies = {}

        def z_send(s, c):
            z_copies[s, c] = remote(
                cut(s).at[c], pieces[0][s].at[c], s_z.at[s, c], r_z.at[s, c], dp_peer(s, 0)
            )

        for c in (0, 1):
            for s in steps:
                z_send(s, c)
        own = fetch(cut(0), pieces[0][0], 0)
        y_copies = {}

        def pass_on(j, s, c):
            src = cut(0) if (j, s) == (1, 0) else pieces[j - 1][s]
            y_copies[j, s, c] = remote(
                src.at[c], pieces[j][s].at[c], s_y.at[j, s, c], r_y.at[j, s, c], dp_peer(0, 1)
            )

        if inner > 1:
            for c in range(3):
                pass_on(1, 0, c)
        duties = []
        for c in range(3):
            for s in steps:

                def duty(s=s, c=c):
                    z_copies[s, c].wait_recv()
                    if inner > 1:
                        pass_on(1, s, c)
                    if c == 0:
                        z_send(s, 2)

                duties.append(duty)
        for j in range(2, inner):
            for c in range(3):
                for s in [0] + steps:

                    def duty(j=j, s=s, c=c):
                        y_copies[j - 1, s, c].wait_recv()
                        pass_on(j, s, c)

                    duties.append(duty)

        def next_duties(times):
            for _ in range(times):
                if duties:
                    duties.pop(0)()

        for item in order:
            hops[n - 2, item].wait_recv()
        for copy in row_copies[chips - 1 :]:
            copy.wait_recv()
        kept.wait()
        outs = [fetch(qkv_ref, qkv_out, 3), fetch(out_w_ref, flat_out, 4), fetch(seq_ref, seq_out, 5)]

        def spread(i):
            gain_rows[:, rows_of(i, slab)] = all_gains[i].astype(f32)[:8]

        looped(n, spread)

        def project(i):
            at = rows_of(i, tall)
            x = seq_ref[at]
            lane = lax.broadcasted_iota(jnp.int32, (tall, 128), 1)
            sums = jnp.zeros((tall, 128), f32)
            for c in range(2):
                value = dot(x, qkv_ref[c], ((1,), (0,)))
                hat_ref[c, at] = value
                sums = jnp.where(lane == c, jnp.sum(value * value, axis=1, keepdims=True), sums)
            v_low[at] = dot(x, qkv_ref[2], ((1,), (0,))).astype(bf16)
            square[:, at] = sums.T[:8]

        looped(length // tall, project)
        sq_copies = []
        for k in range(chips):
            for f in (0, 1):
                if (k, f) != (0, 0):
                    at = k * 2 + f - 1
                    sq_copies.append(
                        remote(square, squares.at[at], s_sq.at[at], r_sq.at[at], tensor_peer(k, f))
                    )
        for copy in sq_copies:
            copy.wait_recv()
        sign = jnp.where(lax.broadcasted_iota(jnp.int32, (tall, HEAD), 1) < HEAD // 2, -1.0, 1.0)

        def rotate(i):
            at = rows_of(i, tall)
            sums = square[:, at]
            for copy_at in range(tensor - 1):
                sums = sums + squares[copy_at, :, at]
            column = jnp.concatenate([sums, jnp.zeros((120, tall), f32)], axis=0).T
            scales = lax.rsqrt(column / width + norm_eps)
            scale_ref[at] = scales
            cosine, sine = cos_ref[at], sin_ref[at] * sign
            for c, low in ((0, q_low), (1, k_low)):
                hat = hat_ref[c, at] * scales[:, c : c + 1]
                hat_ref[c, at] = hat
                normed = hat * gain_rows[c : c + 1, rows_of(t_at, span)]
                for h in range(heads):
                    cols = slice(h * HEAD, (h + 1) * HEAD)
                    value = normed[:, cols]
                    turned = pltpu.roll(value, HEAD // 2, 1)
                    low[at, cols] = (value * cosine + turned * sine).astype(bf16)

        looped(length // tall, rotate)
        scale = HEAD ** (-0.5)
        top_ref[...] = jnp.full((8, 128), masked_value, f32)
        for h in range(heads):
            cols = slice(h * HEAD, (h + 1) * HEAD)

            def attend(i, best, cols=cols, h=h):
                at = rows_of(i, tall)
                raw = dot(q_low[at, cols], k_low[:, cols], ((1,), (1,))) * scale
                masked = jnp.where(id_row[...] <= id_col[at], raw, masked_value)
                top = jnp.max(masked, axis=1, keepdims=True)
                weight = jnp.exp(masked - top)
                total = jnp.sum(weight, axis=1, keepdims=True)
                probs = (weight / total).astype(bf16)
                context[at, cols] = dot(probs, v_low[:, cols], ((1,), (0,))).astype(bf16)
                lse_ref[at, h : h + 1] = top + jnp.log(total)
                return jnp.maximum(best, jnp.max(top, axis=0, keepdims=True))

            best = lax.fori_loop(
                0, length // tall, attend, jnp.full((1, 1), masked_value, f32)
            )
            top_ref[h : h + 1] = jnp.broadcast_to(best, (1, 128))
            if 2 * (h + 1) == heads:
                next_duties(1)
        next_duties(2 * len(steps) - 1)

        def out_rows(k, flip, store):
            chip = lax.rem(g.chip_at + k, chips)
            core = 1 - g.core_at if flip else g.core_at
            at = rows_of(chip * 2 + core, count)

            def columns(i):
                cols = rows_of(i, tile)
                store(cols, dot(context[at], out_w_ref[:, cols], ((1,), (0,))))

            looped(width // tile, columns)

        chip_order = list(range(1, chips)) + [0]
        core_copies, chip_copies = {}, {}
        for k in chip_order:

            def store(cols, value, k=k):
                core_send[k, :, cols] = value.astype(bf16)

            out_rows(k, True, store)
            core_copies[k] = remote(
                core_send.at[k], core_land.at[k], s_core.at[k], r_core.at[k], tensor_peer(0, 1)
            )
        for k in chip_order:

            def store(cols, value, k=k):
                hold[k, :, cols] = value

            out_rows(k, False, store)
            if k:
                core_copies[k].wait_recv()

                def add(i, k=k):
                    at = rows_of(i, lines)
                    chip_send[k - 1, at] = (hold[k, at] + core_land[k, at].astype(f32)).astype(bf16)

                looped(count // lines, add)
                chip_copies[k] = remote(
                    chip_send.at[k - 1], chip_land.at[k - 1], s_chip.at[k], r_chip.at[k], tensor_peer(k, 0)
                )
        core_copies[0].wait_recv()
        for k in range(1, chips):
            chip_copies[k].wait_recv()

        def close(i):
            at = rows_of(i, lines)
            raw = hold[0, at] + core_land[0, at].astype(f32)
            for k in range(1, chips):
                raw = raw + chip_land[k - 1, at].astype(f32)
            scale_o = lax.rsqrt(jnp.mean(raw * raw, axis=1, keepdims=True) + norm_eps)
            hat = raw * scale_o
            attn_hat[at] = hat
            o_scale[at] = scale_o
            value = rows_ref[at].astype(f32) + hat * gain_rows[2:3]
            resid[at] = value
            resid_low[at] = value.astype(bf16)

        looped(count // lines, close)
        next_duties(len(duties))
        own.wait()
        for key, copy in y_copies.items():
            if key[0] == inner - 1:
                copy.wait_recv()
        for copy in outs:
            copy.wait()
        sent = list(hops.values()) + row_copies + list(z_copies.values()) + list(y_copies.values()) + sq_copies
        for copy in sent + list(core_copies.values()) + list(chip_copies.values()):
            copy.wait_send()

    shape = jax.ShapeDtypeStruct
    anywhere = pl.BlockSpec(memory_space=pl.ANY)
    vmem = pl.BlockSpec(memory_space=pltpu.VMEM)
    sems = pltpu.SemaphoreType.DMA
    results = pl.pallas_call(
        kernel,
        out_shape=(shape((3, slab, units), bf16),) * parts
        + (
            shape((lead, width, span), bf16),
            shape((span, width), bf16),
            shape((length, width), bf16),
            shape((8, width), f32),
            shape((2, length, span), f32),
            shape((length, 128), f32),
            shape((length, span), bf16),
            shape((length, span), bf16),
            shape((length, span), bf16),
            shape((length, heads), f32),
            shape((length, span), bf16),
            shape((count, width), f32),
            shape((count, 1), f32),
            shape((count, width), f32),
            shape((count, width), bf16),
            shape((8, 128), f32),
        ),
        in_specs=[anywhere] * 5 + [vmem] * 6,
        out_specs=(anywhere,) * (parts + 3) + (vmem,) * 13,
        scratch_shapes=[
            pltpu.VMEM((lead, width, span), bf16),
            pltpu.VMEM((span, width), bf16),
            pltpu.VMEM((length, width), bf16),
            pltpu.VMEM((n, 16, slab), bf16),
            pltpu.VMEM(w_qkv.shape, f32),
            pltpu.VMEM(w_out.shape, f32),
            pltpu.VMEM(w_gu.shape, f32),
            pltpu.VMEM(w_down.shape, f32),
            pltpu.VMEM((3, slab, shard_units), bf16),
            pltpu.VMEM((8, length), f32),
            pltpu.VMEM((tensor - 1, 8, length), f32),
            pltpu.VMEM((chips, count, width), bf16),
            pltpu.VMEM((chips, count, width), bf16),
            pltpu.VMEM((chips, count, width), f32),
            pltpu.VMEM((max(chips - 1, 1), count, width), bf16),
            pltpu.VMEM((max(chips - 1, 1), count, width), bf16),
            sems((n - 1, ring)),
            sems((n - 1, ring)),
            sems((2 * chips - 1,)),
            sems((2 * chips - 1,)),
            sems((outer, 3)),
            sems((outer, 3)),
            sems((inner, outer, 3)),
            sems((inner, outer, 3)),
            sems((tensor - 1,)),
            sems((tensor - 1,)),
            sems((chips,)),
            sems((chips,)),
            sems((chips,)),
            sems((chips,)),
            sems((7,)),
        ],
        compiler_params=pltpu.CompilerParams(
            collective_id=0, has_side_effects=True, vmem_limit_bytes=58 * 2**20
        ),
    )(
        w_qkv, w_out, rows, w_gu, w_down, gains, tables[0], tables[1],
        blocks[:, None], blocks[None, :], rows,
    )
    pieces = [results[j * outer : (j + 1) * outer] for j in range(inner)]
    return pieces, results[parts:]


def unit_kernel_call(rows_low, resid, cotangent, gain, pieces):
    grid = Grid()
    outer, chips, inner = grid.outer, grid.chips, grid.inner
    total_rows, width = rows_low.shape
    units = pieces[0][0].shape[2]
    slab = pieces[0][0].shape[1]
    flat_pieces = [piece for row in pieces for piece in row]
    parts = len(flat_pieces)
    halves = 2
    count = total_rows // halves
    both = 2 * count
    per = min(2, chips)
    groups = chips // per
    blocks = outer * groups
    tall = per * both
    held = per if groups > 1 else max(per - 1, 1)
    links = outer * (chips - 1)
    steps = list(range(outer))
    far_first = [0] + steps[2:] + steps[1:2]

    def units_of(of_steps):
        return [(s, i) for s in of_steps for i in range(groups)]

    orders = {
        (0, 0): units_of(far_first),
        (0, 1): units_of(far_first),
        (1, 0): units_of(steps),
        (1, 1): units_of(far_first),
    }
    grad_order = units_of(far_first)
    tile = 512
    wide_tiles = width // tile
    unit_tile = min(256, units)
    lines = 32
    bf16, f32 = jnp.bfloat16, jnp.float32
    mesh_id = pl.DeviceIdType.MESH

    def plan():
        chip_us, core_us, hop_us = 5.6, 0.6, 2.0
        free = {"x": 0.0, "core": 0.0, "z near": 0.0, "z far": 0.0}
        arrive, done, tasks = {}, {}, {}

        def send(link, when, us):
            free[link] = max(free[link], when) + us
            return free[link] + hop_us

        def add(name, needs, us, after=None):
            tasks[name] = (needs, us, after)

        def send_outer(s, now):
            return send("z near", now, 8.0) if s == 1 else send("z far", now, 10.5)

        def go(p, h):
            def then(now):
                if (p, h) != (0, 1):
                    for s in steps[1:]:
                        arrive["z", p, h, s] = send_outer(s, now)
                for k in range(1, chips):
                    arrive["x", p, h, 0, k] = send("x", now, chip_us)
                arrive["c", p, h, 0, 0] = send("core", now, core_us)

            return then

        def zf(p, h, s):
            def then(now):
                for k in range(1, chips):
                    arrive["x", p, h, s, k] = send("x", now, chip_us)
                arrive["c", p, h, s, 0] = send("core", now, core_us)
                if (p, h) == (0, 0):
                    arrive["z", 0, 1, s] = send_outer(s, now)

            return then

        def xf(p, h, s, k):
            def then(now):
                arrive["c", p, h, s, k] = send("core", now, core_us)

            return then

        def compute(p, h, s, i):
            def then(now):
                arrive["cr", p, h, s, i] = send("core", now, per * core_us)

            return then

        def cr(p, h, s, i):
            def then(now):
                for k in range(i * per, i * per + per):
                    if k:
                        arrive["xr", p, h, s, k] = send("x", now, chip_us)

            return then

        def xr(p, h, s):
            def then(now):
                if s:
                    arrive["zr", p, h, s] = send_outer(s, now)

            return then

        for p in (0, 1):
            for h in range(halves):
                if p == 0:
                    needs = [("do", ("go", 0, h - 1))] if h else []
                else:
                    needs = [("do", ("between", h))]
                add(("go", p, h), needs, 0.2, go(p, h))
                for s in steps[1:]:
                    add(("zf", p, h, s), [("at", ("z", p, h, s))], 0.2, zf(p, h, s))
                for s in steps:
                    for k in range(1, chips):
                        add(("xf", p, h, s, k), [("at", ("x", p, h, s, k))], 0.2, xf(p, h, s, k))
                order = orders[p, h]
                for n, (s, i) in enumerate(order):
                    needs = [("at", ("c", p, h, s, i * per + j)) for j in range(per)]
                    if n:
                        needs.append(("do", ("compute", p, h) + order[n - 1]))
                    add(("load", p, h, s, i), needs, 0.2)
                    needs = [("do", ("load", p, h, s, i))]
                    if n:
                        needs.append(("do", ("cr", p, h) + order[n - 1]))
                    add(("compute", p, h, s, i), needs, 4.0, compute(p, h, s, i))
                    needs = [("at", ("cr", p, h, s, i)), ("do", ("compute", p, h, s, i))]
                    add(("cr", p, h, s, i), needs, 0.5, cr(p, h, s, i))
                for s in steps:
                    needs = [("do", ("cr", p, h, s, 0))]
                    needs += [("at", ("xr", p, h, s, k)) for k in range(1, chips)]
                    add(("xr", p, h, s), needs, 0.4, xr(p, h, s))
                for s in steps[1:]:
                    needs = [("at", ("zr", p, h, s)), ("do", ("xr", p, h, 0))]
                    add(("zr", p, h, s), needs, 0.4)
        for h in range(halves):
            needs = [("do", ("zr", 0, h, s)) for s in steps[1:]] + [("do", ("xr", 0, h, 0))]
            add(("between", h), needs, 1.0)
        for n, (s, i) in enumerate(grad_order):
            needs = [("do", ("compute", 1, h, s, i)) for h in range(halves)]
            if n:
                needs.append(("do", ("grads",) + grad_order[n - 1] + (2,)))
            add(("fetch", s, i), needs, 0.2)
            for c in range(3):
                needs = [("do", ("grads", s, i, c - 1) if c else ("fetch", s, i))]
                add(("grads", s, i, c), needs, 2.8)
        written = [(j, s) for j in range(inner) for s in range(outer)]
        for n, at in enumerate(written):
            needs = [("do", ("grads",) + grad_order[-1] + (2,))]
            if n:
                needs = [("do", ("write",) + written[n - 1])]
            add(("write",) + at, needs, 0.6)
        rank = {"compute": 1, "fetch": 2, "grads": 2, "write": 3}
        result = []
        now = 0.0
        while tasks:
            best = None
            for name, (needs, us, then) in tasks.items():
                ready = 0.0
                for kind, key in needs:
                    table = arrive if kind == "at" else done
                    if key not in table:
                        ready = None
                        break
                    ready = max(ready, table[key] + (1.0 if key[0] in ("load", "fetch") else 0.0))
                if ready is None:
                    continue
                key = (max(ready, now), rank.get(name[0], 0))
                if best is None or key < best[0]:
                    best = (key, name)
            (ready, _), name = best
            needs, us, then = tasks.pop(name)
            now = ready + us
            done[name] = now
            if then is not None:
                then(now)
            result.append(name)
        return result

    def kernel(*refs):
        piece_refs = refs[:parts]
        fixed = refs[parts : parts + 9]
        grad_refs = refs[parts + 9 : parts + 9 + 3 * inner]
        body(piece_refs, *fixed, grad_refs, *refs[parts + 9 + 3 * inner :])

    def body(
        piece_refs, rows_ref, resid_ref, cot_ref, gain_ref,
        out_ref, dres_ref, gain_out, all_x, all_dm, grad_refs,
        wg, wu, wd, buf, wide_buf, act, coef_gate, coef_up, d_gate, d_up, turned, acc_gate, acc_up, acc_down, stage,
        core_send, core_land, hold, keep, chip_send, chip_land, outer_send, outer_land, raw, d_mlp,
        s_outer, r_outer, s_chip, r_chip, s_core, r_core,
        s_core_sum, r_core_sum, s_chip_sum, r_chip_sum, s_outer_sum, r_outer_sum,
        local, local_own, local_wide, local_w, local_g,
    ):
        g = Grid()
        core_peer = (g.dp_at, g.chip_at * 2 + 1 - g.core_at)

        def chip_peer(k):
            return (g.dp_at, lax.rem(g.chip_at + k + chips, chips) * 2 + g.core_at)

        def outer_peer(s):
            return (g.outer_flip(g.outer_at, s) * inner + g.inner_at, g.tensor_at)

        greet(
            [core_peer]
            + [chip_peer(k) for k in range(1, chips)]
            + [outer_peer(s) for s in range(1, outer)]
        )

        def remote(src, dst, send, recv, peer):
            copy = pltpu.make_async_remote_copy(
                src_ref=src, dst_ref=dst, send_sem=send, recv_sem=recv,
                device_id=peer, device_id_type=mesh_id,
            )
            copy.start()
            return copy

        def fetch(src, dst, sem):
            copy = pltpu.make_async_copy(src, dst, sem)
            copy.start()
            return copy

        def dot(a, b, contract):
            return lax.dot_general(a, b, (contract, ((), ())), preferred_element_type=f32)

        def looped(total, make):
            lax.fori_loop(0, total, lambda i, c: (make(i), c)[1], 0)

        def by_lines(make):
            looped(count // lines, lambda i: make(pl.ds(pl.multiple_of(i * lines, lines), lines)))

        def by_tiles(make):
            looped(wide_tiles, lambda i: make(pl.ds(pl.multiple_of(i * tile, tile), tile)))

        weights = (wg, wu, wd)
        fetches = []

        def fetch_weights():
            for j in range(inner):
                for s in range(outer):
                    index = g.outer_flip(g.outer_at, s) * inner
                    index = index + lax.rem(g.inner_at - j + inner, inner)
                    span = pl.ds(pl.multiple_of(index * slab, slab), slab)
                    for c in range(3):
                        at = j * outer + s
                        fetches.append(
                            fetch(piece_refs[at].at[c], weights[c].at[span], local_w.at[at, c])
                        )

        mine, theirs = pl.ds(0, count), pl.ds(count, count)
        every = (all_x, all_dm)
        copies, sums, loads, own = {}, {}, {}, {}
        unsent = {(p, h): [] for p in (0, 1) for h in range(halves)}

        def track(p, h, copy):
            unsent[p, h].append(copy)
            return copy

        def core_copy(p, h, s, k, src):
            dst = every[p].at[h, s, k, theirs]
            copies["c", p, h, s, k] = track(
                p, h, remote(src, dst, s_core.at[p, h, s, k], r_core.at[p, h, s, k], core_peer)
            )

        def chip_copy(p, h, s, k, src):
            dst = every[p].at[h, s, k, mine]
            copies["x", p, h, s, k] = track(
                p, h, remote(src, dst, s_chip.at[p, h, s, k], r_chip.at[p, h, s, k], chip_peer(k))
            )

        def outer_copy(p, h, s):
            source = (rows_ref, d_mlp)[p].at[pl.ds(h * count, count)]
            dst = every[p].at[h, s, 0, mine]
            copies["z", p, h, s] = track(
                p, h, remote(source, dst, s_outer.at[p, h, s], r_outer.at[p, h, s], outer_peer(s))
            )

        def go(p, h):
            source = (rows_ref, d_mlp)[p].at[pl.ds(h * count, count)]
            if (p, h) != (0, 1):
                for s in steps[1:]:
                    outer_copy(p, h, s)
            for k in range(1, chips):
                chip_copy(p, h, 0, k, source)
            core_copy(p, h, 0, 0, source)
            own[p, h] = fetch(source, every[p].at[h, 0, 0, mine], local_own.at[p, h])
            if p == 0 and h == 0:
                fetch_weights()

        def part_out(h, s, i, cols, part_sum):
            for j in range(per):
                own_rows = part_sum[j * both : j * both + count]
                if i * per + j == 0:
                    keep[h, s, :, cols] = own_rows
                else:
                    hold[h, min(j, held - 1), :, cols] = own_rows
                core_send[h, j, :, cols] = part_sum[j * both + count : (j + 1) * both].astype(bf16)

        def forward(h, unit, s, i):
            for j in range(units // unit_tile):
                cols = pl.ds(j * unit_tile, unit_tile)
                rows = buf[h].reshape(tall, width)
                gate = dot(rows, wg[:, cols], ((1,), (0,)))
                up = dot(rows, wu[:, cols], ((1,), (0,)))
                sigma = jax.nn.sigmoid(gate)
                silu = gate * sigma
                act[unit, h, :, cols] = (silu * up).astype(bf16)
                coef_up[unit, h, :, cols] = silu.astype(bf16)
                coef_gate[unit, h, :, cols] = (
                    up * sigma * (1.0 + gate * (1.0 - sigma))
                ).astype(bf16)
            by_tiles(
                lambda cols: part_out(h, s, i, cols, dot(act[unit, h], wd[cols, :], ((1,), (1,))))
            )

        def backward(h, unit, s, i):
            for j in range(units // unit_tile):
                cols = pl.ds(j * unit_tile, unit_tile)
                d_act = dot(buf[h].reshape(tall, width), wd[:, cols], ((1,), (0,)))
                d_gate[unit, h, :, cols] = (d_act * coef_gate[unit, h, :, cols].astype(f32)).astype(bf16)
                d_up[unit, h, :, cols] = (d_act * coef_up[unit, h, :, cols].astype(f32)).astype(bf16)

            def into(cols):
                part_sum = dot(d_gate[unit, h], wg[cols, :], ((1,), (1,)))
                part_sum = part_sum + dot(d_up[unit, h], wu[cols, :], ((1,), (1,)))
                part_out(h, s, i, cols, part_sum)

            by_tiles(into)

        def weight_grads(unit, c):
            first = unit == grad_order[0][0] * groups + grad_order[0][1]
            left, right, acc = ((d_gate, 0, acc_gate), (d_up, 0, acc_up), (act, 1, acc_down))[c]
            turned[...] = left[unit].reshape(halves * tall, units).T

            def grads(cols):
                rows = wide_buf[right, :, :, :, cols].reshape(halves * tall, tile)
                value = dot(turned[...], rows, ((1,), (0,)))
                acc[:, cols] = value if first else acc[:, cols] + value

            by_tiles(grads)

        def between(h):
            def lines_of(i, total):
                at_rows = pl.ds(pl.multiple_of(h * count + i * lines, lines), lines)
                value = raw[at_rows]
                scale = lax.rsqrt(jnp.mean(value * value, axis=1, keepdims=True) + norm_eps)
                hat = value * scale
                gain_row = gain_ref[3:4]
                out_ref[at_rows] = (resid_ref[at_rows] + hat * gain_row).astype(bf16)
                top = cot_ref[at_rows].astype(f32)
                upstream = top * gain_row
                mean = jnp.mean(upstream * hat, axis=1, keepdims=True)
                d_mlp[at_rows] = (scale * (upstream - hat * mean)).astype(bf16)
                return total + jnp.sum(top * hat, axis=0, keepdims=True)

            zero = jnp.zeros((1, width), f32)
            total = lax.fori_loop(0, count // lines, lines_of, zero)
            gain_out[...] = total if h == 0 else gain_out[...] + total

        batches = []

        def write_grads(j, s):
            index = g.outer_flip(g.outer_at, s) * inner
            index = index + lax.rem(g.inner_at + j, inner)
            span = pl.ds(pl.multiple_of(index * slab, slab), slab)
            slot = len(batches) % 2
            if len(batches) >= 2:
                for copy in batches[-2]:
                    copy.wait()
            batch = []
            for c, acc in enumerate((acc_gate, acc_up, acc_down)):
                stage[slot, c] = acc[:, span].astype(bf16)
                batch.append(
                    fetch(stage.at[slot, c], grad_refs[j * 3 + c].at[s], local_g.at[slot, c])
                )
            batches.append(batch)

        def core_sum(p, h, s, i):
            unit = s * groups + i
            sums["c", p, h, unit].wait_recv()
            for j in range(per):
                chip = i * per + j
                if chip == 0:

                    def add(at_rows):
                        keep[h, s, at_rows] = keep[h, s, at_rows] + core_land[h, unit, j, at_rows].astype(f32)

                    by_lines(add)
                    continue
                there = s * (chips - 1) + chip - 1

                def add(at_rows):
                    total = hold[h, min(j, held - 1), at_rows] + core_land[h, unit, j, at_rows].astype(f32)
                    chip_send[h, there, at_rows] = total.astype(bf16)

                by_lines(add)
                sums["x", p, h, s, chip] = track(
                    p, h,
                    remote(
                        chip_send.at[h, there], chip_land.at[h, there],
                        s_chip_sum.at[p, h, there], r_chip_sum.at[p, h, there], chip_peer(-chip),
                    ),
                )

        def chip_sum(p, h, s):
            for k in range(1, chips):
                sums["x", p, h, s, k].wait_recv()

            def add(at_rows):
                total = keep[h, s, at_rows]
                for k in range(1, chips):
                    total = total + chip_land[h, s * (chips - 1) + k - 1, at_rows].astype(f32)
                if s == 0:
                    raw[pl.ds(pl.multiple_of(h * count + at_rows.start, lines), lines)] = total
                else:
                    outer_send[h, s - 1, at_rows] = total.astype(bf16)

            by_lines(add)
            if s:
                sums["z", p, h, s] = track(
                    p, h,
                    remote(
                        outer_send.at[h, s - 1], outer_land.at[h, s - 1],
                        s_outer_sum.at[p, h, s], r_outer_sum.at[p, h, s], outer_peer(s),
                    ),
                )

        def outer_sum(p, h, s):
            sums["z", p, h, s].wait_recv()

            def add(at_rows):
                there = pl.ds(pl.multiple_of(h * count + at_rows.start, lines), lines)
                raw[there] = raw[there] + outer_land[h, s - 1, at_rows].astype(f32)

            by_lines(add)

        def all_sent(p, h):
            for copy in unsent[p, h]:
                copy.wait_send()

        last_core = {}
        for task in plan():
            name, args = task[0], task[1:]
            if name == "go":
                go(*args)
            elif name == "zf":
                p, h, s = args
                copies["z", p, h, s].wait_recv()
                source = every[p].at[h, s, 0, mine]
                for k in range(1, chips):
                    chip_copy(p, h, s, k, source)
                core_copy(p, h, s, 0, source)
                if (p, h) == (0, 0):
                    outer_copy(0, 1, s)
            elif name == "xf":
                p, h, s, k = args
                copies["x", p, h, s, k].wait_recv()
                core_copy(p, h, s, k, every[p].at[h, s, k, mine])
            elif name == "load":
                p, h, s, i = args
                for j in range(per):
                    copies["c", p, h, s, i * per + j].wait_recv()
                if (s, i) == (0, 0):
                    own[p, h].wait()
                src = every[p].at[h, s, pl.ds(i * per, per)]
                loads[args] = fetch(src, buf.at[h], local.at[p, h, s * groups + i])
            elif name == "compute":
                p, h, s, i = args
                unit = s * groups + i
                if p == 0 and not loads.get("weights"):
                    loads["weights"] = True
                    for copy in fetches:
                        copy.wait()
                loads[args].wait()
                if h in last_core:
                    last_core[h].wait_send()
                (forward, backward)[p](h, unit, s, i)
                last_core[h] = remote(
                    core_send.at[h], core_land.at[h, unit],
                    s_core_sum.at[p, h, unit], r_core_sum.at[p, h, unit], core_peer,
                )
                sums["c", p, h, unit] = last_core[h]
            elif name == "cr":
                core_sum(*args)
            elif name == "xr":
                chip_sum(*args)
            elif name == "zr":
                outer_sum(*args)
            elif name == "between":
                all_sent(0, args[0])
                between(args[0])
            elif name == "fetch":
                s, i = args
                loads[task] = []
                for at, src in enumerate((all_x, all_dm)):
                    for h in range(halves):
                        loads[task].append(
                            fetch(
                                src.at[h, s, pl.ds(i * per, per)],
                                wide_buf.at[at, h],
                                local_wide.at[s * groups + i, at * halves + h],
                            )
                        )
            elif name == "grads":
                s, i, c = args
                if c == 0:
                    for copy in loads["fetch", s, i]:
                        copy.wait()
                weight_grads(s * groups + i, c)
            elif name == "write":
                write_grads(*args)

        looped(
            total_rows // lines,
            lambda i: close_rows(pl.ds(pl.multiple_of(i * lines, lines), lines), dres_ref, raw, cot_ref),
        )
        for h in range(halves):
            all_sent(1, h)
            last_core[h].wait_send()
        for batch in batches[-2:]:
            for copy in batch:
                copy.wait()

    shape = jax.ShapeDtypeStruct
    anywhere = pl.BlockSpec(memory_space=pl.ANY)
    near = pl.BlockSpec(memory_space=pltpu.VMEM)
    sems = pltpu.SemaphoreType.DMA
    flops = 2 * 9 * halves * tall * blocks * width * units
    results = pl.pallas_call(
        kernel,
        out_shape=(
            shape((total_rows, width), bf16),
            shape((total_rows, width), f32),
            shape((1, width), f32),
            shape((halves, outer, chips, both, width), bf16),
            shape((halves, outer, chips, both, width), bf16),
        )
        + (shape((outer, units, slab), bf16),) * (3 * inner),
        in_specs=[anywhere] * (parts + 1) + [near] * 3,
        out_specs=(near, near, near) + (anywhere,) * (2 + 3 * inner),
        scratch_shapes=[
            pltpu.VMEM((width, units), bf16),
            pltpu.VMEM((width, units), bf16),
            pltpu.VMEM((width, units), bf16),
            pltpu.VMEM((halves, per, both, width), bf16),
            pltpu.VMEM((2, halves, per, both, width), bf16),
            pltpu.VMEM((blocks, halves, tall, units), bf16),
            pltpu.VMEM((blocks, halves, tall, units), bf16),
            pltpu.VMEM((blocks, halves, tall, units), bf16),
            pltpu.VMEM((blocks, halves, tall, units), bf16),
            pltpu.VMEM((blocks, halves, tall, units), bf16),
            pltpu.VMEM((units, halves * tall), bf16),
            pltpu.VMEM((units, width), f32),
            pltpu.VMEM((units, width), f32),
            pltpu.VMEM((units, width), f32),
            pltpu.VMEM((2, 3, units, slab), bf16),
            pltpu.VMEM((halves, per, count, width), bf16),
            pltpu.VMEM((halves, blocks, per, count, width), bf16),
            pltpu.VMEM((halves, held, count, width), f32),
            pltpu.VMEM((halves, outer, count, width), f32),
            pltpu.VMEM((halves, links, count, width), bf16),
            pltpu.VMEM((halves, links, count, width), bf16),
            pltpu.VMEM((halves, outer - 1, count, width), bf16),
            pltpu.VMEM((halves, outer - 1, count, width), bf16),
            pltpu.VMEM((total_rows, width), f32),
            pltpu.VMEM((total_rows, width), bf16),
            sems((2, halves, outer)),
            sems((2, halves, outer)),
            sems((2, halves, outer, chips)),
            sems((2, halves, outer, chips)),
            sems((2, halves, outer, chips)),
            sems((2, halves, outer, chips)),
            sems((2, halves, blocks)),
            sems((2, halves, blocks)),
            sems((2, halves, links)),
            sems((2, halves, links)),
            sems((2, halves, outer)),
            sems((2, halves, outer)),
            sems((2, halves, blocks)),
            sems((2, halves)),
            sems((blocks, 2 * halves)),
            sems((parts, 3)),
            sems((2, 3)),
        ],
        compiler_params=pltpu.CompilerParams(
            collective_id=2, has_side_effects=True, vmem_limit_bytes=62 * 2**20
        ),
        cost_estimate=pl.CostEstimate(flops=flops, bytes_accessed=64 * 2**20, transcendentals=0),
    )(*flat_pieces, rows_low, resid, cotangent, gain)
    grads = results[5:]
    return results[:3] + ([[grads[j * 3 + c] for j in range(inner)] for c in range(3)],)


def close_rows(at_rows, dres_ref, raw, cot_ref):
    dres_ref[at_rows] = raw[at_rows] + cot_ref[at_rows].astype(jnp.float32)


def adam_kernel(turned, w_ref, m_ref, v_ref, g_ref, *rest):
    scale_ref = rest[0] if len(rest) == 5 else None
    w_out, m_out, v_out, c_out = rest[-4:]
    grad = g_ref[...].T if turned else g_ref[...]
    new, first, second = adam_step(
        w_ref[...], grad, m_ref[...], v_ref[...], rate_matrix, weight_decay
    )
    if scale_ref is not None:
        new = new * scale_ref[...]
    w_out[...] = new
    m_out[...] = first
    v_out[...] = second
    c_out[...] = new.astype(jnp.bfloat16)


def adam_call(param, grads, at, first, second, scale=None):
    mats, rows, columns = param.shape
    turned = scale is not None
    spec = pl.BlockSpec((None, rows, columns), lambda k: (k, 0, 0))
    grad_spec = pl.BlockSpec((None,) + grads.shape[1:], lambda k: (at + k, 0, 0))
    specs = [spec] * 3 + [grad_spec]
    values = [param, first, second, grads]
    if turned:
        values.append(scale)
        specs.append(pl.BlockSpec((None, 1, columns), lambda k: (k, 0, 0)))
    outs = [jax.ShapeDtypeStruct(param.shape, jnp.float32)] * 3
    outs.append(jax.ShapeDtypeStruct(param.shape, jnp.bfloat16))
    size = param.size
    return pl.pallas_call(
        functools.partial(adam_kernel, turned),
        grid=(mats,),
        in_specs=specs,
        out_specs=[spec] * 4,
        out_shape=outs,
        cost_estimate=pl.CostEstimate(
            flops=20 * size, bytes_accessed=28 * size, transcendentals=2 * size
        ),
        compiler_params=pltpu.CompilerParams(vmem_limit_bytes=60 * 2**20),
    )(*values)


def adam_units_kernel(turned, at_ref, w_ref, m_ref, v_ref, g_ref, w_out, m_out, v_out, c_out):
    grad = g_ref[...].astype(jnp.float32)
    if turned:
        grad = grad.T
    new, first, second = adam_step(
        w_ref[...], grad, m_ref[...], v_ref[...], rate_matrix, weight_decay
    )
    w_out[...] = new
    m_out[...] = first
    v_out[...] = second
    c_out[...] = new.astype(jnp.bfloat16)


def adam_units(grid, param, first, second, grads, begin, turned):
    n = grid.outer
    _, _, units, wide = grads.shape
    mats = param.shape[0] if turned else 1
    if not turned:
        spec = pl.BlockSpec((units, wide), lambda c, k, at: (k, 0))
    else:
        spec = pl.BlockSpec((None, wide, units), lambda c, k, at: (c, 0, k))
    grad_spec = pl.BlockSpec(
        (None, None, units, wide), lambda c, k, at: (begin + c, lax.bitwise_xor(at[0], k), 0, 0)
    )
    size = param.size
    outs = [jax.ShapeDtypeStruct(param.shape, jnp.float32)] * 3
    outs.append(jax.ShapeDtypeStruct(param.shape, jnp.bfloat16))
    return pl.pallas_call(
        functools.partial(adam_units_kernel, turned),
        grid_spec=pltpu.PrefetchScalarGridSpec(
            num_scalar_prefetch=1,
            grid=(mats, n),
            in_specs=[spec] * 3 + [grad_spec],
            out_specs=[spec] * 4,
        ),
        out_shape=outs,
        cost_estimate=pl.CostEstimate(
            flops=20 * size, bytes_accessed=28 * size, transcendentals=2 * size
        ),
        compiler_params=pltpu.CompilerParams(vmem_limit_bytes=60 * 2**20),
    )(grid.outer_at.astype(jnp.int32)[None], param, first, second, grads)


def local(
    tokens,
    cotangent,
    block_ids,
    w_qkv,
    m_qkv,
    v_qkv,
    w_out,
    m_out,
    v_out,
    w_gu,
    m_gu,
    v_gu,
    w_down,
    m_down,
    v_down,
    gains,
    gain_m,
    gain_v,
):
    grid = Grid()
    local_x = tokens[0]
    gain_count = gains.shape[0]
    tables = rope_tables(local_x.shape[0] * grid.tensor, HEAD)
    pieces, kept = open_call(
        w_qkv,
        w_out,
        gains,
        local_x,
        w_gu,
        w_down,
        tables,
        block_ids[0],
    )
    full_qkv, full_out, seq_x, gain_rows = kept[:4]
    hats, scales, q_low, k_low, v_low, log_total, context_low = kept[4:11]
    attn_hat, o_scale, resid, resid_low, tops = kept[11:]
    output, d_resid, gain_last, unit_grads = unit_kernel_call(
        resid_low, resid, cotangent[0], gain_rows, pieces
    )
    backs, part, part_gains, tops, grad_tokens = attend_back_call(
        d_resid,
        attn_hat,
        o_scale,
        gain_rows,
        full_out,
        context_low,
        q_low,
        k_low,
        v_low,
        log_total,
        hats,
        scales,
        tables,
        block_ids[0],
        seq_x,
        full_qkv,
        gain_last,
        tops,
        unit_grads,
    )
    part_gains = part_gains[:gain_count]
    head_top = tops[: w_qkv.shape[2] // HEAD, 0]
    factor = clip_tau / jnp.maximum(head_top, clip_tau)
    column = jnp.repeat(jnp.sqrt(factor), HEAD)
    column_scale = jnp.stack([column, column, jnp.ones_like(column)])[:, None, :]
    new_qkv, new_m_qkv, new_v_qkv, copy_qkv = adam_call(w_qkv, part, 0, m_qkv, v_qkv, column_scale)
    new_out, new_m_out, new_v_out, copy_out = [
        v[0] for v in adam_call(w_out[None], part, 3, m_out[None], v_out[None])
    ]
    new_gu, new_m_gu, new_v_gu, copy_gu = adam_units(grid, w_gu, m_gu, v_gu, backs, 0, True)
    new_down, new_m_down, new_v_down, copy_down = adam_units(
        grid, w_down, m_down, v_down, backs, 2, False
    )
    new_gains, new_gain_m, new_gain_v = adam_step(gains, part_gains, gain_m, gain_v, rate_gain, 0.0)
    return (
        output[None],
        grad_tokens[None],
        new_qkv,
        new_m_qkv,
        new_v_qkv,
        copy_qkv,
        new_out,
        new_m_out,
        new_v_out,
        copy_out,
        new_gu,
        new_m_gu,
        new_v_gu,
        copy_gu,
        new_down,
        new_m_down,
        new_v_down,
        copy_down,
        new_gains,
        new_gain_m,
        new_gain_v,
        factor,
    )


def solution(mesh):
    return jax.shard_map(
        local,
        mesh=mesh,
        in_specs=(
            P("dp", "tensor", None),
            P("dp", "tensor", None),
            P("dp", None),
            P(None, "dp", "tensor"),
            P(None, "dp", "tensor"),
            P(None, "dp", "tensor"),
            P("tensor", "dp"),
            P("tensor", "dp"),
            P("tensor", "dp"),
            P(None, "dp", "tensor"),
            P(None, "dp", "tensor"),
            P(None, "dp", "tensor"),
            P("tensor", "dp"),
            P("tensor", "dp"),
            P("tensor", "dp"),
            P(None, "dp"),
            P(None, "dp"),
            P(None, "dp"),
        ),
        out_specs=(
            P("dp", "tensor", None),
            P("dp", "tensor", None),
            P(None, "dp", "tensor"),
            P(None, "dp", "tensor"),
            P(None, "dp", "tensor"),
            P(None, "dp", "tensor"),
            P("tensor", "dp"),
            P("tensor", "dp"),
            P("tensor", "dp"),
            P("tensor", "dp"),
            P(None, "dp", "tensor"),
            P(None, "dp", "tensor"),
            P(None, "dp", "tensor"),
            P(None, "dp", "tensor"),
            P("tensor", "dp"),
            P("tensor", "dp"),
            P("tensor", "dp"),
            P("tensor", "dp"),
            P(None, "dp"),
            P(None, "dp"),
            P(None, "dp"),
            P("tensor"),
        ),
        check_vma=False,
    )
```

```python
import functools

import jax
import jax.numpy as jnp
import numpy as np
from jax import lax
from jax.experimental import pallas as pl
from jax.experimental.pallas import tpu as pltpu
from jax.sharding import PartitionSpec as P

HEAD = 128
STEP = 5


norm_eps = 1e-06
rope_base = 500000.0
beta_one = 0.9
beta_two = 0.95
rate_matrix = 0.01
rate_gain = 0.6
weight_decay = 0.1
adam_eps = 1e-08
clip_tau = 9.0
masked_value = -1e30


def rope_tables(length, size):
    half = size // 2
    freq = np.float32(rope_base) ** (-(np.arange(half, dtype=np.float32) * np.float32(2.0 / size)))
    angle = np.arange(length, dtype=np.float32)[:, None] * freq[None, :]
    angle = np.concatenate([angle, angle], axis=1)
    return (jnp.asarray(np.cos(angle)), jnp.asarray(np.sin(angle)))


def adam_step(param, grad, first, second, rate, decay):
    first = beta_one * first + (1.0 - beta_one) * grad
    second = beta_two * second + (1.0 - beta_two) * grad * grad
    fix_one = 1.0 - beta_one**STEP
    fix_two = 1.0 - beta_two**STEP
    update = first / fix_one / (jnp.sqrt(second / fix_two) + adam_eps)
    return (param - rate * (update + decay * param), first, second)


class Grid:
    def __init__(self):
        self.dp = lax.axis_size("dp")
        self.tensor = lax.axis_size("tensor")
        self.inner = 1
        while self.inner * self.inner * 4 <= self.dp:
            self.inner *= 2
        self.outer = self.dp // self.inner
        self.chips = self.tensor // 2
        self.dp_at = lax.axis_index("dp")
        self.tensor_at = lax.axis_index("tensor")
        self.inner_at = self.dp_at % self.inner
        self.chip_at = self.tensor_at // 2
        self.core_at = self.tensor_at % 2
        self.outer_at = self.dp_at // self.inner

    def path_of(self, index):
        column, row = index // self.inner, index % self.inner
        return row * self.outer + column + (row % 2) * (self.outer - 1 - 2 * column)

    def outer_flip(self, index, step):
        result = 0
        for bit in bits(self.outer):
            side = index // bit % 2
            result = result + bit * (1 - side if step & bit else side)
        return result

    def index_of(self, place):
        row, column = place // self.outer, place % self.outer
        return (column + (row % 2) * (self.outer - 1 - 2 * column)) * self.inner + row


def bits(count):
    return [1 << k for k in range(count.bit_length() - 1)]


def greet(peers):
    barrier = pltpu.get_barrier_semaphore()
    for peer in peers:
        pl.semaphore_signal(barrier, inc=1, device_id=peer, device_id_type=pl.DeviceIdType.MESH)
    pl.semaphore_wait(barrier, len(peers))


def attend_back_call(
    d_resid, attn_hat, o_scale, gain_rows, full_out, context, q_low, k_low, v_low, lse, hats, scales,
    tables, blocks, seq, full_qkv, gain_last, tops, unit_grads,
):
    grid = Grid()
    n, outer, inner, chips, tensor = grid.dp, grid.outer, grid.inner, grid.chips, grid.tensor
    count, width = d_resid.shape
    length, span = context.shape
    heads = span // HEAD
    units, slab = unit_grads[0][0].shape[1:]
    thin = width // n
    half = span // 2
    tall = min(256, length)
    tile = 512
    lines = 32
    ring = 8 + 2
    gain_item, top_item = 8, 9
    bf16, f32 = jnp.bfloat16, jnp.float32
    mesh_id = pl.DeviceIdType.MESH
    flat_grads = [unit_grads[c][j] for j in range(inner) for c in range(3)]
    some = len(flat_grads)
    z_steps = list(range(1, outer))

    def kernel(*refs):
        fixed, far_in, grads_in = refs[:17], refs[17:20], refs[20 : 20 + some]
        rest = refs[20 + some :]
        body(*fixed, far_in, grads_in, *rest)

    def body(
        dres_ref, hat_ref, o_scale_ref, gain_ref, out_w, ctx, q_ref, k_ref, v_ref, lse_ref, scale_ref,
        cos_ref, sin_ref, id_col, id_row, last_ref, tops_ref, far_in, grads_in,
        backs, part_ref, gains_out, tops_out, tokens_out,
        hats, seq, qkv_w, seq_do, d_ctx, d_q, d_k, d_v, d_low, probs_low, whole, terms, row_terms, turned,
        land, land_gain, land_top, own_gain, peer_gain, inners, peer_inners,
        grad_own, grad_land, grad_sum, core_send, core_land, hold, chip_send, chip_land,
        s_ring, r_ring, s_row, r_row, s_in, r_in, s_y, r_y, s_z, r_z, s_core, r_core, s_chip, r_chip, s_gain, r_gain, local,
    ):
        hats_in, seq_in, qkv_in = far_in
        g = Grid()

        def tensor_peer(k, flip):
            core = 1 - g.core_at if flip else g.core_at
            return (g.dp_at, lax.rem(g.chip_at + k + chips, chips) * 2 + core)

        def dp_peer(s, j):
            across = g.outer_flip(g.outer_at, s) * inner
            return (across + lax.rem(g.inner_at + j + inner, inner), g.tensor_at)

        place = g.path_of(g.dp_at)
        after_dp = (g.index_of(lax.rem(place + 1, n)), g.tensor_at)
        before_dp = (g.index_of(lax.rem(place + n - 1, n)), g.tensor_at)
        near = [tensor_peer(k, f) for k in range(chips) for f in (0, 1) if (k, f) != (0, 0)]
        far = [dp_peer(s, 0) for s in range(1, outer)] + [dp_peer(0, j) for j in range(1, inner)]
        greet(near + far + [after_dp, before_dp])

        def remote(src, dst, send, recv, peer):
            copy = pltpu.make_async_remote_copy(
                src_ref=src, dst_ref=dst, send_sem=send, recv_sem=recv,
                device_id=peer, device_id_type=mesh_id,
            )
            copy.start()
            return copy

        def fetch(src, dst, at):
            copy = pltpu.make_async_copy(src, dst, local.at[at])
            copy.start()
            return copy

        def dot(a, b, contract):
            return lax.dot_general(a, b, (contract, ((), ())), preferred_element_type=f32)

        def looped(total, make):
            lax.fori_loop(0, total, lambda i, c: (make(i), c)[1], 0)

        def rows_of(i, size):
            return pl.ds(pl.multiple_of(i * size, size), size)

        sent = []
        y_copies = {}
        sum_steps = [(c, s) for c in range(3) for s in z_steps + [0]]
        for c, s in sum_steps:
            for j in range(1, inner):
                copy = remote(
                    grads_in[j * 3 + c].at[s],
                    grad_land.at[j - 1, c, s],
                    s_y.at[j, c, s],
                    r_y.at[j, c, s],
                    dp_peer(0, j),
                )
                y_copies[j, c, s] = copy
                sent.append(copy)
        own_grads = [fetch(grads_in[c], grad_own.at[c], c) for c in range(3)]
        fetched = [fetch(hats_in, hats, 3), fetch(seq_in, seq, 4), fetch(qkv_in, qkv_w, 5)]
        z_copies = []
        keeps = []

        def unit_sums(times):
            for _ in range(times):
                if sum_steps:
                    unit_sum(*sum_steps.pop(0))

        def unit_sum(c, s):
            if s == (z_steps + [0])[0]:
                own_grads[c].wait()
            for j in range(1, inner):
                y_copies[j, c, s].wait_recv()

            def add(i):
                rows = rows_of(i, 64)
                total = grad_own[c, s, rows].astype(f32)
                for j in range(1, inner):
                    total = total + grad_land[j - 1, c, s, rows].astype(f32)
                grad_sum[c, s, rows] = total.astype(bf16)

            looped(units // 64, add)
            if s:
                z_copies.append(
                    remote(grad_sum.at[c, s], backs.at[c, s], s_z.at[c, s], r_z.at[c, s], dp_peer(s, 0))
                )
            else:
                keeps.append(fetch(grad_sum.at[c, 0], backs.at[c, 0], 6 + c))

        def way_of(item):
            return 1 if item >= 8 else 1 - 2 * (item // 4)

        def own(item, away):
            index = g.index_of(lax.rem(place - way_of(item) * away + 2 * n, n))
            if item == gain_item:
                return terms.at[index]
            if item == top_item:
                return tops_ref
            side, c = item // 4, item % 4
            return whole.at[c, pl.ds(side * half, half), rows_of(index, thin)]

        def landed(step, item):
            if item == gain_item:
                return land_gain.at[step]
            if item == top_item:
                return land_top.at[step]
            return land.at[step, item]

        hops = {}
        on_path = {}

        def hop(step, item):
            hops[step, item] = remote(
                own(item, 1) if step == 0 else landed(step - 1, item),
                landed(step, item),
                s_ring.at[step, item],
                r_ring.at[step, item],
                after_dp if way_of(item) == 1 else before_dp,
            )

        def depart(*items):
            for item in items:
                on_path[item] = 0
                hop(0, item)

        def advance(*items):
            for item in items:
                step = on_path.get(item, n) + 1
                if step >= n:
                    continue
                on_path[item] = step
                hops[step - 1, item].wait_recv()
                here = landed(step - 1, item)
                if item == top_item:
                    summed = jnp.maximum(here[...], tops_ref[...])
                else:
                    summed = here[...].astype(f32) + own(item, step + 1)[...].astype(f32)
                if step < n - 1:
                    here[...] = summed.astype(here.dtype)
                    hop(step, item)
                elif item == gain_item:
                    own_gain[0] = summed
                elif item == top_item:
                    tops_out[...] = summed
                else:
                    side, c = item // 4, item % 4
                    part_ref[c, pl.ds(side * half, half)] = summed

        def matrix_grad(c, left, right):
            turned[...] = left.T

            def columns(i):
                cols = rows_of(i, tile)
                whole[c, :, cols] = dot(turned[...], right[:, cols], ((1,), (0,))).astype(bf16)

            looped(width // tile, columns)

        t_at = g.tensor_at
        mine = rows_of(t_at, count)

        def open_rows(i, total):
            at = rows_of(i, lines)
            value, hat = dres_ref[at], hat_ref[at]
            upstream = value * gain_ref[2:3]
            mean = jnp.mean(upstream * hat, axis=1, keepdims=True)
            d_attn = (o_scale_ref[at] * (upstream - hat * mean)).astype(bf16)
            seq_do[pl.ds(pl.multiple_of(t_at * count + i * lines, lines), lines)] = d_attn
            return total + jnp.sum(value * hat, axis=0, keepdims=True)

        gain_attn = lax.fori_loop(0, count // lines, open_rows, jnp.zeros((1, width), f32))
        row_terms[...] = jnp.zeros((8, width), f32)
        row_terms[2:3] = gain_attn
        row_terms[3:4] = last_ref[...]
        moves, passed = [], []

        def row_copy(slot, index, peer):
            at = rows_of(index, count)
            copy = remote(seq_do.at[at], seq_do.at[at], s_row.at[slot], r_row.at[slot], peer)
            sent.append(copy)
            return copy

        for k in range(1, chips):
            moves.append(row_copy(k - 1, t_at, tensor_peer(k, 0)))
        to_core = row_copy(chips - 1, t_at, tensor_peer(0, 1))
        unit_sums(1)
        scale = HEAD ** (-0.5)
        for h in range(heads):
            cols = slice(h * HEAD, (h + 1) * HEAD)

            def weigh(i, c, cols=cols, h=h):
                at = rows_of(i, tall)
                raw = dot(q_ref[at, cols], k_ref[:, cols], ((1,), (1,))) * scale
                masked = jnp.where(id_row[...] <= id_col[at], raw, masked_value)
                probs_low[h, at] = jnp.exp(masked - lse_ref[at, h : h + 1]).astype(bf16)
                return c

            lax.fori_loop(0, length // tall, weigh, 0)
            if 2 * (h + 1) == heads:
                unit_sums(1)
        for k in range(1, chips):
            moves[k - 1].wait_recv()
            source = lax.rem(g.chip_at - k + chips, chips) * 2 + g.core_at
            passed.append(row_copy(chips - 1 + k, source, tensor_peer(0, 1)))
        to_core.wait_recv()
        unit_sums(1)
        for copy in passed:
            copy.wait_recv()

        def context_grad(i):
            at = rows_of(i, tall)
            d_ctx[at] = dot(seq_do[at], out_w[...], ((1,), (1,))).astype(bf16)

        looped(length // tall, context_grad)
        unit_sums(1)

        for h in range(heads):
            cols = slice(h * HEAD, (h + 1) * HEAD)

            def head(i, c, cols=cols, h=h):
                at = rows_of(i, tall)
                q_part, ctx_part = q_ref[at, cols], d_ctx[at, cols]
                probs_part = probs_low[h, at]
                probs = probs_part.astype(f32)
                d_probs = dot(ctx_part, v_ref[:, cols], ((1,), (1,)))
                mean = jnp.sum(probs * d_probs, axis=1, keepdims=True)
                d_scores = (probs * (d_probs - mean)).astype(bf16)
                d_q[at, cols] = dot(d_scores, k_ref[:, cols], ((1,), (0,))) * scale
                key = dot(d_scores, q_part, ((0,), (0,))) * scale
                value = dot(probs_part, ctx_part, ((0,), (0,)))
                d_k[:, cols] = jnp.where(i == 0, key, d_k[:, cols] + key)
                d_v[:, cols] = jnp.where(i == 0, value, d_v[:, cols] + value)
                return c

            d_k[:, cols] = jnp.zeros((length, HEAD), f32)
            d_v[:, cols] = jnp.zeros((length, HEAD), f32)
            lax.fori_loop(0, length // tall, head, 0)
            unit_sums(1)
        fetched[0].wait()
        sign = jnp.where(lax.broadcasted_iota(jnp.int32, (tall, HEAD), 1) < HEAD // 2, -1.0, 1.0)

        def unrotate(i, sums):
            at = rows_of(i, tall)
            cosine, sine = cos_ref[at], sin_ref[at]
            lane = lax.broadcasted_iota(jnp.int32, (tall, 128), 1)
            columns = jnp.zeros((tall, 128), f32)
            result = []
            for c, grad in ((0, d_q), (1, d_k)):
                total = jnp.zeros((tall, 1), f32)
                terms_row = []
                for h in range(heads):
                    cols = slice(h * HEAD, (h + 1) * HEAD)
                    value = grad[at, cols]
                    back = value * cosine - pltpu.roll(value * sine, HEAD // 2, 1) * sign
                    hat = hats[c, at, cols]
                    terms_row.append(jnp.sum(back * hat, axis=0, keepdims=True))
                    at_head = pl.ds(pl.multiple_of(t_at * span + h * HEAD, HEAD), HEAD)
                    back = back * gain_ref[c : c + 1, at_head]
                    grad[at, cols] = back
                    total = total + jnp.sum(back * hat, axis=1, keepdims=True)
                columns = jnp.where(lane == c, total, columns)
                result.append(sums[c] + jnp.concatenate(terms_row, axis=1))
            inners[:, at] = columns.T[:8]
            return tuple(result)

        zero = jnp.zeros((1, span), f32)
        gain_q, gain_k = lax.fori_loop(0, length // tall, unrotate, (zero, zero))
        offset = rows_of(t_at, span)
        row_terms[0:1, offset] = gain_q
        row_terms[1:2, offset] = gain_k
        in_copies = []
        for k in range(chips):
            for f in (0, 1):
                if (k, f) != (0, 0):
                    at = k * 2 + f - 1
                    in_copies.append(
                        remote(inners, peer_inners.at[at], s_in.at[at], r_in.at[at], tensor_peer(k, f))
                    )
        sent.extend(in_copies)
        matrix_grad(3, ctx[...], seq_do)
        depart(3, 7)
        for copy in in_copies:
            copy.wait_recv()
        unit_sums(1)

        def normed(i):
            at = rows_of(i, tall)
            sums = inners[:, at]
            for other in range(tensor - 1):
                sums = sums + peer_inners[other, :, at]
            column = jnp.concatenate([sums, jnp.zeros((120, tall), f32)], axis=0).T / width
            for c, grad in ((0, d_q), (1, d_k)):
                value = grad[at] - hats[c, at] * column[:, c : c + 1]
                d_low[c, at] = (scale_ref[at, c : c + 1] * value).astype(bf16)
            d_low[2, at] = d_v[at].astype(bf16)

        looped(length // tall, normed)
        fetched[1].wait()
        for c in (2, 0, 1):
            matrix_grad(c, d_low[c], seq)
            depart(c, c + 4)
            unit_sums(1)

        def place_terms(i, c):
            cols = pl.ds(pl.multiple_of(i * thin, thin), thin)
            terms[i] = row_terms[:, cols]
            return c

        lax.fori_loop(0, n, place_terms, 0)

        depart(gain_item, top_item)
        unit_sums(len(sum_steps))

        fetched[2].wait()
        chip_order = list(range(1, chips)) + [0]
        core_copies, chip_copies = {}, {}

        def token_rows(k, flip, store):
            chip = lax.rem(g.chip_at + k, chips)
            core = 1 - g.core_at if flip else g.core_at
            at = rows_of(chip * 2 + core, count)

            def columns(i):
                cols = rows_of(i, tile)
                total = dot(d_low[0, at], qkv_w[0, cols], ((1,), (1,)))
                for c in (1, 2):
                    total = total + dot(d_low[c, at], qkv_w[c, cols], ((1,), (1,)))
                store(cols, total)

            looped(width // tile, columns)

        duties = []
        for k in chip_order:

            def away(k=k):
                def store(cols, value):
                    core_send[k, :, cols] = value.astype(bf16)

                token_rows(k, True, store)
                core_copies[k] = remote(
                    core_send.at[k], core_land.at[k], s_core.at[k], r_core.at[k], tensor_peer(0, 1)
                )

            def here(k=k):
                def store(cols, value):
                    hold[k, :, cols] = value

                token_rows(k, False, store)

            def join(k=k):
                core_copies[k].wait_recv()

                def add(i):
                    at = rows_of(i, lines)
                    chip_send[k - 1, at] = (hold[k, at] + core_land[k, at].astype(f32)).astype(bf16)

                looped(count // lines, add)
                chip_copies[k] = remote(
                    chip_send.at[k - 1], chip_land.at[k - 1], s_chip.at[k], r_chip.at[k], tensor_peer(k, 0)
                )

            duties += [away, here] + ([join] if k else [])

        def close_tokens():
            core_copies[0].wait_recv()
            for k in range(1, chips):
                chip_copies[k].wait_recv()

            def close(i):
                at = rows_of(i, lines)
                total = dres_ref[at] + hold[0, at] + core_land[0, at].astype(f32)
                for k in range(1, chips):
                    total = total + chip_land[k - 1, at].astype(f32)
                tokens_out[at] = total

            looped(count // lines, close)

        duties.append(close_tokens)
        per_step = -(-len(duties) // (n - 2))
        for step in range(1, n):
            advance(3, 7, 2, 6, 0, 4, 1, 5, gain_item, top_item)
            for _ in range(per_step):
                if duties:
                    duties.pop(0)()
        peers = [tensor_peer(0, 1)] + [tensor_peer(k, 0) for k in range(1, chips)]
        first = remote(own_gain.at[0], peer_gain.at[0], s_gain.at[0], r_gain.at[0], peers[0])
        first.wait_recv()
        own_gain[1] = own_gain[0] + peer_gain[0]
        others = [
            remote(own_gain.at[1], peer_gain.at[k], s_gain.at[k], r_gain.at[k], peers[k])
            for k in range(1, chips)
        ]
        result = own_gain[1]
        for k in range(1, chips):
            others[k - 1].wait_recv()
            result = result + peer_gain[k]
        gains_out[...] = result
        for copy in z_copies:
            copy.wait()
        for copy in keeps:
            copy.wait()
        for copy in sent + list(hops.values()) + list(core_copies.values()):
            copy.wait_send()
        for copy in list(chip_copies.values()) + [first] + others:
            copy.wait_send()

    shape = jax.ShapeDtypeStruct
    anywhere = pl.BlockSpec(memory_space=pl.ANY)
    vmem = pl.BlockSpec(memory_space=pltpu.VMEM)
    sems = pltpu.SemaphoreType.DMA
    results = pl.pallas_call(
        kernel,
        out_shape=(
            shape((3, outer, units, slab), bf16),
            shape((4, span, thin), f32),
            shape((8, thin), f32),
            shape(tops.shape, f32),
            shape((count, width), f32),
        ),
        in_specs=[vmem] * 17 + [anywhere] * 3 + [anywhere] * some,
        out_specs=(anywhere,) + (vmem,) * 4,
        scratch_shapes=[
            pltpu.VMEM(hats.shape, f32),
            pltpu.VMEM(seq.shape, bf16),
            pltpu.VMEM(full_qkv.shape, bf16),
            pltpu.VMEM((length, width), bf16),
            pltpu.VMEM((length, span), bf16),
            pltpu.VMEM((length, span), f32),
            pltpu.VMEM((length, span), f32),
            pltpu.VMEM((length, span), f32),
            pltpu.VMEM((3, length, span), bf16),
            pltpu.VMEM((heads, length, length), bf16),
            pltpu.VMEM((4, span, width), bf16),
            pltpu.VMEM((n, 8, thin), f32),
            pltpu.VMEM((8, width), f32),
            pltpu.VMEM((span, length), bf16),
            pltpu.VMEM((n - 1, 8, half, thin), bf16),
            pltpu.VMEM((n - 1, 8, thin), f32),
            pltpu.VMEM((n - 1,) + tops.shape, f32),
            pltpu.VMEM((2, 8, thin), f32),
            pltpu.VMEM((chips, 8, thin), f32),
            pltpu.VMEM((8, length), f32),
            pltpu.VMEM((tensor - 1, 8, length), f32),
            pltpu.VMEM((3, outer, units, slab), bf16),
            pltpu.VMEM((max(inner - 1, 1), 3, outer, units, slab), bf16),
            pltpu.VMEM((3, outer, units, slab), bf16),
            pltpu.VMEM((chips, count, width), bf16),
            pltpu.VMEM((chips, count, width), bf16),
            pltpu.VMEM((chips, count, width), f32),
            pltpu.VMEM((max(chips - 1, 1), count, width), bf16),
            pltpu.VMEM((max(chips - 1, 1), count, width), bf16),
            sems((n - 1, ring)),
            sems((n - 1, ring)),
            sems((2 * chips - 1,)),
            sems((2 * chips - 1,)),
            sems((tensor - 1,)),
            sems((tensor - 1,)),
            sems((inner, 3, outer)),
            sems((inner, 3, outer)),
            sems((3, outer)),
            sems((3, outer)),
            sems((chips,)),
            sems((chips,)),
            sems((chips,)),
            sems((chips,)),
            sems((chips,)),
            sems((chips,)),
            sems((9,)),
        ],
        compiler_params=pltpu.CompilerParams(
            collective_id=1, has_side_effects=True, vmem_limit_bytes=62 * 2**20
        ),
    )(
        d_resid, attn_hat, o_scale, gain_rows, full_out, context, q_low, k_low, v_low, lse, scales,
        tables[0], tables[1], blocks[:, None], blocks[None, :], gain_last, tops,
        hats, seq, full_qkv, *flat_grads,
    )
    return results


def open_call(w_qkv, w_out, gains, rows, w_gu, w_down, tables, blocks):
    grid = Grid()
    n, outer, inner = grid.dp, grid.outer, grid.inner
    chips, tensor = grid.chips, grid.tensor
    count, width = rows.shape
    length = count * tensor
    lead, slab, span = w_qkv.shape
    gain_count = gains.shape[0]
    half = slab // 2
    part_tall = span // 2
    heads = span // HEAD
    shard_units = w_gu.shape[2]
    units = shard_units // outer
    parts = outer * inner
    ring = 2 * lead + 3
    steps = list(range(1, outer))
    tall = min(256, length)
    tile = 512
    lines = 32
    bf16, f32 = jnp.bfloat16, jnp.float32
    mesh_id = pl.DeviceIdType.MESH

    def kernel(*refs):
        pieces = [refs[11 + j * outer : 11 + (j + 1) * outer] for j in range(inner)]
        body(*refs[:11], pieces, *refs[11 + parts :])

    def body(
        qkv_any, out_any, rows_any, gu_any, down_any, gains_ref, cos_ref, sin_ref, id_col, id_row, rows_ref,
        pieces, qkv_out, flat_out, seq_out,
        gain_rows, hat_ref, scale_ref, q_low, k_low, v_low, lse_ref, context, attn_hat, o_scale, resid, resid_low, top_ref,
        qkv_ref, out_w_ref, seq_ref, all_gains, qkv_wide, out_wide, gu_wide, down_wide, cast,
        square, squares, core_send, core_land, hold, chip_send, chip_land,
        s_ring, r_ring, s_row, r_row, s_z, r_z, s_y, r_y, s_sq, r_sq, s_core, r_core, s_chip, r_chip, local,
    ):
        g = Grid()

        def tensor_peer(k, flip):
            core = 1 - g.core_at if flip else g.core_at
            return (g.dp_at, lax.rem(g.chip_at + k + chips, chips) * 2 + core)

        def dp_peer(s, j):
            across = g.outer_flip(g.outer_at, s) * inner
            return (across + lax.rem(g.inner_at + j + inner, inner), g.tensor_at)

        near = [tensor_peer(k, f) for k in range(chips) for f in (0, 1) if (k, f) != (0, 0)]
        far = [dp_peer(s, 0) for s in range(1, outer)]
        far += [dp_peer(0, j) for j in sorted({1 % inner, inner - 1} - {0})]
        t_at = g.tensor_at
        place = g.path_of(g.dp_at)
        after = (g.index_of(lax.rem(place + 1, n)), t_at)
        before = (g.index_of(lax.rem(place + n - 1, n)), t_at)
        firsts = []
        for at, (src, dst) in enumerate(((qkv_any, qkv_wide), (out_any, out_wide))):
            firsts.append(pltpu.make_async_copy(src, dst, local.at[3 + at]))
            firsts[-1].start()
        greet(near + far + [after, before])

        def remote(src, dst, send, recv, peer):
            copy = pltpu.make_async_remote_copy(
                src_ref=src, dst_ref=dst, send_sem=send, recv_sem=recv,
                device_id=peer, device_id_type=mesh_id,
            )
            copy.start()
            return copy

        def dot(a, b, contract):
            return lax.dot_general(a, b, (contract, ((), ())), preferred_element_type=f32)

        def looped(total, make):
            lax.fori_loop(0, total, lambda i, c: (make(i), c)[1], 0)

        def rows_of(i, size):
            return pl.ds(pl.multiple_of(i * size, size), size)

        def fetch(src, dst, at):
            copy = pltpu.make_async_copy(src, dst, local.at[at])
            copy.start()
            return copy

        def views(item, index):
            if item == ring - 1:
                return 1, all_gains.at[index]
            if item >= 2 * lead:
                side = item - 2 * lead
                part = pl.ds(side * part_tall, part_tall)
                return 1 - 2 * side, out_w_ref.at[part, rows_of(index, slab)]
            side, c = item // lead, item % lead
            at = pl.ds(pl.multiple_of(index * slab + side * half, half), half)
            return 1 - 2 * side, qkv_ref.at[c, at]

        hops = {}

        def hop(step, item):
            way = views(item, 0)[0]
            index = g.index_of(lax.rem(place - way * step + n, n))
            _, view = views(item, index)
            hops[step, item] = remote(
                view,
                view,
                s_ring.at[step, item],
                r_ring.at[step, item],
                after if way == 1 else before,
            )

        def row_copy(slot, index, peer, src=None):
            at = seq_ref.at[rows_of(index, count)]
            return remote(at if src is None else src, at, s_row.at[slot], r_row.at[slot], peer)

        order = [c + side * lead for c in range(lead) for side in (0, 1)]
        order += list(range(2 * lead, ring))
        firsts[0].wait()
        for c in range(lead):

            def cast_own(i, c=c):
                at = rows_of(i, lines)
                there = pl.ds(pl.multiple_of(g.dp_at * slab + i * lines, lines), lines)
                qkv_ref[c, there] = qkv_wide[c, at].astype(bf16)

            looped(slab // lines, cast_own)
            for side in (0, 1):
                hop(0, c + side * lead)
        firsts[1].wait()

        def cast_flat(i):
            at = rows_of(i, lines)
            out_w_ref[at, rows_of(g.dp_at, slab)] = out_wide[at].astype(bf16)

        looped(span // lines, cast_flat)
        empty = jnp.zeros((16 - gain_count, slab), f32)
        all_gains[g.dp_at] = jnp.concatenate([gains_ref[...], empty], axis=0).astype(bf16)
        for item in range(2 * lead, ring):
            hop(0, item)
        row_copies = [
            row_copy(k - 1, t_at, tensor_peer(k, 0), rows_any) for k in range(1, chips)
        ]
        row_copies.append(row_copy(chips - 1, t_at, tensor_peer(0, 1), rows_any))
        wide = [fetch(gu_any, gu_wide, 1), fetch(down_any, down_wide, 2)]
        kept = fetch(rows_any, seq_ref.at[rows_of(t_at, count)], 5)

        def cast_wide(c):
            if c == 0:
                wide[0].wait()

            def cast_rows(i):
                at = rows_of(i, lines)
                cast[c, at] = gu_wide[c, at].astype(bf16)

            looped(slab // lines, cast_rows)

        def cast_turned():
            wide[1].wait()

            def cast_rows(i):
                at = rows_of(i, 256)
                cast[2, :, at] = down_wide[at].T.astype(bf16)

            looped(shard_units // 256, cast_rows)

        shadows = [lambda: cast_wide(0), lambda: cast_wide(1), cast_turned]
        for step in range(1, n - 1):
            for item in order:
                hops[step - 1, item].wait_recv()
                hop(step, item)
            if step <= chips - 1:
                row_copies[step - 1].wait_recv()
                source = lax.rem(g.chip_at - step + chips, chips) * 2 + g.core_at
                row_copies.append(row_copy(chips - 1 + step, source, tensor_peer(0, 1)))
            if shadows:
                shadows.pop(0)()

        def cut(s):
            return cast.at[:, :, rows_of(g.outer_flip(g.outer_at, s), units)]

        z_copies = {}

        def z_send(s):
            z_copies[s] = remote(cut(s), pieces[0][s], s_z.at[s], r_z.at[s], dp_peer(s, 0))

        for s in steps[:2]:
            z_send(s)
        own = fetch(cut(0), pieces[0][0], 0)
        y_copies = {}

        def pass_on(j, s):
            src = cut(0) if (j, s) == (1, 0) else pieces[j - 1][s]
            y_copies[j, s] = remote(src, pieces[j][s], s_y.at[j, s], r_y.at[j, s], dp_peer(0, 1))

        if inner > 1:
            pass_on(1, 0)
        duties = []
        for s in steps:

            def duty(s=s):
                z_copies[s].wait_recv()
                if s >= 2 and s + 1 < outer:
                    z_send(s + 1)
                if inner > 1:
                    pass_on(1, s)

            duties.append(duty)
        for j in range(2, inner):
            for s in [0] + steps:

                def duty(j=j, s=s):
                    y_copies[j - 1, s].wait_recv()
                    pass_on(j, s)

                duties.append(duty)

        def next_duties(times):
            for _ in range(times):
                if duties:
                    duties.pop(0)()

        for item in order:
            hops[n - 2, item].wait_recv()
        for copy in row_copies[chips - 1 :]:
            copy.wait_recv()
        kept.wait()
        outs = [fetch(qkv_ref, qkv_out, 3), fetch(out_w_ref, flat_out, 4), fetch(seq_ref, seq_out, 5)]

        def spread(i):
            gain_rows[:, rows_of(i, slab)] = all_gains[i].astype(f32)[:8]

        looped(n, spread)

        def project(i):
            at = rows_of(i, tall)
            x = seq_ref[at]
            lane = lax.broadcasted_iota(jnp.int32, (tall, 128), 1)
            sums = jnp.zeros((tall, 128), f32)
            for c in range(2):
                value = dot(x, qkv_ref[c], ((1,), (0,)))
                hat_ref[c, at] = value
                sums = jnp.where(lane == c, jnp.sum(value * value, axis=1, keepdims=True), sums)
            v_low[at] = dot(x, qkv_ref[2], ((1,), (0,))).astype(bf16)
            square[:, at] = sums.T[:8]

        looped(length // tall, project)
        sq_copies = []
        for k in range(chips):
            for f in (0, 1):
                if (k, f) != (0, 0):
                    at = k * 2 + f - 1
                    sq_copies.append(
                        remote(square, squares.at[at], s_sq.at[at], r_sq.at[at], tensor_peer(k, f))
                    )
        for copy in sq_copies:
            copy.wait_recv()
        sign = jnp.where(lax.broadcasted_iota(jnp.int32, (tall, HEAD), 1) < HEAD // 2, -1.0, 1.0)

        def rotate(i):
            at = rows_of(i, tall)
            sums = square[:, at]
            for copy_at in range(tensor - 1):
                sums = sums + squares[copy_at, :, at]
            column = jnp.concatenate([sums, jnp.zeros((120, tall), f32)], axis=0).T
            scales = lax.rsqrt(column / width + norm_eps)
            scale_ref[at] = scales
            cosine, sine = cos_ref[at], sin_ref[at] * sign
            for c, low in ((0, q_low), (1, k_low)):
                hat = hat_ref[c, at] * scales[:, c : c + 1]
                hat_ref[c, at] = hat
                normed = hat * gain_rows[c : c + 1, rows_of(t_at, span)]
                for h in range(heads):
                    cols = slice(h * HEAD, (h + 1) * HEAD)
                    value = normed[:, cols]
                    turned = pltpu.roll(value, HEAD // 2, 1)
                    low[at, cols] = (value * cosine + turned * sine).astype(bf16)

        looped(length // tall, rotate)
        scale = HEAD ** (-0.5)
        top_ref[...] = jnp.full((8, 128), masked_value, f32)
        for h in range(heads):
            cols = slice(h * HEAD, (h + 1) * HEAD)

            def attend(i, best, cols=cols, h=h):
                at = rows_of(i, tall)
                raw = dot(q_low[at, cols], k_low[:, cols], ((1,), (1,))) * scale
                masked = jnp.where(id_row[...] <= id_col[at], raw, masked_value)
                top = jnp.max(masked, axis=1, keepdims=True)
                weight = jnp.exp(masked - top)
                total = jnp.sum(weight, axis=1, keepdims=True)
                probs = (weight / total).astype(bf16)
                context[at, cols] = dot(probs, v_low[:, cols], ((1,), (0,))).astype(bf16)
                lse_ref[at, h : h + 1] = top + jnp.log(total)
                return jnp.maximum(best, jnp.max(top, axis=0, keepdims=True))

            best = lax.fori_loop(
                0, length // tall, attend, jnp.full((1, 1), masked_value, f32)
            )
            top_ref[h : h + 1] = jnp.broadcast_to(best, (1, 128))
            if h + 1 == heads - 1:
                next_duties(2)

        def out_rows(k, flip, store):
            chip = lax.rem(g.chip_at + k, chips)
            core = 1 - g.core_at if flip else g.core_at
            at = rows_of(chip * 2 + core, count)

            def columns(i):
                cols = rows_of(i, tile)
                store(cols, dot(context[at], out_w_ref[:, cols], ((1,), (0,))))

            looped(width // tile, columns)

        chip_order = list(range(1, chips)) + [0]
        core_copies, chip_copies = {}, {}
        for k in chip_order:

            def store(cols, value, k=k):
                core_send[k, :, cols] = value.astype(bf16)

            out_rows(k, True, store)
            core_copies[k] = remote(
                core_send.at[k], core_land.at[k], s_core.at[k], r_core.at[k], tensor_peer(0, 1)
            )
        for k in chip_order:

            def store(cols, value, k=k):
                hold[k, :, cols] = value

            out_rows(k, False, store)
            if k:
                core_copies[k].wait_recv()

                def add(i, k=k):
                    at = rows_of(i, lines)
                    chip_send[k - 1, at] = (hold[k, at] + core_land[k, at].astype(f32)).astype(bf16)

                looped(count // lines, add)
                chip_copies[k] = remote(
                    chip_send.at[k - 1], chip_land.at[k - 1], s_chip.at[k], r_chip.at[k], tensor_peer(k, 0)
                )
        core_copies[0].wait_recv()
        for k in range(1, chips):
            chip_copies[k].wait_recv()

        def close(i):
            at = rows_of(i, lines)
            raw = hold[0, at] + core_land[0, at].astype(f32)
            for k in range(1, chips):
                raw = raw + chip_land[k - 1, at].astype(f32)
            scale_o = lax.rsqrt(jnp.mean(raw * raw, axis=1, keepdims=True) + norm_eps)
            hat = raw * scale_o
            attn_hat[at] = hat
            o_scale[at] = scale_o
            value = rows_ref[at].astype(f32) + hat * gain_rows[2:3]
            resid[at] = value
            resid_low[at] = value.astype(bf16)

        looped(count // lines, close)
        next_duties(len(duties))
        own.wait()
        for key, copy in y_copies.items():
            if key[0] == inner - 1:
                copy.wait_recv()
        for copy in outs:
            copy.wait()
        sent = list(hops.values()) + row_copies + list(z_copies.values()) + list(y_copies.values()) + sq_copies
        for copy in sent + list(core_copies.values()) + list(chip_copies.values()):
            copy.wait_send()

    shape = jax.ShapeDtypeStruct
    anywhere = pl.BlockSpec(memory_space=pl.ANY)
    vmem = pl.BlockSpec(memory_space=pltpu.VMEM)
    sems = pltpu.SemaphoreType.DMA
    results = pl.pallas_call(
        kernel,
        out_shape=(shape((3, slab, units), bf16),) * parts
        + (
            shape((lead, width, span), bf16),
            shape((span, width), bf16),
            shape((length, width), bf16),
            shape((8, width), f32),
            shape((2, length, span), f32),
            shape((length, 128), f32),
            shape((length, span), bf16),
            shape((length, span), bf16),
            shape((length, span), bf16),
            shape((length, heads), f32),
            shape((length, span), bf16),
            shape((count, width), f32),
            shape((count, 1), f32),
            shape((count, width), f32),
            shape((count, width), bf16),
            shape((8, 128), f32),
        ),
        in_specs=[anywhere] * 5 + [vmem] * 6,
        out_specs=(anywhere,) * (parts + 3) + (vmem,) * 13,
        scratch_shapes=[
            pltpu.VMEM((lead, width, span), bf16),
            pltpu.VMEM((span, width), bf16),
            pltpu.VMEM((length, width), bf16),
            pltpu.VMEM((n, 16, slab), bf16),
            pltpu.VMEM(w_qkv.shape, f32),
            pltpu.VMEM(w_out.shape, f32),
            pltpu.VMEM(w_gu.shape, f32),
            pltpu.VMEM(w_down.shape, f32),
            pltpu.VMEM((3, slab, shard_units), bf16),
            pltpu.VMEM((8, length), f32),
            pltpu.VMEM((tensor - 1, 8, length), f32),
            pltpu.VMEM((chips, count, width), bf16),
            pltpu.VMEM((chips, count, width), bf16),
            pltpu.VMEM((chips, count, width), f32),
            pltpu.VMEM((max(chips - 1, 1), count, width), bf16),
            pltpu.VMEM((max(chips - 1, 1), count, width), bf16),
            sems((n - 1, ring)),
            sems((n - 1, ring)),
            sems((2 * chips - 1,)),
            sems((2 * chips - 1,)),
            sems((outer,)),
            sems((outer,)),
            sems((inner, outer)),
            sems((inner, outer)),
            sems((tensor - 1,)),
            sems((tensor - 1,)),
            sems((chips,)),
            sems((chips,)),
            sems((chips,)),
            sems((chips,)),
            sems((7,)),
        ],
        compiler_params=pltpu.CompilerParams(
            collective_id=0, has_side_effects=True, vmem_limit_bytes=58 * 2**20
        ),
    )(
        w_qkv, w_out, rows, w_gu, w_down, gains, tables[0], tables[1],
        blocks[:, None], blocks[None, :], rows,
    )
    pieces = [results[j * outer : (j + 1) * outer] for j in range(inner)]
    return pieces, results[parts:]


def unit_kernel_call(rows_low, resid, cotangent, gain, pieces):
    grid = Grid()
    outer, chips, inner = grid.outer, grid.chips, grid.inner
    total_rows, width = rows_low.shape
    units = pieces[0][0].shape[2]
    slab = pieces[0][0].shape[1]
    flat_pieces = [piece for row in pieces for piece in row]
    parts = len(flat_pieces)
    halves = 2
    count = total_rows // halves
    both = 2 * count
    per = min(2, chips)
    groups = chips // per
    blocks = outer * groups
    tall = per * both
    held = per if groups > 1 else max(per - 1, 1)
    links = outer * (chips - 1)
    steps = list(range(outer))
    far_first = [0] + steps[2:] + steps[1:2]

    def units_of(of_steps):
        return [(s, i) for s in of_steps for i in range(groups)]

    orders = {
        (0, 0): units_of(far_first),
        (0, 1): units_of(far_first),
        (1, 0): units_of(steps),
        (1, 1): units_of(far_first),
    }
    grad_order = units_of(far_first)
    tile = 512
    wide_tiles = width // tile
    unit_tile = min(256, units)
    lines = 32
    bf16, f32 = jnp.bfloat16, jnp.float32
    mesh_id = pl.DeviceIdType.MESH

    def plan():
        chip_us, core_us, hop_us = 5.6, 0.6, 2.0
        free = {"x": 0.0, "core": 0.0, "z near": 0.0, "z far": 0.0}
        arrive, done, tasks = {}, {}, {}

        def send(link, when, us):
            free[link] = max(free[link], when) + us
            return free[link] + hop_us

        def add(name, needs, us, after=None):
            tasks[name] = (needs, us, after)

        def send_outer(s, now):
            return send("z near", now, 8.0) if s == 1 else send("z far", now, 10.5)

        def go(p, h):
            def then(now):
                if (p, h) != (0, 1):
                    for s in steps[1:]:
                        arrive["z", p, h, s] = send_outer(s, now)
                for k in range(1, chips):
                    arrive["x", p, h, 0, k] = send("x", now, chip_us)
                arrive["c", p, h, 0, 0] = send("core", now, core_us)

            return then

        def zf(p, h, s):
            def then(now):
                for k in range(1, chips):
                    arrive["x", p, h, s, k] = send("x", now, chip_us)
                arrive["c", p, h, s, 0] = send("core", now, core_us)
                if (p, h) == (0, 0):
                    arrive["z", 0, 1, s] = send_outer(s, now)

            return then

        def xf(p, h, s, k):
            def then(now):
                arrive["c", p, h, s, k] = send("core", now, core_us)

            return then

        def compute(p, h, s, i):
            def then(now):
                arrive["cr", p, h, s, i] = send("core", now, per * core_us)

            return then

        def cr(p, h, s, i):
            def then(now):
                for k in range(i * per, i * per + per):
                    if k:
                        arrive["xr", p, h, s, k] = send("x", now, chip_us)

            return then

        def xr(p, h, s):
            def then(now):
                if s:
                    arrive["zr", p, h, s] = send_outer(s, now)

            return then

        for p in (0, 1):
            for h in range(halves):
                if p == 0:
                    needs = [("do", ("go", 0, h - 1))] if h else []
                else:
                    needs = [("do", ("between", h))]
                add(("go", p, h), needs, 0.2, go(p, h))
                for s in steps[1:]:
                    add(("zf", p, h, s), [("at", ("z", p, h, s))], 0.2, zf(p, h, s))
                for s in steps:
                    for k in range(1, chips):
                        add(("xf", p, h, s, k), [("at", ("x", p, h, s, k))], 0.2, xf(p, h, s, k))
                order = orders[p, h]
                for n, (s, i) in enumerate(order):
                    needs = [("at", ("c", p, h, s, i * per + j)) for j in range(per)]
                    if n:
                        needs.append(("do", ("front", p, h) + order[n - 1]))
                    add(("load", p, h, s, i), needs, 0.2)
                    add(("front", p, h, s, i), [("do", ("load", p, h, s, i))], (2.4, 1.6)[p])
                    needs = [("do", ("front", p, h, s, i))]
                    if n:
                        needs.append(("do", ("cr", p, h) + order[n - 1]))
                    add(("compute", p, h, s, i), needs, (1.6, 2.4)[p], compute(p, h, s, i))
                    needs = [("at", ("cr", p, h, s, i)), ("do", ("compute", p, h, s, i))]
                    add(("cr", p, h, s, i), needs, 0.5, cr(p, h, s, i))
                for s in steps:
                    needs = [("do", ("cr", p, h, s, 0))]
                    needs += [("at", ("xr", p, h, s, k)) for k in range(1, chips)]
                    add(("xr", p, h, s), needs, 0.4, xr(p, h, s))
                for s in steps[1:]:
                    needs = [("at", ("zr", p, h, s)), ("do", ("xr", p, h, 0))]
                    add(("zr", p, h, s), needs, 0.4)
        for h in range(halves):
            needs = [("do", ("zr", 0, h, s)) for s in steps[1:]] + [("do", ("xr", 0, h, 0))]
            add(("between", h), needs, 1.0)
        for n, (s, i) in enumerate(grad_order):
            needs = [("do", ("compute", 1, h, s, i)) for h in range(halves)]
            if n:
                needs.append(("do", ("grads",) + grad_order[n - 1] + (2,)))
            add(("fetch", s, i), needs, 0.2)
            for c in range(3):
                needs = [("do", ("grads", s, i, c - 1) if c else ("fetch", s, i))]
                add(("grads", s, i, c), needs, 2.8)
        written = [(j, s) for j in range(inner) for s in range(outer)]
        for n, at in enumerate(written):
            needs = [("do", ("grads",) + grad_order[-1] + (2,))]
            if n:
                needs = [("do", ("write",) + written[n - 1])]
            add(("write",) + at, needs, 0.6)
        rank = {"compute": 1, "front": 2, "fetch": 2, "grads": 3, "write": 4}
        result = []
        now = 0.0
        while tasks:
            best = None
            for name, (needs, us, then) in tasks.items():
                ready = 0.0
                for kind, key in needs:
                    table = arrive if kind == "at" else done
                    if key not in table:
                        ready = None
                        break
                    ready = max(ready, table[key] + (1.0 if key[0] in ("load", "fetch") else 0.0))
                if ready is None:
                    continue
                key = (max(ready, now), rank.get(name[0], 0))
                if best is None or key < best[0]:
                    best = (key, name)
            (ready, _), name = best
            needs, us, then = tasks.pop(name)
            now = ready + us
            done[name] = now
            if then is not None:
                then(now)
            result.append(name)
        return result

    def kernel(*refs):
        piece_refs = refs[:parts]
        fixed = refs[parts : parts + 9]
        grad_refs = refs[parts + 9 : parts + 9 + 3 * inner]
        body(piece_refs, *fixed, grad_refs, *refs[parts + 9 + 3 * inner :])

    def body(
        piece_refs, rows_ref, resid_ref, cot_ref, gain_ref,
        out_ref, dres_ref, gain_out, all_x, all_dm, grad_refs,
        wg, wu, wd, buf, wide_buf, act, coef_gate, coef_up, d_gate, d_up, turned, acc_gate, acc_up, acc_down, stage,
        core_send, core_land, hold, keep, chip_send, chip_land, outer_send, outer_land, raw, d_mlp,
        s_outer, r_outer, s_chip, r_chip, s_core, r_core,
        s_core_sum, r_core_sum, s_chip_sum, r_chip_sum, s_outer_sum, r_outer_sum,
        local, local_own, local_wide, local_w, local_g,
    ):
        g = Grid()
        core_peer = (g.dp_at, g.chip_at * 2 + 1 - g.core_at)

        def chip_peer(k):
            return (g.dp_at, lax.rem(g.chip_at + k + chips, chips) * 2 + g.core_at)

        def outer_peer(s):
            return (g.outer_flip(g.outer_at, s) * inner + g.inner_at, g.tensor_at)

        greet(
            [core_peer]
            + [chip_peer(k) for k in range(1, chips)]
            + [outer_peer(s) for s in range(1, outer)]
        )

        def remote(src, dst, send, recv, peer):
            copy = pltpu.make_async_remote_copy(
                src_ref=src, dst_ref=dst, send_sem=send, recv_sem=recv,
                device_id=peer, device_id_type=mesh_id,
            )
            copy.start()
            return copy

        def fetch(src, dst, sem):
            copy = pltpu.make_async_copy(src, dst, sem)
            copy.start()
            return copy

        def dot(a, b, contract):
            return lax.dot_general(a, b, (contract, ((), ())), preferred_element_type=f32)

        def looped(total, make):
            lax.fori_loop(0, total, lambda i, c: (make(i), c)[1], 0)

        def by_lines(make):
            looped(count // lines, lambda i: make(pl.ds(pl.multiple_of(i * lines, lines), lines)))

        def by_tiles(make):
            looped(wide_tiles, lambda i: make(pl.ds(pl.multiple_of(i * tile, tile), tile)))

        weights = (wg, wu, wd)
        fetches = []

        def fetch_weights():
            for j in range(inner):
                for s in range(outer):
                    index = g.outer_flip(g.outer_at, s) * inner
                    index = index + lax.rem(g.inner_at - j + inner, inner)
                    span = pl.ds(pl.multiple_of(index * slab, slab), slab)
                    for c in range(3):
                        at = j * outer + s
                        fetches.append(
                            fetch(piece_refs[at].at[c], weights[c].at[span], local_w.at[at, c])
                        )

        mine, theirs = pl.ds(0, count), pl.ds(count, count)
        every = (all_x, all_dm)
        copies, sums, loads, own = {}, {}, {}, {}
        unsent = {(p, h): [] for p in (0, 1) for h in range(halves)}

        def track(p, h, copy):
            unsent[p, h].append(copy)
            return copy

        def core_copy(p, h, s, k, src):
            dst = every[p].at[h, s, k, theirs]
            copies["c", p, h, s, k] = track(
                p, h, remote(src, dst, s_core.at[p, h, s, k], r_core.at[p, h, s, k], core_peer)
            )

        def chip_copy(p, h, s, k, src):
            dst = every[p].at[h, s, k, mine]
            copies["x", p, h, s, k] = track(
                p, h, remote(src, dst, s_chip.at[p, h, s, k], r_chip.at[p, h, s, k], chip_peer(k))
            )

        def outer_copy(p, h, s):
            source = (rows_ref, d_mlp)[p].at[pl.ds(h * count, count)]
            dst = every[p].at[h, s, 0, mine]
            copies["z", p, h, s] = track(
                p, h, remote(source, dst, s_outer.at[p, h, s], r_outer.at[p, h, s], outer_peer(s))
            )

        def go(p, h):
            source = (rows_ref, d_mlp)[p].at[pl.ds(h * count, count)]
            if (p, h) != (0, 1):
                for s in steps[1:]:
                    outer_copy(p, h, s)
            for k in range(1, chips):
                chip_copy(p, h, 0, k, source)
            core_copy(p, h, 0, 0, source)
            own[p, h] = fetch(source, every[p].at[h, 0, 0, mine], local_own.at[p, h])
            if p == 0 and h == 0:
                fetch_weights()

        def part_out(h, s, i, cols, part_sum):
            for j in range(per):
                own_rows = part_sum[j * both : j * both + count]
                if i * per + j == 0:
                    keep[h, s, :, cols] = own_rows
                else:
                    hold[h, min(j, held - 1), :, cols] = own_rows
                core_send[h, j, :, cols] = part_sum[j * both + count : (j + 1) * both].astype(bf16)

        def forward(h, unit):
            for j in range(units // unit_tile):
                cols = pl.ds(j * unit_tile, unit_tile)
                rows = buf[h].reshape(tall, width)
                gate = dot(rows, wg[:, cols], ((1,), (0,)))
                up = dot(rows, wu[:, cols], ((1,), (0,)))
                sigma = jax.nn.sigmoid(gate)
                silu = gate * sigma
                act[unit, h, :, cols] = (silu * up).astype(bf16)
                coef_up[unit, h, :, cols] = silu.astype(bf16)
                coef_gate[unit, h, :, cols] = (
                    up * sigma * (1.0 + gate * (1.0 - sigma))
                ).astype(bf16)

        def forward_out(h, unit, s, i):
            by_tiles(
                lambda cols: part_out(h, s, i, cols, dot(act[unit, h], wd[cols, :], ((1,), (1,))))
            )

        def backward(h, unit):
            for j in range(units // unit_tile):
                cols = pl.ds(j * unit_tile, unit_tile)
                d_act = dot(buf[h].reshape(tall, width), wd[:, cols], ((1,), (0,)))
                d_gate[unit, h, :, cols] = (d_act * coef_gate[unit, h, :, cols].astype(f32)).astype(bf16)
                d_up[unit, h, :, cols] = (d_act * coef_up[unit, h, :, cols].astype(f32)).astype(bf16)

        def backward_out(h, unit, s, i):
            def into(cols):
                part_sum = dot(d_gate[unit, h], wg[cols, :], ((1,), (1,)))
                part_sum = part_sum + dot(d_up[unit, h], wu[cols, :], ((1,), (1,)))
                part_out(h, s, i, cols, part_sum)

            by_tiles(into)

        def weight_grads(unit, c):
            first = unit == grad_order[0][0] * groups + grad_order[0][1]
            left, right, acc = ((d_gate, 0, acc_gate), (d_up, 0, acc_up), (act, 1, acc_down))[c]
            turned[...] = left[unit].reshape(halves * tall, units).T

            def grads(cols):
                rows = wide_buf[right, :, :, :, cols].reshape(halves * tall, tile)
                value = dot(turned[...], rows, ((1,), (0,)))
                acc[:, cols] = value if first else acc[:, cols] + value

            by_tiles(grads)

        def between(h):
            def lines_of(i, total):
                at_rows = pl.ds(pl.multiple_of(h * count + i * lines, lines), lines)
                value = raw[at_rows]
                scale = lax.rsqrt(jnp.mean(value * value, axis=1, keepdims=True) + norm_eps)
                hat = value * scale
                gain_row = gain_ref[3:4]
                out_ref[at_rows] = (resid_ref[at_rows] + hat * gain_row).astype(bf16)
                top = cot_ref[at_rows].astype(f32)
                upstream = top * gain_row
                mean = jnp.mean(upstream * hat, axis=1, keepdims=True)
                d_mlp[at_rows] = (scale * (upstream - hat * mean)).astype(bf16)
                return total + jnp.sum(top * hat, axis=0, keepdims=True)

            zero = jnp.zeros((1, width), f32)
            total = lax.fori_loop(0, count // lines, lines_of, zero)
            gain_out[...] = total if h == 0 else gain_out[...] + total

        batches = []

        def write_grads(j, s):
            index = g.outer_flip(g.outer_at, s) * inner
            index = index + lax.rem(g.inner_at + j, inner)
            span = pl.ds(pl.multiple_of(index * slab, slab), slab)
            slot = len(batches) % 2
            if len(batches) >= 2:
                for copy in batches[-2]:
                    copy.wait()
            batch = []
            for c, acc in enumerate((acc_gate, acc_up, acc_down)):
                stage[slot, c] = acc[:, span].astype(bf16)
                batch.append(
                    fetch(stage.at[slot, c], grad_refs[j * 3 + c].at[s], local_g.at[slot, c])
                )
            batches.append(batch)

        def core_sum(p, h, s, i):
            unit = s * groups + i
            sums["c", p, h, unit].wait_recv()
            for j in range(per):
                chip = i * per + j
                if chip == 0:

                    def add(at_rows):
                        keep[h, s, at_rows] = keep[h, s, at_rows] + core_land[h, unit, j, at_rows].astype(f32)

                    by_lines(add)
                    continue
                there = s * (chips - 1) + chip - 1

                def add(at_rows):
                    total = hold[h, min(j, held - 1), at_rows] + core_land[h, unit, j, at_rows].astype(f32)
                    chip_send[h, there, at_rows] = total.astype(bf16)

                by_lines(add)
                sums["x", p, h, s, chip] = track(
                    p, h,
                    remote(
                        chip_send.at[h, there], chip_land.at[h, there],
                        s_chip_sum.at[p, h, there], r_chip_sum.at[p, h, there], chip_peer(-chip),
                    ),
                )

        def chip_sum(p, h, s):
            for k in range(1, chips):
                sums["x", p, h, s, k].wait_recv()

            def add(at_rows):
                total = keep[h, s, at_rows]
                for k in range(1, chips):
                    total = total + chip_land[h, s * (chips - 1) + k - 1, at_rows].astype(f32)
                if s == 0:
                    raw[pl.ds(pl.multiple_of(h * count + at_rows.start, lines), lines)] = total
                else:
                    outer_send[h, s - 1, at_rows] = total.astype(bf16)

            by_lines(add)
            if s:
                sums["z", p, h, s] = track(
                    p, h,
                    remote(
                        outer_send.at[h, s - 1], outer_land.at[h, s - 1],
                        s_outer_sum.at[p, h, s], r_outer_sum.at[p, h, s], outer_peer(s),
                    ),
                )

        def outer_sum(p, h, s):
            sums["z", p, h, s].wait_recv()

            def add(at_rows):
                there = pl.ds(pl.multiple_of(h * count + at_rows.start, lines), lines)
                raw[there] = raw[there] + outer_land[h, s - 1, at_rows].astype(f32)

            by_lines(add)

        def all_sent(p, h):
            for copy in unsent[p, h]:
                copy.wait_send()

        last_core = {}
        for task in plan():
            name, args = task[0], task[1:]
            if name == "go":
                go(*args)
            elif name == "zf":
                p, h, s = args
                copies["z", p, h, s].wait_recv()
                source = every[p].at[h, s, 0, mine]
                for k in range(1, chips):
                    chip_copy(p, h, s, k, source)
                core_copy(p, h, s, 0, source)
                if (p, h) == (0, 0):
                    outer_copy(0, 1, s)
            elif name == "xf":
                p, h, s, k = args
                copies["x", p, h, s, k].wait_recv()
                core_copy(p, h, s, k, every[p].at[h, s, k, mine])
            elif name == "load":
                p, h, s, i = args
                for j in range(per):
                    copies["c", p, h, s, i * per + j].wait_recv()
                if (s, i) == (0, 0):
                    own[p, h].wait()
                src = every[p].at[h, s, pl.ds(i * per, per)]
                loads[args] = fetch(src, buf.at[h], local.at[p, h, s * groups + i])
            elif name == "front":
                p, h, s, i = args
                if p == 0 and not loads.get("weights"):
                    loads["weights"] = True
                    for copy in fetches:
                        copy.wait()
                loads[args].wait()
                (forward, backward)[p](h, s * groups + i)
            elif name == "compute":
                p, h, s, i = args
                unit = s * groups + i
                if h in last_core:
                    last_core[h].wait_send()
                (forward_out, backward_out)[p](h, unit, s, i)
                last_core[h] = remote(
                    core_send.at[h], core_land.at[h, unit],
                    s_core_sum.at[p, h, unit], r_core_sum.at[p, h, unit], core_peer,
                )
                sums["c", p, h, unit] = last_core[h]
            elif name == "cr":
                core_sum(*args)
            elif name == "xr":
                chip_sum(*args)
            elif name == "zr":
                outer_sum(*args)
            elif name == "between":
                all_sent(0, args[0])
                between(args[0])
            elif name == "fetch":
                s, i = args
                loads[task] = []
                for at, src in enumerate((all_x, all_dm)):
                    for h in range(halves):
                        loads[task].append(
                            fetch(
                                src.at[h, s, pl.ds(i * per, per)],
                                wide_buf.at[at, h],
                                local_wide.at[s * groups + i, at * halves + h],
                            )
                        )
            elif name == "grads":
                s, i, c = args
                if c == 0:
                    for copy in loads["fetch", s, i]:
                        copy.wait()
                weight_grads(s * groups + i, c)
            elif name == "write":
                write_grads(*args)

        looped(
            total_rows // lines,
            lambda i: close_rows(pl.ds(pl.multiple_of(i * lines, lines), lines), dres_ref, raw, cot_ref),
        )
        for h in range(halves):
            all_sent(1, h)
            last_core[h].wait_send()
        for batch in batches[-2:]:
            for copy in batch:
                copy.wait()

    shape = jax.ShapeDtypeStruct
    anywhere = pl.BlockSpec(memory_space=pl.ANY)
    near = pl.BlockSpec(memory_space=pltpu.VMEM)
    sems = pltpu.SemaphoreType.DMA
    flops = 2 * 9 * halves * tall * blocks * width * units
    results = pl.pallas_call(
        kernel,
        out_shape=(
            shape((total_rows, width), bf16),
            shape((total_rows, width), f32),
            shape((1, width), f32),
            shape((halves, outer, chips, both, width), bf16),
            shape((halves, outer, chips, both, width), bf16),
        )
        + (shape((outer, units, slab), bf16),) * (3 * inner),
        in_specs=[anywhere] * (parts + 1) + [near] * 3,
        out_specs=(near, near, near) + (anywhere,) * (2 + 3 * inner),
        scratch_shapes=[
            pltpu.VMEM((width, units), bf16),
            pltpu.VMEM((width, units), bf16),
            pltpu.VMEM((width, units), bf16),
            pltpu.VMEM((halves, per, both, width), bf16),
            pltpu.VMEM((2, halves, per, both, width), bf16),
            pltpu.VMEM((blocks, halves, tall, units), bf16),
            pltpu.VMEM((blocks, halves, tall, units), bf16),
            pltpu.VMEM((blocks, halves, tall, units), bf16),
            pltpu.VMEM((blocks, halves, tall, units), bf16),
            pltpu.VMEM((blocks, halves, tall, units), bf16),
            pltpu.VMEM((units, halves * tall), bf16),
            pltpu.VMEM((units, width), f32),
            pltpu.VMEM((units, width), f32),
            pltpu.VMEM((units, width), f32),
            pltpu.VMEM((2, 3, units, slab), bf16),
            pltpu.VMEM((halves, per, count, width), bf16),
            pltpu.VMEM((halves, blocks, per, count, width), bf16),
            pltpu.VMEM((halves, held, count, width), f32),
            pltpu.VMEM((halves, outer, count, width), f32),
            pltpu.VMEM((halves, links, count, width), bf16),
            pltpu.VMEM((halves, links, count, width), bf16),
            pltpu.VMEM((halves, outer - 1, count, width), bf16),
            pltpu.VMEM((halves, outer - 1, count, width), bf16),
            pltpu.VMEM((total_rows, width), f32),
            pltpu.VMEM((total_rows, width), bf16),
            sems((2, halves, outer)),
            sems((2, halves, outer)),
            sems((2, halves, outer, chips)),
            sems((2, halves, outer, chips)),
            sems((2, halves, outer, chips)),
            sems((2, halves, outer, chips)),
            sems((2, halves, blocks)),
            sems((2, halves, blocks)),
            sems((2, halves, links)),
            sems((2, halves, links)),
            sems((2, halves, outer)),
            sems((2, halves, outer)),
            sems((2, halves, blocks)),
            sems((2, halves)),
            sems((blocks, 2 * halves)),
            sems((parts, 3)),
            sems((2, 3)),
        ],
        compiler_params=pltpu.CompilerParams(
            collective_id=2, has_side_effects=True, vmem_limit_bytes=62 * 2**20
        ),
        cost_estimate=pl.CostEstimate(flops=flops, bytes_accessed=64 * 2**20, transcendentals=0),
    )(*flat_pieces, rows_low, resid, cotangent, gain)
    grads = results[5:]
    return results[:3] + ([[grads[j * 3 + c] for j in range(inner)] for c in range(3)],)


def close_rows(at_rows, dres_ref, raw, cot_ref):
    dres_ref[at_rows] = raw[at_rows] + cot_ref[at_rows].astype(jnp.float32)


def adam_kernel(turned, w_ref, m_ref, v_ref, g_ref, *rest):
    scale_ref = rest[0] if len(rest) == 5 else None
    w_out, m_out, v_out, c_out = rest[-4:]
    grad = g_ref[...].T if turned else g_ref[...]
    new, first, second = adam_step(
        w_ref[...], grad, m_ref[...], v_ref[...], rate_matrix, weight_decay
    )
    if scale_ref is not None:
        new = new * scale_ref[...]
    w_out[...] = new
    m_out[...] = first
    v_out[...] = second
    c_out[...] = new.astype(jnp.bfloat16)


def adam_call(param, grads, at, first, second, scale=None):
    mats, rows, columns = param.shape
    turned = scale is not None
    spec = pl.BlockSpec((None, rows, columns), lambda k: (k, 0, 0))
    grad_spec = pl.BlockSpec((None,) + grads.shape[1:], lambda k: (at + k, 0, 0))
    specs = [spec] * 3 + [grad_spec]
    values = [param, first, second, grads]
    if turned:
        values.append(scale)
        specs.append(pl.BlockSpec((None, 1, columns), lambda k: (k, 0, 0)))
    outs = [jax.ShapeDtypeStruct(param.shape, jnp.float32)] * 3
    outs.append(jax.ShapeDtypeStruct(param.shape, jnp.bfloat16))
    size = param.size
    return pl.pallas_call(
        functools.partial(adam_kernel, turned),
        grid=(mats,),
        in_specs=specs,
        out_specs=[spec] * 4,
        out_shape=outs,
        cost_estimate=pl.CostEstimate(
            flops=20 * size, bytes_accessed=28 * size, transcendentals=2 * size
        ),
        compiler_params=pltpu.CompilerParams(vmem_limit_bytes=32 * 2**20),
    )(*values)


def adam_units_kernel(turned, at_ref, w_ref, m_ref, v_ref, g_ref, w_out, m_out, v_out, c_out):
    grad = g_ref[...].astype(jnp.float32)
    if turned:
        grad = grad.T
    new, first, second = adam_step(
        w_ref[...], grad, m_ref[...], v_ref[...], rate_matrix, weight_decay
    )
    w_out[...] = new
    m_out[...] = first
    v_out[...] = second
    c_out[...] = new.astype(jnp.bfloat16)


def adam_units(grid, param, first, second, grads, begin, turned):
    n = grid.outer
    _, _, units, wide = grads.shape
    mats = param.shape[0] if turned else 1
    if not turned:
        spec = pl.BlockSpec((units, wide), lambda c, k, at: (k, 0))
    else:
        spec = pl.BlockSpec((None, wide, units), lambda c, k, at: (c, 0, k))
    grad_spec = pl.BlockSpec(
        (None, None, units, wide), lambda c, k, at: (begin + c, lax.bitwise_xor(at[0], k), 0, 0)
    )
    size = param.size
    outs = [jax.ShapeDtypeStruct(param.shape, jnp.float32)] * 3
    outs.append(jax.ShapeDtypeStruct(param.shape, jnp.bfloat16))
    return pl.pallas_call(
        functools.partial(adam_units_kernel, turned),
        grid_spec=pltpu.PrefetchScalarGridSpec(
            num_scalar_prefetch=1,
            grid=(mats, n),
            in_specs=[spec] * 3 + [grad_spec],
            out_specs=[spec] * 4,
        ),
        out_shape=outs,
        cost_estimate=pl.CostEstimate(
            flops=20 * size, bytes_accessed=28 * size, transcendentals=2 * size
        ),
        compiler_params=pltpu.CompilerParams(vmem_limit_bytes=32 * 2**20),
    )(grid.outer_at.astype(jnp.int32)[None], param, first, second, grads)


def local(
    tokens,
    cotangent,
    block_ids,
    w_qkv,
    m_qkv,
    v_qkv,
    w_out,
    m_out,
    v_out,
    w_gu,
    m_gu,
    v_gu,
    w_down,
    m_down,
    v_down,
    gains,
    gain_m,
    gain_v,
):
    grid = Grid()
    local_x = tokens[0]
    gain_count = gains.shape[0]
    tables = rope_tables(local_x.shape[0] * grid.tensor, HEAD)
    pieces, kept = open_call(
        w_qkv,
        w_out,
        gains,
        local_x,
        w_gu,
        w_down,
        tables,
        block_ids[0],
    )
    full_qkv, full_out, seq_x, gain_rows = kept[:4]
    hats, scales, q_low, k_low, v_low, log_total, context_low = kept[4:11]
    attn_hat, o_scale, resid, resid_low, tops = kept[11:]
    output, d_resid, gain_last, unit_grads = unit_kernel_call(
        resid_low, resid, cotangent[0], gain_rows, pieces
    )
    backs, part, part_gains, tops, grad_tokens = attend_back_call(
        d_resid,
        attn_hat,
        o_scale,
        gain_rows,
        full_out,
        context_low,
        q_low,
        k_low,
        v_low,
        log_total,
        hats,
        scales,
        tables,
        block_ids[0],
        seq_x,
        full_qkv,
        gain_last,
        tops,
        unit_grads,
    )
    part_gains = part_gains[:gain_count]
    head_top = tops[: w_qkv.shape[2] // HEAD, 0]
    factor = clip_tau / jnp.maximum(head_top, clip_tau)
    column = jnp.repeat(jnp.sqrt(factor), HEAD)
    column_scale = jnp.stack([column, column, jnp.ones_like(column)])[:, None, :]
    new_qkv, new_m_qkv, new_v_qkv, copy_qkv = adam_call(w_qkv, part, 0, m_qkv, v_qkv, column_scale)
    new_out, new_m_out, new_v_out, copy_out = [
        v[0] for v in adam_call(w_out[None], part, 3, m_out[None], v_out[None])
    ]
    new_gu, new_m_gu, new_v_gu, copy_gu = adam_units(grid, w_gu, m_gu, v_gu, backs, 0, True)
    new_down, new_m_down, new_v_down, copy_down = adam_units(
        grid, w_down, m_down, v_down, backs, 2, False
    )
    new_gains, new_gain_m, new_gain_v = adam_step(gains, part_gains, gain_m, gain_v, rate_gain, 0.0)
    return (
        output[None],
        grad_tokens[None],
        new_qkv,
        new_m_qkv,
        new_v_qkv,
        copy_qkv,
        new_out,
        new_m_out,
        new_v_out,
        copy_out,
        new_gu,
        new_m_gu,
        new_v_gu,
        copy_gu,
        new_down,
        new_m_down,
        new_v_down,
        copy_down,
        new_gains,
        new_gain_m,
        new_gain_v,
        factor,
    )


def solution(mesh):
    return jax.shard_map(
        local,
        mesh=mesh,
        in_specs=(
            P("dp", "tensor", None),
            P("dp", "tensor", None),
            P("dp", None),
            P(None, "dp", "tensor"),
            P(None, "dp", "tensor"),
            P(None, "dp", "tensor"),
            P("tensor", "dp"),
            P("tensor", "dp"),
            P("tensor", "dp"),
            P(None, "dp", "tensor"),
            P(None, "dp", "tensor"),
            P(None, "dp", "tensor"),
            P("tensor", "dp"),
            P("tensor", "dp"),
            P("tensor", "dp"),
            P(None, "dp"),
            P(None, "dp"),
            P(None, "dp"),
        ),
        out_specs=(
            P("dp", "tensor", None),
            P("dp", "tensor", None),
            P(None, "dp", "tensor"),
            P(None, "dp", "tensor"),
            P(None, "dp", "tensor"),
            P(None, "dp", "tensor"),
            P("tensor", "dp"),
            P("tensor", "dp"),
            P("tensor", "dp"),
            P("tensor", "dp"),
            P(None, "dp", "tensor"),
            P(None, "dp", "tensor"),
            P(None, "dp", "tensor"),
            P(None, "dp", "tensor"),
            P("tensor", "dp"),
            P("tensor", "dp"),
            P("tensor", "dp"),
            P("tensor", "dp"),
            P(None, "dp"),
            P(None, "dp"),
            P(None, "dp"),
            P("tensor"),
        ),
        check_vma=False,
    )
```

```python
import functools

import jax
import jax.numpy as jnp
import numpy as np
from jax import lax
from jax.experimental import pallas as pl
from jax.experimental.pallas import tpu as pltpu
from jax.sharding import PartitionSpec as P

HEAD = 128
STEP = 5


norm_eps = 1e-06
rope_base = 500000.0
beta_one = 0.9
beta_two = 0.95
rate_matrix = 0.01
rate_gain = 0.6
weight_decay = 0.1
adam_eps = 1e-08
clip_tau = 9.0
masked_value = -1e30


def rope_tables(length, size):
    half = size // 2
    freq = np.float32(rope_base) ** (-(np.arange(half, dtype=np.float32) * np.float32(2.0 / size)))
    angle = np.arange(length, dtype=np.float32)[:, None] * freq[None, :]
    angle = np.concatenate([angle, angle], axis=1)
    return (jnp.asarray(np.cos(angle)), jnp.asarray(np.sin(angle)))


def adam_step(param, grad, first, second, rate, decay):
    first = beta_one * first + (1.0 - beta_one) * grad
    second = beta_two * second + (1.0 - beta_two) * grad * grad
    fix_one = 1.0 - beta_one**STEP
    fix_two = 1.0 - beta_two**STEP
    update = first / fix_one / (jnp.sqrt(second / fix_two) + adam_eps)
    return (param - rate * (update + decay * param), first, second)


class Grid:
    def __init__(self):
        self.dp = lax.axis_size("dp")
        self.tensor = lax.axis_size("tensor")
        self.inner = 1
        while self.inner * self.inner * 4 <= self.dp:
            self.inner *= 2
        self.outer = self.dp // self.inner
        self.chips = self.tensor // 2
        self.dp_at = lax.axis_index("dp")
        self.tensor_at = lax.axis_index("tensor")
        self.inner_at = self.dp_at % self.inner
        self.chip_at = self.tensor_at // 2
        self.core_at = self.tensor_at % 2
        self.outer_at = self.dp_at // self.inner

    def path_of(self, index):
        column, row = index // self.inner, index % self.inner
        return row * self.outer + column + (row % 2) * (self.outer - 1 - 2 * column)

    def outer_flip(self, index, step):
        result = 0
        for bit in bits(self.outer):
            side = index // bit % 2
            result = result + bit * (1 - side if step & bit else side)
        return result

    def index_of(self, place):
        row, column = place // self.outer, place % self.outer
        return (column + (row % 2) * (self.outer - 1 - 2 * column)) * self.inner + row


def bits(count):
    return [1 << k for k in range(count.bit_length() - 1)]


def greet(peers):
    barrier = pltpu.get_barrier_semaphore()
    for peer in peers:
        pl.semaphore_signal(barrier, inc=1, device_id=peer, device_id_type=pl.DeviceIdType.MESH)
    pl.semaphore_wait(barrier, len(peers))


def attend_back_call(
    d_resid, attn_hat, o_scale, gain_rows, full_out, context, q_low, k_low, v_low, lse, hats, scales,
    tables, blocks, seq, full_qkv, gain_last, tops, unit_grads,
):
    grid = Grid()
    n, outer, inner, chips, tensor = grid.dp, grid.outer, grid.inner, grid.chips, grid.tensor
    count, width = d_resid.shape
    length, span = context.shape
    heads = span // HEAD
    units, slab = unit_grads[0][0].shape[1:]
    thin = width // n
    half = span // 2
    tall = min(256, length)
    tile = 512
    lines = 32
    ring = 8 + 2
    gain_item, top_item = 8, 9
    bf16, f32 = jnp.bfloat16, jnp.float32
    mesh_id = pl.DeviceIdType.MESH
    flat_grads = [unit_grads[c][j] for j in range(inner) for c in range(3)]
    some = len(flat_grads)
    z_steps = list(range(1, outer))

    def kernel(*refs):
        fixed, far_in, grads_in = refs[:17], refs[17:20], refs[20 : 20 + some]
        rest = refs[20 + some :]
        body(*fixed, far_in, grads_in, *rest)

    def body(
        dres_ref, hat_ref, o_scale_ref, gain_ref, out_w, ctx, q_ref, k_ref, v_ref, lse_ref, scale_ref,
        cos_ref, sin_ref, id_col, id_row, last_ref, tops_ref, far_in, grads_in,
        backs, part_ref, gains_out, tops_out, tokens_out,
        hats, seq, qkv_w, seq_do, d_ctx, d_q, d_k, d_v, d_low, probs_low, whole, terms, row_terms, turned,
        land, land_gain, land_top, own_gain, peer_gain, inners, peer_inners,
        grad_own, grad_land, grad_sum, core_send, core_land, hold, chip_send, chip_land,
        s_ring, r_ring, s_row, r_row, s_in, r_in, s_y, r_y, s_z, r_z, s_core, r_core, s_chip, r_chip, s_gain, r_gain, local,
    ):
        hats_in, seq_in, qkv_in = far_in
        g = Grid()

        def tensor_peer(k, flip):
            core = 1 - g.core_at if flip else g.core_at
            return (g.dp_at, lax.rem(g.chip_at + k + chips, chips) * 2 + core)

        def dp_peer(s, j):
            across = g.outer_flip(g.outer_at, s) * inner
            return (across + lax.rem(g.inner_at + j + inner, inner), g.tensor_at)

        place = g.path_of(g.dp_at)
        after_dp = (g.index_of(lax.rem(place + 1, n)), g.tensor_at)
        before_dp = (g.index_of(lax.rem(place + n - 1, n)), g.tensor_at)
        near = [tensor_peer(k, f) for k in range(chips) for f in (0, 1) if (k, f) != (0, 0)]
        far = [dp_peer(s, 0) for s in range(1, outer)] + [dp_peer(0, j) for j in range(1, inner)]
        greet(near + far + [after_dp, before_dp])

        def remote(src, dst, send, recv, peer):
            copy = pltpu.make_async_remote_copy(
                src_ref=src, dst_ref=dst, send_sem=send, recv_sem=recv,
                device_id=peer, device_id_type=mesh_id,
            )
            copy.start()
            return copy

        def fetch(src, dst, at):
            copy = pltpu.make_async_copy(src, dst, local.at[at])
            copy.start()
            return copy

        def dot(a, b, contract):
            return lax.dot_general(a, b, (contract, ((), ())), preferred_element_type=f32)

        def looped(total, make):
            lax.fori_loop(0, total, lambda i, c: (make(i), c)[1], 0)

        def rows_of(i, size):
            return pl.ds(pl.multiple_of(i * size, size), size)

        sent = []
        y_copies = {}
        sum_steps = [(c, s) for c in range(3) for s in z_steps + [0]]
        for c, s in sum_steps:
            for j in range(1, inner):
                copy = remote(
                    grads_in[j * 3 + c].at[s],
                    grad_land.at[j - 1, c, s],
                    s_y.at[j, c, s],
                    r_y.at[j, c, s],
                    dp_peer(0, j),
                )
                y_copies[j, c, s] = copy
                sent.append(copy)
        own_grads = [fetch(grads_in[c], grad_own.at[c], c) for c in range(3)]
        fetched = [fetch(hats_in, hats, 3), fetch(seq_in, seq, 4), fetch(qkv_in, qkv_w, 5)]
        z_copies = []
        keeps = []

        def unit_sums(times):
            for _ in range(times):
                if sum_steps:
                    unit_sum(*sum_steps.pop(0))

        def unit_sum(c, s):
            if s == (z_steps + [0])[0]:
                own_grads[c].wait()
            for j in range(1, inner):
                y_copies[j, c, s].wait_recv()

            def add(i):
                rows = rows_of(i, 64)
                total = grad_own[c, s, rows].astype(f32)
                for j in range(1, inner):
                    total = total + grad_land[j - 1, c, s, rows].astype(f32)
                grad_sum[c, s, rows] = total.astype(bf16)

            looped(units // 64, add)
            if s:
                z_copies.append(
                    remote(grad_sum.at[c, s], backs.at[c, s], s_z.at[c, s], r_z.at[c, s], dp_peer(s, 0))
                )
            else:
                keeps.append(fetch(grad_sum.at[c, 0], backs.at[c, 0], 6 + c))

        def way_of(item):
            return 1 if item >= 8 else 1 - 2 * (item // 4)

        def own(item, away):
            index = g.index_of(lax.rem(place - way_of(item) * away + 2 * n, n))
            if item == gain_item:
                return terms.at[index]
            if item == top_item:
                return tops_ref
            side, c = item // 4, item % 4
            return whole.at[c, pl.ds(side * half, half), rows_of(index, thin)]

        def landed(step, item):
            if item == gain_item:
                return land_gain.at[step]
            if item == top_item:
                return land_top.at[step]
            return land.at[step, item]

        hops = {}
        on_path = {}

        def hop(step, item):
            hops[step, item] = remote(
                own(item, 1) if step == 0 else landed(step - 1, item),
                landed(step, item),
                s_ring.at[step, item],
                r_ring.at[step, item],
                after_dp if way_of(item) == 1 else before_dp,
            )

        def depart(*items):
            for item in items:
                on_path[item] = 0
                hop(0, item)

        def advance(*items):
            for item in items:
                step = on_path.get(item, n) + 1
                if step >= n:
                    continue
                on_path[item] = step
                hops[step - 1, item].wait_recv()
                here = landed(step - 1, item)
                if item == top_item:
                    summed = jnp.maximum(here[...], tops_ref[...])
                else:
                    summed = here[...].astype(f32) + own(item, step + 1)[...].astype(f32)
                if step < n - 1:
                    here[...] = summed.astype(here.dtype)
                    hop(step, item)
                elif item == gain_item:
                    own_gain[0] = summed
                elif item == top_item:
                    tops_out[...] = summed
                else:
                    side, c = item // 4, item % 4
                    part_ref[c, pl.ds(side * half, half)] = summed

        def matrix_grad(c, left, right):
            turned[...] = left.T

            def columns(i):
                cols = rows_of(i, tile)
                whole[c, :, cols] = dot(turned[...], right[:, cols], ((1,), (0,))).astype(bf16)

            looped(width // tile, columns)

        t_at = g.tensor_at
        mine = rows_of(t_at, count)

        def open_rows(i, total):
            at = rows_of(i, lines)
            value, hat = dres_ref[at], hat_ref[at]
            upstream = value * gain_ref[2:3]
            mean = jnp.mean(upstream * hat, axis=1, keepdims=True)
            d_attn = (o_scale_ref[at] * (upstream - hat * mean)).astype(bf16)
            seq_do[pl.ds(pl.multiple_of(t_at * count + i * lines, lines), lines)] = d_attn
            return total + jnp.sum(value * hat, axis=0, keepdims=True)

        gain_attn = lax.fori_loop(0, count // lines, open_rows, jnp.zeros((1, width), f32))
        row_terms[...] = jnp.zeros((8, width), f32)
        row_terms[2:3] = gain_attn
        row_terms[3:4] = last_ref[...]
        moves, passed = [], []

        def row_copy(slot, index, peer):
            at = rows_of(index, count)
            copy = remote(seq_do.at[at], seq_do.at[at], s_row.at[slot], r_row.at[slot], peer)
            sent.append(copy)
            return copy

        for k in range(1, chips):
            moves.append(row_copy(k - 1, t_at, tensor_peer(k, 0)))
        to_core = row_copy(chips - 1, t_at, tensor_peer(0, 1))
        unit_sums(1)
        scale = HEAD ** (-0.5)
        for h in range(heads):
            cols = slice(h * HEAD, (h + 1) * HEAD)

            def weigh(i, c, cols=cols, h=h):
                at = rows_of(i, tall)
                raw = dot(q_ref[at, cols], k_ref[:, cols], ((1,), (1,))) * scale
                masked = jnp.where(id_row[...] <= id_col[at], raw, masked_value)
                probs_low[h, at] = jnp.exp(masked - lse_ref[at, h : h + 1]).astype(bf16)
                return c

            lax.fori_loop(0, length // tall, weigh, 0)
            if 2 * (h + 1) == heads:
                unit_sums(1)
        for k in range(1, chips):
            moves[k - 1].wait_recv()
            source = lax.rem(g.chip_at - k + chips, chips) * 2 + g.core_at
            passed.append(row_copy(chips - 1 + k, source, tensor_peer(0, 1)))
        to_core.wait_recv()
        unit_sums(1)
        for copy in passed:
            copy.wait_recv()

        def context_grad(i):
            at = rows_of(i, tall)
            d_ctx[at] = dot(seq_do[at], out_w[...], ((1,), (1,))).astype(bf16)

        looped(length // tall, context_grad)
        unit_sums(1)

        for h in range(heads):
            cols = slice(h * HEAD, (h + 1) * HEAD)

            def head(i, c, cols=cols, h=h):
                at = rows_of(i, tall)
                q_part, ctx_part = q_ref[at, cols], d_ctx[at, cols]
                probs_part = probs_low[h, at]
                probs = probs_part.astype(f32)
                d_probs = dot(ctx_part, v_ref[:, cols], ((1,), (1,)))
                mean = jnp.sum(probs * d_probs, axis=1, keepdims=True)
                d_scores = (probs * (d_probs - mean)).astype(bf16)
                d_q[at, cols] = dot(d_scores, k_ref[:, cols], ((1,), (0,))) * scale
                key = dot(d_scores, q_part, ((0,), (0,))) * scale
                value = dot(probs_part, ctx_part, ((0,), (0,)))
                d_k[:, cols] = jnp.where(i == 0, key, d_k[:, cols] + key)
                d_v[:, cols] = jnp.where(i == 0, value, d_v[:, cols] + value)
                return c

            d_k[:, cols] = jnp.zeros((length, HEAD), f32)
            d_v[:, cols] = jnp.zeros((length, HEAD), f32)
            lax.fori_loop(0, length // tall, head, 0)
            unit_sums(1)
        fetched[0].wait()
        sign = jnp.where(lax.broadcasted_iota(jnp.int32, (tall, HEAD), 1) < HEAD // 2, -1.0, 1.0)

        def unrotate(i, sums):
            at = rows_of(i, tall)
            cosine, sine = cos_ref[at], sin_ref[at]
            lane = lax.broadcasted_iota(jnp.int32, (tall, 128), 1)
            columns = jnp.zeros((tall, 128), f32)
            result = []
            for c, grad in ((0, d_q), (1, d_k)):
                total = jnp.zeros((tall, 1), f32)
                terms_row = []
                for h in range(heads):
                    cols = slice(h * HEAD, (h + 1) * HEAD)
                    value = grad[at, cols]
                    back = value * cosine - pltpu.roll(value * sine, HEAD // 2, 1) * sign
                    hat = hats[c, at, cols]
                    terms_row.append(jnp.sum(back * hat, axis=0, keepdims=True))
                    at_head = pl.ds(pl.multiple_of(t_at * span + h * HEAD, HEAD), HEAD)
                    back = back * gain_ref[c : c + 1, at_head]
                    grad[at, cols] = back
                    total = total + jnp.sum(back * hat, axis=1, keepdims=True)
                columns = jnp.where(lane == c, total, columns)
                result.append(sums[c] + jnp.concatenate(terms_row, axis=1))
            inners[:, at] = columns.T[:8]
            return tuple(result)

        zero = jnp.zeros((1, span), f32)
        gain_q, gain_k = lax.fori_loop(0, length // tall, unrotate, (zero, zero))
        offset = rows_of(t_at, span)
        row_terms[0:1, offset] = gain_q
        row_terms[1:2, offset] = gain_k
        in_copies = []
        for k in range(chips):
            for f in (0, 1):
                if (k, f) != (0, 0):
                    at = k * 2 + f - 1
                    in_copies.append(
                        remote(inners, peer_inners.at[at], s_in.at[at], r_in.at[at], tensor_peer(k, f))
                    )
        sent.extend(in_copies)
        matrix_grad(3, ctx[...], seq_do)
        depart(3, 7)
        for copy in in_copies:
            copy.wait_recv()
        unit_sums(1)

        def normed(i):
            at = rows_of(i, tall)
            sums = inners[:, at]
            for other in range(tensor - 1):
                sums = sums + peer_inners[other, :, at]
            column = jnp.concatenate([sums, jnp.zeros((120, tall), f32)], axis=0).T / width
            for c, grad in ((0, d_q), (1, d_k)):
                value = grad[at] - hats[c, at] * column[:, c : c + 1]
                d_low[c, at] = (scale_ref[at, c : c + 1] * value).astype(bf16)
            d_low[2, at] = d_v[at].astype(bf16)

        looped(length // tall, normed)
        fetched[1].wait()
        for c in (2, 0, 1):
            matrix_grad(c, d_low[c], seq)
            depart(c, c + 4)
            unit_sums(1)

        def place_terms(i, c):
            cols = pl.ds(pl.multiple_of(i * thin, thin), thin)
            terms[i] = row_terms[:, cols]
            return c

        lax.fori_loop(0, n, place_terms, 0)

        depart(gain_item, top_item)
        unit_sums(len(sum_steps))

        fetched[2].wait()
        chip_order = list(range(1, chips)) + [0]
        core_copies, chip_copies = {}, {}

        def token_rows(k, flip, store):
            chip = lax.rem(g.chip_at + k, chips)
            core = 1 - g.core_at if flip else g.core_at
            at = rows_of(chip * 2 + core, count)

            def columns(i):
                cols = rows_of(i, tile)
                total = dot(d_low[0, at], qkv_w[0, cols], ((1,), (1,)))
                for c in (1, 2):
                    total = total + dot(d_low[c, at], qkv_w[c, cols], ((1,), (1,)))
                store(cols, total)

            looped(width // tile, columns)

        duties = []
        for k in chip_order:

            def away(k=k):
                def store(cols, value):
                    core_send[k, :, cols] = value.astype(bf16)

                token_rows(k, True, store)
                core_copies[k] = remote(
                    core_send.at[k], core_land.at[k], s_core.at[k], r_core.at[k], tensor_peer(0, 1)
                )

            def here(k=k):
                def store(cols, value):
                    hold[k, :, cols] = value

                token_rows(k, False, store)

            def join(k=k):
                core_copies[k].wait_recv()

                def add(i):
                    at = rows_of(i, lines)
                    chip_send[k - 1, at] = (hold[k, at] + core_land[k, at].astype(f32)).astype(bf16)

                looped(count // lines, add)
                chip_copies[k] = remote(
                    chip_send.at[k - 1], chip_land.at[k - 1], s_chip.at[k], r_chip.at[k], tensor_peer(k, 0)
                )

            duties += [away, here] + ([join] if k else [])

        def close_tokens():
            core_copies[0].wait_recv()
            for k in range(1, chips):
                chip_copies[k].wait_recv()

            def close(i):
                at = rows_of(i, lines)
                total = dres_ref[at] + hold[0, at] + core_land[0, at].astype(f32)
                for k in range(1, chips):
                    total = total + chip_land[k - 1, at].astype(f32)
                tokens_out[at] = total

            looped(count // lines, close)

        duties.append(close_tokens)
        per_step = -(-len(duties) // (n - 2))
        for step in range(1, n):
            advance(3, 7, 2, 6, 0, 4, 1, 5, gain_item, top_item)
            for _ in range(per_step):
                if duties:
                    duties.pop(0)()
        peers = [tensor_peer(0, 1)] + [tensor_peer(k, 0) for k in range(1, chips)]
        first = remote(own_gain.at[0], peer_gain.at[0], s_gain.at[0], r_gain.at[0], peers[0])
        first.wait_recv()
        own_gain[1] = own_gain[0] + peer_gain[0]
        others = [
            remote(own_gain.at[1], peer_gain.at[k], s_gain.at[k], r_gain.at[k], peers[k])
            for k in range(1, chips)
        ]
        result = own_gain[1]
        for k in range(1, chips):
            others[k - 1].wait_recv()
            result = result + peer_gain[k]
        gains_out[...] = result
        for copy in z_copies:
            copy.wait()
        for copy in keeps:
            copy.wait()
        for copy in sent + list(hops.values()) + list(core_copies.values()):
            copy.wait_send()
        for copy in list(chip_copies.values()) + [first] + others:
            copy.wait_send()

    shape = jax.ShapeDtypeStruct
    anywhere = pl.BlockSpec(memory_space=pl.ANY)
    vmem = pl.BlockSpec(memory_space=pltpu.VMEM)
    sems = pltpu.SemaphoreType.DMA
    results = pl.pallas_call(
        kernel,
        out_shape=(
            shape((3, outer, units, slab), bf16),
            shape((4, span, thin), f32),
            shape((8, thin), f32),
            shape(tops.shape, f32),
            shape((count, width), f32),
        ),
        in_specs=[vmem] * 17 + [anywhere] * 3 + [anywhere] * some,
        out_specs=(anywhere,) + (vmem,) * 4,
        scratch_shapes=[
            pltpu.VMEM(hats.shape, f32),
            pltpu.VMEM(seq.shape, bf16),
            pltpu.VMEM(full_qkv.shape, bf16),
            pltpu.VMEM((length, width), bf16),
            pltpu.VMEM((length, span), bf16),
            pltpu.VMEM((length, span), f32),
            pltpu.VMEM((length, span), f32),
            pltpu.VMEM((length, span), f32),
            pltpu.VMEM((3, length, span), bf16),
            pltpu.VMEM((heads, length, length), bf16),
            pltpu.VMEM((4, span, width), bf16),
            pltpu.VMEM((n, 8, thin), f32),
            pltpu.VMEM((8, width), f32),
            pltpu.VMEM((span, length), bf16),
            pltpu.VMEM((n - 1, 8, half, thin), bf16),
            pltpu.VMEM((n - 1, 8, thin), f32),
            pltpu.VMEM((n - 1,) + tops.shape, f32),
            pltpu.VMEM((2, 8, thin), f32),
            pltpu.VMEM((chips, 8, thin), f32),
            pltpu.VMEM((8, length), f32),
            pltpu.VMEM((tensor - 1, 8, length), f32),
            pltpu.VMEM((3, outer, units, slab), bf16),
            pltpu.VMEM((max(inner - 1, 1), 3, outer, units, slab), bf16),
            pltpu.VMEM((3, outer, units, slab), bf16),
            pltpu.VMEM((chips, count, width), bf16),
            pltpu.VMEM((chips, count, width), bf16),
            pltpu.VMEM((chips, count, width), f32),
            pltpu.VMEM((max(chips - 1, 1), count, width), bf16),
            pltpu.VMEM((max(chips - 1, 1), count, width), bf16),
            sems((n - 1, ring)),
            sems((n - 1, ring)),
            sems((2 * chips - 1,)),
            sems((2 * chips - 1,)),
            sems((tensor - 1,)),
            sems((tensor - 1,)),
            sems((inner, 3, outer)),
            sems((inner, 3, outer)),
            sems((3, outer)),
            sems((3, outer)),
            sems((chips,)),
            sems((chips,)),
            sems((chips,)),
            sems((chips,)),
            sems((chips,)),
            sems((chips,)),
            sems((9,)),
        ],
        compiler_params=pltpu.CompilerParams(
            collective_id=1, has_side_effects=True, vmem_limit_bytes=62 * 2**20
        ),
    )(
        d_resid, attn_hat, o_scale, gain_rows, full_out, context, q_low, k_low, v_low, lse, scales,
        tables[0], tables[1], blocks[:, None], blocks[None, :], gain_last, tops,
        hats, seq, full_qkv, *flat_grads,
    )
    return results


def open_call(w_qkv, w_out, gains, rows, w_gu, w_down, tables, blocks):
    grid = Grid()
    n, outer, inner = grid.dp, grid.outer, grid.inner
    chips, tensor = grid.chips, grid.tensor
    count, width = rows.shape
    length = count * tensor
    lead, slab, span = w_qkv.shape
    gain_count = gains.shape[0]
    half = slab // 2
    part_tall = span // 2
    heads = span // HEAD
    shard_units = w_gu.shape[2]
    units = shard_units // outer
    parts = outer * inner
    ring = 2 * lead + 3
    steps = list(range(1, outer))
    tall = min(256, length)
    tile = 512
    lines = 32
    bf16, f32 = jnp.bfloat16, jnp.float32
    mesh_id = pl.DeviceIdType.MESH

    def kernel(*refs):
        pieces = [refs[11 + j * outer : 11 + (j + 1) * outer] for j in range(inner)]
        body(*refs[:11], pieces, *refs[11 + parts :])

    def body(
        qkv_any, out_any, rows_any, gu_any, down_any, gains_ref, cos_ref, sin_ref, id_col, id_row, rows_ref,
        pieces, qkv_out, flat_out, seq_out,
        gain_rows, hat_ref, scale_ref, q_low, k_low, v_low, lse_ref, context, attn_hat, o_scale, resid, resid_low, top_ref,
        qkv_ref, out_w_ref, seq_ref, all_gains, qkv_wide, out_wide, gu_wide, down_wide, cast,
        square, squares, core_send, core_land, hold, chip_send, chip_land,
        s_ring, r_ring, s_row, r_row, s_z, r_z, s_y, r_y, s_sq, r_sq, s_core, r_core, s_chip, r_chip, local,
    ):
        g = Grid()

        def tensor_peer(k, flip):
            core = 1 - g.core_at if flip else g.core_at
            return (g.dp_at, lax.rem(g.chip_at + k + chips, chips) * 2 + core)

        def dp_peer(s, j):
            across = g.outer_flip(g.outer_at, s) * inner
            return (across + lax.rem(g.inner_at + j + inner, inner), g.tensor_at)

        near = [tensor_peer(k, f) for k in range(chips) for f in (0, 1) if (k, f) != (0, 0)]
        far = [dp_peer(s, 0) for s in range(1, outer)]
        far += [dp_peer(0, j) for j in sorted({1 % inner, inner - 1} - {0})]
        t_at = g.tensor_at
        place = g.path_of(g.dp_at)
        after = (g.index_of(lax.rem(place + 1, n)), t_at)
        before = (g.index_of(lax.rem(place + n - 1, n)), t_at)
        firsts = []
        for at, (src, dst) in enumerate(((qkv_any, qkv_wide), (out_any, out_wide))):
            firsts.append(pltpu.make_async_copy(src, dst, local.at[3 + at]))
            firsts[-1].start()
        greet(near + far + [after, before])

        def remote(src, dst, send, recv, peer):
            copy = pltpu.make_async_remote_copy(
                src_ref=src, dst_ref=dst, send_sem=send, recv_sem=recv,
                device_id=peer, device_id_type=mesh_id,
            )
            copy.start()
            return copy

        def dot(a, b, contract):
            return lax.dot_general(a, b, (contract, ((), ())), preferred_element_type=f32)

        def looped(total, make):
            lax.fori_loop(0, total, lambda i, c: (make(i), c)[1], 0)

        def rows_of(i, size):
            return pl.ds(pl.multiple_of(i * size, size), size)

        def fetch(src, dst, at):
            copy = pltpu.make_async_copy(src, dst, local.at[at])
            copy.start()
            return copy

        def views(item, index):
            if item == ring - 1:
                return 1, all_gains.at[index]
            if item >= 2 * lead:
                side = item - 2 * lead
                part = pl.ds(side * part_tall, part_tall)
                return 1 - 2 * side, out_w_ref.at[part, rows_of(index, slab)]
            side, c = item // lead, item % lead
            at = pl.ds(pl.multiple_of(index * slab + side * half, half), half)
            return 1 - 2 * side, qkv_ref.at[c, at]

        hops = {}

        def hop(step, item):
            way = views(item, 0)[0]
            index = g.index_of(lax.rem(place - way * step + n, n))
            _, view = views(item, index)
            hops[step, item] = remote(
                view,
                view,
                s_ring.at[step, item],
                r_ring.at[step, item],
                after if way == 1 else before,
            )

        def row_copy(slot, index, peer, src=None):
            at = seq_ref.at[rows_of(index, count)]
            return remote(at if src is None else src, at, s_row.at[slot], r_row.at[slot], peer)

        order = [c + side * lead for c in range(lead) for side in (0, 1)]
        order += list(range(2 * lead, ring))
        firsts[0].wait()
        for c in range(lead):

            def cast_own(i, c=c):
                at = rows_of(i, lines)
                there = pl.ds(pl.multiple_of(g.dp_at * slab + i * lines, lines), lines)
                qkv_ref[c, there] = qkv_wide[c, at].astype(bf16)

            looped(slab // lines, cast_own)
            for side in (0, 1):
                hop(0, c + side * lead)
        firsts[1].wait()

        def cast_flat(i):
            at = rows_of(i, lines)
            out_w_ref[at, rows_of(g.dp_at, slab)] = out_wide[at].astype(bf16)

        looped(span // lines, cast_flat)
        empty = jnp.zeros((16 - gain_count, slab), f32)
        all_gains[g.dp_at] = jnp.concatenate([gains_ref[...], empty], axis=0).astype(bf16)
        for item in range(2 * lead, ring):
            hop(0, item)
        row_copies = [
            row_copy(k - 1, t_at, tensor_peer(k, 0), rows_any) for k in range(1, chips)
        ]
        row_copies.append(row_copy(chips - 1, t_at, tensor_peer(0, 1), rows_any))
        wide = [fetch(gu_any, gu_wide, 1), fetch(down_any, down_wide, 2)]
        kept = fetch(rows_any, seq_ref.at[rows_of(t_at, count)], 5)

        def cast_wide(c):
            if c == 0:
                wide[0].wait()

            def cast_rows(i):
                at = rows_of(i, lines)
                cast[c, at] = gu_wide[c, at].astype(bf16)

            looped(slab // lines, cast_rows)

        def cast_turned():
            wide[1].wait()

            def cast_rows(i):
                at = rows_of(i, 256)
                cast[2, :, at] = down_wide[at].T.astype(bf16)

            looped(shard_units // 256, cast_rows)

        shadows = [lambda: cast_wide(0), lambda: cast_wide(1), cast_turned]
        for step in range(1, n - 1):
            for item in order:
                hops[step - 1, item].wait_recv()
                hop(step, item)
            if step <= chips - 1:
                row_copies[step - 1].wait_recv()
                source = lax.rem(g.chip_at - step + chips, chips) * 2 + g.core_at
                row_copies.append(row_copy(chips - 1 + step, source, tensor_peer(0, 1)))
            if shadows:
                shadows.pop(0)()

        def cut(s):
            return cast.at[:, :, rows_of(g.outer_flip(g.outer_at, s), units)]

        z_copies = {}

        def z_send(s):
            z_copies[s] = remote(cut(s), pieces[0][s], s_z.at[s], r_z.at[s], dp_peer(s, 0))

        for s in steps[:2]:
            z_send(s)
        own = fetch(cut(0), pieces[0][0], 0)
        y_copies = {}

        def pass_on(j, s):
            src = cut(0) if (j, s) == (1, 0) else pieces[j - 1][s]
            y_copies[j, s] = remote(src, pieces[j][s], s_y.at[j, s], r_y.at[j, s], dp_peer(0, 1))

        if inner > 1:
            pass_on(1, 0)
        duties = []
        for s in steps:

            def duty(s=s):
                z_copies[s].wait_recv()
                if s >= 2 and s + 1 < outer:
                    z_send(s + 1)
                if inner > 1:
                    pass_on(1, s)

            duties.append(duty)
        for j in range(2, inner):
            for s in [0] + steps:

                def duty(j=j, s=s):
                    y_copies[j - 1, s].wait_recv()
                    pass_on(j, s)

                duties.append(duty)

        def next_duties(times):
            for _ in range(times):
                if duties:
                    duties.pop(0)()

        for item in order:
            hops[n - 2, item].wait_recv()
        for copy in row_copies[chips - 1 :]:
            copy.wait_recv()
        kept.wait()
        outs = [fetch(qkv_ref, qkv_out, 3), fetch(out_w_ref, flat_out, 4), fetch(seq_ref, seq_out, 5)]

        def spread(i):
            gain_rows[:, rows_of(i, slab)] = all_gains[i].astype(f32)[:8]

        looped(n, spread)

        def project(i):
            at = rows_of(i, tall)
            x = seq_ref[at]
            lane = lax.broadcasted_iota(jnp.int32, (tall, 128), 1)
            sums = jnp.zeros((tall, 128), f32)
            for c in range(2):
                value = dot(x, qkv_ref[c], ((1,), (0,)))
                hat_ref[c, at] = value
                sums = jnp.where(lane == c, jnp.sum(value * value, axis=1, keepdims=True), sums)
            v_low[at] = dot(x, qkv_ref[2], ((1,), (0,))).astype(bf16)
            square[:, at] = sums.T[:8]

        looped(length // tall, project)
        sq_copies = []
        for k in range(chips):
            for f in (0, 1):
                if (k, f) != (0, 0):
                    at = k * 2 + f - 1
                    sq_copies.append(
                        remote(square, squares.at[at], s_sq.at[at], r_sq.at[at], tensor_peer(k, f))
                    )
        for copy in sq_copies:
            copy.wait_recv()
        sign = jnp.where(lax.broadcasted_iota(jnp.int32, (tall, HEAD), 1) < HEAD // 2, -1.0, 1.0)

        def rotate(i):
            at = rows_of(i, tall)
            sums = square[:, at]
            for copy_at in range(tensor - 1):
                sums = sums + squares[copy_at, :, at]
            column = jnp.concatenate([sums, jnp.zeros((120, tall), f32)], axis=0).T
            scales = lax.rsqrt(column / width + norm_eps)
            scale_ref[at] = scales
            cosine, sine = cos_ref[at], sin_ref[at] * sign
            for c, low in ((0, q_low), (1, k_low)):
                hat = hat_ref[c, at] * scales[:, c : c + 1]
                hat_ref[c, at] = hat
                normed = hat * gain_rows[c : c + 1, rows_of(t_at, span)]
                for h in range(heads):
                    cols = slice(h * HEAD, (h + 1) * HEAD)
                    value = normed[:, cols]
                    turned = pltpu.roll(value, HEAD // 2, 1)
                    low[at, cols] = (value * cosine + turned * sine).astype(bf16)

        looped(length // tall, rotate)
        scale = HEAD ** (-0.5)
        top_ref[...] = jnp.full((8, 128), masked_value, f32)
        for h in range(heads):
            cols = slice(h * HEAD, (h + 1) * HEAD)

            def attend(i, best, cols=cols, h=h):
                at = rows_of(i, tall)
                raw = dot(q_low[at, cols], k_low[:, cols], ((1,), (1,))) * scale
                masked = jnp.where(id_row[...] <= id_col[at], raw, masked_value)
                top = jnp.max(masked, axis=1, keepdims=True)
                weight = jnp.exp(masked - top)
                total = jnp.sum(weight, axis=1, keepdims=True)
                probs = (weight * (1.0 / total)).astype(bf16)
                context[at, cols] = dot(probs, v_low[:, cols], ((1,), (0,))).astype(bf16)
                lse_ref[at, h : h + 1] = top + jnp.log(total)
                return jnp.maximum(best, jnp.max(top, axis=0, keepdims=True))

            best = lax.fori_loop(
                0, length // tall, attend, jnp.full((1, 1), masked_value, f32)
            )
            top_ref[h : h + 1] = jnp.broadcast_to(best, (1, 128))
            if h + 1 == heads // 2:
                next_duties(2)

        def out_rows(k, flip, store):
            chip = lax.rem(g.chip_at + k, chips)
            core = 1 - g.core_at if flip else g.core_at
            at = rows_of(chip * 2 + core, count)

            def columns(i):
                cols = rows_of(i, tile)
                store(cols, dot(context[at], out_w_ref[:, cols], ((1,), (0,))))

            looped(width // tile, columns)

        chip_order = list(range(1, chips)) + [0]
        core_copies, chip_copies = {}, {}
        for k in chip_order:

            def store(cols, value, k=k):
                core_send[k, :, cols] = value.astype(bf16)

            out_rows(k, True, store)
            core_copies[k] = remote(
                core_send.at[k], core_land.at[k], s_core.at[k], r_core.at[k], tensor_peer(0, 1)
            )
        for k in chip_order:

            def store(cols, value, k=k):
                hold[k, :, cols] = value

            out_rows(k, False, store)
            if k:
                core_copies[k].wait_recv()

                def add(i, k=k):
                    at = rows_of(i, lines)
                    chip_send[k - 1, at] = (hold[k, at] + core_land[k, at].astype(f32)).astype(bf16)

                looped(count // lines, add)
                chip_copies[k] = remote(
                    chip_send.at[k - 1], chip_land.at[k - 1], s_chip.at[k], r_chip.at[k], tensor_peer(k, 0)
                )
        core_copies[0].wait_recv()
        for k in range(1, chips):
            chip_copies[k].wait_recv()

        def close(i):
            at = rows_of(i, lines)
            raw = hold[0, at] + core_land[0, at].astype(f32)
            for k in range(1, chips):
                raw = raw + chip_land[k - 1, at].astype(f32)
            scale_o = lax.rsqrt(jnp.mean(raw * raw, axis=1, keepdims=True) + norm_eps)
            hat = raw * scale_o
            attn_hat[at] = hat
            o_scale[at] = scale_o
            value = rows_ref[at].astype(f32) + hat * gain_rows[2:3]
            resid[at] = value
            resid_low[at] = value.astype(bf16)

        looped(count // lines, close)
        next_duties(len(duties))
        own.wait()
        for key, copy in y_copies.items():
            if key[0] == inner - 1:
                copy.wait_recv()
        for copy in outs:
            copy.wait()
        sent = list(hops.values()) + row_copies + list(z_copies.values()) + list(y_copies.values()) + sq_copies
        for copy in sent + list(core_copies.values()) + list(chip_copies.values()):
            copy.wait_send()

    shape = jax.ShapeDtypeStruct
    anywhere = pl.BlockSpec(memory_space=pl.ANY)
    vmem = pl.BlockSpec(memory_space=pltpu.VMEM)
    sems = pltpu.SemaphoreType.DMA
    results = pl.pallas_call(
        kernel,
        out_shape=(shape((3, slab, units), bf16),) * parts
        + (
            shape((lead, width, span), bf16),
            shape((span, width), bf16),
            shape((length, width), bf16),
            shape((8, width), f32),
            shape((2, length, span), f32),
            shape((length, 128), f32),
            shape((length, span), bf16),
            shape((length, span), bf16),
            shape((length, span), bf16),
            shape((length, heads), f32),
            shape((length, span), bf16),
            shape((count, width), f32),
            shape((count, 1), f32),
            shape((count, width), f32),
            shape((count, width), bf16),
            shape((8, 128), f32),
        ),
        in_specs=[anywhere] * 5 + [vmem] * 6,
        out_specs=(anywhere,) * (parts + 3) + (vmem,) * 13,
        scratch_shapes=[
            pltpu.VMEM((lead, width, span), bf16),
            pltpu.VMEM((span, width), bf16),
            pltpu.VMEM((length, width), bf16),
            pltpu.VMEM((n, 16, slab), bf16),
            pltpu.VMEM(w_qkv.shape, f32),
            pltpu.VMEM(w_out.shape, f32),
            pltpu.VMEM(w_gu.shape, f32),
            pltpu.VMEM(w_down.shape, f32),
            pltpu.VMEM((3, slab, shard_units), bf16),
            pltpu.VMEM((8, length), f32),
            pltpu.VMEM((tensor - 1, 8, length), f32),
            pltpu.VMEM((chips, count, width), bf16),
            pltpu.VMEM((chips, count, width), bf16),
            pltpu.VMEM((chips, count, width), f32),
            pltpu.VMEM((max(chips - 1, 1), count, width), bf16),
            pltpu.VMEM((max(chips - 1, 1), count, width), bf16),
            sems((n - 1, ring)),
            sems((n - 1, ring)),
            sems((2 * chips - 1,)),
            sems((2 * chips - 1,)),
            sems((outer,)),
            sems((outer,)),
            sems((inner, outer)),
            sems((inner, outer)),
            sems((tensor - 1,)),
            sems((tensor - 1,)),
            sems((chips,)),
            sems((chips,)),
            sems((chips,)),
            sems((chips,)),
            sems((7,)),
        ],
        compiler_params=pltpu.CompilerParams(
            collective_id=0, has_side_effects=True, vmem_limit_bytes=58 * 2**20
        ),
    )(
        w_qkv, w_out, rows, w_gu, w_down, gains, tables[0], tables[1],
        blocks[:, None], blocks[None, :], rows,
    )
    pieces = [results[j * outer : (j + 1) * outer] for j in range(inner)]
    return pieces, results[parts:]


def unit_kernel_call(rows_low, resid, cotangent, gain, pieces):
    grid = Grid()
    outer, chips, inner = grid.outer, grid.chips, grid.inner
    total_rows, width = rows_low.shape
    units = pieces[0][0].shape[2]
    slab = pieces[0][0].shape[1]
    flat_pieces = [piece for row in pieces for piece in row]
    parts = len(flat_pieces)
    halves = 2
    count = total_rows // halves
    both = 2 * count
    per = min(2, chips)
    groups = chips // per
    blocks = outer * groups
    tall = per * both
    held = per if groups > 1 else max(per - 1, 1)
    links = outer * (chips - 1)
    steps = list(range(outer))
    far_first = [0] + steps[2:] + steps[1:2]

    def units_of(of_steps):
        return [(s, i) for s in of_steps for i in range(groups)]

    orders = {
        (0, 0): units_of(far_first),
        (0, 1): units_of(far_first),
        (1, 0): units_of(steps),
        (1, 1): units_of(far_first),
    }
    grad_order = units_of(far_first)
    tile = 512
    wide_tiles = width // tile
    unit_tile = min(256, units)
    lines = 32
    bf16, f32 = jnp.bfloat16, jnp.float32
    mesh_id = pl.DeviceIdType.MESH

    def plan():
        chip_us, core_us, hop_us = 5.6, 0.6, 2.0
        free = {"x": 0.0, "core": 0.0, "z near": 0.0, "z far": 0.0}
        arrive, done, tasks = {}, {}, {}

        def send(link, when, us):
            free[link] = max(free[link], when) + us
            return free[link] + hop_us

        def add(name, needs, us, after=None):
            tasks[name] = (needs, us, after)

        def send_outer(s, now):
            return send("z near", now, 8.0) if s == 1 else send("z far", now, 10.5)

        def go(p, h):
            def then(now):
                if (p, h) != (0, 1):
                    for s in steps[1:]:
                        arrive["z", p, h, s] = send_outer(s, now)
                for k in range(1, chips):
                    arrive["x", p, h, 0, k] = send("x", now, chip_us)
                arrive["c", p, h, 0, 0] = send("core", now, core_us)

            return then

        def zf(p, h, s):
            def then(now):
                for k in range(1, chips):
                    arrive["x", p, h, s, k] = send("x", now, chip_us)
                arrive["c", p, h, s, 0] = send("core", now, core_us)
                if (p, h) == (0, 0):
                    arrive["z", 0, 1, s] = send_outer(s, now)

            return then

        def xf(p, h, s, k):
            def then(now):
                arrive["c", p, h, s, k] = send("core", now, core_us)

            return then

        def compute(p, h, s, i):
            def then(now):
                arrive["cr", p, h, s, i] = send("core", now, per * core_us)

            return then

        def cr(p, h, s, i):
            def then(now):
                for k in range(i * per, i * per + per):
                    if k:
                        arrive["xr", p, h, s, k] = send("x", now, chip_us)

            return then

        def xr(p, h, s):
            def then(now):
                if s:
                    arrive["zr", p, h, s] = send_outer(s, now)

            return then

        for p in (0, 1):
            for h in range(halves):
                if p == 0:
                    needs = [("do", ("go", 0, h - 1))] if h else []
                else:
                    needs = [("do", ("between", h))]
                add(("go", p, h), needs, 0.2, go(p, h))
                for s in steps[1:]:
                    add(("zf", p, h, s), [("at", ("z", p, h, s))], 0.2, zf(p, h, s))
                for s in steps:
                    for k in range(1, chips):
                        add(("xf", p, h, s, k), [("at", ("x", p, h, s, k))], 0.2, xf(p, h, s, k))
                order = orders[p, h]
                for n, (s, i) in enumerate(order):
                    needs = [("at", ("c", p, h, s, i * per + j)) for j in range(per)]
                    if n:
                        needs.append(("do", ("front", p, h) + order[n - 1]))
                    add(("load", p, h, s, i), needs, 0.2)
                    add(("front", p, h, s, i), [("do", ("load", p, h, s, i))], (2.4, 1.6)[p])
                    needs = [("do", ("front", p, h, s, i))]
                    if n:
                        needs.append(("do", ("cr", p, h) + order[n - 1]))
                    add(("compute", p, h, s, i), needs, (1.6, 2.4)[p], compute(p, h, s, i))
                    needs = [("at", ("cr", p, h, s, i)), ("do", ("compute", p, h, s, i))]
                    add(("cr", p, h, s, i), needs, 0.5, cr(p, h, s, i))
                for s in steps:
                    needs = [("do", ("cr", p, h, s, 0))]
                    needs += [("at", ("xr", p, h, s, k)) for k in range(1, chips)]
                    add(("xr", p, h, s), needs, 0.4, xr(p, h, s))
                for s in steps[1:]:
                    needs = [("at", ("zr", p, h, s)), ("do", ("xr", p, h, 0))]
                    add(("zr", p, h, s), needs, 0.4)
        for h in range(halves):
            needs = [("do", ("zr", 0, h, s)) for s in steps[1:]] + [("do", ("xr", 0, h, 0))]
            add(("between", h), needs, 1.0)
        for n, (s, i) in enumerate(grad_order):
            needs = [("do", ("compute", 1, h, s, i)) for h in range(halves)]
            if n:
                needs.append(("do", ("grads",) + grad_order[n - 1] + (2,)))
            add(("fetch", s, i), needs, 0.2)
            for c in range(3):
                needs = [("do", ("grads", s, i, c - 1) if c else ("fetch", s, i))]
                add(("grads", s, i, c), needs, 2.8)
        written = [(j, s) for j in range(inner) for s in range(outer)]
        for n, at in enumerate(written):
            needs = [("do", ("grads",) + grad_order[-1] + (2,))]
            if n:
                needs = [("do", ("write",) + written[n - 1])]
            add(("write",) + at, needs, 0.6)
        rank = {"compute": 1, "front": 2, "fetch": 2, "grads": 3, "write": 4}
        result = []
        now = 0.0
        while tasks:
            best = None
            for name, (needs, us, then) in tasks.items():
                ready = 0.0
                for kind, key in needs:
                    table = arrive if kind == "at" else done
                    if key not in table:
                        ready = None
                        break
                    ready = max(ready, table[key] + (1.0 if key[0] in ("load", "fetch") else 0.0))
                if ready is None:
                    continue
                key = (max(ready, now), rank.get(name[0], 0))
                if best is None or key < best[0]:
                    best = (key, name)
            (ready, _), name = best
            needs, us, then = tasks.pop(name)
            now = ready + us
            done[name] = now
            if then is not None:
                then(now)
            result.append(name)
        return result

    def kernel(*refs):
        piece_refs = refs[:parts]
        fixed = refs[parts : parts + 9]
        grad_refs = refs[parts + 9 : parts + 9 + 3 * inner]
        body(piece_refs, *fixed, grad_refs, *refs[parts + 9 + 3 * inner :])

    def body(
        piece_refs, rows_ref, resid_ref, cot_ref, gain_ref,
        out_ref, dres_ref, gain_out, all_x, all_dm, grad_refs,
        wg, wu, wd, buf, wide_buf, act, coef_gate, coef_up, d_gate, d_up, turned, acc_gate, acc_up, acc_down, stage,
        core_send, core_land, hold, keep, chip_send, chip_land, outer_send, outer_land, raw, d_mlp,
        s_outer, r_outer, s_chip, r_chip, s_core, r_core,
        s_core_sum, r_core_sum, s_chip_sum, r_chip_sum, s_outer_sum, r_outer_sum,
        local, local_own, local_wide, local_w, local_g,
    ):
        g = Grid()
        core_peer = (g.dp_at, g.chip_at * 2 + 1 - g.core_at)

        def chip_peer(k):
            return (g.dp_at, lax.rem(g.chip_at + k + chips, chips) * 2 + g.core_at)

        def outer_peer(s):
            return (g.outer_flip(g.outer_at, s) * inner + g.inner_at, g.tensor_at)

        greet(
            [core_peer]
            + [chip_peer(k) for k in range(1, chips)]
            + [outer_peer(s) for s in range(1, outer)]
        )

        def remote(src, dst, send, recv, peer):
            copy = pltpu.make_async_remote_copy(
                src_ref=src, dst_ref=dst, send_sem=send, recv_sem=recv,
                device_id=peer, device_id_type=mesh_id,
            )
            copy.start()
            return copy

        def fetch(src, dst, sem):
            copy = pltpu.make_async_copy(src, dst, sem)
            copy.start()
            return copy

        def dot(a, b, contract):
            return lax.dot_general(a, b, (contract, ((), ())), preferred_element_type=f32)

        def looped(total, make):
            lax.fori_loop(0, total, lambda i, c: (make(i), c)[1], 0)

        def by_lines(make):
            looped(count // lines, lambda i: make(pl.ds(pl.multiple_of(i * lines, lines), lines)))

        def by_tiles(make):
            looped(wide_tiles, lambda i: make(pl.ds(pl.multiple_of(i * tile, tile), tile)))

        weights = (wg, wu, wd)
        fetches = []

        def fetch_weights():
            for j in range(inner):
                for s in range(outer):
                    index = g.outer_flip(g.outer_at, s) * inner
                    index = index + lax.rem(g.inner_at - j + inner, inner)
                    span = pl.ds(pl.multiple_of(index * slab, slab), slab)
                    for c in range(3):
                        at = j * outer + s
                        fetches.append(
                            fetch(piece_refs[at].at[c], weights[c].at[span], local_w.at[at, c])
                        )

        mine, theirs = pl.ds(0, count), pl.ds(count, count)
        every = (all_x, all_dm)
        copies, sums, loads, own = {}, {}, {}, {}
        unsent = {(p, h): [] for p in (0, 1) for h in range(halves)}

        def track(p, h, copy):
            unsent[p, h].append(copy)
            return copy

        def core_copy(p, h, s, k, src):
            dst = every[p].at[h, s, k, theirs]
            copies["c", p, h, s, k] = track(
                p, h, remote(src, dst, s_core.at[p, h, s, k], r_core.at[p, h, s, k], core_peer)
            )

        def chip_copy(p, h, s, k, src):
            dst = every[p].at[h, s, k, mine]
            copies["x", p, h, s, k] = track(
                p, h, remote(src, dst, s_chip.at[p, h, s, k], r_chip.at[p, h, s, k], chip_peer(k))
            )

        def outer_copy(p, h, s):
            source = (rows_ref, d_mlp)[p].at[pl.ds(h * count, count)]
            dst = every[p].at[h, s, 0, mine]
            copies["z", p, h, s] = track(
                p, h, remote(source, dst, s_outer.at[p, h, s], r_outer.at[p, h, s], outer_peer(s))
            )

        def go(p, h):
            source = (rows_ref, d_mlp)[p].at[pl.ds(h * count, count)]
            if (p, h) != (0, 1):
                for s in steps[1:]:
                    outer_copy(p, h, s)
            for k in range(1, chips):
                chip_copy(p, h, 0, k, source)
            core_copy(p, h, 0, 0, source)
            own[p, h] = fetch(source, every[p].at[h, 0, 0, mine], local_own.at[p, h])
            if p == 0 and h == 0:
                fetch_weights()

        def part_out(h, s, i, cols, part_sum):
            for j in range(per):
                own_rows = part_sum[j * both : j * both + count]
                if i * per + j == 0:
                    keep[h, s, :, cols] = own_rows
                else:
                    hold[h, min(j, held - 1), :, cols] = own_rows
                core_send[h, j, :, cols] = part_sum[j * both + count : (j + 1) * both].astype(bf16)

        def forward(h, unit):
            for j in range(units // unit_tile):
                cols = pl.ds(j * unit_tile, unit_tile)
                rows = buf[h].reshape(tall, width)
                gate = dot(rows, wg[:, cols], ((1,), (0,)))
                up = dot(rows, wu[:, cols], ((1,), (0,)))
                sigma = jax.nn.sigmoid(gate)
                silu = gate * sigma
                act[unit, h, :, cols] = (silu * up).astype(bf16)
                coef_up[unit, h, :, cols] = silu.astype(bf16)
                coef_gate[unit, h, :, cols] = (
                    up * sigma * (1.0 + gate * (1.0 - sigma))
                ).astype(bf16)

        def forward_out(h, unit, s, i):
            by_tiles(
                lambda cols: part_out(h, s, i, cols, dot(act[unit, h], wd[cols, :], ((1,), (1,))))
            )

        def backward(h, unit):
            for j in range(units // unit_tile):
                cols = pl.ds(j * unit_tile, unit_tile)
                d_act = dot(buf[h].reshape(tall, width), wd[:, cols], ((1,), (0,)))
                d_gate[unit, h, :, cols] = (d_act * coef_gate[unit, h, :, cols].astype(f32)).astype(bf16)
                d_up[unit, h, :, cols] = (d_act * coef_up[unit, h, :, cols].astype(f32)).astype(bf16)

        def backward_out(h, unit, s, i):
            def into(cols):
                part_sum = dot(d_gate[unit, h], wg[cols, :], ((1,), (1,)))
                part_sum = part_sum + dot(d_up[unit, h], wu[cols, :], ((1,), (1,)))
                part_out(h, s, i, cols, part_sum)

            by_tiles(into)

        def weight_grads(unit, c):
            first = unit == grad_order[0][0] * groups + grad_order[0][1]
            left, right, acc = ((d_gate, 0, acc_gate), (d_up, 0, acc_up), (act, 1, acc_down))[c]
            turned[...] = left[unit].reshape(halves * tall, units).T

            def grads(cols):
                rows = wide_buf[right, :, :, :, cols].reshape(halves * tall, tile)
                value = dot(turned[...], rows, ((1,), (0,)))
                acc[:, cols] = value if first else acc[:, cols] + value

            by_tiles(grads)

        def between(h):
            def lines_of(i, total):
                at_rows = pl.ds(pl.multiple_of(h * count + i * lines, lines), lines)
                value = raw[at_rows]
                scale = lax.rsqrt(jnp.mean(value * value, axis=1, keepdims=True) + norm_eps)
                hat = value * scale
                gain_row = gain_ref[3:4]
                out_ref[at_rows] = (resid_ref[at_rows] + hat * gain_row).astype(bf16)
                top = cot_ref[at_rows].astype(f32)
                upstream = top * gain_row
                mean = jnp.mean(upstream * hat, axis=1, keepdims=True)
                d_mlp[at_rows] = (scale * (upstream - hat * mean)).astype(bf16)
                return total + jnp.sum(top * hat, axis=0, keepdims=True)

            zero = jnp.zeros((1, width), f32)
            total = lax.fori_loop(0, count // lines, lines_of, zero)
            gain_out[...] = total if h == 0 else gain_out[...] + total

        batches = []

        def write_grads(j, s):
            index = g.outer_flip(g.outer_at, s) * inner
            index = index + lax.rem(g.inner_at + j, inner)
            span = pl.ds(pl.multiple_of(index * slab, slab), slab)
            slot = len(batches) % 2
            if len(batches) >= 2:
                for copy in batches[-2]:
                    copy.wait()
            batch = []
            for c, acc in enumerate((acc_gate, acc_up, acc_down)):
                stage[slot, c] = acc[:, span].astype(bf16)
                batch.append(
                    fetch(stage.at[slot, c], grad_refs[j * 3 + c].at[s], local_g.at[slot, c])
                )
            batches.append(batch)

        def core_sum(p, h, s, i):
            unit = s * groups + i
            sums["c", p, h, unit].wait_recv()
            for j in range(per):
                chip = i * per + j
                if chip == 0:

                    def add(at_rows):
                        keep[h, s, at_rows] = keep[h, s, at_rows] + core_land[h, unit, j, at_rows].astype(f32)

                    by_lines(add)
                    continue
                there = s * (chips - 1) + chip - 1

                def add(at_rows):
                    total = hold[h, min(j, held - 1), at_rows] + core_land[h, unit, j, at_rows].astype(f32)
                    chip_send[h, there, at_rows] = total.astype(bf16)

                by_lines(add)
                sums["x", p, h, s, chip] = track(
                    p, h,
                    remote(
                        chip_send.at[h, there], chip_land.at[h, there],
                        s_chip_sum.at[p, h, there], r_chip_sum.at[p, h, there], chip_peer(-chip),
                    ),
                )

        def chip_sum(p, h, s):
            for k in range(1, chips):
                sums["x", p, h, s, k].wait_recv()

            def add(at_rows):
                total = keep[h, s, at_rows]
                for k in range(1, chips):
                    total = total + chip_land[h, s * (chips - 1) + k - 1, at_rows].astype(f32)
                if s == 0:
                    raw[pl.ds(pl.multiple_of(h * count + at_rows.start, lines), lines)] = total
                else:
                    outer_send[h, s - 1, at_rows] = total.astype(bf16)

            by_lines(add)
            if s:
                sums["z", p, h, s] = track(
                    p, h,
                    remote(
                        outer_send.at[h, s - 1], outer_land.at[h, s - 1],
                        s_outer_sum.at[p, h, s], r_outer_sum.at[p, h, s], outer_peer(s),
                    ),
                )

        def outer_sum(p, h, s):
            sums["z", p, h, s].wait_recv()

            def add(at_rows):
                there = pl.ds(pl.multiple_of(h * count + at_rows.start, lines), lines)
                raw[there] = raw[there] + outer_land[h, s - 1, at_rows].astype(f32)

            by_lines(add)

        def all_sent(p, h):
            for copy in unsent[p, h]:
                copy.wait_send()

        last_core = {}
        for task in plan():
            name, args = task[0], task[1:]
            if name == "go":
                go(*args)
            elif name == "zf":
                p, h, s = args
                copies["z", p, h, s].wait_recv()
                source = every[p].at[h, s, 0, mine]
                for k in range(1, chips):
                    chip_copy(p, h, s, k, source)
                core_copy(p, h, s, 0, source)
                if (p, h) == (0, 0):
                    outer_copy(0, 1, s)
            elif name == "xf":
                p, h, s, k = args
                copies["x", p, h, s, k].wait_recv()
                core_copy(p, h, s, k, every[p].at[h, s, k, mine])
            elif name == "load":
                p, h, s, i = args
                for j in range(per):
                    copies["c", p, h, s, i * per + j].wait_recv()
                if (s, i) == (0, 0):
                    own[p, h].wait()
                src = every[p].at[h, s, pl.ds(i * per, per)]
                loads[args] = fetch(src, buf.at[h], local.at[p, h, s * groups + i])
            elif name == "front":
                p, h, s, i = args
                if p == 0 and not loads.get("weights"):
                    loads["weights"] = True
                    for copy in fetches:
                        copy.wait()
                loads[args].wait()
                (forward, backward)[p](h, s * groups + i)
            elif name == "compute":
                p, h, s, i = args
                unit = s * groups + i
                if h in last_core:
                    last_core[h].wait_send()
                (forward_out, backward_out)[p](h, unit, s, i)
                last_core[h] = remote(
                    core_send.at[h], core_land.at[h, unit],
                    s_core_sum.at[p, h, unit], r_core_sum.at[p, h, unit], core_peer,
                )
                sums["c", p, h, unit] = last_core[h]
            elif name == "cr":
                core_sum(*args)
            elif name == "xr":
                chip_sum(*args)
            elif name == "zr":
                outer_sum(*args)
            elif name == "between":
                all_sent(0, args[0])
                between(args[0])
            elif name == "fetch":
                s, i = args
                loads[task] = []
                for at, src in enumerate((all_x, all_dm)):
                    for h in range(halves):
                        loads[task].append(
                            fetch(
                                src.at[h, s, pl.ds(i * per, per)],
                                wide_buf.at[at, h],
                                local_wide.at[s * groups + i, at * halves + h],
                            )
                        )
            elif name == "grads":
                s, i, c = args
                if c == 0:
                    for copy in loads["fetch", s, i]:
                        copy.wait()
                weight_grads(s * groups + i, c)
            elif name == "write":
                write_grads(*args)

        looped(
            total_rows // lines,
            lambda i: close_rows(pl.ds(pl.multiple_of(i * lines, lines), lines), dres_ref, raw, cot_ref),
        )
        for h in range(halves):
            all_sent(1, h)
            last_core[h].wait_send()
        for batch in batches[-2:]:
            for copy in batch:
                copy.wait()

    shape = jax.ShapeDtypeStruct
    anywhere = pl.BlockSpec(memory_space=pl.ANY)
    near = pl.BlockSpec(memory_space=pltpu.VMEM)
    sems = pltpu.SemaphoreType.DMA
    flops = 2 * 9 * halves * tall * blocks * width * units
    results = pl.pallas_call(
        kernel,
        out_shape=(
            shape((total_rows, width), bf16),
            shape((total_rows, width), f32),
            shape((1, width), f32),
            shape((halves, outer, chips, both, width), bf16),
            shape((halves, outer, chips, both, width), bf16),
        )
        + (shape((outer, units, slab), bf16),) * (3 * inner),
        in_specs=[anywhere] * (parts + 1) + [near] * 3,
        out_specs=(near, near, near) + (anywhere,) * (2 + 3 * inner),
        scratch_shapes=[
            pltpu.VMEM((width, units), bf16),
            pltpu.VMEM((width, units), bf16),
            pltpu.VMEM((width, units), bf16),
            pltpu.VMEM((halves, per, both, width), bf16),
            pltpu.VMEM((2, halves, per, both, width), bf16),
            pltpu.VMEM((blocks, halves, tall, units), bf16),
            pltpu.VMEM((blocks, halves, tall, units), bf16),
            pltpu.VMEM((blocks, halves, tall, units), bf16),
            pltpu.VMEM((blocks, halves, tall, units), bf16),
            pltpu.VMEM((blocks, halves, tall, units), bf16),
            pltpu.VMEM((units, halves * tall), bf16),
            pltpu.VMEM((units, width), f32),
            pltpu.VMEM((units, width), f32),
            pltpu.VMEM((units, width), f32),
            pltpu.VMEM((2, 3, units, slab), bf16),
            pltpu.VMEM((halves, per, count, width), bf16),
            pltpu.VMEM((halves, blocks, per, count, width), bf16),
            pltpu.VMEM((halves, held, count, width), f32),
            pltpu.VMEM((halves, outer, count, width), f32),
            pltpu.VMEM((halves, links, count, width), bf16),
            pltpu.VMEM((halves, links, count, width), bf16),
            pltpu.VMEM((halves, outer - 1, count, width), bf16),
            pltpu.VMEM((halves, outer - 1, count, width), bf16),
            pltpu.VMEM((total_rows, width), f32),
            pltpu.VMEM((total_rows, width), bf16),
            sems((2, halves, outer)),
            sems((2, halves, outer)),
            sems((2, halves, outer, chips)),
            sems((2, halves, outer, chips)),
            sems((2, halves, outer, chips)),
            sems((2, halves, outer, chips)),
            sems((2, halves, blocks)),
            sems((2, halves, blocks)),
            sems((2, halves, links)),
            sems((2, halves, links)),
            sems((2, halves, outer)),
            sems((2, halves, outer)),
            sems((2, halves, blocks)),
            sems((2, halves)),
            sems((blocks, 2 * halves)),
            sems((parts, 3)),
            sems((2, 3)),
        ],
        compiler_params=pltpu.CompilerParams(
            collective_id=2, has_side_effects=True, vmem_limit_bytes=62 * 2**20
        ),
        cost_estimate=pl.CostEstimate(flops=flops, bytes_accessed=64 * 2**20, transcendentals=0),
    )(*flat_pieces, rows_low, resid, cotangent, gain)
    grads = results[5:]
    return results[:3] + ([[grads[j * 3 + c] for j in range(inner)] for c in range(3)],)


def close_rows(at_rows, dres_ref, raw, cot_ref):
    dres_ref[at_rows] = raw[at_rows] + cot_ref[at_rows].astype(jnp.float32)


def adam_tile(param, grad, first, second):
    fix_one = 1.0 - beta_one**STEP
    fix_two = 1.0 - beta_two**STEP
    first = beta_one * first + (1.0 - beta_one) * grad
    second = beta_two * second + (1.0 - beta_two) * (grad * grad)
    square = second * (1.0 / fix_two)
    below = square * lax.rsqrt(square) + adam_eps
    guess = pl.reciprocal(below, approx=True)
    inverse = guess * (2.0 - below * guess)
    step = (rate_matrix / fix_one) * (first * inverse)
    return (1.0 - rate_matrix * weight_decay) * param - step, first, second


def adam_kernel(turned, w_ref, m_ref, v_ref, g_ref, *rest):
    scale_ref = rest[0] if len(rest) == 5 else None
    w_out, m_out, v_out, c_out = rest[-4:]
    grad = g_ref[...].T if turned else g_ref[...]
    new, first, second = adam_tile(w_ref[...], grad, m_ref[...], v_ref[...])
    if scale_ref is not None:
        new = new * scale_ref[...]
    w_out[...] = new
    m_out[...] = first
    v_out[...] = second
    c_out[...] = new.astype(jnp.bfloat16)


def adam_call(param, grads, at, first, second, scale=None):
    mats, rows, columns = param.shape
    turned = scale is not None
    spec = pl.BlockSpec((None, rows, columns), lambda k: (k, 0, 0))
    grad_spec = pl.BlockSpec((None,) + grads.shape[1:], lambda k: (at + k, 0, 0))
    specs = [spec] * 3 + [grad_spec]
    values = [param, first, second, grads]
    if turned:
        values.append(scale)
        specs.append(pl.BlockSpec((None, 1, columns), lambda k: (k, 0, 0)))
    outs = [jax.ShapeDtypeStruct(param.shape, jnp.float32)] * 3
    outs.append(jax.ShapeDtypeStruct(param.shape, jnp.bfloat16))
    size = param.size
    return pl.pallas_call(
        functools.partial(adam_kernel, turned),
        grid=(mats,),
        in_specs=specs,
        out_specs=[spec] * 4,
        out_shape=outs,
        cost_estimate=pl.CostEstimate(
            flops=20 * size, bytes_accessed=28 * size, transcendentals=2 * size
        ),
        compiler_params=pltpu.CompilerParams(vmem_limit_bytes=60 * 2**20),
    )(*values)


def adam_units_kernel(turned, at_ref, w_ref, m_ref, v_ref, g_ref, w_out, m_out, v_out, c_out):
    grad = (g_ref[...].T if turned else g_ref[...]).astype(jnp.float32)
    new, first, second = adam_tile(w_ref[...], grad, m_ref[...], v_ref[...])
    w_out[...] = new
    m_out[...] = first
    v_out[...] = second
    c_out[...] = new.astype(jnp.bfloat16)


def adam_units(grid, param, first, second, grads, begin, turned):
    n = grid.outer
    _, _, units, wide = grads.shape
    mats = param.shape[0] if turned else 1
    if not turned:
        spec = pl.BlockSpec((units, wide), lambda c, k, at: (k, 0))
    else:
        spec = pl.BlockSpec((None, wide, units), lambda c, k, at: (c, 0, k))
    grad_spec = pl.BlockSpec(
        (None, None, units, wide), lambda c, k, at: (begin + c, lax.bitwise_xor(at[0], k), 0, 0)
    )
    size = param.size
    outs = [jax.ShapeDtypeStruct(param.shape, jnp.float32)] * 3
    outs.append(jax.ShapeDtypeStruct(param.shape, jnp.bfloat16))
    return pl.pallas_call(
        functools.partial(adam_units_kernel, turned),
        grid_spec=pltpu.PrefetchScalarGridSpec(
            num_scalar_prefetch=1,
            grid=(mats, n),
            in_specs=[spec] * 3 + [grad_spec],
            out_specs=[spec] * 4,
        ),
        out_shape=outs,
        cost_estimate=pl.CostEstimate(
            flops=20 * size, bytes_accessed=28 * size, transcendentals=2 * size
        ),
        compiler_params=pltpu.CompilerParams(vmem_limit_bytes=60 * 2**20),
    )(grid.outer_at.astype(jnp.int32)[None], param, first, second, grads)


def local(
    tokens,
    cotangent,
    block_ids,
    w_qkv,
    m_qkv,
    v_qkv,
    w_out,
    m_out,
    v_out,
    w_gu,
    m_gu,
    v_gu,
    w_down,
    m_down,
    v_down,
    gains,
    gain_m,
    gain_v,
):
    grid = Grid()
    local_x = tokens[0]
    gain_count = gains.shape[0]
    tables = rope_tables(local_x.shape[0] * grid.tensor, HEAD)
    pieces, kept = open_call(
        w_qkv,
        w_out,
        gains,
        local_x,
        w_gu,
        w_down,
        tables,
        block_ids[0],
    )
    full_qkv, full_out, seq_x, gain_rows = kept[:4]
    hats, scales, q_low, k_low, v_low, log_total, context_low = kept[4:11]
    attn_hat, o_scale, resid, resid_low, tops = kept[11:]
    output, d_resid, gain_last, unit_grads = unit_kernel_call(
        resid_low, resid, cotangent[0], gain_rows, pieces
    )
    backs, part, part_gains, tops, grad_tokens = attend_back_call(
        d_resid,
        attn_hat,
        o_scale,
        gain_rows,
        full_out,
        context_low,
        q_low,
        k_low,
        v_low,
        log_total,
        hats,
        scales,
        tables,
        block_ids[0],
        seq_x,
        full_qkv,
        gain_last,
        tops,
        unit_grads,
    )
    part_gains = part_gains[:gain_count]
    head_top = tops[: w_qkv.shape[2] // HEAD, 0]
    factor = clip_tau / jnp.maximum(head_top, clip_tau)
    column = jnp.repeat(jnp.sqrt(factor), HEAD)
    column_scale = jnp.stack([column, column, jnp.ones_like(column)])[:, None, :]
    new_qkv, new_m_qkv, new_v_qkv, copy_qkv = adam_call(w_qkv, part, 0, m_qkv, v_qkv, column_scale)
    new_out, new_m_out, new_v_out, copy_out = [
        v[0] for v in adam_call(w_out[None], part, 3, m_out[None], v_out[None])
    ]
    new_gu, new_m_gu, new_v_gu, copy_gu = adam_units(grid, w_gu, m_gu, v_gu, backs, 0, True)
    new_down, new_m_down, new_v_down, copy_down = adam_units(
        grid, w_down, m_down, v_down, backs, 2, False
    )
    new_gains, new_gain_m, new_gain_v = adam_step(gains, part_gains, gain_m, gain_v, rate_gain, 0.0)
    return (
        output[None],
        grad_tokens[None],
        new_qkv,
        new_m_qkv,
        new_v_qkv,
        copy_qkv,
        new_out,
        new_m_out,
        new_v_out,
        copy_out,
        new_gu,
        new_m_gu,
        new_v_gu,
        copy_gu,
        new_down,
        new_m_down,
        new_v_down,
        copy_down,
        new_gains,
        new_gain_m,
        new_gain_v,
        factor,
    )


def solution(mesh):
    return jax.shard_map(
        local,
        mesh=mesh,
        in_specs=(
            P("dp", "tensor", None),
            P("dp", "tensor", None),
            P("dp", None),
            P(None, "dp", "tensor"),
            P(None, "dp", "tensor"),
            P(None, "dp", "tensor"),
            P("tensor", "dp"),
            P("tensor", "dp"),
            P("tensor", "dp"),
            P(None, "dp", "tensor"),
            P(None, "dp", "tensor"),
            P(None, "dp", "tensor"),
            P("tensor", "dp"),
            P("tensor", "dp"),
            P("tensor", "dp"),
            P(None, "dp"),
            P(None, "dp"),
            P(None, "dp"),
        ),
        out_specs=(
            P("dp", "tensor", None),
            P("dp", "tensor", None),
            P(None, "dp", "tensor"),
            P(None, "dp", "tensor"),
            P(None, "dp", "tensor"),
            P(None, "dp", "tensor"),
            P("tensor", "dp"),
            P("tensor", "dp"),
            P("tensor", "dp"),
            P("tensor", "dp"),
            P(None, "dp", "tensor"),
            P(None, "dp", "tensor"),
            P(None, "dp", "tensor"),
            P(None, "dp", "tensor"),
            P("tensor", "dp"),
            P("tensor", "dp"),
            P("tensor", "dp"),
            P("tensor", "dp"),
            P(None, "dp"),
            P(None, "dp"),
            P(None, "dp"),
            P("tensor"),
        ),
        check_vma=False,
    )
```

```python
import functools

import jax
import jax.numpy as jnp
import numpy as np
from jax import lax
from jax.experimental import pallas as pl
from jax.experimental.pallas import tpu as pltpu
from jax.sharding import PartitionSpec as P

HEAD = 128
STEP = 5


norm_eps = 1e-06
rope_base = 500000.0
beta_one = 0.9
beta_two = 0.95
rate_matrix = 0.01
rate_gain = 0.6
weight_decay = 0.1
adam_eps = 1e-08
clip_tau = 9.0
masked_value = -1e30


def rope_tables(length, size):
    half = size // 2
    freq = np.float32(rope_base) ** (-(np.arange(half, dtype=np.float32) * np.float32(2.0 / size)))
    angle = np.arange(length, dtype=np.float32)[:, None] * freq[None, :]
    angle = np.concatenate([angle, angle], axis=1)
    return (jnp.asarray(np.cos(angle)), jnp.asarray(np.sin(angle)))


def adam_step(param, grad, first, second, rate, decay):
    first = beta_one * first + (1.0 - beta_one) * grad
    second = beta_two * second + (1.0 - beta_two) * grad * grad
    fix_one = 1.0 - beta_one**STEP
    fix_two = 1.0 - beta_two**STEP
    update = first / fix_one / (jnp.sqrt(second / fix_two) + adam_eps)
    return (param - rate * (update + decay * param), first, second)


class Grid:
    def __init__(self):
        self.dp = lax.axis_size("dp")
        self.tensor = lax.axis_size("tensor")
        self.inner = 1
        while self.inner * self.inner * 4 <= self.dp:
            self.inner *= 2
        self.outer = self.dp // self.inner
        self.chips = self.tensor // 2
        self.dp_at = lax.axis_index("dp")
        self.tensor_at = lax.axis_index("tensor")
        self.inner_at = self.dp_at % self.inner
        self.chip_at = self.tensor_at // 2
        self.core_at = self.tensor_at % 2
        self.outer_at = self.dp_at // self.inner

    def path_of(self, index):
        column, row = index // self.inner, index % self.inner
        return row * self.outer + column + (row % 2) * (self.outer - 1 - 2 * column)

    def outer_flip(self, index, step):
        result = 0
        for bit in bits(self.outer):
            side = index // bit % 2
            result = result + bit * (1 - side if step & bit else side)
        return result

    def index_of(self, place):
        row, column = place // self.outer, place % self.outer
        return (column + (row % 2) * (self.outer - 1 - 2 * column)) * self.inner + row


def bits(count):
    return [1 << k for k in range(count.bit_length() - 1)]


def greet(peers):
    barrier = pltpu.get_barrier_semaphore()
    for peer in peers:
        pl.semaphore_signal(barrier, inc=1, device_id=peer, device_id_type=pl.DeviceIdType.MESH)
    pl.semaphore_wait(barrier, len(peers))


def attend_back_call(
    d_resid, attn_hat, o_scale, gain_rows, full_out, context, q_low, k_low, v_low, lse, hats, scales,
    tables, blocks, seq, full_qkv, gain_last, tops, unit_grads,
):
    grid = Grid()
    n, outer, inner, chips, tensor = grid.dp, grid.outer, grid.inner, grid.chips, grid.tensor
    count, width = d_resid.shape
    length, span = context.shape
    heads = span // HEAD
    units, slab = unit_grads[0][0].shape[1:]
    thin = width // n
    half = span // 2
    tall = min(256, length)
    tile = 512
    lines = 32
    ring = 8 + 2
    gain_item, top_item = 8, 9
    bf16, f32 = jnp.bfloat16, jnp.float32
    mesh_id = pl.DeviceIdType.MESH
    flat_grads = [unit_grads[c][j] for j in range(inner) for c in range(3)]
    some = len(flat_grads)
    z_steps = list(range(1, outer))

    def kernel(*refs):
        fixed, far_in, grads_in = refs[:17], refs[17:20], refs[20 : 20 + some]
        rest = refs[20 + some :]
        body(*fixed, far_in, grads_in, *rest)

    def body(
        dres_ref, hat_ref, o_scale_ref, gain_ref, out_w, ctx, q_ref, k_ref, v_ref, lse_ref, scale_ref,
        cos_ref, sin_ref, id_col, id_row, last_ref, tops_ref, far_in, grads_in,
        backs, part_ref, gains_out, tops_out, tokens_out,
        hats, seq, qkv_w, seq_do, d_ctx, d_q, d_k, d_v, d_low, probs_low, whole, terms, row_terms, turned,
        land, land_gain, land_top, own_gain, peer_gain, inners, peer_inners,
        grad_own, grad_land, grad_sum, core_send, core_land, hold, chip_send, chip_land,
        s_ring, r_ring, s_row, r_row, s_in, r_in, s_y, r_y, s_z, r_z, s_core, r_core, s_chip, r_chip, s_gain, r_gain, local,
    ):
        hats_in, seq_in, qkv_in = far_in
        g = Grid()

        def tensor_peer(k, flip):
            core = 1 - g.core_at if flip else g.core_at
            return (g.dp_at, lax.rem(g.chip_at + k + chips, chips) * 2 + core)

        def dp_peer(s, j):
            across = g.outer_flip(g.outer_at, s) * inner
            return (across + lax.rem(g.inner_at + j + inner, inner), g.tensor_at)

        place = g.path_of(g.dp_at)
        after_dp = (g.index_of(lax.rem(place + 1, n)), g.tensor_at)
        before_dp = (g.index_of(lax.rem(place + n - 1, n)), g.tensor_at)
        near = [tensor_peer(k, f) for k in range(chips) for f in (0, 1) if (k, f) != (0, 0)]
        far = [dp_peer(s, 0) for s in range(1, outer)] + [dp_peer(0, j) for j in range(1, inner)]
        greet(near + far + [after_dp, before_dp])

        def remote(src, dst, send, recv, peer):
            copy = pltpu.make_async_remote_copy(
                src_ref=src, dst_ref=dst, send_sem=send, recv_sem=recv,
                device_id=peer, device_id_type=mesh_id,
            )
            copy.start()
            return copy

        def fetch(src, dst, at):
            copy = pltpu.make_async_copy(src, dst, local.at[at])
            copy.start()
            return copy

        def dot(a, b, contract):
            return lax.dot_general(a, b, (contract, ((), ())), preferred_element_type=f32)

        def looped(total, make):
            lax.fori_loop(0, total, lambda i, c: (make(i), c)[1], 0, unroll=total <= 4)

        def rows_of(i, size):
            return pl.ds(pl.multiple_of(i * size, size), size)

        sent = []
        y_copies = {}
        sum_steps = [(c, s) for c in range(3) for s in z_steps + [0]]
        for c, s in sum_steps:
            for j in range(1, inner):
                copy = remote(
                    grads_in[j * 3 + c].at[s],
                    grad_land.at[j - 1, c, s],
                    s_y.at[j, c, s],
                    r_y.at[j, c, s],
                    dp_peer(0, j),
                )
                y_copies[j, c, s] = copy
                sent.append(copy)
        own_grads = [fetch(grads_in[c], grad_own.at[c], c) for c in range(3)]
        fetched = [fetch(hats_in, hats, 3), fetch(seq_in, seq, 4), fetch(qkv_in, qkv_w, 5)]
        z_copies = []
        keeps = []

        def unit_sums(times):
            for _ in range(times):
                if sum_steps:
                    unit_sum(*sum_steps.pop(0))

        def unit_sum(c, s):
            if s == (z_steps + [0])[0]:
                own_grads[c].wait()
            for j in range(1, inner):
                y_copies[j, c, s].wait_recv()

            def add(i):
                rows = rows_of(i, 64)
                total = grad_own[c, s, rows].astype(f32)
                for j in range(1, inner):
                    total = total + grad_land[j - 1, c, s, rows].astype(f32)
                grad_sum[c, s, rows] = total.astype(bf16)

            looped(units // 64, add)
            if s:
                z_copies.append(
                    remote(grad_sum.at[c, s], backs.at[c, s], s_z.at[c, s], r_z.at[c, s], dp_peer(s, 0))
                )
            else:
                keeps.append(fetch(grad_sum.at[c, 0], backs.at[c, 0], 6 + c))

        def way_of(item):
            return 1 if item >= 8 else 1 - 2 * (item // 4)

        def own(item, away):
            index = g.index_of(lax.rem(place - way_of(item) * away + 2 * n, n))
            if item == gain_item:
                return terms.at[index]
            if item == top_item:
                return tops_ref
            side, c = item // 4, item % 4
            return whole.at[c, pl.ds(side * half, half), rows_of(index, thin)]

        def landed(step, item):
            if item == gain_item:
                return land_gain.at[step]
            if item == top_item:
                return land_top.at[step]
            return land.at[step, item]

        hops = {}
        on_path = {}

        def hop(step, item):
            hops[step, item] = remote(
                own(item, 1) if step == 0 else landed(step - 1, item),
                landed(step, item),
                s_ring.at[step, item],
                r_ring.at[step, item],
                after_dp if way_of(item) == 1 else before_dp,
            )

        def depart(*items):
            for item in items:
                on_path[item] = 0
                hop(0, item)

        def advance(*items):
            for item in items:
                step = on_path.get(item, n) + 1
                if step >= n:
                    continue
                on_path[item] = step
                hops[step - 1, item].wait_recv()
                here = landed(step - 1, item)
                if item == top_item:
                    summed = jnp.maximum(here[...], tops_ref[...])
                else:
                    summed = here[...].astype(f32) + own(item, step + 1)[...].astype(f32)
                if step < n - 1:
                    here[...] = summed.astype(here.dtype)
                    hop(step, item)
                elif item == gain_item:
                    own_gain[0] = summed
                elif item == top_item:
                    tops_out[...] = summed
                else:
                    side, c = item // 4, item % 4
                    part_ref[c, pl.ds(side * half, half)] = summed

        def matrix_grad(c, left, right):
            turned[...] = left.T

            def columns(i):
                cols = rows_of(i, tile)
                whole[c, :, cols] = dot(turned[...], right[:, cols], ((1,), (0,))).astype(bf16)

            looped(width // tile, columns)

        t_at = g.tensor_at
        mine = rows_of(t_at, count)

        def open_rows(i, total):
            at = rows_of(i, lines)
            value, hat = dres_ref[at], hat_ref[at]
            upstream = value * gain_ref[2:3]
            mean = jnp.mean(upstream * hat, axis=1, keepdims=True)
            d_attn = (o_scale_ref[at] * (upstream - hat * mean)).astype(bf16)
            seq_do[pl.ds(pl.multiple_of(t_at * count + i * lines, lines), lines)] = d_attn
            return total + jnp.sum(value * hat, axis=0, keepdims=True)

        gain_attn = lax.fori_loop(0, count // lines, open_rows, jnp.zeros((1, width), f32))
        row_terms[...] = jnp.zeros((8, width), f32)
        row_terms[2:3] = gain_attn
        row_terms[3:4] = last_ref[...]
        moves, passed = [], []

        def row_copy(slot, index, peer):
            at = rows_of(index, count)
            copy = remote(seq_do.at[at], seq_do.at[at], s_row.at[slot], r_row.at[slot], peer)
            sent.append(copy)
            return copy

        for k in range(1, chips):
            moves.append(row_copy(k - 1, t_at, tensor_peer(k, 0)))
        to_core = row_copy(chips - 1, t_at, tensor_peer(0, 1))
        unit_sums(1)
        scale = HEAD ** (-0.5)
        for h in range(heads):
            cols = slice(h * HEAD, (h + 1) * HEAD)

            def weigh(i, c, cols=cols, h=h):
                at = rows_of(i, tall)
                raw = dot(q_ref[at, cols], k_ref[:, cols], ((1,), (1,))) * scale
                masked = jnp.where(id_row[...] <= id_col[at], raw, masked_value)
                probs_low[h, at] = jnp.exp(masked - lse_ref[at, h : h + 1]).astype(bf16)
                return c

            lax.fori_loop(0, length // tall, weigh, 0, unroll=length // tall <= 4)
            if 2 * (h + 1) == heads:
                unit_sums(1)
        for k in range(1, chips):
            moves[k - 1].wait_recv()
            source = lax.rem(g.chip_at - k + chips, chips) * 2 + g.core_at
            passed.append(row_copy(chips - 1 + k, source, tensor_peer(0, 1)))
        to_core.wait_recv()
        unit_sums(1)
        for copy in passed:
            copy.wait_recv()

        def context_grad(i):
            at = rows_of(i, tall)
            d_ctx[at] = dot(seq_do[at], out_w[...], ((1,), (1,))).astype(bf16)

        looped(length // tall, context_grad)
        unit_sums(1)

        for h in range(heads):
            cols = slice(h * HEAD, (h + 1) * HEAD)

            def head(i, c, cols=cols, h=h):
                at = rows_of(i, tall)
                q_part, ctx_part = q_ref[at, cols], d_ctx[at, cols]
                probs_part = probs_low[h, at]
                probs = probs_part.astype(f32)
                d_probs = dot(ctx_part, v_ref[:, cols], ((1,), (1,)))
                mean = jnp.sum(probs * d_probs, axis=1, keepdims=True)
                d_scores = (probs * (d_probs - mean)).astype(bf16)
                d_q[at, cols] = dot(d_scores, k_ref[:, cols], ((1,), (0,))) * scale
                key = dot(d_scores, q_part, ((0,), (0,))) * scale
                value = dot(probs_part, ctx_part, ((0,), (0,)))
                d_k[:, cols] = jnp.where(i == 0, key, d_k[:, cols] + key)
                d_v[:, cols] = jnp.where(i == 0, value, d_v[:, cols] + value)
                return c

            d_k[:, cols] = jnp.zeros((length, HEAD), f32)
            d_v[:, cols] = jnp.zeros((length, HEAD), f32)
            lax.fori_loop(0, length // tall, head, 0, unroll=length // tall <= 4)
            unit_sums(1)
        fetched[0].wait()
        sign = jnp.where(lax.broadcasted_iota(jnp.int32, (tall, HEAD), 1) < HEAD // 2, -1.0, 1.0)

        def unrotate(i, sums):
            at = rows_of(i, tall)
            cosine, sine = cos_ref[at], sin_ref[at]
            lane = lax.broadcasted_iota(jnp.int32, (tall, 128), 1)
            columns = jnp.zeros((tall, 128), f32)
            result = []
            for c, grad in ((0, d_q), (1, d_k)):
                total = jnp.zeros((tall, 1), f32)
                terms_row = []
                for h in range(heads):
                    cols = slice(h * HEAD, (h + 1) * HEAD)
                    value = grad[at, cols]
                    back = value * cosine - pltpu.roll(value * sine, HEAD // 2, 1) * sign
                    hat = hats[c, at, cols]
                    terms_row.append(jnp.sum(back * hat, axis=0, keepdims=True))
                    at_head = pl.ds(pl.multiple_of(t_at * span + h * HEAD, HEAD), HEAD)
                    back = back * gain_ref[c : c + 1, at_head]
                    grad[at, cols] = back
                    total = total + jnp.sum(back * hat, axis=1, keepdims=True)
                columns = jnp.where(lane == c, total, columns)
                result.append(sums[c] + jnp.concatenate(terms_row, axis=1))
            inners[:, at] = columns.T[:8]
            return tuple(result)

        zero = jnp.zeros((1, span), f32)
        gain_q, gain_k = lax.fori_loop(0, length // tall, unrotate, (zero, zero))
        offset = rows_of(t_at, span)
        row_terms[0:1, offset] = gain_q
        row_terms[1:2, offset] = gain_k
        in_copies = []
        for k in range(chips):
            for f in (0, 1):
                if (k, f) != (0, 0):
                    at = k * 2 + f - 1
                    in_copies.append(
                        remote(inners, peer_inners.at[at], s_in.at[at], r_in.at[at], tensor_peer(k, f))
                    )
        sent.extend(in_copies)
        matrix_grad(3, ctx[...], seq_do)
        depart(3, 7)
        for copy in in_copies:
            copy.wait_recv()
        unit_sums(1)

        def normed(i):
            at = rows_of(i, tall)
            sums = inners[:, at]
            for other in range(tensor - 1):
                sums = sums + peer_inners[other, :, at]
            column = jnp.concatenate([sums, jnp.zeros((120, tall), f32)], axis=0).T / width
            for c, grad in ((0, d_q), (1, d_k)):
                value = grad[at] - hats[c, at] * column[:, c : c + 1]
                d_low[c, at] = (scale_ref[at, c : c + 1] * value).astype(bf16)
            d_low[2, at] = d_v[at].astype(bf16)

        looped(length // tall, normed)
        fetched[1].wait()
        for c in (2, 0, 1):
            matrix_grad(c, d_low[c], seq)
            depart(c, c + 4)
            unit_sums(1)

        def place_terms(i, c):
            cols = pl.ds(pl.multiple_of(i * thin, thin), thin)
            terms[i] = row_terms[:, cols]
            return c

        lax.fori_loop(0, n, place_terms, 0)

        depart(gain_item, top_item)
        unit_sums(len(sum_steps))

        fetched[2].wait()
        chip_order = list(range(1, chips)) + [0]
        core_copies, chip_copies = {}, {}

        def token_rows(k, flip, store):
            chip = lax.rem(g.chip_at + k, chips)
            core = 1 - g.core_at if flip else g.core_at
            at = rows_of(chip * 2 + core, count)

            def columns(i):
                cols = rows_of(i, tile)
                total = dot(d_low[0, at], qkv_w[0, cols], ((1,), (1,)))
                for c in (1, 2):
                    total = total + dot(d_low[c, at], qkv_w[c, cols], ((1,), (1,)))
                store(cols, total)

            looped(width // tile, columns)

        duties = []
        for k in chip_order:

            def away(k=k):
                def store(cols, value):
                    core_send[k, :, cols] = value.astype(bf16)

                token_rows(k, True, store)
                core_copies[k] = remote(
                    core_send.at[k], core_land.at[k], s_core.at[k], r_core.at[k], tensor_peer(0, 1)
                )

            def here(k=k):
                def store(cols, value):
                    hold[k, :, cols] = value

                token_rows(k, False, store)

            def join(k=k):
                core_copies[k].wait_recv()

                def add(i):
                    at = rows_of(i, lines)
                    chip_send[k - 1, at] = (hold[k, at] + core_land[k, at].astype(f32)).astype(bf16)

                looped(count // lines, add)
                chip_copies[k] = remote(
                    chip_send.at[k - 1], chip_land.at[k - 1], s_chip.at[k], r_chip.at[k], tensor_peer(k, 0)
                )

            duties += [away, here] + ([join] if k else [])

        def close_tokens():
            core_copies[0].wait_recv()
            for k in range(1, chips):
                chip_copies[k].wait_recv()

            def close(i):
                at = rows_of(i, lines)
                total = dres_ref[at] + hold[0, at] + core_land[0, at].astype(f32)
                for k in range(1, chips):
                    total = total + chip_land[k - 1, at].astype(f32)
                tokens_out[at] = total

            looped(count // lines, close)

        duties.append(close_tokens)
        per_step = -(-len(duties) // (n - 2))
        for step in range(1, n):
            advance(3, 7, 2, 6, 0, 4, 1, 5, gain_item, top_item)
            for _ in range(per_step):
                if duties:
                    duties.pop(0)()
        peers = [tensor_peer(0, 1)] + [tensor_peer(k, 0) for k in range(1, chips)]
        first = remote(own_gain.at[0], peer_gain.at[0], s_gain.at[0], r_gain.at[0], peers[0])
        first.wait_recv()
        own_gain[1] = own_gain[0] + peer_gain[0]
        others = [
            remote(own_gain.at[1], peer_gain.at[k], s_gain.at[k], r_gain.at[k], peers[k])
            for k in range(1, chips)
        ]
        result = own_gain[1]
        for k in range(1, chips):
            others[k - 1].wait_recv()
            result = result + peer_gain[k]
        gains_out[...] = result
        for copy in z_copies:
            copy.wait()
        for copy in keeps:
            copy.wait()
        for copy in sent + list(hops.values()) + list(core_copies.values()):
            copy.wait_send()
        for copy in list(chip_copies.values()) + [first] + others:
            copy.wait_send()

    shape = jax.ShapeDtypeStruct
    anywhere = pl.BlockSpec(memory_space=pl.ANY)
    vmem = pl.BlockSpec(memory_space=pltpu.VMEM)
    sems = pltpu.SemaphoreType.DMA
    results = pl.pallas_call(
        kernel,
        out_shape=(
            shape((3, outer, units, slab), bf16),
            shape((4, span, thin), f32),
            shape((8, thin), f32),
            shape(tops.shape, f32),
            shape((count, width), f32),
        ),
        in_specs=[vmem] * 17 + [anywhere] * 3 + [anywhere] * some,
        out_specs=(anywhere,) + (vmem,) * 4,
        scratch_shapes=[
            pltpu.VMEM(hats.shape, f32),
            pltpu.VMEM(seq.shape, bf16),
            pltpu.VMEM(full_qkv.shape, bf16),
            pltpu.VMEM((length, width), bf16),
            pltpu.VMEM((length, span), bf16),
            pltpu.VMEM((length, span), f32),
            pltpu.VMEM((length, span), f32),
            pltpu.VMEM((length, span), f32),
            pltpu.VMEM((3, length, span), bf16),
            pltpu.VMEM((heads, length, length), bf16),
            pltpu.VMEM((4, span, width), bf16),
            pltpu.VMEM((n, 8, thin), f32),
            pltpu.VMEM((8, width), f32),
            pltpu.VMEM((span, length), bf16),
            pltpu.VMEM((n - 1, 8, half, thin), bf16),
            pltpu.VMEM((n - 1, 8, thin), f32),
            pltpu.VMEM((n - 1,) + tops.shape, f32),
            pltpu.VMEM((2, 8, thin), f32),
            pltpu.VMEM((chips, 8, thin), f32),
            pltpu.VMEM((8, length), f32),
            pltpu.VMEM((tensor - 1, 8, length), f32),
            pltpu.VMEM((3, outer, units, slab), bf16),
            pltpu.VMEM((max(inner - 1, 1), 3, outer, units, slab), bf16),
            pltpu.VMEM((3, outer, units, slab), bf16),
            pltpu.VMEM((chips, count, width), bf16),
            pltpu.VMEM((chips, count, width), bf16),
            pltpu.VMEM((chips, count, width), f32),
            pltpu.VMEM((max(chips - 1, 1), count, width), bf16),
            pltpu.VMEM((max(chips - 1, 1), count, width), bf16),
            sems((n - 1, ring)),
            sems((n - 1, ring)),
            sems((2 * chips - 1,)),
            sems((2 * chips - 1,)),
            sems((tensor - 1,)),
            sems((tensor - 1,)),
            sems((inner, 3, outer)),
            sems((inner, 3, outer)),
            sems((3, outer)),
            sems((3, outer)),
            sems((chips,)),
            sems((chips,)),
            sems((chips,)),
            sems((chips,)),
            sems((chips,)),
            sems((chips,)),
            sems((9,)),
        ],
        compiler_params=pltpu.CompilerParams(
            collective_id=1, has_side_effects=True, vmem_limit_bytes=62 * 2**20
        ),
    )(
        d_resid, attn_hat, o_scale, gain_rows, full_out, context, q_low, k_low, v_low, lse, scales,
        tables[0], tables[1], blocks[:, None], blocks[None, :], gain_last, tops,
        hats, seq, full_qkv, *flat_grads,
    )
    return results


def open_call(w_qkv, w_out, gains, rows, w_gu, w_down, tables, blocks):
    grid = Grid()
    n, outer, inner = grid.dp, grid.outer, grid.inner
    chips, tensor = grid.chips, grid.tensor
    count, width = rows.shape
    length = count * tensor
    lead, slab, span = w_qkv.shape
    gain_count = gains.shape[0]
    half = slab // 2
    part_tall = span // 2
    heads = span // HEAD
    shard_units = w_gu.shape[2]
    units = shard_units // outer
    parts = outer * inner
    ring = 2 * lead + 3
    steps = list(range(1, outer))
    tall = min(256, length)
    tile = 512
    lines = 32
    bf16, f32 = jnp.bfloat16, jnp.float32
    mesh_id = pl.DeviceIdType.MESH

    def kernel(*refs):
        pieces = [refs[11 + j * outer : 11 + (j + 1) * outer] for j in range(inner)]
        body(*refs[:11], pieces, *refs[11 + parts :])

    def body(
        qkv_any, out_any, rows_any, gu_any, down_any, gains_ref, cos_ref, sin_ref, id_col, id_row, rows_ref,
        pieces, qkv_out, flat_out, seq_out,
        gain_rows, hat_ref, scale_ref, q_low, k_low, v_low, lse_ref, context, attn_hat, o_scale, resid, resid_low, top_ref,
        qkv_ref, out_w_ref, seq_ref, all_gains, qkv_wide, out_wide, gu_wide, down_wide, cast,
        square, squares, core_send, core_land, hold, chip_send, chip_land,
        s_ring, r_ring, s_row, r_row, s_z, r_z, s_y, r_y, s_sq, r_sq, s_core, r_core, s_chip, r_chip, local,
    ):
        g = Grid()

        def tensor_peer(k, flip):
            core = 1 - g.core_at if flip else g.core_at
            return (g.dp_at, lax.rem(g.chip_at + k + chips, chips) * 2 + core)

        def dp_peer(s, j):
            across = g.outer_flip(g.outer_at, s) * inner
            return (across + lax.rem(g.inner_at + j + inner, inner), g.tensor_at)

        near = [tensor_peer(k, f) for k in range(chips) for f in (0, 1) if (k, f) != (0, 0)]
        far = [dp_peer(s, 0) for s in range(1, outer)]
        far += [dp_peer(0, j) for j in sorted({1 % inner, inner - 1} - {0})]
        t_at = g.tensor_at
        place = g.path_of(g.dp_at)
        after = (g.index_of(lax.rem(place + 1, n)), t_at)
        before = (g.index_of(lax.rem(place + n - 1, n)), t_at)
        firsts = []
        for at, (src, dst) in enumerate(((qkv_any, qkv_wide), (out_any, out_wide))):
            firsts.append(pltpu.make_async_copy(src, dst, local.at[3 + at]))
            firsts[-1].start()
        greet(near + far + [after, before])

        def remote(src, dst, send, recv, peer):
            copy = pltpu.make_async_remote_copy(
                src_ref=src, dst_ref=dst, send_sem=send, recv_sem=recv,
                device_id=peer, device_id_type=mesh_id,
            )
            copy.start()
            return copy

        def dot(a, b, contract):
            return lax.dot_general(a, b, (contract, ((), ())), preferred_element_type=f32)

        def looped(total, make):
            lax.fori_loop(0, total, lambda i, c: (make(i), c)[1], 0, unroll=total <= 4)

        def rows_of(i, size):
            return pl.ds(pl.multiple_of(i * size, size), size)

        def fetch(src, dst, at):
            copy = pltpu.make_async_copy(src, dst, local.at[at])
            copy.start()
            return copy

        def views(item, index):
            if item == ring - 1:
                return 1, all_gains.at[index]
            if item >= 2 * lead:
                side = item - 2 * lead
                part = pl.ds(side * part_tall, part_tall)
                return 1 - 2 * side, out_w_ref.at[part, rows_of(index, slab)]
            side, c = item // lead, item % lead
            at = pl.ds(pl.multiple_of(index * slab + side * half, half), half)
            return 1 - 2 * side, qkv_ref.at[c, at]

        hops = {}

        def hop(step, item):
            way = views(item, 0)[0]
            index = g.index_of(lax.rem(place - way * step + n, n))
            _, view = views(item, index)
            hops[step, item] = remote(
                view,
                view,
                s_ring.at[step, item],
                r_ring.at[step, item],
                after if way == 1 else before,
            )

        def row_copy(slot, index, peer, src=None):
            at = seq_ref.at[rows_of(index, count)]
            return remote(at if src is None else src, at, s_row.at[slot], r_row.at[slot], peer)

        order = [c + side * lead for c in range(lead) for side in (0, 1)]
        order += list(range(2 * lead, ring))
        firsts[0].wait()
        for c in range(lead):

            def cast_own(i, c=c):
                at = rows_of(i, lines)
                there = pl.ds(pl.multiple_of(g.dp_at * slab + i * lines, lines), lines)
                qkv_ref[c, there] = qkv_wide[c, at].astype(bf16)

            looped(slab // lines, cast_own)
            for side in (0, 1):
                hop(0, c + side * lead)
        firsts[1].wait()

        def cast_flat(i):
            at = rows_of(i, lines)
            out_w_ref[at, rows_of(g.dp_at, slab)] = out_wide[at].astype(bf16)

        looped(span // lines, cast_flat)
        empty = jnp.zeros((16 - gain_count, slab), f32)
        all_gains[g.dp_at] = jnp.concatenate([gains_ref[...], empty], axis=0).astype(bf16)
        for item in range(2 * lead, ring):
            hop(0, item)
        row_copies = [
            row_copy(k - 1, t_at, tensor_peer(k, 0), rows_any) for k in range(1, chips)
        ]
        row_copies.append(row_copy(chips - 1, t_at, tensor_peer(0, 1), rows_any))
        wide = [fetch(gu_any, gu_wide, 1), fetch(down_any, down_wide, 2)]
        kept = fetch(rows_any, seq_ref.at[rows_of(t_at, count)], 5)

        def cast_wide(c):
            if c == 0:
                wide[0].wait()

            def cast_rows(i):
                at = rows_of(i, lines)
                cast[c, at] = gu_wide[c, at].astype(bf16)

            looped(slab // lines, cast_rows)

        def cast_turned():
            wide[1].wait()

            def cast_rows(i):
                at = rows_of(i, 256)
                cast[2, :, at] = down_wide[at].T.astype(bf16)

            looped(shard_units // 256, cast_rows)

        shadows = [lambda: cast_wide(0), lambda: cast_wide(1), cast_turned]
        for step in range(1, n - 1):
            for item in order:
                hops[step - 1, item].wait_recv()
                hop(step, item)
            if step <= chips - 1:
                row_copies[step - 1].wait_recv()
                source = lax.rem(g.chip_at - step + chips, chips) * 2 + g.core_at
                row_copies.append(row_copy(chips - 1 + step, source, tensor_peer(0, 1)))
            if shadows:
                shadows.pop(0)()

        def cut(s):
            return cast.at[:, :, rows_of(g.outer_flip(g.outer_at, s), units)]

        z_copies = {}

        def z_send(s, c):
            some = pl.ds(0, 3) if c is None else pl.ds(c, 1)
            at = c or 0
            z_copies[s, c] = remote(
                cut(s).at[some], pieces[0][s].at[some], s_z.at[s, at], r_z.at[s, at], dp_peer(s, 0)
            )

        chunks = [(s, None) for s in steps[:-1]] + [(steps[-1], c) for c in range(3)]
        for chunk in chunks:
            z_send(*chunk)
        own = fetch(cut(0), pieces[0][0], 0)
        y_copies = {}

        def pass_on(j, s, c):
            src = cut(0) if (j, s) == (1, 0) else pieces[j - 1][s]
            some = pl.ds(0, 3) if c is None else pl.ds(c, 1)
            at = c or 0
            y_copies[j, s, c] = remote(
                src.at[some], pieces[j][s].at[some], s_y.at[j, s, at], r_y.at[j, s, at], dp_peer(0, 1)
            )

        if inner > 1:
            pass_on(1, 0, None)
        duties = []
        for chunk in chunks:

            def duty(chunk=chunk):
                z_copies[chunk].wait_recv()
                if inner > 1:
                    pass_on(1, *chunk)

            duties.append(duty)
        for j in range(2, inner):
            for chunk in [(0, None)] + chunks:

                def duty(j=j, chunk=chunk):
                    y_copies[(j - 1,) + chunk].wait_recv()
                    pass_on(j, *chunk)

                duties.append(duty)

        def next_duties(times):
            for _ in range(times):
                if duties:
                    duties.pop(0)()

        for item in order:
            hops[n - 2, item].wait_recv()
        for copy in row_copies[chips - 1 :]:
            copy.wait_recv()
        kept.wait()
        outs = [fetch(qkv_ref, qkv_out, 3), fetch(out_w_ref, flat_out, 4), fetch(seq_ref, seq_out, 5)]

        def spread(i):
            gain_rows[:, rows_of(i, slab)] = all_gains[i].astype(f32)[:8]

        looped(n, spread)

        def project(i):
            at = rows_of(i, tall)
            x = seq_ref[at]
            lane = lax.broadcasted_iota(jnp.int32, (tall, 128), 1)
            sums = jnp.zeros((tall, 128), f32)
            for c in range(2):
                value = dot(x, qkv_ref[c], ((1,), (0,)))
                hat_ref[c, at] = value
                sums = jnp.where(lane == c, jnp.sum(value * value, axis=1, keepdims=True), sums)
            v_low[at] = dot(x, qkv_ref[2], ((1,), (0,))).astype(bf16)
            square[:, at] = sums.T[:8]

        looped(length // tall, project)
        sq_copies = []
        for k in range(chips):
            for f in (0, 1):
                if (k, f) != (0, 0):
                    at = k * 2 + f - 1
                    sq_copies.append(
                        remote(square, squares.at[at], s_sq.at[at], r_sq.at[at], tensor_peer(k, f))
                    )
        for copy in sq_copies:
            copy.wait_recv()
        sign = jnp.where(lax.broadcasted_iota(jnp.int32, (tall, HEAD), 1) < HEAD // 2, -1.0, 1.0)

        def rotate(i):
            at = rows_of(i, tall)
            sums = square[:, at]
            for copy_at in range(tensor - 1):
                sums = sums + squares[copy_at, :, at]
            column = jnp.concatenate([sums, jnp.zeros((120, tall), f32)], axis=0).T
            scales = lax.rsqrt(column / width + norm_eps)
            scale_ref[at] = scales
            cosine, sine = cos_ref[at], sin_ref[at] * sign
            for c, low in ((0, q_low), (1, k_low)):
                hat = hat_ref[c, at] * scales[:, c : c + 1]
                hat_ref[c, at] = hat
                normed = hat * gain_rows[c : c + 1, rows_of(t_at, span)]
                for h in range(heads):
                    cols = slice(h * HEAD, (h + 1) * HEAD)
                    value = normed[:, cols]
                    turned = pltpu.roll(value, HEAD // 2, 1)
                    low[at, cols] = (value * cosine + turned * sine).astype(bf16)

        looped(length // tall, rotate)
        scale = HEAD ** (-0.5)
        top_ref[...] = jnp.full((8, 128), masked_value, f32)
        for h in range(heads):
            cols = slice(h * HEAD, (h + 1) * HEAD)

            def attend(i, best, cols=cols, h=h):
                at = rows_of(i, tall)
                raw = dot(q_low[at, cols], k_low[:, cols], ((1,), (1,))) * scale
                masked = jnp.where(id_row[...] <= id_col[at], raw, masked_value)
                top = jnp.max(masked, axis=1, keepdims=True)
                weight = jnp.exp(masked - top)
                total = jnp.sum(weight, axis=1, keepdims=True)
                probs = (weight * (1.0 / total)).astype(bf16)
                context[at, cols] = dot(probs, v_low[:, cols], ((1,), (0,))).astype(bf16)
                lse_ref[at, h : h + 1] = top + jnp.log(total)
                return jnp.maximum(best, jnp.max(top, axis=0, keepdims=True))

            best = lax.fori_loop(
                0, length // tall, attend, jnp.full((1, 1), masked_value, f32), unroll=length // tall <= 4
            )
            top_ref[h : h + 1] = jnp.broadcast_to(best, (1, 128))
            if h + 1 == max(heads // 2, 1):
                next_duties(1)
        next_duties(1)

        def out_rows(k, flip, store):
            chip = lax.rem(g.chip_at + k, chips)
            core = 1 - g.core_at if flip else g.core_at
            at = rows_of(chip * 2 + core, count)

            def columns(i):
                cols = rows_of(i, tile)
                store(cols, dot(context[at], out_w_ref[:, cols], ((1,), (0,))))

            looped(width // tile, columns)

        chip_order = list(range(1, chips)) + [0]
        core_copies, chip_copies = {}, {}
        for k in chip_order:

            def store(cols, value, k=k):
                core_send[k, :, cols] = value.astype(bf16)

            out_rows(k, True, store)
            core_copies[k] = remote(
                core_send.at[k], core_land.at[k], s_core.at[k], r_core.at[k], tensor_peer(0, 1)
            )
        for k in chip_order:

            def store(cols, value, k=k):
                hold[k, :, cols] = value

            out_rows(k, False, store)
            if k:
                core_copies[k].wait_recv()

                def add(i, k=k):
                    at = rows_of(i, lines)
                    chip_send[k - 1, at] = (hold[k, at] + core_land[k, at].astype(f32)).astype(bf16)

                looped(count // lines, add)
                chip_copies[k] = remote(
                    chip_send.at[k - 1], chip_land.at[k - 1], s_chip.at[k], r_chip.at[k], tensor_peer(k, 0)
                )
        core_copies[0].wait_recv()
        for k in range(1, chips):
            chip_copies[k].wait_recv()

        def close(i):
            at = rows_of(i, lines)
            raw = hold[0, at] + core_land[0, at].astype(f32)
            for k in range(1, chips):
                raw = raw + chip_land[k - 1, at].astype(f32)
            scale_o = lax.rsqrt(jnp.mean(raw * raw, axis=1, keepdims=True) + norm_eps)
            hat = raw * scale_o
            attn_hat[at] = hat
            o_scale[at] = scale_o
            value = rows_ref[at].astype(f32) + hat * gain_rows[2:3]
            resid[at] = value
            resid_low[at] = value.astype(bf16)

        looped(count // lines, close)
        next_duties(len(duties))
        own.wait()
        for key, copy in y_copies.items():
            if key[0] == inner - 1:
                copy.wait_recv()
        for copy in outs:
            copy.wait()
        sent = list(hops.values()) + row_copies + list(z_copies.values()) + list(y_copies.values()) + sq_copies
        for copy in sent + list(core_copies.values()) + list(chip_copies.values()):
            copy.wait_send()

    shape = jax.ShapeDtypeStruct
    anywhere = pl.BlockSpec(memory_space=pl.ANY)
    vmem = pl.BlockSpec(memory_space=pltpu.VMEM)
    sems = pltpu.SemaphoreType.DMA
    results = pl.pallas_call(
        kernel,
        out_shape=(shape((3, slab, units), bf16),) * parts
        + (
            shape((lead, width, span), bf16),
            shape((span, width), bf16),
            shape((length, width), bf16),
            shape((8, width), f32),
            shape((2, length, span), f32),
            shape((length, 128), f32),
            shape((length, span), bf16),
            shape((length, span), bf16),
            shape((length, span), bf16),
            shape((length, heads), f32),
            shape((length, span), bf16),
            shape((count, width), f32),
            shape((count, 1), f32),
            shape((count, width), f32),
            shape((count, width), bf16),
            shape((8, 128), f32),
        ),
        in_specs=[anywhere] * 5 + [vmem] * 6,
        out_specs=(anywhere,) * (parts + 3) + (vmem,) * 13,
        scratch_shapes=[
            pltpu.VMEM((lead, width, span), bf16),
            pltpu.VMEM((span, width), bf16),
            pltpu.VMEM((length, width), bf16),
            pltpu.VMEM((n, 16, slab), bf16),
            pltpu.VMEM(w_qkv.shape, f32),
            pltpu.VMEM(w_out.shape, f32),
            pltpu.VMEM(w_gu.shape, f32),
            pltpu.VMEM(w_down.shape, f32),
            pltpu.VMEM((3, slab, shard_units), bf16),
            pltpu.VMEM((8, length), f32),
            pltpu.VMEM((tensor - 1, 8, length), f32),
            pltpu.VMEM((chips, count, width), bf16),
            pltpu.VMEM((chips, count, width), bf16),
            pltpu.VMEM((chips, count, width), f32),
            pltpu.VMEM((max(chips - 1, 1), count, width), bf16),
            pltpu.VMEM((max(chips - 1, 1), count, width), bf16),
            sems((n - 1, ring)),
            sems((n - 1, ring)),
            sems((2 * chips - 1,)),
            sems((2 * chips - 1,)),
            sems((outer, 3)),
            sems((outer, 3)),
            sems((inner, outer, 3)),
            sems((inner, outer, 3)),
            sems((tensor - 1,)),
            sems((tensor - 1,)),
            sems((chips,)),
            sems((chips,)),
            sems((chips,)),
            sems((chips,)),
            sems((7,)),
        ],
        compiler_params=pltpu.CompilerParams(
            collective_id=0, has_side_effects=True, vmem_limit_bytes=58 * 2**20
        ),
    )(
        w_qkv, w_out, rows, w_gu, w_down, gains, tables[0], tables[1],
        blocks[:, None], blocks[None, :], rows,
    )
    pieces = [results[j * outer : (j + 1) * outer] for j in range(inner)]
    return pieces, results[parts:]


def unit_kernel_call(rows_low, resid, cotangent, gain, pieces):
    grid = Grid()
    outer, chips, inner = grid.outer, grid.chips, grid.inner
    total_rows, width = rows_low.shape
    units = pieces[0][0].shape[2]
    slab = pieces[0][0].shape[1]
    flat_pieces = [piece for row in pieces for piece in row]
    parts = len(flat_pieces)
    halves = 2
    count = total_rows // halves
    both = 2 * count
    per = min(2, chips)
    groups = chips // per
    blocks = outer * groups
    tall = per * both
    held = per if groups > 1 else max(per - 1, 1)
    links = outer * (chips - 1)
    steps = list(range(outer))
    far_first = [0] + steps[2:] + steps[1:2]

    def units_of(of_steps):
        return [(s, i) for s in of_steps for i in range(groups)]

    orders = {
        (0, 0): units_of(far_first),
        (0, 1): units_of(far_first),
        (1, 0): units_of(steps),
        (1, 1): units_of(far_first),
    }
    grad_order = units_of(far_first)
    tile = 512
    wide_tiles = width // tile
    unit_tile = min(256, units)
    lines = 32
    bf16, f32 = jnp.bfloat16, jnp.float32
    mesh_id = pl.DeviceIdType.MESH

    def plan():
        chip_us, core_us, hop_us = 5.6, 0.6, 2.0
        free = {"x": 0.0, "core": 0.0, "z near": 0.0, "z far": 0.0}
        arrive, done, tasks = {}, {}, {}

        def send(link, when, us):
            free[link] = max(free[link], when) + us
            return free[link] + hop_us

        def add(name, needs, us, after=None):
            tasks[name] = (needs, us, after)

        def send_outer(s, now):
            return send("z near", now, 8.0) if s == 1 else send("z far", now, 10.5)

        def go(p, h):
            def then(now):
                if (p, h) != (0, 1):
                    for s in steps[1:]:
                        arrive["z", p, h, s] = send_outer(s, now)
                for k in range(1, chips):
                    arrive["x", p, h, 0, k] = send("x", now, chip_us)
                arrive["c", p, h, 0, 0] = send("core", now, core_us)

            return then

        def zf(p, h, s):
            def then(now):
                for k in range(1, chips):
                    arrive["x", p, h, s, k] = send("x", now, chip_us)
                arrive["c", p, h, s, 0] = send("core", now, core_us)
                if (p, h) == (0, 0):
                    arrive["z", 0, 1, s] = send_outer(s, now)

            return then

        def xf(p, h, s, k):
            def then(now):
                arrive["c", p, h, s, k] = send("core", now, core_us)

            return then

        def compute(p, h, s, i):
            def then(now):
                arrive["cr", p, h, s, i] = send("core", now, per * core_us)

            return then

        def cr(p, h, s, i):
            def then(now):
                for k in range(i * per, i * per + per):
                    if k:
                        arrive["xr", p, h, s, k] = send("x", now, chip_us)

            return then

        def xr(p, h, s):
            def then(now):
                if s:
                    arrive["zr", p, h, s] = send_outer(s, now)

            return then

        for p in (0, 1):
            for h in range(halves):
                if p == 0:
                    needs = [("do", ("go", 0, h - 1))] if h else []
                else:
                    needs = [("do", ("between", h))]
                add(("go", p, h), needs, 0.2, go(p, h))
                for s in steps[1:]:
                    add(("zf", p, h, s), [("at", ("z", p, h, s))], 0.2, zf(p, h, s))
                for s in steps:
                    for k in range(1, chips):
                        add(("xf", p, h, s, k), [("at", ("x", p, h, s, k))], 0.2, xf(p, h, s, k))
                order = orders[p, h]
                for n, (s, i) in enumerate(order):
                    needs = [("at", ("c", p, h, s, i * per + j)) for j in range(per)]
                    if n:
                        needs.append(("do", ("front", p, h) + order[n - 1]))
                    add(("load", p, h, s, i), needs, 0.2)
                    add(("front", p, h, s, i), [("do", ("load", p, h, s, i))], (2.4, 1.6)[p])
                    needs = [("do", ("front", p, h, s, i))]
                    if n:
                        needs.append(("do", ("cr", p, h) + order[n - 1]))
                    add(("compute", p, h, s, i), needs, (1.6, 2.4)[p], compute(p, h, s, i))
                    needs = [("at", ("cr", p, h, s, i)), ("do", ("compute", p, h, s, i))]
                    add(("cr", p, h, s, i), needs, 0.5, cr(p, h, s, i))
                for s in steps:
                    needs = [("do", ("cr", p, h, s, 0))]
                    needs += [("at", ("xr", p, h, s, k)) for k in range(1, chips)]
                    add(("xr", p, h, s), needs, 0.4, xr(p, h, s))
                for s in steps[1:]:
                    needs = [("at", ("zr", p, h, s)), ("do", ("xr", p, h, 0))]
                    add(("zr", p, h, s), needs, 0.4)
        for h in range(halves):
            needs = [("do", ("zr", 0, h, s)) for s in steps[1:]] + [("do", ("xr", 0, h, 0))]
            add(("between", h), needs, 1.0)
        for n, (s, i) in enumerate(grad_order):
            needs = [("do", ("compute", 1, h, s, i)) for h in range(halves)]
            if n:
                needs.append(("do", ("grads",) + grad_order[n - 1] + (2,)))
            add(("fetch", s, i), needs, 0.2)
            for c in range(3):
                needs = [("do", ("grads", s, i, c - 1) if c else ("fetch", s, i))]
                add(("grads", s, i, c), needs, 2.8)
        written = [(j, s) for j in range(inner) for s in range(outer)]
        for n, at in enumerate(written):
            needs = [("do", ("grads",) + grad_order[-1] + (2,))]
            if n:
                needs = [("do", ("write",) + written[n - 1])]
            add(("write",) + at, needs, 0.6)
        rank = {"compute": 1, "front": 2, "fetch": 2, "grads": 3, "write": 4}
        result = []
        now = 0.0
        while tasks:
            best = None
            for name, (needs, us, then) in tasks.items():
                ready = 0.0
                for kind, key in needs:
                    table = arrive if kind == "at" else done
                    if key not in table:
                        ready = None
                        break
                    ready = max(ready, table[key] + (1.0 if key[0] in ("load", "fetch") else 0.0))
                if ready is None:
                    continue
                key = (max(ready, now), rank.get(name[0], 0))
                if best is None or key < best[0]:
                    best = (key, name)
            (ready, _), name = best
            needs, us, then = tasks.pop(name)
            now = ready + us
            done[name] = now
            if then is not None:
                then(now)
            result.append(name)
        return result

    def kernel(*refs):
        piece_refs = refs[:parts]
        fixed = refs[parts : parts + 9]
        grad_refs = refs[parts + 9 : parts + 9 + 3 * inner]
        body(piece_refs, *fixed, grad_refs, *refs[parts + 9 + 3 * inner :])

    def body(
        piece_refs, rows_ref, resid_ref, cot_ref, gain_ref,
        out_ref, dres_ref, gain_out, all_x, all_dm, grad_refs,
        wg, wu, wd, buf, wide_buf, act, coef_gate, coef_up, d_gate, d_up, turned, acc_gate, acc_up, acc_down, stage,
        core_send, core_land, hold, keep, chip_send, chip_land, outer_send, outer_land, raw, d_mlp,
        s_outer, r_outer, s_chip, r_chip, s_core, r_core,
        s_core_sum, r_core_sum, s_chip_sum, r_chip_sum, s_outer_sum, r_outer_sum,
        local, local_own, local_wide, local_w, local_g,
    ):
        g = Grid()
        core_peer = (g.dp_at, g.chip_at * 2 + 1 - g.core_at)

        def chip_peer(k):
            return (g.dp_at, lax.rem(g.chip_at + k + chips, chips) * 2 + g.core_at)

        def outer_peer(s):
            return (g.outer_flip(g.outer_at, s) * inner + g.inner_at, g.tensor_at)

        greet(
            [core_peer]
            + [chip_peer(k) for k in range(1, chips)]
            + [outer_peer(s) for s in range(1, outer)]
        )

        def remote(src, dst, send, recv, peer):
            copy = pltpu.make_async_remote_copy(
                src_ref=src, dst_ref=dst, send_sem=send, recv_sem=recv,
                device_id=peer, device_id_type=mesh_id,
            )
            copy.start()
            return copy

        def fetch(src, dst, sem):
            copy = pltpu.make_async_copy(src, dst, sem)
            copy.start()
            return copy

        def dot(a, b, contract):
            return lax.dot_general(a, b, (contract, ((), ())), preferred_element_type=f32)

        def looped(total, make):
            lax.fori_loop(0, total, lambda i, c: (make(i), c)[1], 0, unroll=total <= 4)

        def by_lines(make):
            looped(count // lines, lambda i: make(pl.ds(pl.multiple_of(i * lines, lines), lines)))

        def by_tiles(make):
            looped(wide_tiles, lambda i: make(pl.ds(pl.multiple_of(i * tile, tile), tile)))

        weights = (wg, wu, wd)
        fetches = []

        def fetch_weights():
            for j in range(inner):
                for s in range(outer):
                    index = g.outer_flip(g.outer_at, s) * inner
                    index = index + lax.rem(g.inner_at - j + inner, inner)
                    span = pl.ds(pl.multiple_of(index * slab, slab), slab)
                    for c in range(3):
                        at = j * outer + s
                        fetches.append(
                            fetch(piece_refs[at].at[c], weights[c].at[span], local_w.at[at, c])
                        )

        mine, theirs = pl.ds(0, count), pl.ds(count, count)
        every = (all_x, all_dm)
        copies, sums, loads, own = {}, {}, {}, {}
        unsent = {(p, h): [] for p in (0, 1) for h in range(halves)}

        def track(p, h, copy):
            unsent[p, h].append(copy)
            return copy

        def core_copy(p, h, s, k, src):
            dst = every[p].at[h, s, k, theirs]
            copies["c", p, h, s, k] = track(
                p, h, remote(src, dst, s_core.at[p, h, s, k], r_core.at[p, h, s, k], core_peer)
            )

        def chip_copy(p, h, s, k, src):
            dst = every[p].at[h, s, k, mine]
            copies["x", p, h, s, k] = track(
                p, h, remote(src, dst, s_chip.at[p, h, s, k], r_chip.at[p, h, s, k], chip_peer(k))
            )

        def outer_copy(p, h, s):
            source = (rows_ref, d_mlp)[p].at[pl.ds(h * count, count)]
            dst = every[p].at[h, s, 0, mine]
            copies["z", p, h, s] = track(
                p, h, remote(source, dst, s_outer.at[p, h, s], r_outer.at[p, h, s], outer_peer(s))
            )

        def go(p, h):
            source = (rows_ref, d_mlp)[p].at[pl.ds(h * count, count)]
            if (p, h) != (0, 1):
                for s in steps[1:]:
                    outer_copy(p, h, s)
            for k in range(1, chips):
                chip_copy(p, h, 0, k, source)
            core_copy(p, h, 0, 0, source)
            own[p, h] = fetch(source, every[p].at[h, 0, 0, mine], local_own.at[p, h])
            if p == 0 and h == 0:
                fetch_weights()

        def part_out(h, s, i, cols, part_sum):
            for j in range(per):
                own_rows = part_sum[j * both : j * both + count]
                if i * per + j == 0:
                    keep[h, s, :, cols] = own_rows
                else:
                    hold[h, min(j, held - 1), :, cols] = own_rows
                core_send[h, j, :, cols] = part_sum[j * both + count : (j + 1) * both].astype(bf16)

        def forward(h, unit):
            for j in range(units // unit_tile):
                cols = pl.ds(j * unit_tile, unit_tile)
                rows = buf[h].reshape(tall, width)
                gate = dot(rows, wg[:, cols], ((1,), (0,)))
                up = dot(rows, wu[:, cols], ((1,), (0,)))
                sigma = jax.nn.sigmoid(gate)
                silu = gate * sigma
                act[unit, h, :, cols] = (silu * up).astype(bf16)
                coef_up[unit, h, :, cols] = silu.astype(bf16)
                coef_gate[unit, h, :, cols] = (
                    up * sigma * (1.0 + gate * (1.0 - sigma))
                ).astype(bf16)

        def forward_out(h, unit, s, i):
            by_tiles(
                lambda cols: part_out(h, s, i, cols, dot(act[unit, h], wd[cols, :], ((1,), (1,))))
            )

        def backward(h, unit):
            for j in range(units // unit_tile):
                cols = pl.ds(j * unit_tile, unit_tile)
                d_act = dot(buf[h].reshape(tall, width), wd[:, cols], ((1,), (0,)))
                d_gate[unit, h, :, cols] = (d_act * coef_gate[unit, h, :, cols].astype(f32)).astype(bf16)
                d_up[unit, h, :, cols] = (d_act * coef_up[unit, h, :, cols].astype(f32)).astype(bf16)

        def backward_out(h, unit, s, i):
            def into(cols):
                part_sum = dot(d_gate[unit, h], wg[cols, :], ((1,), (1,)))
                part_sum = part_sum + dot(d_up[unit, h], wu[cols, :], ((1,), (1,)))
                part_out(h, s, i, cols, part_sum)

            by_tiles(into)

        def weight_grads(unit, c):
            first = unit == grad_order[0][0] * groups + grad_order[0][1]
            left, right, acc = ((d_gate, 0, acc_gate), (d_up, 0, acc_up), (act, 1, acc_down))[c]
            turned[...] = left[unit].reshape(halves * tall, units).T

            def grads(cols):
                rows = wide_buf[right, :, :, :, cols].reshape(halves * tall, tile)
                value = dot(turned[...], rows, ((1,), (0,)))
                acc[:, cols] = value if first else acc[:, cols] + value

            by_tiles(grads)

        def between(h):
            def lines_of(i, total):
                at_rows = pl.ds(pl.multiple_of(h * count + i * lines, lines), lines)
                value = raw[at_rows]
                scale = lax.rsqrt(jnp.mean(value * value, axis=1, keepdims=True) + norm_eps)
                hat = value * scale
                gain_row = gain_ref[3:4]
                out_ref[at_rows] = (resid_ref[at_rows] + hat * gain_row).astype(bf16)
                top = cot_ref[at_rows].astype(f32)
                upstream = top * gain_row
                mean = jnp.mean(upstream * hat, axis=1, keepdims=True)
                d_mlp[at_rows] = (scale * (upstream - hat * mean)).astype(bf16)
                return total + jnp.sum(top * hat, axis=0, keepdims=True)

            zero = jnp.zeros((1, width), f32)
            total = lax.fori_loop(0, count // lines, lines_of, zero)
            gain_out[...] = total if h == 0 else gain_out[...] + total

        batches = []

        def write_grads(j, s):
            index = g.outer_flip(g.outer_at, s) * inner
            index = index + lax.rem(g.inner_at + j, inner)
            span = pl.ds(pl.multiple_of(index * slab, slab), slab)
            slot = len(batches) % 2
            if len(batches) >= 2:
                for copy in batches[-2]:
                    copy.wait()
            batch = []
            for c, acc in enumerate((acc_gate, acc_up, acc_down)):
                stage[slot, c] = acc[:, span].astype(bf16)
                batch.append(
                    fetch(stage.at[slot, c], grad_refs[j * 3 + c].at[s], local_g.at[slot, c])
                )
            batches.append(batch)

        def core_sum(p, h, s, i):
            unit = s * groups + i
            sums["c", p, h, unit].wait_recv()
            for j in range(per):
                chip = i * per + j
                if chip == 0:

                    def add(at_rows):
                        keep[h, s, at_rows] = keep[h, s, at_rows] + core_land[h, unit, j, at_rows].astype(f32)

                    by_lines(add)
                    continue
                there = s * (chips - 1) + chip - 1

                def add(at_rows):
                    total = hold[h, min(j, held - 1), at_rows] + core_land[h, unit, j, at_rows].astype(f32)
                    chip_send[h, there, at_rows] = total.astype(bf16)

                by_lines(add)
                sums["x", p, h, s, chip] = track(
                    p, h,
                    remote(
                        chip_send.at[h, there], chip_land.at[h, there],
                        s_chip_sum.at[p, h, there], r_chip_sum.at[p, h, there], chip_peer(-chip),
                    ),
                )

        def chip_sum(p, h, s):
            for k in range(1, chips):
                sums["x", p, h, s, k].wait_recv()

            def add(at_rows):
                total = keep[h, s, at_rows]
                for k in range(1, chips):
                    total = total + chip_land[h, s * (chips - 1) + k - 1, at_rows].astype(f32)
                if s == 0:
                    raw[pl.ds(pl.multiple_of(h * count + at_rows.start, lines), lines)] = total
                else:
                    outer_send[h, s - 1, at_rows] = total.astype(bf16)

            by_lines(add)
            if s:
                sums["z", p, h, s] = track(
                    p, h,
                    remote(
                        outer_send.at[h, s - 1], outer_land.at[h, s - 1],
                        s_outer_sum.at[p, h, s], r_outer_sum.at[p, h, s], outer_peer(s),
                    ),
                )

        def outer_sum(p, h, s):
            sums["z", p, h, s].wait_recv()

            def add(at_rows):
                there = pl.ds(pl.multiple_of(h * count + at_rows.start, lines), lines)
                raw[there] = raw[there] + outer_land[h, s - 1, at_rows].astype(f32)

            by_lines(add)

        def all_sent(p, h):
            for copy in unsent[p, h]:
                copy.wait_send()

        last_core = {}
        for task in plan():
            name, args = task[0], task[1:]
            if name == "go":
                go(*args)
            elif name == "zf":
                p, h, s = args
                copies["z", p, h, s].wait_recv()
                source = every[p].at[h, s, 0, mine]
                for k in range(1, chips):
                    chip_copy(p, h, s, k, source)
                core_copy(p, h, s, 0, source)
                if (p, h) == (0, 0):
                    outer_copy(0, 1, s)
            elif name == "xf":
                p, h, s, k = args
                copies["x", p, h, s, k].wait_recv()
                core_copy(p, h, s, k, every[p].at[h, s, k, mine])
            elif name == "load":
                p, h, s, i = args
                for j in range(per):
                    copies["c", p, h, s, i * per + j].wait_recv()
                if (s, i) == (0, 0):
                    own[p, h].wait()
                src = every[p].at[h, s, pl.ds(i * per, per)]
                loads[args] = fetch(src, buf.at[h], local.at[p, h, s * groups + i])
            elif name == "front":
                p, h, s, i = args
                if p == 0 and not loads.get("weights"):
                    loads["weights"] = True
                    for copy in fetches:
                        copy.wait()
                loads[args].wait()
                (forward, backward)[p](h, s * groups + i)
            elif name == "compute":
                p, h, s, i = args
                unit = s * groups + i
                if h in last_core:
                    last_core[h].wait_send()
                (forward_out, backward_out)[p](h, unit, s, i)
                last_core[h] = remote(
                    core_send.at[h], core_land.at[h, unit],
                    s_core_sum.at[p, h, unit], r_core_sum.at[p, h, unit], core_peer,
                )
                sums["c", p, h, unit] = last_core[h]
            elif name == "cr":
                core_sum(*args)
            elif name == "xr":
                chip_sum(*args)
            elif name == "zr":
                outer_sum(*args)
            elif name == "between":
                all_sent(0, args[0])
                between(args[0])
            elif name == "fetch":
                s, i = args
                loads[task] = []
                for at, src in enumerate((all_x, all_dm)):
                    for h in range(halves):
                        loads[task].append(
                            fetch(
                                src.at[h, s, pl.ds(i * per, per)],
                                wide_buf.at[at, h],
                                local_wide.at[s * groups + i, at * halves + h],
                            )
                        )
            elif name == "grads":
                s, i, c = args
                if c == 0:
                    for copy in loads["fetch", s, i]:
                        copy.wait()
                weight_grads(s * groups + i, c)
            elif name == "write":
                write_grads(*args)

        looped(
            total_rows // lines,
            lambda i: close_rows(pl.ds(pl.multiple_of(i * lines, lines), lines), dres_ref, raw, cot_ref),
        )
        for h in range(halves):
            all_sent(1, h)
            last_core[h].wait_send()
        for batch in batches[-2:]:
            for copy in batch:
                copy.wait()

    shape = jax.ShapeDtypeStruct
    anywhere = pl.BlockSpec(memory_space=pl.ANY)
    near = pl.BlockSpec(memory_space=pltpu.VMEM)
    sems = pltpu.SemaphoreType.DMA
    flops = 2 * 9 * halves * tall * blocks * width * units
    results = pl.pallas_call(
        kernel,
        out_shape=(
            shape((total_rows, width), bf16),
            shape((total_rows, width), f32),
            shape((1, width), f32),
            shape((halves, outer, chips, both, width), bf16),
            shape((halves, outer, chips, both, width), bf16),
        )
        + (shape((outer, units, slab), bf16),) * (3 * inner),
        in_specs=[anywhere] * (parts + 1) + [near] * 3,
        out_specs=(near, near, near) + (anywhere,) * (2 + 3 * inner),
        scratch_shapes=[
            pltpu.VMEM((width, units), bf16),
            pltpu.VMEM((width, units), bf16),
            pltpu.VMEM((width, units), bf16),
            pltpu.VMEM((halves, per, both, width), bf16),
            pltpu.VMEM((2, halves, per, both, width), bf16),
            pltpu.VMEM((blocks, halves, tall, units), bf16),
            pltpu.VMEM((blocks, halves, tall, units), bf16),
            pltpu.VMEM((blocks, halves, tall, units), bf16),
            pltpu.VMEM((blocks, halves, tall, units), bf16),
            pltpu.VMEM((blocks, halves, tall, units), bf16),
            pltpu.VMEM((units, halves * tall), bf16),
            pltpu.VMEM((units, width), f32),
            pltpu.VMEM((units, width), f32),
            pltpu.VMEM((units, width), f32),
            pltpu.VMEM((2, 3, units, slab), bf16),
            pltpu.VMEM((halves, per, count, width), bf16),
            pltpu.VMEM((halves, blocks, per, count, width), bf16),
            pltpu.VMEM((halves, held, count, width), f32),
            pltpu.VMEM((halves, outer, count, width), f32),
            pltpu.VMEM((halves, links, count, width), bf16),
            pltpu.VMEM((halves, links, count, width), bf16),
            pltpu.VMEM((halves, outer - 1, count, width), bf16),
            pltpu.VMEM((halves, outer - 1, count, width), bf16),
            pltpu.VMEM((total_rows, width), f32),
            pltpu.VMEM((total_rows, width), bf16),
            sems((2, halves, outer)),
            sems((2, halves, outer)),
            sems((2, halves, outer, chips)),
            sems((2, halves, outer, chips)),
            sems((2, halves, outer, chips)),
            sems((2, halves, outer, chips)),
            sems((2, halves, blocks)),
            sems((2, halves, blocks)),
            sems((2, halves, links)),
            sems((2, halves, links)),
            sems((2, halves, outer)),
            sems((2, halves, outer)),
            sems((2, halves, blocks)),
            sems((2, halves)),
            sems((blocks, 2 * halves)),
            sems((parts, 3)),
            sems((2, 3)),
        ],
        compiler_params=pltpu.CompilerParams(
            collective_id=2, has_side_effects=True, vmem_limit_bytes=62 * 2**20
        ),
        cost_estimate=pl.CostEstimate(flops=flops, bytes_accessed=64 * 2**20, transcendentals=0),
    )(*flat_pieces, rows_low, resid, cotangent, gain)
    grads = results[5:]
    return results[:3] + ([[grads[j * 3 + c] for j in range(inner)] for c in range(3)],)


def close_rows(at_rows, dres_ref, raw, cot_ref):
    dres_ref[at_rows] = raw[at_rows] + cot_ref[at_rows].astype(jnp.float32)


def adam_tile(param, grad, first, second):
    fix_one = 1.0 - beta_one**STEP
    fix_two = 1.0 - beta_two**STEP
    first = beta_one * first + (1.0 - beta_one) * grad
    second = beta_two * second + (1.0 - beta_two) * (grad * grad)
    square = second * (1.0 / fix_two)
    below = square * lax.rsqrt(square) + adam_eps
    guess = pl.reciprocal(below, approx=True)
    inverse = guess * (2.0 - below * guess)
    step = (rate_matrix / fix_one) * (first * inverse)
    return (1.0 - rate_matrix * weight_decay) * param - step, first, second


def adam_kernel(turned, w_ref, m_ref, v_ref, g_ref, *rest):
    scale_ref = rest[0] if len(rest) == 5 else None
    w_out, m_out, v_out, c_out = rest[-4:]
    grad = g_ref[...].T if turned else g_ref[...]
    new, first, second = adam_tile(w_ref[...], grad, m_ref[...], v_ref[...])
    if scale_ref is not None:
        new = new * scale_ref[...]
    w_out[...] = new
    m_out[...] = first
    v_out[...] = second
    c_out[...] = new.astype(jnp.bfloat16)


def adam_call(param, grads, at, first, second, scale=None):
    mats, rows, columns = param.shape
    turned = scale is not None
    spec = pl.BlockSpec((None, rows, columns), lambda k: (k, 0, 0))
    grad_spec = pl.BlockSpec((None,) + grads.shape[1:], lambda k: (at + k, 0, 0))
    specs = [spec] * 3 + [grad_spec]
    values = [param, first, second, grads]
    if turned:
        values.append(scale)
        specs.append(pl.BlockSpec((None, 1, columns), lambda k: (k, 0, 0)))
    outs = [jax.ShapeDtypeStruct(param.shape, jnp.float32)] * 3
    outs.append(jax.ShapeDtypeStruct(param.shape, jnp.bfloat16))
    size = param.size
    return pl.pallas_call(
        functools.partial(adam_kernel, turned),
        grid=(mats,),
        in_specs=specs,
        out_specs=[spec] * 4,
        out_shape=outs,
        cost_estimate=pl.CostEstimate(
            flops=20 * size, bytes_accessed=28 * size, transcendentals=2 * size
        ),
        compiler_params=pltpu.CompilerParams(vmem_limit_bytes=32 * 2**20),
    )(*values)


def adam_units_kernel(turned, at_ref, w_ref, m_ref, v_ref, g_ref, w_out, m_out, v_out, c_out):
    grad = (g_ref[...].T if turned else g_ref[...]).astype(jnp.float32)
    new, first, second = adam_tile(w_ref[...], grad, m_ref[...], v_ref[...])
    w_out[...] = new
    m_out[...] = first
    v_out[...] = second
    c_out[...] = new.astype(jnp.bfloat16)


def adam_units(grid, param, first, second, grads, begin, turned):
    n = grid.outer
    _, _, units, wide = grads.shape
    mats = param.shape[0] if turned else 1
    if not turned:
        spec = pl.BlockSpec((units, wide), lambda c, k, at: (k, 0))
    else:
        spec = pl.BlockSpec((None, wide, units), lambda c, k, at: (c, 0, k))
    grad_spec = pl.BlockSpec(
        (None, None, units, wide), lambda c, k, at: (begin + c, lax.bitwise_xor(at[0], k), 0, 0)
    )
    size = param.size
    outs = [jax.ShapeDtypeStruct(param.shape, jnp.float32)] * 3
    outs.append(jax.ShapeDtypeStruct(param.shape, jnp.bfloat16))
    return pl.pallas_call(
        functools.partial(adam_units_kernel, turned),
        grid_spec=pltpu.PrefetchScalarGridSpec(
            num_scalar_prefetch=1,
            grid=(mats, n),
            in_specs=[spec] * 3 + [grad_spec],
            out_specs=[spec] * 4,
        ),
        out_shape=outs,
        cost_estimate=pl.CostEstimate(
            flops=20 * size, bytes_accessed=28 * size, transcendentals=2 * size
        ),
        compiler_params=pltpu.CompilerParams(vmem_limit_bytes=32 * 2**20),
    )(grid.outer_at.astype(jnp.int32)[None], param, first, second, grads)


def local(
    tokens,
    cotangent,
    block_ids,
    w_qkv,
    m_qkv,
    v_qkv,
    w_out,
    m_out,
    v_out,
    w_gu,
    m_gu,
    v_gu,
    w_down,
    m_down,
    v_down,
    gains,
    gain_m,
    gain_v,
):
    grid = Grid()
    local_x = tokens[0]
    gain_count = gains.shape[0]
    tables = rope_tables(local_x.shape[0] * grid.tensor, HEAD)
    pieces, kept = open_call(
        w_qkv,
        w_out,
        gains,
        local_x,
        w_gu,
        w_down,
        tables,
        block_ids[0],
    )
    full_qkv, full_out, seq_x, gain_rows = kept[:4]
    hats, scales, q_low, k_low, v_low, log_total, context_low = kept[4:11]
    attn_hat, o_scale, resid, resid_low, tops = kept[11:]
    output, d_resid, gain_last, unit_grads = unit_kernel_call(
        resid_low, resid, cotangent[0], gain_rows, pieces
    )
    backs, part, part_gains, tops, grad_tokens = attend_back_call(
        d_resid,
        attn_hat,
        o_scale,
        gain_rows,
        full_out,
        context_low,
        q_low,
        k_low,
        v_low,
        log_total,
        hats,
        scales,
        tables,
        block_ids[0],
        seq_x,
        full_qkv,
        gain_last,
        tops,
        unit_grads,
    )
    part_gains = part_gains[:gain_count]
    head_top = tops[: w_qkv.shape[2] // HEAD, 0]
    factor = clip_tau / jnp.maximum(head_top, clip_tau)
    column = jnp.repeat(jnp.sqrt(factor), HEAD)
    column_scale = jnp.stack([column, column, jnp.ones_like(column)])[:, None, :]
    new_qkv, new_m_qkv, new_v_qkv, copy_qkv = adam_call(w_qkv, part, 0, m_qkv, v_qkv, column_scale)
    new_out, new_m_out, new_v_out, copy_out = [
        v[0] for v in adam_call(w_out[None], part, 3, m_out[None], v_out[None])
    ]
    new_gu, new_m_gu, new_v_gu, copy_gu = adam_units(grid, w_gu, m_gu, v_gu, backs, 0, True)
    new_down, new_m_down, new_v_down, copy_down = adam_units(
        grid, w_down, m_down, v_down, backs, 2, False
    )
    new_gains, new_gain_m, new_gain_v = adam_step(gains, part_gains, gain_m, gain_v, rate_gain, 0.0)
    return (
        output[None],
        grad_tokens[None],
        new_qkv,
        new_m_qkv,
        new_v_qkv,
        copy_qkv,
        new_out,
        new_m_out,
        new_v_out,
        copy_out,
        new_gu,
        new_m_gu,
        new_v_gu,
        copy_gu,
        new_down,
        new_m_down,
        new_v_down,
        copy_down,
        new_gains,
        new_gain_m,
        new_gain_v,
        factor,
    )


def solution(mesh):
    return jax.shard_map(
        local,
        mesh=mesh,
        in_specs=(
            P("dp", "tensor", None),
            P("dp", "tensor", None),
            P("dp", None),
            P(None, "dp", "tensor"),
            P(None, "dp", "tensor"),
            P(None, "dp", "tensor"),
            P("tensor", "dp"),
            P("tensor", "dp"),
            P("tensor", "dp"),
            P(None, "dp", "tensor"),
            P(None, "dp", "tensor"),
            P(None, "dp", "tensor"),
            P("tensor", "dp"),
            P("tensor", "dp"),
            P("tensor", "dp"),
            P(None, "dp"),
            P(None, "dp"),
            P(None, "dp"),
        ),
        out_specs=(
            P("dp", "tensor", None),
            P("dp", "tensor", None),
            P(None, "dp", "tensor"),
            P(None, "dp", "tensor"),
            P(None, "dp", "tensor"),
            P(None, "dp", "tensor"),
            P("tensor", "dp"),
            P("tensor", "dp"),
            P("tensor", "dp"),
            P("tensor", "dp"),
            P(None, "dp", "tensor"),
            P(None, "dp", "tensor"),
            P(None, "dp", "tensor"),
            P(None, "dp", "tensor"),
            P("tensor", "dp"),
            P("tensor", "dp"),
            P("tensor", "dp"),
            P("tensor", "dp"),
            P(None, "dp"),
            P(None, "dp"),
            P(None, "dp"),
            P("tensor"),
        ),
        check_vma=False,
    )
```

```python
import jax
import jax.numpy as jnp
import numpy as np
from jax import lax
from jax.experimental import pallas as pl
from jax.experimental.pallas import tpu as pltpu
from jax.sharding import PartitionSpec as P

HEAD = 128
STEP = 5


norm_eps = 1e-06
rope_base = 500000.0
beta_one = 0.9
beta_two = 0.95
rate_matrix = 0.01
rate_gain = 0.6
weight_decay = 0.1
adam_eps = 1e-08
clip_tau = 9.0
masked_value = -1e30


def rope_tables(length, size):
    half = size // 2
    freq = np.float32(rope_base) ** (-(np.arange(half, dtype=np.float32) * np.float32(2.0 / size)))
    angle = np.arange(length, dtype=np.float32)[:, None] * freq[None, :]
    angle = np.concatenate([angle, angle], axis=1)
    return (jnp.asarray(np.cos(angle)), jnp.asarray(np.sin(angle)))


def adam_step(param, grad, first, second, rate, decay):
    first = beta_one * first + (1.0 - beta_one) * grad
    second = beta_two * second + (1.0 - beta_two) * grad * grad
    fix_one = 1.0 - beta_one**STEP
    fix_two = 1.0 - beta_two**STEP
    update = first / fix_one / (jnp.sqrt(second / fix_two) + adam_eps)
    return (param - rate * (update + decay * param), first, second)


class Grid:
    def __init__(self):
        self.dp = lax.axis_size("dp")
        self.tensor = lax.axis_size("tensor")
        self.inner = 1
        while self.inner * self.inner * 4 <= self.dp:
            self.inner *= 2
        self.outer = self.dp // self.inner
        self.chips = self.tensor // 2
        self.dp_at = lax.axis_index("dp")
        self.tensor_at = lax.axis_index("tensor")
        self.inner_at = self.dp_at % self.inner
        self.chip_at = self.tensor_at // 2
        self.core_at = self.tensor_at % 2
        self.outer_at = self.dp_at // self.inner

    def path_of(self, index):
        column, row = index // self.inner, index % self.inner
        return row * self.outer + column + (row % 2) * (self.outer - 1 - 2 * column)

    def outer_flip(self, index, step):
        result = 0
        for bit in bits(self.outer):
            side = index // bit % 2
            result = result + bit * (1 - side if step & bit else side)
        return result

    def index_of(self, place):
        row, column = place // self.outer, place % self.outer
        return (column + (row % 2) * (self.outer - 1 - 2 * column)) * self.inner + row


def bits(count):
    return [1 << k for k in range(count.bit_length() - 1)]


def greet(peers):
    barrier = pltpu.get_barrier_semaphore()
    for peer in peers:
        pl.semaphore_signal(barrier, inc=1, device_id=peer, device_id_type=pl.DeviceIdType.MESH)
    pl.semaphore_wait(barrier, len(peers))


def attend_back_call(
    d_resid, attn_hat, o_scale, gain_rows, full_out, context, q_low, k_low, v_low, lse, hats, scales,
    tables, blocks, seq, full_qkv, gain_last, tops, unit_grads,
):
    grid = Grid()
    n, outer, inner, chips, tensor = grid.dp, grid.outer, grid.inner, grid.chips, grid.tensor
    count, width = d_resid.shape
    length, span = context.shape
    heads = span // HEAD
    slab, units = unit_grads[0][0].shape[1:]
    thin = width // n
    half = span // 2
    tall = min(256, length)
    tile = 512
    lines = 32
    ring = 8 + 2
    gain_item, top_item = 8, 9
    bf16, f32 = jnp.bfloat16, jnp.float32
    mesh_id = pl.DeviceIdType.MESH
    flat_grads = [unit_grads[c][j] for j in range(inner) for c in range(3)]
    some = len(flat_grads)
    z_steps = list(range(1, outer))

    def kernel(*refs):
        fixed, far_in, grads_in = refs[:17], refs[17:20], refs[20 : 20 + some]
        rest = refs[20 + some :]
        body(*fixed, far_in, grads_in, *rest)

    def body(
        dres_ref, hat_ref, o_scale_ref, gain_ref, out_w, ctx, q_ref, k_ref, v_ref, lse_ref, scale_ref,
        cos_ref, sin_ref, id_col, id_row, last_ref, tops_ref, far_in, grads_in,
        gu_out, down_out, part_ref, part_out, gains_out, tops_out, tokens_out,
        hats, seq, qkv_w, seq_do, d_ctx, d_q, d_k, d_v, d_low, probs_low, whole, terms, row_terms, turned,
        land, land_gain, land_top, own_gain, peer_gain, inners, peer_inners,
        gu_land, gu_sum, down_land, down_sum, core_send, core_land, hold, chip_send, chip_land,
        s_ring, r_ring, s_row, r_row, s_in, r_in, s_y, r_y, s_z, r_z, s_core, r_core, s_chip, r_chip, s_gain, r_gain, local,
    ):
        hats_in, seq_in, qkv_in = far_in
        g = Grid()

        def tensor_peer(k, flip):
            core = 1 - g.core_at if flip else g.core_at
            return (g.dp_at, lax.rem(g.chip_at + k + chips, chips) * 2 + core)

        def dp_peer(s, j):
            across = g.outer_flip(g.outer_at, s) * inner
            return (across + lax.rem(g.inner_at + j + inner, inner), g.tensor_at)

        place = g.path_of(g.dp_at)
        after_dp = (g.index_of(lax.rem(place + 1, n)), g.tensor_at)
        before_dp = (g.index_of(lax.rem(place + n - 1, n)), g.tensor_at)
        near = [tensor_peer(k, f) for k in range(chips) for f in (0, 1) if (k, f) != (0, 0)]
        far = [dp_peer(s, 0) for s in range(1, outer)] + [dp_peer(0, j) for j in range(1, inner)]
        greet(near + far + [after_dp, before_dp])

        def remote(src, dst, send, recv, peer):
            copy = pltpu.make_async_remote_copy(
                src_ref=src, dst_ref=dst, send_sem=send, recv_sem=recv,
                device_id=peer, device_id_type=mesh_id,
            )
            copy.start()
            return copy

        def fetch(src, dst, at):
            copy = pltpu.make_async_copy(src, dst, local.at[at])
            copy.start()
            return copy

        def dot(a, b, contract):
            return lax.dot_general(a, b, (contract, ((), ())), preferred_element_type=f32)

        def looped(total, make):
            lax.fori_loop(0, total, lambda i, c: (make(i), c)[1], 0, unroll=total <= 4)

        def rows_of(i, size):
            return pl.ds(pl.multiple_of(i * size, size), size)

        sent = []
        y_copies = {}
        sum_steps = [(c, s) for c in range(3) for s in z_steps + [0]]
        for c, s in sum_steps:
            for j in range(1, inner):
                copy = remote(
                    grads_in[j * 3 + c].at[s],
                    down_land.at[j - 1, s] if c == 2 else gu_land.at[j - 1, c, s],
                    s_y.at[j, c, s],
                    r_y.at[j, c, s],
                    dp_peer(0, j),
                )
                y_copies[j, c, s] = copy
                sent.append(copy)
        own_refs = (gu_sum.at[0], gu_sum.at[1], down_sum)
        own_grads = [fetch(grads_in[c], own_refs[c], c) for c in range(3)]
        fetched = [fetch(hats_in, hats, 3), fetch(seq_in, seq, 4), fetch(qkv_in, qkv_w, 5)]
        z_copies = []
        keeps = []

        def unit_sums(times):
            for _ in range(times):
                if sum_steps:
                    unit_sum(*sum_steps.pop(0))

        def unit_sum(c, s):
            if s == (z_steps + [0])[0]:
                own_grads[c].wait()
            for j in range(1, inner):
                y_copies[j, c, s].wait_recv()

            def add_gu(i):
                rows = rows_of(i, 64)
                total = gu_sum[c, s, rows].astype(f32)
                for j in range(1, inner):
                    total = total + gu_land[j - 1, c, s, rows].astype(f32)
                gu_sum[c, s, rows] = total.astype(bf16)

            def add_down(i):
                rows = rows_of(i, 64)
                total = down_sum[s, rows].astype(f32)
                for j in range(1, inner):
                    total = total + down_land[j - 1, s, rows].astype(f32)
                down_sum[s, rows] = total.astype(bf16)

            there = rows_of(g.outer_at, units)
            if c == 2:
                looped(units // 64, add_down)
                src, dst = down_sum.at[s], down_out.at[there]
            else:
                looped(slab // 64, add_gu)
                src, dst = gu_sum.at[c, s], gu_out.at[c, :, there]
            if s:
                z_copies.append(remote(src, dst, s_z.at[c, s], r_z.at[c, s], dp_peer(s, 0)))
            else:
                keeps.append(fetch(src, dst, 6 + c))

        def way_of(item):
            return 1 if item >= 8 else 1 - 2 * (item // 4)

        def own(item, away):
            index = g.index_of(lax.rem(place - way_of(item) * away + 2 * n, n))
            if item == gain_item:
                return terms.at[index]
            if item == top_item:
                return tops_ref
            side, c = item // 4, item % 4
            return whole.at[c, pl.ds(side * half, half), rows_of(index, thin)]

        def landed(step, item):
            if item == gain_item:
                return land_gain.at[step]
            if item == top_item:
                return land_top.at[step]
            return land.at[step, item]

        hops = {}
        on_path = {}

        def hop(step, item):
            hops[step, item] = remote(
                own(item, 1) if step == 0 else landed(step - 1, item),
                landed(step, item),
                s_ring.at[step, item],
                r_ring.at[step, item],
                after_dp if way_of(item) == 1 else before_dp,
            )

        def depart(*items):
            for item in items:
                on_path[item] = 0
                hop(0, item)

        def advance(*items):
            for item in items:
                step = on_path.get(item, n) + 1
                if step >= n:
                    continue
                on_path[item] = step
                hops[step - 1, item].wait_recv()
                here = landed(step - 1, item)
                if item == top_item:
                    summed = jnp.maximum(here[...], tops_ref[...])
                else:
                    summed = here[...].astype(f32) + own(item, step + 1)[...].astype(f32)
                if step < n - 1:
                    here[...] = summed.astype(here.dtype)
                    hop(step, item)
                elif item == gain_item:
                    own_gain[0] = summed
                elif item == top_item:
                    tops_out[...] = summed
                else:
                    side, c = item // 4, item % 4
                    span_half = pl.ds(side * half, half)
                    if c == 3:
                        part_out[span_half] = summed
                    else:
                        part_ref[c, :, span_half] = summed.T

        def matrix_grad(c, left, right):
            turned[...] = left.T

            def columns(i):
                cols = rows_of(i, tile)
                whole[c, :, cols] = dot(turned[...], right[:, cols], ((1,), (0,))).astype(bf16)

            looped(width // tile, columns)

        t_at = g.tensor_at
        mine = rows_of(t_at, count)

        def open_rows(i, total):
            at = rows_of(i, lines)
            value, hat = dres_ref[at], hat_ref[at]
            upstream = value * gain_ref[2:3]
            mean = jnp.mean(upstream * hat, axis=1, keepdims=True)
            d_attn = (o_scale_ref[at] * (upstream - hat * mean)).astype(bf16)
            seq_do[pl.ds(pl.multiple_of(t_at * count + i * lines, lines), lines)] = d_attn
            return total + jnp.sum(value * hat, axis=0, keepdims=True)

        gain_attn = lax.fori_loop(0, count // lines, open_rows, jnp.zeros((1, width), f32))
        row_terms[...] = jnp.zeros((8, width), f32)
        row_terms[2:3] = gain_attn
        row_terms[3:4] = last_ref[...]
        moves, passed = [], []

        def row_copy(slot, index, peer):
            at = rows_of(index, count)
            copy = remote(seq_do.at[at], seq_do.at[at], s_row.at[slot], r_row.at[slot], peer)
            sent.append(copy)
            return copy

        for k in range(1, chips):
            moves.append(row_copy(k - 1, t_at, tensor_peer(k, 0)))
        to_core = row_copy(chips - 1, t_at, tensor_peer(0, 1))
        unit_sums(1)
        scale = HEAD ** (-0.5)
        for h in range(heads):
            cols = slice(h * HEAD, (h + 1) * HEAD)

            def weigh(i, c, cols=cols, h=h):
                at = rows_of(i, tall)
                raw = dot(q_ref[at, cols], k_ref[:, cols], ((1,), (1,))) * scale
                masked = jnp.where(id_row[...] <= id_col[at], raw, masked_value)
                probs_low[h, at] = jnp.exp(masked - lse_ref[at, h : h + 1]).astype(bf16)
                return c

            lax.fori_loop(0, length // tall, weigh, 0, unroll=length // tall <= 4)
            if 2 * (h + 1) == heads:
                unit_sums(1)
        for k in range(1, chips):
            moves[k - 1].wait_recv()
            source = lax.rem(g.chip_at - k + chips, chips) * 2 + g.core_at
            passed.append(row_copy(chips - 1 + k, source, tensor_peer(0, 1)))
        to_core.wait_recv()
        unit_sums(1)
        for copy in passed:
            copy.wait_recv()

        def context_grad(i):
            at = rows_of(i, tall)
            d_ctx[at] = dot(seq_do[at], out_w[...], ((1,), (1,))).astype(bf16)

        looped(length // tall, context_grad)
        unit_sums(1)

        for h in range(heads):
            cols = slice(h * HEAD, (h + 1) * HEAD)

            def head(i, c, cols=cols, h=h):
                at = rows_of(i, tall)
                q_part, ctx_part = q_ref[at, cols], d_ctx[at, cols]
                probs_part = probs_low[h, at]
                probs = probs_part.astype(f32)
                d_probs = dot(ctx_part, v_ref[:, cols], ((1,), (1,)))
                mean = jnp.sum(probs * d_probs, axis=1, keepdims=True)
                d_scores = (probs * (d_probs - mean)).astype(bf16)
                d_q[at, cols] = dot(d_scores, k_ref[:, cols], ((1,), (0,))) * scale
                key = dot(d_scores, q_part, ((0,), (0,))) * scale
                value = dot(probs_part, ctx_part, ((0,), (0,)))
                d_k[:, cols] = jnp.where(i == 0, key, d_k[:, cols] + key)
                d_v[:, cols] = jnp.where(i == 0, value, d_v[:, cols] + value)
                return c

            d_k[:, cols] = jnp.zeros((length, HEAD), f32)
            d_v[:, cols] = jnp.zeros((length, HEAD), f32)
            lax.fori_loop(0, length // tall, head, 0, unroll=length // tall <= 4)
            unit_sums(1)
        fetched[0].wait()
        sign = jnp.where(lax.broadcasted_iota(jnp.int32, (tall, HEAD), 1) < HEAD // 2, -1.0, 1.0)

        def unrotate(i, sums):
            at = rows_of(i, tall)
            cosine, sine = cos_ref[at], sin_ref[at]
            lane = lax.broadcasted_iota(jnp.int32, (tall, 128), 1)
            columns = jnp.zeros((tall, 128), f32)
            result = []
            for c, grad in ((0, d_q), (1, d_k)):
                total = jnp.zeros((tall, 1), f32)
                terms_row = []
                for h in range(heads):
                    cols = slice(h * HEAD, (h + 1) * HEAD)
                    value = grad[at, cols]
                    back = value * cosine - pltpu.roll(value * sine, HEAD // 2, 1) * sign
                    hat = hats[c, at, cols]
                    terms_row.append(jnp.sum(back * hat, axis=0, keepdims=True))
                    at_head = pl.ds(pl.multiple_of(t_at * span + h * HEAD, HEAD), HEAD)
                    back = back * gain_ref[c : c + 1, at_head]
                    grad[at, cols] = back
                    total = total + jnp.sum(back * hat, axis=1, keepdims=True)
                columns = jnp.where(lane == c, total, columns)
                result.append(sums[c] + jnp.concatenate(terms_row, axis=1))
            inners[:, at] = columns.T[:8]
            return tuple(result)

        zero = jnp.zeros((1, span), f32)
        gain_q, gain_k = lax.fori_loop(0, length // tall, unrotate, (zero, zero))
        offset = rows_of(t_at, span)
        row_terms[0:1, offset] = gain_q
        row_terms[1:2, offset] = gain_k
        in_copies = []
        for k in range(chips):
            for f in (0, 1):
                if (k, f) != (0, 0):
                    at = k * 2 + f - 1
                    in_copies.append(
                        remote(inners, peer_inners.at[at], s_in.at[at], r_in.at[at], tensor_peer(k, f))
                    )
        sent.extend(in_copies)
        matrix_grad(3, ctx[...], seq_do)
        depart(3, 7)
        for copy in in_copies:
            copy.wait_recv()
        unit_sums(1)

        def normed(i):
            at = rows_of(i, tall)
            sums = inners[:, at]
            for other in range(tensor - 1):
                sums = sums + peer_inners[other, :, at]
            column = jnp.concatenate([sums, jnp.zeros((120, tall), f32)], axis=0).T / width
            for c, grad in ((0, d_q), (1, d_k)):
                value = grad[at] - hats[c, at] * column[:, c : c + 1]
                d_low[c, at] = (scale_ref[at, c : c + 1] * value).astype(bf16)
            d_low[2, at] = d_v[at].astype(bf16)

        looped(length // tall, normed)
        fetched[1].wait()
        for c in (2, 0, 1):
            matrix_grad(c, d_low[c], seq)
            depart(c, c + 4)
            unit_sums(1)

        def place_terms(i, c):
            cols = pl.ds(pl.multiple_of(i * thin, thin), thin)
            terms[i] = row_terms[:, cols]
            return c

        lax.fori_loop(0, n, place_terms, 0)

        depart(gain_item, top_item)
        unit_sums(len(sum_steps))

        fetched[2].wait()
        chip_order = list(range(1, chips)) + [0]
        core_copies, chip_copies = {}, {}

        def token_rows(k, flip, store):
            chip = lax.rem(g.chip_at + k, chips)
            core = 1 - g.core_at if flip else g.core_at
            at = rows_of(chip * 2 + core, count)

            def columns(i):
                cols = rows_of(i, tile)
                total = dot(d_low[0, at], qkv_w[0, cols], ((1,), (1,)))
                for c in (1, 2):
                    total = total + dot(d_low[c, at], qkv_w[c, cols], ((1,), (1,)))
                store(cols, total)

            looped(width // tile, columns)

        duties = []
        for k in chip_order:

            def away(k=k):
                def store(cols, value):
                    core_send[k, :, cols] = value.astype(bf16)

                token_rows(k, True, store)
                core_copies[k] = remote(
                    core_send.at[k], core_land.at[k], s_core.at[k], r_core.at[k], tensor_peer(0, 1)
                )

            def here(k=k):
                def store(cols, value):
                    hold[k, :, cols] = value

                token_rows(k, False, store)

            def join(k=k):
                core_copies[k].wait_recv()

                def add(i):
                    at = rows_of(i, lines)
                    chip_send[k - 1, at] = (hold[k, at] + core_land[k, at].astype(f32)).astype(bf16)

                looped(count // lines, add)
                chip_copies[k] = remote(
                    chip_send.at[k - 1], chip_land.at[k - 1], s_chip.at[k], r_chip.at[k], tensor_peer(k, 0)
                )

            duties += [away, here] + ([join] if k else [])

        def close_tokens():
            core_copies[0].wait_recv()
            for k in range(1, chips):
                chip_copies[k].wait_recv()

            def close(i):
                at = rows_of(i, lines)
                total = dres_ref[at] + hold[0, at] + core_land[0, at].astype(f32)
                for k in range(1, chips):
                    total = total + chip_land[k - 1, at].astype(f32)
                tokens_out[at] = total

            looped(count // lines, close)

        duties.append(close_tokens)
        per_step = -(-len(duties) // (n - 2))
        for step in range(1, n):
            advance(3, 7, 2, 6, 0, 4, 1, 5, gain_item, top_item)
            for _ in range(per_step):
                if duties:
                    duties.pop(0)()
        peers = [tensor_peer(0, 1)] + [tensor_peer(k, 0) for k in range(1, chips)]
        first = remote(own_gain.at[0], peer_gain.at[0], s_gain.at[0], r_gain.at[0], peers[0])
        first.wait_recv()
        own_gain[1] = own_gain[0] + peer_gain[0]
        others = [
            remote(own_gain.at[1], peer_gain.at[k], s_gain.at[k], r_gain.at[k], peers[k])
            for k in range(1, chips)
        ]
        result = own_gain[1]
        for k in range(1, chips):
            others[k - 1].wait_recv()
            result = result + peer_gain[k]
        gains_out[...] = result
        for copy in z_copies:
            copy.wait()
        for copy in keeps:
            copy.wait()
        for copy in sent + list(hops.values()) + list(core_copies.values()):
            copy.wait_send()
        for copy in list(chip_copies.values()) + [first] + others:
            copy.wait_send()

    shape = jax.ShapeDtypeStruct
    anywhere = pl.BlockSpec(memory_space=pl.ANY)
    vmem = pl.BlockSpec(memory_space=pltpu.VMEM)
    sems = pltpu.SemaphoreType.DMA
    results = pl.pallas_call(
        kernel,
        out_shape=(
            shape((2, slab, outer * units), bf16),
            shape((outer * units, slab), bf16),
            shape((3, thin, span), f32),
            shape((span, thin), f32),
            shape((8, thin), f32),
            shape(tops.shape, f32),
            shape((count, width), f32),
        ),
        in_specs=[vmem] * 17 + [anywhere] * 3 + [anywhere] * some,
        out_specs=(anywhere,) * 2 + (vmem,) * 5,
        scratch_shapes=[
            pltpu.VMEM(hats.shape, f32),
            pltpu.VMEM(seq.shape, bf16),
            pltpu.VMEM(full_qkv.shape, bf16),
            pltpu.VMEM((length, width), bf16),
            pltpu.VMEM((length, span), bf16),
            pltpu.VMEM((length, span), f32),
            pltpu.VMEM((length, span), f32),
            pltpu.VMEM((length, span), f32),
            pltpu.VMEM((3, length, span), bf16),
            pltpu.VMEM((heads, length, length), bf16),
            pltpu.VMEM((4, span, width), bf16),
            pltpu.VMEM((n, 8, thin), f32),
            pltpu.VMEM((8, width), f32),
            pltpu.VMEM((span, length), bf16),
            pltpu.VMEM((n - 1, 8, half, thin), bf16),
            pltpu.VMEM((n - 1, 8, thin), f32),
            pltpu.VMEM((n - 1,) + tops.shape, f32),
            pltpu.VMEM((2, 8, thin), f32),
            pltpu.VMEM((chips, 8, thin), f32),
            pltpu.VMEM((8, length), f32),
            pltpu.VMEM((tensor - 1, 8, length), f32),
            pltpu.VMEM((max(inner - 1, 1), 2, outer, slab, units), bf16),
            pltpu.VMEM((2, outer, slab, units), bf16),
            pltpu.VMEM((max(inner - 1, 1), outer, units, slab), bf16),
            pltpu.VMEM((outer, units, slab), bf16),
            pltpu.VMEM((chips, count, width), bf16),
            pltpu.VMEM((chips, count, width), bf16),
            pltpu.VMEM((chips, count, width), f32),
            pltpu.VMEM((max(chips - 1, 1), count, width), bf16),
            pltpu.VMEM((max(chips - 1, 1), count, width), bf16),
            sems((n - 1, ring)),
            sems((n - 1, ring)),
            sems((2 * chips - 1,)),
            sems((2 * chips - 1,)),
            sems((tensor - 1,)),
            sems((tensor - 1,)),
            sems((inner, 3, outer)),
            sems((inner, 3, outer)),
            sems((3, outer)),
            sems((3, outer)),
            sems((chips,)),
            sems((chips,)),
            sems((chips,)),
            sems((chips,)),
            sems((chips,)),
            sems((chips,)),
            sems((9,)),
        ],
        compiler_params=pltpu.CompilerParams(
            collective_id=1, has_side_effects=True, vmem_limit_bytes=61 * 2**20
        ),
    )(
        d_resid, attn_hat, o_scale, gain_rows, full_out, context, q_low, k_low, v_low, lse, scales,
        tables[0], tables[1], blocks[:, None], blocks[None, :], gain_last, tops,
        hats, seq, full_qkv, *flat_grads,
    )
    return results


def open_call(w_qkv, w_out, gains, rows, w_gu, w_down, tables, blocks):
    grid = Grid()
    n, outer, inner = grid.dp, grid.outer, grid.inner
    chips, tensor = grid.chips, grid.tensor
    count, width = rows.shape
    length = count * tensor
    lead, slab, span = w_qkv.shape
    gain_count = gains.shape[0]
    half = slab // 2
    part_tall = span // 2
    heads = span // HEAD
    shard_units = w_gu.shape[2]
    units = shard_units // outer
    places = [(j, s) for j in range(inner) for s in range(outer) if not (j and s == outer - 1)]
    parts = len(places)
    ring = 2 * lead + 3
    steps = list(range(1, outer))
    tall = min(256, length)
    tile = 512
    lines = 32
    bf16, f32 = jnp.bfloat16, jnp.float32
    mesh_id = pl.DeviceIdType.MESH

    def kernel(*refs):
        body(*refs[:11], dict(zip(places, refs[11 : 11 + parts])), *refs[11 + parts :])

    def body(
        qkv_any, out_any, rows_any, gu_any, down_any, gains_ref, cos_ref, sin_ref, id_col, id_row, rows_ref,
        pieces, qkv_out, flat_out, seq_out,
        gain_rows, hat_ref, scale_ref, q_low, k_low, v_low, lse_ref, context, attn_hat, o_scale, resid, resid_low, top_ref,
        qkv_ref, out_w_ref, seq_ref, all_gains, qkv_wide, out_wide, gu_wide, down_wide, cast,
        square, squares, core_send, core_land, hold, chip_send, chip_land,
        s_ring, r_ring, s_row, r_row, s_z, r_z, s_y, r_y, s_sq, r_sq, s_core, r_core, s_chip, r_chip, local,
    ):
        g = Grid()

        def tensor_peer(k, flip):
            core = 1 - g.core_at if flip else g.core_at
            return (g.dp_at, lax.rem(g.chip_at + k + chips, chips) * 2 + core)

        def dp_peer(s, j):
            across = g.outer_flip(g.outer_at, s) * inner
            return (across + lax.rem(g.inner_at + j + inner, inner), g.tensor_at)

        near = [tensor_peer(k, f) for k in range(chips) for f in (0, 1) if (k, f) != (0, 0)]
        far = [dp_peer(s, 0) for s in range(1, outer)]
        far += [dp_peer(0, j) for j in sorted({1 % inner, inner - 1} - {0})]
        t_at = g.tensor_at
        place = g.path_of(g.dp_at)
        after = (g.index_of(lax.rem(place + 1, n)), t_at)
        before = (g.index_of(lax.rem(place + n - 1, n)), t_at)
        firsts = []
        for at, (src, dst) in enumerate(((qkv_any, qkv_wide), (out_any, out_wide))):
            firsts.append(pltpu.make_async_copy(src, dst, local.at[3 + at]))
            firsts[-1].start()
        greet(near + far + [after, before])

        def remote(src, dst, send, recv, peer):
            copy = pltpu.make_async_remote_copy(
                src_ref=src, dst_ref=dst, send_sem=send, recv_sem=recv,
                device_id=peer, device_id_type=mesh_id,
            )
            copy.start()
            return copy

        def dot(a, b, contract):
            return lax.dot_general(a, b, (contract, ((), ())), preferred_element_type=f32)

        def looped(total, make):
            lax.fori_loop(0, total, lambda i, c: (make(i), c)[1], 0, unroll=total <= 4)

        def rows_of(i, size):
            return pl.ds(pl.multiple_of(i * size, size), size)

        def fetch(src, dst, at):
            copy = pltpu.make_async_copy(src, dst, local.at[at])
            copy.start()
            return copy

        def views(item, index):
            if item == ring - 1:
                return 1, all_gains.at[index]
            if item >= 2 * lead:
                side = item - 2 * lead
                part = pl.ds(side * part_tall, part_tall)
                return 1 - 2 * side, out_w_ref.at[part, rows_of(index, slab)]
            side, c = item // lead, item % lead
            at = pl.ds(pl.multiple_of(index * slab + side * half, half), half)
            return 1 - 2 * side, qkv_ref.at[c, at]

        hops = {}

        def hop(step, item):
            way = views(item, 0)[0]
            index = g.index_of(lax.rem(place - way * step + n, n))
            _, view = views(item, index)
            hops[step, item] = remote(
                view,
                view,
                s_ring.at[step, item],
                r_ring.at[step, item],
                after if way == 1 else before,
            )

        def row_copy(slot, index, peer, src=None):
            at = seq_ref.at[rows_of(index, count)]
            return remote(at if src is None else src, at, s_row.at[slot], r_row.at[slot], peer)

        order = [c + side * lead for c in range(lead) for side in (0, 1)]
        order += list(range(2 * lead, ring))
        firsts[0].wait()
        for c in range(lead):

            def cast_own(i, c=c):
                at = rows_of(i, lines)
                there = pl.ds(pl.multiple_of(g.dp_at * slab + i * lines, lines), lines)
                qkv_ref[c, there] = qkv_wide[c, at].astype(bf16)

            looped(slab // lines, cast_own)
            for side in (0, 1):
                hop(0, c + side * lead)
        firsts[1].wait()

        def cast_flat(i):
            at = rows_of(i, lines)
            out_w_ref[at, rows_of(g.dp_at, slab)] = out_wide[at].astype(bf16)

        looped(span // lines, cast_flat)
        empty = jnp.zeros((16 - gain_count, slab), f32)
        all_gains[g.dp_at] = jnp.concatenate([gains_ref[...], empty], axis=0).astype(bf16)
        for item in range(2 * lead, ring):
            hop(0, item)
        row_copies = [
            row_copy(k - 1, t_at, tensor_peer(k, 0), rows_any) for k in range(1, chips)
        ]
        row_copies.append(row_copy(chips - 1, t_at, tensor_peer(0, 1), rows_any))
        wide = [fetch(gu_any, gu_wide, 1), fetch(down_any, down_wide, 2)]
        kept = fetch(rows_any, seq_ref.at[rows_of(t_at, count)], 5)

        def cast_wide(c):
            if c == 0:
                wide[0].wait()

            def cast_rows(i):
                at = rows_of(i, lines)
                cast[c, at] = gu_wide[c, at].astype(bf16)

            looped(slab // lines, cast_rows)

        def cast_turned():
            wide[1].wait()

            def cast_rows(i):
                at = rows_of(i, 256)
                cast[2, :, at] = down_wide[at].T.astype(bf16)

            looped(shard_units // 256, cast_rows)

        shadows = [lambda: cast_wide(0), lambda: cast_wide(1), cast_turned]
        for step in range(1, n - 1):
            for item in order:
                hops[step - 1, item].wait_recv()
                hop(step, item)
            if step <= chips - 1:
                row_copies[step - 1].wait_recv()
                source = lax.rem(g.chip_at - step + chips, chips) * 2 + g.core_at
                row_copies.append(row_copy(chips - 1 + step, source, tensor_peer(0, 1)))
            if shadows:
                shadows.pop(0)()

        def cut(s):
            return cast.at[:, :, rows_of(g.outer_flip(g.outer_at, s), units)]

        z_copies = {}

        for s in steps:
            z_copies[s] = remote(cut(s), pieces[0, s], s_z.at[s], r_z.at[s], dp_peer(s, 0))
        own = fetch(cut(0), pieces[0, 0], 0)
        y_copies = {}

        def pass_on(j, s):
            if (j, s) in pieces:
                src = cut(0) if (j, s) == (1, 0) else pieces[j - 1, s]
                y_copies[j, s] = remote(src, pieces[j, s], s_y.at[j, s], r_y.at[j, s], dp_peer(0, 1))

        pass_on(1, 0)
        duties = []
        for s in steps:

            def duty(s=s):
                z_copies[s].wait_recv()
                pass_on(1, s)

            duties.append(duty)
        for j in range(2, inner):
            for s in range(outer - 1):

                def duty(j=j, s=s):
                    y_copies[j - 1, s].wait_recv()
                    pass_on(j, s)

                duties.append(duty)

        def next_duties(times):
            for _ in range(times):
                if duties:
                    duties.pop(0)()

        for item in order:
            hops[n - 2, item].wait_recv()
        for copy in row_copies[chips - 1 :]:
            copy.wait_recv()
        kept.wait()
        outs = [fetch(qkv_ref, qkv_out, 3), fetch(out_w_ref, flat_out, 4), fetch(seq_ref, seq_out, 5)]

        def spread(i):
            gain_rows[:, rows_of(i, slab)] = all_gains[i].astype(f32)[:8]

        looped(n, spread)

        def project(i):
            at = rows_of(i, tall)
            x = seq_ref[at]
            lane = lax.broadcasted_iota(jnp.int32, (tall, 128), 1)
            sums = jnp.zeros((tall, 128), f32)
            for c in range(2):
                value = dot(x, qkv_ref[c], ((1,), (0,)))
                hat_ref[c, at] = value
                sums = jnp.where(lane == c, jnp.sum(value * value, axis=1, keepdims=True), sums)
            v_low[at] = dot(x, qkv_ref[2], ((1,), (0,))).astype(bf16)
            square[:, at] = sums.T[:8]

        looped(length // tall, project)
        sq_copies = []
        for k in range(chips):
            for f in (0, 1):
                if (k, f) != (0, 0):
                    at = k * 2 + f - 1
                    sq_copies.append(
                        remote(square, squares.at[at], s_sq.at[at], r_sq.at[at], tensor_peer(k, f))
                    )
        for copy in sq_copies:
            copy.wait_recv()
        sign = jnp.where(lax.broadcasted_iota(jnp.int32, (tall, HEAD), 1) < HEAD // 2, -1.0, 1.0)

        def rotate(i):
            at = rows_of(i, tall)
            sums = square[:, at]
            for copy_at in range(tensor - 1):
                sums = sums + squares[copy_at, :, at]
            column = jnp.concatenate([sums, jnp.zeros((120, tall), f32)], axis=0).T
            scales = lax.rsqrt(column / width + norm_eps)
            scale_ref[at] = scales
            cosine, sine = cos_ref[at], sin_ref[at] * sign
            for c, low in ((0, q_low), (1, k_low)):
                hat = hat_ref[c, at] * scales[:, c : c + 1]
                hat_ref[c, at] = hat
                normed = hat * gain_rows[c : c + 1, rows_of(t_at, span)]
                for h in range(heads):
                    cols = slice(h * HEAD, (h + 1) * HEAD)
                    value = normed[:, cols]
                    turned = pltpu.roll(value, HEAD // 2, 1)
                    low[at, cols] = (value * cosine + turned * sine).astype(bf16)

        looped(length // tall, rotate)
        scale = HEAD ** (-0.5)
        top_ref[...] = jnp.full((8, 128), masked_value, f32)
        for h in range(heads):
            cols = slice(h * HEAD, (h + 1) * HEAD)

            def attend(i, best, cols=cols, h=h):
                at = rows_of(i, tall)
                raw = dot(q_low[at, cols], k_low[:, cols], ((1,), (1,))) * scale
                masked = jnp.where(id_row[...] <= id_col[at], raw, masked_value)
                top = jnp.max(masked, axis=1, keepdims=True)
                weight = jnp.exp(masked - top)
                total = jnp.sum(weight, axis=1, keepdims=True)
                probs = (weight * (1.0 / total)).astype(bf16)
                context[at, cols] = dot(probs, v_low[:, cols], ((1,), (0,))).astype(bf16)
                lse_ref[at, h : h + 1] = top + jnp.log(total)
                return jnp.maximum(best, jnp.max(top, axis=0, keepdims=True))

            best = lax.fori_loop(
                0, length // tall, attend, jnp.full((1, 1), masked_value, f32), unroll=length // tall <= 4
            )
            top_ref[h : h + 1] = jnp.broadcast_to(best, (1, 128))
            if h + 1 == max(heads // 2, 1):
                next_duties(1)
        next_duties(1)

        def out_rows(k, flip, store):
            chip = lax.rem(g.chip_at + k, chips)
            core = 1 - g.core_at if flip else g.core_at
            at = rows_of(chip * 2 + core, count)

            def columns(i):
                cols = rows_of(i, tile)
                store(cols, dot(context[at], out_w_ref[:, cols], ((1,), (0,))))

            looped(width // tile, columns)

        chip_order = list(range(1, chips)) + [0]
        core_copies, chip_copies = {}, {}
        for k in chip_order:

            def store(cols, value, k=k):
                core_send[k, :, cols] = value.astype(bf16)

            out_rows(k, True, store)
            core_copies[k] = remote(
                core_send.at[k], core_land.at[k], s_core.at[k], r_core.at[k], tensor_peer(0, 1)
            )
        for k in chip_order:

            def store(cols, value, k=k):
                hold[k, :, cols] = value

            out_rows(k, False, store)
            if k:
                core_copies[k].wait_recv()

                def add(i, k=k):
                    at = rows_of(i, lines)
                    chip_send[k - 1, at] = (hold[k, at] + core_land[k, at].astype(f32)).astype(bf16)

                looped(count // lines, add)
                chip_copies[k] = remote(
                    chip_send.at[k - 1], chip_land.at[k - 1], s_chip.at[k], r_chip.at[k], tensor_peer(k, 0)
                )
        core_copies[0].wait_recv()
        for k in range(1, chips):
            chip_copies[k].wait_recv()

        def close(i):
            at = rows_of(i, lines)
            raw = hold[0, at] + core_land[0, at].astype(f32)
            for k in range(1, chips):
                raw = raw + chip_land[k - 1, at].astype(f32)
            scale_o = lax.rsqrt(jnp.mean(raw * raw, axis=1, keepdims=True) + norm_eps)
            hat = raw * scale_o
            attn_hat[at] = hat
            o_scale[at] = scale_o
            value = rows_ref[at].astype(f32) + hat * gain_rows[2:3]
            resid[at] = value
            resid_low[at] = value.astype(bf16)

        looped(count // lines, close)
        next_duties(len(duties))
        own.wait()
        for key, copy in y_copies.items():
            if key[0] == inner - 1:
                copy.wait_recv()
        for copy in outs:
            copy.wait()
        sent = list(hops.values()) + row_copies + list(z_copies.values()) + list(y_copies.values()) + sq_copies
        for copy in sent + list(core_copies.values()) + list(chip_copies.values()):
            copy.wait_send()

    shape = jax.ShapeDtypeStruct
    anywhere = pl.BlockSpec(memory_space=pl.ANY)
    vmem = pl.BlockSpec(memory_space=pltpu.VMEM)
    sems = pltpu.SemaphoreType.DMA
    results = pl.pallas_call(
        kernel,
        out_shape=(shape((3, slab, units), bf16),) * parts
        + (
            shape((lead, width, span), bf16),
            shape((span, width), bf16),
            shape((length, width), bf16),
            shape((8, width), f32),
            shape((2, length, span), f32),
            shape((length, 128), f32),
            shape((length, span), bf16),
            shape((length, span), bf16),
            shape((length, span), bf16),
            shape((length, heads), f32),
            shape((length, span), bf16),
            shape((count, width), f32),
            shape((count, 1), f32),
            shape((count, width), f32),
            shape((count, width), bf16),
            shape((8, 128), f32),
        ),
        in_specs=[anywhere] * 5 + [vmem] * 6,
        out_specs=(anywhere,) * (parts + 3) + (vmem,) * 13,
        scratch_shapes=[
            pltpu.VMEM((lead, width, span), bf16),
            pltpu.VMEM((span, width), bf16),
            pltpu.VMEM((length, width), bf16),
            pltpu.VMEM((n, 16, slab), bf16),
            pltpu.VMEM(w_qkv.shape, f32),
            pltpu.VMEM(w_out.shape, f32),
            pltpu.VMEM(w_gu.shape, f32),
            pltpu.VMEM(w_down.shape, f32),
            pltpu.VMEM((3, slab, shard_units), bf16),
            pltpu.VMEM((8, length), f32),
            pltpu.VMEM((tensor - 1, 8, length), f32),
            pltpu.VMEM((chips, count, width), bf16),
            pltpu.VMEM((chips, count, width), bf16),
            pltpu.VMEM((chips, count, width), f32),
            pltpu.VMEM((max(chips - 1, 1), count, width), bf16),
            pltpu.VMEM((max(chips - 1, 1), count, width), bf16),
            sems((n - 1, ring)),
            sems((n - 1, ring)),
            sems((2 * chips - 1,)),
            sems((2 * chips - 1,)),
            sems((outer,)),
            sems((outer,)),
            sems((inner, outer)),
            sems((inner, outer)),
            sems((tensor - 1,)),
            sems((tensor - 1,)),
            sems((chips,)),
            sems((chips,)),
            sems((chips,)),
            sems((chips,)),
            sems((7,)),
        ],
        compiler_params=pltpu.CompilerParams(
            collective_id=0, has_side_effects=True, vmem_limit_bytes=58 * 2**20
        ),
    )(
        w_qkv, w_out, rows, w_gu, w_down, gains, tables[0], tables[1],
        blocks[:, None], blocks[None, :], rows,
    )
    return dict(zip(places, results[:parts])), results[parts:]


def unit_kernel_call(rows_low, resid, cotangent, gain, pieces):
    grid = Grid()
    outer, chips, inner = grid.outer, grid.chips, grid.inner
    total_rows, width = rows_low.shape
    slab, units = pieces[0, 0].shape[1:]
    places = list(pieces)
    parts = len(places)
    last = (0, outer - 1)
    halves = 2
    count = total_rows // halves
    both = 2 * count
    per = min(2, chips)
    groups = chips // per
    blocks = outer * groups
    tall = per * both
    held = per if groups > 1 else max(per - 1, 1)
    links = outer * (chips - 1)
    steps = list(range(outer))
    far_first = [0] + steps[2:] + steps[1:2]

    def units_of(of_steps):
        return [(s, i) for s in of_steps for i in range(groups)]

    orders = {
        (0, 0): units_of(far_first),
        (0, 1): units_of(far_first),
        (1, 0): units_of(steps),
        (1, 1): units_of(far_first),
    }
    grad_order = units_of(far_first)
    tile = 512
    wide_tiles = width // tile
    unit_tile = min(256, units)
    lines = 32
    bf16, f32 = jnp.bfloat16, jnp.float32
    mesh_id = pl.DeviceIdType.MESH

    def plan():
        chip_us, core_us, hop_us = 5.6, 0.6, 2.0
        free = {"x": 0.0, "core": 0.0, "z near": 0.0, "z far": 0.0}
        arrive, done, tasks = {("w",): 20.0}, {}, {}

        def send(link, when, us):
            free[link] = max(free[link], when) + us
            return free[link] + hop_us

        def add(name, needs, us, after=None):
            tasks[name] = (needs, us, after)

        def send_outer(s, now):
            return send("z near", now, 8.0) if s == 1 else send("z far", now, 10.5)

        def go(p, h):
            def then(now):
                if (p, h) != (0, 1):
                    for s in steps[1:]:
                        arrive["z", p, h, s] = send_outer(s, now)
                for k in range(1, chips):
                    arrive["x", p, h, 0, k] = send("x", now, chip_us)
                arrive["c", p, h, 0, 0] = send("core", now, core_us)

            return then

        def zf(p, h, s):
            def then(now):
                for k in range(1, chips):
                    arrive["x", p, h, s, k] = send("x", now, chip_us)
                arrive["c", p, h, s, 0] = send("core", now, core_us)
                if (p, h) == (0, 0):
                    arrive["z", 0, 1, s] = send_outer(s, now)

            return then

        def xf(p, h, s, k):
            def then(now):
                arrive["c", p, h, s, k] = send("core", now, core_us)

            return then

        def compute(p, h, s, i):
            def then(now):
                arrive["cr", p, h, s, i] = send("core", now, per * core_us)

            return then

        def cr(p, h, s, i):
            def then(now):
                for k in range(i * per, i * per + per):
                    if k:
                        arrive["xr", p, h, s, k] = send("x", now, chip_us)

            return then

        def xr(p, h, s):
            def then(now):
                if s:
                    arrive["zr", p, h, s] = send_outer(s, now)

            return then

        for p in (0, 1):
            for h in range(halves):
                if p == 0:
                    needs = [("do", ("go", 0, h - 1))] if h else []
                else:
                    needs = [("do", ("between", h))]
                add(("go", p, h), needs, 0.2, go(p, h))
                for s in steps[1:]:
                    add(("zf", p, h, s), [("at", ("z", p, h, s))], 0.2, zf(p, h, s))
                for s in steps:
                    for k in range(1, chips):
                        add(("xf", p, h, s, k), [("at", ("x", p, h, s, k))], 0.2, xf(p, h, s, k))
                order = orders[p, h]
                for n, (s, i) in enumerate(order):
                    needs = [("at", ("c", p, h, s, i * per + j)) for j in range(per)]
                    if n:
                        needs.append(("do", ("front", p, h) + order[n - 1]))
                    add(("load", p, h, s, i), needs, 0.2)
                    needs = [("do", ("load", p, h, s, i)), ("do", ("weights",))]
                    add(("front", p, h, s, i), needs, (2.4, 1.6)[p])
                    needs = [("do", ("front", p, h, s, i))]
                    if n:
                        needs.append(("do", ("cr", p, h) + order[n - 1]))
                    add(("compute", p, h, s, i), needs, (1.6, 2.4)[p], compute(p, h, s, i))
                    needs = [("at", ("cr", p, h, s, i)), ("do", ("compute", p, h, s, i))]
                    add(("cr", p, h, s, i), needs, 0.5, cr(p, h, s, i))
                for s in steps:
                    needs = [("do", ("cr", p, h, s, 0))]
                    needs += [("at", ("xr", p, h, s, k)) for k in range(1, chips)]
                    add(("xr", p, h, s), needs, 0.4, xr(p, h, s))
                for s in steps[1:]:
                    needs = [("at", ("zr", p, h, s)), ("do", ("xr", p, h, 0))]
                    add(("zr", p, h, s), needs, 0.4)
        add(("weights",), [("at", ("w",))], 0.2)
        for h in range(halves):
            needs = [("do", ("zr", 0, h, s)) for s in steps[1:]] + [("do", ("xr", 0, h, 0))]
            add(("between", h), needs, 1.0)
        for n, (s, i) in enumerate(grad_order):
            needs = [("do", ("compute", 1, h, s, i)) for h in range(halves)]
            if n:
                needs.append(("do", ("grads",) + grad_order[n - 1] + (2,)))
            add(("fetch", s, i), needs, 0.2)
            for c in range(3):
                needs = [("do", ("grads", s, i, c - 1) if c else ("fetch", s, i))]
                add(("grads", s, i, c), needs, 2.8)
        written = [(j, s) for j in range(inner) for s in range(outer)]
        for n, at in enumerate(written):
            needs = [("do", ("grads",) + grad_order[-1] + (2,))]
            if n:
                needs = [("do", ("write",) + written[n - 1])]
            add(("write",) + at, needs, 0.6)
        rank = {"compute": 1, "front": 2, "fetch": 2, "grads": 3, "write": 4}
        result = []
        now = 0.0
        while tasks:
            best = None
            for name, (needs, us, then) in tasks.items():
                ready = 0.0
                for kind, key in needs:
                    table = arrive if kind == "at" else done
                    if key not in table:
                        ready = None
                        break
                    ready = max(ready, table[key] + (1.0 if key[0] in ("load", "fetch") else 0.0))
                if ready is None:
                    continue
                key = (max(ready, now), rank.get(name[0], 0))
                if best is None or key < best[0]:
                    best = (key, name)
            (ready, _), name = best
            needs, us, then = tasks.pop(name)
            now = ready + us
            done[name] = now
            if then is not None:
                then(now)
            result.append(name)
        return result

    def kernel(*refs):
        piece_refs = dict(zip(places, refs[:parts]))
        fixed = refs[parts : parts + 9]
        k = parts + 9
        late, grad_refs = refs[k : k + inner - 1], refs[k + inner - 1 : k + inner - 1 + 3 * inner]
        for j in range(1, inner):
            piece_refs[j, outer - 1] = late[j - 1]
        body(piece_refs, *fixed, grad_refs, *refs[k + inner - 1 + 3 * inner :])

    def body(
        piece_refs, rows_ref, resid_ref, cot_ref, gain_ref,
        out_ref, dres_ref, gain_out, all_x, all_dm, grad_refs,
        wg, wu, wd, buf, wide_buf, act, coef_gate, coef_up, d_gate, d_up, turned, acc_gate, acc_up, acc_down, stage, stage_down,
        core_send, core_land, hold, keep, chip_send, chip_land, outer_send, outer_land, raw, d_mlp,
        s_outer, r_outer, s_chip, r_chip, s_core, r_core,
        s_core_sum, r_core_sum, s_chip_sum, r_chip_sum, s_outer_sum, r_outer_sum,
        local, local_own, local_wide, local_w, local_g, s_late, r_late,
    ):
        g = Grid()
        core_peer = (g.dp_at, g.chip_at * 2 + 1 - g.core_at)

        def chip_peer(k):
            return (g.dp_at, lax.rem(g.chip_at + k + chips, chips) * 2 + g.core_at)

        def outer_peer(s):
            return (g.outer_flip(g.outer_at, s) * inner + g.inner_at, g.tensor_at)

        def inner_peer(j):
            return (g.outer_at * inner + lax.rem(g.inner_at + j, inner), g.tensor_at)

        greet(
            [core_peer]
            + [chip_peer(k) for k in range(1, chips)]
            + [outer_peer(s) for s in range(1, outer)]
            + [inner_peer(j) for j in range(1, inner)]
        )

        def remote(src, dst, send, recv, peer):
            copy = pltpu.make_async_remote_copy(
                src_ref=src, dst_ref=dst, send_sem=send, recv_sem=recv,
                device_id=peer, device_id_type=mesh_id,
            )
            copy.start()
            return copy

        def fetch(src, dst, sem):
            copy = pltpu.make_async_copy(src, dst, sem)
            copy.start()
            return copy

        def dot(a, b, contract):
            return lax.dot_general(a, b, (contract, ((), ())), preferred_element_type=f32)

        def looped(total, make):
            lax.fori_loop(0, total, lambda i, c: (make(i), c)[1], 0, unroll=total <= 4)

        def by_lines(make):
            looped(count // lines, lambda i: make(pl.ds(pl.multiple_of(i * lines, lines), lines)))

        def by_tiles(make):
            looped(wide_tiles, lambda i: make(pl.ds(pl.multiple_of(i * tile, tile), tile)))

        weights = (wg, wu, wd)
        fetches = []

        late_copies = []

        def send_late():
            for j in range(1, inner):
                late_copies.append(
                    remote(piece_refs[last], piece_refs[j, last[1]], s_late.at[j], r_late.at[j], inner_peer(j))
                )

        def fetch_weights(which):
            for j, s in which:
                index = g.outer_flip(g.outer_at, s) * inner
                index = index + lax.rem(g.inner_at - j + inner, inner)
                span = pl.ds(pl.multiple_of(index * slab, slab), slab)
                for c in range(3):
                    fetches.append(
                        fetch(piece_refs[j, s].at[c], weights[c].at[span], local_w.at[j * outer + s, c])
                    )

        mine, theirs = pl.ds(0, count), pl.ds(count, count)
        every = (all_x, all_dm)
        copies, sums, loads, own = {}, {}, {}, {}
        unsent = {(p, h): [] for p in (0, 1) for h in range(halves)}

        def track(p, h, copy):
            unsent[p, h].append(copy)
            return copy

        def core_copy(p, h, s, k, src):
            dst = every[p].at[h, s, k, theirs]
            copies["c", p, h, s, k] = track(
                p, h, remote(src, dst, s_core.at[p, h, s, k], r_core.at[p, h, s, k], core_peer)
            )

        def chip_copy(p, h, s, k, src):
            dst = every[p].at[h, s, k, mine]
            copies["x", p, h, s, k] = track(
                p, h, remote(src, dst, s_chip.at[p, h, s, k], r_chip.at[p, h, s, k], chip_peer(k))
            )

        def outer_copy(p, h, s):
            source = (rows_ref, d_mlp)[p].at[pl.ds(h * count, count)]
            dst = every[p].at[h, s, 0, mine]
            copies["z", p, h, s] = track(
                p, h, remote(source, dst, s_outer.at[p, h, s], r_outer.at[p, h, s], outer_peer(s))
            )

        def go(p, h):
            source = (rows_ref, d_mlp)[p].at[pl.ds(h * count, count)]
            if (p, h) != (0, 1):
                for s in steps[1:]:
                    outer_copy(p, h, s)
            for k in range(1, chips):
                chip_copy(p, h, 0, k, source)
            core_copy(p, h, 0, 0, source)
            own[p, h] = fetch(source, every[p].at[h, 0, 0, mine], local_own.at[p, h])
            if p == 0 and h == 0:
                fetch_weights(places)

        def part_out(h, s, i, cols, part_sum):
            for j in range(per):
                own_rows = part_sum[j * both : j * both + count]
                if i * per + j == 0:
                    keep[h, s, :, cols] = own_rows
                else:
                    hold[h, min(j, held - 1), :, cols] = own_rows
                core_send[h, j, :, cols] = part_sum[j * both + count : (j + 1) * both].astype(bf16)

        def forward(h, unit):
            for j in range(units // unit_tile):
                cols = pl.ds(j * unit_tile, unit_tile)
                rows = buf[h].reshape(tall, width)
                gate = dot(rows, wg[:, cols], ((1,), (0,)))
                up = dot(rows, wu[:, cols], ((1,), (0,)))
                sigma = jax.nn.sigmoid(gate)
                silu = gate * sigma
                act[unit, h, :, cols] = (silu * up).astype(bf16)
                coef_up[unit, h, :, cols] = silu.astype(bf16)
                coef_gate[unit, h, :, cols] = (
                    up * sigma * (1.0 + gate * (1.0 - sigma))
                ).astype(bf16)

        def forward_out(h, unit, s, i):
            by_tiles(
                lambda cols: part_out(h, s, i, cols, dot(act[unit, h], wd[cols, :], ((1,), (1,))))
            )

        def backward(h, unit):
            for j in range(units // unit_tile):
                cols = pl.ds(j * unit_tile, unit_tile)
                d_act = dot(buf[h].reshape(tall, width), wd[:, cols], ((1,), (0,)))
                d_gate[unit, h, :, cols] = (d_act * coef_gate[unit, h, :, cols].astype(f32)).astype(bf16)
                d_up[unit, h, :, cols] = (d_act * coef_up[unit, h, :, cols].astype(f32)).astype(bf16)

        def backward_out(h, unit, s, i):
            def into(cols):
                part_sum = dot(d_gate[unit, h], wg[cols, :], ((1,), (1,)))
                part_sum = part_sum + dot(d_up[unit, h], wu[cols, :], ((1,), (1,)))
                part_out(h, s, i, cols, part_sum)

            by_tiles(into)

        def weight_grads(unit, c):
            first = unit == grad_order[0][0] * groups + grad_order[0][1]
            left, right, acc = ((d_gate, 0, acc_gate), (d_up, 0, acc_up), (act, 1, acc_down))[c]
            turned[...] = left[unit].reshape(halves * tall, units).T

            def grads(cols):
                rows = wide_buf[right, :, :, :, cols].reshape(halves * tall, tile)
                value = dot(turned[...], rows, ((1,), (0,)))
                acc[:, cols] = value if first else acc[:, cols] + value

            by_tiles(grads)

        def between(h):
            def lines_of(i, total):
                at_rows = pl.ds(pl.multiple_of(h * count + i * lines, lines), lines)
                value = raw[at_rows]
                scale = lax.rsqrt(jnp.mean(value * value, axis=1, keepdims=True) + norm_eps)
                hat = value * scale
                gain_row = gain_ref[3:4]
                out_ref[at_rows] = (resid_ref[at_rows] + hat * gain_row).astype(bf16)
                top = cot_ref[at_rows].astype(f32)
                upstream = top * gain_row
                mean = jnp.mean(upstream * hat, axis=1, keepdims=True)
                d_mlp[at_rows] = (scale * (upstream - hat * mean)).astype(bf16)
                return total + jnp.sum(top * hat, axis=0, keepdims=True)

            zero = jnp.zeros((1, width), f32)
            total = lax.fori_loop(0, count // lines, lines_of, zero)
            gain_out[...] = total if h == 0 else gain_out[...] + total

        batches = []

        def write_grads(j, s):
            index = g.outer_flip(g.outer_at, s) * inner
            index = index + lax.rem(g.inner_at + j, inner)
            span = pl.ds(pl.multiple_of(index * slab, slab), slab)
            for copy in batches:
                copy.wait()
            batches.clear()
            for c, src in enumerate((stage.at[0], stage.at[1], stage_down)):
                if c == 0:
                    stage[0] = acc_gate[:, span].astype(bf16).T
                elif c == 1:
                    stage[1] = acc_up[:, span].astype(bf16).T
                else:
                    stage_down[...] = acc_down[:, span].astype(bf16)
                batches.append(fetch(src, grad_refs[j * 3 + c].at[s], local_g.at[c]))

        def core_sum(p, h, s, i):
            unit = s * groups + i
            sums["c", p, h, unit].wait_recv()
            for j in range(per):
                chip = i * per + j
                if chip == 0:

                    def add(at_rows):
                        keep[h, s, at_rows] = keep[h, s, at_rows] + core_land[h, unit, j, at_rows].astype(f32)

                    by_lines(add)
                    continue
                there = s * (chips - 1) + chip - 1

                def add(at_rows):
                    total = hold[h, min(j, held - 1), at_rows] + core_land[h, unit, j, at_rows].astype(f32)
                    chip_send[h, there, at_rows] = total.astype(bf16)

                by_lines(add)
                sums["x", p, h, s, chip] = track(
                    p, h,
                    remote(
                        chip_send.at[h, there], chip_land.at[h, there],
                        s_chip_sum.at[p, h, there], r_chip_sum.at[p, h, there], chip_peer(-chip),
                    ),
                )

        def chip_sum(p, h, s):
            for k in range(1, chips):
                sums["x", p, h, s, k].wait_recv()

            def add(at_rows):
                total = keep[h, s, at_rows]
                for k in range(1, chips):
                    total = total + chip_land[h, s * (chips - 1) + k - 1, at_rows].astype(f32)
                if s == 0:
                    raw[pl.ds(pl.multiple_of(h * count + at_rows.start, lines), lines)] = total
                else:
                    outer_send[h, s - 1, at_rows] = total.astype(bf16)

            by_lines(add)
            if s:
                sums["z", p, h, s] = track(
                    p, h,
                    remote(
                        outer_send.at[h, s - 1], outer_land.at[h, s - 1],
                        s_outer_sum.at[p, h, s], r_outer_sum.at[p, h, s], outer_peer(s),
                    ),
                )

        def outer_sum(p, h, s):
            sums["z", p, h, s].wait_recv()

            def add(at_rows):
                there = pl.ds(pl.multiple_of(h * count + at_rows.start, lines), lines)
                raw[there] = raw[there] + outer_land[h, s - 1, at_rows].astype(f32)

            by_lines(add)

        def all_sent(p, h):
            for copy in unsent[p, h]:
                copy.wait_send()

        last_core = {}
        send_late()
        for task in plan():
            name, args = task[0], task[1:]
            if name == "go":
                go(*args)
            elif name == "zf":
                p, h, s = args
                copies["z", p, h, s].wait_recv()
                source = every[p].at[h, s, 0, mine]
                for k in range(1, chips):
                    chip_copy(p, h, s, k, source)
                core_copy(p, h, s, 0, source)
                if (p, h) == (0, 0):
                    outer_copy(0, 1, s)
            elif name == "xf":
                p, h, s, k = args
                copies["x", p, h, s, k].wait_recv()
                core_copy(p, h, s, k, every[p].at[h, s, k, mine])
            elif name == "load":
                p, h, s, i = args
                for j in range(per):
                    copies["c", p, h, s, i * per + j].wait_recv()
                if (s, i) == (0, 0):
                    own[p, h].wait()
                src = every[p].at[h, s, pl.ds(i * per, per)]
                loads[args] = fetch(src, buf.at[h], local.at[p, h, s * groups + i])
            elif name == "weights":
                for copy in late_copies:
                    copy.wait_recv()
                fetch_weights([(j, last[1]) for j in range(1, inner)])
            elif name == "front":
                p, h, s, i = args
                if p == 0 and not loads.get("weights"):
                    loads["weights"] = True
                    for copy in fetches:
                        copy.wait()
                loads[args].wait()
                (forward, backward)[p](h, s * groups + i)
            elif name == "compute":
                p, h, s, i = args
                unit = s * groups + i
                if h in last_core:
                    last_core[h].wait_send()
                (forward_out, backward_out)[p](h, unit, s, i)
                last_core[h] = remote(
                    core_send.at[h], core_land.at[h, unit],
                    s_core_sum.at[p, h, unit], r_core_sum.at[p, h, unit], core_peer,
                )
                sums["c", p, h, unit] = last_core[h]
            elif name == "cr":
                core_sum(*args)
            elif name == "xr":
                chip_sum(*args)
            elif name == "zr":
                outer_sum(*args)
            elif name == "between":
                all_sent(0, args[0])
                between(args[0])
            elif name == "fetch":
                s, i = args
                loads[task] = []
                for at, src in enumerate((all_x, all_dm)):
                    for h in range(halves):
                        loads[task].append(
                            fetch(
                                src.at[h, s, pl.ds(i * per, per)],
                                wide_buf.at[at, h],
                                local_wide.at[s * groups + i, at * halves + h],
                            )
                        )
            elif name == "grads":
                s, i, c = args
                if c == 0:
                    for copy in loads["fetch", s, i]:
                        copy.wait()
                weight_grads(s * groups + i, c)
            elif name == "write":
                write_grads(*args)

        looped(
            total_rows // lines,
            lambda i: close_rows(pl.ds(pl.multiple_of(i * lines, lines), lines), dres_ref, raw, cot_ref),
        )
        for h in range(halves):
            all_sent(1, h)
            last_core[h].wait_send()
        for copy in batches:
            copy.wait()
        for copy in late_copies:
            copy.wait_send()

    shape = jax.ShapeDtypeStruct
    anywhere = pl.BlockSpec(memory_space=pl.ANY)
    near = pl.BlockSpec(memory_space=pltpu.VMEM)
    sems = pltpu.SemaphoreType.DMA
    flops = 2 * 9 * halves * tall * blocks * width * units
    results = pl.pallas_call(
        kernel,
        out_shape=(
            shape((total_rows, width), bf16),
            shape((total_rows, width), f32),
            shape((1, width), f32),
            shape((halves, outer, chips, both, width), bf16),
            shape((halves, outer, chips, both, width), bf16),
        )
        + (shape((3, slab, units), bf16),) * (inner - 1)
        + (
            shape((outer, slab, units), bf16),
            shape((outer, slab, units), bf16),
            shape((outer, units, slab), bf16),
        )
        * inner,
        in_specs=[anywhere] * (parts + 1) + [near] * 3,
        out_specs=(near, near, near) + (anywhere,) * (2 + inner - 1 + 3 * inner),
        scratch_shapes=[
            pltpu.VMEM((width, units), bf16),
            pltpu.VMEM((width, units), bf16),
            pltpu.VMEM((width, units), bf16),
            pltpu.VMEM((halves, per, both, width), bf16),
            pltpu.VMEM((2, halves, per, both, width), bf16),
            pltpu.VMEM((blocks, halves, tall, units), bf16),
            pltpu.VMEM((blocks, halves, tall, units), bf16),
            pltpu.VMEM((blocks, halves, tall, units), bf16),
            pltpu.VMEM((blocks, halves, tall, units), bf16),
            pltpu.VMEM((blocks, halves, tall, units), bf16),
            pltpu.VMEM((units, halves * tall), bf16),
            pltpu.VMEM((units, width), f32),
            pltpu.VMEM((units, width), f32),
            pltpu.VMEM((units, width), f32),
            pltpu.VMEM((2, slab, units), bf16),
            pltpu.VMEM((units, slab), bf16),
            pltpu.VMEM((halves, per, count, width), bf16),
            pltpu.VMEM((halves, blocks, per, count, width), bf16),
            pltpu.VMEM((halves, held, count, width), f32),
            pltpu.VMEM((halves, outer, count, width), f32),
            pltpu.VMEM((halves, links, count, width), bf16),
            pltpu.VMEM((halves, links, count, width), bf16),
            pltpu.VMEM((halves, outer - 1, count, width), bf16),
            pltpu.VMEM((halves, outer - 1, count, width), bf16),
            pltpu.VMEM((total_rows, width), f32),
            pltpu.VMEM((total_rows, width), bf16),
            sems((2, halves, outer)),
            sems((2, halves, outer)),
            sems((2, halves, outer, chips)),
            sems((2, halves, outer, chips)),
            sems((2, halves, outer, chips)),
            sems((2, halves, outer, chips)),
            sems((2, halves, blocks)),
            sems((2, halves, blocks)),
            sems((2, halves, links)),
            sems((2, halves, links)),
            sems((2, halves, outer)),
            sems((2, halves, outer)),
            sems((2, halves, blocks)),
            sems((2, halves)),
            sems((blocks, 2 * halves)),
            sems((inner * outer, 3)),
            sems((3,)),
            sems((inner,)),
            sems((inner,)),
        ],
        compiler_params=pltpu.CompilerParams(
            collective_id=2, has_side_effects=True, vmem_limit_bytes=62 * 2**20
        ),
        cost_estimate=pl.CostEstimate(flops=flops, bytes_accessed=64 * 2**20, transcendentals=0),
    )(*pieces.values(), rows_low, resid, cotangent, gain)
    grads = results[5 + inner - 1 :]
    return results[:3] + ([[grads[j * 3 + c] for j in range(inner)] for c in range(3)],)


def close_rows(at_rows, dres_ref, raw, cot_ref):
    dres_ref[at_rows] = raw[at_rows] + cot_ref[at_rows].astype(jnp.float32)


def local(
    tokens,
    cotangent,
    block_ids,
    w_qkv,
    m_qkv,
    v_qkv,
    w_out,
    m_out,
    v_out,
    w_gu,
    m_gu,
    v_gu,
    w_down,
    m_down,
    v_down,
    gains,
    gain_m,
    gain_v,
):
    grid = Grid()
    local_x = tokens[0]
    gain_count = gains.shape[0]
    tables = rope_tables(local_x.shape[0] * grid.tensor, HEAD)
    pieces, kept = open_call(
        w_qkv,
        w_out,
        gains,
        local_x,
        w_gu,
        w_down,
        tables,
        block_ids[0],
    )
    full_qkv, full_out, seq_x, gain_rows = kept[:4]
    hats, scales, q_low, k_low, v_low, log_total, context_low = kept[4:11]
    attn_hat, o_scale, resid, resid_low, tops = kept[11:]
    output, d_resid, gain_last, unit_grads = unit_kernel_call(
        resid_low, resid, cotangent[0], gain_rows, pieces
    )
    part_gu, part_down, part_qkv, part_out, part_gains, tops, grad_tokens = attend_back_call(
        d_resid,
        attn_hat,
        o_scale,
        gain_rows,
        full_out,
        context_low,
        q_low,
        k_low,
        v_low,
        log_total,
        hats,
        scales,
        tables,
        block_ids[0],
        seq_x,
        full_qkv,
        gain_last,
        tops,
        unit_grads,
    )
    part_gains = part_gains[:gain_count]
    head_top = tops[: w_qkv.shape[2] // HEAD, 0]
    factor = clip_tau / jnp.maximum(head_top, clip_tau)
    column = jnp.repeat(jnp.sqrt(factor), HEAD)
    column_scale = jnp.stack([column, column, jnp.ones_like(column)])[:, None, :]
    new_qkv, new_m_qkv, new_v_qkv = adam_step(
        w_qkv, part_qkv, m_qkv, v_qkv, rate_matrix, weight_decay
    )
    new_qkv = new_qkv * column_scale
    new_out, new_m_out, new_v_out = adam_step(
        w_out, part_out, m_out, v_out, rate_matrix, weight_decay
    )
    new_gu, new_m_gu, new_v_gu = adam_step(
        w_gu, part_gu.astype(jnp.float32), m_gu, v_gu, rate_matrix, weight_decay
    )
    new_down, new_m_down, new_v_down = adam_step(
        w_down, part_down.astype(jnp.float32), m_down, v_down, rate_matrix, weight_decay
    )
    new_gains, new_gain_m, new_gain_v = adam_step(gains, part_gains, gain_m, gain_v, rate_gain, 0.0)
    return (
        output[None],
        grad_tokens[None],
        new_qkv,
        new_m_qkv,
        new_v_qkv,
        new_qkv.astype(jnp.bfloat16),
        new_out,
        new_m_out,
        new_v_out,
        new_out.astype(jnp.bfloat16),
        new_gu,
        new_m_gu,
        new_v_gu,
        new_gu.astype(jnp.bfloat16),
        new_down,
        new_m_down,
        new_v_down,
        new_down.astype(jnp.bfloat16),
        new_gains,
        new_gain_m,
        new_gain_v,
        factor,
    )


def solution(mesh):
    return jax.shard_map(
        local,
        mesh=mesh,
        in_specs=(
            P("dp", "tensor", None),
            P("dp", "tensor", None),
            P("dp", None),
            P(None, "dp", "tensor"),
            P(None, "dp", "tensor"),
            P(None, "dp", "tensor"),
            P("tensor", "dp"),
            P("tensor", "dp"),
            P("tensor", "dp"),
            P(None, "dp", "tensor"),
            P(None, "dp", "tensor"),
            P(None, "dp", "tensor"),
            P("tensor", "dp"),
            P("tensor", "dp"),
            P("tensor", "dp"),
            P(None, "dp"),
            P(None, "dp"),
            P(None, "dp"),
        ),
        out_specs=(
            P("dp", "tensor", None),
            P("dp", "tensor", None),
            P(None, "dp", "tensor"),
            P(None, "dp", "tensor"),
            P(None, "dp", "tensor"),
            P(None, "dp", "tensor"),
            P("tensor", "dp"),
            P("tensor", "dp"),
            P("tensor", "dp"),
            P("tensor", "dp"),
            P(None, "dp", "tensor"),
            P(None, "dp", "tensor"),
            P(None, "dp", "tensor"),
            P(None, "dp", "tensor"),
            P("tensor", "dp"),
            P("tensor", "dp"),
            P("tensor", "dp"),
            P("tensor", "dp"),
            P(None, "dp"),
            P(None, "dp"),
            P(None, "dp"),
            P("tensor"),
        ),
        check_vma=False,
    )
```

```python
import jax
import jax.numpy as jnp
import numpy as np
from jax import lax
from jax.experimental import pallas as pl
from jax.experimental.pallas import tpu as pltpu
from jax.sharding import PartitionSpec as P

HEAD = 128
STEP = 5


norm_eps = 1e-06
rope_base = 500000.0
beta_one = 0.9
beta_two = 0.95
rate_matrix = 0.01
rate_gain = 0.6
weight_decay = 0.1
adam_eps = 1e-08
clip_tau = 9.0
masked_value = -1e30


def rope_tables(length, size):
    half = size // 2
    freq = np.float32(rope_base) ** (-(np.arange(half, dtype=np.float32) * np.float32(2.0 / size)))
    angle = np.arange(length, dtype=np.float32)[:, None] * freq[None, :]
    angle = np.concatenate([angle, angle], axis=1)
    return (jnp.asarray(np.cos(angle)), jnp.asarray(np.sin(angle)))


def adam_step(param, grad, first, second, rate, decay):
    first = beta_one * first + (1.0 - beta_one) * grad
    second = beta_two * second + (1.0 - beta_two) * grad * grad
    fix_one = 1.0 - beta_one**STEP
    fix_two = 1.0 - beta_two**STEP
    update = first / fix_one / (jnp.sqrt(second / fix_two) + adam_eps)
    return (param - rate * (update + decay * param), first, second)


class Grid:
    def __init__(self):
        self.dp = lax.axis_size("dp")
        self.tensor = lax.axis_size("tensor")
        self.inner = 1
        while self.inner * self.inner * 4 <= self.dp:
            self.inner *= 2
        self.outer = self.dp // self.inner
        self.chips = self.tensor // 2
        self.dp_at = lax.axis_index("dp")
        self.tensor_at = lax.axis_index("tensor")
        self.inner_at = self.dp_at % self.inner
        self.chip_at = self.tensor_at // 2
        self.core_at = self.tensor_at % 2
        self.outer_at = self.dp_at // self.inner

    def path_of(self, index):
        column, row = index // self.inner, index % self.inner
        return row * self.outer + column + (row % 2) * (self.outer - 1 - 2 * column)

    def outer_flip(self, index, step):
        result = 0
        for bit in bits(self.outer):
            side = index // bit % 2
            result = result + bit * (1 - side if step & bit else side)
        return result

    def index_of(self, place):
        row, column = place // self.outer, place % self.outer
        return (column + (row % 2) * (self.outer - 1 - 2 * column)) * self.inner + row


def bits(count):
    return [1 << k for k in range(count.bit_length() - 1)]


def greet(peers):
    barrier = pltpu.get_barrier_semaphore()
    for peer in peers:
        pl.semaphore_signal(barrier, inc=1, device_id=peer, device_id_type=pl.DeviceIdType.MESH)
    pl.semaphore_wait(barrier, len(peers))


def attend_back_call(
    d_resid, attn_hat, o_scale, gain_rows, full_out, context, q_low, k_low, v_low, lse, hats, scales,
    tables, blocks, seq, full_qkv, gain_last, tops, unit_grads,
):
    grid = Grid()
    n, outer, inner, chips, tensor = grid.dp, grid.outer, grid.inner, grid.chips, grid.tensor
    count, width = d_resid.shape
    length, span = context.shape
    heads = span // HEAD
    slab, units = unit_grads[0][0].shape[1:]
    thin = width // n
    half = span // 2
    tall = min(256, length)
    tile = 512
    lines = 32
    ring = 8 + 2
    gain_item, top_item = 8, 9
    bf16, f32 = jnp.bfloat16, jnp.float32
    mesh_id = pl.DeviceIdType.MESH
    flat_grads = [unit_grads[c][j] for j in range(inner) for c in range(3)]
    some = len(flat_grads)
    z_steps = list(range(1, outer))

    def kernel(*refs):
        fixed, far_in, grads_in = refs[:16], refs[16:19], refs[19 : 19 + some]
        rest = refs[19 + some :]
        body(*fixed, far_in, grads_in, *rest)

    def body(
        dres_ref, hat_ref, o_scale_ref, gain_ref, out_w, ctx, q_ref, k_ref, v_ref, lse_ref, scale_ref,
        cos_ref, sin_ref, id_row, last_ref, tops_ref, far_in, grads_in,
        gu_out, down_out, part_ref, part_out, gains_out, tops_out, tokens_out,
        hats, seq, qkv_w, seq_do, d_ctx, d_q, d_k, d_v, d_low, probs_low, id_col, whole, terms, row_terms, turned,
        land, land_gain, land_top, own_gain, peer_gain, inners, peer_inners,
        gu_land, gu_sum, down_land, down_sum, core_send, core_land, hold, chip_send, chip_land,
        s_ring, r_ring, s_row, r_row, s_in, r_in, s_y, r_y, s_z, r_z, s_core, r_core, s_chip, r_chip, s_gain, r_gain, local,
    ):
        hats_in, seq_in, qkv_in = far_in
        g = Grid()

        def tensor_peer(k, flip):
            core = 1 - g.core_at if flip else g.core_at
            return (g.dp_at, lax.rem(g.chip_at + k + chips, chips) * 2 + core)

        def dp_peer(s, j):
            across = g.outer_flip(g.outer_at, s) * inner
            return (across + lax.rem(g.inner_at + j + inner, inner), g.tensor_at)

        place = g.path_of(g.dp_at)
        after_dp = (g.index_of(lax.rem(place + 1, n)), g.tensor_at)
        before_dp = (g.index_of(lax.rem(place + n - 1, n)), g.tensor_at)
        near = [tensor_peer(k, f) for k in range(chips) for f in (0, 1) if (k, f) != (0, 0)]
        far = [dp_peer(s, 0) for s in range(1, outer)] + [dp_peer(0, j) for j in range(1, inner)]
        greet(near + far + [after_dp, before_dp])

        def remote(src, dst, send, recv, peer):
            copy = pltpu.make_async_remote_copy(
                src_ref=src, dst_ref=dst, send_sem=send, recv_sem=recv,
                device_id=peer, device_id_type=mesh_id,
            )
            copy.start()
            return copy

        def fetch(src, dst, at):
            copy = pltpu.make_async_copy(src, dst, local.at[at])
            copy.start()
            return copy

        def dot(a, b, contract):
            return lax.dot_general(a, b, (contract, ((), ())), preferred_element_type=f32)

        def looped(total, make):
            lax.fori_loop(0, total, lambda i, c: (make(i), c)[1], 0, unroll=total <= 4)

        def rows_of(i, size):
            return pl.ds(pl.multiple_of(i * size, size), size)

        sent = []
        y_copies = {}
        sum_steps = [(c, s) for c in range(3) for s in z_steps + [0]]
        for c, s in sum_steps:
            for j in range(1, inner):
                copy = remote(
                    grads_in[j * 3 + c].at[s],
                    down_land.at[j - 1, s] if c == 2 else gu_land.at[j - 1, c, s],
                    s_y.at[j, c, s],
                    r_y.at[j, c, s],
                    dp_peer(0, j),
                )
                y_copies[j, c, s] = copy
                sent.append(copy)
        own_refs = (gu_sum.at[0], gu_sum.at[1], down_sum)
        own_grads = [fetch(grads_in[c], own_refs[c], c) for c in range(3)]
        fetched = [fetch(hats_in, hats, 3), fetch(seq_in, seq, 4), fetch(qkv_in, qkv_w, 5)]
        z_copies = []
        keeps = []

        def unit_sums(times):
            for _ in range(times):
                if sum_steps:
                    unit_sum(*sum_steps.pop(0))

        def unit_sum(c, s):
            if s == (z_steps + [0])[0]:
                own_grads[c].wait()
            for j in range(1, inner):
                y_copies[j, c, s].wait_recv()

            def add_gu(i):
                rows = rows_of(i, 64)
                total = gu_sum[c, s, rows].astype(f32)
                for j in range(1, inner):
                    total = total + gu_land[j - 1, c, s, rows].astype(f32)
                gu_sum[c, s, rows] = total.astype(bf16)

            def add_down(i):
                rows = rows_of(i, 64)
                total = down_sum[s, rows].astype(f32)
                for j in range(1, inner):
                    total = total + down_land[j - 1, s, rows].astype(f32)
                down_sum[s, rows] = total.astype(bf16)

            there = rows_of(g.outer_at, units)
            if c == 2:
                looped(units // 64, add_down)
                src, dst = down_sum.at[s], down_out.at[there]
            else:
                looped(slab // 64, add_gu)
                src, dst = gu_sum.at[c, s], gu_out.at[c, :, there]
            if s:
                z_copies.append(remote(src, dst, s_z.at[c, s], r_z.at[c, s], dp_peer(s, 0)))
            else:
                keeps.append(fetch(src, dst, 6 + c))

        def way_of(item):
            return 1 if item >= 8 else 1 - 2 * (item // 4)

        def own(item, away):
            index = g.index_of(lax.rem(place - way_of(item) * away + 2 * n, n))
            if item == gain_item:
                return terms.at[index]
            if item == top_item:
                return tops_ref
            side, c = item // 4, item % 4
            return whole.at[c, pl.ds(side * half, half), rows_of(index, thin)]

        def landed(step, item):
            if item == gain_item:
                return land_gain.at[step]
            if item == top_item:
                return land_top.at[step]
            return land.at[step, item]

        hops = {}
        on_path = {}

        def hop(step, item):
            hops[step, item] = remote(
                own(item, 1) if step == 0 else landed(step - 1, item),
                landed(step, item),
                s_ring.at[step, item],
                r_ring.at[step, item],
                after_dp if way_of(item) == 1 else before_dp,
            )

        def depart(*items):
            for item in items:
                on_path[item] = 0
                hop(0, item)

        def advance(*items):
            for item in items:
                step = on_path.get(item, n) + 1
                if step >= n:
                    continue
                on_path[item] = step
                hops[step - 1, item].wait_recv()
                here = landed(step - 1, item)
                if item == top_item:
                    summed = jnp.maximum(here[...], tops_ref[...])
                else:
                    summed = here[...].astype(f32) + own(item, step + 1)[...].astype(f32)
                if step < n - 1:
                    here[...] = summed.astype(here.dtype)
                    hop(step, item)
                elif item == gain_item:
                    own_gain[0] = summed
                elif item == top_item:
                    tops_out[...] = summed
                else:
                    side, c = item // 4, item % 4
                    span_half = pl.ds(side * half, half)
                    if c == 3:
                        part_out[span_half] = summed
                    else:
                        part_ref[c, :, span_half] = summed.T

        def matrix_grad(c, left, right):
            turned[...] = left.T

            def columns(i):
                cols = rows_of(i, tile)
                whole[c, :, cols] = dot(turned[...], right[:, cols], ((1,), (0,))).astype(bf16)

            looped(width // tile, columns)

        t_at = g.tensor_at
        mine = rows_of(t_at, count)

        def open_rows(i, total):
            at = rows_of(i, lines)
            value, hat = dres_ref[at], hat_ref[at]
            upstream = value * gain_ref[2:3]
            mean = jnp.mean(upstream * hat, axis=1, keepdims=True)
            d_attn = (o_scale_ref[at] * (upstream - hat * mean)).astype(bf16)
            seq_do[pl.ds(pl.multiple_of(t_at * count + i * lines, lines), lines)] = d_attn
            return total + jnp.sum(value * hat, axis=0, keepdims=True)

        gain_attn = lax.fori_loop(0, count // lines, open_rows, jnp.zeros((1, width), f32))
        row_terms[...] = jnp.zeros((8, width), f32)
        row_terms[2:3] = gain_attn
        row_terms[3:4] = last_ref[...]
        moves, passed = [], []

        def row_copy(slot, index, peer):
            at = rows_of(index, count)
            copy = remote(seq_do.at[at], seq_do.at[at], s_row.at[slot], r_row.at[slot], peer)
            sent.append(copy)
            return copy

        for k in range(1, chips):
            moves.append(row_copy(k - 1, t_at, tensor_peer(k, 0)))
        to_core = row_copy(chips - 1, t_at, tensor_peer(0, 1))
        id_col[...] = jnp.broadcast_to(id_row[...], (128, length)).T
        unit_sums(1)
        scale = HEAD ** (-0.5)
        for h in range(heads):
            cols = slice(h * HEAD, (h + 1) * HEAD)

            def weigh(i, c, cols=cols, h=h):
                at = rows_of(i, tall)
                raw = dot(q_ref[at, cols], k_ref[:, cols], ((1,), (1,))) * scale
                masked = jnp.where(id_row[...] <= id_col[at, 0:1], raw, masked_value)
                probs_low[h, at] = jnp.exp(masked - lse_ref[at, h : h + 1]).astype(bf16)
                return c

            lax.fori_loop(0, length // tall, weigh, 0, unroll=length // tall <= 4)
            if 2 * (h + 1) == heads:
                unit_sums(1)
        for k in range(1, chips):
            moves[k - 1].wait_recv()
            source = lax.rem(g.chip_at - k + chips, chips) * 2 + g.core_at
            passed.append(row_copy(chips - 1 + k, source, tensor_peer(0, 1)))
        to_core.wait_recv()
        unit_sums(1)
        for copy in passed:
            copy.wait_recv()

        def context_grad(i):
            at = rows_of(i, tall)
            d_ctx[at] = dot(seq_do[at], out_w[...], ((1,), (1,))).astype(bf16)

        looped(length // tall, context_grad)
        unit_sums(1)

        for h in range(heads):
            cols = slice(h * HEAD, (h + 1) * HEAD)

            def head(i, c, cols=cols, h=h):
                at = rows_of(i, tall)
                q_part, ctx_part = q_ref[at, cols], d_ctx[at, cols]
                probs_part = probs_low[h, at]
                probs = probs_part.astype(f32)
                d_probs = dot(ctx_part, v_ref[:, cols], ((1,), (1,)))
                mean = jnp.sum(probs * d_probs, axis=1, keepdims=True)
                d_scores = (probs * (d_probs - mean)).astype(bf16)
                d_q[at, cols] = dot(d_scores, k_ref[:, cols], ((1,), (0,))) * scale
                key = dot(d_scores, q_part, ((0,), (0,))) * scale
                value = dot(probs_part, ctx_part, ((0,), (0,)))
                d_k[:, cols] = jnp.where(i == 0, key, d_k[:, cols] + key)
                d_v[:, cols] = jnp.where(i == 0, value, d_v[:, cols] + value)
                return c

            d_k[:, cols] = jnp.zeros((length, HEAD), f32)
            d_v[:, cols] = jnp.zeros((length, HEAD), f32)
            lax.fori_loop(0, length // tall, head, 0, unroll=length // tall <= 4)
            unit_sums(1)
        fetched[0].wait()
        sign = jnp.where(lax.broadcasted_iota(jnp.int32, (tall, HEAD), 1) < HEAD // 2, -1.0, 1.0)

        def unrotate(i, sums):
            at = rows_of(i, tall)
            cosine, sine = cos_ref[at], sin_ref[at]
            lane = lax.broadcasted_iota(jnp.int32, (tall, 128), 1)
            columns = jnp.zeros((tall, 128), f32)
            result = []
            for c, grad in ((0, d_q), (1, d_k)):
                total = jnp.zeros((tall, 1), f32)
                terms_row = []
                for h in range(heads):
                    cols = slice(h * HEAD, (h + 1) * HEAD)
                    value = grad[at, cols]
                    back = value * cosine - pltpu.roll(value * sine, HEAD // 2, 1) * sign
                    hat = hats[c, at, cols]
                    terms_row.append(jnp.sum(back * hat, axis=0, keepdims=True))
                    at_head = pl.ds(pl.multiple_of(t_at * span + h * HEAD, HEAD), HEAD)
                    back = back * gain_ref[c : c + 1, at_head]
                    grad[at, cols] = back
                    total = total + jnp.sum(back * hat, axis=1, keepdims=True)
                columns = jnp.where(lane == c, total, columns)
                result.append(sums[c] + jnp.concatenate(terms_row, axis=1))
            inners[:, at] = columns.T[:8]
            return tuple(result)

        zero = jnp.zeros((1, span), f32)
        gain_q, gain_k = lax.fori_loop(0, length // tall, unrotate, (zero, zero))
        offset = rows_of(t_at, span)
        row_terms[0:1, offset] = gain_q
        row_terms[1:2, offset] = gain_k
        in_copies = []
        for k in range(chips):
            for f in (0, 1):
                if (k, f) != (0, 0):
                    at = k * 2 + f - 1
                    in_copies.append(
                        remote(inners, peer_inners.at[at], s_in.at[at], r_in.at[at], tensor_peer(k, f))
                    )
        sent.extend(in_copies)
        matrix_grad(3, ctx[...], seq_do)
        depart(3, 7)
        for copy in in_copies:
            copy.wait_recv()
        unit_sums(1)

        def normed(i):
            at = rows_of(i, tall)
            sums = inners[:, at]
            for other in range(tensor - 1):
                sums = sums + peer_inners[other, :, at]
            column = jnp.concatenate([sums, jnp.zeros((120, tall), f32)], axis=0).T / width
            for c, grad in ((0, d_q), (1, d_k)):
                value = grad[at] - hats[c, at] * column[:, c : c + 1]
                d_low[c, at] = (scale_ref[at, c : c + 1] * value).astype(bf16)
            d_low[2, at] = d_v[at].astype(bf16)

        looped(length // tall, normed)
        fetched[1].wait()
        for c in (2, 0, 1):
            matrix_grad(c, d_low[c], seq)
            depart(c, c + 4)
            unit_sums(1)

        def place_terms(i, c):
            cols = pl.ds(pl.multiple_of(i * thin, thin), thin)
            terms[i] = row_terms[:, cols]
            return c

        lax.fori_loop(0, n, place_terms, 0)

        depart(gain_item, top_item)
        unit_sums(len(sum_steps))

        fetched[2].wait()
        chip_order = list(range(1, chips)) + [0]
        core_copies, chip_copies = {}, {}

        def token_rows(k, flip, store):
            chip = lax.rem(g.chip_at + k, chips)
            core = 1 - g.core_at if flip else g.core_at
            at = rows_of(chip * 2 + core, count)

            def columns(i):
                cols = rows_of(i, tile)
                total = dot(d_low[0, at], qkv_w[0, cols], ((1,), (1,)))
                for c in (1, 2):
                    total = total + dot(d_low[c, at], qkv_w[c, cols], ((1,), (1,)))
                store(cols, total)

            looped(width // tile, columns)

        duties = []
        for k in chip_order:

            def away(k=k):
                def store(cols, value):
                    core_send[k, :, cols] = value.astype(bf16)

                token_rows(k, True, store)
                core_copies[k] = remote(
                    core_send.at[k], core_land.at[k], s_core.at[k], r_core.at[k], tensor_peer(0, 1)
                )

            def here(k=k):
                def store(cols, value):
                    hold[k, :, cols] = value

                token_rows(k, False, store)

            def join(k=k):
                core_copies[k].wait_recv()

                def add(i):
                    at = rows_of(i, lines)
                    chip_send[k - 1, at] = (hold[k, at] + core_land[k, at].astype(f32)).astype(bf16)

                looped(count // lines, add)
                chip_copies[k] = remote(
                    chip_send.at[k - 1], chip_land.at[k - 1], s_chip.at[k], r_chip.at[k], tensor_peer(k, 0)
                )

            duties += [away, here] + ([join] if k else [])

        def close_tokens():
            core_copies[0].wait_recv()
            for k in range(1, chips):
                chip_copies[k].wait_recv()

            def close(i):
                at = rows_of(i, lines)
                total = dres_ref[at] + hold[0, at] + core_land[0, at].astype(f32)
                for k in range(1, chips):
                    total = total + chip_land[k - 1, at].astype(f32)
                tokens_out[at] = total

            looped(count // lines, close)

        duties.append(close_tokens)
        per_step = -(-len(duties) // (n - 2))
        for step in range(1, n):
            advance(3, 7, 2, 6, 0, 4, 1, 5, gain_item, top_item)
            for _ in range(per_step):
                if duties:
                    duties.pop(0)()
        peers = [tensor_peer(0, 1)] + [tensor_peer(k, 0) for k in range(1, chips)]
        first = remote(own_gain.at[0], peer_gain.at[0], s_gain.at[0], r_gain.at[0], peers[0])
        first.wait_recv()
        own_gain[1] = own_gain[0] + peer_gain[0]
        others = [
            remote(own_gain.at[1], peer_gain.at[k], s_gain.at[k], r_gain.at[k], peers[k])
            for k in range(1, chips)
        ]
        result = own_gain[1]
        for k in range(1, chips):
            others[k - 1].wait_recv()
            result = result + peer_gain[k]
        gains_out[...] = result
        for copy in z_copies:
            copy.wait()
        for copy in keeps:
            copy.wait()
        for copy in sent + list(hops.values()) + list(core_copies.values()):
            copy.wait_send()
        for copy in list(chip_copies.values()) + [first] + others:
            copy.wait_send()

    shape = jax.ShapeDtypeStruct
    anywhere = pl.BlockSpec(memory_space=pl.ANY)
    vmem = pl.BlockSpec(memory_space=pltpu.VMEM)
    sems = pltpu.SemaphoreType.DMA
    results = pl.pallas_call(
        kernel,
        out_shape=(
            shape((2, slab, outer * units), bf16),
            shape((outer * units, slab), bf16),
            shape((3, thin, span), f32),
            shape((span, thin), f32),
            shape((8, thin), f32),
            shape(tops.shape, f32),
            shape((count, width), f32),
        ),
        in_specs=[vmem] * 16 + [anywhere] * 3 + [anywhere] * some,
        out_specs=(anywhere,) * 2 + (vmem,) * 5,
        scratch_shapes=[
            pltpu.VMEM(hats.shape, f32),
            pltpu.VMEM(seq.shape, bf16),
            pltpu.VMEM(full_qkv.shape, bf16),
            pltpu.VMEM((length, width), bf16),
            pltpu.VMEM((length, span), bf16),
            pltpu.VMEM((length, span), f32),
            pltpu.VMEM((length, span), f32),
            pltpu.VMEM((length, span), f32),
            pltpu.VMEM((3, length, span), bf16),
            pltpu.VMEM((heads, length, length), bf16),
            pltpu.VMEM((length, 128), jnp.int32),
            pltpu.VMEM((4, span, width), bf16),
            pltpu.VMEM((n, 8, thin), f32),
            pltpu.VMEM((8, width), f32),
            pltpu.VMEM((span, length), bf16),
            pltpu.VMEM((n - 1, 8, half, thin), bf16),
            pltpu.VMEM((n - 1, 8, thin), f32),
            pltpu.VMEM((n - 1,) + tops.shape, f32),
            pltpu.VMEM((2, 8, thin), f32),
            pltpu.VMEM((chips, 8, thin), f32),
            pltpu.VMEM((8, length), f32),
            pltpu.VMEM((tensor - 1, 8, length), f32),
            pltpu.VMEM((max(inner - 1, 1), 2, outer, slab, units), bf16),
            pltpu.VMEM((2, outer, slab, units), bf16),
            pltpu.VMEM((max(inner - 1, 1), outer, units, slab), bf16),
            pltpu.VMEM((outer, units, slab), bf16),
            pltpu.VMEM((chips, count, width), bf16),
            pltpu.VMEM((chips, count, width), bf16),
            pltpu.VMEM((chips, count, width), f32),
            pltpu.VMEM((max(chips - 1, 1), count, width), bf16),
            pltpu.VMEM((max(chips - 1, 1), count, width), bf16),
            sems((n - 1, ring)),
            sems((n - 1, ring)),
            sems((2 * chips - 1,)),
            sems((2 * chips - 1,)),
            sems((tensor - 1,)),
            sems((tensor - 1,)),
            sems((inner, 3, outer)),
            sems((inner, 3, outer)),
            sems((3, outer)),
            sems((3, outer)),
            sems((chips,)),
            sems((chips,)),
            sems((chips,)),
            sems((chips,)),
            sems((chips,)),
            sems((chips,)),
            sems((9,)),
        ],
        compiler_params=pltpu.CompilerParams(
            collective_id=1, has_side_effects=True, vmem_limit_bytes=61 * 2**20
        ),
    )(
        d_resid, attn_hat, o_scale, gain_rows, full_out, context, q_low, k_low, v_low, lse, scales,
        tables[0], tables[1], blocks[None, :], gain_last, tops,
        hats, seq, full_qkv, *flat_grads,
    )
    return results


def open_call(w_qkv, w_out, gains, rows, w_gu, w_down, tables, blocks):
    grid = Grid()
    n, outer, inner = grid.dp, grid.outer, grid.inner
    chips, tensor = grid.chips, grid.tensor
    count, width = rows.shape
    length = count * tensor
    lead, slab, span = w_qkv.shape
    gain_count = gains.shape[0]
    half = slab // 2
    part_tall = span // 2
    heads = span // HEAD
    shard_units = w_gu.shape[2]
    units = shard_units // outer
    places = [(j, s) for j in range(inner) for s in range(outer) if not (j and s == outer - 1)]
    parts = len(places)
    ring = 2 * lead + 3
    steps = list(range(1, outer))
    tall = min(256, length)
    tile = 512
    lines = 32
    bf16, f32 = jnp.bfloat16, jnp.float32
    mesh_id = pl.DeviceIdType.MESH

    def kernel(*refs):
        body(*refs[:10], dict(zip(places, refs[10 : 10 + parts])), *refs[10 + parts :])

    def body(
        qkv_any, out_any, rows_any, gu_any, down_any, gains_ref, cos_ref, sin_ref, id_row, rows_ref,
        pieces, qkv_out, flat_out, seq_out,
        gain_rows, hat_ref, scale_ref, q_low, k_low, v_low, lse_ref, context, attn_hat, o_scale, resid, resid_low, top_ref,
        qkv_ref, out_w_ref, seq_ref, all_gains, qkv_wide, out_wide, gu_wide, down_wide, cast, id_col,
        square, squares, core_send, core_land, hold, chip_send, chip_land,
        s_ring, r_ring, s_row, r_row, s_z, r_z, s_y, r_y, s_sq, r_sq, s_core, r_core, s_chip, r_chip, local,
    ):
        g = Grid()

        def tensor_peer(k, flip):
            core = 1 - g.core_at if flip else g.core_at
            return (g.dp_at, lax.rem(g.chip_at + k + chips, chips) * 2 + core)

        def dp_peer(s, j):
            across = g.outer_flip(g.outer_at, s) * inner
            return (across + lax.rem(g.inner_at + j + inner, inner), g.tensor_at)

        near = [tensor_peer(k, f) for k in range(chips) for f in (0, 1) if (k, f) != (0, 0)]
        far = [dp_peer(s, 0) for s in range(1, outer)]
        far += [dp_peer(0, j) for j in sorted({1 % inner, inner - 1} - {0})]
        t_at = g.tensor_at
        place = g.path_of(g.dp_at)
        after = (g.index_of(lax.rem(place + 1, n)), t_at)
        before = (g.index_of(lax.rem(place + n - 1, n)), t_at)
        firsts = []
        for at, (src, dst) in enumerate(((qkv_any, qkv_wide), (out_any, out_wide))):
            firsts.append(pltpu.make_async_copy(src, dst, local.at[3 + at]))
            firsts[-1].start()
        greet(near + far + [after, before])

        def remote(src, dst, send, recv, peer):
            copy = pltpu.make_async_remote_copy(
                src_ref=src, dst_ref=dst, send_sem=send, recv_sem=recv,
                device_id=peer, device_id_type=mesh_id,
            )
            copy.start()
            return copy

        def dot(a, b, contract):
            return lax.dot_general(a, b, (contract, ((), ())), preferred_element_type=f32)

        def looped(total, make):
            lax.fori_loop(0, total, lambda i, c: (make(i), c)[1], 0, unroll=total <= 4)

        def rows_of(i, size):
            return pl.ds(pl.multiple_of(i * size, size), size)

        def fetch(src, dst, at):
            copy = pltpu.make_async_copy(src, dst, local.at[at])
            copy.start()
            return copy

        def views(item, index):
            if item == ring - 1:
                return 1, all_gains.at[index]
            if item >= 2 * lead:
                side = item - 2 * lead
                part = pl.ds(side * part_tall, part_tall)
                return 1 - 2 * side, out_w_ref.at[part, rows_of(index, slab)]
            side, c = item // lead, item % lead
            at = pl.ds(pl.multiple_of(index * slab + side * half, half), half)
            return 1 - 2 * side, qkv_ref.at[c, at]

        hops = {}

        def hop(step, item):
            way = views(item, 0)[0]
            index = g.index_of(lax.rem(place - way * step + n, n))
            _, view = views(item, index)
            hops[step, item] = remote(
                view,
                view,
                s_ring.at[step, item],
                r_ring.at[step, item],
                after if way == 1 else before,
            )

        def row_copy(slot, index, peer, src=None):
            at = seq_ref.at[rows_of(index, count)]
            return remote(at if src is None else src, at, s_row.at[slot], r_row.at[slot], peer)

        order = [c + side * lead for c in range(lead) for side in (0, 1)]
        order += list(range(2 * lead, ring))
        firsts[0].wait()
        for c in range(lead):

            def cast_own(i, c=c):
                at = rows_of(i, lines)
                there = pl.ds(pl.multiple_of(g.dp_at * slab + i * lines, lines), lines)
                qkv_ref[c, there] = qkv_wide[c, at].astype(bf16)

            looped(slab // lines, cast_own)
            for side in (0, 1):
                hop(0, c + side * lead)
        firsts[1].wait()

        def cast_flat(i):
            at = rows_of(i, lines)
            out_w_ref[at, rows_of(g.dp_at, slab)] = out_wide[at].astype(bf16)

        looped(span // lines, cast_flat)
        empty = jnp.zeros((16 - gain_count, slab), f32)
        all_gains[g.dp_at] = jnp.concatenate([gains_ref[...], empty], axis=0).astype(bf16)
        for item in range(2 * lead, ring):
            hop(0, item)
        row_copies = [
            row_copy(k - 1, t_at, tensor_peer(k, 0), rows_any) for k in range(1, chips)
        ]
        row_copies.append(row_copy(chips - 1, t_at, tensor_peer(0, 1), rows_any))
        wide = [fetch(gu_any, gu_wide, 1), fetch(down_any, down_wide, 2)]
        kept = fetch(rows_any, seq_ref.at[rows_of(t_at, count)], 5)

        def cast_wide(c):
            if c == 0:
                wide[0].wait()

            def cast_rows(i):
                at = rows_of(i, lines)
                cast[c, at] = gu_wide[c, at].astype(bf16)

            looped(slab // lines, cast_rows)

        def cast_turned():
            wide[1].wait()

            def cast_rows(i):
                at = rows_of(i, 256)
                cast[2, :, at] = down_wide[at].T.astype(bf16)

            looped(shard_units // 256, cast_rows)

        def ids():
            id_col[...] = jnp.broadcast_to(id_row[...], (128, length)).T

        shadows = [ids, lambda: cast_wide(0), lambda: cast_wide(1), cast_turned]
        for step in range(1, n - 1):
            for item in order:
                hops[step - 1, item].wait_recv()
                hop(step, item)
            if step <= chips - 1:
                row_copies[step - 1].wait_recv()
                source = lax.rem(g.chip_at - step + chips, chips) * 2 + g.core_at
                row_copies.append(row_copy(chips - 1 + step, source, tensor_peer(0, 1)))
            if shadows:
                shadows.pop(0)()

        def cut(s):
            return cast.at[:, :, rows_of(g.outer_flip(g.outer_at, s), units)]

        z_copies = {}

        for s in steps:
            z_copies[s] = remote(cut(s), pieces[0, s], s_z.at[s], r_z.at[s], dp_peer(s, 0))
        own = fetch(cut(0), pieces[0, 0], 0)
        y_copies = {}

        def pass_on(j, s):
            if (j, s) in pieces:
                src = cut(0) if (j, s) == (1, 0) else pieces[j - 1, s]
                y_copies[j, s] = remote(src, pieces[j, s], s_y.at[j, s], r_y.at[j, s], dp_peer(0, 1))

        pass_on(1, 0)
        duties = []
        for s in steps:

            def duty(s=s):
                z_copies[s].wait_recv()
                pass_on(1, s)

            duties.append(duty)
        for j in range(2, inner):
            for s in range(outer - 1):

                def duty(j=j, s=s):
                    y_copies[j - 1, s].wait_recv()
                    pass_on(j, s)

                duties.append(duty)

        def next_duties(times):
            for _ in range(times):
                if duties:
                    duties.pop(0)()

        for item in order:
            hops[n - 2, item].wait_recv()
        for copy in row_copies[chips - 1 :]:
            copy.wait_recv()
        kept.wait()
        outs = [fetch(qkv_ref, qkv_out, 3), fetch(out_w_ref, flat_out, 4), fetch(seq_ref, seq_out, 5)]

        def spread(i):
            gain_rows[:, rows_of(i, slab)] = all_gains[i].astype(f32)[:8]

        looped(n, spread)

        def project(i):
            at = rows_of(i, tall)
            x = seq_ref[at]
            lane = lax.broadcasted_iota(jnp.int32, (tall, 128), 1)
            sums = jnp.zeros((tall, 128), f32)
            for c in range(2):
                value = dot(x, qkv_ref[c], ((1,), (0,)))
                hat_ref[c, at] = value
                sums = jnp.where(lane == c, jnp.sum(value * value, axis=1, keepdims=True), sums)
            v_low[at] = dot(x, qkv_ref[2], ((1,), (0,))).astype(bf16)
            square[:, at] = sums.T[:8]

        looped(length // tall, project)
        sq_copies = []
        for k in range(chips):
            for f in (0, 1):
                if (k, f) != (0, 0):
                    at = k * 2 + f - 1
                    sq_copies.append(
                        remote(square, squares.at[at], s_sq.at[at], r_sq.at[at], tensor_peer(k, f))
                    )
        for copy in sq_copies:
            copy.wait_recv()
        sign = jnp.where(lax.broadcasted_iota(jnp.int32, (tall, HEAD), 1) < HEAD // 2, -1.0, 1.0)

        def rotate(i):
            at = rows_of(i, tall)
            sums = square[:, at]
            for copy_at in range(tensor - 1):
                sums = sums + squares[copy_at, :, at]
            column = jnp.concatenate([sums, jnp.zeros((120, tall), f32)], axis=0).T
            scales = lax.rsqrt(column / width + norm_eps)
            scale_ref[at] = scales
            cosine, sine = cos_ref[at], sin_ref[at] * sign
            for c, low in ((0, q_low), (1, k_low)):
                hat = hat_ref[c, at] * scales[:, c : c + 1]
                hat_ref[c, at] = hat
                normed = hat * gain_rows[c : c + 1, rows_of(t_at, span)]
                for h in range(heads):
                    cols = slice(h * HEAD, (h + 1) * HEAD)
                    value = normed[:, cols]
                    turned = pltpu.roll(value, HEAD // 2, 1)
                    low[at, cols] = (value * cosine + turned * sine).astype(bf16)

        looped(length // tall, rotate)
        scale = HEAD ** (-0.5)
        top_ref[...] = jnp.full((8, 128), masked_value, f32)
        for h in range(heads):
            cols = slice(h * HEAD, (h + 1) * HEAD)

            def attend(i, best, cols=cols, h=h):
                at = rows_of(i, tall)
                raw = dot(q_low[at, cols], k_low[:, cols], ((1,), (1,))) * scale
                masked = jnp.where(id_row[...] <= id_col[at, 0:1], raw, masked_value)
                top = jnp.max(masked, axis=1, keepdims=True)
                weight = jnp.exp(masked - top)
                total = jnp.sum(weight, axis=1, keepdims=True)
                probs = (weight * (1.0 / total)).astype(bf16)
                context[at, cols] = dot(probs, v_low[:, cols], ((1,), (0,))).astype(bf16)
                lse_ref[at, h : h + 1] = top + jnp.log(total)
                return jnp.maximum(best, jnp.max(top, axis=0, keepdims=True))

            best = lax.fori_loop(
                0, length // tall, attend, jnp.full((1, 1), masked_value, f32), unroll=length // tall <= 4
            )
            top_ref[h : h + 1] = jnp.broadcast_to(best, (1, 128))
            if h + 1 == max(heads // 2, 1):
                next_duties(1)
        next_duties(1)

        def out_rows(k, flip, store):
            chip = lax.rem(g.chip_at + k, chips)
            core = 1 - g.core_at if flip else g.core_at
            at = rows_of(chip * 2 + core, count)

            def columns(i):
                cols = rows_of(i, tile)
                store(cols, dot(context[at], out_w_ref[:, cols], ((1,), (0,))))

            looped(width // tile, columns)

        chip_order = list(range(1, chips)) + [0]
        core_copies, chip_copies = {}, {}
        for k in chip_order:

            def store(cols, value, k=k):
                core_send[k, :, cols] = value.astype(bf16)

            out_rows(k, True, store)
            core_copies[k] = remote(
                core_send.at[k], core_land.at[k], s_core.at[k], r_core.at[k], tensor_peer(0, 1)
            )
        for k in chip_order:

            def store(cols, value, k=k):
                hold[k, :, cols] = value

            out_rows(k, False, store)
            if k:
                core_copies[k].wait_recv()

                def add(i, k=k):
                    at = rows_of(i, lines)
                    chip_send[k - 1, at] = (hold[k, at] + core_land[k, at].astype(f32)).astype(bf16)

                looped(count // lines, add)
                chip_copies[k] = remote(
                    chip_send.at[k - 1], chip_land.at[k - 1], s_chip.at[k], r_chip.at[k], tensor_peer(k, 0)
                )
        core_copies[0].wait_recv()
        for k in range(1, chips):
            chip_copies[k].wait_recv()

        def close(i):
            at = rows_of(i, lines)
            raw = hold[0, at] + core_land[0, at].astype(f32)
            for k in range(1, chips):
                raw = raw + chip_land[k - 1, at].astype(f32)
            scale_o = lax.rsqrt(jnp.mean(raw * raw, axis=1, keepdims=True) + norm_eps)
            hat = raw * scale_o
            attn_hat[at] = hat
            o_scale[at] = scale_o
            value = rows_ref[at].astype(f32) + hat * gain_rows[2:3]
            resid[at] = value
            resid_low[at] = value.astype(bf16)

        looped(count // lines, close)
        next_duties(len(duties))
        own.wait()
        for key, copy in y_copies.items():
            if key[0] == inner - 1:
                copy.wait_recv()
        for copy in outs:
            copy.wait()
        sent = list(hops.values()) + row_copies + list(z_copies.values()) + list(y_copies.values()) + sq_copies
        for copy in sent + list(core_copies.values()) + list(chip_copies.values()):
            copy.wait_send()

    shape = jax.ShapeDtypeStruct
    anywhere = pl.BlockSpec(memory_space=pl.ANY)
    vmem = pl.BlockSpec(memory_space=pltpu.VMEM)
    sems = pltpu.SemaphoreType.DMA
    results = pl.pallas_call(
        kernel,
        out_shape=(shape((3, slab, units), bf16),) * parts
        + (
            shape((lead, width, span), bf16),
            shape((span, width), bf16),
            shape((length, width), bf16),
            shape((8, width), f32),
            shape((2, length, span), f32),
            shape((length, 128), f32),
            shape((length, span), bf16),
            shape((length, span), bf16),
            shape((length, span), bf16),
            shape((length, heads), f32),
            shape((length, span), bf16),
            shape((count, width), f32),
            shape((count, 1), f32),
            shape((count, width), f32),
            shape((count, width), bf16),
            shape((8, 128), f32),
        ),
        in_specs=[anywhere] * 5 + [vmem] * 5,
        out_specs=(anywhere,) * (parts + 3) + (vmem,) * 13,
        scratch_shapes=[
            pltpu.VMEM((lead, width, span), bf16),
            pltpu.VMEM((span, width), bf16),
            pltpu.VMEM((length, width), bf16),
            pltpu.VMEM((n, 16, slab), bf16),
            pltpu.VMEM(w_qkv.shape, f32),
            pltpu.VMEM(w_out.shape, f32),
            pltpu.VMEM(w_gu.shape, f32),
            pltpu.VMEM(w_down.shape, f32),
            pltpu.VMEM((3, slab, shard_units), bf16),
            pltpu.VMEM((length, 128), jnp.int32),
            pltpu.VMEM((8, length), f32),
            pltpu.VMEM((tensor - 1, 8, length), f32),
            pltpu.VMEM((chips, count, width), bf16),
            pltpu.VMEM((chips, count, width), bf16),
            pltpu.VMEM((chips, count, width), f32),
            pltpu.VMEM((max(chips - 1, 1), count, width), bf16),
            pltpu.VMEM((max(chips - 1, 1), count, width), bf16),
            sems((n - 1, ring)),
            sems((n - 1, ring)),
            sems((2 * chips - 1,)),
            sems((2 * chips - 1,)),
            sems((outer,)),
            sems((outer,)),
            sems((inner, outer)),
            sems((inner, outer)),
            sems((tensor - 1,)),
            sems((tensor - 1,)),
            sems((chips,)),
            sems((chips,)),
            sems((chips,)),
            sems((chips,)),
            sems((7,)),
        ],
        compiler_params=pltpu.CompilerParams(
            collective_id=0, has_side_effects=True, vmem_limit_bytes=58 * 2**20
        ),
    )(
        w_qkv, w_out, rows, w_gu, w_down, gains, tables[0], tables[1],
        blocks[None, :], rows,
    )
    return dict(zip(places, results[:parts])), results[parts:]


def unit_kernel_call(rows_low, resid, cotangent, gain, pieces):
    grid = Grid()
    outer, chips, inner = grid.outer, grid.chips, grid.inner
    total_rows, width = rows_low.shape
    slab, units = pieces[0, 0].shape[1:]
    places = list(pieces)
    parts = len(places)
    last = (0, outer - 1)
    halves = 2
    count = total_rows // halves
    both = 2 * count
    per = min(2, chips)
    groups = chips // per
    blocks = outer * groups
    tall = per * both
    held = per if groups > 1 else max(per - 1, 1)
    links = outer * (chips - 1)
    steps = list(range(outer))
    near, far, rest = steps[1:2], steps[2:3], steps[3:]

    def units_of(of_steps):
        return [(s, i) for s in of_steps for i in range(groups)]

    orders = {
        (0, 0): units_of(far + [0] + rest + near),
        (0, 1): units_of(far + rest + near + [0]),
        (1, 0): units_of([0] + far + near + rest),
        (1, 1): units_of([0] + far + near + rest),
    }
    grad_order = units_of([0] + far + rest + near)
    tile = 512
    wide_tiles = width // tile
    unit_tile = min(512, units)
    lines = 32
    bf16, f32 = jnp.bfloat16, jnp.float32
    mesh_id = pl.DeviceIdType.MESH

    def plan():
        chip_us, core_us, hop_us = 5.6, 0.6, 2.0
        free = {"x": 0.0, "core": 0.0, "z near": 0.0, "z far": 0.0}
        arrive, done, tasks = {("w",): 20.0}, {}, {}

        def send(link, when, us):
            free[link] = max(free[link], when) + us
            return free[link] + hop_us

        def add(name, needs, us, after=None):
            tasks[name] = (needs, us, after)

        def send_outer(s, now):
            return send("z near", now, 8.0) if s == 1 else send("z far", now, 10.5)

        def go(p, h):
            def then(now):
                if (p, h) != (0, 1):
                    for s in steps[1:]:
                        arrive["z", p, h, s] = send_outer(s, now)
                for k in range(1, chips):
                    arrive["x", p, h, 0, k] = send("x", now, chip_us)
                arrive["c", p, h, 0, 0] = send("core", now, core_us)

            return then

        def zf(p, h, s):
            def then(now):
                for k in range(1, chips):
                    arrive["x", p, h, s, k] = send("x", now, chip_us)
                arrive["c", p, h, s, 0] = send("core", now, core_us)
                if (p, h) == (0, 0):
                    arrive["z", 0, 1, s] = send_outer(s, now)

            return then

        def xf(p, h, s, k):
            def then(now):
                arrive["c", p, h, s, k] = send("core", now, core_us)

            return then

        def compute(p, h, s, i):
            def then(now):
                arrive["cr", p, h, s, i] = send("core", now, per * core_us)

            return then

        def cr(p, h, s, i):
            def then(now):
                for k in range(i * per, i * per + per):
                    if k:
                        arrive["xr", p, h, s, k] = send("x", now, chip_us)

            return then

        def xr(p, h, s):
            def then(now):
                if s:
                    arrive["zr", p, h, s] = send_outer(s, now)

            return then

        for p in (0, 1):
            for h in range(halves):
                if p == 0:
                    needs = [("do", ("go", 0, h - 1))] if h else []
                else:
                    needs = [("do", ("between", h))]
                add(("go", p, h), needs, 0.2, go(p, h))
                for s in steps[1:]:
                    add(("zf", p, h, s), [("at", ("z", p, h, s))], 0.2, zf(p, h, s))
                for s in steps:
                    for k in range(1, chips):
                        add(("xf", p, h, s, k), [("at", ("x", p, h, s, k))], 0.2, xf(p, h, s, k))
                order = orders[p, h]
                for n, (s, i) in enumerate(order):
                    needs = [("at", ("c", p, h, s, i * per + j)) for j in range(per)]
                    if n:
                        needs.append(("do", ("front", p, h) + order[n - 1]))
                    add(("load", p, h, s, i), needs, 0.2)
                    needs = [("do", ("load", p, h, s, i)), ("do", ("weights",))]
                    add(("front", p, h, s, i), needs, (2.4, 1.6)[p])
                    needs = [("do", ("front", p, h, s, i))]
                    if n:
                        needs.append(("do", ("cr", p, h) + order[n - 1]))
                    add(("compute", p, h, s, i), needs, (1.6, 2.4)[p], compute(p, h, s, i))
                    needs = [("at", ("cr", p, h, s, i)), ("do", ("compute", p, h, s, i))]
                    add(("cr", p, h, s, i), needs, 0.5, cr(p, h, s, i))
                for s in steps:
                    needs = [("do", ("cr", p, h, s, 0))]
                    needs += [("at", ("xr", p, h, s, k)) for k in range(1, chips)]
                    add(("xr", p, h, s), needs, 0.4, xr(p, h, s))
                for s in steps[1:]:
                    needs = [("at", ("zr", p, h, s)), ("do", ("xr", p, h, 0))]
                    add(("zr", p, h, s), needs, 0.4)
        add(("weights",), [("at", ("w",))], 0.2)
        for h in range(halves):
            needs = [("do", ("zr", 0, h, s)) for s in steps[1:]] + [("do", ("xr", 0, h, 0))]
            add(("between", h), needs, 1.0)
        for n, (s, i) in enumerate(grad_order):
            needs = [("do", ("compute", 1, h, s, i)) for h in range(halves)]
            if n:
                needs.append(("do", ("grads",) + grad_order[n - 1] + (2,)))
            add(("fetch", s, i), needs, 0.2)
            for c in range(3):
                needs = [("do", ("grads", s, i, c - 1) if c else ("fetch", s, i))]
                add(("grads", s, i, c), needs, 2.8)
        written = [(j, s) for j in range(inner) for s in range(outer)]
        for n, at in enumerate(written):
            needs = [("do", ("grads",) + grad_order[-1] + (2,))]
            if n:
                needs = [("do", ("write",) + written[n - 1])]
            add(("write",) + at, needs, 0.6)
        rank = {"compute": 1, "front": 2, "fetch": 2, "grads": 3, "write": 4}
        result = []
        now = 0.0
        while tasks:
            best = None
            for name, (needs, us, then) in tasks.items():
                ready = 0.0
                for kind, key in needs:
                    table = arrive if kind == "at" else done
                    if key not in table:
                        ready = None
                        break
                    ready = max(ready, table[key] + (1.0 if key[0] in ("load", "fetch") else 0.0))
                if ready is None:
                    continue
                key = (max(ready, now), rank.get(name[0], 0))
                if best is None or key < best[0]:
                    best = (key, name)
            (ready, _), name = best
            needs, us, then = tasks.pop(name)
            now = ready + us
            done[name] = now
            if then is not None:
                then(now)
            result.append(name)
        return result

    def kernel(*refs):
        piece_refs = dict(zip(places, refs[:parts]))
        fixed = refs[parts : parts + 9]
        k = parts + 9
        late, grad_refs = refs[k : k + inner - 1], refs[k + inner - 1 : k + inner - 1 + 3 * inner]
        for j in range(1, inner):
            piece_refs[j, outer - 1] = late[j - 1]
        body(piece_refs, *fixed, grad_refs, *refs[k + inner - 1 + 3 * inner :])

    def body(
        piece_refs, rows_ref, resid_ref, cot_ref, gain_ref,
        out_ref, dres_ref, gain_out, all_x, all_dm, grad_refs,
        wg, wu, wd, buf, wide_buf, act, coef_gate, coef_up, d_gate, d_up, turned, acc_gate, acc_up, acc_down, stage, stage_down,
        core_send, core_land, hold, keep, chip_send, chip_land, outer_send, outer_land, raw, d_mlp,
        s_outer, r_outer, s_chip, r_chip, s_core, r_core,
        s_core_sum, r_core_sum, s_chip_sum, r_chip_sum, s_outer_sum, r_outer_sum,
        local, local_own, local_wide, local_w, local_g, s_late, r_late,
    ):
        g = Grid()
        core_peer = (g.dp_at, g.chip_at * 2 + 1 - g.core_at)

        def chip_peer(k):
            return (g.dp_at, lax.rem(g.chip_at + k + chips, chips) * 2 + g.core_at)

        def outer_peer(s):
            return (g.outer_flip(g.outer_at, s) * inner + g.inner_at, g.tensor_at)

        def inner_peer(j):
            return (g.outer_at * inner + lax.rem(g.inner_at + j, inner), g.tensor_at)

        greet(
            [core_peer]
            + [chip_peer(k) for k in range(1, chips)]
            + [outer_peer(s) for s in range(1, outer)]
            + [inner_peer(j) for j in range(1, inner)]
        )

        def remote(src, dst, send, recv, peer):
            copy = pltpu.make_async_remote_copy(
                src_ref=src, dst_ref=dst, send_sem=send, recv_sem=recv,
                device_id=peer, device_id_type=mesh_id,
            )
            copy.start()
            return copy

        def fetch(src, dst, sem):
            copy = pltpu.make_async_copy(src, dst, sem)
            copy.start()
            return copy

        def dot(a, b, contract):
            return lax.dot_general(a, b, (contract, ((), ())), preferred_element_type=f32)

        def looped(total, make):
            lax.fori_loop(0, total, lambda i, c: (make(i), c)[1], 0, unroll=total <= 4)

        def by_lines(make):
            looped(count // lines, lambda i: make(pl.ds(pl.multiple_of(i * lines, lines), lines)))

        def by_tiles(make):
            looped(wide_tiles, lambda i: make(pl.ds(pl.multiple_of(i * tile, tile), tile)))

        weights = (wg, wu, wd)
        fetches = []

        late_copies = []

        def send_late():
            for j in range(1, inner):
                late_copies.append(
                    remote(piece_refs[last], piece_refs[j, last[1]], s_late.at[j], r_late.at[j], inner_peer(j))
                )

        def fetch_weights(which):
            for j, s in which:
                index = g.outer_flip(g.outer_at, s) * inner
                index = index + lax.rem(g.inner_at - j + inner, inner)
                span = pl.ds(pl.multiple_of(index * slab, slab), slab)
                for c in range(3):
                    fetches.append(
                        fetch(piece_refs[j, s].at[c], weights[c].at[span], local_w.at[j * outer + s, c])
                    )

        mine, theirs = pl.ds(0, count), pl.ds(count, count)
        every = (all_x, all_dm)
        copies, sums, loads, own = {}, {}, {}, {}
        unsent = {(p, h): [] for p in (0, 1) for h in range(halves)}

        def track(p, h, copy):
            unsent[p, h].append(copy)
            return copy

        def core_copy(p, h, s, k, src):
            dst = every[p].at[h, s, k, theirs]
            copies["c", p, h, s, k] = track(
                p, h, remote(src, dst, s_core.at[p, h, s, k], r_core.at[p, h, s, k], core_peer)
            )

        def chip_copy(p, h, s, k, src):
            dst = every[p].at[h, s, k, mine]
            copies["x", p, h, s, k] = track(
                p, h, remote(src, dst, s_chip.at[p, h, s, k], r_chip.at[p, h, s, k], chip_peer(k))
            )

        def outer_copy(p, h, s):
            source = (rows_ref, d_mlp)[p].at[pl.ds(h * count, count)]
            dst = every[p].at[h, s, 0, mine]
            copies["z", p, h, s] = track(
                p, h, remote(source, dst, s_outer.at[p, h, s], r_outer.at[p, h, s], outer_peer(s))
            )

        def go(p, h):
            source = (rows_ref, d_mlp)[p].at[pl.ds(h * count, count)]
            if (p, h) != (0, 1):
                for s in steps[1:]:
                    outer_copy(p, h, s)
            for k in range(1, chips):
                chip_copy(p, h, 0, k, source)
            core_copy(p, h, 0, 0, source)
            own[p, h] = fetch(source, every[p].at[h, 0, 0, mine], local_own.at[p, h])
            if p == 0 and h == 0:
                fetch_weights(places)

        def part_out(h, s, i, cols, part_sum):
            for j in range(per):
                own_rows = part_sum[j * both : j * both + count]
                if i * per + j == 0:
                    keep[h, s, :, cols] = own_rows
                else:
                    hold[h, min(j, held - 1), :, cols] = own_rows
                core_send[h, j, :, cols] = part_sum[j * both + count : (j + 1) * both].astype(bf16)

        def forward(h, unit):
            for j in range(units // unit_tile):
                cols = pl.ds(j * unit_tile, unit_tile)
                rows = buf[h].reshape(tall, width)
                gate = dot(rows, wg[:, cols], ((1,), (0,)))
                up = dot(rows, wu[:, cols], ((1,), (0,)))
                sigma = jax.nn.sigmoid(gate)
                silu = gate * sigma
                act[unit, h, :, cols] = (silu * up).astype(bf16)
                coef_up[unit, h, :, cols] = silu.astype(bf16)
                coef_gate[unit, h, :, cols] = (
                    up * sigma * (1.0 + gate * (1.0 - sigma))
                ).astype(bf16)

        def forward_out(h, unit, s, i):
            by_tiles(
                lambda cols: part_out(h, s, i, cols, dot(act[unit, h], wd[cols, :], ((1,), (1,))))
            )

        def backward(h, unit):
            for j in range(units // unit_tile):
                cols = pl.ds(j * unit_tile, unit_tile)
                d_act = dot(buf[h].reshape(tall, width), wd[:, cols], ((1,), (0,)))
                d_gate[unit, h, :, cols] = (d_act * coef_gate[unit, h, :, cols].astype(f32)).astype(bf16)
                d_up[unit, h, :, cols] = (d_act * coef_up[unit, h, :, cols].astype(f32)).astype(bf16)

        def backward_out(h, unit, s, i):
            def into(cols):
                part_sum = dot(d_gate[unit, h], wg[cols, :], ((1,), (1,)))
                part_sum = part_sum + dot(d_up[unit, h], wu[cols, :], ((1,), (1,)))
                part_out(h, s, i, cols, part_sum)

            by_tiles(into)

        def weight_grads(unit, c):
            first = unit == grad_order[0][0] * groups + grad_order[0][1]
            left, right, acc = ((d_gate, 0, acc_gate), (d_up, 0, acc_up), (act, 1, acc_down))[c]
            turned[...] = left[unit].reshape(halves * tall, units).T

            def grads(cols):
                rows = wide_buf[right, :, :, :, cols].reshape(halves * tall, tile)
                value = dot(turned[...], rows, ((1,), (0,)))
                acc[:, cols] = value if first else acc[:, cols] + value

            by_tiles(grads)

        def between(h):
            def lines_of(i, total):
                at_rows = pl.ds(pl.multiple_of(h * count + i * lines, lines), lines)
                value = raw[at_rows]
                scale = lax.rsqrt(jnp.mean(value * value, axis=1, keepdims=True) + norm_eps)
                hat = value * scale
                gain_row = gain_ref[3:4]
                out_ref[at_rows] = (resid_ref[at_rows] + hat * gain_row).astype(bf16)
                top = cot_ref[at_rows].astype(f32)
                upstream = top * gain_row
                mean = jnp.mean(upstream * hat, axis=1, keepdims=True)
                d_mlp[at_rows] = (scale * (upstream - hat * mean)).astype(bf16)
                return total + jnp.sum(top * hat, axis=0, keepdims=True)

            zero = jnp.zeros((1, width), f32)
            total = lax.fori_loop(0, count // lines, lines_of, zero)
            gain_out[...] = total if h == 0 else gain_out[...] + total

        batches = []

        def write_grads(j, s):
            index = g.outer_flip(g.outer_at, s) * inner
            index = index + lax.rem(g.inner_at + j, inner)
            span = pl.ds(pl.multiple_of(index * slab, slab), slab)
            for copy in batches:
                copy.wait()
            batches.clear()
            for c, src in enumerate((stage.at[0], stage.at[1], stage_down)):
                if c == 0:
                    stage[0] = acc_gate[:, span].astype(bf16).T
                elif c == 1:
                    stage[1] = acc_up[:, span].astype(bf16).T
                else:
                    stage_down[...] = acc_down[:, span].astype(bf16)
                batches.append(fetch(src, grad_refs[j * 3 + c].at[s], local_g.at[c]))

        def core_sum(p, h, s, i):
            unit = s * groups + i
            sums["c", p, h, unit].wait_recv()
            for j in range(per):
                chip = i * per + j
                if chip == 0:

                    def add(at_rows):
                        keep[h, s, at_rows] = keep[h, s, at_rows] + core_land[h, unit, j, at_rows].astype(f32)

                    by_lines(add)
                    continue
                there = s * (chips - 1) + chip - 1

                def add(at_rows):
                    total = hold[h, min(j, held - 1), at_rows] + core_land[h, unit, j, at_rows].astype(f32)
                    chip_send[h, there, at_rows] = total.astype(bf16)

                by_lines(add)
                sums["x", p, h, s, chip] = track(
                    p, h,
                    remote(
                        chip_send.at[h, there], chip_land.at[h, there],
                        s_chip_sum.at[p, h, there], r_chip_sum.at[p, h, there], chip_peer(-chip),
                    ),
                )

        def chip_sum(p, h, s):
            for k in range(1, chips):
                sums["x", p, h, s, k].wait_recv()

            def add(at_rows):
                total = keep[h, s, at_rows]
                for k in range(1, chips):
                    total = total + chip_land[h, s * (chips - 1) + k - 1, at_rows].astype(f32)
                if s == 0:
                    raw[pl.ds(pl.multiple_of(h * count + at_rows.start, lines), lines)] = total
                else:
                    outer_send[h, s - 1, at_rows] = total.astype(bf16)

            by_lines(add)
            if s:
                sums["z", p, h, s] = track(
                    p, h,
                    remote(
                        outer_send.at[h, s - 1], outer_land.at[h, s - 1],
                        s_outer_sum.at[p, h, s], r_outer_sum.at[p, h, s], outer_peer(s),
                    ),
                )

        def outer_sum(p, h, s):
            sums["z", p, h, s].wait_recv()

            def add(at_rows):
                there = pl.ds(pl.multiple_of(h * count + at_rows.start, lines), lines)
                raw[there] = raw[there] + outer_land[h, s - 1, at_rows].astype(f32)

            by_lines(add)

        def all_sent(p, h):
            for copy in unsent[p, h]:
                copy.wait_send()

        last_core = {}
        send_late()
        for task in plan():
            name, args = task[0], task[1:]
            if name == "go":
                go(*args)
            elif name == "zf":
                p, h, s = args
                copies["z", p, h, s].wait_recv()
                source = every[p].at[h, s, 0, mine]
                for k in range(1, chips):
                    chip_copy(p, h, s, k, source)
                core_copy(p, h, s, 0, source)
                if (p, h) == (0, 0):
                    outer_copy(0, 1, s)
            elif name == "xf":
                p, h, s, k = args
                copies["x", p, h, s, k].wait_recv()
                core_copy(p, h, s, k, every[p].at[h, s, k, mine])
            elif name == "load":
                p, h, s, i = args
                for j in range(per):
                    copies["c", p, h, s, i * per + j].wait_recv()
                if (s, i) == (0, 0):
                    own[p, h].wait()
                src = every[p].at[h, s, pl.ds(i * per, per)]
                loads[args] = fetch(src, buf.at[h], local.at[p, h, s * groups + i])
            elif name == "weights":
                for copy in late_copies:
                    copy.wait_recv()
                fetch_weights([(j, last[1]) for j in range(1, inner)])
            elif name == "front":
                p, h, s, i = args
                if p == 0 and not loads.get("weights"):
                    loads["weights"] = True
                    for copy in fetches:
                        copy.wait()
                loads[args].wait()
                (forward, backward)[p](h, s * groups + i)
            elif name == "compute":
                p, h, s, i = args
                unit = s * groups + i
                if h in last_core:
                    last_core[h].wait_send()
                (forward_out, backward_out)[p](h, unit, s, i)
                last_core[h] = remote(
                    core_send.at[h], core_land.at[h, unit],
                    s_core_sum.at[p, h, unit], r_core_sum.at[p, h, unit], core_peer,
                )
                sums["c", p, h, unit] = last_core[h]
            elif name == "cr":
                core_sum(*args)
            elif name == "xr":
                chip_sum(*args)
            elif name == "zr":
                outer_sum(*args)
            elif name == "between":
                all_sent(0, args[0])
                between(args[0])
            elif name == "fetch":
                s, i = args
                loads[task] = []
                for at, src in enumerate((all_x, all_dm)):
                    for h in range(halves):
                        loads[task].append(
                            fetch(
                                src.at[h, s, pl.ds(i * per, per)],
                                wide_buf.at[at, h],
                                local_wide.at[s * groups + i, at * halves + h],
                            )
                        )
            elif name == "grads":
                s, i, c = args
                if c == 0:
                    for copy in loads["fetch", s, i]:
                        copy.wait()
                weight_grads(s * groups + i, c)
            elif name == "write":
                write_grads(*args)

        looped(
            total_rows // lines,
            lambda i: close_rows(pl.ds(pl.multiple_of(i * lines, lines), lines), dres_ref, raw, cot_ref),
        )
        for h in range(halves):
            all_sent(1, h)
            last_core[h].wait_send()
        for copy in batches:
            copy.wait()
        for copy in late_copies:
            copy.wait_send()

    shape = jax.ShapeDtypeStruct
    anywhere = pl.BlockSpec(memory_space=pl.ANY)
    near = pl.BlockSpec(memory_space=pltpu.VMEM)
    sems = pltpu.SemaphoreType.DMA
    flops = 2 * 9 * halves * tall * blocks * width * units
    results = pl.pallas_call(
        kernel,
        out_shape=(
            shape((total_rows, width), bf16),
            shape((total_rows, width), f32),
            shape((1, width), f32),
            shape((halves, outer, chips, both, width), bf16),
            shape((halves, outer, chips, both, width), bf16),
        )
        + (shape((3, slab, units), bf16),) * (inner - 1)
        + (
            shape((outer, slab, units), bf16),
            shape((outer, slab, units), bf16),
            shape((outer, units, slab), bf16),
        )
        * inner,
        in_specs=[anywhere] * (parts + 1) + [near] * 3,
        out_specs=(near, near, near) + (anywhere,) * (2 + inner - 1 + 3 * inner),
        scratch_shapes=[
            pltpu.VMEM((width, units), bf16),
            pltpu.VMEM((width, units), bf16),
            pltpu.VMEM((width, units), bf16),
            pltpu.VMEM((halves, per, both, width), bf16),
            pltpu.VMEM((2, halves, per, both, width), bf16),
            pltpu.VMEM((blocks, halves, tall, units), bf16),
            pltpu.VMEM((blocks, halves, tall, units), bf16),
            pltpu.VMEM((blocks, halves, tall, units), bf16),
            pltpu.VMEM((blocks, halves, tall, units), bf16),
            pltpu.VMEM((blocks, halves, tall, units), bf16),
            pltpu.VMEM((units, halves * tall), bf16),
            pltpu.VMEM((units, width), f32),
            pltpu.VMEM((units, width), f32),
            pltpu.VMEM((units, width), f32),
            pltpu.VMEM((2, slab, units), bf16),
            pltpu.VMEM((units, slab), bf16),
            pltpu.VMEM((halves, per, count, width), bf16),
            pltpu.VMEM((halves, blocks, per, count, width), bf16),
            pltpu.VMEM((halves, held, count, width), f32),
            pltpu.VMEM((halves, outer, count, width), f32),
            pltpu.VMEM((halves, links, count, width), bf16),
            pltpu.VMEM((halves, links, count, width), bf16),
            pltpu.VMEM((halves, outer - 1, count, width), bf16),
            pltpu.VMEM((halves, outer - 1, count, width), bf16),
            pltpu.VMEM((total_rows, width), f32),
            pltpu.VMEM((total_rows, width), bf16),
            sems((2, halves, outer)),
            sems((2, halves, outer)),
            sems((2, halves, outer, chips)),
            sems((2, halves, outer, chips)),
            sems((2, halves, outer, chips)),
            sems((2, halves, outer, chips)),
            sems((2, halves, blocks)),
            sems((2, halves, blocks)),
            sems((2, halves, links)),
            sems((2, halves, links)),
            sems((2, halves, outer)),
            sems((2, halves, outer)),
            sems((2, halves, blocks)),
            sems((2, halves)),
            sems((blocks, 2 * halves)),
            sems((inner * outer, 3)),
            sems((3,)),
            sems((inner,)),
            sems((inner,)),
        ],
        compiler_params=pltpu.CompilerParams(
            collective_id=2, has_side_effects=True, vmem_limit_bytes=62 * 2**20
        ),
        cost_estimate=pl.CostEstimate(flops=flops, bytes_accessed=64 * 2**20, transcendentals=0),
    )(*pieces.values(), rows_low, resid, cotangent, gain)
    grads = results[5 + inner - 1 :]
    return results[:3] + ([[grads[j * 3 + c] for j in range(inner)] for c in range(3)],)


def close_rows(at_rows, dres_ref, raw, cot_ref):
    dres_ref[at_rows] = raw[at_rows] + cot_ref[at_rows].astype(jnp.float32)


def local(
    tokens,
    cotangent,
    block_ids,
    w_qkv,
    m_qkv,
    v_qkv,
    w_out,
    m_out,
    v_out,
    w_gu,
    m_gu,
    v_gu,
    w_down,
    m_down,
    v_down,
    gains,
    gain_m,
    gain_v,
):
    grid = Grid()
    local_x = tokens[0]
    gain_count = gains.shape[0]
    tables = rope_tables(local_x.shape[0] * grid.tensor, HEAD)
    pieces, kept = open_call(
        w_qkv,
        w_out,
        gains,
        local_x,
        w_gu,
        w_down,
        tables,
        block_ids[0],
    )
    full_qkv, full_out, seq_x, gain_rows = kept[:4]
    hats, scales, q_low, k_low, v_low, log_total, context_low = kept[4:11]
    attn_hat, o_scale, resid, resid_low, tops = kept[11:]
    output, d_resid, gain_last, unit_grads = unit_kernel_call(
        resid_low, resid, cotangent[0], gain_rows, pieces
    )
    part_gu, part_down, part_qkv, part_out, part_gains, tops, grad_tokens = attend_back_call(
        d_resid,
        attn_hat,
        o_scale,
        gain_rows,
        full_out,
        context_low,
        q_low,
        k_low,
        v_low,
        log_total,
        hats,
        scales,
        tables,
        block_ids[0],
        seq_x,
        full_qkv,
        gain_last,
        tops,
        unit_grads,
    )
    part_gains = part_gains[:gain_count]
    head_top = tops[: w_qkv.shape[2] // HEAD, 0]
    factor = clip_tau / jnp.maximum(head_top, clip_tau)
    column = jnp.repeat(jnp.sqrt(factor), HEAD)
    column_scale = jnp.stack([column, column, jnp.ones_like(column)])[:, None, :]
    new_qkv, new_m_qkv, new_v_qkv = adam_step(
        w_qkv, part_qkv, m_qkv, v_qkv, rate_matrix, weight_decay
    )
    new_qkv = new_qkv * column_scale
    new_out, new_m_out, new_v_out = adam_step(
        w_out, part_out, m_out, v_out, rate_matrix, weight_decay
    )
    new_gu, new_m_gu, new_v_gu = adam_step(
        w_gu, part_gu.astype(jnp.float32), m_gu, v_gu, rate_matrix, weight_decay
    )
    new_down, new_m_down, new_v_down = adam_step(
        w_down, part_down.astype(jnp.float32), m_down, v_down, rate_matrix, weight_decay
    )
    new_gains, new_gain_m, new_gain_v = adam_step(gains, part_gains, gain_m, gain_v, rate_gain, 0.0)
    return (
        output[None],
        grad_tokens[None],
        new_qkv,
        new_m_qkv,
        new_v_qkv,
        new_qkv.astype(jnp.bfloat16),
        new_out,
        new_m_out,
        new_v_out,
        new_out.astype(jnp.bfloat16),
        new_gu,
        new_m_gu,
        new_v_gu,
        new_gu.astype(jnp.bfloat16),
        new_down,
        new_m_down,
        new_v_down,
        new_down.astype(jnp.bfloat16),
        new_gains,
        new_gain_m,
        new_gain_v,
        factor,
    )


def solution(mesh):
    return jax.shard_map(
        local,
        mesh=mesh,
        in_specs=(
            P("dp", "tensor", None),
            P("dp", "tensor", None),
            P("dp", None),
            P(None, "dp", "tensor"),
            P(None, "dp", "tensor"),
            P(None, "dp", "tensor"),
            P("tensor", "dp"),
            P("tensor", "dp"),
            P("tensor", "dp"),
            P(None, "dp", "tensor"),
            P(None, "dp", "tensor"),
            P(None, "dp", "tensor"),
            P("tensor", "dp"),
            P("tensor", "dp"),
            P("tensor", "dp"),
            P(None, "dp"),
            P(None, "dp"),
            P(None, "dp"),
        ),
        out_specs=(
            P("dp", "tensor", None),
            P("dp", "tensor", None),
            P(None, "dp", "tensor"),
            P(None, "dp", "tensor"),
            P(None, "dp", "tensor"),
            P(None, "dp", "tensor"),
            P("tensor", "dp"),
            P("tensor", "dp"),
            P("tensor", "dp"),
            P("tensor", "dp"),
            P(None, "dp", "tensor"),
            P(None, "dp", "tensor"),
            P(None, "dp", "tensor"),
            P(None, "dp", "tensor"),
            P("tensor", "dp"),
            P("tensor", "dp"),
            P("tensor", "dp"),
            P("tensor", "dp"),
            P(None, "dp"),
            P(None, "dp"),
            P(None, "dp"),
            P("tensor"),
        ),
        check_vma=False,
    )
```

```python
import jax
import jax.numpy as jnp
import numpy as np
from jax import lax
from jax.experimental import pallas as pl
from jax.experimental.pallas import tpu as pltpu
from jax.sharding import PartitionSpec as P

HEAD = 128
STEP = 5


norm_eps = 1e-06
rope_base = 500000.0
beta_one = 0.9
beta_two = 0.95
rate_matrix = 0.01
rate_gain = 0.6
weight_decay = 0.1
adam_eps = 1e-08
clip_tau = 9.0
masked_value = -1e30


def rope_tables(length, size):
    half = size // 2
    freq = np.float32(rope_base) ** (-(np.arange(half, dtype=np.float32) * np.float32(2.0 / size)))
    angle = np.arange(length, dtype=np.float32)[:, None] * freq[None, :]
    angle = np.concatenate([angle, angle], axis=1)
    return (jnp.asarray(np.cos(angle)), jnp.asarray(np.sin(angle)))


def adam_step(param, grad, first, second, rate, decay):
    first = beta_one * first + (1.0 - beta_one) * grad
    second = beta_two * second + (1.0 - beta_two) * grad * grad
    fix_one = 1.0 - beta_one**STEP
    fix_two = 1.0 - beta_two**STEP
    update = first / fix_one / (jnp.sqrt(second / fix_two) + adam_eps)
    return (param - rate * (update + decay * param), first, second)


class Grid:
    def __init__(self):
        self.dp = lax.axis_size("dp")
        self.tensor = lax.axis_size("tensor")
        self.inner = 1
        while self.inner * self.inner * 4 <= self.dp:
            self.inner *= 2
        self.outer = self.dp // self.inner
        self.chips = self.tensor // 2
        self.dp_at = lax.axis_index("dp")
        self.tensor_at = lax.axis_index("tensor")
        self.inner_at = self.dp_at % self.inner
        self.chip_at = self.tensor_at // 2
        self.core_at = self.tensor_at % 2
        self.outer_at = self.dp_at // self.inner

    def path_of(self, index):
        column, row = index // self.inner, index % self.inner
        return row * self.outer + column + (row % 2) * (self.outer - 1 - 2 * column)

    def outer_flip(self, index, step):
        result = 0
        for bit in bits(self.outer):
            side = index // bit % 2
            result = result + bit * (1 - side if step & bit else side)
        return result

    def index_of(self, place):
        row, column = place // self.outer, place % self.outer
        return (column + (row % 2) * (self.outer - 1 - 2 * column)) * self.inner + row


def bits(count):
    return [1 << k for k in range(count.bit_length() - 1)]


def greet(peers):
    barrier = pltpu.get_barrier_semaphore()
    for peer in peers:
        pl.semaphore_signal(barrier, inc=1, device_id=peer, device_id_type=pl.DeviceIdType.MESH)
    pl.semaphore_wait(barrier, len(peers))


def attend_back_call(
    d_resid, attn_hat, o_scale, gain_rows, full_out, context, q_low, k_low, v_low, lse, hats, scales,
    tables, blocks, seq, full_qkv, gain_last, tops, unit_grads,
):
    grid = Grid()
    n, outer, inner, chips, tensor = grid.dp, grid.outer, grid.inner, grid.chips, grid.tensor
    count, width = d_resid.shape
    length, span = context.shape
    heads = span // HEAD
    slab, units = unit_grads[0][0].shape[1:]
    thin = width // n
    half = span // 2
    tall = min(256, length)
    tile = 512
    lines = 32
    ring = 8 + 2
    gain_item, top_item = 8, 9
    bf16, f32 = jnp.bfloat16, jnp.float32
    mesh_id = pl.DeviceIdType.MESH
    flat_grads = [unit_grads[c][j] for j in range(inner) for c in range(3)]
    some = len(flat_grads)
    z_steps = list(range(1, outer))

    def kernel(*refs):
        fixed, far_in, grads_in = refs[:16], refs[16:19], refs[19 : 19 + some]
        rest = refs[19 + some :]
        body(*fixed, far_in, grads_in, *rest)

    def body(
        dres_ref, hat_ref, o_scale_ref, gain_ref, out_w, ctx, q_ref, k_ref, v_ref, lse_ref, scale_ref,
        cos_ref, sin_ref, id_row, last_ref, tops_ref, far_in, grads_in,
        gu_out, down_out, part_ref, part_out, gains_out, tops_out, tokens_out,
        hats, seq, qkv_w, seq_do, d_ctx, d_q, d_k, d_v, d_low, probs_low, id_col, whole, terms, row_terms, turned,
        land, land_gain, land_top, peer_terms, inners, peer_inners,
        gu_land, gu_sum, down_land, down_sum, core_send, core_land, hold, chip_send, chip_land,
        s_ring, r_ring, s_row, r_row, s_in, r_in, s_y, r_y, s_z, r_z, s_core, r_core, s_chip, r_chip, s_gain, r_gain, local,
    ):
        hats_in, seq_in, qkv_in = far_in
        g = Grid()

        def tensor_peer(k, flip):
            core = 1 - g.core_at if flip else g.core_at
            return (g.dp_at, lax.rem(g.chip_at + k + chips, chips) * 2 + core)

        def dp_peer(s, j):
            across = g.outer_flip(g.outer_at, s) * inner
            return (across + lax.rem(g.inner_at + j + inner, inner), g.tensor_at)

        place = g.path_of(g.dp_at)
        after_dp = (g.index_of(lax.rem(place + 1, n)), g.tensor_at)
        before_dp = (g.index_of(lax.rem(place + n - 1, n)), g.tensor_at)
        near = [tensor_peer(k, f) for k in range(chips) for f in (0, 1) if (k, f) != (0, 0)]
        far = [dp_peer(s, 0) for s in range(1, outer)] + [dp_peer(0, j) for j in range(1, inner)]
        greet(near + far + [after_dp, before_dp])

        def remote(src, dst, send, recv, peer):
            copy = pltpu.make_async_remote_copy(
                src_ref=src, dst_ref=dst, send_sem=send, recv_sem=recv,
                device_id=peer, device_id_type=mesh_id,
            )
            copy.start()
            return copy

        def fetch(src, dst, at):
            copy = pltpu.make_async_copy(src, dst, local.at[at])
            copy.start()
            return copy

        def dot(a, b, contract):
            return lax.dot_general(a, b, (contract, ((), ())), preferred_element_type=f32)

        def looped(total, make):
            lax.fori_loop(0, total, lambda i, c: (make(i), c)[1], 0, unroll=total <= 4)

        def rows_of(i, size):
            return pl.ds(pl.multiple_of(i * size, size), size)

        sent = []
        y_copies = {}
        sum_steps = [(c, s) for c in range(3) for s in z_steps + [0]]
        for c, s in sum_steps:
            for j in range(1, inner):
                copy = remote(
                    grads_in[j * 3 + c].at[s],
                    down_land.at[j - 1, s] if c == 2 else gu_land.at[j - 1, c, s],
                    s_y.at[j, c, s],
                    r_y.at[j, c, s],
                    dp_peer(0, j),
                )
                y_copies[j, c, s] = copy
                sent.append(copy)
        own_refs = (gu_sum.at[0], gu_sum.at[1], down_sum)
        own_grads = [fetch(grads_in[c], own_refs[c], c) for c in range(3)]
        fetched = [fetch(hats_in, hats, 3), fetch(seq_in, seq, 4), fetch(qkv_in, qkv_w, 5)]
        z_copies = []
        keeps = []

        def unit_sums(times):
            for _ in range(times):
                if sum_steps:
                    unit_sum(*sum_steps.pop(0))

        def unit_sum(c, s):
            if s == (z_steps + [0])[0]:
                own_grads[c].wait()
            for j in range(1, inner):
                y_copies[j, c, s].wait_recv()

            def add_gu(i):
                rows = rows_of(i, 64)
                total = gu_sum[c, s, rows].astype(f32)
                for j in range(1, inner):
                    total = total + gu_land[j - 1, c, s, rows].astype(f32)
                gu_sum[c, s, rows] = total.astype(bf16)

            def add_down(i):
                rows = rows_of(i, 64)
                total = down_sum[s, rows].astype(f32)
                for j in range(1, inner):
                    total = total + down_land[j - 1, s, rows].astype(f32)
                down_sum[s, rows] = total.astype(bf16)

            there = rows_of(g.outer_at, units)
            if c == 2:
                looped(units // 64, add_down)
                src, dst = down_sum.at[s], down_out.at[there]
            else:
                looped(slab // 64, add_gu)
                src, dst = gu_sum.at[c, s], gu_out.at[c, :, there]
            if s:
                z_copies.append(remote(src, dst, s_z.at[c, s], r_z.at[c, s], dp_peer(s, 0)))
            else:
                keeps.append(fetch(src, dst, 6 + c))

        def way_of(item):
            return 1 if item >= 8 else 1 - 2 * (item // 4)

        def own(item, away):
            index = g.index_of(lax.rem(place - way_of(item) * away + 2 * n, n))
            if item == gain_item:
                return terms.at[index]
            if item == top_item:
                return tops_ref
            side, c = item // 4, item % 4
            return whole.at[c, pl.ds(side * half, half), rows_of(index, thin)]

        def landed(step, item):
            if item == gain_item:
                return land_gain.at[step]
            if item == top_item:
                return land_top.at[step]
            return land.at[step, item]

        hops = {}
        on_path = {}

        def hop(step, item):
            hops[step, item] = remote(
                own(item, 1) if step == 0 else landed(step - 1, item),
                landed(step, item),
                s_ring.at[step, item],
                r_ring.at[step, item],
                after_dp if way_of(item) == 1 else before_dp,
            )

        def depart(*items):
            for item in items:
                on_path[item] = 0
                hop(0, item)

        def advance(*items):
            for item in items:
                step = on_path.get(item, n) + 1
                if step >= n:
                    continue
                on_path[item] = step
                hops[step - 1, item].wait_recv()
                here = landed(step - 1, item)
                if item == top_item:
                    summed = jnp.maximum(here[...], tops_ref[...])
                else:
                    summed = here[...].astype(f32) + own(item, step + 1)[...].astype(f32)
                if step < n - 1:
                    here[...] = summed.astype(here.dtype)
                    hop(step, item)
                elif item == gain_item:
                    gains_out[...] = summed
                elif item == top_item:
                    tops_out[...] = summed
                else:
                    side, c = item // 4, item % 4
                    span_half = pl.ds(side * half, half)
                    if c == 3:
                        part_out[span_half] = summed
                    else:
                        part_ref[c, :, span_half] = summed.T

        def matrix_grad(c, left, right):
            turned[...] = left.T

            def columns(i):
                cols = rows_of(i, tile)
                whole[c, :, cols] = dot(turned[...], right[:, cols], ((1,), (0,))).astype(bf16)

            looped(width // tile, columns)

        t_at = g.tensor_at
        mine = rows_of(t_at, count)

        def open_rows(i, total):
            at = rows_of(i, lines)
            value, hat = dres_ref[at], hat_ref[at]
            upstream = value * gain_ref[2:3]
            mean = jnp.mean(upstream * hat, axis=1, keepdims=True)
            d_attn = (o_scale_ref[at] * (upstream - hat * mean)).astype(bf16)
            seq_do[pl.ds(pl.multiple_of(t_at * count + i * lines, lines), lines)] = d_attn
            return total + jnp.sum(value * hat, axis=0, keepdims=True)

        gain_attn = lax.fori_loop(0, count // lines, open_rows, jnp.zeros((1, width), f32))
        row_terms[0] = jnp.zeros((8, width), f32)
        row_terms[0, 2:3] = gain_attn
        row_terms[0, 3:4] = last_ref[...]
        moves, passed = [], []

        def row_copy(slot, index, peer):
            at = rows_of(index, count)
            copy = remote(seq_do.at[at], seq_do.at[at], s_row.at[slot], r_row.at[slot], peer)
            sent.append(copy)
            return copy

        for k in range(1, chips):
            moves.append(row_copy(k - 1, t_at, tensor_peer(k, 0)))
        to_core = row_copy(chips - 1, t_at, tensor_peer(0, 1))
        id_col[...] = jnp.broadcast_to(id_row[...], (128, length)).T
        unit_sums(1)
        scale = HEAD ** (-0.5)
        for h in range(heads):
            cols = slice(h * HEAD, (h + 1) * HEAD)

            def weigh(i, c, cols=cols, h=h):
                at = rows_of(i, tall)
                raw = dot(q_ref[at, cols], k_ref[:, cols], ((1,), (1,))) * scale
                masked = jnp.where(id_row[...] <= id_col[at, 0:1], raw, masked_value)
                probs_low[h, at] = jnp.exp(masked - lse_ref[at, h : h + 1]).astype(bf16)
                return c

            lax.fori_loop(0, length // tall, weigh, 0, unroll=length // tall <= 4)
            if 2 * (h + 1) == heads:
                unit_sums(1)
        for k in range(1, chips):
            moves[k - 1].wait_recv()
            source = lax.rem(g.chip_at - k + chips, chips) * 2 + g.core_at
            passed.append(row_copy(chips - 1 + k, source, tensor_peer(0, 1)))
        to_core.wait_recv()
        unit_sums(1)
        for copy in passed:
            copy.wait_recv()

        def context_grad(i):
            at = rows_of(i, tall)
            d_ctx[at] = dot(seq_do[at], out_w[...], ((1,), (1,))).astype(bf16)

        looped(length // tall, context_grad)
        unit_sums(1)

        for h in range(heads):
            cols = slice(h * HEAD, (h + 1) * HEAD)

            def head(i, c, cols=cols, h=h):
                at = rows_of(i, tall)
                q_part, ctx_part = q_ref[at, cols], d_ctx[at, cols]
                probs_part = probs_low[h, at]
                probs = probs_part.astype(f32)
                d_probs = dot(ctx_part, v_ref[:, cols], ((1,), (1,)))
                mean = jnp.sum(probs * d_probs, axis=1, keepdims=True)
                d_scores = (probs * (d_probs - mean)).astype(bf16)
                d_q[at, cols] = dot(d_scores, k_ref[:, cols], ((1,), (0,))) * scale
                key = dot(d_scores, q_part, ((0,), (0,))) * scale
                value = dot(probs_part, ctx_part, ((0,), (0,)))
                d_k[:, cols] = jnp.where(i == 0, key, d_k[:, cols] + key)
                d_v[:, cols] = jnp.where(i == 0, value, d_v[:, cols] + value)
                return c

            d_k[:, cols] = jnp.zeros((length, HEAD), f32)
            d_v[:, cols] = jnp.zeros((length, HEAD), f32)
            lax.fori_loop(0, length // tall, head, 0, unroll=length // tall <= 4)
            unit_sums(1)
        fetched[0].wait()
        sign = jnp.where(lax.broadcasted_iota(jnp.int32, (tall, HEAD), 1) < HEAD // 2, -1.0, 1.0)

        def unrotate(i, sums):
            at = rows_of(i, tall)
            cosine, sine = cos_ref[at], sin_ref[at]
            lane = lax.broadcasted_iota(jnp.int32, (tall, 128), 1)
            columns = jnp.zeros((tall, 128), f32)
            result = []
            for c, grad in ((0, d_q), (1, d_k)):
                total = jnp.zeros((tall, 1), f32)
                terms_row = []
                for h in range(heads):
                    cols = slice(h * HEAD, (h + 1) * HEAD)
                    value = grad[at, cols]
                    back = value * cosine - pltpu.roll(value * sine, HEAD // 2, 1) * sign
                    hat = hats[c, at, cols]
                    terms_row.append(jnp.sum(back * hat, axis=0, keepdims=True))
                    at_head = pl.ds(pl.multiple_of(t_at * span + h * HEAD, HEAD), HEAD)
                    back = back * gain_ref[c : c + 1, at_head]
                    grad[at, cols] = back
                    total = total + jnp.sum(back * hat, axis=1, keepdims=True)
                columns = jnp.where(lane == c, total, columns)
                result.append(sums[c] + jnp.concatenate(terms_row, axis=1))
            inners[:, at] = columns.T[:8]
            return tuple(result)

        zero = jnp.zeros((1, span), f32)
        gain_q, gain_k = lax.fori_loop(0, length // tall, unrotate, (zero, zero))
        offset = rows_of(t_at, span)
        row_terms[0, 0:1, offset] = gain_q
        row_terms[0, 1:2, offset] = gain_k
        in_copies = []
        for k in range(chips):
            for f in (0, 1):
                if (k, f) != (0, 0):
                    at = k * 2 + f - 1
                    in_copies.append(
                        remote(inners, peer_inners.at[at], s_in.at[at], r_in.at[at], tensor_peer(k, f))
                    )
        sent.extend(in_copies)
        first = remote(row_terms.at[0], peer_terms.at[0], s_gain.at[0], r_gain.at[0], tensor_peer(0, 1))
        matrix_grad(3, ctx[...], seq_do)
        depart(3, 7)
        for copy in in_copies:
            copy.wait_recv()
        first.wait_recv()
        row_terms[1] = row_terms[0] + peer_terms[0]
        others = [
            remote(row_terms.at[1], peer_terms.at[k], s_gain.at[k], r_gain.at[k], tensor_peer(k, 0))
            for k in range(1, chips)
        ]
        unit_sums(1)

        def normed(i):
            at = rows_of(i, tall)
            sums = inners[:, at]
            for other in range(tensor - 1):
                sums = sums + peer_inners[other, :, at]
            column = jnp.concatenate([sums, jnp.zeros((120, tall), f32)], axis=0).T / width
            for c, grad in ((0, d_q), (1, d_k)):
                value = grad[at] - hats[c, at] * column[:, c : c + 1]
                d_low[c, at] = (scale_ref[at, c : c + 1] * value).astype(bf16)
            d_low[2, at] = d_v[at].astype(bf16)

        looped(length // tall, normed)
        fetched[1].wait()
        for c in (2, 0, 1):
            matrix_grad(c, d_low[c], seq)
            depart(c, c + 4)
            unit_sums(1)

        for copy in others:
            copy.wait_recv()

        def place_terms(i, c):
            cols = pl.ds(pl.multiple_of(i * thin, thin), thin)
            total = row_terms[1, :, cols]
            for k in range(1, chips):
                total = total + peer_terms[k, :, cols]
            terms[i] = total
            return c

        lax.fori_loop(0, n, place_terms, 0)

        depart(gain_item, top_item)
        unit_sums(len(sum_steps))

        fetched[2].wait()
        chip_order = list(range(1, chips)) + [0]
        core_copies, chip_copies = {}, {}

        def token_rows(k, flip, store):
            chip = lax.rem(g.chip_at + k, chips)
            core = 1 - g.core_at if flip else g.core_at
            at = rows_of(chip * 2 + core, count)

            def columns(i):
                cols = rows_of(i, tile)
                total = dot(d_low[0, at], qkv_w[0, cols], ((1,), (1,)))
                for c in (1, 2):
                    total = total + dot(d_low[c, at], qkv_w[c, cols], ((1,), (1,)))
                store(cols, total)

            looped(width // tile, columns)

        duties = []
        for k in chip_order:

            def away(k=k):
                def store(cols, value):
                    core_send[k, :, cols] = value.astype(bf16)

                token_rows(k, True, store)
                core_copies[k] = remote(
                    core_send.at[k], core_land.at[k], s_core.at[k], r_core.at[k], tensor_peer(0, 1)
                )

            def here(k=k):
                def store(cols, value):
                    hold[k, :, cols] = value

                token_rows(k, False, store)

            def join(k=k):
                core_copies[k].wait_recv()

                def add(i):
                    at = rows_of(i, lines)
                    chip_send[k - 1, at] = (hold[k, at] + core_land[k, at].astype(f32)).astype(bf16)

                looped(count // lines, add)
                chip_copies[k] = remote(
                    chip_send.at[k - 1], chip_land.at[k - 1], s_chip.at[k], r_chip.at[k], tensor_peer(k, 0)
                )

            duties += [away, here] + ([join] if k else [])

        def close_tokens():
            core_copies[0].wait_recv()
            for k in range(1, chips):
                chip_copies[k].wait_recv()

            def close(i):
                at = rows_of(i, lines)
                total = dres_ref[at] + hold[0, at] + core_land[0, at].astype(f32)
                for k in range(1, chips):
                    total = total + chip_land[k - 1, at].astype(f32)
                tokens_out[at] = total

            looped(count // lines, close)

        duties.append(close_tokens)
        per_step = -(-len(duties) // (n - 2))
        for step in range(1, n):
            advance(3, 7, 2, 6, 0, 4, 1, 5, gain_item, top_item)
            for _ in range(per_step):
                if duties:
                    duties.pop(0)()
        for copy in z_copies:
            copy.wait()
        for copy in keeps:
            copy.wait()
        for copy in sent + list(hops.values()) + list(core_copies.values()):
            copy.wait_send()
        for copy in list(chip_copies.values()) + [first] + others:
            copy.wait_send()

    shape = jax.ShapeDtypeStruct
    anywhere = pl.BlockSpec(memory_space=pl.ANY)
    vmem = pl.BlockSpec(memory_space=pltpu.VMEM)
    sems = pltpu.SemaphoreType.DMA
    results = pl.pallas_call(
        kernel,
        out_shape=(
            shape((2, slab, outer * units), bf16),
            shape((outer * units, slab), bf16),
            shape((3, thin, span), f32),
            shape((span, thin), f32),
            shape((8, thin), f32),
            shape(tops.shape, f32),
            shape((count, width), f32),
        ),
        in_specs=[vmem] * 16 + [anywhere] * 3 + [anywhere] * some,
        out_specs=(anywhere,) * 2 + (vmem,) * 5,
        scratch_shapes=[
            pltpu.VMEM(hats.shape, f32),
            pltpu.VMEM(seq.shape, bf16),
            pltpu.VMEM(full_qkv.shape, bf16),
            pltpu.VMEM((length, width), bf16),
            pltpu.VMEM((length, span), bf16),
            pltpu.VMEM((length, span), f32),
            pltpu.VMEM((length, span), f32),
            pltpu.VMEM((length, span), f32),
            pltpu.VMEM((3, length, span), bf16),
            pltpu.VMEM((heads, length, length), bf16),
            pltpu.VMEM((length, 128), jnp.int32),
            pltpu.VMEM((4, span, width), bf16),
            pltpu.VMEM((n, 8, thin), f32),
            pltpu.VMEM((2, 8, width), f32),
            pltpu.VMEM((span, length), bf16),
            pltpu.VMEM((n - 1, 8, half, thin), bf16),
            pltpu.VMEM((n - 1, 8, thin), f32),
            pltpu.VMEM((n - 1,) + tops.shape, f32),
            pltpu.VMEM((chips, 8, width), f32),
            pltpu.VMEM((8, length), f32),
            pltpu.VMEM((tensor - 1, 8, length), f32),
            pltpu.VMEM((max(inner - 1, 1), 2, outer, slab, units), bf16),
            pltpu.VMEM((2, outer, slab, units), bf16),
            pltpu.VMEM((max(inner - 1, 1), outer, units, slab), bf16),
            pltpu.VMEM((outer, units, slab), bf16),
            pltpu.VMEM((chips, count, width), bf16),
            pltpu.VMEM((chips, count, width), bf16),
            pltpu.VMEM((chips, count, width), f32),
            pltpu.VMEM((max(chips - 1, 1), count, width), bf16),
            pltpu.VMEM((max(chips - 1, 1), count, width), bf16),
            sems((n - 1, ring)),
            sems((n - 1, ring)),
            sems((2 * chips - 1,)),
            sems((2 * chips - 1,)),
            sems((tensor - 1,)),
            sems((tensor - 1,)),
            sems((inner, 3, outer)),
            sems((inner, 3, outer)),
            sems((3, outer)),
            sems((3, outer)),
            sems((chips,)),
            sems((chips,)),
            sems((chips,)),
            sems((chips,)),
            sems((chips,)),
            sems((chips,)),
            sems((9,)),
        ],
        compiler_params=pltpu.CompilerParams(
            collective_id=1, has_side_effects=True, vmem_limit_bytes=61 * 2**20
        ),
    )(
        d_resid, attn_hat, o_scale, gain_rows, full_out, context, q_low, k_low, v_low, lse, scales,
        tables[0], tables[1], blocks[None, :], gain_last, tops,
        hats, seq, full_qkv, *flat_grads,
    )
    return results


def open_call(w_qkv, w_out, gains, rows, w_gu, w_down, tables, blocks):
    grid = Grid()
    n, outer, inner = grid.dp, grid.outer, grid.inner
    chips, tensor = grid.chips, grid.tensor
    count, width = rows.shape
    length = count * tensor
    lead, slab, span = w_qkv.shape
    gain_count = gains.shape[0]
    half = slab // 2
    part_tall = span // 2
    heads = span // HEAD
    shard_units = w_gu.shape[2]
    units = shard_units // outer
    places = [(j, s) for j in range(inner) for s in range(outer) if not (j and s == outer - 1)]
    parts = len(places)
    ring = 2 * lead + 3
    steps = list(range(1, outer))
    tall = min(256, length)
    tile = 512
    lines = 32
    bf16, f32 = jnp.bfloat16, jnp.float32
    mesh_id = pl.DeviceIdType.MESH

    def kernel(*refs):
        body(*refs[:10], dict(zip(places, refs[10 : 10 + parts])), *refs[10 + parts :])

    def body(
        qkv_any, out_any, rows_any, gu_any, down_any, gains_ref, cos_ref, sin_ref, id_row, rows_ref,
        pieces, qkv_out, flat_out, seq_out,
        gain_rows, hat_ref, scale_ref, q_low, k_low, v_low, lse_ref, context, attn_hat, o_scale, resid, resid_low, top_ref,
        qkv_ref, out_w_ref, seq_ref, all_gains, qkv_wide, out_wide, gu_wide, down_wide, cast, id_col,
        square, squares, core_send, core_land, hold, chip_send, chip_land,
        s_ring, r_ring, s_row, r_row, s_z, r_z, s_y, r_y, s_sq, r_sq, s_core, r_core, s_chip, r_chip, local,
    ):
        g = Grid()

        def tensor_peer(k, flip):
            core = 1 - g.core_at if flip else g.core_at
            return (g.dp_at, lax.rem(g.chip_at + k + chips, chips) * 2 + core)

        def dp_peer(s, j):
            across = g.outer_flip(g.outer_at, s) * inner
            return (across + lax.rem(g.inner_at + j + inner, inner), g.tensor_at)

        near = [tensor_peer(k, f) for k in range(chips) for f in (0, 1) if (k, f) != (0, 0)]
        far = [dp_peer(s, 0) for s in range(1, outer)]
        far += [dp_peer(0, j) for j in sorted({1 % inner, inner - 1} - {0})]
        t_at = g.tensor_at
        place = g.path_of(g.dp_at)
        after = (g.index_of(lax.rem(place + 1, n)), t_at)
        before = (g.index_of(lax.rem(place + n - 1, n)), t_at)
        firsts = []
        for at, (src, dst) in enumerate(((qkv_any, qkv_wide), (out_any, out_wide))):
            firsts.append(pltpu.make_async_copy(src, dst, local.at[3 + at]))
            firsts[-1].start()
        greet(near + far + [after, before])

        def remote(src, dst, send, recv, peer):
            copy = pltpu.make_async_remote_copy(
                src_ref=src, dst_ref=dst, send_sem=send, recv_sem=recv,
                device_id=peer, device_id_type=mesh_id,
            )
            copy.start()
            return copy

        def dot(a, b, contract):
            return lax.dot_general(a, b, (contract, ((), ())), preferred_element_type=f32)

        def looped(total, make):
            lax.fori_loop(0, total, lambda i, c: (make(i), c)[1], 0, unroll=total <= 4)

        def rows_of(i, size):
            return pl.ds(pl.multiple_of(i * size, size), size)

        def fetch(src, dst, at):
            copy = pltpu.make_async_copy(src, dst, local.at[at])
            copy.start()
            return copy

        def views(item, index):
            if item == ring - 1:
                return 1, all_gains.at[index]
            if item >= 2 * lead:
                side = item - 2 * lead
                part = pl.ds(side * part_tall, part_tall)
                return 1 - 2 * side, out_w_ref.at[part, rows_of(index, slab)]
            side, c = item // lead, item % lead
            at = pl.ds(pl.multiple_of(index * slab + side * half, half), half)
            return 1 - 2 * side, qkv_ref.at[c, at]

        hops = {}

        def hop(step, item):
            way = views(item, 0)[0]
            index = g.index_of(lax.rem(place - way * step + n, n))
            _, view = views(item, index)
            hops[step, item] = remote(
                view,
                view,
                s_ring.at[step, item],
                r_ring.at[step, item],
                after if way == 1 else before,
            )

        def row_copy(slot, index, peer, src=None):
            at = seq_ref.at[rows_of(index, count)]
            return remote(at if src is None else src, at, s_row.at[slot], r_row.at[slot], peer)

        order = [c + side * lead for c in range(lead) for side in (0, 1)]
        order += list(range(2 * lead, ring))
        firsts[0].wait()
        for c in range(lead):

            def cast_own(i, c=c):
                at = rows_of(i, lines)
                there = pl.ds(pl.multiple_of(g.dp_at * slab + i * lines, lines), lines)
                qkv_ref[c, there] = qkv_wide[c, at].astype(bf16)

            looped(slab // lines, cast_own)
            for side in (0, 1):
                hop(0, c + side * lead)
        firsts[1].wait()

        def cast_flat(i):
            at = rows_of(i, lines)
            out_w_ref[at, rows_of(g.dp_at, slab)] = out_wide[at].astype(bf16)

        looped(span // lines, cast_flat)
        empty = jnp.zeros((16 - gain_count, slab), f32)
        all_gains[g.dp_at] = jnp.concatenate([gains_ref[...], empty], axis=0).astype(bf16)
        for item in range(2 * lead, ring):
            hop(0, item)
        row_copies = [
            row_copy(k - 1, t_at, tensor_peer(k, 0), rows_any) for k in range(1, chips)
        ]
        row_copies.append(row_copy(chips - 1, t_at, tensor_peer(0, 1), rows_any))
        wide = [fetch(gu_any, gu_wide, 1), fetch(down_any, down_wide, 2)]
        kept = fetch(rows_any, seq_ref.at[rows_of(t_at, count)], 5)

        def cast_wide(c):
            if c == 0:
                wide[0].wait()

            def cast_rows(i):
                at = rows_of(i, lines)
                cast[c, at] = gu_wide[c, at].astype(bf16)

            looped(slab // lines, cast_rows)

        def cast_turned():
            wide[1].wait()

            def cast_rows(i):
                at = rows_of(i, 256)
                cast[2, :, at] = down_wide[at].T.astype(bf16)

            looped(shard_units // 256, cast_rows)

        def ids():
            id_col[...] = jnp.broadcast_to(id_row[...], (128, length)).T

        shadows = [ids, lambda: cast_wide(0), lambda: cast_wide(1), cast_turned]
        for step in range(1, n - 1):
            for item in order:
                hops[step - 1, item].wait_recv()
                hop(step, item)
            if step <= chips - 1:
                row_copies[step - 1].wait_recv()
                source = lax.rem(g.chip_at - step + chips, chips) * 2 + g.core_at
                row_copies.append(row_copy(chips - 1 + step, source, tensor_peer(0, 1)))
            if shadows:
                shadows.pop(0)()

        def cut(s):
            return cast.at[:, :, rows_of(g.outer_flip(g.outer_at, s), units)]

        z_copies = {}

        for s in steps:
            z_copies[s] = remote(cut(s), pieces[0, s], s_z.at[s], r_z.at[s], dp_peer(s, 0))
        own = fetch(cut(0), pieces[0, 0], 0)
        y_copies = {}

        def pass_on(j, s):
            if (j, s) in pieces:
                src = cut(0) if (j, s) == (1, 0) else pieces[j - 1, s]
                y_copies[j, s] = remote(src, pieces[j, s], s_y.at[j, s], r_y.at[j, s], dp_peer(0, 1))

        pass_on(1, 0)
        duties = []
        for s in steps:

            def duty(s=s):
                z_copies[s].wait_recv()
                pass_on(1, s)

            duties.append(duty)
        for j in range(2, inner):
            for s in range(outer - 1):

                def duty(j=j, s=s):
                    y_copies[j - 1, s].wait_recv()
                    pass_on(j, s)

                duties.append(duty)

        def next_duties(times):
            for _ in range(times):
                if duties:
                    duties.pop(0)()

        for item in order:
            hops[n - 2, item].wait_recv()
        for copy in row_copies[chips - 1 :]:
            copy.wait_recv()
        kept.wait()
        outs = [fetch(qkv_ref, qkv_out, 3), fetch(out_w_ref, flat_out, 4), fetch(seq_ref, seq_out, 5)]

        def spread(i):
            gain_rows[:, rows_of(i, slab)] = all_gains[i].astype(f32)[:8]

        looped(n, spread)

        def project(i):
            at = rows_of(i, tall)
            x = seq_ref[at]
            lane = lax.broadcasted_iota(jnp.int32, (tall, 128), 1)
            sums = jnp.zeros((tall, 128), f32)
            for c in range(2):
                value = dot(x, qkv_ref[c], ((1,), (0,)))
                hat_ref[c, at] = value
                sums = jnp.where(lane == c, jnp.sum(value * value, axis=1, keepdims=True), sums)
            v_low[at] = dot(x, qkv_ref[2], ((1,), (0,))).astype(bf16)
            square[:, at] = sums.T[:8]

        looped(length // tall, project)
        sq_copies = []
        for k in range(chips):
            for f in (0, 1):
                if (k, f) != (0, 0):
                    at = k * 2 + f - 1
                    sq_copies.append(
                        remote(square, squares.at[at], s_sq.at[at], r_sq.at[at], tensor_peer(k, f))
                    )
        for copy in sq_copies:
            copy.wait_recv()
        sign = jnp.where(lax.broadcasted_iota(jnp.int32, (tall, HEAD), 1) < HEAD // 2, -1.0, 1.0)

        def rotate(i):
            at = rows_of(i, tall)
            sums = square[:, at]
            for copy_at in range(tensor - 1):
                sums = sums + squares[copy_at, :, at]
            column = jnp.concatenate([sums, jnp.zeros((120, tall), f32)], axis=0).T
            scales = lax.rsqrt(column / width + norm_eps)
            scale_ref[at] = scales
            cosine, sine = cos_ref[at], sin_ref[at] * sign
            for c, low in ((0, q_low), (1, k_low)):
                hat = hat_ref[c, at] * scales[:, c : c + 1]
                hat_ref[c, at] = hat
                normed = hat * gain_rows[c : c + 1, rows_of(t_at, span)]
                for h in range(heads):
                    cols = slice(h * HEAD, (h + 1) * HEAD)
                    value = normed[:, cols]
                    turned = pltpu.roll(value, HEAD // 2, 1)
                    low[at, cols] = (value * cosine + turned * sine).astype(bf16)

        looped(length // tall, rotate)
        scale = HEAD ** (-0.5)
        top_ref[...] = jnp.full((8, 128), masked_value, f32)
        for h in range(heads):
            cols = slice(h * HEAD, (h + 1) * HEAD)

            def attend(i, best, cols=cols, h=h):
                at = rows_of(i, tall)
                raw = dot(q_low[at, cols], k_low[:, cols], ((1,), (1,))) * scale
                masked = jnp.where(id_row[...] <= id_col[at, 0:1], raw, masked_value)
                top = jnp.max(masked, axis=1, keepdims=True)
                weight = jnp.exp(masked - top)
                total = jnp.sum(weight, axis=1, keepdims=True)
                probs = (weight * (1.0 / total)).astype(bf16)
                context[at, cols] = dot(probs, v_low[:, cols], ((1,), (0,))).astype(bf16)
                lse_ref[at, h : h + 1] = top + jnp.log(total)
                return jnp.maximum(best, jnp.max(top, axis=0, keepdims=True))

            best = lax.fori_loop(
                0, length // tall, attend, jnp.full((1, 1), masked_value, f32), unroll=length // tall <= 4
            )
            top_ref[h : h + 1] = jnp.broadcast_to(best, (1, 128))
            if h + 1 == max(heads // 2, 1):
                next_duties(1)
        next_duties(1)

        def out_rows(k, flip, store):
            chip = lax.rem(g.chip_at + k, chips)
            core = 1 - g.core_at if flip else g.core_at
            at = rows_of(chip * 2 + core, count)

            def columns(i):
                cols = rows_of(i, tile)
                store(cols, dot(context[at], out_w_ref[:, cols], ((1,), (0,))))

            looped(width // tile, columns)

        chip_order = list(range(1, chips)) + [0]
        core_copies, chip_copies = {}, {}
        for k in chip_order:

            def store(cols, value, k=k):
                core_send[k, :, cols] = value.astype(bf16)

            out_rows(k, True, store)
            core_copies[k] = remote(
                core_send.at[k], core_land.at[k], s_core.at[k], r_core.at[k], tensor_peer(0, 1)
            )
        for k in chip_order:

            def store(cols, value, k=k):
                hold[k, :, cols] = value

            out_rows(k, False, store)
            if k:
                core_copies[k].wait_recv()

                def add(i, k=k):
                    at = rows_of(i, lines)
                    chip_send[k - 1, at] = (hold[k, at] + core_land[k, at].astype(f32)).astype(bf16)

                looped(count // lines, add)
                chip_copies[k] = remote(
                    chip_send.at[k - 1], chip_land.at[k - 1], s_chip.at[k], r_chip.at[k], tensor_peer(k, 0)
                )
        core_copies[0].wait_recv()
        for k in range(1, chips):
            chip_copies[k].wait_recv()

        def close(i):
            at = rows_of(i, lines)
            raw = hold[0, at] + core_land[0, at].astype(f32)
            for k in range(1, chips):
                raw = raw + chip_land[k - 1, at].astype(f32)
            scale_o = lax.rsqrt(jnp.mean(raw * raw, axis=1, keepdims=True) + norm_eps)
            hat = raw * scale_o
            attn_hat[at] = hat
            o_scale[at] = scale_o
            value = rows_ref[at].astype(f32) + hat * gain_rows[2:3]
            resid[at] = value
            resid_low[at] = value.astype(bf16)

        looped(count // lines, close)
        next_duties(len(duties))
        own.wait()
        for key, copy in y_copies.items():
            if key[0] == inner - 1:
                copy.wait_recv()
        for copy in outs:
            copy.wait()
        sent = list(hops.values()) + row_copies + list(z_copies.values()) + list(y_copies.values()) + sq_copies
        for copy in sent + list(core_copies.values()) + list(chip_copies.values()):
            copy.wait_send()

    shape = jax.ShapeDtypeStruct
    anywhere = pl.BlockSpec(memory_space=pl.ANY)
    vmem = pl.BlockSpec(memory_space=pltpu.VMEM)
    sems = pltpu.SemaphoreType.DMA
    results = pl.pallas_call(
        kernel,
        out_shape=(shape((3, slab, units), bf16),) * parts
        + (
            shape((lead, width, span), bf16),
            shape((span, width), bf16),
            shape((length, width), bf16),
            shape((8, width), f32),
            shape((2, length, span), f32),
            shape((length, 128), f32),
            shape((length, span), bf16),
            shape((length, span), bf16),
            shape((length, span), bf16),
            shape((length, heads), f32),
            shape((length, span), bf16),
            shape((count, width), f32),
            shape((count, 1), f32),
            shape((count, width), f32),
            shape((count, width), bf16),
            shape((8, 128), f32),
        ),
        in_specs=[anywhere] * 5 + [vmem] * 5,
        out_specs=(anywhere,) * (parts + 3) + (vmem,) * 13,
        scratch_shapes=[
            pltpu.VMEM((lead, width, span), bf16),
            pltpu.VMEM((span, width), bf16),
            pltpu.VMEM((length, width), bf16),
            pltpu.VMEM((n, 16, slab), bf16),
            pltpu.VMEM(w_qkv.shape, f32),
            pltpu.VMEM(w_out.shape, f32),
            pltpu.VMEM(w_gu.shape, f32),
            pltpu.VMEM(w_down.shape, f32),
            pltpu.VMEM((3, slab, shard_units), bf16),
            pltpu.VMEM((length, 128), jnp.int32),
            pltpu.VMEM((8, length), f32),
            pltpu.VMEM((tensor - 1, 8, length), f32),
            pltpu.VMEM((chips, count, width), bf16),
            pltpu.VMEM((chips, count, width), bf16),
            pltpu.VMEM((chips, count, width), f32),
            pltpu.VMEM((max(chips - 1, 1), count, width), bf16),
            pltpu.VMEM((max(chips - 1, 1), count, width), bf16),
            sems((n - 1, ring)),
            sems((n - 1, ring)),
            sems((2 * chips - 1,)),
            sems((2 * chips - 1,)),
            sems((outer,)),
            sems((outer,)),
            sems((inner, outer)),
            sems((inner, outer)),
            sems((tensor - 1,)),
            sems((tensor - 1,)),
            sems((chips,)),
            sems((chips,)),
            sems((chips,)),
            sems((chips,)),
            sems((7,)),
        ],
        compiler_params=pltpu.CompilerParams(
            collective_id=0, has_side_effects=True, vmem_limit_bytes=58 * 2**20
        ),
    )(
        w_qkv, w_out, rows, w_gu, w_down, gains, tables[0], tables[1],
        blocks[None, :], rows,
    )
    return dict(zip(places, results[:parts])), results[parts:]


def unit_kernel_call(rows_low, resid, cotangent, gain, pieces):
    grid = Grid()
    outer, chips, inner = grid.outer, grid.chips, grid.inner
    total_rows, width = rows_low.shape
    slab, units = pieces[0, 0].shape[1:]
    places = list(pieces)
    parts = len(places)
    last = (0, outer - 1)
    halves = 2
    count = total_rows // halves
    both = 2 * count
    per = min(2, chips)
    groups = chips // per
    blocks = outer * groups
    tall = per * both
    held = per if groups > 1 else max(per - 1, 1)
    links = outer * (chips - 1)
    steps = list(range(outer))
    far_first = [0] + steps[2:] + steps[1:2]

    def units_of(of_steps):
        return [(s, i) for s in of_steps for i in range(groups)]

    orders = {
        (0, 0): units_of(far_first),
        (0, 1): units_of(far_first),
        (1, 0): units_of(steps),
        (1, 1): units_of(far_first),
    }
    grad_order = units_of(far_first)
    tile = 512
    wide_tiles = width // tile
    unit_tile = min(256, units)
    lines = 32
    bf16, f32 = jnp.bfloat16, jnp.float32
    mesh_id = pl.DeviceIdType.MESH

    def plan():
        chip_us, core_us, hop_us = 5.6, 0.6, 2.0
        free = {"x": 0.0, "core": 0.0, "z near": 0.0, "z far": 0.0}
        arrive, done, tasks = {("w",): 20.0}, {}, {}

        def send(link, when, us):
            free[link] = max(free[link], when) + us
            return free[link] + hop_us

        def add(name, needs, us, after=None):
            tasks[name] = (needs, us, after)

        def send_outer(s, now):
            return send("z near", now, 8.0) if s == 1 else send("z far", now, 10.5)

        def go(p, h):
            def then(now):
                if (p, h) != (0, 1):
                    for s in steps[1:]:
                        arrive["z", p, h, s] = send_outer(s, now)
                for k in range(1, chips):
                    arrive["x", p, h, 0, k] = send("x", now, chip_us)
                arrive["c", p, h, 0, 0] = send("core", now, core_us)

            return then

        def zf(p, h, s):
            def then(now):
                for k in range(1, chips):
                    arrive["x", p, h, s, k] = send("x", now, chip_us)
                arrive["c", p, h, s, 0] = send("core", now, core_us)
                if (p, h) == (0, 0):
                    arrive["z", 0, 1, s] = send_outer(s, now)

            return then

        def xf(p, h, s, k):
            def then(now):
                arrive["c", p, h, s, k] = send("core", now, core_us)

            return then

        def compute(p, h, s, i):
            def then(now):
                arrive["cr", p, h, s, i] = send("core", now, per * core_us)

            return then

        def cr(p, h, s, i):
            def then(now):
                for k in range(i * per, i * per + per):
                    if k:
                        arrive["xr", p, h, s, k] = send("x", now, chip_us)

            return then

        def xr(p, h, s):
            def then(now):
                if s:
                    arrive["zr", p, h, s] = send_outer(s, now)

            return then

        for p in (0, 1):
            for h in range(halves):
                if p == 0:
                    needs = [("do", ("go", 0, h - 1))] if h else []
                else:
                    needs = [("do", ("between", h))]
                add(("go", p, h), needs, 0.2, go(p, h))
                for s in steps[1:]:
                    add(("zf", p, h, s), [("at", ("z", p, h, s))], 0.2, zf(p, h, s))
                for s in steps:
                    for k in range(1, chips):
                        add(("xf", p, h, s, k), [("at", ("x", p, h, s, k))], 0.2, xf(p, h, s, k))
                order = orders[p, h]
                for n, (s, i) in enumerate(order):
                    needs = [("at", ("c", p, h, s, i * per + j)) for j in range(per)]
                    if n:
                        needs.append(("do", ("front", p, h) + order[n - 1]))
                    add(("load", p, h, s, i), needs, 0.2)
                    needs = [("do", ("load", p, h, s, i)), ("do", ("weights",))]
                    add(("front", p, h, s, i), needs, (2.4, 1.6)[p])
                    needs = [("do", ("front", p, h, s, i))]
                    if n:
                        needs.append(("do", ("cr", p, h) + order[n - 1]))
                    add(("compute", p, h, s, i), needs, (1.6, 2.4)[p], compute(p, h, s, i))
                    needs = [("at", ("cr", p, h, s, i)), ("do", ("compute", p, h, s, i))]
                    add(("cr", p, h, s, i), needs, 0.5, cr(p, h, s, i))
                for s in steps:
                    needs = [("do", ("cr", p, h, s, 0))]
                    needs += [("at", ("xr", p, h, s, k)) for k in range(1, chips)]
                    add(("xr", p, h, s), needs, 0.4, xr(p, h, s))
                for s in steps[1:]:
                    needs = [("at", ("zr", p, h, s)), ("do", ("xr", p, h, 0))]
                    add(("zr", p, h, s), needs, 0.4)
        add(("weights",), [("at", ("w",))], 0.2)
        for h in range(halves):
            needs = [("do", ("zr", 0, h, s)) for s in steps[1:]] + [("do", ("xr", 0, h, 0))]
            add(("between", h), needs, 1.0)
        for n, (s, i) in enumerate(grad_order):
            needs = [("do", ("compute", 1, h, s, i)) for h in range(halves)]
            if n:
                needs.append(("do", ("grads",) + grad_order[n - 1] + (2,)))
            add(("fetch", s, i), needs, 0.2)
            for c in range(3):
                needs = [("do", ("grads", s, i, c - 1) if c else ("fetch", s, i))]
                add(("grads", s, i, c), needs, 2.8)
        written = [(j, s) for j in range(inner) for s in range(outer)]
        for n, at in enumerate(written):
            needs = [("do", ("grads",) + grad_order[-1] + (2,))]
            if n:
                needs = [("do", ("write",) + written[n - 1])]
            add(("write",) + at, needs, 0.6)
        rank = {"compute": 1, "front": 2, "fetch": 2, "grads": 3, "write": 4}
        result = []
        now = 0.0
        while tasks:
            best = None
            for name, (needs, us, then) in tasks.items():
                ready = 0.0
                for kind, key in needs:
                    table = arrive if kind == "at" else done
                    if key not in table:
                        ready = None
                        break
                    ready = max(ready, table[key] + (1.0 if key[0] in ("load", "fetch") else 0.0))
                if ready is None:
                    continue
                key = (max(ready, now), rank.get(name[0], 0))
                if best is None or key < best[0]:
                    best = (key, name)
            (ready, _), name = best
            needs, us, then = tasks.pop(name)
            now = ready + us
            done[name] = now
            if then is not None:
                then(now)
            result.append(name)
        return result

    def kernel(*refs):
        piece_refs = dict(zip(places, refs[:parts]))
        fixed = refs[parts : parts + 9]
        k = parts + 9
        late, grad_refs = refs[k : k + inner - 1], refs[k + inner - 1 : k + inner - 1 + 3 * inner]
        for j in range(1, inner):
            piece_refs[j, outer - 1] = late[j - 1]
        body(piece_refs, *fixed, grad_refs, *refs[k + inner - 1 + 3 * inner :])

    def body(
        piece_refs, rows_ref, resid_ref, cot_ref, gain_ref,
        out_ref, dres_ref, gain_out, all_x, all_dm, grad_refs,
        wg, wu, wd, buf, wide_buf, act, coef_gate, coef_up, d_gate, d_up, turned, acc_gate, acc_up, acc_down, stage, stage_down,
        core_send, core_land, hold, keep, chip_send, chip_land, outer_send, outer_land, raw, d_mlp,
        s_outer, r_outer, s_chip, r_chip, s_core, r_core,
        s_core_sum, r_core_sum, s_chip_sum, r_chip_sum, s_outer_sum, r_outer_sum,
        local, local_own, local_wide, local_w, local_g, s_late, r_late,
    ):
        g = Grid()
        core_peer = (g.dp_at, g.chip_at * 2 + 1 - g.core_at)

        def chip_peer(k):
            return (g.dp_at, lax.rem(g.chip_at + k + chips, chips) * 2 + g.core_at)

        def outer_peer(s):
            return (g.outer_flip(g.outer_at, s) * inner + g.inner_at, g.tensor_at)

        def inner_peer(j):
            return (g.outer_at * inner + lax.rem(g.inner_at + j, inner), g.tensor_at)

        greet(
            [core_peer]
            + [chip_peer(k) for k in range(1, chips)]
            + [outer_peer(s) for s in range(1, outer)]
            + [inner_peer(j) for j in range(1, inner)]
        )

        def remote(src, dst, send, recv, peer):
            copy = pltpu.make_async_remote_copy(
                src_ref=src, dst_ref=dst, send_sem=send, recv_sem=recv,
                device_id=peer, device_id_type=mesh_id,
            )
            copy.start()
            return copy

        def fetch(src, dst, sem):
            copy = pltpu.make_async_copy(src, dst, sem)
            copy.start()
            return copy

        def dot(a, b, contract):
            return lax.dot_general(a, b, (contract, ((), ())), preferred_element_type=f32)

        def looped(total, make):
            lax.fori_loop(0, total, lambda i, c: (make(i), c)[1], 0, unroll=total <= 4)

        def by_lines(make):
            looped(count // lines, lambda i: make(pl.ds(pl.multiple_of(i * lines, lines), lines)))

        def by_tiles(make):
            looped(wide_tiles, lambda i: make(pl.ds(pl.multiple_of(i * tile, tile), tile)))

        weights = (wg, wu, wd)
        fetches = []

        late_copies = []

        def send_late():
            for j in range(1, inner):
                late_copies.append(
                    remote(piece_refs[last], piece_refs[j, last[1]], s_late.at[j], r_late.at[j], inner_peer(j))
                )

        def fetch_weights(which):
            for j, s in which:
                index = g.outer_flip(g.outer_at, s) * inner
                index = index + lax.rem(g.inner_at - j + inner, inner)
                span = pl.ds(pl.multiple_of(index * slab, slab), slab)
                for c in range(3):
                    fetches.append(
                        fetch(piece_refs[j, s].at[c], weights[c].at[span], local_w.at[j * outer + s, c])
                    )

        mine, theirs = pl.ds(0, count), pl.ds(count, count)
        every = (all_x, all_dm)
        copies, sums, loads, own = {}, {}, {}, {}
        unsent = {(p, h): [] for p in (0, 1) for h in range(halves)}

        def track(p, h, copy):
            unsent[p, h].append(copy)
            return copy

        def core_copy(p, h, s, k, src):
            dst = every[p].at[h, s, k, theirs]
            copies["c", p, h, s, k] = track(
                p, h, remote(src, dst, s_core.at[p, h, s, k], r_core.at[p, h, s, k], core_peer)
            )

        def chip_copy(p, h, s, k, src):
            dst = every[p].at[h, s, k, mine]
            copies["x", p, h, s, k] = track(
                p, h, remote(src, dst, s_chip.at[p, h, s, k], r_chip.at[p, h, s, k], chip_peer(k))
            )

        def outer_copy(p, h, s):
            source = (rows_ref, d_mlp)[p].at[pl.ds(h * count, count)]
            dst = every[p].at[h, s, 0, mine]
            copies["z", p, h, s] = track(
                p, h, remote(source, dst, s_outer.at[p, h, s], r_outer.at[p, h, s], outer_peer(s))
            )

        def go(p, h):
            source = (rows_ref, d_mlp)[p].at[pl.ds(h * count, count)]
            if (p, h) != (0, 1):
                for s in steps[1:]:
                    outer_copy(p, h, s)
            for k in range(1, chips):
                chip_copy(p, h, 0, k, source)
            core_copy(p, h, 0, 0, source)
            own[p, h] = fetch(source, every[p].at[h, 0, 0, mine], local_own.at[p, h])
            if p == 0 and h == 0:
                fetch_weights(places)

        def part_out(h, s, i, cols, part_sum):
            for j in range(per):
                own_rows = part_sum[j * both : j * both + count]
                if i * per + j == 0:
                    keep[h, s, :, cols] = own_rows
                else:
                    hold[h, min(j, held - 1), :, cols] = own_rows
                core_send[h, j, :, cols] = part_sum[j * both + count : (j + 1) * both].astype(bf16)

        def forward(h, unit):
            for j in range(units // unit_tile):
                cols = pl.ds(j * unit_tile, unit_tile)
                rows = buf[h].reshape(tall, width)
                gate = dot(rows, wg[:, cols], ((1,), (0,)))
                up = dot(rows, wu[:, cols], ((1,), (0,)))
                sigma = jax.nn.sigmoid(gate)
                silu = gate * sigma
                act[unit, h, :, cols] = (silu * up).astype(bf16)
                coef_up[unit, h, :, cols] = silu.astype(bf16)
                coef_gate[unit, h, :, cols] = (
                    up * sigma * (1.0 + gate * (1.0 - sigma))
                ).astype(bf16)

        def forward_out(h, unit, s, i):
            by_tiles(
                lambda cols: part_out(h, s, i, cols, dot(act[unit, h], wd[cols, :], ((1,), (1,))))
            )

        def backward(h, unit):
            for j in range(units // unit_tile):
                cols = pl.ds(j * unit_tile, unit_tile)
                d_act = dot(buf[h].reshape(tall, width), wd[:, cols], ((1,), (0,)))
                d_gate[unit, h, :, cols] = (d_act * coef_gate[unit, h, :, cols].astype(f32)).astype(bf16)
                d_up[unit, h, :, cols] = (d_act * coef_up[unit, h, :, cols].astype(f32)).astype(bf16)

        def backward_out(h, unit, s, i):
            def into(cols):
                part_sum = dot(d_gate[unit, h], wg[cols, :], ((1,), (1,)))
                part_sum = part_sum + dot(d_up[unit, h], wu[cols, :], ((1,), (1,)))
                part_out(h, s, i, cols, part_sum)

            by_tiles(into)

        def weight_grads(unit, c):
            first = unit == grad_order[0][0] * groups + grad_order[0][1]
            left, right, acc = ((d_gate, 0, acc_gate), (d_up, 0, acc_up), (act, 1, acc_down))[c]
            turned[...] = left[unit].reshape(halves * tall, units).T

            def grads(cols):
                rows = wide_buf[right, :, :, :, cols].reshape(halves * tall, tile)
                value = dot(turned[...], rows, ((1,), (0,)))
                acc[:, cols] = value if first else acc[:, cols] + value

            by_tiles(grads)

        def between(h):
            def lines_of(i, total):
                at_rows = pl.ds(pl.multiple_of(h * count + i * lines, lines), lines)
                value = raw[at_rows]
                scale = lax.rsqrt(jnp.mean(value * value, axis=1, keepdims=True) + norm_eps)
                hat = value * scale
                gain_row = gain_ref[3:4]
                out_ref[at_rows] = (resid_ref[at_rows] + hat * gain_row).astype(bf16)
                top = cot_ref[at_rows].astype(f32)
                upstream = top * gain_row
                mean = jnp.mean(upstream * hat, axis=1, keepdims=True)
                d_mlp[at_rows] = (scale * (upstream - hat * mean)).astype(bf16)
                return total + jnp.sum(top * hat, axis=0, keepdims=True)

            zero = jnp.zeros((1, width), f32)
            total = lax.fori_loop(0, count // lines, lines_of, zero)
            gain_out[...] = total if h == 0 else gain_out[...] + total

        batches = []

        def write_grads(j, s):
            index = g.outer_flip(g.outer_at, s) * inner
            index = index + lax.rem(g.inner_at + j, inner)
            span = pl.ds(pl.multiple_of(index * slab, slab), slab)
            for copy in batches:
                copy.wait()
            batches.clear()
            for c, src in enumerate((stage.at[0], stage.at[1], stage_down)):
                if c == 0:
                    stage[0] = acc_gate[:, span].astype(bf16).T
                elif c == 1:
                    stage[1] = acc_up[:, span].astype(bf16).T
                else:
                    stage_down[...] = acc_down[:, span].astype(bf16)
                batches.append(fetch(src, grad_refs[j * 3 + c].at[s], local_g.at[c]))

        def core_sum(p, h, s, i):
            unit = s * groups + i
            sums["c", p, h, unit].wait_recv()
            for j in range(per):
                chip = i * per + j
                if chip == 0:

                    def add(at_rows):
                        keep[h, s, at_rows] = keep[h, s, at_rows] + core_land[h, unit, j, at_rows].astype(f32)

                    by_lines(add)
                    continue
                there = s * (chips - 1) + chip - 1

                def add(at_rows):
                    total = hold[h, min(j, held - 1), at_rows] + core_land[h, unit, j, at_rows].astype(f32)
                    chip_send[h, there, at_rows] = total.astype(bf16)

                by_lines(add)
                sums["x", p, h, s, chip] = track(
                    p, h,
                    remote(
                        chip_send.at[h, there], chip_land.at[h, there],
                        s_chip_sum.at[p, h, there], r_chip_sum.at[p, h, there], chip_peer(-chip),
                    ),
                )

        def chip_sum(p, h, s):
            for k in range(1, chips):
                sums["x", p, h, s, k].wait_recv()

            def add(at_rows):
                total = keep[h, s, at_rows]
                for k in range(1, chips):
                    total = total + chip_land[h, s * (chips - 1) + k - 1, at_rows].astype(f32)
                if s == 0:
                    raw[pl.ds(pl.multiple_of(h * count + at_rows.start, lines), lines)] = total
                else:
                    outer_send[h, s - 1, at_rows] = total.astype(bf16)

            by_lines(add)
            if s:
                sums["z", p, h, s] = track(
                    p, h,
                    remote(
                        outer_send.at[h, s - 1], outer_land.at[h, s - 1],
                        s_outer_sum.at[p, h, s], r_outer_sum.at[p, h, s], outer_peer(s),
                    ),
                )

        def outer_sum(p, h, s):
            sums["z", p, h, s].wait_recv()

            def add(at_rows):
                there = pl.ds(pl.multiple_of(h * count + at_rows.start, lines), lines)
                raw[there] = raw[there] + outer_land[h, s - 1, at_rows].astype(f32)

            by_lines(add)

        def all_sent(p, h):
            for copy in unsent[p, h]:
                copy.wait_send()

        last_core = {}
        send_late()
        for task in plan():
            name, args = task[0], task[1:]
            if name == "go":
                go(*args)
            elif name == "zf":
                p, h, s = args
                copies["z", p, h, s].wait_recv()
                source = every[p].at[h, s, 0, mine]
                for k in range(1, chips):
                    chip_copy(p, h, s, k, source)
                core_copy(p, h, s, 0, source)
                if (p, h) == (0, 0):
                    outer_copy(0, 1, s)
            elif name == "xf":
                p, h, s, k = args
                copies["x", p, h, s, k].wait_recv()
                core_copy(p, h, s, k, every[p].at[h, s, k, mine])
            elif name == "load":
                p, h, s, i = args
                for j in range(per):
                    copies["c", p, h, s, i * per + j].wait_recv()
                if (s, i) == (0, 0):
                    own[p, h].wait()
                src = every[p].at[h, s, pl.ds(i * per, per)]
                loads[args] = fetch(src, buf.at[h], local.at[p, h, s * groups + i])
            elif name == "weights":
                for copy in late_copies:
                    copy.wait_recv()
                fetch_weights([(j, last[1]) for j in range(1, inner)])
            elif name == "front":
                p, h, s, i = args
                if p == 0 and not loads.get("weights"):
                    loads["weights"] = True
                    for copy in fetches:
                        copy.wait()
                loads[args].wait()
                (forward, backward)[p](h, s * groups + i)
            elif name == "compute":
                p, h, s, i = args
                unit = s * groups + i
                if h in last_core:
                    last_core[h].wait_send()
                (forward_out, backward_out)[p](h, unit, s, i)
                last_core[h] = remote(
                    core_send.at[h], core_land.at[h, unit],
                    s_core_sum.at[p, h, unit], r_core_sum.at[p, h, unit], core_peer,
                )
                sums["c", p, h, unit] = last_core[h]
            elif name == "cr":
                core_sum(*args)
            elif name == "xr":
                chip_sum(*args)
            elif name == "zr":
                outer_sum(*args)
            elif name == "between":
                all_sent(0, args[0])
                between(args[0])
            elif name == "fetch":
                s, i = args
                loads[task] = []
                for at, src in enumerate((all_x, all_dm)):
                    for h in range(halves):
                        loads[task].append(
                            fetch(
                                src.at[h, s, pl.ds(i * per, per)],
                                wide_buf.at[at, h],
                                local_wide.at[s * groups + i, at * halves + h],
                            )
                        )
            elif name == "grads":
                s, i, c = args
                if c == 0:
                    for copy in loads["fetch", s, i]:
                        copy.wait()
                weight_grads(s * groups + i, c)
            elif name == "write":
                write_grads(*args)

        looped(
            total_rows // lines,
            lambda i: close_rows(pl.ds(pl.multiple_of(i * lines, lines), lines), dres_ref, raw, cot_ref),
        )
        for h in range(halves):
            all_sent(1, h)
            last_core[h].wait_send()
        for copy in batches:
            copy.wait()
        for copy in late_copies:
            copy.wait_send()

    shape = jax.ShapeDtypeStruct
    anywhere = pl.BlockSpec(memory_space=pl.ANY)
    near = pl.BlockSpec(memory_space=pltpu.VMEM)
    sems = pltpu.SemaphoreType.DMA
    flops = 2 * 9 * halves * tall * blocks * width * units
    results = pl.pallas_call(
        kernel,
        out_shape=(
            shape((total_rows, width), bf16),
            shape((total_rows, width), f32),
            shape((1, width), f32),
            shape((halves, outer, chips, both, width), bf16),
            shape((halves, outer, chips, both, width), bf16),
        )
        + (shape((3, slab, units), bf16),) * (inner - 1)
        + (
            shape((outer, slab, units), bf16),
            shape((outer, slab, units), bf16),
            shape((outer, units, slab), bf16),
        )
        * inner,
        in_specs=[anywhere] * (parts + 1) + [near] * 3,
        out_specs=(near, near, near) + (anywhere,) * (2 + inner - 1 + 3 * inner),
        scratch_shapes=[
            pltpu.VMEM((width, units), bf16),
            pltpu.VMEM((width, units), bf16),
            pltpu.VMEM((width, units), bf16),
            pltpu.VMEM((halves, per, both, width), bf16),
            pltpu.VMEM((2, halves, per, both, width), bf16),
            pltpu.VMEM((blocks, halves, tall, units), bf16),
            pltpu.VMEM((blocks, halves, tall, units), bf16),
            pltpu.VMEM((blocks, halves, tall, units), bf16),
            pltpu.VMEM((blocks, halves, tall, units), bf16),
            pltpu.VMEM((blocks, halves, tall, units), bf16),
            pltpu.VMEM((units, halves * tall), bf16),
            pltpu.VMEM((units, width), f32),
            pltpu.VMEM((units, width), f32),
            pltpu.VMEM((units, width), f32),
            pltpu.VMEM((2, slab, units), bf16),
            pltpu.VMEM((units, slab), bf16),
            pltpu.VMEM((halves, per, count, width), bf16),
            pltpu.VMEM((halves, blocks, per, count, width), bf16),
            pltpu.VMEM((halves, held, count, width), f32),
            pltpu.VMEM((halves, outer, count, width), f32),
            pltpu.VMEM((halves, links, count, width), bf16),
            pltpu.VMEM((halves, links, count, width), bf16),
            pltpu.VMEM((halves, outer - 1, count, width), bf16),
            pltpu.VMEM((halves, outer - 1, count, width), bf16),
            pltpu.VMEM((total_rows, width), f32),
            pltpu.VMEM((total_rows, width), bf16),
            sems((2, halves, outer)),
            sems((2, halves, outer)),
            sems((2, halves, outer, chips)),
            sems((2, halves, outer, chips)),
            sems((2, halves, outer, chips)),
            sems((2, halves, outer, chips)),
            sems((2, halves, blocks)),
            sems((2, halves, blocks)),
            sems((2, halves, links)),
            sems((2, halves, links)),
            sems((2, halves, outer)),
            sems((2, halves, outer)),
            sems((2, halves, blocks)),
            sems((2, halves)),
            sems((blocks, 2 * halves)),
            sems((inner * outer, 3)),
            sems((3,)),
            sems((inner,)),
            sems((inner,)),
        ],
        compiler_params=pltpu.CompilerParams(
            collective_id=2, has_side_effects=True, vmem_limit_bytes=62 * 2**20
        ),
        cost_estimate=pl.CostEstimate(flops=flops, bytes_accessed=64 * 2**20, transcendentals=0),
    )(*pieces.values(), rows_low, resid, cotangent, gain)
    grads = results[5 + inner - 1 :]
    return results[:3] + ([[grads[j * 3 + c] for j in range(inner)] for c in range(3)],)


def close_rows(at_rows, dres_ref, raw, cot_ref):
    dres_ref[at_rows] = raw[at_rows] + cot_ref[at_rows].astype(jnp.float32)


def local(
    tokens,
    cotangent,
    block_ids,
    w_qkv,
    m_qkv,
    v_qkv,
    w_out,
    m_out,
    v_out,
    w_gu,
    m_gu,
    v_gu,
    w_down,
    m_down,
    v_down,
    gains,
    gain_m,
    gain_v,
):
    grid = Grid()
    local_x = tokens[0]
    gain_count = gains.shape[0]
    tables = rope_tables(local_x.shape[0] * grid.tensor, HEAD)
    pieces, kept = open_call(
        w_qkv,
        w_out,
        gains,
        local_x,
        w_gu,
        w_down,
        tables,
        block_ids[0],
    )
    full_qkv, full_out, seq_x, gain_rows = kept[:4]
    hats, scales, q_low, k_low, v_low, log_total, context_low = kept[4:11]
    attn_hat, o_scale, resid, resid_low, tops = kept[11:]
    output, d_resid, gain_last, unit_grads = unit_kernel_call(
        resid_low, resid, cotangent[0], gain_rows, pieces
    )
    part_gu, part_down, part_qkv, part_out, part_gains, tops, grad_tokens = attend_back_call(
        d_resid,
        attn_hat,
        o_scale,
        gain_rows,
        full_out,
        context_low,
        q_low,
        k_low,
        v_low,
        log_total,
        hats,
        scales,
        tables,
        block_ids[0],
        seq_x,
        full_qkv,
        gain_last,
        tops,
        unit_grads,
    )
    part_gains = part_gains[:gain_count]
    head_top = tops[: w_qkv.shape[2] // HEAD, 0]
    factor = clip_tau / jnp.maximum(head_top, clip_tau)
    column = jnp.repeat(jnp.sqrt(factor), HEAD)
    column_scale = jnp.stack([column, column, jnp.ones_like(column)])[:, None, :]
    new_qkv, new_m_qkv, new_v_qkv = adam_step(
        w_qkv, part_qkv, m_qkv, v_qkv, rate_matrix, weight_decay
    )
    new_qkv = new_qkv * column_scale
    new_out, new_m_out, new_v_out = adam_step(
        w_out, part_out, m_out, v_out, rate_matrix, weight_decay
    )
    new_gu, new_m_gu, new_v_gu = adam_step(
        w_gu, part_gu.astype(jnp.float32), m_gu, v_gu, rate_matrix, weight_decay
    )
    new_down, new_m_down, new_v_down = adam_step(
        w_down, part_down.astype(jnp.float32), m_down, v_down, rate_matrix, weight_decay
    )
    new_gains, new_gain_m, new_gain_v = adam_step(gains, part_gains, gain_m, gain_v, rate_gain, 0.0)
    return (
        output[None],
        grad_tokens[None],
        new_qkv,
        new_m_qkv,
        new_v_qkv,
        new_qkv.astype(jnp.bfloat16),
        new_out,
        new_m_out,
        new_v_out,
        new_out.astype(jnp.bfloat16),
        new_gu,
        new_m_gu,
        new_v_gu,
        new_gu.astype(jnp.bfloat16),
        new_down,
        new_m_down,
        new_v_down,
        new_down.astype(jnp.bfloat16),
        new_gains,
        new_gain_m,
        new_gain_v,
        factor,
    )


def solution(mesh):
    return jax.shard_map(
        local,
        mesh=mesh,
        in_specs=(
            P("dp", "tensor", None),
            P("dp", "tensor", None),
            P("dp", None),
            P(None, "dp", "tensor"),
            P(None, "dp", "tensor"),
            P(None, "dp", "tensor"),
            P("tensor", "dp"),
            P("tensor", "dp"),
            P("tensor", "dp"),
            P(None, "dp", "tensor"),
            P(None, "dp", "tensor"),
            P(None, "dp", "tensor"),
            P("tensor", "dp"),
            P("tensor", "dp"),
            P("tensor", "dp"),
            P(None, "dp"),
            P(None, "dp"),
            P(None, "dp"),
        ),
        out_specs=(
            P("dp", "tensor", None),
            P("dp", "tensor", None),
            P(None, "dp", "tensor"),
            P(None, "dp", "tensor"),
            P(None, "dp", "tensor"),
            P(None, "dp", "tensor"),
            P("tensor", "dp"),
            P("tensor", "dp"),
            P("tensor", "dp"),
            P("tensor", "dp"),
            P(None, "dp", "tensor"),
            P(None, "dp", "tensor"),
            P(None, "dp", "tensor"),
            P(None, "dp", "tensor"),
            P("tensor", "dp"),
            P("tensor", "dp"),
            P("tensor", "dp"),
            P("tensor", "dp"),
            P(None, "dp"),
            P(None, "dp"),
            P(None, "dp"),
            P("tensor"),
        ),
        check_vma=False,
    )
```

```python
import jax
import jax.numpy as jnp
import numpy as np
from jax import lax
from jax.experimental import pallas as pl
from jax.experimental.pallas import tpu as pltpu
from jax.sharding import PartitionSpec as P

HEAD = 128
STEP = 5


norm_eps = 1e-06
rope_base = 500000.0
beta_one = 0.9
beta_two = 0.95
rate_matrix = 0.01
rate_gain = 0.6
weight_decay = 0.1
adam_eps = 1e-08
clip_tau = 9.0
masked_value = -1e30


def rope_tables(length, size):
    half = size // 2
    freq = np.float32(rope_base) ** (-(np.arange(half, dtype=np.float32) * np.float32(2.0 / size)))
    angle = np.arange(length, dtype=np.float32)[:, None] * freq[None, :]
    angle = np.concatenate([angle, angle], axis=1)
    return (jnp.asarray(np.cos(angle)), jnp.asarray(np.sin(angle)))


def adam_step(param, grad, first, second, rate, decay):
    first = beta_one * first + (1.0 - beta_one) * grad
    second = beta_two * second + (1.0 - beta_two) * grad * grad
    fix_one = 1.0 - beta_one**STEP
    fix_two = 1.0 - beta_two**STEP
    update = first / fix_one / (jnp.sqrt(second / fix_two) + adam_eps)
    return (param - rate * (update + decay * param), first, second)


class Grid:
    def __init__(self):
        self.dp = lax.axis_size("dp")
        self.tensor = lax.axis_size("tensor")
        self.inner = 1
        while self.inner * self.inner * 4 <= self.dp:
            self.inner *= 2
        self.outer = self.dp // self.inner
        self.chips = self.tensor // 2
        self.dp_at = lax.axis_index("dp")
        self.tensor_at = lax.axis_index("tensor")
        self.inner_at = self.dp_at % self.inner
        self.chip_at = self.tensor_at // 2
        self.core_at = self.tensor_at % 2
        self.outer_at = self.dp_at // self.inner

    def path_of(self, index):
        column, row = index // self.inner, index % self.inner
        return row * self.outer + column + (row % 2) * (self.outer - 1 - 2 * column)

    def outer_flip(self, index, step):
        result = 0
        for bit in bits(self.outer):
            side = index // bit % 2
            result = result + bit * (1 - side if step & bit else side)
        return result

    def index_of(self, place):
        row, column = place // self.outer, place % self.outer
        return (column + (row % 2) * (self.outer - 1 - 2 * column)) * self.inner + row


def bits(count):
    return [1 << k for k in range(count.bit_length() - 1)]


def greet(peers):
    barrier = pltpu.get_barrier_semaphore()
    for peer in peers:
        pl.semaphore_signal(barrier, inc=1, device_id=peer, device_id_type=pl.DeviceIdType.MESH)
    pl.semaphore_wait(barrier, len(peers))


def attend_back_call(
    d_resid, attn_hat, o_scale, gain_rows, full_out, context, q_low, k_low, v_low, lse, hats, scales,
    tables, blocks, seq, full_qkv, gain_last, tops, unit_grads,
):
    grid = Grid()
    n, outer, inner, chips, tensor = grid.dp, grid.outer, grid.inner, grid.chips, grid.tensor
    count, width = d_resid.shape
    length, span = context.shape
    heads = span // HEAD
    slab, units = unit_grads[0][0].shape[1:]
    thin = width // n
    half = span // 2
    tall = min(256, length)
    tile = 512
    lines = 32
    ring = 8 + 2
    gain_item, top_item = 8, 9
    bf16, f32 = jnp.bfloat16, jnp.float32
    mesh_id = pl.DeviceIdType.MESH
    flat_grads = [unit_grads[c][j] for j in range(inner) for c in range(3)]
    some = len(flat_grads)
    z_steps = list(range(1, outer))

    def kernel(*refs):
        fixed, far_in, grads_in = refs[:16], refs[16:19], refs[19 : 19 + some]
        rest = refs[19 + some :]
        body(*fixed, far_in, grads_in, *rest)

    def body(
        dres_ref, hat_ref, o_scale_ref, gain_ref, out_w, ctx, q_ref, k_ref, v_ref, lse_ref, scale_ref,
        cos_ref, sin_ref, id_row, last_ref, tops_ref, far_in, grads_in,
        gu_out, down_out, part_ref, part_out, gains_out, tops_out, tokens_out,
        hats, seq, qkv_w, seq_do, d_ctx, d_q, d_k, d_v, d_low, probs_low, id_col, whole, terms, row_terms, turned,
        land, land_gain, land_top, peer_terms, inners, peer_inners,
        gu_land, gu_sum, down_land, down_sum, core_send, core_land, hold, chip_send, chip_land,
        s_ring, r_ring, s_row, r_row, s_in, r_in, s_y, r_y, s_z, r_z, s_core, r_core, s_chip, r_chip, s_gain, r_gain, local,
    ):
        hats_in, seq_in, qkv_in = far_in
        g = Grid()

        def tensor_peer(k, flip):
            core = 1 - g.core_at if flip else g.core_at
            return (g.dp_at, lax.rem(g.chip_at + k + chips, chips) * 2 + core)

        def dp_peer(s, j):
            across = g.outer_flip(g.outer_at, s) * inner
            return (across + lax.rem(g.inner_at + j + inner, inner), g.tensor_at)

        place = g.path_of(g.dp_at)
        after_dp = (g.index_of(lax.rem(place + 1, n)), g.tensor_at)
        before_dp = (g.index_of(lax.rem(place + n - 1, n)), g.tensor_at)
        near = [tensor_peer(k, f) for k in range(chips) for f in (0, 1) if (k, f) != (0, 0)]
        far = [dp_peer(s, 0) for s in range(1, outer)] + [dp_peer(0, j) for j in range(1, inner)]
        greet(near + far + [after_dp, before_dp])

        def remote(src, dst, send, recv, peer):
            copy = pltpu.make_async_remote_copy(
                src_ref=src, dst_ref=dst, send_sem=send, recv_sem=recv,
                device_id=peer, device_id_type=mesh_id,
            )
            copy.start()
            return copy

        def fetch(src, dst, at):
            copy = pltpu.make_async_copy(src, dst, local.at[at])
            copy.start()
            return copy

        def dot(a, b, contract):
            return lax.dot_general(a, b, (contract, ((), ())), preferred_element_type=f32)

        def looped(total, make):
            lax.fori_loop(0, total, lambda i, c: (make(i), c)[1], 0, unroll=total <= 4)

        def rows_of(i, size):
            return pl.ds(pl.multiple_of(i * size, size), size)

        sent = []
        y_copies = {}
        sum_steps = [(c, s) for c in range(3) for s in z_steps + [0]]
        for c, s in sum_steps:
            for j in range(1, inner):
                copy = remote(
                    grads_in[j * 3 + c].at[s],
                    down_land.at[j - 1, s] if c == 2 else gu_land.at[j - 1, c, s],
                    s_y.at[j, c, s],
                    r_y.at[j, c, s],
                    dp_peer(0, j),
                )
                y_copies[j, c, s] = copy
                sent.append(copy)
        own_refs = (gu_sum.at[0], gu_sum.at[1], down_sum)
        own_grads = [fetch(grads_in[c], own_refs[c], c) for c in range(3)]
        fetched = [fetch(hats_in, hats, 3), fetch(seq_in, seq, 4), fetch(qkv_in, qkv_w, 5)]
        z_copies = []
        keeps = []

        def unit_sums(times):
            for _ in range(times):
                if sum_steps:
                    unit_sum(*sum_steps.pop(0))

        def unit_sum(c, s):
            if s == (z_steps + [0])[0]:
                own_grads[c].wait()
            for j in range(1, inner):
                y_copies[j, c, s].wait_recv()

            def add_gu(i):
                rows = rows_of(i, 64)
                total = gu_sum[c, s, rows].astype(f32)
                for j in range(1, inner):
                    total = total + gu_land[j - 1, c, s, rows].astype(f32)
                gu_sum[c, s, rows] = total.astype(bf16)

            def add_down(i):
                rows = rows_of(i, 64)
                total = down_sum[s, rows].astype(f32)
                for j in range(1, inner):
                    total = total + down_land[j - 1, s, rows].astype(f32)
                down_sum[s, rows] = total.astype(bf16)

            there = rows_of(g.outer_at, units)
            if c == 2:
                looped(units // 64, add_down)
                src, dst = down_sum.at[s], down_out.at[there]
            else:
                looped(slab // 64, add_gu)
                src, dst = gu_sum.at[c, s], gu_out.at[c, :, there]
            if s:
                z_copies.append(remote(src, dst, s_z.at[c, s], r_z.at[c, s], dp_peer(s, 0)))
            else:
                keeps.append(fetch(src, dst, 6 + c))

        def way_of(item):
            return 1 if item >= 8 else 1 - 2 * (item // 4)

        def own(item, away):
            index = g.index_of(lax.rem(place - way_of(item) * away + 2 * n, n))
            if item == gain_item:
                return terms.at[index]
            if item == top_item:
                return tops_ref
            side, c = item // 4, item % 4
            return whole.at[c, pl.ds(side * half, half), rows_of(index, thin)]

        def landed(step, item):
            if item == gain_item:
                return land_gain.at[step]
            if item == top_item:
                return land_top.at[step]
            return land.at[step, item]

        hops = {}
        on_path = {}

        def hop(step, item):
            hops[step, item] = remote(
                own(item, 1) if step == 0 else landed(step - 1, item),
                landed(step, item),
                s_ring.at[step, item],
                r_ring.at[step, item],
                after_dp if way_of(item) == 1 else before_dp,
            )

        def depart(*items):
            for item in items:
                on_path[item] = 0
                hop(0, item)

        def advance(*items):
            for item in items:
                step = on_path.get(item, n) + 1
                if step >= n:
                    continue
                on_path[item] = step
                hops[step - 1, item].wait_recv()
                here = landed(step - 1, item)
                if item == top_item:
                    summed = jnp.maximum(here[...], tops_ref[...])
                else:
                    summed = here[...].astype(f32) + own(item, step + 1)[...].astype(f32)
                if step < n - 1:
                    here[...] = summed.astype(here.dtype)
                    hop(step, item)
                elif item == gain_item:
                    gains_out[...] = summed
                elif item == top_item:
                    tops_out[...] = summed
                else:
                    side, c = item // 4, item % 4
                    span_half = pl.ds(side * half, half)
                    if c == 3:
                        part_out[span_half] = summed
                    else:
                        part_ref[c, :, span_half] = summed.T

        def matrix_grad(c, left, right):
            turned[...] = left.T

            def columns(i):
                cols = rows_of(i, tile)
                whole[c, :, cols] = dot(turned[...], right[:, cols], ((1,), (0,))).astype(bf16)

            looped(width // tile, columns)

        t_at = g.tensor_at
        mine = rows_of(t_at, count)

        def open_rows(i, total):
            at = rows_of(i, lines)
            value, hat = dres_ref[at], hat_ref[at]
            upstream = value * gain_ref[2:3]
            mean = jnp.mean(upstream * hat, axis=1, keepdims=True)
            d_attn = (o_scale_ref[at] * (upstream - hat * mean)).astype(bf16)
            seq_do[pl.ds(pl.multiple_of(t_at * count + i * lines, lines), lines)] = d_attn
            return total + jnp.sum(value * hat, axis=0, keepdims=True)

        gain_attn = lax.fori_loop(0, count // lines, open_rows, jnp.zeros((1, width), f32))
        row_terms[0] = jnp.zeros((8, width), f32)
        row_terms[0, 2:3] = gain_attn
        row_terms[0, 3:4] = last_ref[...]
        moves, passed = [], []

        def row_copy(slot, index, peer):
            at = rows_of(index, count)
            copy = remote(seq_do.at[at], seq_do.at[at], s_row.at[slot], r_row.at[slot], peer)
            sent.append(copy)
            return copy

        for k in range(1, chips):
            moves.append(row_copy(k - 1, t_at, tensor_peer(k, 0)))
        to_core = row_copy(chips - 1, t_at, tensor_peer(0, 1))
        id_col[...] = jnp.broadcast_to(id_row[...], (128, length)).T
        unit_sums(1)
        scale = HEAD ** (-0.5)
        for h in range(heads):
            cols = slice(h * HEAD, (h + 1) * HEAD)

            def weigh(i, c, cols=cols, h=h):
                at = rows_of(i, tall)
                raw = dot(q_ref[at, cols], k_ref[:, cols], ((1,), (1,))) * scale
                masked = jnp.where(id_row[...] <= id_col[at, 0:1], raw, masked_value)
                probs_low[h, at] = jnp.exp(masked - lse_ref[at, h : h + 1]).astype(bf16)
                return c

            lax.fori_loop(0, length // tall, weigh, 0, unroll=length // tall <= 4)
            if 2 * (h + 1) == heads:
                unit_sums(1)
        for k in range(1, chips):
            moves[k - 1].wait_recv()
            source = lax.rem(g.chip_at - k + chips, chips) * 2 + g.core_at
            passed.append(row_copy(chips - 1 + k, source, tensor_peer(0, 1)))
        to_core.wait_recv()
        unit_sums(1)
        for copy in passed:
            copy.wait_recv()

        def context_grad(i):
            at = rows_of(i, tall)
            d_ctx[at] = dot(seq_do[at], out_w[...], ((1,), (1,))).astype(bf16)

        looped(length // tall, context_grad)
        unit_sums(1)

        for h in range(heads):
            cols = slice(h * HEAD, (h + 1) * HEAD)

            def head(i, c, cols=cols, h=h):
                at = rows_of(i, tall)
                q_part, ctx_part = q_ref[at, cols], d_ctx[at, cols]
                probs_part = probs_low[h, at]
                probs = probs_part.astype(f32)
                d_probs = dot(ctx_part, v_ref[:, cols], ((1,), (1,)))
                mean = jnp.sum(probs * d_probs, axis=1, keepdims=True)
                d_scores = (probs * (d_probs - mean)).astype(bf16)
                d_q[at, cols] = dot(d_scores, k_ref[:, cols], ((1,), (0,))) * scale
                key = dot(d_scores, q_part, ((0,), (0,))) * scale
                value = dot(probs_part, ctx_part, ((0,), (0,)))
                d_k[:, cols] = jnp.where(i == 0, key, d_k[:, cols] + key)
                d_v[:, cols] = jnp.where(i == 0, value, d_v[:, cols] + value)
                return c

            d_k[:, cols] = jnp.zeros((length, HEAD), f32)
            d_v[:, cols] = jnp.zeros((length, HEAD), f32)
            lax.fori_loop(0, length // tall, head, 0, unroll=length // tall <= 4)
            unit_sums(1)
        fetched[0].wait()
        sign = jnp.where(lax.broadcasted_iota(jnp.int32, (tall, HEAD), 1) < HEAD // 2, -1.0, 1.0)

        def unrotate(i, sums):
            at = rows_of(i, tall)
            cosine, sine = cos_ref[at], sin_ref[at]
            lane = lax.broadcasted_iota(jnp.int32, (tall, 128), 1)
            columns = jnp.zeros((tall, 128), f32)
            result = []
            for c, grad in ((0, d_q), (1, d_k)):
                total = jnp.zeros((tall, 1), f32)
                terms_row = []
                for h in range(heads):
                    cols = slice(h * HEAD, (h + 1) * HEAD)
                    value = grad[at, cols]
                    back = value * cosine - pltpu.roll(value * sine, HEAD // 2, 1) * sign
                    hat = hats[c, at, cols]
                    terms_row.append(jnp.sum(back * hat, axis=0, keepdims=True))
                    at_head = pl.ds(pl.multiple_of(t_at * span + h * HEAD, HEAD), HEAD)
                    back = back * gain_ref[c : c + 1, at_head]
                    grad[at, cols] = back
                    total = total + jnp.sum(back * hat, axis=1, keepdims=True)
                columns = jnp.where(lane == c, total, columns)
                result.append(sums[c] + jnp.concatenate(terms_row, axis=1))
            inners[:, at] = columns.T[:8]
            return tuple(result)

        zero = jnp.zeros((1, span), f32)
        gain_q, gain_k = lax.fori_loop(0, length // tall, unrotate, (zero, zero))
        offset = rows_of(t_at, span)
        row_terms[0, 0:1, offset] = gain_q
        row_terms[0, 1:2, offset] = gain_k
        in_copies = []
        for k in range(chips):
            for f in (0, 1):
                if (k, f) != (0, 0):
                    at = k * 2 + f - 1
                    in_copies.append(
                        remote(inners, peer_inners.at[at], s_in.at[at], r_in.at[at], tensor_peer(k, f))
                    )
        sent.extend(in_copies)
        first = remote(row_terms.at[0], peer_terms.at[0], s_gain.at[0], r_gain.at[0], tensor_peer(0, 1))
        matrix_grad(3, ctx[...], seq_do)
        depart(3, 7)
        for copy in in_copies:
            copy.wait_recv()
        first.wait_recv()
        row_terms[1] = row_terms[0] + peer_terms[0]
        others = [
            remote(row_terms.at[1], peer_terms.at[k], s_gain.at[k], r_gain.at[k], tensor_peer(k, 0))
            for k in range(1, chips)
        ]
        unit_sums(1)

        def normed(i):
            at = rows_of(i, tall)
            sums = inners[:, at]
            for other in range(tensor - 1):
                sums = sums + peer_inners[other, :, at]
            column = jnp.concatenate([sums, jnp.zeros((120, tall), f32)], axis=0).T / width
            for c, grad in ((0, d_q), (1, d_k)):
                value = grad[at] - hats[c, at] * column[:, c : c + 1]
                d_low[c, at] = (scale_ref[at, c : c + 1] * value).astype(bf16)
            d_low[2, at] = d_v[at].astype(bf16)

        looped(length // tall, normed)
        fetched[1].wait()
        for c in (2, 0, 1):
            matrix_grad(c, d_low[c], seq)
            depart(c, c + 4)
            unit_sums(1)

        for copy in others:
            copy.wait_recv()

        def place_terms(i, c):
            cols = pl.ds(pl.multiple_of(i * thin, thin), thin)
            total = row_terms[1, :, cols]
            for k in range(1, chips):
                total = total + peer_terms[k, :, cols]
            terms[i] = total
            return c

        lax.fori_loop(0, n, place_terms, 0)

        depart(gain_item, top_item)
        unit_sums(len(sum_steps))

        fetched[2].wait()
        chip_order = list(range(1, chips)) + [0]
        core_copies, chip_copies = {}, {}

        def token_rows(k, flip, store):
            chip = lax.rem(g.chip_at + k, chips)
            core = 1 - g.core_at if flip else g.core_at
            at = rows_of(chip * 2 + core, count)

            def columns(i):
                cols = rows_of(i, tile)
                total = dot(d_low[0, at], qkv_w[0, cols], ((1,), (1,)))
                for c in (1, 2):
                    total = total + dot(d_low[c, at], qkv_w[c, cols], ((1,), (1,)))
                store(cols, total)

            looped(width // tile, columns)

        duties = []
        for k in chip_order:

            def away(k=k):
                def store(cols, value):
                    core_send[k, :, cols] = value.astype(bf16)

                token_rows(k, True, store)
                core_copies[k] = remote(
                    core_send.at[k], core_land.at[k], s_core.at[k], r_core.at[k], tensor_peer(0, 1)
                )

            def here(k=k):
                def store(cols, value):
                    hold[k, :, cols] = value

                token_rows(k, False, store)

            def join(k=k):
                core_copies[k].wait_recv()

                def add(i):
                    at = rows_of(i, lines)
                    chip_send[k - 1, at] = (hold[k, at] + core_land[k, at].astype(f32)).astype(bf16)

                looped(count // lines, add)
                chip_copies[k] = remote(
                    chip_send.at[k - 1], chip_land.at[k - 1], s_chip.at[k], r_chip.at[k], tensor_peer(k, 0)
                )

            duties += [away, here] + ([join] if k else [])

        def close_tokens():
            core_copies[0].wait_recv()
            for k in range(1, chips):
                chip_copies[k].wait_recv()

            def close(i):
                at = rows_of(i, lines)
                total = dres_ref[at] + hold[0, at] + core_land[0, at].astype(f32)
                for k in range(1, chips):
                    total = total + chip_land[k - 1, at].astype(f32)
                tokens_out[at] = total

            looped(count // lines, close)

        duties.append(close_tokens)
        per_step = -(-len(duties) // (n - 2))
        for step in range(1, n):
            advance(3, 7, 2, 6, 0, 4, 1, 5, gain_item, top_item)
            for _ in range(per_step):
                if duties:
                    duties.pop(0)()
        for copy in z_copies:
            copy.wait()
        for copy in keeps:
            copy.wait()
        for copy in sent + list(hops.values()) + list(core_copies.values()):
            copy.wait_send()
        for copy in list(chip_copies.values()) + [first] + others:
            copy.wait_send()

    shape = jax.ShapeDtypeStruct
    anywhere = pl.BlockSpec(memory_space=pl.ANY)
    vmem = pl.BlockSpec(memory_space=pltpu.VMEM)
    sems = pltpu.SemaphoreType.DMA
    results = pl.pallas_call(
        kernel,
        out_shape=(
            shape((2, slab, outer * units), bf16),
            shape((outer * units, slab), bf16),
            shape((3, thin, span), f32),
            shape((span, thin), f32),
            shape((8, thin), f32),
            shape(tops.shape, f32),
            shape((count, width), f32),
        ),
        in_specs=[vmem] * 16 + [anywhere] * 3 + [anywhere] * some,
        out_specs=(anywhere,) * 2 + (vmem,) * 5,
        scratch_shapes=[
            pltpu.VMEM(hats.shape, f32),
            pltpu.VMEM(seq.shape, bf16),
            pltpu.VMEM(full_qkv.shape, bf16),
            pltpu.VMEM((length, width), bf16),
            pltpu.VMEM((length, span), bf16),
            pltpu.VMEM((length, span), f32),
            pltpu.VMEM((length, span), f32),
            pltpu.VMEM((length, span), f32),
            pltpu.VMEM((3, length, span), bf16),
            pltpu.VMEM((heads, length, length), bf16),
            pltpu.VMEM((length, 128), jnp.int32),
            pltpu.VMEM((4, span, width), bf16),
            pltpu.VMEM((n, 8, thin), f32),
            pltpu.VMEM((2, 8, width), f32),
            pltpu.VMEM((span, length), bf16),
            pltpu.VMEM((n - 1, 8, half, thin), bf16),
            pltpu.VMEM((n - 1, 8, thin), f32),
            pltpu.VMEM((n - 1,) + tops.shape, f32),
            pltpu.VMEM((chips, 8, width), f32),
            pltpu.VMEM((8, length), f32),
            pltpu.VMEM((tensor - 1, 8, length), f32),
            pltpu.VMEM((max(inner - 1, 1), 2, outer, slab, units), bf16),
            pltpu.VMEM((2, outer, slab, units), bf16),
            pltpu.VMEM((max(inner - 1, 1), outer, units, slab), bf16),
            pltpu.VMEM((outer, units, slab), bf16),
            pltpu.VMEM((chips, count, width), bf16),
            pltpu.VMEM((chips, count, width), bf16),
            pltpu.VMEM((chips, count, width), f32),
            pltpu.VMEM((max(chips - 1, 1), count, width), bf16),
            pltpu.VMEM((max(chips - 1, 1), count, width), bf16),
            sems((n - 1, ring)),
            sems((n - 1, ring)),
            sems((2 * chips - 1,)),
            sems((2 * chips - 1,)),
            sems((tensor - 1,)),
            sems((tensor - 1,)),
            sems((inner, 3, outer)),
            sems((inner, 3, outer)),
            sems((3, outer)),
            sems((3, outer)),
            sems((chips,)),
            sems((chips,)),
            sems((chips,)),
            sems((chips,)),
            sems((chips,)),
            sems((chips,)),
            sems((9,)),
        ],
        compiler_params=pltpu.CompilerParams(
            collective_id=1, has_side_effects=True, vmem_limit_bytes=61 * 2**20
        ),
    )(
        d_resid, attn_hat, o_scale, gain_rows, full_out, context, q_low, k_low, v_low, lse, scales,
        tables[0], tables[1], blocks[None, :], gain_last, tops,
        hats, seq, full_qkv, *flat_grads,
    )
    return results


def open_call(w_qkv, w_out, gains, rows, w_gu, w_down, tables, blocks):
    grid = Grid()
    n, outer, inner = grid.dp, grid.outer, grid.inner
    chips, tensor = grid.chips, grid.tensor
    count, width = rows.shape
    length = count * tensor
    lead, slab, span = w_qkv.shape
    gain_count = gains.shape[0]
    half = slab // 2
    part_tall = span // 2
    heads = span // HEAD
    shard_units = w_gu.shape[2]
    units = shard_units // outer
    places = [(j, s) for j in range(inner) for s in range(outer) if not (j and s == outer - 1)]
    parts = len(places)
    ring = 2 * lead + 3
    steps = list(range(1, outer))
    tall = min(256, length)
    tile = 512
    lines = 32
    bf16, f32 = jnp.bfloat16, jnp.float32
    mesh_id = pl.DeviceIdType.MESH

    def kernel(*refs):
        body(*refs[:10], dict(zip(places, refs[10 : 10 + parts])), *refs[10 + parts :])

    def body(
        qkv_any, out_any, rows_any, gu_any, down_any, gains_ref, cos_ref, sin_ref, id_row, rows_ref,
        pieces, qkv_out, flat_out, seq_out,
        gain_rows, hat_ref, scale_ref, q_low, k_low, v_low, lse_ref, context, attn_hat, o_scale, resid, resid_low, top_ref,
        qkv_ref, out_w_ref, seq_ref, all_gains, qkv_wide, out_wide, gu_wide, down_wide, cast, id_col,
        square, squares, core_send, core_land, hold, chip_send, chip_land,
        s_ring, r_ring, s_row, r_row, s_z, r_z, s_y, r_y, s_sq, r_sq, s_core, r_core, s_chip, r_chip, local,
    ):
        g = Grid()

        def tensor_peer(k, flip):
            core = 1 - g.core_at if flip else g.core_at
            return (g.dp_at, lax.rem(g.chip_at + k + chips, chips) * 2 + core)

        def dp_peer(s, j):
            across = g.outer_flip(g.outer_at, s) * inner
            return (across + lax.rem(g.inner_at + j + inner, inner), g.tensor_at)

        near = [tensor_peer(k, f) for k in range(chips) for f in (0, 1) if (k, f) != (0, 0)]
        far = [dp_peer(s, 0) for s in range(1, outer)]
        far += [dp_peer(0, j) for j in sorted({1 % inner, inner - 1} - {0})]
        t_at = g.tensor_at
        place = g.path_of(g.dp_at)
        after = (g.index_of(lax.rem(place + 1, n)), t_at)
        before = (g.index_of(lax.rem(place + n - 1, n)), t_at)
        firsts = []
        for at, (src, dst) in enumerate(((qkv_any, qkv_wide), (out_any, out_wide))):
            firsts.append(pltpu.make_async_copy(src, dst, local.at[3 + at]))
            firsts[-1].start()
        greet(near + far + [after, before])

        def remote(src, dst, send, recv, peer):
            copy = pltpu.make_async_remote_copy(
                src_ref=src, dst_ref=dst, send_sem=send, recv_sem=recv,
                device_id=peer, device_id_type=mesh_id,
            )
            copy.start()
            return copy

        def dot(a, b, contract):
            return lax.dot_general(a, b, (contract, ((), ())), preferred_element_type=f32)

        def looped(total, make):
            lax.fori_loop(0, total, lambda i, c: (make(i), c)[1], 0, unroll=total <= 4)

        def rows_of(i, size):
            return pl.ds(pl.multiple_of(i * size, size), size)

        def fetch(src, dst, at):
            copy = pltpu.make_async_copy(src, dst, local.at[at])
            copy.start()
            return copy

        def views(item, index):
            if item == ring - 1:
                return 1, all_gains.at[index]
            if item >= 2 * lead:
                side = item - 2 * lead
                part = pl.ds(side * part_tall, part_tall)
                return 1 - 2 * side, out_w_ref.at[part, rows_of(index, slab)]
            side, c = item // lead, item % lead
            at = pl.ds(pl.multiple_of(index * slab + side * half, half), half)
            return 1 - 2 * side, qkv_ref.at[c, at]

        hops = {}

        def hop(step, item):
            way = views(item, 0)[0]
            index = g.index_of(lax.rem(place - way * step + n, n))
            _, view = views(item, index)
            hops[step, item] = remote(
                view,
                view,
                s_ring.at[step, item],
                r_ring.at[step, item],
                after if way == 1 else before,
            )

        def row_copy(slot, index, peer, src=None):
            at = seq_ref.at[rows_of(index, count)]
            return remote(at if src is None else src, at, s_row.at[slot], r_row.at[slot], peer)

        order = [c + side * lead for c in range(lead) for side in (0, 1)]
        order += list(range(2 * lead, ring))
        firsts[0].wait()
        for c in range(lead):

            def cast_own(i, c=c):
                at = rows_of(i, lines)
                there = pl.ds(pl.multiple_of(g.dp_at * slab + i * lines, lines), lines)
                qkv_ref[c, there] = qkv_wide[c, at].astype(bf16)

            looped(slab // lines, cast_own)
            for side in (0, 1):
                hop(0, c + side * lead)
        firsts[1].wait()

        def cast_flat(i):
            at = rows_of(i, lines)
            out_w_ref[at, rows_of(g.dp_at, slab)] = out_wide[at].astype(bf16)

        looped(span // lines, cast_flat)
        empty = jnp.zeros((16 - gain_count, slab), f32)
        all_gains[g.dp_at] = jnp.concatenate([gains_ref[...], empty], axis=0).astype(bf16)
        for item in range(2 * lead, ring):
            hop(0, item)
        row_copies = [
            row_copy(k - 1, t_at, tensor_peer(k, 0), rows_any) for k in range(1, chips)
        ]
        row_copies.append(row_copy(chips - 1, t_at, tensor_peer(0, 1), rows_any))
        wide = [fetch(gu_any, gu_wide, 1), fetch(down_any, down_wide, 2)]
        kept = fetch(rows_any, seq_ref.at[rows_of(t_at, count)], 5)

        def cast_wide(c):
            if c == 0:
                wide[0].wait()

            def cast_rows(i):
                at = rows_of(i, lines)
                cast[c, at] = gu_wide[c, at].astype(bf16)

            looped(slab // lines, cast_rows)

        def cast_turned():
            wide[1].wait()

            def cast_rows(i):
                at = rows_of(i, 256)
                cast[2, :, at] = down_wide[at].T.astype(bf16)

            looped(shard_units // 256, cast_rows)

        def ids():
            id_col[...] = jnp.broadcast_to(id_row[...], (128, length)).T

        shadows = [ids, lambda: cast_wide(0), lambda: cast_wide(1), cast_turned]
        for step in range(1, n - 1):
            for item in order:
                hops[step - 1, item].wait_recv()
                hop(step, item)
            if step <= chips - 1:
                row_copies[step - 1].wait_recv()
                source = lax.rem(g.chip_at - step + chips, chips) * 2 + g.core_at
                row_copies.append(row_copy(chips - 1 + step, source, tensor_peer(0, 1)))
            if shadows:
                shadows.pop(0)()

        def cut(s):
            return cast.at[:, :, rows_of(g.outer_flip(g.outer_at, s), units)]

        z_copies = {}

        for s in steps:
            z_copies[s] = remote(cut(s), pieces[0, s], s_z.at[s], r_z.at[s], dp_peer(s, 0))
        own = fetch(cut(0), pieces[0, 0], 0)
        y_copies = {}

        def pass_on(j, s):
            if (j, s) in pieces:
                src = cut(0) if (j, s) == (1, 0) else pieces[j - 1, s]
                y_copies[j, s] = remote(src, pieces[j, s], s_y.at[j, s], r_y.at[j, s], dp_peer(0, 1))

        pass_on(1, 0)
        duties = []
        for s in steps:

            def duty(s=s):
                z_copies[s].wait_recv()
                pass_on(1, s)

            duties.append(duty)
        for j in range(2, inner):
            for s in range(outer - 1):

                def duty(j=j, s=s):
                    y_copies[j - 1, s].wait_recv()
                    pass_on(j, s)

                duties.append(duty)

        def next_duties(times):
            for _ in range(times):
                if duties:
                    duties.pop(0)()

        for item in order:
            hops[n - 2, item].wait_recv()
        for copy in row_copies[chips - 1 :]:
            copy.wait_recv()
        kept.wait()
        outs = [fetch(qkv_ref, qkv_out, 3), fetch(out_w_ref, flat_out, 4), fetch(seq_ref, seq_out, 5)]

        def spread(i):
            gain_rows[:, rows_of(i, slab)] = all_gains[i].astype(f32)[:8]

        looped(n, spread)

        def project(i):
            at = rows_of(i, tall)
            x = seq_ref[at]
            lane = lax.broadcasted_iota(jnp.int32, (tall, 128), 1)
            sums = jnp.zeros((tall, 128), f32)
            for c in range(2):
                value = dot(x, qkv_ref[c], ((1,), (0,)))
                hat_ref[c, at] = value
                sums = jnp.where(lane == c, jnp.sum(value * value, axis=1, keepdims=True), sums)
            v_low[at] = dot(x, qkv_ref[2], ((1,), (0,))).astype(bf16)
            square[:, at] = sums.T[:8]

        looped(length // tall, project)
        sq_copies = []
        for k in range(chips):
            for f in (0, 1):
                if (k, f) != (0, 0):
                    at = k * 2 + f - 1
                    sq_copies.append(
                        remote(square, squares.at[at], s_sq.at[at], r_sq.at[at], tensor_peer(k, f))
                    )
        for copy in sq_copies:
            copy.wait_recv()
        sign = jnp.where(lax.broadcasted_iota(jnp.int32, (tall, HEAD), 1) < HEAD // 2, -1.0, 1.0)

        def rotate(i):
            at = rows_of(i, tall)
            sums = square[:, at]
            for copy_at in range(tensor - 1):
                sums = sums + squares[copy_at, :, at]
            column = jnp.concatenate([sums, jnp.zeros((120, tall), f32)], axis=0).T
            scales = lax.rsqrt(column / width + norm_eps)
            scale_ref[at] = scales
            cosine, sine = cos_ref[at], sin_ref[at] * sign
            for c, low in ((0, q_low), (1, k_low)):
                hat = hat_ref[c, at] * scales[:, c : c + 1]
                hat_ref[c, at] = hat
                normed = hat * gain_rows[c : c + 1, rows_of(t_at, span)]
                for h in range(heads):
                    cols = slice(h * HEAD, (h + 1) * HEAD)
                    value = normed[:, cols]
                    turned = pltpu.roll(value, HEAD // 2, 1)
                    low[at, cols] = (value * cosine + turned * sine).astype(bf16)

        looped(length // tall, rotate)
        scale = HEAD ** (-0.5)
        top_ref[...] = jnp.full((8, 128), masked_value, f32)
        for h in range(heads):
            cols = slice(h * HEAD, (h + 1) * HEAD)

            def attend(i, best, cols=cols, h=h):
                at = rows_of(i, tall)
                raw = dot(q_low[at, cols], k_low[:, cols], ((1,), (1,))) * scale
                masked = jnp.where(id_row[...] <= id_col[at, 0:1], raw, masked_value)
                top = jnp.max(masked, axis=1, keepdims=True)
                weight = jnp.exp(masked - top)
                total = jnp.sum(weight, axis=1, keepdims=True)
                probs = (weight * (1.0 / total)).astype(bf16)
                context[at, cols] = dot(probs, v_low[:, cols], ((1,), (0,))).astype(bf16)
                lse_ref[at, h : h + 1] = top + jnp.log(total)
                return jnp.maximum(best, jnp.max(top, axis=0, keepdims=True))

            best = lax.fori_loop(
                0, length // tall, attend, jnp.full((1, 1), masked_value, f32), unroll=length // tall <= 4
            )
            top_ref[h : h + 1] = jnp.broadcast_to(best, (1, 128))
            if h + 1 == max(heads // 2, 1):
                next_duties(1)
        next_duties(1)

        def out_rows(k, flip, store):
            chip = lax.rem(g.chip_at + k, chips)
            core = 1 - g.core_at if flip else g.core_at
            at = rows_of(chip * 2 + core, count)

            def columns(i):
                cols = rows_of(i, tile)
                store(cols, dot(context[at], out_w_ref[:, cols], ((1,), (0,))))

            looped(width // tile, columns)

        chip_order = list(range(1, chips)) + [0]
        core_copies, chip_copies = {}, {}
        for k in chip_order:

            def store(cols, value, k=k):
                core_send[k, :, cols] = value.astype(bf16)

            out_rows(k, True, store)
            core_copies[k] = remote(
                core_send.at[k], core_land.at[k], s_core.at[k], r_core.at[k], tensor_peer(0, 1)
            )
        for k in chip_order:

            def store(cols, value, k=k):
                hold[k, :, cols] = value

            out_rows(k, False, store)
            if k:
                core_copies[k].wait_recv()

                def add(i, k=k):
                    at = rows_of(i, lines)
                    chip_send[k - 1, at] = (hold[k, at] + core_land[k, at].astype(f32)).astype(bf16)

                looped(count // lines, add)
                chip_copies[k] = remote(
                    chip_send.at[k - 1], chip_land.at[k - 1], s_chip.at[k], r_chip.at[k], tensor_peer(k, 0)
                )
        core_copies[0].wait_recv()
        for k in range(1, chips):
            chip_copies[k].wait_recv()

        def close(i):
            at = rows_of(i, lines)
            raw = hold[0, at] + core_land[0, at].astype(f32)
            for k in range(1, chips):
                raw = raw + chip_land[k - 1, at].astype(f32)
            scale_o = lax.rsqrt(jnp.mean(raw * raw, axis=1, keepdims=True) + norm_eps)
            hat = raw * scale_o
            attn_hat[at] = hat
            o_scale[at] = scale_o
            value = rows_ref[at].astype(f32) + hat * gain_rows[2:3]
            resid[at] = value
            resid_low[at] = value.astype(bf16)

        looped(count // lines, close)
        next_duties(len(duties))
        own.wait()
        for key, copy in y_copies.items():
            if key[0] == inner - 1:
                copy.wait_recv()
        for copy in outs:
            copy.wait()
        sent = list(hops.values()) + row_copies + list(z_copies.values()) + list(y_copies.values()) + sq_copies
        for copy in sent + list(core_copies.values()) + list(chip_copies.values()):
            copy.wait_send()

    shape = jax.ShapeDtypeStruct
    anywhere = pl.BlockSpec(memory_space=pl.ANY)
    vmem = pl.BlockSpec(memory_space=pltpu.VMEM)
    sems = pltpu.SemaphoreType.DMA
    results = pl.pallas_call(
        kernel,
        out_shape=(shape((3, slab, units), bf16),) * parts
        + (
            shape((lead, width, span), bf16),
            shape((span, width), bf16),
            shape((length, width), bf16),
            shape((8, width), f32),
            shape((2, length, span), f32),
            shape((length, 128), f32),
            shape((length, span), bf16),
            shape((length, span), bf16),
            shape((length, span), bf16),
            shape((length, heads), f32),
            shape((length, span), bf16),
            shape((count, width), f32),
            shape((count, 1), f32),
            shape((count, width), f32),
            shape((count, width), bf16),
            shape((8, 128), f32),
        ),
        in_specs=[anywhere] * 5 + [vmem] * 5,
        out_specs=(anywhere,) * (parts + 3) + (vmem,) * 13,
        scratch_shapes=[
            pltpu.VMEM((lead, width, span), bf16),
            pltpu.VMEM((span, width), bf16),
            pltpu.VMEM((length, width), bf16),
            pltpu.VMEM((n, 16, slab), bf16),
            pltpu.VMEM(w_qkv.shape, f32),
            pltpu.VMEM(w_out.shape, f32),
            pltpu.VMEM(w_gu.shape, f32),
            pltpu.VMEM(w_down.shape, f32),
            pltpu.VMEM((3, slab, shard_units), bf16),
            pltpu.VMEM((length, 128), jnp.int32),
            pltpu.VMEM((8, length), f32),
            pltpu.VMEM((tensor - 1, 8, length), f32),
            pltpu.VMEM((chips, count, width), bf16),
            pltpu.VMEM((chips, count, width), bf16),
            pltpu.VMEM((chips, count, width), f32),
            pltpu.VMEM((max(chips - 1, 1), count, width), bf16),
            pltpu.VMEM((max(chips - 1, 1), count, width), bf16),
            sems((n - 1, ring)),
            sems((n - 1, ring)),
            sems((2 * chips - 1,)),
            sems((2 * chips - 1,)),
            sems((outer,)),
            sems((outer,)),
            sems((inner, outer)),
            sems((inner, outer)),
            sems((tensor - 1,)),
            sems((tensor - 1,)),
            sems((chips,)),
            sems((chips,)),
            sems((chips,)),
            sems((chips,)),
            sems((7,)),
        ],
        compiler_params=pltpu.CompilerParams(
            collective_id=0, has_side_effects=True, vmem_limit_bytes=58 * 2**20
        ),
    )(
        w_qkv, w_out, rows, w_gu, w_down, gains, tables[0], tables[1],
        blocks[None, :], rows,
    )
    return dict(zip(places, results[:parts])), results[parts:]


def unit_kernel_call(rows_low, resid, cotangent, gain, pieces):
    grid = Grid()
    outer, chips, inner = grid.outer, grid.chips, grid.inner
    total_rows, width = rows_low.shape
    slab, units = pieces[0, 0].shape[1:]
    places = list(pieces)
    parts = len(places)
    last = (0, outer - 1)
    halves = 2
    count = total_rows // halves
    both = 2 * count
    per = min(2, chips)
    groups = chips // per
    blocks = outer * groups
    tall = per * both
    held = per if groups > 1 else max(per - 1, 1)
    links = outer * (chips - 1)
    steps = list(range(outer))
    far_first = [0] + steps[2:] + steps[1:2]

    def units_of(of_steps):
        return [(s, i) for s in of_steps for i in range(groups)]

    orders = {
        (0, 0): units_of(far_first),
        (0, 1): units_of(far_first),
        (1, 0): units_of(steps),
        (1, 1): units_of(far_first),
    }
    grad_order = units_of(far_first)
    tile = 512
    wide_tiles = width // tile
    unit_tile = min(256, units)
    lines = 32
    bf16, f32 = jnp.bfloat16, jnp.float32
    mesh_id = pl.DeviceIdType.MESH

    def plan():
        chip_us, core_us, hop_us = 5.6, 0.6, 2.0
        free = {"x": 0.0, "core": 0.0, "z near": 0.0, "z far": 0.0}
        arrive, done, tasks = {("w",): 20.0}, {}, {}

        def send(link, when, us):
            free[link] = max(free[link], when) + us
            return free[link] + hop_us

        def add(name, needs, us, after=None):
            tasks[name] = (needs, us, after)

        def send_outer(s, now):
            return send("z near", now, 8.0) if s == 1 else send("z far", now, 10.5)

        def go(p, h):
            def then(now):
                if (p, h) != (0, 1):
                    for s in steps[1:]:
                        arrive["z", p, h, s] = send_outer(s, now)
                for k in range(1, chips):
                    arrive["x", p, h, 0, k] = send("x", now, chip_us)
                arrive["c", p, h, 0, 0] = send("core", now, core_us)

            return then

        def zf(p, h, s):
            def then(now):
                for k in range(1, chips):
                    arrive["x", p, h, s, k] = send("x", now, chip_us)
                arrive["c", p, h, s, 0] = send("core", now, core_us)
                if (p, h) == (0, 0):
                    arrive["z", 0, 1, s] = send_outer(s, now)

            return then

        def xf(p, h, s, k):
            def then(now):
                arrive["c", p, h, s, k] = send("core", now, core_us)

            return then

        def compute(p, h, s, i):
            def then(now):
                arrive["cr", p, h, s, i] = send("core", now, per * core_us)

            return then

        def cr(p, h, s, i):
            def then(now):
                for k in range(i * per, i * per + per):
                    if k:
                        arrive["xr", p, h, s, k] = send("x", now, chip_us)

            return then

        def xr(p, h, s):
            def then(now):
                if s:
                    arrive["zr", p, h, s] = send_outer(s, now)

            return then

        for p in (0, 1):
            for h in range(halves):
                if p == 0:
                    needs = [("do", ("go", 0, h - 1))] if h else []
                else:
                    needs = [("do", ("between", h))]
                add(("go", p, h), needs, 0.2, go(p, h))
                for s in steps[1:]:
                    add(("zf", p, h, s), [("at", ("z", p, h, s))], 0.2, zf(p, h, s))
                for s in steps:
                    for k in range(1, chips):
                        add(("xf", p, h, s, k), [("at", ("x", p, h, s, k))], 0.2, xf(p, h, s, k))
                order = orders[p, h]
                for n, (s, i) in enumerate(order):
                    needs = [("at", ("c", p, h, s, i * per + j)) for j in range(per)]
                    if n:
                        needs.append(("do", ("front", p, h) + order[n - 1]))
                    add(("load", p, h, s, i), needs, 0.2)
                    needs = [("do", ("load", p, h, s, i)), ("do", ("weights",))]
                    add(("front", p, h, s, i), needs, (3.0, 2.0)[p])
                    needs = [("do", ("front", p, h, s, i))]
                    if n:
                        needs.append(("do", ("cr", p, h) + order[n - 1]))
                    add(("compute", p, h, s, i), needs, (2.0, 3.0)[p], compute(p, h, s, i))
                    needs = [("at", ("cr", p, h, s, i)), ("do", ("compute", p, h, s, i))]
                    add(("cr", p, h, s, i), needs, 0.6, cr(p, h, s, i))
                for s in steps:
                    needs = [("do", ("cr", p, h, s, 0))]
                    needs += [("at", ("xr", p, h, s, k)) for k in range(1, chips)]
                    add(("xr", p, h, s), needs, 0.5, xr(p, h, s))
                for s in steps[1:]:
                    needs = [("at", ("zr", p, h, s)), ("do", ("xr", p, h, 0))]
                    add(("zr", p, h, s), needs, 0.4)
        add(("weights",), [("at", ("w",))], 0.2)
        for h in range(halves):
            needs = [("do", ("zr", 0, h, s)) for s in steps[1:]] + [("do", ("xr", 0, h, 0))]
            add(("between", h), needs, 1.0)
        for n, (s, i) in enumerate(grad_order):
            needs = [("do", ("compute", 1, h, s, i)) for h in range(halves)]
            if n:
                needs.append(("do", ("grads",) + grad_order[n - 1] + (2,)))
            add(("fetch", s, i), needs, 0.2)
            for c in range(3):
                needs = [("do", ("grads", s, i, c - 1) if c else ("fetch", s, i))]
                add(("grads", s, i, c), needs, 3.5)
        written = [(j, s) for j in range(inner) for s in range(outer)]
        for n, at in enumerate(written):
            needs = [("do", ("grads",) + grad_order[-1] + (2,))]
            if n:
                needs = [("do", ("write",) + written[n - 1])]
            add(("write",) + at, needs, 0.6)
        rank = {"compute": 1, "front": 2, "fetch": 2, "grads": 3, "write": 4}
        result = []
        now = 0.0
        while tasks:
            best = None
            for name, (needs, us, then) in tasks.items():
                ready = 0.0
                for kind, key in needs:
                    table = arrive if kind == "at" else done
                    if key not in table:
                        ready = None
                        break
                    ready = max(ready, table[key] + (1.0 if key[0] in ("load", "fetch") else 0.0))
                if ready is None:
                    continue
                key = (max(ready, now), rank.get(name[0], 0))
                if best is None or key < best[0]:
                    best = (key, name)
            (ready, _), name = best
            needs, us, then = tasks.pop(name)
            now = ready + us
            done[name] = now
            if then is not None:
                then(now)
            result.append(name)
        return result

    def kernel(*refs):
        piece_refs = dict(zip(places, refs[:parts]))
        fixed = refs[parts : parts + 9]
        k = parts + 9
        late, grad_refs = refs[k : k + inner - 1], refs[k + inner - 1 : k + inner - 1 + 3 * inner]
        for j in range(1, inner):
            piece_refs[j, outer - 1] = late[j - 1]
        body(piece_refs, *fixed, grad_refs, *refs[k + inner - 1 + 3 * inner :])

    def body(
        piece_refs, rows_ref, resid_ref, cot_ref, gain_ref,
        out_ref, dres_ref, gain_out, all_x, all_dm, grad_refs,
        wg, wu, wd, buf, wide_buf, act, coef_gate, coef_up, d_gate, d_up, turned, acc_gate, acc_up, acc_down, stage, stage_down,
        core_send, core_land, hold, keep, chip_send, chip_land, outer_send, outer_land, raw, d_mlp,
        s_outer, r_outer, s_chip, r_chip, s_core, r_core,
        s_core_sum, r_core_sum, s_chip_sum, r_chip_sum, s_outer_sum, r_outer_sum,
        local, local_own, local_wide, local_w, local_g, s_late, r_late,
    ):
        g = Grid()
        core_peer = (g.dp_at, g.chip_at * 2 + 1 - g.core_at)

        def chip_peer(k):
            return (g.dp_at, lax.rem(g.chip_at + k + chips, chips) * 2 + g.core_at)

        def outer_peer(s):
            return (g.outer_flip(g.outer_at, s) * inner + g.inner_at, g.tensor_at)

        def inner_peer(j):
            return (g.outer_at * inner + lax.rem(g.inner_at + j, inner), g.tensor_at)

        greet(
            [core_peer]
            + [chip_peer(k) for k in range(1, chips)]
            + [outer_peer(s) for s in range(1, outer)]
            + [inner_peer(j) for j in range(1, inner)]
        )

        def remote(src, dst, send, recv, peer):
            copy = pltpu.make_async_remote_copy(
                src_ref=src, dst_ref=dst, send_sem=send, recv_sem=recv,
                device_id=peer, device_id_type=mesh_id,
            )
            copy.start()
            return copy

        def fetch(src, dst, sem):
            copy = pltpu.make_async_copy(src, dst, sem)
            copy.start()
            return copy

        def dot(a, b, contract):
            return lax.dot_general(a, b, (contract, ((), ())), preferred_element_type=f32)

        def looped(total, make):
            lax.fori_loop(0, total, lambda i, c: (make(i), c)[1], 0, unroll=total <= 4)

        def by_lines(make):
            looped(count // lines, lambda i: make(pl.ds(pl.multiple_of(i * lines, lines), lines)))

        def by_tiles(make):
            looped(wide_tiles, lambda i: make(pl.ds(pl.multiple_of(i * tile, tile), tile)))

        weights = (wg, wu, wd)
        fetches = []

        late_copies = []

        def send_late():
            for j in range(1, inner):
                late_copies.append(
                    remote(piece_refs[last], piece_refs[j, last[1]], s_late.at[j], r_late.at[j], inner_peer(j))
                )

        def fetch_weights(which):
            for j, s in which:
                index = g.outer_flip(g.outer_at, s) * inner
                index = index + lax.rem(g.inner_at - j + inner, inner)
                span = pl.ds(pl.multiple_of(index * slab, slab), slab)
                for c in range(3):
                    fetches.append(
                        fetch(piece_refs[j, s].at[c], weights[c].at[span], local_w.at[j * outer + s, c])
                    )

        mine, theirs = pl.ds(0, count), pl.ds(count, count)
        every = (all_x, all_dm)
        copies, sums, loads, own = {}, {}, {}, {}
        unsent = {(p, h): [] for p in (0, 1) for h in range(halves)}

        def track(p, h, copy):
            unsent[p, h].append(copy)
            return copy

        def core_copy(p, h, s, k, src):
            dst = every[p].at[h, s, k, theirs]
            copies["c", p, h, s, k] = track(
                p, h, remote(src, dst, s_core.at[p, h, s, k], r_core.at[p, h, s, k], core_peer)
            )

        def chip_copy(p, h, s, k, src):
            dst = every[p].at[h, s, k, mine]
            copies["x", p, h, s, k] = track(
                p, h, remote(src, dst, s_chip.at[p, h, s, k], r_chip.at[p, h, s, k], chip_peer(k))
            )

        def outer_copy(p, h, s):
            source = (rows_ref, d_mlp)[p].at[pl.ds(h * count, count)]
            dst = every[p].at[h, s, 0, mine]
            copies["z", p, h, s] = track(
                p, h, remote(source, dst, s_outer.at[p, h, s], r_outer.at[p, h, s], outer_peer(s))
            )

        def go(p, h):
            source = (rows_ref, d_mlp)[p].at[pl.ds(h * count, count)]
            if (p, h) != (0, 1):
                for s in steps[1:]:
                    outer_copy(p, h, s)
            for k in range(1, chips):
                chip_copy(p, h, 0, k, source)
            core_copy(p, h, 0, 0, source)
            own[p, h] = fetch(source, every[p].at[h, 0, 0, mine], local_own.at[p, h])
            if p == 0 and h == 0:
                fetch_weights(places)

        def part_out(h, s, i, cols, part_sum):
            for j in range(per):
                own_rows = part_sum[j * both : j * both + count]
                if i * per + j == 0:
                    keep[h, s, :, cols] = own_rows
                else:
                    hold[h, min(j, held - 1), :, cols] = own_rows
                core_send[h, j, :, cols] = part_sum[j * both + count : (j + 1) * both].astype(bf16)

        def forward(h, unit):
            for j in range(units // unit_tile):
                cols = pl.ds(j * unit_tile, unit_tile)
                rows = buf[h].reshape(tall, width)
                gate = dot(rows, wg[:, cols], ((1,), (0,)))
                up = dot(rows, wu[:, cols], ((1,), (0,)))
                sigma = jax.nn.sigmoid(gate)
                silu = gate * sigma
                act[unit, h, :, cols] = (silu * up).astype(bf16)
                coef_up[unit, h, :, cols] = silu.astype(bf16)
                coef_gate[unit, h, :, cols] = (
                    up * sigma * (1.0 + gate * (1.0 - sigma))
                ).astype(bf16)

        def forward_out(h, unit, s, i):
            by_tiles(
                lambda cols: part_out(h, s, i, cols, dot(act[unit, h], wd[cols, :], ((1,), (1,))))
            )

        def backward(h, unit):
            for j in range(units // unit_tile):
                cols = pl.ds(j * unit_tile, unit_tile)
                d_act = dot(buf[h].reshape(tall, width), wd[:, cols], ((1,), (0,)))
                d_gate[unit, h, :, cols] = (d_act * coef_gate[unit, h, :, cols].astype(f32)).astype(bf16)
                d_up[unit, h, :, cols] = (d_act * coef_up[unit, h, :, cols].astype(f32)).astype(bf16)

        def backward_out(h, unit, s, i):
            def into(cols):
                part_sum = dot(d_gate[unit, h], wg[cols, :], ((1,), (1,)))
                part_sum = part_sum + dot(d_up[unit, h], wu[cols, :], ((1,), (1,)))
                part_out(h, s, i, cols, part_sum)

            by_tiles(into)

        def weight_grads(unit, c):
            first = unit == grad_order[0][0] * groups + grad_order[0][1]
            left, right, acc = ((d_gate, 0, acc_gate), (d_up, 0, acc_up), (act, 1, acc_down))[c]
            turned[...] = left[unit].reshape(halves * tall, units).T

            def grads(cols):
                rows = wide_buf[right, :, :, :, cols].reshape(halves * tall, tile)
                value = dot(turned[...], rows, ((1,), (0,)))
                acc[:, cols] = value if first else acc[:, cols] + value

            by_tiles(grads)

        def between(h):
            def lines_of(i, total):
                at_rows = pl.ds(pl.multiple_of(h * count + i * lines, lines), lines)
                value = raw[at_rows]
                scale = lax.rsqrt(jnp.mean(value * value, axis=1, keepdims=True) + norm_eps)
                hat = value * scale
                gain_row = gain_ref[3:4]
                out_ref[at_rows] = (resid_ref[at_rows] + hat * gain_row).astype(bf16)
                top = cot_ref[at_rows].astype(f32)
                upstream = top * gain_row
                mean = jnp.mean(upstream * hat, axis=1, keepdims=True)
                d_mlp[at_rows] = (scale * (upstream - hat * mean)).astype(bf16)
                return total + jnp.sum(top * hat, axis=0, keepdims=True)

            zero = jnp.zeros((1, width), f32)
            total = lax.fori_loop(0, count // lines, lines_of, zero)
            gain_out[...] = total if h == 0 else gain_out[...] + total

        batches = []

        def write_grads(j, s):
            index = g.outer_flip(g.outer_at, s) * inner
            index = index + lax.rem(g.inner_at + j, inner)
            span = pl.ds(pl.multiple_of(index * slab, slab), slab)
            for copy in batches:
                copy.wait()
            batches.clear()
            for c, src in enumerate((stage.at[0], stage.at[1], stage_down)):
                if c == 0:
                    stage[0] = acc_gate[:, span].astype(bf16).T
                elif c == 1:
                    stage[1] = acc_up[:, span].astype(bf16).T
                else:
                    stage_down[...] = acc_down[:, span].astype(bf16)
                batches.append(fetch(src, grad_refs[j * 3 + c].at[s], local_g.at[c]))

        def core_sum(p, h, s, i):
            unit = s * groups + i
            sums["c", p, h, unit].wait_recv()
            for j in range(per):
                chip = i * per + j
                if chip == 0:

                    def add(at_rows):
                        keep[h, s, at_rows] = keep[h, s, at_rows] + core_land[h, unit, j, at_rows].astype(f32)

                    by_lines(add)
                    continue
                there = s * (chips - 1) + chip - 1

                def add(at_rows):
                    total = hold[h, min(j, held - 1), at_rows] + core_land[h, unit, j, at_rows].astype(f32)
                    chip_send[h, there, at_rows] = total.astype(bf16)

                by_lines(add)
                sums["x", p, h, s, chip] = track(
                    p, h,
                    remote(
                        chip_send.at[h, there], chip_land.at[h, there],
                        s_chip_sum.at[p, h, there], r_chip_sum.at[p, h, there], chip_peer(-chip),
                    ),
                )

        def chip_sum(p, h, s):
            for k in range(1, chips):
                sums["x", p, h, s, k].wait_recv()

            def add(at_rows):
                total = keep[h, s, at_rows]
                for k in range(1, chips):
                    total = total + chip_land[h, s * (chips - 1) + k - 1, at_rows].astype(f32)
                if s == 0:
                    raw[pl.ds(pl.multiple_of(h * count + at_rows.start, lines), lines)] = total
                else:
                    outer_send[h, s - 1, at_rows] = total.astype(bf16)

            by_lines(add)
            if s:
                sums["z", p, h, s] = track(
                    p, h,
                    remote(
                        outer_send.at[h, s - 1], outer_land.at[h, s - 1],
                        s_outer_sum.at[p, h, s], r_outer_sum.at[p, h, s], outer_peer(s),
                    ),
                )

        def outer_sum(p, h, s):
            sums["z", p, h, s].wait_recv()

            def add(at_rows):
                there = pl.ds(pl.multiple_of(h * count + at_rows.start, lines), lines)
                raw[there] = raw[there] + outer_land[h, s - 1, at_rows].astype(f32)

            by_lines(add)

        def all_sent(p, h):
            for copy in unsent[p, h]:
                copy.wait_send()

        last_core = {}
        send_late()
        for task in plan():
            name, args = task[0], task[1:]
            if name == "go":
                go(*args)
            elif name == "zf":
                p, h, s = args
                copies["z", p, h, s].wait_recv()
                source = every[p].at[h, s, 0, mine]
                for k in range(1, chips):
                    chip_copy(p, h, s, k, source)
                core_copy(p, h, s, 0, source)
                if (p, h) == (0, 0):
                    outer_copy(0, 1, s)
            elif name == "xf":
                p, h, s, k = args
                copies["x", p, h, s, k].wait_recv()
                core_copy(p, h, s, k, every[p].at[h, s, k, mine])
            elif name == "load":
                p, h, s, i = args
                for j in range(per):
                    copies["c", p, h, s, i * per + j].wait_recv()
                if (s, i) == (0, 0):
                    own[p, h].wait()
                src = every[p].at[h, s, pl.ds(i * per, per)]
                loads[args] = fetch(src, buf.at[h], local.at[p, h, s * groups + i])
            elif name == "weights":
                for copy in late_copies:
                    copy.wait_recv()
                fetch_weights([(j, last[1]) for j in range(1, inner)])
            elif name == "front":
                p, h, s, i = args
                if p == 0 and not loads.get("weights"):
                    loads["weights"] = True
                    for copy in fetches:
                        copy.wait()
                loads[args].wait()
                (forward, backward)[p](h, s * groups + i)
            elif name == "compute":
                p, h, s, i = args
                unit = s * groups + i
                if h in last_core:
                    last_core[h].wait_send()
                (forward_out, backward_out)[p](h, unit, s, i)
                last_core[h] = remote(
                    core_send.at[h], core_land.at[h, unit],
                    s_core_sum.at[p, h, unit], r_core_sum.at[p, h, unit], core_peer,
                )
                sums["c", p, h, unit] = last_core[h]
            elif name == "cr":
                core_sum(*args)
            elif name == "xr":
                chip_sum(*args)
            elif name == "zr":
                outer_sum(*args)
            elif name == "between":
                all_sent(0, args[0])
                between(args[0])
            elif name == "fetch":
                s, i = args
                loads[task] = []
                for at, src in enumerate((all_x, all_dm)):
                    for h in range(halves):
                        loads[task].append(
                            fetch(
                                src.at[h, s, pl.ds(i * per, per)],
                                wide_buf.at[at, h],
                                local_wide.at[s * groups + i, at * halves + h],
                            )
                        )
            elif name == "grads":
                s, i, c = args
                if c == 0:
                    for copy in loads["fetch", s, i]:
                        copy.wait()
                weight_grads(s * groups + i, c)
            elif name == "write":
                write_grads(*args)

        looped(
            total_rows // lines,
            lambda i: close_rows(pl.ds(pl.multiple_of(i * lines, lines), lines), dres_ref, raw, cot_ref),
        )
        for h in range(halves):
            all_sent(1, h)
            last_core[h].wait_send()
        for copy in batches:
            copy.wait()
        for copy in late_copies:
            copy.wait_send()

    shape = jax.ShapeDtypeStruct
    anywhere = pl.BlockSpec(memory_space=pl.ANY)
    near = pl.BlockSpec(memory_space=pltpu.VMEM)
    sems = pltpu.SemaphoreType.DMA
    flops = 2 * 9 * halves * tall * blocks * width * units
    results = pl.pallas_call(
        kernel,
        out_shape=(
            shape((total_rows, width), bf16),
            shape((total_rows, width), f32),
            shape((1, width), f32),
            shape((halves, outer, chips, both, width), bf16),
            shape((halves, outer, chips, both, width), bf16),
        )
        + (shape((3, slab, units), bf16),) * (inner - 1)
        + (
            shape((outer, slab, units), bf16),
            shape((outer, slab, units), bf16),
            shape((outer, units, slab), bf16),
        )
        * inner,
        in_specs=[anywhere] * (parts + 1) + [near] * 3,
        out_specs=(near, near, near) + (anywhere,) * (2 + inner - 1 + 3 * inner),
        scratch_shapes=[
            pltpu.VMEM((width, units), bf16),
            pltpu.VMEM((width, units), bf16),
            pltpu.VMEM((width, units), bf16),
            pltpu.VMEM((halves, per, both, width), bf16),
            pltpu.VMEM((2, halves, per, both, width), bf16),
            pltpu.VMEM((blocks, halves, tall, units), bf16),
            pltpu.VMEM((blocks, halves, tall, units), bf16),
            pltpu.VMEM((blocks, halves, tall, units), bf16),
            pltpu.VMEM((blocks, halves, tall, units), bf16),
            pltpu.VMEM((blocks, halves, tall, units), bf16),
            pltpu.VMEM((units, halves * tall), bf16),
            pltpu.VMEM((units, width), f32),
            pltpu.VMEM((units, width), f32),
            pltpu.VMEM((units, width), f32),
            pltpu.VMEM((2, slab, units), bf16),
            pltpu.VMEM((units, slab), bf16),
            pltpu.VMEM((halves, per, count, width), bf16),
            pltpu.VMEM((halves, blocks, per, count, width), bf16),
            pltpu.VMEM((halves, held, count, width), f32),
            pltpu.VMEM((halves, outer, count, width), f32),
            pltpu.VMEM((halves, links, count, width), bf16),
            pltpu.VMEM((halves, links, count, width), bf16),
            pltpu.VMEM((halves, outer - 1, count, width), bf16),
            pltpu.VMEM((halves, outer - 1, count, width), bf16),
            pltpu.VMEM((total_rows, width), f32),
            pltpu.VMEM((total_rows, width), bf16),
            sems((2, halves, outer)),
            sems((2, halves, outer)),
            sems((2, halves, outer, chips)),
            sems((2, halves, outer, chips)),
            sems((2, halves, outer, chips)),
            sems((2, halves, outer, chips)),
            sems((2, halves, blocks)),
            sems((2, halves, blocks)),
            sems((2, halves, links)),
            sems((2, halves, links)),
            sems((2, halves, outer)),
            sems((2, halves, outer)),
            sems((2, halves, blocks)),
            sems((2, halves)),
            sems((blocks, 2 * halves)),
            sems((inner * outer, 3)),
            sems((3,)),
            sems((inner,)),
            sems((inner,)),
        ],
        compiler_params=pltpu.CompilerParams(
            collective_id=2, has_side_effects=True, vmem_limit_bytes=62 * 2**20
        ),
        cost_estimate=pl.CostEstimate(flops=flops, bytes_accessed=64 * 2**20, transcendentals=0),
    )(*pieces.values(), rows_low, resid, cotangent, gain)
    grads = results[5 + inner - 1 :]
    return results[:3] + ([[grads[j * 3 + c] for j in range(inner)] for c in range(3)],)


def close_rows(at_rows, dres_ref, raw, cot_ref):
    dres_ref[at_rows] = raw[at_rows] + cot_ref[at_rows].astype(jnp.float32)


def local(
    tokens,
    cotangent,
    block_ids,
    w_qkv,
    m_qkv,
    v_qkv,
    w_out,
    m_out,
    v_out,
    w_gu,
    m_gu,
    v_gu,
    w_down,
    m_down,
    v_down,
    gains,
    gain_m,
    gain_v,
):
    grid = Grid()
    local_x = tokens[0]
    gain_count = gains.shape[0]
    tables = rope_tables(local_x.shape[0] * grid.tensor, HEAD)
    pieces, kept = open_call(
        w_qkv,
        w_out,
        gains,
        local_x,
        w_gu,
        w_down,
        tables,
        block_ids[0],
    )
    full_qkv, full_out, seq_x, gain_rows = kept[:4]
    hats, scales, q_low, k_low, v_low, log_total, context_low = kept[4:11]
    attn_hat, o_scale, resid, resid_low, tops = kept[11:]
    output, d_resid, gain_last, unit_grads = unit_kernel_call(
        resid_low, resid, cotangent[0], gain_rows, pieces
    )
    part_gu, part_down, part_qkv, part_out, part_gains, tops, grad_tokens = attend_back_call(
        d_resid,
        attn_hat,
        o_scale,
        gain_rows,
        full_out,
        context_low,
        q_low,
        k_low,
        v_low,
        log_total,
        hats,
        scales,
        tables,
        block_ids[0],
        seq_x,
        full_qkv,
        gain_last,
        tops,
        unit_grads,
    )
    part_gains = part_gains[:gain_count]
    head_top = tops[: w_qkv.shape[2] // HEAD, 0]
    factor = clip_tau / jnp.maximum(head_top, clip_tau)
    column = jnp.repeat(jnp.sqrt(factor), HEAD)
    column_scale = jnp.stack([column, column, jnp.ones_like(column)])[:, None, :]
    new_qkv, new_m_qkv, new_v_qkv = adam_step(
        w_qkv, part_qkv, m_qkv, v_qkv, rate_matrix, weight_decay
    )
    new_qkv = new_qkv * column_scale
    new_out, new_m_out, new_v_out = adam_step(
        w_out, part_out, m_out, v_out, rate_matrix, weight_decay
    )
    new_gu, new_m_gu, new_v_gu = adam_step(
        w_gu, part_gu.astype(jnp.float32), m_gu, v_gu, rate_matrix, weight_decay
    )
    new_down, new_m_down, new_v_down = adam_step(
        w_down, part_down.astype(jnp.float32), m_down, v_down, rate_matrix, weight_decay
    )
    new_gains, new_gain_m, new_gain_v = adam_step(gains, part_gains, gain_m, gain_v, rate_gain, 0.0)
    return (
        output[None],
        grad_tokens[None],
        new_qkv,
        new_m_qkv,
        new_v_qkv,
        new_qkv.astype(jnp.bfloat16),
        new_out,
        new_m_out,
        new_v_out,
        new_out.astype(jnp.bfloat16),
        new_gu,
        new_m_gu,
        new_v_gu,
        new_gu.astype(jnp.bfloat16),
        new_down,
        new_m_down,
        new_v_down,
        new_down.astype(jnp.bfloat16),
        new_gains,
        new_gain_m,
        new_gain_v,
        factor,
    )


def solution(mesh):
    return jax.shard_map(
        local,
        mesh=mesh,
        in_specs=(
            P("dp", "tensor", None),
            P("dp", "tensor", None),
            P("dp", None),
            P(None, "dp", "tensor"),
            P(None, "dp", "tensor"),
            P(None, "dp", "tensor"),
            P("tensor", "dp"),
            P("tensor", "dp"),
            P("tensor", "dp"),
            P(None, "dp", "tensor"),
            P(None, "dp", "tensor"),
            P(None, "dp", "tensor"),
            P("tensor", "dp"),
            P("tensor", "dp"),
            P("tensor", "dp"),
            P(None, "dp"),
            P(None, "dp"),
            P(None, "dp"),
        ),
        out_specs=(
            P("dp", "tensor", None),
            P("dp", "tensor", None),
            P(None, "dp", "tensor"),
            P(None, "dp", "tensor"),
            P(None, "dp", "tensor"),
            P(None, "dp", "tensor"),
            P("tensor", "dp"),
            P("tensor", "dp"),
            P("tensor", "dp"),
            P("tensor", "dp"),
            P(None, "dp", "tensor"),
            P(None, "dp", "tensor"),
            P(None, "dp", "tensor"),
            P(None, "dp", "tensor"),
            P("tensor", "dp"),
            P("tensor", "dp"),
            P("tensor", "dp"),
            P("tensor", "dp"),
            P(None, "dp"),
            P(None, "dp"),
            P(None, "dp"),
            P("tensor"),
        ),
        check_vma=False,
    )
```
